32 devices in a mesh: blk: 8 (over z, y), head: 4 (over x, core).
Axes of the slice: x: 2, y: 2, z: 4, core: 2. Of those that a mesh axis runs over, the one named last changes fastest.
Arguments:
- inputs: bfloat16 [4096, 704], P('blk'), may hold values from -6 to 6
- out_queries: bfloat16 [8192, 1026], P('blk'), may hold values from -6 to 6
- clip_lengths: int32 [6], replicated, may hold values from 1 to 7767, as said below
- labels: int32 [8192], P('blk'), may hold values from 0 to 703
- modality: int32 [8192], P('blk'), may hold values from 0 to 2
- labeled: int32 [8192], P('blk'), may hold values from 0 to 1
- head_params: float32 [4751360], P(('head', 'blk')), may hold values from -4 to 4
- head_first: float32 [4751360], P(('head', 'blk')), may hold values from -1 to 1
- head_second: float32 [4751360], P(('head', 'blk')), may hold values from 0 to 1
- common_params: float32 [928768], P('blk'), may hold values from -4 to 4
- common_first: float32 [928768], P('blk'), may hold values from -1 to 1
- common_second: float32 [928768], P('blk'), may hold values from 0 to 1
Outputs:
- head_new: float32 [4751360], P(('head', 'blk'))
- head_first_new: float32 [4751360], P(('head', 'blk'))
- head_second_new: float32 [4751360], P(('head', 'blk'))
- head_copy: bfloat16 [4751360], P(('head', 'blk'))
- common_new: float32 [928768], P('blk')
- common_first_new: float32 [928768], P('blk')
- common_second_new: float32 [928768], P('blk')
- common_copy: bfloat16 [928768], P('blk')
- loss_sums: float32 [3], replicated
- label_counts: float32 [3], replicated
- clip_norm: float32 [], replicated
The draws below stay inside these ranges and needn't reach their ends.
Inputs may be any that keep to these rules, and one draw needn't show every extreme that they name: `clip_lengths`: 6 lengths summing to 8192; one clip, at a place drawn from the seed, holds exactly the largest length and runs from the rows of the first index of blk to those of the last; the others hold together (5) * (85) rows, each fewer than 170.
All inputs are finite; a program needn't handle non-finite values.
Results may differ from the reference program's by a relative error of at most 0.017.
Values may be sent and summed in bfloat16 or wider, within the bound.
A program may use at most 192 MiB of HBM per device.

```python
import math
import jax
import jax.numpy as jnp
from jax import lax

D = 512
HEADS = 8
HD = 64
FF = 2048
DI = 704
DQ = 1026
C = 704
LAT = 784
MODES = 3
CLIPS = 6
STEP = 10
L_DEV = 1024
I_DEV = 512
HL = 128
FF_DEV = 512
C_DEV = 176
ROWS = 8192
INPUTS = 4096
P_H = 1187840
P_C = 928768
N_BLK = 8
N_HEAD = 4


def draw_clip_lengths(key, part):
    key = jax.random.fold_in(key, 11)
    first_key, second_key = jax.random.split(key)
    base = L_DEV // (2 * CLIPS)
    others = CLIPS - 1
    shifts = jax.random.randint(first_key, (others,), 0, base)
    shorter = (base + shifts - jnp.roll(shifts, -1)).astype(jnp.int32)
    longest = jax.random.randint(second_key, (), 0, CLIPS)
    numbers = jnp.arange(CLIPS, dtype=jnp.int32)
    source = jnp.where(numbers < longest, numbers, numbers - 1)
    source = jnp.clip(source, 0, others - 1)
    picked = jnp.sum(jnp.where(source[:, None] == jnp.arange(others, dtype=jnp.int32)[None, :], shorter[None, :], 0), 1)
    return jnp.where(numbers == longest, ROWS - others * base, picked).astype(jnp.int32)


def draw_labeled(key, part):
    key = jax.random.fold_in(key, 12)
    places = jnp.arange(ROWS, dtype=jnp.int32)
    ticket = jax.random.randint(key, (ROWS,), 0, 4 * ROWS)
    return (ticket < ROWS + 2 * places).astype(jnp.int32)


def head_scale(top):
    position = jnp.arange(N_HEAD * P_H, dtype=jnp.int32)
    device = position // P_H
    within = position % P_H
    segment_sizes = [D * HL, DI * 2 * HL, HL * D, D * 3 * HL, HL * D, D * FF_DEV, FF_DEV * D, D * C_DEV]
    segment_scales = [D ** (-0.5), DI ** (-0.5), 3.0 * D ** (-0.5), D ** (-0.5), 3.0 * D ** (-0.5), D ** (-0.5), FF ** (-0.5), D ** (-0.5)]
    result = jnp.zeros(position.shape, jnp.float32)
    border = 0
    for amount, factor in zip(segment_sizes, segment_scales):
        inside = (within >= border) & (within < border + amount)
        result = jnp.where(inside, factor, result)
        border += amount
    rising = 1.0 + (top - 1.0) * device.astype(jnp.float32) / max(N_HEAD - 1, 1)
    return jnp.where(within >= border - D * C_DEV, result * rising, result)


def common_layout():
    position = jnp.arange(P_C, dtype=jnp.int32)
    gain_start = DQ * D + LAT * D
    weight_scale = jnp.where(position < DQ * D, DQ ** (-0.5), 0.25)
    column = (position - gain_start) % D
    slope = 0.6 + 0.8 * column.astype(jnp.float32) / D
    is_gain = position >= gain_start
    return (weight_scale, slope, is_gain)


def draw_head_params(key, part):
    key = jax.random.fold_in(key, 13)
    noise = jnp.clip(jax.random.normal(key, (N_HEAD * P_H,), jnp.float32), -4.0, 4.0)
    return noise * head_scale(3.0)


def draw_common_params(key, part):
    key = jax.random.fold_in(key, 14)
    weight_scale, slope, is_gain = common_layout()
    noise = jnp.clip(jax.random.normal(key, (P_C,), jnp.float32), -4.0, 4.0)
    return jnp.where(is_gain, slope * (1.0 + 0.1 * noise), weight_scale * noise)


def typical_grad():
    return 0.05 / (N_HEAD * P_H + P_C) ** 0.5


def draw_head_first(key, part):
    key = jax.random.fold_in(key, 15)
    noise = jnp.clip(jax.random.normal(key, (N_HEAD * P_H,), jnp.float32), -4.0, 4.0)
    return 0.111 * typical_grad() * noise


def draw_head_second(key, part):
    key = jax.random.fold_in(key, 16)
    spread = jax.random.uniform(key, (N_HEAD * P_H,), jnp.float32, 0.0, 1.3862944)
    return 0.001001 * typical_grad() ** 2 * jnp.exp(spread)


def draw_common_first(key, part):
    key = jax.random.fold_in(key, 17)
    weight_scale, slope, is_gain = common_layout()
    noise = jnp.clip(jax.random.normal(key, (P_C,), jnp.float32), -4.0, 4.0)
    return 0.111 * typical_grad() * noise * jnp.where(is_gain, 4.0, 1.0)


def draw_common_second(key, part):
    key = jax.random.fold_in(key, 18)
    weight_scale, slope, is_gain = common_layout()
    spread = jax.random.uniform(key, (P_C,), jnp.float32, 0.0, 1.3862944)
    return 0.001001 * typical_grad() ** 2 * jnp.exp(spread) * jnp.where(is_gain, 16.0, 1.0)


def set_ends(values, rng, smallest, largest):
    longest = values.shape.index(max(values.shape))
    spots = []
    for shift in (0, 1):
        where = [jax.random.randint(jax.random.fold_in(rng, axis), (), 0, length) for axis, length in enumerate(values.shape)]
        where[longest] = (where[longest] + shift) % values.shape[longest]
        spots.append(tuple(where))
    return values.at[spots[0]].set(smallest).at[spots[1]].set(largest)


def levels(stream_key, dims, cuts, smallest, largest):
    def one(axis_at, blocks):
        heights = jax.random.uniform(jax.random.fold_in(jax.random.fold_in(stream_key, 6), axis_at), (blocks,), jnp.float32, smallest / len(cuts), largest / len(cuts))
        return jnp.repeat(jnp.exp(heights), dims[axis_at] // blocks).reshape((-1,) + (1,) * (len(dims) - axis_at - 1))

    level = one(*cuts[0])
    for cut in cuts[1:]:
        level = level * one(*cut)
    return level


def bell_draw(stream_key, dims, deviation, limit, cuts=(), held_as=jnp.bfloat16):
    array = deviation * jax.random.normal(stream_key, dims, jnp.float32)
    if cuts:
        array = array * levels(stream_key, dims, cuts, -0.22, 0.18)
    return jnp.clip(array, -limit, limit).astype(held_as)


def setup_inputs(seed: int = 0) -> dict:
    arg_keys = jax.random.split(jax.random.key(seed), 13)
    inputs = bell_draw(arg_keys[0], (INPUTS, DI), 1.0, 6.0, ((0, 8),))
    out_queries = bell_draw(arg_keys[1], (ROWS, DQ), 1.0, 6.0, ((0, 8),))
    clip_lengths = draw_clip_lengths(jax.random.fold_in(arg_keys[12], 71), 0)
    labels = set_ends(jax.random.randint(arg_keys[3], (ROWS,), 0, C), jax.random.fold_in(arg_keys[3], 1), 0, C - 1).astype(jnp.int32)
    modality = set_ends(jax.random.randint(arg_keys[4], (ROWS,), 0, MODES), jax.random.fold_in(arg_keys[4], 1), 0, MODES - 1).astype(jnp.int32)
    labeled = draw_labeled(jax.random.fold_in(arg_keys[12], 71), 0)
    head_params = draw_head_params(jax.random.fold_in(arg_keys[12], 71), 0)
    head_first = draw_head_first(jax.random.fold_in(arg_keys[12], 71), 0)
    head_second = draw_head_second(jax.random.fold_in(arg_keys[12], 71), 0)
    common_params = draw_common_params(jax.random.fold_in(arg_keys[12], 71), 0)
    common_first = draw_common_first(jax.random.fold_in(arg_keys[12], 71), 0)
    common_second = draw_common_second(jax.random.fold_in(arg_keys[12], 71), 0)
    return dict(inputs=inputs, out_queries=out_queries, clip_lengths=clip_lengths, labels=labels, modality=modality, labeled=labeled, head_params=head_params, head_first=head_first, head_second=head_second, common_params=common_params, common_first=common_first, common_second=common_second)


@jax.custom_vjp
def low(v):
    return lax.optimization_barrier(v.astype(jnp.bfloat16)).astype(jnp.float32)

@jax.custom_vjp
def low_back(v):
    return v

def low_keep(v):
    return (low(v), None)

def low_pass(kept, grad):
    return (grad,)

def back_keep(v):
    return (v, None)

def back_low(kept, grad):
    return (low(grad),)
low.defvjp(low_keep, low_pass)
low_back.defvjp(back_keep, back_low)
highest = lax.Precision.HIGHEST
norm_eps = 1e-05
learn_rate = 0.1
beta_one = 0.9
beta_two = 0.999
adam_eps = 1e-08
weight_decay = 0.01
clip_limit = 0.05
big_negative = -1e+30

def matmul(a, b):
    return jnp.dot(a, b, precision=highest)

def layer_norm(x, gain):
    centre = x - lax.optimization_barrier(jnp.mean(x, -1, keepdims=True))
    return centre * lax.rsqrt(lax.optimization_barrier(jnp.mean(centre * centre, -1, keepdims=True)) + norm_eps) * gain

def clip_index(lengths, first, amount):
    places = (first + jnp.arange(amount, dtype=jnp.int32)).astype(jnp.int32)
    finish = jnp.cumsum(lengths).astype(jnp.int32)
    clip_id = lax.optimization_barrier(jnp.sum((places[:, None] >= finish[None, :]).astype(jnp.int32), 1)).astype(jnp.int32)
    begins = (finish - lengths).astype(jnp.int32)
    clip_numbers = jnp.arange(lengths.shape[0], dtype=jnp.int32)
    opening = lax.optimization_barrier(jnp.sum(jnp.where(clip_id[:, None] == clip_numbers[None, :], begins[None, :], 0), 1))
    return (clip_id, (places - opening).astype(jnp.int32))

def head_parts(flat, n_head):
    width = HEADS // n_head * HD
    hidden = FF // n_head
    classes = C // n_head
    shapes = ((D, width), (DI, 2 * width), (width, D), (D, 3 * width), (width, D), (D, hidden), (hidden, D), (D, classes))
    pieces = []
    border = 0
    for shape in shapes:
        amount = shape[0] * shape[1]
        pieces.append(flat[..., border:border + amount].reshape(flat.shape[:-1] + shape))
        border += amount
    return pieces

def common_parts(flat):
    border = DQ * D
    query_table = flat[:border].reshape(DQ, D)
    latent_table = flat[border:border + LAT * D].reshape(LAT, D)
    border += LAT * D
    norm_gains = flat[border:border + 4 * D].reshape(4, D)
    return (query_table, latent_table, norm_gains)

def attend_rows(query, keys, values, visible):
    scores = low_back(jnp.einsum('qhd,khd->hqk', query, keys, precision=highest) * HD ** (-0.5))
    scores = jnp.where(visible[None], scores, big_negative)
    shifted = scores - lax.optimization_barrier(jnp.max(scores, -1, keepdims=True))
    weights = jnp.exp(shifted)
    probs = weights / lax.optimization_barrier(jnp.sum(weights, -1, keepdims=True))
    return jnp.einsum('hqk,khd->qhd', probs, values, precision=highest)

def forward(head_flat, common_flat, inputs, queries, lengths, labels, modality, labeled):
    width = HEADS // N_HEAD * HD
    parts = head_parts(low(head_flat).reshape(N_HEAD, P_H), N_HEAD)
    enc_query, enc_keyval, enc_output, self_project, self_output, hidden_in, hidden_out, class_table = parts
    query_table, latent_table, norm_gains = common_parts(low(common_flat))

    def spread(w):
        return jnp.transpose(w, (1, 0, 2)).reshape(w.shape[1], -1)

    def stacked(w):
        return w.reshape(-1, w.shape[2])

    def rounded(x):
        return low_back(low(x))
    clip_id, offset = clip_index(lengths, 0, ROWS)
    z_zero = latent_table[offset % LAT]
    h_zero = low(layer_norm(z_zero, norm_gains[0]))
    x_norm = low(layer_norm(inputs, 1.0))
    q_enc = rounded(matmul(h_zero, spread(enc_query)))
    k_enc = rounded(matmul(x_norm, spread(enc_keyval[:, :, :width])))
    v_enc = rounded(matmul(x_norm, spread(enc_keyval[:, :, width:])))
    every = jnp.ones((L_DEV, I_DEV), bool)

    def window(args):
        return attend_rows(args[0], args[1], args[2], every)
    o_enc = lax.map(jax.checkpoint(window), (q_enc.reshape(N_BLK, L_DEV, HEADS, HD), k_enc.reshape(N_BLK, I_DEV, HEADS, HD), v_enc.reshape(N_BLK, I_DEV, HEADS, HD)))
    o_enc = rounded(o_enc.reshape(ROWS, HEADS * HD))
    z_one = z_zero + low_back(matmul(o_enc, stacked(enc_output)))
    h_one = low(layer_norm(z_one, norm_gains[1]))
    q_self = rounded(matmul(h_one, spread(self_project[:, :, :width]))).reshape(ROWS, HEADS, HD)
    k_self = rounded(matmul(h_one, spread(self_project[:, :, width:2 * width]))).reshape(ROWS, HEADS, HD)
    v_self = rounded(matmul(h_one, spread(self_project[:, :, 2 * width:]))).reshape(ROWS, HEADS, HD)
    block = math.gcd(ROWS, 256)

    def query_block(args):
        return attend_rows(args[0], k_self, v_self, args[1][:, None] == clip_id[None, :])
    o_self = lax.map(jax.checkpoint(query_block), (q_self.reshape(ROWS // block, block, HEADS, HD), clip_id.reshape(ROWS // block, block)))
    o_self = rounded(o_self.reshape(ROWS, HEADS * HD))
    z_two = z_one + low_back(matmul(o_self, stacked(self_output)))
    h_two = low(layer_norm(z_two, norm_gains[2]))
    pre_act = low_back(matmul(h_two, spread(hidden_in)))
    activ = low(jax.nn.gelu(pre_act))
    z_three = z_two + low_back(matmul(activ, stacked(hidden_out)))
    decoded = layer_norm(z_three, norm_gains[3]) + low_back(matmul(queries, query_table))
    logits = low_back(matmul(low(decoded), spread(class_table)))
    top = lax.optimization_barrier(jnp.max(logits, -1, keepdims=True))
    row_lse = top[:, 0] + jnp.log(lax.optimization_barrier(jnp.sum(jnp.exp(logits - top), -1)))
    target = jnp.take_along_axis(logits, labels[:, None], 1)[:, 0]
    member = ((modality[:, None] == jnp.arange(MODES, dtype=jnp.int32)[None, :]) & (labeled[:, None] == 1)).astype(jnp.float32)
    loss_sums = lax.optimization_barrier(jnp.sum((row_lse - target)[:, None] * member, 0))
    label_counts = lax.optimization_barrier(jnp.sum(member, 0))
    loss = jnp.sum(loss_sums / jnp.maximum(label_counts, 1.0))
    return (loss, (loss_sums, label_counts))

def adam_step(weight, first, second, grad):
    first = beta_one * first + (1 - beta_one) * grad
    second = beta_two * second + (1 - beta_two) * grad * grad
    fixed_first = first / (1 - beta_one ** STEP)
    fixed_second = second / (1 - beta_two ** STEP)
    weight = weight - learn_rate * (fixed_first / (jnp.sqrt(fixed_second) + adam_eps) + weight_decay * weight)
    return (weight, first, second, weight.astype(jnp.bfloat16))

def reference(inputs, out_queries, clip_lengths, labels, modality, labeled, head_params, head_first, head_second, common_params, common_first, common_second):

    def objective(head_flat, common_flat):
        return forward(head_flat, common_flat, inputs.astype(jnp.float32), out_queries.astype(jnp.float32), clip_lengths, labels, modality, labeled)
    loss, pull, extras = jax.vjp(objective, head_params, common_params, has_aux=True)
    grad_head, grad_common = pull(jnp.ones_like(loss))
    clip_norm = jnp.sqrt(jnp.sum(grad_head * grad_head) + jnp.sum(grad_common * grad_common))
    factor = jnp.minimum(1.0, clip_limit / clip_norm)
    head_new = adam_step(head_params, head_first, head_second, grad_head * factor)
    common_new = adam_step(common_params, common_first, common_second, grad_common * factor)
    return (head_new[0], head_new[1], head_new[2], head_new[3], common_new[0], common_new[1], common_new[2], common_new[3], extras[0], extras[1], clip_norm)
```

```python
import functools

import jax
import jax.numpy as jnp
from jax import lax
from jax.experimental import pallas as pl
from jax.experimental.pallas import tpu as pltpu
from jax.sharding import PartitionSpec as P

D = 512
HEADS = 8
HD = 64
FF = 2048
DI = 704
DQ = 1026
C = 704
LAT = 784
MODES = 3
STEP = 10
LANES = 128
TILE = 16

norm_eps = 1e-05
learn_rate = 0.1
beta_one = 0.9
beta_two = 0.999
adam_eps = 1e-08
weight_decay = 0.01
clip_limit = 0.05
big_negative = -1e30
low = jnp.bfloat16
MESH = pl.DeviceIdType.MESH
MIB = 1 << 20


def round_up(n, unit):
    return -(-n // unit) * unit


def grid_of(n_blk, n_head):
    cores = 2 if n_head % 2 == 0 else 1
    x = n_head // cores
    y = x if n_blk % x == 0 else 1
    return (n_blk // y, y, x, cores)


def my_place(dims):
    blk, head = lax.axis_index("blk"), lax.axis_index("head")
    return (blk // dims[1], lax.rem(blk, dims[1]), head // dims[3], lax.rem(head, dims[3]))


def shifted(dims, me, offset, sign):
    return tuple(
        m if o == 0 else lax.rem(m + (o if sign > 0 else n - o), n)
        for m, o, n in zip(me, offset, dims)
    )


def blk_of(dims, place):
    return place[0] * dims[1] + place[1]


def head_of(dims, place):
    return place[2] * dims[3] + place[3]


def device_of(dims, place):
    return {"blk": blk_of(dims, place), "head": head_of(dims, place)}


def along(axis, d):
    return tuple(d if a == axis else 0 for a in range(4))


def greet(dims, me, offsets):
    barrier = pltpu.get_barrier_semaphore()
    for offset in offsets:
        pl.semaphore_signal(
            barrier,
            inc=1,
            device_id=device_of(dims, shifted(dims, me, offset, 1)),
            device_id_type=MESH,
        )
    pl.semaphore_wait(barrier, len(offsets))


def axis_peers(dims, axes):
    return [along(axis, d) for axis in axes for d in range(1, dims[axis])]


def remote(src, dst, send_sem, recv_sem, place, dims):
    return pltpu.make_async_remote_copy(
        src_ref=src,
        dst_ref=dst,
        send_sem=send_sem,
        recv_sem=recv_sem,
        device_id=device_of(dims, place),
        device_id_type=MESH,
    )


def gather_plan(dims, parts):
    plan = []
    for position in range(4):
        for p, (first, rows, order) in enumerate(parts):
            axis = order[position]
            done = order[:position]
            offsets = [(0, 0, 0, 0)]
            for a in done:
                offsets = [
                    tuple(d if i == a else o[i] for i in range(4))
                    for d in range(dims[a])
                    for o in offsets
                ]
            for d in range(1, dims[axis]):
                for o in offsets:
                    plan.append((p, tuple(d if i == axis else o[i] for i in range(4)), position))
    return plan


def gather_kernel(dims, parts, src, out, send_sem, recv_sem, own_sem):
    me = my_place(dims)
    plan = gather_plan(dims, parts)
    number = {(p, offset): i for i, (p, offset, position) in enumerate(plan)}
    axes = [a for a in range(4) if dims[a] > 1]
    greet(dims, me, axis_peers(dims, axes))
    own = pltpu.make_async_copy(src, out.at[blk_of(dims, me), head_of(dims, me)], own_sem)
    own.start()
    started = []

    def block(p, offset):
        place = shifted(dims, me, offset, -1)
        first, rows, order = parts[p]
        return out.at[blk_of(dims, place), head_of(dims, place), pl.ds(first, rows)]

    def forward(p, offset, position):
        first, rows, order = parts[p]
        source = src.at[pl.ds(first, rows)] if position < 0 else block(p, offset)
        for axis in order[position + 1 :]:
            for d in range(1, dims[axis]):
                i = number[(p, tuple(d if a == axis else offset[a] for a in range(4)))]
                copy = remote(
                    source,
                    block(p, offset),
                    send_sem.at[i],
                    recv_sem.at[i],
                    shifted(dims, me, along(axis, d), 1),
                    dims,
                )
                copy.start()
                started.append(copy)

    for p in range(len(parts)):
        forward(p, (0, 0, 0, 0), -1)
    for i, (p, offset, position) in enumerate(plan):
        landed = block(p, offset)
        axis = parts[p][2][position]
        remote(
            landed,
            landed,
            send_sem.at[i],
            recv_sem.at[i],
            shifted(dims, me, along(axis, offset[axis]), -1),
            dims,
        ).wait_recv()
        forward(p, offset, position)
    for copy in started:
        copy.wait_send()
    own.wait()


def gather_all(dims, shard, collective_id):
    rows = shard.shape[0]
    first = rows // 2 // TILE * TILE
    parts = ((0, first, (0, 1, 2, 3)), (first, rows - first, (0, 2, 1, 3)))
    count = len(gather_plan(dims, parts))
    z, y, x, cores = dims
    return pl.pallas_call(
        functools.partial(gather_kernel, dims, parts),
        out_shape=jax.ShapeDtypeStruct((z * y, x * cores) + shard.shape, shard.dtype),
        in_specs=[pl.BlockSpec(memory_space=pl.ANY)],
        out_specs=pl.BlockSpec(memory_space=pl.ANY),
        scratch_shapes=[
            pltpu.SemaphoreType.DMA((count,)),
            pltpu.SemaphoreType.DMA((count,)),
            pltpu.SemaphoreType.DMA(()),
        ],
        compiler_params=pltpu.CompilerParams(collective_id=collective_id, has_side_effects=True),
        name="gather_weights",
    )(shard)


def reduce_plan(dims, order):
    stages = []
    for position, axis in enumerate(order):
        rest = order[position + 1 :]
        offsets = [(0, 0, 0, 0)]
        for a in reversed(rest):
            offsets = [
                tuple(d if i == a else o[i] for i in range(4))
                for d in list(range(1, dims[a])) + [0]
                for o in offsets
            ]
        stages.append((axis, offsets))
    return stages


def reduce_kernel(dims, parts, chunk, src, out, *scratch):
    me = my_place(dims)
    places = len(parts) * 4
    buffers, send_sem, recv_sem = scratch[:places], scratch[places], scratch[places + 1]
    axes = [a for a in range(4) if dims[a] > 1]
    greet(dims, me, axis_peers(dims, axes))
    started = []
    numbers = [0]
    pending = {}

    def source(p, position, offset):
        first, rows, order = parts[p]
        if position == 0:
            place = shifted(dims, me, offset, 1)
            return src.at[blk_of(dims, place), head_of(dims, place), pl.ds(first, rows)]
        k = stages[p][position - 1][1].index(offset)
        return buffers[p * 4 + position - 1].at[k, 0]

    stages = [reduce_plan(dims, order) for first, rows, order in parts]

    def send(p, position, k, d):
        axis, offsets = stages[p][position]
        i = numbers[0]
        numbers[0] += 1
        there = tuple(d if a == axis else offsets[k][a] for a in range(4))
        copy = remote(
            source(p, position, there),
            buffers[p * 4 + position].at[k, d - 1],
            send_sem.at[i],
            recv_sem.at[i],
            shifted(dims, me, along(axis, d), 1),
            dims,
        )
        copy.start()
        started.append(copy)
        pending[(p, position, k, d)] = copy

    def add(p, position, k):
        first, rows, order = parts[p]
        axis, offsets = stages[p][position]
        for d in range(1, dims[axis]):
            pending[(p, position, k, d)].wait_recv()
        mine = source(p, position, offsets[k])
        arrived = buffers[p * 4 + position]
        step = chunk(rows)
        last = position == 3

        @pl.loop(0, rows // step)
        def some_rows(n):
            at = pl.ds(pl.multiple_of(n * step, step), step)
            total = mine[at].astype(jnp.float32)
            for d in range(1, dims[axis]):
                total = total + arrived[k, d - 1, at].astype(jnp.float32)
            if last:
                out[pl.ds(pl.multiple_of(first + n * step, TILE), step)] = total
            else:
                arrived[k, 0, at] = total.astype(low)

    for position in range(4):
        for k in range(len(stages[0][position][1])):
            for p in range(len(parts)):
                if position == 0:
                    for d in range(1, dims[stages[p][0][0]]):
                        send(p, 0, k, d)
        for k in range(len(stages[0][position][1])):
            for p in range(len(parts)):
                add(p, position, k)
                if position < 3:
                    axis, offsets = stages[p][position + 1]
                    offset = stages[p][position][1][k]
                    rest = tuple(0 if a == axis else offset[a] for a in range(4))
                    if offset[axis]:
                        send(p, position + 1, offsets.index(rest), offset[axis])
    for copy in started:
        copy.wait_send()


def row_chunk(rows):
    for count in (4, 3, 2):
        if rows % (count * TILE) == 0:
            return rows // count
    return rows


def reduce_all(dims, blocks, collective_id):
    rows = blocks.shape[2]
    first = rows // 2 // TILE * TILE
    parts = ((0, first, (3, 2, 1, 0)), (first, rows - first, (3, 1, 2, 0)))
    scratch = []
    count = 0
    for start, amount, order in parts:
        for axis, offsets in reduce_plan(dims, order):
            others = max(dims[axis] - 1, 1)
            count += len(offsets) * (dims[axis] - 1)
            scratch.append(pltpu.VMEM((len(offsets), others, amount, LANES), low))
    return pl.pallas_call(
        functools.partial(reduce_kernel, dims, parts, row_chunk),
        out_shape=jax.ShapeDtypeStruct((rows, LANES), jnp.float32),
        in_specs=[pl.BlockSpec(memory_space=pltpu.VMEM)],
        out_specs=pl.BlockSpec(memory_space=pltpu.VMEM),
        scratch_shapes=scratch
        + [pltpu.SemaphoreType.DMA((count,)), pltpu.SemaphoreType.DMA((count,))],
        compiler_params=pltpu.CompilerParams(
            collective_id=collective_id, has_side_effects=True, vmem_limit_bytes=56 * MIB
        ),
        name="reduce_gradients",
    )(blocks)


def spread_kernel(dims, q_in, kv_in, q_out, kv_out, send_sem, recv_sem, own_sem):
    z, y, x, cores = dims
    me = my_place(dims)
    heads = x * cores
    my_blk, my_head = blk_of(dims, me), head_of(dims, me)
    across = [(0, 0, a, c) for a in range(x) for c in range(cores) if (a, c) != (0, 0)]
    across.sort(key=lambda o: (o[2] == 0, o[3]))
    ups = [along(0, d) for d in range(1, z)]
    sides = [along(1, d) for d in range(1, y)]
    greet(dims, me, across + ups + sides)
    own_q = pltpu.make_async_copy(q_in.at[my_head], q_out.at[my_head], own_sem.at[0])
    own_kv = pltpu.make_async_copy(kv_in.at[my_head], kv_out.at[my_blk, my_head], own_sem.at[1])
    own_kv.start()
    own_q.start()
    started = []
    count = [0]

    def push(src, dst, place):
        i = count[0]
        count[0] += 1
        copy = remote(src, dst, send_sem.at[i], recv_sem.at[i], place, dims)
        copy.start()
        started.append(copy)
        return copy

    landed_kv = []
    for o in across:
        place = shifted(dims, me, o, 1)
        landed_kv.append(push(kv_in.at[head_of(dims, place)], kv_out.at[my_blk, my_head], place))
    landed_q = []
    for o in across:
        place = shifted(dims, me, o, 1)
        landed_q.append(push(q_in.at[head_of(dims, place)], q_out.at[my_head], place))
    pieces = [(0, 0, 0, 0)] + across
    up_copies = {}
    side_copies = {}

    def kv_block(place_blk, offset):
        place = shifted(dims, me, offset, -1)
        return kv_out.at[place_blk, head_of(dims, place)]

    def spread_own(n):
        block = kv_block(my_blk, pieces[n])
        for o in ups:
            up_copies[(n, o)] = push(block, block, shifted(dims, me, o, 1))
        for o in sides:
            side_copies[(n, along(0, 0), o)] = push(block, block, shifted(dims, me, o, 1))

    own_kv.wait()
    spread_own(0)
    order = sorted(range(1, len(pieces)), key=lambda n: (pieces[n][2] != 0, pieces[n][3]))
    for n in order:
        landed_kv[n - 1].wait_recv()
        spread_own(n)
    for u in ups:
        for n in [0] + order:
            up_copies[(n, u)].wait_recv()
            block = kv_block(blk_of(dims, shifted(dims, me, u, -1)), pieces[n])
            for o in sides:
                side_copies[(n, u, o)] = push(block, block, shifted(dims, me, o, 1))
    for copy in landed_q:
        copy.wait_recv()
    for copy in side_copies.values():
        copy.wait_recv()
    for copy in started:
        copy.wait_send()
    own_q.wait()


def spread_rows(dims, q, kv, collective_id):
    z, y, x, cores = dims
    heads = x * cores
    count = 2 * (heads - 1) + heads * (z - 1 + z * (y - 1))
    return pl.pallas_call(
        functools.partial(spread_kernel, dims),
        out_shape=(
            jax.ShapeDtypeStruct(q.shape, low),
            jax.ShapeDtypeStruct((z * y,) + kv.shape, low),
        ),
        in_specs=[pl.BlockSpec(memory_space=pl.ANY)] * 2,
        out_specs=[pl.BlockSpec(memory_space=pl.ANY)] * 2,
        scratch_shapes=[
            pltpu.SemaphoreType.DMA((count,)),
            pltpu.SemaphoreType.DMA((count,)),
            pltpu.SemaphoreType.DMA((2,)),
        ],
        compiler_params=pltpu.CompilerParams(collective_id=collective_id, has_side_effects=True),
        name="spread_rows",
    )(q, kv)


def swap_kernel(dims, src, out, send_sem, recv_sem, own_sem):
    z, y, x, cores = dims
    me = my_place(dims)
    my_head = head_of(dims, me)
    across = [(0, 0, a, c) for a in range(x) for c in range(cores) if (a, c) != (0, 0)]
    greet(dims, me, across)
    copies = []
    for i, o in enumerate(across):
        place = shifted(dims, me, o, 1)
        copy = remote(
            src.at[head_of(dims, place)], out.at[my_head], send_sem.at[i], recv_sem.at[i], place, dims
        )
        copy.start()
        copies.append(copy)
    own = pltpu.make_async_copy(src.at[my_head], out.at[my_head], own_sem)
    own.start()
    for copy in copies:
        copy.wait_recv()
    for copy in copies:
        copy.wait_send()
    own.wait()


def swap_heads(dims, blocks, collective_id):
    count = dims[2] * dims[3] - 1
    return pl.pallas_call(
        functools.partial(swap_kernel, dims),
        out_shape=jax.ShapeDtypeStruct(blocks.shape, blocks.dtype),
        in_specs=[pl.BlockSpec(memory_space=pl.ANY)],
        out_specs=pl.BlockSpec(memory_space=pl.ANY),
        scratch_shapes=[
            pltpu.SemaphoreType.DMA((count,)),
            pltpu.SemaphoreType.DMA((count,)),
            pltpu.SemaphoreType.DMA(()),
        ],
        compiler_params=pltpu.CompilerParams(collective_id=collective_id, has_side_effects=True),
        name="swap_heads",
    )(blocks)


def collect_kernel(dims, src, out, side_buf, up_buf, send_sem, recv_sem):
    z, y, x, cores = dims
    me = my_place(dims)
    greet(dims, me, axis_peers(dims, (0, 1)))
    started = []
    rows = src.shape[1]
    step = 256

    def push(s, dst, place):
        i = len(started)
        copy = remote(s, dst, send_sem.at[i], recv_sem.at[i], place, dims)
        copy.start()
        started.append(copy)
        return copy

    side = {}
    for u in list(range(1, z)) + [0]:
        for d in range(1, y):
            place = shifted(dims, me, (u, d, 0, 0), 1)
            side[(u, d)] = push(
                src.at[blk_of(dims, place)], side_buf.at[u, d - 1], shifted(dims, me, along(1, d), 1)
            )
    up = {}
    for u in list(range(1, z)) + [0]:
        for d in range(1, y):
            side[(u, d)].wait_recv()
        mine = src.at[blk_of(dims, shifted(dims, me, along(0, u), 1))]

        @pl.loop(0, rows // step)
        def some_rows(n):
            at = pl.ds(pl.multiple_of(n * step, step), step)
            total = mine[at].astype(jnp.float32)
            for d in range(1, y):
                total = total + side_buf[u, d - 1, at].astype(jnp.float32)
            side_buf[u, 0, at] = total.astype(low)

        if u:
            up[u] = push(
                side_buf.at[u, 0], up_buf.at[u - 1], shifted(dims, me, along(0, u), 1)
            )
    for u in range(1, z):
        up[u].wait_recv()

    @pl.loop(0, rows // step)
    def last_rows(n):
        at = pl.ds(pl.multiple_of(n * step, step), step)
        total = side_buf[0, 0, at].astype(jnp.float32)
        for u in range(1, z):
            total = total + up_buf[u - 1, at].astype(jnp.float32)
        out[at] = total.astype(low)

    for copy in started:
        copy.wait_send()


def collect_rows(dims, parts, collective_id):
    z, y, x, cores = dims
    shape = parts.shape[1:]
    count = z * (y - 1) + z - 1
    return pl.pallas_call(
        functools.partial(collect_kernel, dims),
        out_shape=jax.ShapeDtypeStruct(shape, low),
        in_specs=[pl.BlockSpec(memory_space=pltpu.VMEM)],
        out_specs=pl.BlockSpec(memory_space=pltpu.VMEM),
        scratch_shapes=[
            pltpu.VMEM((z, max(y - 1, 1)) + shape, low),
            pltpu.VMEM((max(z - 1, 1),) + shape, low),
            pltpu.SemaphoreType.DMA((count,)),
            pltpu.SemaphoreType.DMA((count,)),
        ],
        compiler_params=pltpu.CompilerParams(
            collective_id=collective_id, has_side_effects=True, vmem_limit_bytes=48 * MIB
        ),
        name="collect_rows",
    )(parts)


def contract_first(a, b):
    return lax.dot_general(a, b, (((0,), (0,)), ((), ())), preferred_element_type=jnp.float32)


def product(a, b):
    return jnp.dot(a, b, preferred_element_type=jnp.float32)


def against(a, b):
    return lax.dot_general(a, b, (((1,), (1,)), ((), ())), preferred_element_type=jnp.float32)


def clip_borders(bounds, where):
    clips = bounds.shape[1]
    opening = jnp.zeros(where.shape, jnp.int32)
    ending = jnp.full(where.shape, 1 << 30, jnp.int32)
    for clip in range(clips):
        here = where == HD + clip
        opening = jnp.where(here, bounds[0, clip], opening)
        ending = jnp.where(here, bounds[1, clip], ending)
    return opening, ending


def extend_keys(bounds, heads, rows_at_once, kv, keys, values):
    width = heads * HD
    clips = bounds.shape[1]
    lane = lax.broadcasted_iota(jnp.int32, (1, LANES), 1)
    opening, ending = clip_borders(bounds, lane)
    ones = jnp.where((lane >= HD + clips) & (lane < HD + clips + 3), 1.0, 0.0)
    value_tail = jnp.where((lane >= HD) & (lane < HD + 3), 1.0, 0.0) + jnp.zeros(
        (rows_at_once, LANES), jnp.float32
    )

    @pl.loop(0, kv.shape[0] // rows_at_once)
    def some_rows(n):
        first = pl.multiple_of(n * rows_at_once, rows_at_once)
        at = pl.ds(first, rows_at_once)
        row = first + lax.broadcasted_iota(jnp.int32, (rows_at_once, LANES), 0)
        tail = jnp.where((row >= opening) & (row < ending), ones, big_negative)
        block = kv[at, :].astype(jnp.float32)
        for a in range(heads):
            for first_column, target, end in ((0, keys, tail), (width, values, value_tail)):
                columns = block[:, first_column + a * HD : first_column + (a + 1) * HD]
                target[a, at, :] = jnp.concatenate([columns, end[:, HD:]], 1).astype(low)


def extend_queries(bounds, first_row, heads, q_t, a, extra):
    clips = bounds.shape[1]
    amount = q_t.shape[1]
    place = HD + lax.broadcasted_iota(jnp.int32, (HD, 1), 0)
    opening, ending = clip_borders(bounds, place)
    row = first_row + lax.broadcasted_iota(jnp.int32, (1, amount), 1)
    is_clip = place < HD + clips
    tail = jnp.where(is_clip & (row >= opening) & (row < ending), 1.0, 0.0)
    if extra is not None:
        tail = tail + in_three(place - HD - clips, -extra)
    return jnp.concatenate([q_t[a * HD : (a + 1) * HD] * HD ** (-0.5), tail], 0).astype(low)


def in_three(place, value):
    top = value.astype(low).astype(jnp.float32)
    middle = (value - top).astype(low).astype(jnp.float32)
    bottom = value - top - middle
    return (
        jnp.where(place == 0, top, 0.0)
        + jnp.where(place == 1, middle, 0.0)
        + jnp.where(place == 2, bottom, 0.0)
    )


def attend_kernel(heads, key_step, query_step, bounds, q, kv, out, lse, out_t, keys, values, queries, top, accum):
    first_row = lax.axis_index("blk") * q.shape[0]
    amount, total_keys = q.shape[0], kv.shape[0]
    extend_keys(bounds, heads, key_step, kv, keys, values)
    q_t = q[...].astype(jnp.float32).T
    for a in range(heads):
        queries[a] = extend_queries(bounds, first_row, heads, q_t, a, None)

    @pl.loop(0, amount // query_step)
    def query_block(n):
        at = pl.ds(pl.multiple_of(n * query_step, query_step), query_step)
        top[...] = jnp.full(top.shape, -1e38, jnp.float32)
        accum[...] = jnp.zeros(accum.shape, jnp.float32)

        @pl.loop(0, total_keys // key_step)
        def key_block(k):
            rows = pl.ds(pl.multiple_of(k * key_step, key_step), key_step)
            for a in range(heads):
                scores = product(keys[a, rows, :], queries[a, :, at])
                old = top[a : a + 1, :]
                new = jnp.maximum(old, jnp.max(scores, 0, keepdims=True))
                probs = jnp.exp(scores - new).astype(low)
                top[a : a + 1, :] = new
                accum[a] = accum[a] * jnp.exp(old - new) + contract_first(values[a, rows, :], probs)

        for a in range(heads):
            total = accum[a, HD : HD + 1, :]
            out_t[a * HD : (a + 1) * HD, at] = accum[a, :HD, :] / total
            lse[a : a + 1, at] = top[a : a + 1, :] + jnp.log(total)

    out[...] = out_t[...].T.astype(low)


def attend(bounds, q, kv, heads):
    amount, width = q.shape
    total_keys = kv.shape[0]
    key_step, query_step = 1024, 256
    vmem = pl.BlockSpec(memory_space=pltpu.VMEM)
    return pl.pallas_call(
        functools.partial(attend_kernel, heads, key_step, query_step),
        out_shape=(
            jax.ShapeDtypeStruct((amount, width), low),
            jax.ShapeDtypeStruct((heads, amount), jnp.float32),
            jax.ShapeDtypeStruct((width, amount), jnp.float32),
        ),
        in_specs=[pl.BlockSpec(memory_space=pltpu.SMEM), vmem, vmem],
        out_specs=[vmem] * 3,
        scratch_shapes=[
            pltpu.VMEM((heads, total_keys, LANES), low),
            pltpu.VMEM((heads, total_keys, LANES), low),
            pltpu.VMEM((heads, LANES, amount), low),
            pltpu.VMEM((heads, query_step), jnp.float32),
            pltpu.VMEM((heads, LANES, query_step), jnp.float32),
        ],
        compiler_params=pltpu.CompilerParams(vmem_limit_bytes=56 * MIB),
        name="attend",
    )(bounds, q, kv)


def attend_back_kernel(
    heads, key_step, bounds, q, kv, dout, out_t, lse, d_q, d_kv, keys, values, queries, douts, d_q_t, q_rows, do_rows
):
    first_row = lax.axis_index("blk") * q.shape[0]
    amount, total_keys = q.shape[0], kv.shape[0]
    width = heads * HD
    extend_keys(bounds, heads, 1024, kv, keys, values)
    q_low = q[...].astype(jnp.float32)
    do_low = dout[...].astype(jnp.float32)
    q_t, do_t = q_low.T, do_low.T
    place = lax.broadcasted_iota(jnp.int32, (HD, 1), 0)
    lane = lax.broadcasted_iota(jnp.int32, (1, width), 1)
    for a in range(heads):
        mine = slice(a * HD, (a + 1) * HD)
        queries[a] = extend_queries(bounds, first_row, heads, q_t, a, lse[a : a + 1, :])
        delta = jnp.sum(do_t[mine] * out_t[mine, :], 0, keepdims=True)
        douts[a] = jnp.concatenate([do_t[mine], in_three(place, -delta)], 0).astype(low)
        here = (lane >= a * HD) & (lane < (a + 1) * HD)
        q_rows[a] = jnp.where(here, q_low * HD ** (-0.5), 0.0).astype(low)
        do_rows[a] = jnp.where(here, do_low, 0.0).astype(low)
    d_q_t[...] = jnp.zeros(d_q_t.shape, jnp.float32)

    @pl.loop(0, total_keys // key_step)
    def key_block(k):
        rows = pl.ds(pl.multiple_of(k * key_step, key_step), key_step)
        d_key = jnp.zeros((key_step, width), jnp.float32)
        d_value = jnp.zeros((key_step, width), jnp.float32)
        for a in range(heads):
            probs = jnp.exp(product(keys[a, rows, :], queries[a]))
            d_probs = product(values[a, rows, :], douts[a])
            d_scores = (probs * d_probs).astype(low)
            d_value = d_value + product(probs.astype(low), do_rows[a])
            d_key = d_key + product(d_scores, q_rows[a])
            d_q_t[a] = d_q_t[a] + contract_first(keys[a, rows, :], d_scores)
        d_kv[rows, :] = jnp.concatenate([d_key, d_value], 1).astype(low)

    whole = jnp.concatenate([d_q_t[a, :HD, :] for a in range(heads)], 0) * HD ** (-0.5)
    d_q[...] = whole.T.astype(low)


def attend_back(bounds, q, kv, dout, out_t, lse, heads):
    amount, width = q.shape
    total_keys = kv.shape[0]
    key_step = 256
    vmem = pl.BlockSpec(memory_space=pltpu.VMEM)
    return pl.pallas_call(
        functools.partial(attend_back_kernel, heads, key_step),
        out_shape=(
            jax.ShapeDtypeStruct((amount, width), low),
            jax.ShapeDtypeStruct((total_keys, 2 * width), low),
        ),
        in_specs=[pl.BlockSpec(memory_space=pltpu.SMEM)] + [vmem] * 5,
        out_specs=[vmem] * 2,
        scratch_shapes=[
            pltpu.VMEM((heads, total_keys, LANES), low),
            pltpu.VMEM((heads, total_keys, LANES), low),
            pltpu.VMEM((heads, LANES, amount), low),
            pltpu.VMEM((heads, LANES, amount), low),
            pltpu.VMEM((heads, LANES, amount), jnp.float32),
            pltpu.VMEM((heads, amount, width), low),
            pltpu.VMEM((heads, amount, width), low),
        ],
        compiler_params=pltpu.CompilerParams(vmem_limit_bytes=56 * MIB),
        name="attend_back",
    )(bounds, q, kv, dout, out_t, lse)


def layer_norm(x, gain):
    centre = x - jnp.mean(x, -1, keepdims=True)
    return centre * lax.rsqrt(jnp.mean(centre * centre, -1, keepdims=True) + norm_eps) * gain


def norm_pullback(x, gain, grad):
    unused, pull = jax.vjp(layer_norm, x, gain)
    return pull(grad)


def inner(a, b):
    return lax.dot_general(a, b, (((0,), (0,)), ((), ())), preferred_element_type=jnp.float32)


def part_shapes(n_head):
    width = HEADS // n_head * HD
    hidden = FF // n_head
    classes = C // n_head
    return (
        (D, width),
        (DI, 2 * width),
        (width, D),
        (D, 3 * width),
        (width, D),
        (D, hidden),
        (hidden, D),
        (D, classes),
    )


def adam_step(weight, first, second, grad):
    first = beta_one * first + (1 - beta_one) * grad
    second = beta_two * second + (1 - beta_two) * grad * grad
    fixed_first = first / (1 - beta_one**STEP)
    fixed_second = second / (1 - beta_two**STEP)
    weight = weight - learn_rate * (
        fixed_first / (jnp.sqrt(fixed_second) + adam_eps) + weight_decay * weight
    )
    return (weight, first, second, weight.astype(low))


def per_device(
    inputs,
    out_queries,
    clip_lengths,
    labels,
    modality,
    labeled,
    head_params,
    head_first,
    head_second,
    common_params,
    common_first,
    common_second,
):
    n_head, n_blk = lax.axis_size("head"), lax.axis_size("blk")
    dims = grid_of(n_blk, n_head)
    head_rank, blk_rank = lax.axis_index("head"), lax.axis_index("blk")
    blk_rows = labels.shape[0]
    rows = blk_rows // n_head
    heads_here = HEADS // n_head
    width = heads_here * HD
    n_h, n_c = head_params.shape[0], common_params.shape[0]
    head_rows = round_up(-(-n_h // LANES), TILE)
    piece_rows = round_up(-(-(-(-n_c // LANES)) // n_head), TILE)

    def mine(x):
        return lax.dynamic_slice_in_dim(x, head_rank * rows, rows, 0)

    head_low = jnp.pad(head_params.astype(low), (0, head_rows * LANES - n_h)).reshape(head_rows, LANES)
    common_low = jnp.pad(common_params.astype(low), (0, n_head * piece_rows * LANES - n_c))
    common_low = lax.dynamic_slice_in_dim(
        common_low.reshape(n_head * piece_rows, LANES), head_rank * piece_rows, piece_rows, 0
    )
    everything = gather_all(dims, jnp.concatenate([head_low, common_low], 0), 0)
    head_flat = [
        everything[:, g, :head_rows].reshape(n_blk, head_rows * LANES)[:, :n_h].reshape(-1)
        for g in range(n_head)
    ]
    common_flat = everything[:, :, head_rows:].reshape(n_blk, n_head * piece_rows * LANES)[:, :n_c]
    common_flat = common_flat.reshape(-1)
    shapes = part_shapes(n_head)
    parts = []
    border = 0
    for shape in shapes:
        amount = shape[0] * shape[1]
        parts.append([flat[border : border + amount].reshape(shape) for flat in head_flat])
        border += amount
    enc_query = jnp.concatenate(parts[0], 1)
    enc_key = jnp.concatenate([w[:, :width] for w in parts[1]], 1)
    enc_value = jnp.concatenate([w[:, width:] for w in parts[1]], 1)
    enc_output = jnp.concatenate(parts[2], 0)
    self_project = jnp.concatenate(parts[3], 1)
    self_output = jnp.concatenate(parts[4], 0)
    hidden_in = jnp.concatenate(parts[5], 1)
    hidden_out = jnp.concatenate(parts[6], 0)
    class_table = jnp.concatenate(parts[7], 1)
    query_table = common_flat[: DQ * D].reshape(DQ, D)
    latent_table = common_flat[DQ * D : (DQ + LAT) * D].reshape(LAT, D)
    norm_gains = common_flat[(DQ + LAT) * D :].reshape(4, D).astype(jnp.float32)

    finish = jnp.cumsum(clip_lengths)
    bounds = jnp.stack([finish - clip_lengths, finish])
    places = blk_rank * blk_rows + head_rank * rows + jnp.arange(rows, dtype=jnp.int32)
    inside = (places[:, None] >= bounds[0][None]) & (places[:, None] < bounds[1][None])
    offset = places - jnp.sum(jnp.where(inside, bounds[0][None], 0), 1)
    latent_rows = offset % LAT
    picked = (latent_rows[:, None] == jnp.arange(LAT, dtype=jnp.int32)[None]).astype(low)
    labels, modality, labeled = mine(labels), mine(modality), mine(labeled)
    out_queries = mine(out_queries)

    def split(x):
        return x.reshape(x.shape[0], HEADS, HD)

    z_zero = product(picked, latent_table)
    h_zero = layer_norm(z_zero, norm_gains[0]).astype(low)
    x_norm = layer_norm(inputs.astype(jnp.float32), 1.0).astype(low)
    q_enc = split(product(h_zero, enc_query).astype(low))
    k_enc = split(product(x_norm, enc_key).astype(low))
    v_enc = split(product(x_norm, enc_value).astype(low))

    def scores_of(q, k):
        return jnp.einsum("qhd,khd->hqk", q, k, preferred_element_type=jnp.float32) * HD ** (-0.5)

    p_enc = jax.nn.softmax(scores_of(q_enc, k_enc), axis=-1)
    o_enc = jnp.einsum("hqk,khd->qhd", p_enc.astype(low), v_enc, preferred_element_type=jnp.float32)
    o_enc_low = o_enc.reshape(rows, HEADS * HD).astype(low)
    z_one = z_zero + product(o_enc_low, enc_output)
    h_one = layer_norm(z_one, norm_gains[1]).astype(low)
    projected = product(h_one, self_project).astype(low).reshape(rows, n_head, 3 * width)
    projected = projected.transpose(1, 0, 2)
    q_self, kv_self = spread_rows(dims, projected[:, :, :width], projected[:, :, width:], 1)
    q_self = q_self.reshape(blk_rows, width)
    kv_self = kv_self.reshape(n_blk * blk_rows, 2 * width)
    out_self, lse_self, out_self_t = attend(bounds, q_self, kv_self, heads_here)
    o_self_low = swap_heads(dims, out_self.reshape(n_head, rows, width), 2)
    o_self_low = o_self_low.transpose(1, 0, 2).reshape(rows, HEADS * HD)
    z_two = z_one + product(o_self_low, self_output)
    h_two = layer_norm(z_two, norm_gains[2]).astype(low)
    pre_act = product(h_two, hidden_in)
    activ = jax.nn.gelu(pre_act).astype(low)
    z_three = z_two + product(activ, hidden_out)
    decoded_low = (layer_norm(z_three, norm_gains[3]) + product(out_queries, query_table)).astype(low)
    logits = product(decoded_low, class_table)
    is_target = (labels[:, None] == jnp.arange(C, dtype=jnp.int32)[None, :]).astype(jnp.float32)
    row_top = jnp.max(logits, -1, keepdims=True)
    row_lse = row_top + jnp.log(jnp.sum(jnp.exp(logits - row_top), -1, keepdims=True))
    target = jnp.sum(is_target * logits, -1, keepdims=True)
    member = (
        (modality[:, None] == jnp.arange(MODES, dtype=jnp.int32)[None, :]) & (labeled[:, None] == 1)
    ).astype(jnp.float32)
    label_counts = lax.psum(jnp.sum(member, 0), ("blk", "head"))
    loss_sums = lax.psum(jnp.sum((row_lse - target) * member, 0), ("blk", "head"))

    row_weight = jnp.sum(member / jnp.maximum(label_counts, 1.0)[None, :], 1, keepdims=True)
    dlogits = (row_weight * (jnp.exp(logits - row_lse) - is_target)).astype(low)
    class_grad = inner(decoded_low, dlogits)
    d_decoded = against(dlogits, class_table)
    query_grad = inner(out_queries, d_decoded.astype(low))
    d_three, gain_three = norm_pullback(z_three, norm_gains[3], d_decoded)
    d_branch = d_three.astype(low)
    out_grad = inner(activ, d_branch)
    unused, gelu_pull = jax.vjp(jax.nn.gelu, pre_act)
    d_pre = gelu_pull(against(d_branch, hidden_out))[0].astype(low)
    in_grad = inner(h_two, d_pre)
    d_middle, gain_two = norm_pullback(z_two, norm_gains[2], against(d_pre, hidden_in))
    d_two = d_three + d_middle
    d_branch = d_two.astype(low)
    self_out_grad = inner(o_self_low, d_branch)
    dout_self = against(d_branch, self_output).astype(low)
    dout_self = swap_heads(
        dims, dout_self.reshape(rows, n_head, width).transpose(1, 0, 2), 3
    ).reshape(blk_rows, width)
    d_q, d_kv = attend_back(bounds, q_self, kv_self, dout_self, out_self_t, lse_self, heads_here)
    d_kv = collect_rows(dims, d_kv.reshape(n_blk, blk_rows, 2 * width), 4)
    d_projected = swap_heads(
        dims, jnp.concatenate([d_q, d_kv], 1).reshape(n_head, rows, 3 * width), 5
    )
    d_projected = d_projected.transpose(1, 0, 2).reshape(rows, n_head * 3 * width)
    project_grad = inner(h_one, d_projected)
    d_middle, gain_one = norm_pullback(z_one, norm_gains[1], against(d_projected, self_project))
    d_one = d_two + d_middle
    d_branch = d_one.astype(low)
    enc_out_grad = inner(o_enc_low, d_branch)
    dout_enc = split(against(d_branch, enc_output).astype(low))
    dp_enc = jnp.einsum("qhd,khd->hqk", dout_enc, v_enc, preferred_element_type=jnp.float32)
    delta_enc = jnp.einsum("qhd,qhd->hq", dout_enc.astype(jnp.float32), o_enc)
    ds_enc = (p_enc * (dp_enc - delta_enc[..., None])).astype(low)
    d_q_enc = jnp.einsum("hqk,khd->qhd", ds_enc, k_enc, preferred_element_type=jnp.float32) * HD ** (-0.5)
    d_k_enc = jnp.einsum("hqk,qhd->khd", ds_enc, q_enc, preferred_element_type=jnp.float32) * HD ** (-0.5)
    d_v_enc = jnp.einsum(
        "hqk,qhd->khd", p_enc.astype(low), dout_enc, preferred_element_type=jnp.float32
    )
    d_q_enc, d_k_enc, d_v_enc = (x.reshape(-1, HEADS * HD).astype(low) for x in (d_q_enc, d_k_enc, d_v_enc))
    enc_query_grad = inner(h_zero, d_q_enc)
    enc_key_grad = inner(x_norm, d_k_enc)
    enc_value_grad = inner(x_norm, d_v_enc)
    d_middle, gain_zero = norm_pullback(z_zero, norm_gains[0], against(d_q_enc, enc_query))
    d_zero = d_one + d_middle
    d_zero_top = d_zero.astype(low)
    d_zero_rest = (d_zero - d_zero_top.astype(jnp.float32)).astype(low)
    latent_grad = inner(picked, d_zero_top) + inner(picked, d_zero_rest)

    def columns(whole, g):
        size = whole.shape[1] // n_head
        return whole[:, g * size : (g + 1) * size]

    def of_rows(whole, g):
        size = whole.shape[0] // n_head
        return whole[g * size : (g + 1) * size]

    flat = []
    for g in range(n_head):
        group = [
            columns(enc_query_grad, g),
            jnp.concatenate([columns(enc_key_grad, g), columns(enc_value_grad, g)], 1),
            of_rows(enc_out_grad, g),
            columns(project_grad, g),
            of_rows(self_out_grad, g),
            columns(in_grad, g),
            of_rows(out_grad, g),
            columns(class_grad, g),
        ]
        flat.append(jnp.concatenate([w.astype(low).reshape(-1) for w in group]).reshape(n_blk, n_h))
    flat = jnp.pad(jnp.stack(flat, 1), ((0, 0), (0, 0), (0, head_rows * LANES - n_h)))
    gains = jnp.stack([gain_zero, gain_one, gain_two, gain_three])
    common = jnp.concatenate([w.astype(low).reshape(-1) for w in (query_grad, latent_grad, gains)])
    common = jnp.pad(common.reshape(n_blk, n_c), ((0, 0), (0, n_head * piece_rows * LANES - n_c)))
    blocks = jnp.concatenate(
        [
            flat.reshape(n_blk, n_head, head_rows, LANES),
            common.reshape(n_blk, n_head, piece_rows, LANES),
        ],
        2,
    )
    share = reduce_all(dims, blocks, 6)
    clip_norm = jnp.sqrt(lax.psum(jnp.sum(share * share), ("blk", "head")))
    factor = jnp.minimum(1.0, clip_limit / clip_norm)
    head_share = share[:head_rows].reshape(-1)[:n_h]
    common_share = lax.all_gather(share[head_rows:].astype(low), "head", axis=0, tiled=True)
    common_share = common_share.reshape(-1)[:n_c].astype(jnp.float32)
    head_out = adam_step(head_params, head_first, head_second, head_share * factor)
    common_out = adam_step(common_params, common_first, common_second, common_share * factor)
    return head_out + common_out + (loss_sums, label_counts, clip_norm)


def solution(mesh):
    placed = (
        P("blk", None),
        P("blk", None),
        P(),
        P("blk"),
        P("blk"),
        P("blk"),
        P(("head", "blk")),
        P(("head", "blk")),
        P(("head", "blk")),
        P("blk"),
        P("blk"),
        P("blk"),
    )
    return jax.shard_map(
        per_device,
        mesh=mesh,
        in_specs=placed,
        out_specs=(
            P(("head", "blk")),
            P(("head", "blk")),
            P(("head", "blk")),
            P(("head", "blk")),
            P("blk"),
            P("blk"),
            P("blk"),
            P("blk"),
            P(),
            P(),
            P(),
        ),
        check_vma=False,
    )
```

```python
import functools

import jax
import jax.numpy as jnp
from jax import lax
from jax.experimental import pallas as pl
from jax.experimental.pallas import tpu as pltpu
from jax.sharding import PartitionSpec as P

D = 512
HEADS = 8
HD = 64
FF = 2048
DI = 704
DQ = 1026
C = 704
LAT = 784
MODES = 3
STEP = 10
LANES = 128
TILE = 16

norm_eps = 1e-05
learn_rate = 0.1
beta_one = 0.9
beta_two = 0.999
adam_eps = 1e-08
weight_decay = 0.01
clip_limit = 0.05
big_negative = -1e30
low = jnp.bfloat16
MESH = pl.DeviceIdType.MESH
MIB = 1 << 20


def round_up(n, unit):
    return -(-n // unit) * unit


def grid_of(n_blk, n_head):
    cores = 2 if n_head % 2 == 0 else 1
    x = n_head // cores
    y = x if n_blk % x == 0 else 1
    return (n_blk // y, y, x, cores)


def my_place(dims):
    blk, head = lax.axis_index("blk"), lax.axis_index("head")
    return (blk // dims[1], lax.rem(blk, dims[1]), head // dims[3], lax.rem(head, dims[3]))


def shifted(dims, me, offset, sign):
    return tuple(
        m if o == 0 else lax.rem(m + (o if sign > 0 else n - o), n)
        for m, o, n in zip(me, offset, dims)
    )


def blk_of(dims, place):
    return place[0] * dims[1] + place[1]


def head_of(dims, place):
    return place[2] * dims[3] + place[3]


def device_of(dims, place):
    return {"blk": blk_of(dims, place), "head": head_of(dims, place)}


def along(axis, d):
    return tuple(d if a == axis else 0 for a in range(4))


def greet(dims, me, offsets):
    barrier = pltpu.get_barrier_semaphore()
    for offset in offsets:
        pl.semaphore_signal(
            barrier,
            inc=1,
            device_id=device_of(dims, shifted(dims, me, offset, 1)),
            device_id_type=MESH,
        )
    pl.semaphore_wait(barrier, len(offsets))


def axis_peers(dims, axes):
    return [along(axis, d) for axis in axes for d in range(1, dims[axis])]


def remote(src, dst, send_sem, recv_sem, place, dims):
    return pltpu.make_async_remote_copy(
        src_ref=src,
        dst_ref=dst,
        send_sem=send_sem,
        recv_sem=recv_sem,
        device_id=device_of(dims, place),
        device_id_type=MESH,
    )


def gather_plan(dims, parts):
    plan = []
    for position in range(4):
        for p, (array, first, rows, order) in enumerate(parts):
            axis = order[position]
            done = order[:position]
            offsets = [(0, 0, 0, 0)]
            for a in done:
                offsets = [
                    tuple(d if i == a else o[i] for i in range(4))
                    for d in range(dims[a])
                    for o in offsets
                ]
            for d in range(1, dims[axis]):
                for o in offsets:
                    plan.append((p, tuple(d if i == axis else o[i] for i in range(4)), position))
    return plan


def gather_kernel(dims, parts, count, *refs):
    srcs, outs = refs[:count], refs[count : 2 * count]
    send_sem, recv_sem, own_sem = refs[2 * count :]
    me = my_place(dims)
    plan = gather_plan(dims, parts)
    number = {(p, offset): i for i, (p, offset, position) in enumerate(plan)}
    axes = [a for a in range(4) if dims[a] > 1]
    greet(dims, me, axis_peers(dims, axes))
    started = []

    def block(p, offset):
        place = shifted(dims, me, offset, -1)
        array, first, rows, order = parts[p]
        return outs[array].at[blk_of(dims, place), head_of(dims, place), pl.ds(first, rows)]

    def forward(p, offset, position):
        array, first, rows, order = parts[p]
        source = srcs[array].at[pl.ds(first, rows)] if position < 0 else block(p, offset)
        for axis in order[position + 1 :]:
            for d in range(1, dims[axis]):
                i = number[(p, tuple(d if a == axis else offset[a] for a in range(4)))]
                copy = remote(
                    source,
                    block(p, offset),
                    send_sem.at[i],
                    recv_sem.at[i],
                    shifted(dims, me, along(axis, d), 1),
                    dims,
                )
                copy.start()
                started.append(copy)

    for p in range(len(parts)):
        forward(p, (0, 0, 0, 0), -1)
    own = []
    for array in range(count):
        copy = pltpu.make_async_copy(
            srcs[array], outs[array].at[blk_of(dims, me), head_of(dims, me)], own_sem.at[array]
        )
        copy.start()
        own.append(copy)
    for i, (p, offset, position) in enumerate(plan):
        landed = block(p, offset)
        axis = parts[p][3][position]
        remote(
            landed,
            landed,
            send_sem.at[i],
            recv_sem.at[i],
            shifted(dims, me, along(axis, offset[axis]), -1),
            dims,
        ).wait_recv()
        forward(p, offset, position)
    for copy in started:
        copy.wait_send()
    for copy in own:
        copy.wait()


def halves(array, rows, orders):
    first = rows // 2 // TILE * TILE
    return ((array, 0, first, orders[0]), (array, first, rows - first, orders[1]))


def gather_all(dims, shards, collective_id):
    parts = halves(0, shards[0].shape[0], ((0, 1, 2, 3), (0, 2, 1, 3))) + (
        (1, 0, shards[1].shape[0], (0, 2, 1, 3)),
    )
    count = len(gather_plan(dims, parts))
    z, y, x, cores = dims
    any_space = pl.BlockSpec(memory_space=pl.ANY)
    return pl.pallas_call(
        functools.partial(gather_kernel, dims, parts, len(shards)),
        out_shape=[
            jax.ShapeDtypeStruct((z * y, x * cores) + shard.shape, shard.dtype) for shard in shards
        ],
        in_specs=[any_space] * len(shards),
        out_specs=[any_space] * len(shards),
        scratch_shapes=[
            pltpu.SemaphoreType.DMA((count,)),
            pltpu.SemaphoreType.DMA((count,)),
            pltpu.SemaphoreType.DMA((len(shards),)),
        ],
        compiler_params=pltpu.CompilerParams(collective_id=collective_id, has_side_effects=True),
        name="gather_weights",
    )(*shards)


def reduce_plan(dims, order):
    stages = []
    for position, axis in enumerate(order):
        rest = order[position + 1 :]
        offsets = [(0, 0, 0, 0)]
        for a in reversed(rest):
            offsets = [
                tuple(d if i == a else o[i] for i in range(4))
                for d in list(range(1, dims[a])) + [0]
                for o in offsets
            ]
        stages.append((axis, offsets))
    return stages


def reduce_kernel(dims, parts, chunk, valid, *refs):
    count = len(valid)
    srcs, tile = refs[:count], refs[count]
    outs, totals, shares = refs[count + 1 : 2 * count + 1], refs[2 * count + 1], refs[2 * count + 2]
    scratch = refs[2 * count + 3 :]
    me = my_place(dims)
    z, y, x, cores = dims
    places = len(parts) * 4
    buffers = scratch[:places]
    send_sem, recv_sem, near_tiles, far_tiles = scratch[places : places + 4]
    axes = [a for a in range(4) if dims[a] > 1]
    across = [(0, 0, a, c) for a in range(x) for c in range(cores) if (a, c) != (0, 0)]
    others = [(a, b, 0, 0) for a in range(z) for b in range(y) if (a, b) != (0, 0)]
    greet(dims, me, axis_peers(dims, axes) + [o for o in across + others if sum(v != 0 for v in o) > 1])
    started = []
    pending = {}

    def push(src, dst, offset):
        i = len(started)
        copy = remote(src, dst, send_sem.at[i], recv_sem.at[i], shifted(dims, me, offset, 1), dims)
        copy.start()
        started.append(copy)
        return copy

    stages = [reduce_plan(dims, part[3]) for part in parts]

    def source(p, position, offset):
        array, first, rows, order = parts[p]
        if position == 0:
            place = shifted(dims, me, offset, 1)
            return srcs[array].at[blk_of(dims, place), head_of(dims, place), pl.ds(first, rows)]
        k = stages[p][position - 1][1].index(offset)
        return buffers[p * 4 + position - 1].at[k, 0]

    def send(p, position, k, d):
        axis, offsets = stages[p][position]
        there = tuple(d if a == axis else offsets[k][a] for a in range(4))
        pending[(p, position, k, d)] = push(
            source(p, position, there), buffers[p * 4 + position].at[k, d - 1], along(axis, d)
        )

    def add(p, position, k):
        array, first, rows, order = parts[p]
        axis, offsets = stages[p][position]
        for d in range(1, dims[axis]):
            pending[(p, position, k, d)].wait_recv()
        mine = source(p, position, offsets[k])
        arrived = buffers[p * 4 + position]
        step = chunk(rows)
        last = position == 3

        @pl.loop(0, rows // step)
        def some_rows(n):
            at = pl.ds(pl.multiple_of(n * step, step), step)
            total = mine[at].astype(jnp.float32)
            for d in range(1, dims[axis]):
                total = total + arrived[k, d - 1, at].astype(jnp.float32)
            if last:
                outs[array][pl.ds(pl.multiple_of(first + n * step, TILE), step)] = total
            else:
                arrived[k, 0, at] = total.astype(low)

    for k in range(len(stages[0][0][1])):
        for p in range(len(parts)):
            for d in range(1, dims[stages[p][0][0]]):
                send(p, 0, k, d)
    for position in range(4):
        for k in range(len(stages[0][position][1])):
            for p in range(len(parts)):
                add(p, position, k)
                if position < 3:
                    axis, offsets = stages[p][position + 1]
                    offset = stages[p][position][1][k]
                    rest = tuple(0 if a == axis else offset[a] for a in range(4))
                    if offset[axis]:
                        send(p, position + 1, offsets.index(rest), offset[axis])
    my_head, my_blk = head_of(dims, me), blk_of(dims, me)
    shares[my_head] = outs[count - 1][...].astype(low)
    share_copies = [push(shares.at[my_head], shares.at[my_head], o) for o in across]
    squares = jnp.zeros((1, LANES), jnp.float32)
    for out, amount in zip(outs, valid):
        squares = squares + jnp.sum(out[:amount] * out[:amount], 0, keepdims=True)
    lane = lax.broadcasted_iota(jnp.int32, (1, LANES), 1)
    near_tiles[my_head] = tile[...] + jnp.where(
        lane == MODES, jnp.sum(squares, 1, keepdims=True), 0.0
    )
    near = [push(near_tiles.at[my_head], near_tiles.at[my_head], o) for o in across]
    for copy in near:
        copy.wait_recv()
    far_tiles[my_blk] = jnp.sum(near_tiles[...], 0)
    far = [push(far_tiles.at[my_blk], far_tiles.at[my_blk], o) for o in others]
    for copy in far:
        copy.wait_recv()
    totals[...] = jnp.sum(far_tiles[...], 0)
    for copy in share_copies:
        copy.wait_recv()
    for copy in started:
        copy.wait_send()


def row_chunk(rows):
    for count in (4, 3, 2):
        if rows % (count * TILE) == 0:
            return rows // count
    return rows


def reduce_all(dims, arrays, valid, tile, collective_id):
    z, y, x, cores = dims
    parts = halves(0, arrays[0].shape[2], ((3, 2, 1, 0), (3, 1, 2, 0))) + (
        (1, 0, arrays[1].shape[2], (3, 1, 2, 0)),
    )
    scratch = []
    count = 2 * (x * cores - 1) + z * y - 1
    for array, start, amount, order in parts:
        for axis, offsets in reduce_plan(dims, order):
            others = max(dims[axis] - 1, 1)
            count += len(offsets) * (dims[axis] - 1)
            scratch.append(pltpu.VMEM((len(offsets), others, amount, LANES), low))
    vmem = pl.BlockSpec(memory_space=pltpu.VMEM)
    last_rows = arrays[-1].shape[2]
    return pl.pallas_call(
        functools.partial(reduce_kernel, dims, parts, row_chunk, valid),
        out_shape=[jax.ShapeDtypeStruct(array.shape[2:], jnp.float32) for array in arrays]
        + [
            jax.ShapeDtypeStruct((8, LANES), jnp.float32),
            jax.ShapeDtypeStruct((x * cores, last_rows, LANES), low),
        ],
        in_specs=[vmem] * (len(arrays) + 1),
        out_specs=[vmem] * (len(arrays) + 2),
        scratch_shapes=scratch
        + [
            pltpu.SemaphoreType.DMA((count,)),
            pltpu.SemaphoreType.DMA((count,)),
            pltpu.VMEM((x * cores, 8, LANES), jnp.float32),
            pltpu.VMEM((z * y, 8, LANES), jnp.float32),
        ],
        compiler_params=pltpu.CompilerParams(
            collective_id=collective_id, has_side_effects=True, vmem_limit_bytes=56 * MIB
        ),
        name="reduce_gradients",
    )(*arrays, tile)


def spread_kernel(dims, q_in, kv_in, q_out, kv_out, send_sem, recv_sem, own_sem):
    z, y, x, cores = dims
    me = my_place(dims)
    heads = x * cores
    my_blk, my_head = blk_of(dims, me), head_of(dims, me)
    across = [(0, 0, a, c) for a in range(x) for c in range(cores) if (a, c) != (0, 0)]
    across.sort(key=lambda o: (o[2] == 0, o[3]))
    ups = [along(0, d) for d in range(1, z)]
    sides = [along(1, d) for d in range(1, y)]
    greet(dims, me, across + ups + sides)
    own_q = pltpu.make_async_copy(q_in.at[my_head], q_out.at[my_head], own_sem.at[0])
    own_kv = pltpu.make_async_copy(kv_in.at[my_head], kv_out.at[my_blk, my_head], own_sem.at[1])
    own_kv.start()
    own_q.start()
    started = []
    count = [0]

    def push(src, dst, place):
        i = count[0]
        count[0] += 1
        copy = remote(src, dst, send_sem.at[i], recv_sem.at[i], place, dims)
        copy.start()
        started.append(copy)
        return copy

    landed_kv = []
    for o in across:
        place = shifted(dims, me, o, 1)
        landed_kv.append(push(kv_in.at[head_of(dims, place)], kv_out.at[my_blk, my_head], place))
    landed_q = []
    for o in across:
        place = shifted(dims, me, o, 1)
        landed_q.append(push(q_in.at[head_of(dims, place)], q_out.at[my_head], place))
    pieces = [(0, 0, 0, 0)] + across
    up_copies = {}
    side_copies = {}

    def kv_block(place_blk, offset):
        place = shifted(dims, me, offset, -1)
        return kv_out.at[place_blk, head_of(dims, place)]

    def spread_own(n):
        block = kv_block(my_blk, pieces[n])
        for o in ups:
            up_copies[(n, o)] = push(block, block, shifted(dims, me, o, 1))
        for o in sides:
            side_copies[(n, along(0, 0), o)] = push(block, block, shifted(dims, me, o, 1))

    own_kv.wait()
    spread_own(0)
    order = sorted(range(1, len(pieces)), key=lambda n: (pieces[n][2] != 0, pieces[n][3]))
    for n in order:
        landed_kv[n - 1].wait_recv()
        spread_own(n)
    for u in ups:
        for n in [0] + order:
            up_copies[(n, u)].wait_recv()
            block = kv_block(blk_of(dims, shifted(dims, me, u, -1)), pieces[n])
            for o in sides:
                side_copies[(n, u, o)] = push(block, block, shifted(dims, me, o, 1))
    for copy in landed_q:
        copy.wait_recv()
    for copy in side_copies.values():
        copy.wait_recv()
    for copy in started:
        copy.wait_send()
    own_q.wait()


def spread_rows(dims, q, kv, collective_id):
    z, y, x, cores = dims
    heads = x * cores
    count = 2 * (heads - 1) + heads * (z - 1 + z * (y - 1))
    return pl.pallas_call(
        functools.partial(spread_kernel, dims),
        out_shape=(
            jax.ShapeDtypeStruct(q.shape, low),
            jax.ShapeDtypeStruct((z * y,) + kv.shape, low),
        ),
        in_specs=[pl.BlockSpec(memory_space=pl.ANY)] * 2,
        out_specs=[pl.BlockSpec(memory_space=pl.ANY)] * 2,
        scratch_shapes=[
            pltpu.SemaphoreType.DMA((count,)),
            pltpu.SemaphoreType.DMA((count,)),
            pltpu.SemaphoreType.DMA((2,)),
        ],
        compiler_params=pltpu.CompilerParams(collective_id=collective_id, has_side_effects=True),
        name="spread_rows",
    )(q, kv)


def swap_kernel(dims, src, out, send_sem, recv_sem, own_sem):
    z, y, x, cores = dims
    me = my_place(dims)
    my_head = head_of(dims, me)
    across = [(0, 0, a, c) for a in range(x) for c in range(cores) if (a, c) != (0, 0)]
    greet(dims, me, across)
    copies = []
    for i, o in enumerate(across):
        place = shifted(dims, me, o, 1)
        copy = remote(
            src.at[head_of(dims, place)], out.at[my_head], send_sem.at[i], recv_sem.at[i], place, dims
        )
        copy.start()
        copies.append(copy)
    own = pltpu.make_async_copy(src.at[my_head], out.at[my_head], own_sem)
    own.start()
    for copy in copies:
        copy.wait_recv()
    for copy in copies:
        copy.wait_send()
    own.wait()


def swap_heads(dims, blocks, collective_id):
    count = dims[2] * dims[3] - 1
    return pl.pallas_call(
        functools.partial(swap_kernel, dims),
        out_shape=jax.ShapeDtypeStruct(blocks.shape, blocks.dtype),
        in_specs=[pl.BlockSpec(memory_space=pl.ANY)],
        out_specs=pl.BlockSpec(memory_space=pl.ANY),
        scratch_shapes=[
            pltpu.SemaphoreType.DMA((count,)),
            pltpu.SemaphoreType.DMA((count,)),
            pltpu.SemaphoreType.DMA(()),
        ],
        compiler_params=pltpu.CompilerParams(collective_id=collective_id, has_side_effects=True),
        name="swap_heads",
    )(blocks)


def collect_kernel(dims, src, out, side_buf, up_buf, send_sem, recv_sem):
    z, y, x, cores = dims
    me = my_place(dims)
    greet(dims, me, axis_peers(dims, (0, 1)))
    started = []
    rows = src.shape[1]
    step = 256

    def push(s, dst, place):
        i = len(started)
        copy = remote(s, dst, send_sem.at[i], recv_sem.at[i], place, dims)
        copy.start()
        started.append(copy)
        return copy

    side = {}
    for u in list(range(1, z)) + [0]:
        for d in range(1, y):
            place = shifted(dims, me, (u, d, 0, 0), 1)
            side[(u, d)] = push(
                src.at[blk_of(dims, place)], side_buf.at[u, d - 1], shifted(dims, me, along(1, d), 1)
            )
    up = {}
    for u in list(range(1, z)) + [0]:
        for d in range(1, y):
            side[(u, d)].wait_recv()
        mine = src.at[blk_of(dims, shifted(dims, me, along(0, u), 1))]

        @pl.loop(0, rows // step)
        def some_rows(n):
            at = pl.ds(pl.multiple_of(n * step, step), step)
            total = mine[at].astype(jnp.float32)
            for d in range(1, y):
                total = total + side_buf[u, d - 1, at].astype(jnp.float32)
            side_buf[u, 0, at] = total.astype(low)

        if u:
            up[u] = push(
                side_buf.at[u, 0], up_buf.at[u - 1], shifted(dims, me, along(0, u), 1)
            )
    for u in range(1, z):
        up[u].wait_recv()

    @pl.loop(0, rows // step)
    def last_rows(n):
        at = pl.ds(pl.multiple_of(n * step, step), step)
        total = side_buf[0, 0, at].astype(jnp.float32)
        for u in range(1, z):
            total = total + up_buf[u - 1, at].astype(jnp.float32)
        out[at] = total.astype(low)

    for copy in started:
        copy.wait_send()


def collect_rows(dims, parts, collective_id):
    z, y, x, cores = dims
    shape = parts.shape[1:]
    count = z * (y - 1) + z - 1
    return pl.pallas_call(
        functools.partial(collect_kernel, dims),
        out_shape=jax.ShapeDtypeStruct(shape, low),
        in_specs=[pl.BlockSpec(memory_space=pltpu.VMEM)],
        out_specs=pl.BlockSpec(memory_space=pltpu.VMEM),
        scratch_shapes=[
            pltpu.VMEM((z, max(y - 1, 1)) + shape, low),
            pltpu.VMEM((max(z - 1, 1),) + shape, low),
            pltpu.SemaphoreType.DMA((count,)),
            pltpu.SemaphoreType.DMA((count,)),
        ],
        compiler_params=pltpu.CompilerParams(
            collective_id=collective_id, has_side_effects=True, vmem_limit_bytes=48 * MIB
        ),
        name="collect_rows",
    )(parts)


def contract_first(a, b):
    return lax.dot_general(a, b, (((0,), (0,)), ((), ())), preferred_element_type=jnp.float32)


def product(a, b):
    return jnp.dot(a, b, preferred_element_type=jnp.float32)


def against(a, b):
    return lax.dot_general(a, b, (((1,), (1,)), ((), ())), preferred_element_type=jnp.float32)


def clip_borders(bounds, where):
    clips = bounds.shape[1]
    opening = jnp.zeros(where.shape, jnp.int32)
    ending = jnp.full(where.shape, 1 << 30, jnp.int32)
    for clip in range(clips):
        here = where == HD + clip
        opening = jnp.where(here, bounds[0, clip], opening)
        ending = jnp.where(here, bounds[1, clip], ending)
    return opening, ending


def extend_keys(bounds, heads, rows_at_once, kv, keys, values):
    width = heads * HD
    clips = bounds.shape[1]
    lane = lax.broadcasted_iota(jnp.int32, (1, LANES), 1)
    opening, ending = clip_borders(bounds, lane)
    ones = jnp.where((lane >= HD + clips) & (lane < HD + clips + 3), 1.0, 0.0)
    value_tail = jnp.where((lane >= HD) & (lane < HD + 3), 1.0, 0.0) + jnp.zeros(
        (rows_at_once, LANES), jnp.float32
    )

    @pl.loop(0, kv.shape[0] // rows_at_once)
    def some_rows(n):
        first = pl.multiple_of(n * rows_at_once, rows_at_once)
        at = pl.ds(first, rows_at_once)
        row = first + lax.broadcasted_iota(jnp.int32, (rows_at_once, LANES), 0)
        tail = jnp.where((row >= opening) & (row < ending), ones, big_negative)
        block = kv[at, :].astype(jnp.float32)
        for a in range(heads):
            for first_column, target, end in ((0, keys, tail), (width, values, value_tail)):
                columns = block[:, first_column + a * HD : first_column + (a + 1) * HD]
                target[a, at, :] = jnp.concatenate([columns, end[:, HD:]], 1).astype(low)


def extend_queries(bounds, first_row, heads, q_t, a, extra):
    clips = bounds.shape[1]
    amount = q_t.shape[1]
    place = HD + lax.broadcasted_iota(jnp.int32, (HD, 1), 0)
    opening, ending = clip_borders(bounds, place)
    row = first_row + lax.broadcasted_iota(jnp.int32, (1, amount), 1)
    is_clip = place < HD + clips
    tail = jnp.where(is_clip & (row >= opening) & (row < ending), 1.0, 0.0)
    if extra is not None:
        tail = tail + in_three(place - HD - clips, -extra)
    return jnp.concatenate([q_t[a * HD : (a + 1) * HD] * HD ** (-0.5), tail], 0).astype(low)


def in_three(place, value):
    top = value.astype(low).astype(jnp.float32)
    middle = (value - top).astype(low).astype(jnp.float32)
    bottom = value - top - middle
    return (
        jnp.where(place == 0, top, 0.0)
        + jnp.where(place == 1, middle, 0.0)
        + jnp.where(place == 2, bottom, 0.0)
    )


def attend_kernel(heads, key_step, query_step, bounds, q, kv, out, lse, out_t, keys, values, queries, top, accum):
    first_row = lax.axis_index("blk") * q.shape[0]
    amount, total_keys = q.shape[0], kv.shape[0]
    extend_keys(bounds, heads, key_step, kv, keys, values)
    q_t = q[...].astype(jnp.float32).T
    for a in range(heads):
        queries[a] = extend_queries(bounds, first_row, heads, q_t, a, None)

    @pl.loop(0, amount // query_step)
    def query_block(n):
        at = pl.ds(pl.multiple_of(n * query_step, query_step), query_step)
        top[...] = jnp.full(top.shape, -1e38, jnp.float32)
        accum[...] = jnp.zeros(accum.shape, jnp.float32)

        @pl.loop(0, total_keys // key_step)
        def key_block(k):
            rows = pl.ds(pl.multiple_of(k * key_step, key_step), key_step)
            for a in range(heads):
                scores = product(keys[a, rows, :], queries[a, :, at])
                old = top[a : a + 1, :]
                new = jnp.maximum(old, jnp.max(scores, 0, keepdims=True))
                probs = jnp.exp(scores - new).astype(low)
                top[a : a + 1, :] = new
                accum[a] = accum[a] * jnp.exp(old - new) + contract_first(values[a, rows, :], probs)

        for a in range(heads):
            total = accum[a, HD : HD + 1, :]
            out_t[a * HD : (a + 1) * HD, at] = accum[a, :HD, :] / total
            lse[a : a + 1, at] = top[a : a + 1, :] + jnp.log(total)

    out[...] = out_t[...].T.astype(low)


def attend(bounds, q, kv, heads):
    amount, width = q.shape
    total_keys = kv.shape[0]
    key_step, query_step = 1024, 256
    vmem = pl.BlockSpec(memory_space=pltpu.VMEM)
    return pl.pallas_call(
        functools.partial(attend_kernel, heads, key_step, query_step),
        out_shape=(
            jax.ShapeDtypeStruct((amount, width), low),
            jax.ShapeDtypeStruct((heads, amount), jnp.float32),
            jax.ShapeDtypeStruct((width, amount), jnp.float32),
        ),
        in_specs=[pl.BlockSpec(memory_space=pltpu.SMEM), vmem, vmem],
        out_specs=[vmem] * 3,
        scratch_shapes=[
            pltpu.VMEM((heads, total_keys, LANES), low),
            pltpu.VMEM((heads, total_keys, LANES), low),
            pltpu.VMEM((heads, LANES, amount), low),
            pltpu.VMEM((heads, query_step), jnp.float32),
            pltpu.VMEM((heads, LANES, query_step), jnp.float32),
        ],
        compiler_params=pltpu.CompilerParams(vmem_limit_bytes=56 * MIB),
        name="attend",
    )(bounds, q, kv)


def attend_back_kernel(
    heads, key_step, bounds, q, kv, dout, out_t, lse, d_q, d_kv, keys, values, queries, douts, d_q_t, q_rows, do_rows
):
    first_row = lax.axis_index("blk") * q.shape[0]
    amount, total_keys = q.shape[0], kv.shape[0]
    width = heads * HD
    extend_keys(bounds, heads, 1024, kv, keys, values)
    q_low = q[...].astype(jnp.float32)
    do_low = dout[...].astype(jnp.float32)
    q_t, do_t = q_low.T, do_low.T
    place = lax.broadcasted_iota(jnp.int32, (HD, 1), 0)
    lane = lax.broadcasted_iota(jnp.int32, (1, width), 1)
    for a in range(heads):
        mine = slice(a * HD, (a + 1) * HD)
        queries[a] = extend_queries(bounds, first_row, heads, q_t, a, lse[a : a + 1, :])
        delta = jnp.sum(do_t[mine] * out_t[mine, :], 0, keepdims=True)
        douts[a] = jnp.concatenate([do_t[mine], in_three(place, -delta)], 0).astype(low)
        here = (lane >= a * HD) & (lane < (a + 1) * HD)
        q_rows[a] = jnp.where(here, q_low * HD ** (-0.5), 0.0).astype(low)
        do_rows[a] = jnp.where(here, do_low, 0.0).astype(low)
    d_q_t[...] = jnp.zeros(d_q_t.shape, jnp.float32)

    @pl.loop(0, total_keys // key_step)
    def key_block(k):
        rows = pl.ds(pl.multiple_of(k * key_step, key_step), key_step)
        d_key = jnp.zeros((key_step, width), jnp.float32)
        d_value = jnp.zeros((key_step, width), jnp.float32)
        for a in range(heads):
            probs = jnp.exp(product(keys[a, rows, :], queries[a]))
            d_probs = product(values[a, rows, :], douts[a])
            d_scores = (probs * d_probs).astype(low)
            d_value = d_value + product(probs.astype(low), do_rows[a])
            d_key = d_key + product(d_scores, q_rows[a])
            d_q_t[a] = d_q_t[a] + contract_first(keys[a, rows, :], d_scores)
        d_kv[rows, :] = jnp.concatenate([d_key, d_value], 1).astype(low)

    whole = jnp.concatenate([d_q_t[a, :HD, :] for a in range(heads)], 0) * HD ** (-0.5)
    d_q[...] = whole.T.astype(low)


def attend_back(bounds, q, kv, dout, out_t, lse, heads):
    amount, width = q.shape
    total_keys = kv.shape[0]
    key_step = 256
    vmem = pl.BlockSpec(memory_space=pltpu.VMEM)
    return pl.pallas_call(
        functools.partial(attend_back_kernel, heads, key_step),
        out_shape=(
            jax.ShapeDtypeStruct((amount, width), low),
            jax.ShapeDtypeStruct((total_keys, 2 * width), low),
        ),
        in_specs=[pl.BlockSpec(memory_space=pltpu.SMEM)] + [vmem] * 5,
        out_specs=[vmem] * 2,
        scratch_shapes=[
            pltpu.VMEM((heads, total_keys, LANES), low),
            pltpu.VMEM((heads, total_keys, LANES), low),
            pltpu.VMEM((heads, LANES, amount), low),
            pltpu.VMEM((heads, LANES, amount), low),
            pltpu.VMEM((heads, LANES, amount), jnp.float32),
            pltpu.VMEM((heads, amount, width), low),
            pltpu.VMEM((heads, amount, width), low),
        ],
        compiler_params=pltpu.CompilerParams(vmem_limit_bytes=56 * MIB),
        name="attend_back",
    )(bounds, q, kv, dout, out_t, lse)


def part_shapes(n_head):
    width = HEADS // n_head * HD
    hidden = FF // n_head
    return (
        (D, width, True),
        (DI, 2 * width, True),
        (width, D, False),
        (D, 3 * width, True),
        (width, D, False),
        (D, hidden, True),
        (hidden, D, False),
        (D, C // n_head, True),
    )


def borders(n_head):
    result = [0]
    for rows, columns, joined in part_shapes(n_head):
        result.append(result[-1] + rows * columns // LANES)
    return result


def period(columns):
    amount = 1
    while amount * columns % LANES:
        amount *= 2
    return amount


def segments(start, amount, unit):
    result = []
    while amount > 0:
        which, at = divmod(start, unit)
        size = min(unit - at, amount)
        result.append((which, at, at + size))
        start, amount = start + size, amount - size
    return result


def joined_lanes(pieces):
    return pieces[0] if len(pieces) == 1 else jnp.concatenate(pieces, 1)


def lane_blocks(value):
    rows, columns = value.shape
    missing = -columns % LANES
    if missing:
        value = jnp.concatenate([value, jnp.zeros((rows, missing), value.dtype)], 1)
    return [value[:, i : i + LANES] for i in range(0, columns + missing, LANES)]


def every(first, amount, stride):
    return pl.ds(first, amount) if stride == 1 else pl.ds(first, amount, stride=stride)


def matrix_of(stage, first, rows, columns, line):
    if columns % LANES == 0:
        stride = columns // LANES
        for j in range(stride):
            yield j * LANES, stage[every(first + j, rows, stride), :]
        return
    height = period(columns)
    stride = height * columns // LANES
    for k in range(height):
        pieces = [
            stage[every(first + which, rows // height, stride), :][:, begin:end]
            for which, begin, end in segments(k * columns, columns, LANES)
        ]
        for i, piece in enumerate(lane_blocks(joined_lanes(pieces))):
            line[i, every(k, rows // height, height), :] = piece
    for i in range(-(-columns // LANES)):
        yield i * LANES, line[i, :rows, : min(columns - i * LANES, LANES)]


def matrix_into(stage, first, value, line):
    rows, columns = value.shape
    if columns % LANES == 0:
        stride = columns // LANES
        for j in range(stride):
            stage[every(first + j, rows, stride), :] = value[:, j * LANES : (j + 1) * LANES]
        return
    height = period(columns)
    stride = height * columns // LANES
    for i, piece in enumerate(lane_blocks(value)):
        line[i, :rows, :] = piece
    for i in range(stride):
        pieces = [
            line[which, every(k, rows // height, height), :][:, begin:end]
            for k, first_lane, last_lane in segments(i * LANES, LANES, columns)
            for which, begin, end in segments(first_lane, last_lane - first_lane, LANES)
        ]
        stage[every(first + i, rows // height, stride), :] = joined_lanes(pieces)


def load_stage(stage, held, first_shard, shard_rows, group):
    for b in range(held.shape[0]):
        stage[pl.ds(b * shard_rows, shard_rows), :] = held[b, group, :shard_rows, :].astype(jnp.float32)


def load_matrices(stage, first_row, n_head, group, which, targets, line):
    starts, shapes = borders(n_head), part_shapes(n_head)
    for m, target in zip(which, targets):
        rows, columns, joined = shapes[m]
        row = 0 if joined else group * rows
        column = group * columns if joined else 0
        for j, value in matrix_of(stage, starts[m] - first_row, rows, columns, line):
            size = value.shape[1]
            target[row : row + rows, column + j : column + j + size] = value.astype(target.dtype)


def normalized(x):
    centre = x - jnp.mean(x, -1, keepdims=True)
    rate = lax.rsqrt(jnp.mean(centre * centre, -1, keepdims=True) + norm_eps)
    return centre * rate, rate


def layer_norm(x, gain):
    return normalized(x)[0] * gain


def norm_pullback(x, gain, grad):
    unit, rate = normalized(x)
    inside = grad * gain
    both = jnp.mean(inside * unit, -1, keepdims=True)
    d_x = rate * (inside - jnp.mean(inside, -1, keepdims=True) - unit * both)
    return d_x, jnp.sum(grad * unit, 0, keepdims=True)


def head_lanes(group, heads, value):
    width = heads * HD
    block = value[:, group * width : (group + 1) * width]
    lane = lax.broadcasted_iota(jnp.int32, (1, width), 1)
    result = []
    for a in range(heads):
        here = (lane >= a * HD) & (lane < (a + 1) * HD)
        result.append((here, jnp.where(here, block, jnp.zeros_like(block))))
    return result


def place_of(bounds, first, amount):
    row = first + lax.broadcasted_iota(jnp.int32, (amount, 1), 0)
    opening = jnp.zeros((amount, 1), jnp.int32)
    for clip in range(bounds.shape[1]):
        begin, end = bounds[0, clip], bounds[1, clip]
        opening = jnp.where((row >= begin) & (row < end), begin, opening)
    offset = row - opening
    turns = jnp.floor((offset.astype(jnp.float32) + 0.5) * (1.0 / LAT)).astype(jnp.int32)
    return offset - turns * LAT


def picked_rows(bounds, rows, n_head):
    first = lax.axis_index("blk") * (rows * n_head) + lax.axis_index("head") * rows
    lane = lax.broadcasted_iota(jnp.int32, (rows, LAT), 1)
    return jnp.where(lane == place_of(bounds, first, rows), 1.0, 0.0).astype(low)


def enc_scores(q_head, keys):
    return against(q_head, keys) * HD ** (-0.5)


def encode_kernel(
    n_head,
    shard_rows,
    rows,
    bounds,
    weights,
    common,
    inputs,
    enc_query,
    enc_keyval,
    enc_output,
    self_project,
    gains,
    z_zero,
    h_zero,
    x_norm,
    q_enc,
    kv_enc,
    o_enc,
    z_one,
    h_one,
    q_self,
    kv_self,
    held,
    held_common,
    stage,
    stage_common,
    line,
    latent_table,
    sems,
):
    heads = HEADS // n_head
    width = heads * HD
    shards = held.shape[0]
    from_row = DQ * D // LANES // TILE * TILE
    copies = [
        pltpu.make_async_copy(common.at[pl.ds(from_row, held_common.shape[0])], held_common, sems.at[0]),
        pltpu.make_async_copy(weights.at[pl.ds(0, shards)], held, sems.at[1]),
    ]
    for copy in copies:
        copy.start()
    x_norm[...] = normalized(inputs[...].astype(jnp.float32))[0].astype(low)
    copies[0].wait()
    stage_common[...] = held_common[...].astype(jnp.float32)
    first = DQ * D // LANES - from_row
    for j, value in matrix_of(stage_common, first, LAT, D, line):
        latent_table[:, j : j + LANES] = value.astype(low)
    for j, value in matrix_of(stage_common, first + LAT * D // LANES, 4, D, line):
        gains[:, j : j + LANES] = value
    picked = picked_rows(bounds, rows, n_head)
    z_zero[...] = product(picked, latent_table[...])
    h_zero[...] = layer_norm(z_zero[...], gains[0:1, :]).astype(low)
    copies[1].wait()
    for g in range(n_head):
        load_stage(stage, held, 0, shard_rows, g)
        load_matrices(
            stage, 0, n_head, g, (0, 1, 2, 3), (enc_query, enc_keyval, enc_output, self_project), line
        )
    q_enc[...] = product(h_zero[...], enc_query[...]).astype(low)
    kv_enc[...] = product(x_norm[...], enc_keyval[...]).astype(low)
    for g in range(n_head):
        keys = kv_enc[:, 2 * g * width : (2 * g + 1) * width]
        values = kv_enc[:, (2 * g + 1) * width : (2 * g + 2) * width]
        outcome = jnp.zeros((rows, width), jnp.float32)
        for here, q_head in head_lanes(g, heads, q_enc[...]):
            scores = enc_scores(q_head, keys)
            probs = jnp.exp(scores - jnp.max(scores, 1, keepdims=True))
            total = jnp.sum(probs, 1, keepdims=True)
            outcome = jnp.where(here, product(probs.astype(low), values) / total, outcome)
        o_enc[:, g * width : (g + 1) * width] = outcome.astype(low)
    z_one[...] = z_zero[...] + product(o_enc[...], enc_output[...])
    h_one[...] = layer_norm(z_one[...], gains[1:2, :]).astype(low)
    projected = product(h_one[...], self_project[...]).astype(low)
    for g in range(n_head):
        q_self[g] = projected[:, 3 * g * width : (3 * g + 1) * width]
        kv_self[g] = projected[:, (3 * g + 1) * width : (3 * g + 3) * width]


VMEM_SPEC = pl.BlockSpec(memory_space=pltpu.VMEM)
SMEM_SPEC = pl.BlockSpec(memory_space=pltpu.SMEM)
ANY_SPEC = pl.BlockSpec(memory_space=pl.ANY)
LINE = pltpu.VMEM((4, round_up(max(D, DI), 8), LANES), jnp.float32)


def shape_of(shape, dtype=low):
    return jax.ShapeDtypeStruct(shape, dtype)


def shards_of(n_head, shard_rows, first, last):
    starts = borders(n_head)
    begin = starts[first] // shard_rows
    return begin, -(-starts[last] // shard_rows) - begin


def encode(bounds, weights, common, inputs, rows, n_head, shard_rows):
    width = HEADS // n_head * HD
    begin, shards = shards_of(n_head, shard_rows, 0, 4)
    common_rows = common.shape[0] - DQ * D // LANES // TILE * TILE
    keys = inputs.shape[0]
    return pl.pallas_call(
        functools.partial(encode_kernel, n_head, shard_rows, rows),
        out_shape=[
            shape_of((D, D)),
            shape_of((DI, 2 * D)),
            shape_of((D, D)),
            shape_of((D, 3 * D)),
            shape_of((4, D), jnp.float32),
            shape_of((rows, D), jnp.float32),
            shape_of((rows, D)),
            shape_of(inputs.shape),
            shape_of((rows, D)),
            shape_of((keys, 2 * D)),
            shape_of((rows, D)),
            shape_of((rows, D), jnp.float32),
            shape_of((rows, D)),
            shape_of((n_head, rows, width)),
            shape_of((n_head, rows, 2 * width)),
        ],
        in_specs=[SMEM_SPEC, ANY_SPEC, ANY_SPEC, VMEM_SPEC],
        out_specs=[VMEM_SPEC] * 15,
        scratch_shapes=[
            pltpu.VMEM((shards,) + weights.shape[1:], low),
            pltpu.VMEM((common_rows, LANES), low),
            pltpu.VMEM((shards * shard_rows, LANES), jnp.float32),
            pltpu.VMEM((common_rows, LANES), jnp.float32),
            LINE,
            pltpu.VMEM((LAT, D), low),
            pltpu.SemaphoreType.DMA((2,)),
        ],
        compiler_params=pltpu.CompilerParams(vmem_limit_bytes=56 * MIB),
        name="encode",
    )(bounds, weights, common, inputs)


def gelu_and_slope(x):
    rate = (2.0 / jnp.pi) ** 0.5
    cubic = 0.044715
    t = jnp.tanh(rate * (x + cubic * x * x * x))
    slope = 0.5 * (1.0 + t) + 0.5 * x * (1.0 - t * t) * rate * (1.0 + 3.0 * cubic * x * x)
    return 0.5 * x * (1.0 + t), slope


def middle_kernel(
    n_head,
    shard_rows,
    first_shard,
    rows,
    counts,
    weights,
    common,
    z_one,
    o_self,
    out_queries,
    marks,
    gains,
    dout,
    d_two_out,
    tile,
    query_grad,
    gain_grads,
    grads,
    held,
    held_common,
    stage,
    stage_common,
    line,
    self_output,
    hidden_in,
    hidden_out,
    class_table,
    query_table,
    slope,
    activ,
    sems,
):
    heads = HEADS // n_head
    width, hidden, classes = heads * HD, FF // n_head, C // n_head
    shards = held.shape[0]
    first_row = first_shard * shard_rows
    starts = borders(n_head)
    copies = [
        pltpu.make_async_copy(common.at[pl.ds(0, held_common.shape[0])], held_common, sems.at[0]),
        pltpu.make_async_copy(weights.at[pl.ds(first_shard, shards)], held, sems.at[1]),
    ]
    for copy in copies:
        copy.start()
    copies[0].wait()
    stage_common[...] = held_common[...].astype(jnp.float32)
    for j, value in matrix_of(stage_common, 0, DQ, D, line):
        query_table[:, j : j + LANES] = value.astype(low)
    copies[1].wait()
    for g in range(n_head):
        load_stage(stage, held, first_shard, shard_rows, g)
        load_matrices(
            stage, first_row, n_head, g, (4, 5, 6, 7), (self_output, hidden_in, hidden_out, class_table), line
        )
    gain_two, gain_three = gains[2:3, :], gains[3:4, :]
    o_low = jnp.concatenate([o_self[g] for g in range(n_head)], 1)
    z_two = z_one[...] + product(o_low, self_output[...])
    h_two = layer_norm(z_two, gain_two).astype(low)
    value, bend = gelu_and_slope(product(h_two, hidden_in[...]))
    activ[...] = value.astype(low)
    slope[...] = bend
    z_three = z_two + product(activ[...], hidden_out[...])
    queries = out_queries[...]
    decoded = (layer_norm(z_three, gain_three) + product(queries, query_table[...])).astype(low)
    logits = product(decoded, class_table[...])
    at = pl.multiple_of(lax.axis_index("head") * rows, rows)
    mark = marks[:, pl.ds(at, rows)].T
    label, kind, counted = (mark[:, i : i + 1] for i in range(3))
    lane = lax.broadcasted_iota(jnp.int32, (rows, C), 1).astype(jnp.float32)
    is_target = jnp.where(lane == label, 1.0, 0.0)
    row_top = jnp.max(logits, 1, keepdims=True)
    row_lse = row_top + jnp.log(jnp.sum(jnp.exp(logits - row_top), 1, keepdims=True))
    loss = row_lse - jnp.sum(is_target * logits, 1, keepdims=True)
    weight = jnp.zeros((rows, 1), jnp.float32)
    place = lax.broadcasted_iota(jnp.int32, (1, LANES), 1)
    losses = jnp.zeros((1, LANES), jnp.float32)
    for m in range(MODES):
        member = jnp.where((kind == m) & (counted == 1.0), 1.0, 0.0)
        weight = weight + member / jnp.maximum(counts[m], 1.0)
        losses = losses + jnp.where(place == m, jnp.sum(loss * member, 0, keepdims=True), 0.0)
    tile[...] = jnp.broadcast_to(losses, tile.shape)
    dlogits = (weight * (jnp.exp(logits - row_lse) - is_target)).astype(low)
    d_decoded = against(dlogits, class_table[...])
    table_grad = contract_first(queries, d_decoded.astype(low))
    matrix_into(stage_common, 0, table_grad, line)
    query_grad[...] = stage_common[: query_grad.shape[0], :].astype(low)
    d_three, gain_three_grad = norm_pullback(z_three, gain_three, d_decoded)
    d_branch = d_three.astype(low)
    d_pre = (slope[...] * against(d_branch, hidden_out[...])).astype(low)
    d_middle, gain_two_grad = norm_pullback(z_two, gain_two, against(d_pre, hidden_in[...]))
    d_two = d_three + d_middle
    d_two_out[...] = d_two
    gain_grads[...] = jnp.concatenate([gain_two_grad, gain_three_grad], 0)
    d_two_low = d_two.astype(low)
    d_o = against(d_two_low, self_output[...]).astype(low)
    for g in range(n_head):
        dout[g] = d_o[:, g * width : (g + 1) * width]
    for g in range(n_head):
        results = (
            contract_first(o_self[g], d_two_low),
            contract_first(h_two, d_pre[:, g * hidden : (g + 1) * hidden]),
            contract_first(activ[:, g * hidden : (g + 1) * hidden], d_branch),
            contract_first(decoded, dlogits[:, g * classes : (g + 1) * classes]),
        )
        for m, result in zip((4, 5, 6, 7), results):
            matrix_into(stage, starts[m] - first_row, result, line)
        for b in range(shards):
            held[b, g, :shard_rows, :] = stage[pl.ds(b * shard_rows, shard_rows), :].astype(low)
    back = pltpu.make_async_copy(held, grads.at[pl.ds(first_shard, shards)], sems.at[2])
    back.start()
    back.wait()


def middle(counts, weights, common, z_one, o_self, out_queries, marks, gains, n_head, shard_rows):
    rows = z_one.shape[0]
    begin, shards = shards_of(n_head, shard_rows, 4, 8)
    query_rows = DQ * D // LANES
    common_rows = round_up(query_rows, TILE)
    return pl.pallas_call(
        functools.partial(middle_kernel, n_head, shard_rows, begin, rows),
        grid=(1,),
        out_shape=[
            shape_of(o_self.shape),
            shape_of((rows, D), jnp.float32),
            shape_of((8, LANES), jnp.float32),
            shape_of((query_rows, LANES)),
            shape_of((2, D), jnp.float32),
            shape_of(weights.shape),
        ],
        in_specs=[
            SMEM_SPEC,
            ANY_SPEC,
            ANY_SPEC,
            VMEM_SPEC,
            VMEM_SPEC,
            pl.BlockSpec((rows, DQ), lambda i: (lax.axis_index("head"), 0)),
            VMEM_SPEC,
            VMEM_SPEC,
        ],
        out_specs=[VMEM_SPEC] * 5 + [ANY_SPEC],
        scratch_shapes=[
            pltpu.VMEM((shards,) + weights.shape[1:], low),
            pltpu.VMEM((common_rows, LANES), low),
            pltpu.VMEM((shards * shard_rows, LANES), jnp.float32),
            pltpu.VMEM((common_rows, LANES), jnp.float32),
            LINE,
            pltpu.VMEM((D, D), low),
            pltpu.VMEM((D, FF), low),
            pltpu.VMEM((FF, D), low),
            pltpu.VMEM((D, C), low),
            pltpu.VMEM((DQ, D), low),
            pltpu.VMEM((rows, FF), jnp.float32),
            pltpu.VMEM((rows, FF), low),
            pltpu.SemaphoreType.DMA((3,)),
        ],
        compiler_params=pltpu.CompilerParams(vmem_limit_bytes=56 * MIB),
        name="middle",
    )(counts, weights, common, z_one, o_self, out_queries, marks, gains)


def ending_kernel(
    n_head,
    shard_rows,
    rows,
    bounds,
    grads_in,
    d_projected,
    d_two,
    gains,
    gain_grads,
    enc_query,
    enc_keyval,
    enc_output,
    self_project,
    z_zero,
    h_zero,
    x_norm,
    q_enc,
    kv_enc,
    o_enc,
    z_one,
    h_one,
    grads,
    tail_grad,
    held,
    stage,
    stage_common,
    line,
    d_q,
    d_kv,
    sems,
):
    heads = HEADS // n_head
    width = heads * HD
    shards = held.shape[0]
    starts = borders(n_head)
    shared = pltpu.make_async_copy(grads_in.at[pl.ds(shards - 1, 1)], held.at[pl.ds(shards - 1, 1)], sems.at[0])
    shared.start()
    whole = jnp.concatenate([d_projected[g] for g in range(n_head)], 1)
    d_middle, gain_one_grad = norm_pullback(
        z_one[...], gains[1:2, :], against(whole, self_project[...])
    )
    d_one = d_two[...] + d_middle
    d_one_low = d_one.astype(low)
    d_o = against(d_one_low, enc_output[...]).astype(low)
    for g in range(n_head):
        keys = kv_enc[:, 2 * g * width : (2 * g + 1) * width]
        values = kv_enc[:, (2 * g + 1) * width : (2 * g + 2) * width]
        d_key = jnp.zeros(keys.shape, jnp.float32)
        d_value = jnp.zeros(keys.shape, jnp.float32)
        d_query = jnp.zeros((rows, width), jnp.float32)
        for (here, q_head), (unused, do_head) in zip(
            head_lanes(g, heads, q_enc[...]), head_lanes(g, heads, d_o)
        ):
            scores = enc_scores(keys, q_head)
            probs = jnp.exp(scores - jnp.max(scores, 0, keepdims=True))
            probs = probs / jnp.sum(probs, 0, keepdims=True)
            d_probs = against(values, do_head)
            delta = jnp.sum(probs * d_probs, 0, keepdims=True)
            d_scores = (probs * (d_probs - delta)).astype(low)
            d_value = d_value + product(probs.astype(low), do_head)
            d_key = d_key + product(d_scores, q_head)
            d_query = jnp.where(here, contract_first(d_scores, keys), d_query)
        d_q[:, g * width : (g + 1) * width] = (d_query * HD ** (-0.5)).astype(low)
        d_kv[:, 2 * g * width : (2 * g + 1) * width] = (d_key * HD ** (-0.5)).astype(low)
        d_kv[:, (2 * g + 1) * width : (2 * g + 2) * width] = d_value.astype(low)
    d_middle, gain_zero_grad = norm_pullback(
        z_zero[...], gains[0:1, :], against(d_q[...], enc_query[...])
    )
    d_zero = d_one + d_middle
    d_zero_top = d_zero.astype(low)
    d_zero_rest = (d_zero - d_zero_top.astype(jnp.float32)).astype(low)
    picked = picked_rows(bounds, rows, n_head)
    latent_grad = contract_first(picked, d_zero_top) + contract_first(picked, d_zero_rest)
    matrix_into(stage_common, 0, latent_grad, line)
    all_gains = jnp.concatenate([gain_zero_grad, gain_one_grad, gain_grads[...]], 0)
    matrix_into(stage_common, LAT * D // LANES, all_gains, line)
    tail_grad[...] = stage_common[...].astype(low)
    shared.wait()
    kept = shards * shard_rows - starts[4]
    for g in range(n_head):
        results = (
            contract_first(h_zero[...], d_q[:, g * width : (g + 1) * width]),
            contract_first(x_norm[...], d_kv[:, 2 * g * width : (2 * g + 2) * width]),
            contract_first(o_enc[:, g * width : (g + 1) * width], d_one_low),
            contract_first(h_one[...], d_projected[g]),
        )
        if kept:
            stage[pl.ds((shards - 1) * shard_rows, shard_rows), :] = held[
                shards - 1, g, :shard_rows, :
            ].astype(jnp.float32)
        for m, result in zip((0, 1, 2, 3), results):
            matrix_into(stage, starts[m], result, line)
        for b in range(shards):
            held[b, g, :shard_rows, :] = stage[pl.ds(b * shard_rows, shard_rows), :].astype(low)
    back = pltpu.make_async_copy(held, grads.at[pl.ds(0, shards)], sems.at[1])
    back.start()
    back.wait()


def ending(bounds, grads, d_projected, d_two, gains, gain_grads, kept, n_head, shard_rows):
    rows = d_two.shape[0]
    begin, shards = shards_of(n_head, shard_rows, 0, 4)
    keys = kept[6].shape[0]
    tail_rows = (LAT + 4) * D // LANES
    return pl.pallas_call(
        functools.partial(ending_kernel, n_head, shard_rows, rows),
        out_shape=[shape_of(grads.shape), shape_of((tail_rows, LANES))],
        in_specs=[SMEM_SPEC, ANY_SPEC] + [VMEM_SPEC] * 16,
        out_specs=[ANY_SPEC, VMEM_SPEC],
        input_output_aliases={1: 0},
        scratch_shapes=[
            pltpu.VMEM((shards,) + grads.shape[1:], low),
            pltpu.VMEM((shards * shard_rows, LANES), jnp.float32),
            pltpu.VMEM((tail_rows, LANES), jnp.float32),
            LINE,
            pltpu.VMEM((rows, D), low),
            pltpu.VMEM((keys, 2 * D), low),
            pltpu.SemaphoreType.DMA((2,)),
        ],
        compiler_params=pltpu.CompilerParams(vmem_limit_bytes=56 * MIB),
        name="ending",
    )(bounds, grads, d_projected, d_two, gains, gain_grads, *kept)


def adam_step(weight, first, second, grad):
    first = beta_one * first + (1 - beta_one) * grad
    second = beta_two * second + (1 - beta_two) * grad * grad
    fixed_first = first / (1 - beta_one**STEP)
    fixed_second = second / (1 - beta_two**STEP)
    weight = weight - learn_rate * (
        fixed_first / (jnp.sqrt(fixed_second) + adam_eps) + weight_decay * weight
    )
    return (weight, first, second, weight.astype(low))


def per_device(
    inputs,
    out_queries,
    clip_lengths,
    labels,
    modality,
    labeled,
    head_params,
    head_first,
    head_second,
    common_params,
    common_first,
    common_second,
):
    n_head, n_blk = lax.axis_size("head"), lax.axis_size("blk")
    dims = grid_of(n_blk, n_head)
    head_rank = lax.axis_index("head")
    blk_rows = labels.shape[0]
    rows = blk_rows // n_head
    heads_here = HEADS // n_head
    width = heads_here * HD
    n_h, n_c = head_params.shape[0], common_params.shape[0]
    shard_rows = n_h // LANES
    head_rows = round_up(shard_rows + 1, TILE)
    piece_rows = round_up(-(-(-(-n_c // LANES)) // n_head), TILE)

    marks = jnp.stack([labels, modality, labeled] + [jnp.zeros_like(labels)] * 5).astype(jnp.float32)
    mine = lax.dynamic_slice_in_dim(marks, head_rank * rows, rows, 1)
    member = (mine[1][None] == jnp.arange(MODES, dtype=jnp.float32)[:, None]) & (mine[2][None] == 1.0)
    counted = jnp.pad(jnp.sum(member.astype(jnp.float32), 1), (0, LANES - MODES)).astype(low)
    head_low = jnp.concatenate(
        [
            head_params.astype(low).reshape(shard_rows, LANES),
            jnp.broadcast_to(counted[None], (head_rows - shard_rows, LANES)),
        ]
    )
    common_low = jnp.pad(common_params.astype(low), (0, n_head * piece_rows * LANES - n_c))
    common_low = lax.dynamic_slice_in_dim(
        common_low.reshape(n_head * piece_rows, LANES), head_rank * piece_rows, piece_rows, 0
    )
    weights, common = gather_all(dims, (head_low, common_low), 0)
    label_counts = jnp.sum(weights[:, :, shard_rows, :MODES].astype(jnp.float32), (0, 1))
    if n_c % LANES == 0:
        common = common.reshape(n_blk, n_head * piece_rows, LANES)[:, : n_c // LANES]
    else:
        common = common.reshape(n_blk, n_head * piece_rows * LANES)[:, :n_c]
    common = common.reshape(-1, LANES)
    common = jnp.pad(common, ((0, -common.shape[0] % TILE), (0, 0)))

    finish = jnp.cumsum(clip_lengths)
    bounds = jnp.stack([finish - clip_lengths, finish])
    encoded = encode(bounds, weights, common, inputs, rows, n_head, shard_rows)
    gains, z_one = encoded[4], encoded[11]
    q_self, kv_self = spread_rows(dims, encoded[13], encoded[14], 1)
    q_self = q_self.reshape(blk_rows, width)
    kv_self = kv_self.reshape(n_blk * blk_rows, 2 * width)
    out_self, lse_self, out_self_t = attend(bounds, q_self, kv_self, heads_here)
    o_self = swap_heads(dims, out_self.reshape(n_head, rows, width), 2)
    dout, d_two, tile, query_grad, gain_grads, grads = middle(
        label_counts, weights, common, z_one, o_self, out_queries, marks, gains, n_head, shard_rows
    )
    dout = swap_heads(dims, dout, 3).reshape(blk_rows, width)
    d_q, d_kv = attend_back(bounds, q_self, kv_self, dout, out_self_t, lse_self, heads_here)
    d_kv = collect_rows(dims, d_kv.reshape(n_blk, blk_rows, 2 * width), 4)
    d_projected = swap_heads(
        dims, jnp.concatenate([d_q, d_kv], 1).reshape(n_head, rows, 3 * width), 5
    )
    kept = encoded[:4] + encoded[5:13]
    grads, tail_grad = ending(
        bounds, grads, d_projected, d_two, gains, gain_grads, kept, n_head, shard_rows
    )
    common_grad = jnp.concatenate([query_grad, tail_grad])
    space = n_head * piece_rows * LANES
    if n_c % LANES == 0:
        common_grad = jnp.pad(
            common_grad.reshape(n_blk, n_c // LANES, LANES),
            ((0, 0), (0, (space - n_c) // LANES), (0, 0)),
        )
    else:
        common_grad = jnp.pad(common_grad.reshape(n_blk, n_c), ((0, 0), (0, space - n_c)))
    common_grad = common_grad.reshape(n_blk, n_head, piece_rows, LANES)
    head_share, unused, totals, common_share = reduce_all(
        dims, (grads, common_grad), (shard_rows, piece_rows), tile, 6
    )
    clip_norm = jnp.sqrt(totals[0, MODES])
    loss_sums = totals[0, :MODES]
    factor = jnp.minimum(1.0, clip_limit / clip_norm)
    head_share = head_share[:shard_rows].reshape(-1)
    common_share = common_share.reshape(-1)[:n_c].astype(jnp.float32)
    head_out = adam_step(head_params, head_first, head_second, head_share * factor)
    common_out = adam_step(common_params, common_first, common_second, common_share * factor)
    return head_out + common_out + (loss_sums, label_counts, clip_norm)


def solution(mesh):
    placed = (
        P("blk", None),
        P("blk", None),
        P(),
        P("blk"),
        P("blk"),
        P("blk"),
        P(("head", "blk")),
        P(("head", "blk")),
        P(("head", "blk")),
        P("blk"),
        P("blk"),
        P("blk"),
    )
    return jax.shard_map(
        per_device,
        mesh=mesh,
        in_specs=placed,
        out_specs=(
            P(("head", "blk")),
            P(("head", "blk")),
            P(("head", "blk")),
            P(("head", "blk")),
            P("blk"),
            P("blk"),
            P("blk"),
            P("blk"),
            P(),
            P(),
            P(),
        ),
        check_vma=False,
    )
```

```python
import functools

import jax
import jax.numpy as jnp
from jax import lax
from jax.experimental import pallas as pl
from jax.experimental.pallas import tpu as pltpu
from jax.sharding import PartitionSpec as P

D = 512
HEADS = 8
HD = 64
FF = 2048
DI = 704
DQ = 1026
C = 704
LAT = 784
MODES = 3
STEP = 10
LANES = 128
TILE = 16

norm_eps = 1e-05
learn_rate = 0.1
beta_one = 0.9
beta_two = 0.999
adam_eps = 1e-08
weight_decay = 0.01
clip_limit = 0.05
big_negative = -1e30
low = jnp.bfloat16
MESH = pl.DeviceIdType.MESH
MIB = 1 << 20
VMEM_SPEC = pl.BlockSpec(memory_space=pltpu.VMEM)
SMEM_SPEC = pl.BlockSpec(memory_space=pltpu.SMEM)
ANY_SPEC = pl.BlockSpec(memory_space=pl.ANY)


def round_up(n, unit):
    return -(-n // unit) * unit


def grid_of(n_blk, n_head):
    cores = 2 if n_head % 2 == 0 else 1
    x = n_head // cores
    y = x if n_blk % x == 0 else 1
    return (n_blk // y, y, x, cores)


def my_place(dims):
    blk, head = lax.axis_index("blk"), lax.axis_index("head")
    return (blk // dims[1], lax.rem(blk, dims[1]), head // dims[3], lax.rem(head, dims[3]))


def shifted(dims, me, offset, sign):
    return tuple(
        m if o == 0 else lax.rem(m + (o if sign > 0 else n - o), n)
        for m, o, n in zip(me, offset, dims)
    )


def blk_of(dims, place):
    return place[0] * dims[1] + place[1]


def head_of(dims, place):
    return place[2] * dims[3] + place[3]


def device_of(dims, place):
    return {"blk": blk_of(dims, place), "head": head_of(dims, place)}


def along(axis, d):
    return tuple(d if a == axis else 0 for a in range(4))


def greet(dims, me, offsets):
    barrier = pltpu.get_barrier_semaphore()
    for offset in offsets:
        pl.semaphore_signal(
            barrier,
            inc=1,
            device_id=device_of(dims, shifted(dims, me, offset, 1)),
            device_id_type=MESH,
        )
    pl.semaphore_wait(barrier, len(offsets))


def axis_peers(dims, axes):
    return [along(axis, d) for axis in axes for d in range(1, dims[axis])]


def remote(src, dst, send_sem, recv_sem, place, dims):
    return pltpu.make_async_remote_copy(
        src_ref=src,
        dst_ref=dst,
        send_sem=send_sem,
        recv_sem=recv_sem,
        device_id=device_of(dims, place),
        device_id_type=MESH,
    )


def gather_plan(dims, parts):
    plan = []
    for position in range(4):
        for p, (array, first, rows, order) in enumerate(parts):
            axis = order[position]
            done = order[:position]
            offsets = [(0, 0, 0, 0)]
            for a in done:
                offsets = [
                    tuple(d if i == a else o[i] for i in range(4))
                    for d in range(dims[a])
                    for o in offsets
                ]
            for d in range(1, dims[axis]):
                for o in offsets:
                    plan.append((p, tuple(d if i == axis else o[i] for i in range(4)), position))
    return plan


def gather_kernel(dims, parts, count, *refs):
    srcs, outs = refs[:count], refs[count : 2 * count]
    send_sem, recv_sem, own_sem = refs[2 * count :]
    me = my_place(dims)
    plan = gather_plan(dims, parts)
    number = {(p, offset): i for i, (p, offset, position) in enumerate(plan)}
    axes = [a for a in range(4) if dims[a] > 1]
    greet(dims, me, axis_peers(dims, axes))
    started = []

    def block(p, offset):
        place = shifted(dims, me, offset, -1)
        array, first, rows, order = parts[p]
        return outs[array].at[blk_of(dims, place), head_of(dims, place), pl.ds(first, rows)]

    def forward(p, offset, position):
        array, first, rows, order = parts[p]
        source = srcs[array].at[pl.ds(first, rows)] if position < 0 else block(p, offset)
        for axis in order[position + 1 :]:
            for d in range(1, dims[axis]):
                i = number[(p, tuple(d if a == axis else offset[a] for a in range(4)))]
                copy = remote(
                    source,
                    block(p, offset),
                    send_sem.at[i],
                    recv_sem.at[i],
                    shifted(dims, me, along(axis, d), 1),
                    dims,
                )
                copy.start()
                started.append(copy)

    for p in range(len(parts)):
        forward(p, (0, 0, 0, 0), -1)
    own = []
    for array in range(count):
        copy = pltpu.make_async_copy(
            srcs[array], outs[array].at[blk_of(dims, me), head_of(dims, me)], own_sem.at[array]
        )
        copy.start()
        own.append(copy)
    for i, (p, offset, position) in enumerate(plan):
        landed = block(p, offset)
        axis = parts[p][3][position]
        remote(
            landed,
            landed,
            send_sem.at[i],
            recv_sem.at[i],
            shifted(dims, me, along(axis, offset[axis]), -1),
            dims,
        ).wait_recv()
        forward(p, offset, position)
    for copy in started:
        copy.wait_send()
    for copy in own:
        copy.wait()


def halves(array, rows, orders):
    first = rows // 2 // TILE * TILE
    return ((array, 0, first, orders[0]), (array, first, rows - first, orders[1]))


def gather_all(dims, shards, collective_id):
    parts = halves(0, shards[0].shape[0], ((0, 1, 2, 3), (0, 2, 1, 3))) + (
        (1, 0, shards[1].shape[0], (0, 2, 1, 3)),
    )
    count = len(gather_plan(dims, parts))
    z, y, x, cores = dims
    any_space = pl.BlockSpec(memory_space=pl.ANY)
    return pl.pallas_call(
        functools.partial(gather_kernel, dims, parts, len(shards)),
        out_shape=[
            jax.ShapeDtypeStruct((z * y, x * cores) + shard.shape, shard.dtype) for shard in shards
        ],
        in_specs=[any_space] * len(shards),
        out_specs=[any_space] * len(shards),
        scratch_shapes=[
            pltpu.SemaphoreType.DMA((count,)),
            pltpu.SemaphoreType.DMA((count,)),
            pltpu.SemaphoreType.DMA((len(shards),)),
        ],
        compiler_params=pltpu.CompilerParams(collective_id=collective_id, has_side_effects=True),
        name="gather_weights",
    )(*shards)


def reduce_plan(dims, order):
    stages = []
    for position, axis in enumerate(order):
        rest = order[position + 1 :]
        offsets = [(0, 0, 0, 0)]
        for a in reversed(rest):
            offsets = [
                tuple(d if i == a else o[i] for i in range(4))
                for d in list(range(1, dims[a])) + [0]
                for o in offsets
            ]
        stages.append((axis, offsets))
    return stages


def reduce_kernel(dims, parts, chunk, valid, *refs):
    count = len(valid)
    srcs, tile = refs[:count], refs[count]
    outs, totals, shares = refs[count + 1 : 2 * count + 1], refs[2 * count + 1], refs[2 * count + 2]
    scratch = refs[2 * count + 3 :]
    me = my_place(dims)
    z, y, x, cores = dims
    places = len(parts) * 4
    buffers = scratch[:places]
    send_sem, recv_sem, near_tiles, far_tiles = scratch[places : places + 4]
    axes = [a for a in range(4) if dims[a] > 1]
    across = [(0, 0, a, c) for a in range(x) for c in range(cores) if (a, c) != (0, 0)]
    others = [(a, b, 0, 0) for a in range(z) for b in range(y) if (a, b) != (0, 0)]
    greet(dims, me, axis_peers(dims, axes) + [o for o in across + others if sum(v != 0 for v in o) > 1])
    started = []
    pending = {}

    def push(src, dst, offset):
        i = len(started)
        copy = remote(src, dst, send_sem.at[i], recv_sem.at[i], shifted(dims, me, offset, 1), dims)
        copy.start()
        started.append(copy)
        return copy

    stages = [reduce_plan(dims, part[3]) for part in parts]

    def source(p, position, offset):
        array, first, rows, order = parts[p]
        if position == 0:
            place = shifted(dims, me, offset, 1)
            return srcs[array].at[blk_of(dims, place), head_of(dims, place), pl.ds(first, rows)]
        k = stages[p][position - 1][1].index(offset)
        return buffers[p * 4 + position - 1].at[k, 0]

    def send(p, position, k, d):
        axis, offsets = stages[p][position]
        there = tuple(d if a == axis else offsets[k][a] for a in range(4))
        pending[(p, position, k, d)] = push(
            source(p, position, there), buffers[p * 4 + position].at[k, d - 1], along(axis, d)
        )

    def add(p, position, k):
        array, first, rows, order = parts[p]
        axis, offsets = stages[p][position]
        for d in range(1, dims[axis]):
            pending[(p, position, k, d)].wait_recv()
        mine = source(p, position, offsets[k])
        arrived = buffers[p * 4 + position]
        step = chunk(rows)
        last = position == 3

        @pl.loop(0, rows // step)
        def some_rows(n):
            at = pl.ds(pl.multiple_of(n * step, step), step)
            total = mine[at].astype(jnp.float32)
            for d in range(1, dims[axis]):
                total = total + arrived[k, d - 1, at].astype(jnp.float32)
            if last:
                outs[array][pl.ds(pl.multiple_of(first + n * step, TILE), step)] = total
            else:
                arrived[k, 0, at] = total.astype(low)

    for k in range(len(stages[0][0][1])):
        for p in range(len(parts)):
            for d in range(1, dims[stages[p][0][0]]):
                send(p, 0, k, d)
    for position in range(4):
        for k in range(len(stages[0][position][1])):
            for p in range(len(parts)):
                add(p, position, k)
                if position < 3:
                    axis, offsets = stages[p][position + 1]
                    offset = stages[p][position][1][k]
                    rest = tuple(0 if a == axis else offset[a] for a in range(4))
                    if offset[axis]:
                        send(p, position + 1, offsets.index(rest), offset[axis])
    my_head, my_blk = head_of(dims, me), blk_of(dims, me)
    shares[my_head] = outs[count - 1][...].astype(low)
    share_copies = [push(shares.at[my_head], shares.at[my_head], o) for o in across]
    squares = jnp.zeros((1, LANES), jnp.float32)
    for out, amount in zip(outs, valid):
        squares = squares + jnp.sum(out[:amount] * out[:amount], 0, keepdims=True)
    lane = lax.broadcasted_iota(jnp.int32, (1, LANES), 1)
    near_tiles[my_head] = tile[...] + jnp.where(
        lane == MODES, jnp.sum(squares, 1, keepdims=True), 0.0
    )
    near = [push(near_tiles.at[my_head], near_tiles.at[my_head], o) for o in across]
    for copy in near:
        copy.wait_recv()
    far_tiles[my_blk] = jnp.sum(near_tiles[...], 0)
    far = [push(far_tiles.at[my_blk], far_tiles.at[my_blk], o) for o in others]
    for copy in far:
        copy.wait_recv()
    totals[...] = jnp.sum(far_tiles[...], 0)
    for copy in share_copies:
        copy.wait_recv()
    for copy in started:
        copy.wait_send()


def row_chunk(rows):
    for count in (4, 3, 2):
        if rows % (count * TILE) == 0:
            return rows // count
    return rows


def reduce_all(dims, arrays, valid, tile, collective_id):
    z, y, x, cores = dims
    parts = halves(0, arrays[0].shape[2], ((3, 2, 1, 0), (3, 1, 2, 0))) + (
        (1, 0, arrays[1].shape[2], (3, 1, 2, 0)),
    )
    scratch = []
    count = 2 * (x * cores - 1) + z * y - 1
    for array, start, amount, order in parts:
        for axis, offsets in reduce_plan(dims, order):
            others = max(dims[axis] - 1, 1)
            count += len(offsets) * (dims[axis] - 1)
            scratch.append(pltpu.VMEM((len(offsets), others, amount, LANES), low))
    vmem = pl.BlockSpec(memory_space=pltpu.VMEM)
    last_rows = arrays[-1].shape[2]
    return pl.pallas_call(
        functools.partial(reduce_kernel, dims, parts, row_chunk, valid),
        out_shape=[jax.ShapeDtypeStruct(array.shape[2:], jnp.float32) for array in arrays]
        + [
            jax.ShapeDtypeStruct((8, LANES), jnp.float32),
            jax.ShapeDtypeStruct((x * cores, last_rows, LANES), low),
        ],
        in_specs=[vmem] * (len(arrays) + 1),
        out_specs=[vmem] * (len(arrays) + 2),
        scratch_shapes=scratch
        + [
            pltpu.SemaphoreType.DMA((count,)),
            pltpu.SemaphoreType.DMA((count,)),
            pltpu.VMEM((x * cores, 8, LANES), jnp.float32),
            pltpu.VMEM((z * y, 8, LANES), jnp.float32),
        ],
        compiler_params=pltpu.CompilerParams(
            collective_id=collective_id, has_side_effects=True, vmem_limit_bytes=56 * MIB
        ),
        name="reduce_gradients",
    )(*arrays, tile)


def contract_first(a, b):
    return lax.dot_general(a, b, (((0,), (0,)), ((), ())), preferred_element_type=jnp.float32)


def product(a, b):
    return jnp.dot(a, b, preferred_element_type=jnp.float32)


def against(a, b):
    return lax.dot_general(a, b, (((1,), (1,)), ((), ())), preferred_element_type=jnp.float32)


def clip_borders(bounds, place):
    opening = jnp.zeros(place.shape, jnp.int32)
    ending = jnp.full(place.shape, 1 << 30, jnp.int32)
    for clip in range(bounds.shape[1]):
        here = place == clip
        opening = jnp.where(here, bounds[0, clip], opening)
        ending = jnp.where(here, bounds[1, clip], ending)
    return opening, ending


def lane_of_tail(a):
    return HD if a % 2 == 0 else 0


def in_head(a, axis):
    shape = (1, LANES) if axis else (LANES, 1)
    lane = lax.broadcasted_iota(jnp.int32, shape, axis)
    return (lane >= a * HD) & (lane < (a + 1) * HD)


def all_lanes(block, first, width):
    piece = block[:, first : first + width]
    if width < LANES:
        piece = jnp.concatenate([piece, jnp.zeros((piece.shape[0], LANES - width), piece.dtype)], 1)
    return piece


def with_key_tail(bounds, a, first_row, columns):
    clips = bounds.shape[1]
    place = lax.broadcasted_iota(jnp.int32, (1, LANES), 1) - lane_of_tail(a)
    opening, ending = clip_borders(bounds, place)
    ones = jnp.where((place >= clips) & (place < clips + 3), 1.0, 0.0)
    row = first_row + lax.broadcasted_iota(jnp.int32, columns.shape, 0)
    tail = jnp.where((row >= opening) & (row < ending), ones, big_negative)
    return jnp.where(in_head(a, 1), columns.astype(jnp.float32), tail).astype(low)


def in_three(place, value):
    top = value.astype(low).astype(jnp.float32)
    middle = (value - top).astype(low).astype(jnp.float32)
    bottom = value - top - middle
    return (
        jnp.where(place == 0, top, 0.0)
        + jnp.where(place == 1, middle, 0.0)
        + jnp.where(place == 2, bottom, 0.0)
    )


def with_tail(a, rows, tail):
    return jnp.concatenate([rows, tail] if lane_of_tail(a) else [tail, rows], 0)


def with_query_tail(bounds, a, first_row, rows, extra):
    clips = bounds.shape[1]
    place = lax.broadcasted_iota(jnp.int32, (HD, 1), 0)
    opening, ending = clip_borders(bounds, place)
    row = first_row + lax.broadcasted_iota(jnp.int32, (1, rows.shape[1]), 1)
    inside = (place < clips) & (row >= opening) & (row < ending)
    tail = jnp.where(inside, 1.0, 0.0)
    if extra is not None:
        tail = tail + in_three(place - clips, -extra)
    return with_tail(a, rows * HD ** (-0.5), tail).astype(low)


class Pushes:
    def __init__(self, dims, me, send_sem, recv_sem):
        self.dims, self.me, self.send_sem, self.recv_sem = dims, me, send_sem, recv_sem
        self.started = []

    def __call__(self, src, dst, offset):
        i = len(self.started)
        place = shifted(self.dims, self.me, offset, 1)
        copy = remote(src, dst, self.send_sem.at[i], self.recv_sem.at[i], place, self.dims)
        copy.start()
        self.started.append(copy)
        return copy

    def finish(self):
        for copy in self.started:
            copy.wait_send()


def peers_across(dims):
    z, y, x, cores = dims
    across = [(0, 0, a, c) for a in range(x) for c in range(cores) if (a, c) != (0, 0)]
    return sorted(across, key=lambda o: (o[2] == 0, o[3]))


def ring_and_sides(dims):
    z = dims[0]
    ring = sorted({along(0, 1 % z), along(0, (z - 1) % z)} - {(0, 0, 0, 0)})
    return ring + axis_peers(dims, (1,))


def attend_kernel(
    dims,
    heads,
    key_step,
    query_step,
    bounds,
    q_in,
    kv_in,
    o_out,
    lse,
    out_t,
    q_all,
    kv_all,
    keys,
    values_t,
    queries,
    top,
    accum,
    o_mine,
    send_sem,
    recv_sem,
    own_sem,
):
    z, y, x, cores = dims
    me = my_place(dims)
    n_head = x * cores
    rows, width = q_in.shape[1], heads * HD
    amount = n_head * rows
    my_blk, my_head = blk_of(dims, me), head_of(dims, me)
    across = peers_across(dims)
    sides = axis_peers(dims, (1,))
    greet(dims, me, across + ring_and_sides(dims))
    push = Pushes(dims, me, send_sem, recv_sem)
    own_kv = pltpu.make_async_copy(kv_in.at[my_head], kv_all.at[my_blk, my_head], own_sem.at[0])
    own_q = pltpu.make_async_copy(q_in.at[my_head], q_all.at[my_head], own_sem.at[1])
    own_kv.start()
    own_q.start()

    def to_head(src, dst, o):
        return push(src.at[head_of(dims, shifted(dims, me, o, 1))], dst, o)

    kv_copies = {o: to_head(kv_in, kv_all.at[my_blk, my_head], o) for o in across}
    q_copies = [to_head(q_in, q_all.at[my_head], o) for o in across]
    ring, side = {}, {}
    pieces = [(0, 0, 0, 0)] + across[::-1]

    def send_on(s, n):
        block = kv_all.at[
            blk_of(dims, shifted(dims, me, along(0, s), -1)),
            head_of(dims, shifted(dims, me, pieces[n], -1)),
        ]
        if s < z - 1:
            ring[(s + 1, n)] = push(block, block, along(0, 1))
        for o in sides:
            side[(s, n, o)] = push(block, block, o)

    def compute(offset):
        blk = blk_of(dims, shifted(dims, me, offset, -1))

        @pl.loop(0, n_head)
        def build(h):
            at = pl.ds(pl.multiple_of(h * rows, rows), rows)
            block = kv_all[blk, h]
            k_block, v_block = all_lanes(block, 0, width), all_lanes(block, width, width)
            v_t = v_block.astype(jnp.float32).T
            for a in range(heads):
                keys[a, at, :] = with_key_tail(bounds, a, blk * amount + h * rows, k_block)
                values_t[a, :HD, at] = v_t[a * HD : (a + 1) * HD].astype(low)

        @pl.loop(0, amount // query_step)
        def query_block(n):
            at = pl.ds(pl.multiple_of(n * query_step, query_step), query_step)
            for a in range(heads):
                query = queries[a, :, at]
                highest = jnp.full((8, query_step), -1e38, jnp.float32)
                for k in range(0, amount, key_step):
                    scores = product(keys[a, k : k + key_step, :], query)
                    highest = jnp.maximum(
                        highest, jnp.max(scores.reshape(key_step // 8, 8, query_step), 0)
                    )
                old = top[a, :, at]
                new = jnp.maximum(old, jnp.max(highest, 0, keepdims=True))
                top[a, :, at] = new
                total = accum[a, :, at] * jnp.exp(old - new)
                for k in range(0, amount, key_step):
                    scores = product(keys[a, k : k + key_step, :], query)
                    probs = jnp.exp(scores - new).astype(low)
                    total = total + product(values_t[a, :, k : k + key_step], probs)
                accum[a, :, at] = total

    for a in range(heads):
        values_t[a, HD:, :] = jnp.ones((values_t.shape[1] - HD, amount), low)
        top[a] = jnp.full((1, amount), -1e38, jnp.float32)
        accum[a] = jnp.zeros(accum.shape[1:], jnp.float32)
    own_kv.wait()
    send_on(0, 0)
    for n in range(1, n_head):
        kv_copies[pieces[n]].wait_recv()
        send_on(0, n)
    own_q.wait()
    for copy in q_copies:
        copy.wait_recv()
    for a in range(heads):
        for h in range(n_head):
            q_t = all_lanes(q_all[h], 0, width).astype(jnp.float32).T
            queries[a, :, h * rows : (h + 1) * rows] = with_query_tail(
                bounds, a, my_blk * amount + h * rows, q_t[a * HD : (a + 1) * HD], None
            )
    compute((0, 0, 0, 0))
    for s in range(1, z + 1):
        if s < z:
            for n in range(n_head):
                ring[(s, n)].wait_recv()
                send_on(s, n)
            compute(along(0, s))
        for o in sides:
            for n in range(n_head):
                side[(s - 1, n, o)].wait_recv()
            compute((s - 1, o[1], 0, 0))
    for a in range(heads):
        total = accum[a, HD : HD + 1, :]
        out_t[a * HD : (a + 1) * HD, :] = accum[a, :HD, :] / total
        lse[a : a + 1, :] = top[a] + jnp.log(total)
    for h in range(n_head):
        o_mine[h] = out_t[:, h * rows : (h + 1) * rows].T.astype(low)
    o_copies = [to_head(o_mine, o_out.at[my_head], o) for o in across]
    own_o = pltpu.make_async_copy(o_mine.at[my_head], o_out.at[my_head], own_sem.at[2])
    own_o.start()
    own_o.wait()
    for copy in o_copies:
        copy.wait_recv()
    push.finish()


def attend(dims, bounds, q, kv, heads, collective_id):
    z, y, x, cores = dims
    n_head, rows, width = q.shape
    amount = n_head * rows
    count = 3 * (n_head - 1) + n_head * (z - 1 + z * (y - 1))
    return pl.pallas_call(
        functools.partial(attend_kernel, dims, heads, 256, 256),
        out_shape=(
            jax.ShapeDtypeStruct(q.shape, low),
            jax.ShapeDtypeStruct((heads, amount), jnp.float32),
            jax.ShapeDtypeStruct((width, amount), jnp.float32),
            jax.ShapeDtypeStruct(q.shape, low),
            jax.ShapeDtypeStruct((z * y,) + kv.shape, low),
        ),
        in_specs=[SMEM_SPEC, VMEM_SPEC, VMEM_SPEC],
        out_specs=[VMEM_SPEC] * 5,
        scratch_shapes=[
            pltpu.VMEM((heads, amount, LANES), low),
            pltpu.VMEM((heads, HD + TILE, amount), low),
            pltpu.VMEM((heads, LANES, amount), low),
            pltpu.VMEM((heads, 1, amount), jnp.float32),
            pltpu.VMEM((heads, HD + TILE, amount), jnp.float32),
            pltpu.VMEM(q.shape, low),
            pltpu.SemaphoreType.DMA((count,)),
            pltpu.SemaphoreType.DMA((count,)),
            pltpu.SemaphoreType.DMA((3,)),
        ],
        compiler_params=pltpu.CompilerParams(
            collective_id=collective_id, has_side_effects=True, vmem_limit_bytes=56 * MIB
        ),
        name="attend",
    )(bounds, q, kv)


def attend_back_kernel(
    dims,
    heads,
    key_step,
    bounds,
    q_all,
    kv_all,
    do_in,
    out_t,
    lse,
    d_q_out,
    d_kv_out,
    do_all,
    keys,
    keys_t,
    values,
    queries,
    douts,
    d_q_t,
    q_rows,
    do_rows,
    side_out,
    side_in,
    ring_out,
    ring_in,
    mine,
    d_q_mine,
    d_kv_mine,
    send_sem,
    recv_sem,
    own_sem,
):
    z, y, x, cores = dims
    me = my_place(dims)
    n_head, rows, width = q_all.shape
    amount = n_head * rows
    my_blk, my_head = blk_of(dims, me), head_of(dims, me)
    across = peers_across(dims)
    sides = axis_peers(dims, (1,))
    greet(dims, me, across + ring_and_sides(dims))
    push = Pushes(dims, me, send_sem, recv_sem)

    def to_head(src, dst, o):
        return push(src.at[head_of(dims, shifted(dims, me, o, 1))], dst, o)

    do_copies = [to_head(do_in, do_all.at[my_head], o) for o in across]
    own_do = pltpu.make_async_copy(do_in.at[my_head], do_all.at[my_head], own_sem.at[0])
    own_do.start()
    place = lax.broadcasted_iota(jnp.int32, (HD, 1), 0)

    def at_head(h):
        return slice(h * rows, (h + 1) * rows)

    for h in range(n_head):
        block = all_lanes(q_all[h], 0, width).astype(jnp.float32)
        q_t = block.T
        for a in range(heads):
            queries[a, :, at_head(h)] = with_query_tail(
                bounds,
                a,
                my_blk * amount + h * rows,
                q_t[a * HD : (a + 1) * HD],
                lse[a : a + 1, at_head(h)],
            )
            q_rows[a, at_head(h), :] = jnp.where(in_head(a, 1), block * HD ** (-0.5), 0.0).astype(low)
    for a in range(heads):
        d_q_t[a] = jnp.zeros(d_q_t.shape[1:], jnp.float32)
    own_do.wait()
    for copy in do_copies:
        copy.wait_recv()
    for h in range(n_head):
        block = all_lanes(do_all[h], 0, width).astype(jnp.float32)
        do_t = block.T
        for a in range(heads):
            part = do_t[a * HD : (a + 1) * HD]
            delta = jnp.sum(part * out_t[a * HD : (a + 1) * HD, at_head(h)], 0, keepdims=True)
            douts[a, :, at_head(h)] = with_tail(a, part, in_three(place, -delta)).astype(low)
            do_rows[a, at_head(h), :] = jnp.where(in_head(a, 1), block, 0.0).astype(low)

    def compute(offset, target):
        blk = blk_of(dims, shifted(dims, me, offset, 1))

        @pl.loop(0, n_head)
        def build(h):
            at = pl.ds(pl.multiple_of(h * rows, rows), rows)
            block = kv_all[blk, h]
            k_block, v_block = all_lanes(block, 0, width), all_lanes(block, width, width)
            k_t = k_block.astype(jnp.float32).T
            lane = lax.broadcasted_iota(jnp.int32, (1, LANES), 1)
            for a in range(heads):
                keys[a, at, :] = with_key_tail(bounds, a, blk * amount + h * rows, k_block)
                keys_t[a, :, at] = k_t[a * HD : (a + 1) * HD].astype(low)
                tail = lane - lane_of_tail(a)
                ones = jnp.where((tail >= 0) & (tail < 3), 1.0, 0.0)
                values[a, at, :] = jnp.where(
                    in_head(a, 1), v_block.astype(jnp.float32), ones
                ).astype(low)

        @pl.loop(0, amount // key_step)
        def key_block(k):
            at = pl.ds(pl.multiple_of(k * key_step, key_step), key_step)
            d_key = jnp.zeros((key_step, LANES), jnp.float32)
            d_value = jnp.zeros((key_step, LANES), jnp.float32)
            for a in range(heads):
                probs = jnp.exp(product(keys[a, at, :], queries[a]))
                d_probs = product(values[a, at, :], douts[a])
                d_scores = (probs * d_probs).astype(low)
                d_value = d_value + product(probs.astype(low), do_rows[a])
                d_key = d_key + product(d_scores, q_rows[a])
                d_q_t[a] = d_q_t[a] + product(keys_t[a, :, at], d_scores)
            target[at, :] = jnp.concatenate([d_key[:, :width], d_value[:, :width]], 1).astype(
                target.dtype
            )

    side, ring = {}, {}

    def send_sides(s):
        for o in sides:
            compute((z - s, o[1], 0, 0), side_out.at[s - 1, o[1] - 1])
            side[(s, o)] = push(side_out.at[s - 1, o[1] - 1], side_in.at[s - 1, o[1] - 1], o)

    def combine(s):
        for o in sides:
            side[(s, o)].wait_recv()
        if s > 1:
            ring[s - 1].wait_recv()

        for h in range(n_head):
            total = mine[(s - 1) % 2, at_head(h), :]
            for o in sides:
                total = total + side_in[s - 1, o[1] - 1, at_head(h), :].astype(jnp.float32)
            if s > 1:
                total = total + ring_in[s - 2, at_head(h), :].astype(jnp.float32)
            if s < z:
                ring_out[s - 1, at_head(h), :] = total.astype(low)
            else:
                d_kv_mine[h] = total.astype(low)
        if s < z:
            ring[s] = push(ring_out.at[s - 1], ring_in.at[s - 1], along(0, 1))

    for s in range(1, z + 1):
        send_sides(s)
        if s > 1:
            combine(s - 1)
        compute((z - s if s < z else 0, 0, 0, 0), mine.at[(s - 1) % 2])
    for h in range(n_head):
        block = jnp.concatenate([d_q_t[a, :, at_head(h)] for a in range(heads)], 0) * HD ** (-0.5)
        d_q_mine[h] = block.T.astype(low)
    copies = [to_head(d_q_mine, d_q_out.at[my_head], o) for o in across]
    own_q = pltpu.make_async_copy(d_q_mine.at[my_head], d_q_out.at[my_head], own_sem.at[1])
    own_q.start()
    combine(z)
    copies += [to_head(d_kv_mine, d_kv_out.at[my_head], o) for o in across]
    own_kv = pltpu.make_async_copy(d_kv_mine.at[my_head], d_kv_out.at[my_head], own_sem.at[2])
    own_kv.start()
    own_q.wait()
    own_kv.wait()
    for copy in copies:
        copy.wait_recv()
    push.finish()


def attend_back(dims, bounds, q, kv, dout, out_t, lse, heads, collective_id):
    z, y, x, cores = dims
    n_head, rows, width = q.shape
    amount = n_head * rows
    count = 3 * (n_head - 1) + z * (y - 1) + z - 1
    block = (amount, 2 * width)
    others = max(y - 1, 1)
    return pl.pallas_call(
        functools.partial(attend_back_kernel, dims, heads, 256),
        out_shape=(
            jax.ShapeDtypeStruct(q.shape, low),
            jax.ShapeDtypeStruct((n_head, rows, 2 * width), low),
        ),
        in_specs=[SMEM_SPEC] + [VMEM_SPEC] * 5,
        out_specs=[VMEM_SPEC] * 2,
        scratch_shapes=[
            pltpu.VMEM(q.shape, low),
            pltpu.VMEM((heads, amount, LANES), low),
            pltpu.VMEM((heads, HD, amount), low),
            pltpu.VMEM((heads, amount, LANES), low),
            pltpu.VMEM((heads, LANES, amount), low),
            pltpu.VMEM((heads, LANES, amount), low),
            pltpu.VMEM((heads, HD, amount), jnp.float32),
            pltpu.VMEM((heads, amount, LANES), low),
            pltpu.VMEM((heads, amount, LANES), low),
            pltpu.VMEM((z, others) + block, low),
            pltpu.VMEM((z, others) + block, low),
            pltpu.VMEM((max(z - 1, 1),) + block, low),
            pltpu.VMEM((max(z - 1, 1),) + block, low),
            pltpu.VMEM((2,) + block, jnp.float32),
            pltpu.VMEM(q.shape, low),
            pltpu.VMEM((n_head, rows, 2 * width), low),
            pltpu.SemaphoreType.DMA((count,)),
            pltpu.SemaphoreType.DMA((count,)),
            pltpu.SemaphoreType.DMA((3,)),
        ],
        compiler_params=pltpu.CompilerParams(
            collective_id=collective_id, has_side_effects=True, vmem_limit_bytes=60 * MIB
        ),
        name="attend_back",
    )(bounds, q, kv, dout, out_t, lse)


def part_shapes(n_head):
    width = HEADS // n_head * HD
    hidden = FF // n_head
    return (
        (D, width, True),
        (DI, 2 * width, True),
        (width, D, False),
        (D, 3 * width, True),
        (width, D, False),
        (D, hidden, True),
        (hidden, D, False),
        (D, C // n_head, True),
    )


def borders(n_head):
    result = [0]
    for rows, columns, joined in part_shapes(n_head):
        result.append(result[-1] + rows * columns // LANES)
    return result


def period(columns):
    amount = 1
    while amount * columns % LANES:
        amount *= 2
    return amount


def segments(start, amount, unit):
    result = []
    while amount > 0:
        which, at = divmod(start, unit)
        size = min(unit - at, amount)
        result.append((which, at, at + size))
        start, amount = start + size, amount - size
    return result


def joined_lanes(pieces):
    return pieces[0] if len(pieces) == 1 else jnp.concatenate(pieces, 1)


def lane_blocks(value):
    rows, columns = value.shape
    missing = -columns % LANES
    if missing:
        value = jnp.concatenate([value, jnp.zeros((rows, missing), value.dtype)], 1)
    return [value[:, i : i + LANES] for i in range(0, columns + missing, LANES)]


def every(first, amount, stride):
    return pl.ds(first, amount) if stride == 1 else pl.ds(first, amount, stride=stride)


def matrix_of(stage, first, rows, columns, line):
    if columns % LANES == 0:
        stride = columns // LANES
        for j in range(stride):
            yield j * LANES, stage[every(first + j, rows, stride), :]
        return
    height = period(columns)
    stride = height * columns // LANES
    for k in range(height):
        pieces = [
            stage[every(first + which, rows // height, stride), :][:, begin:end]
            for which, begin, end in segments(k * columns, columns, LANES)
        ]
        for i, piece in enumerate(lane_blocks(joined_lanes(pieces))):
            line[i, every(k, rows // height, height), :] = piece
    for i in range(-(-columns // LANES)):
        yield i * LANES, line[i, :rows, : min(columns - i * LANES, LANES)]


def matrix_into(stage, first, value, line):
    rows, columns = value.shape
    if columns % LANES == 0:
        stride = columns // LANES
        for j in range(stride):
            stage[every(first + j, rows, stride), :] = value[:, j * LANES : (j + 1) * LANES]
        return
    height = period(columns)
    stride = height * columns // LANES
    for i, piece in enumerate(lane_blocks(value)):
        line[i, :rows, :] = piece
    for i in range(stride):
        pieces = [
            line[which, every(k, rows // height, height), :][:, begin:end]
            for k, first_lane, last_lane in segments(i * LANES, LANES, columns)
            for which, begin, end in segments(first_lane, last_lane - first_lane, LANES)
        ]
        stage[every(first + i, rows // height, stride), :] = joined_lanes(pieces)


def load_stage(stage, held, first_shard, shard_rows, group):
    for b in range(held.shape[0]):
        stage[pl.ds(b * shard_rows, shard_rows), :] = held[b, group, :shard_rows, :].astype(jnp.float32)


def load_matrices(stage, first_row, n_head, group, which, targets, line):
    starts, shapes = borders(n_head), part_shapes(n_head)
    for m, target in zip(which, targets):
        rows, columns, joined = shapes[m]
        row = 0 if joined else group * rows
        column = group * columns if joined else 0
        for j, value in matrix_of(stage, starts[m] - first_row, rows, columns, line):
            size = value.shape[1]
            target[row : row + rows, column + j : column + j + size] = value.astype(target.dtype)


def normalized(x):
    centre = x - jnp.mean(x, -1, keepdims=True)
    rate = lax.rsqrt(jnp.mean(centre * centre, -1, keepdims=True) + norm_eps)
    return centre * rate, rate


def layer_norm(x, gain):
    return normalized(x)[0] * gain


def norm_pullback(x, gain, grad):
    unit, rate = normalized(x)
    inside = grad * gain
    both = jnp.mean(inside * unit, -1, keepdims=True)
    d_x = rate * (inside - jnp.mean(inside, -1, keepdims=True) - unit * both)
    return d_x, jnp.sum(grad * unit, 0, keepdims=True)


def head_lanes(group, heads, value):
    width = heads * HD
    block = value[:, group * width : (group + 1) * width]
    lane = lax.broadcasted_iota(jnp.int32, (1, width), 1)
    result = []
    for a in range(heads):
        here = (lane >= a * HD) & (lane < (a + 1) * HD)
        result.append((here, jnp.where(here, block, jnp.zeros_like(block))))
    return result


def place_of(bounds, first, amount):
    row = first + lax.broadcasted_iota(jnp.int32, (amount, 1), 0)
    opening = jnp.zeros((amount, 1), jnp.int32)
    for clip in range(bounds.shape[1]):
        begin, end = bounds[0, clip], bounds[1, clip]
        opening = jnp.where((row >= begin) & (row < end), begin, opening)
    offset = row - opening
    turns = jnp.floor((offset.astype(jnp.float32) + 0.5) * (1.0 / LAT)).astype(jnp.int32)
    return offset - turns * LAT


def picked_rows(bounds, rows, n_head):
    first = lax.axis_index("blk") * (rows * n_head) + lax.axis_index("head") * rows
    lane = lax.broadcasted_iota(jnp.int32, (rows, LAT), 1)
    return jnp.where(lane == place_of(bounds, first, rows), 1.0, 0.0).astype(low)


def enc_scores(q_head, keys):
    return against(q_head, keys) * HD ** (-0.5)


def encode_kernel(
    n_head,
    shard_rows,
    rows,
    bounds,
    weights,
    common,
    inputs,
    enc_query,
    enc_keyval,
    enc_output,
    self_project,
    gains,
    z_zero,
    h_zero,
    x_norm,
    q_enc,
    kv_enc,
    o_enc,
    z_one,
    h_one,
    q_self,
    kv_self,
    held,
    held_common,
    stage,
    stage_common,
    line,
    latent_table,
    sems,
):
    heads = HEADS // n_head
    width = heads * HD
    shards = held.shape[0]
    from_row = DQ * D // LANES // TILE * TILE
    copies = [
        pltpu.make_async_copy(common.at[pl.ds(from_row, held_common.shape[0])], held_common, sems.at[0]),
        pltpu.make_async_copy(weights.at[pl.ds(0, shards)], held, sems.at[1]),
    ]
    for copy in copies:
        copy.start()
    x_norm[...] = normalized(inputs[...].astype(jnp.float32))[0].astype(low)
    copies[0].wait()
    stage_common[...] = held_common[...].astype(jnp.float32)
    first = DQ * D // LANES - from_row
    for j, value in matrix_of(stage_common, first, LAT, D, line):
        latent_table[:, j : j + LANES] = value.astype(low)
    for j, value in matrix_of(stage_common, first + LAT * D // LANES, 4, D, line):
        gains[:, j : j + LANES] = value
    picked = picked_rows(bounds, rows, n_head)
    z_zero[...] = product(picked, latent_table[...])
    h_zero[...] = layer_norm(z_zero[...], gains[0:1, :]).astype(low)
    copies[1].wait()
    for g in range(n_head):
        load_stage(stage, held, 0, shard_rows, g)
        load_matrices(
            stage, 0, n_head, g, (0, 1, 2, 3), (enc_query, enc_keyval, enc_output, self_project), line
        )
    q_enc[...] = product(h_zero[...], enc_query[...]).astype(low)
    kv_enc[...] = product(x_norm[...], enc_keyval[...]).astype(low)
    for g in range(n_head):
        keys = kv_enc[:, 2 * g * width : (2 * g + 1) * width]
        values = kv_enc[:, (2 * g + 1) * width : (2 * g + 2) * width]
        outcome = jnp.zeros((rows, width), jnp.float32)
        for here, q_head in head_lanes(g, heads, q_enc[...]):
            scores = enc_scores(q_head, keys)
            probs = jnp.exp(scores - jnp.max(scores, 1, keepdims=True))
            total = jnp.sum(probs, 1, keepdims=True)
            outcome = jnp.where(here, product(probs.astype(low), values) / total, outcome)
        o_enc[:, g * width : (g + 1) * width] = outcome.astype(low)
    z_one[...] = z_zero[...] + product(o_enc[...], enc_output[...])
    h_one[...] = layer_norm(z_one[...], gains[1:2, :]).astype(low)
    projected = product(h_one[...], self_project[...]).astype(low)
    for g in range(n_head):
        q_self[g] = projected[:, 3 * g * width : (3 * g + 1) * width]
        kv_self[g] = projected[:, (3 * g + 1) * width : (3 * g + 3) * width]


LINE = pltpu.VMEM((4, round_up(max(D, DI), 8), LANES), jnp.float32)


def shape_of(shape, dtype=low):
    return jax.ShapeDtypeStruct(shape, dtype)


def shards_of(n_head, shard_rows, first, last):
    starts = borders(n_head)
    begin = starts[first] // shard_rows
    return begin, -(-starts[last] // shard_rows) - begin


def encode(bounds, weights, common, inputs, rows, n_head, shard_rows):
    width = HEADS // n_head * HD
    begin, shards = shards_of(n_head, shard_rows, 0, 4)
    common_rows = common.shape[0] - DQ * D // LANES // TILE * TILE
    keys = inputs.shape[0]
    return pl.pallas_call(
        functools.partial(encode_kernel, n_head, shard_rows, rows),
        out_shape=[
            shape_of((D, D)),
            shape_of((DI, 2 * D)),
            shape_of((D, D)),
            shape_of((D, 3 * D)),
            shape_of((4, D), jnp.float32),
            shape_of((rows, D), jnp.float32),
            shape_of((rows, D)),
            shape_of(inputs.shape),
            shape_of((rows, D)),
            shape_of((keys, 2 * D)),
            shape_of((rows, D)),
            shape_of((rows, D), jnp.float32),
            shape_of((rows, D)),
            shape_of((n_head, rows, width)),
            shape_of((n_head, rows, 2 * width)),
        ],
        in_specs=[SMEM_SPEC, ANY_SPEC, ANY_SPEC, VMEM_SPEC],
        out_specs=[VMEM_SPEC] * 15,
        scratch_shapes=[
            pltpu.VMEM((shards,) + weights.shape[1:], low),
            pltpu.VMEM((common_rows, LANES), low),
            pltpu.VMEM((shards * shard_rows, LANES), jnp.float32),
            pltpu.VMEM((common_rows, LANES), jnp.float32),
            LINE,
            pltpu.VMEM((LAT, D), low),
            pltpu.SemaphoreType.DMA((2,)),
        ],
        compiler_params=pltpu.CompilerParams(vmem_limit_bytes=56 * MIB),
        name="encode",
    )(bounds, weights, common, inputs)


def gelu_and_slope(x):
    rate = (2.0 / jnp.pi) ** 0.5
    cubic = 0.044715
    t = jnp.tanh(rate * (x + cubic * x * x * x))
    slope = 0.5 * (1.0 + t) + 0.5 * x * (1.0 - t * t) * rate * (1.0 + 3.0 * cubic * x * x)
    return 0.5 * x * (1.0 + t), slope


def middle_kernel(
    n_head,
    shard_rows,
    first_shard,
    rows,
    counts,
    weights,
    common,
    z_one,
    o_self,
    out_queries,
    marks,
    gains,
    dout,
    d_two_out,
    tile,
    query_grad,
    gain_grads,
    grads,
    held,
    held_common,
    stage,
    stage_common,
    line,
    self_output,
    hidden_in,
    hidden_out,
    class_table,
    query_table,
    slope,
    activ,
    sems,
):
    heads = HEADS // n_head
    width, hidden, classes = heads * HD, FF // n_head, C // n_head
    shards = held.shape[0]
    first_row = first_shard * shard_rows
    starts = borders(n_head)
    copies = [
        pltpu.make_async_copy(common.at[pl.ds(0, held_common.shape[0])], held_common, sems.at[0]),
        pltpu.make_async_copy(weights.at[pl.ds(first_shard, shards)], held, sems.at[1]),
    ]
    for copy in copies:
        copy.start()
    copies[0].wait()
    stage_common[...] = held_common[...].astype(jnp.float32)
    for j, value in matrix_of(stage_common, 0, DQ, D, line):
        query_table[:, j : j + LANES] = value.astype(low)
    copies[1].wait()
    for g in range(n_head):
        load_stage(stage, held, first_shard, shard_rows, g)
        load_matrices(
            stage, first_row, n_head, g, (4, 5, 6, 7), (self_output, hidden_in, hidden_out, class_table), line
        )
    gain_two, gain_three = gains[2:3, :], gains[3:4, :]
    o_low = jnp.concatenate([o_self[g] for g in range(n_head)], 1)
    z_two = z_one[...] + product(o_low, self_output[...])
    h_two = layer_norm(z_two, gain_two).astype(low)
    value, bend = gelu_and_slope(product(h_two, hidden_in[...]))
    activ[...] = value.astype(low)
    slope[...] = bend
    z_three = z_two + product(activ[...], hidden_out[...])
    queries = out_queries[...]
    decoded = (layer_norm(z_three, gain_three) + product(queries, query_table[...])).astype(low)
    logits = product(decoded, class_table[...])
    at = pl.multiple_of(lax.axis_index("head") * rows, rows)
    mark = marks[:, pl.ds(at, rows)].T
    label, kind, counted = (mark[:, i : i + 1] for i in range(3))
    lane = lax.broadcasted_iota(jnp.int32, (rows, C), 1).astype(jnp.float32)
    is_target = jnp.where(lane == label, 1.0, 0.0)
    row_top = jnp.max(logits, 1, keepdims=True)
    row_lse = row_top + jnp.log(jnp.sum(jnp.exp(logits - row_top), 1, keepdims=True))
    loss = row_lse - jnp.sum(is_target * logits, 1, keepdims=True)
    weight = jnp.zeros((rows, 1), jnp.float32)
    place = lax.broadcasted_iota(jnp.int32, (1, LANES), 1)
    losses = jnp.zeros((1, LANES), jnp.float32)
    for m in range(MODES):
        member = jnp.where((kind == m) & (counted == 1.0), 1.0, 0.0)
        weight = weight + member / jnp.maximum(counts[m], 1.0)
        losses = losses + jnp.where(place == m, jnp.sum(loss * member, 0, keepdims=True), 0.0)
    tile[...] = jnp.broadcast_to(losses, tile.shape)
    dlogits = (weight * (jnp.exp(logits - row_lse) - is_target)).astype(low)
    d_decoded = against(dlogits, class_table[...])
    table_grad = contract_first(queries, d_decoded.astype(low))
    matrix_into(stage_common, 0, table_grad, line)
    query_grad[...] = stage_common[: query_grad.shape[0], :].astype(low)
    d_three, gain_three_grad = norm_pullback(z_three, gain_three, d_decoded)
    d_branch = d_three.astype(low)
    d_pre = (slope[...] * against(d_branch, hidden_out[...])).astype(low)
    d_middle, gain_two_grad = norm_pullback(z_two, gain_two, against(d_pre, hidden_in[...]))
    d_two = d_three + d_middle
    d_two_out[...] = d_two
    gain_grads[...] = jnp.concatenate([gain_two_grad, gain_three_grad], 0)
    d_two_low = d_two.astype(low)
    d_o = against(d_two_low, self_output[...]).astype(low)
    for g in range(n_head):
        dout[g] = d_o[:, g * width : (g + 1) * width]
    for g in range(n_head):
        results = (
            contract_first(o_self[g], d_two_low),
            contract_first(h_two, d_pre[:, g * hidden : (g + 1) * hidden]),
            contract_first(activ[:, g * hidden : (g + 1) * hidden], d_branch),
            contract_first(decoded, dlogits[:, g * classes : (g + 1) * classes]),
        )
        for m, result in zip((4, 5, 6, 7), results):
            matrix_into(stage, starts[m] - first_row, result, line)
        for b in range(shards):
            held[b, g, :shard_rows, :] = stage[pl.ds(b * shard_rows, shard_rows), :].astype(low)
    back = pltpu.make_async_copy(held, grads.at[pl.ds(first_shard, shards)], sems.at[2])
    back.start()
    back.wait()


def middle(counts, weights, common, z_one, o_self, out_queries, marks, gains, n_head, shard_rows):
    rows = z_one.shape[0]
    begin, shards = shards_of(n_head, shard_rows, 4, 8)
    query_rows = DQ * D // LANES
    common_rows = round_up(query_rows, TILE)
    return pl.pallas_call(
        functools.partial(middle_kernel, n_head, shard_rows, begin, rows),
        grid=(1,),
        out_shape=[
            shape_of(o_self.shape),
            shape_of((rows, D), jnp.float32),
            shape_of((8, LANES), jnp.float32),
            shape_of((query_rows, LANES)),
            shape_of((2, D), jnp.float32),
            shape_of(weights.shape),
        ],
        in_specs=[
            SMEM_SPEC,
            ANY_SPEC,
            ANY_SPEC,
            VMEM_SPEC,
            VMEM_SPEC,
            pl.BlockSpec((rows, DQ), lambda i: (lax.axis_index("head"), 0)),
            VMEM_SPEC,
            VMEM_SPEC,
        ],
        out_specs=[VMEM_SPEC] * 5 + [ANY_SPEC],
        scratch_shapes=[
            pltpu.VMEM((shards,) + weights.shape[1:], low),
            pltpu.VMEM((common_rows, LANES), low),
            pltpu.VMEM((shards * shard_rows, LANES), jnp.float32),
            pltpu.VMEM((common_rows, LANES), jnp.float32),
            LINE,
            pltpu.VMEM((D, D), low),
            pltpu.VMEM((D, FF), low),
            pltpu.VMEM((FF, D), low),
            pltpu.VMEM((D, C), low),
            pltpu.VMEM((DQ, D), low),
            pltpu.VMEM((rows, FF), jnp.float32),
            pltpu.VMEM((rows, FF), low),
            pltpu.SemaphoreType.DMA((3,)),
        ],
        compiler_params=pltpu.CompilerParams(vmem_limit_bytes=56 * MIB),
        name="middle",
    )(counts, weights, common, z_one, o_self, out_queries, marks, gains)


def ending_kernel(
    n_head,
    shard_rows,
    rows,
    bounds,
    grads_in,
    d_q_self,
    d_kv_self,
    d_two,
    gains,
    gain_grads,
    enc_query,
    enc_keyval,
    enc_output,
    self_project,
    z_zero,
    h_zero,
    x_norm,
    q_enc,
    kv_enc,
    o_enc,
    z_one,
    h_one,
    grads,
    tail_grad,
    held,
    stage,
    stage_common,
    line,
    d_q,
    d_kv,
    sems,
):
    heads = HEADS // n_head
    width = heads * HD
    shards = held.shape[0]
    starts = borders(n_head)
    shared = pltpu.make_async_copy(grads_in.at[pl.ds(shards - 1, 1)], held.at[pl.ds(shards - 1, 1)], sems.at[0])
    shared.start()
    d_projected = [jnp.concatenate([d_q_self[g], d_kv_self[g]], 1) for g in range(n_head)]
    whole = jnp.concatenate(d_projected, 1)
    d_middle, gain_one_grad = norm_pullback(
        z_one[...], gains[1:2, :], against(whole, self_project[...])
    )
    d_one = d_two[...] + d_middle
    d_one_low = d_one.astype(low)
    d_o = against(d_one_low, enc_output[...]).astype(low)
    for g in range(n_head):
        keys = kv_enc[:, 2 * g * width : (2 * g + 1) * width]
        values = kv_enc[:, (2 * g + 1) * width : (2 * g + 2) * width]
        d_key = jnp.zeros(keys.shape, jnp.float32)
        d_value = jnp.zeros(keys.shape, jnp.float32)
        d_query = jnp.zeros((rows, width), jnp.float32)
        for (here, q_head), (unused, do_head) in zip(
            head_lanes(g, heads, q_enc[...]), head_lanes(g, heads, d_o)
        ):
            scores = enc_scores(keys, q_head)
            probs = jnp.exp(scores - jnp.max(scores, 0, keepdims=True))
            probs = probs / jnp.sum(probs, 0, keepdims=True)
            d_probs = against(values, do_head)
            delta = jnp.sum(probs * d_probs, 0, keepdims=True)
            d_scores = (probs * (d_probs - delta)).astype(low)
            d_value = d_value + product(probs.astype(low), do_head)
            d_key = d_key + product(d_scores, q_head)
            d_query = jnp.where(here, contract_first(d_scores, keys), d_query)
        d_q[:, g * width : (g + 1) * width] = (d_query * HD ** (-0.5)).astype(low)
        d_kv[:, 2 * g * width : (2 * g + 1) * width] = (d_key * HD ** (-0.5)).astype(low)
        d_kv[:, (2 * g + 1) * width : (2 * g + 2) * width] = d_value.astype(low)
    d_middle, gain_zero_grad = norm_pullback(
        z_zero[...], gains[0:1, :], against(d_q[...], enc_query[...])
    )
    d_zero = d_one + d_middle
    d_zero_top = d_zero.astype(low)
    d_zero_rest = (d_zero - d_zero_top.astype(jnp.float32)).astype(low)
    picked = picked_rows(bounds, rows, n_head)
    latent_grad = contract_first(picked, d_zero_top) + contract_first(picked, d_zero_rest)
    matrix_into(stage_common, 0, latent_grad, line)
    all_gains = jnp.concatenate([gain_zero_grad, gain_one_grad, gain_grads[...]], 0)
    matrix_into(stage_common, LAT * D // LANES, all_gains, line)
    tail_grad[...] = stage_common[...].astype(low)
    shared.wait()
    kept = shards * shard_rows - starts[4]
    for g in range(n_head):
        results = (
            contract_first(h_zero[...], d_q[:, g * width : (g + 1) * width]),
            contract_first(x_norm[...], d_kv[:, 2 * g * width : (2 * g + 2) * width]),
            contract_first(o_enc[:, g * width : (g + 1) * width], d_one_low),
            contract_first(h_one[...], d_projected[g]),
        )
        if kept:
            stage[pl.ds((shards - 1) * shard_rows, shard_rows), :] = held[
                shards - 1, g, :shard_rows, :
            ].astype(jnp.float32)
        for m, result in zip((0, 1, 2, 3), results):
            matrix_into(stage, starts[m], result, line)
        for b in range(shards):
            held[b, g, :shard_rows, :] = stage[pl.ds(b * shard_rows, shard_rows), :].astype(low)
    back = pltpu.make_async_copy(held, grads.at[pl.ds(0, shards)], sems.at[1])
    back.start()
    back.wait()


def ending(bounds, grads, d_q_self, d_kv_self, d_two, gains, gain_grads, kept, n_head, shard_rows):
    rows = d_two.shape[0]
    begin, shards = shards_of(n_head, shard_rows, 0, 4)
    keys = kept[6].shape[0]
    tail_rows = (LAT + 4) * D // LANES
    return pl.pallas_call(
        functools.partial(ending_kernel, n_head, shard_rows, rows),
        out_shape=[shape_of(grads.shape), shape_of((tail_rows, LANES))],
        in_specs=[SMEM_SPEC, ANY_SPEC] + [VMEM_SPEC] * 17,
        out_specs=[ANY_SPEC, VMEM_SPEC],
        input_output_aliases={1: 0},
        scratch_shapes=[
            pltpu.VMEM((shards,) + grads.shape[1:], low),
            pltpu.VMEM((shards * shard_rows, LANES), jnp.float32),
            pltpu.VMEM((tail_rows, LANES), jnp.float32),
            LINE,
            pltpu.VMEM((rows, D), low),
            pltpu.VMEM((keys, 2 * D), low),
            pltpu.SemaphoreType.DMA((2,)),
        ],
        compiler_params=pltpu.CompilerParams(vmem_limit_bytes=56 * MIB),
        name="ending",
    )(bounds, grads, d_q_self, d_kv_self, d_two, gains, gain_grads, *kept)


def adam_step(weight, first, second, grad):
    first = beta_one * first + (1 - beta_one) * grad
    second = beta_two * second + (1 - beta_two) * grad * grad
    fixed_first = first / (1 - beta_one**STEP)
    fixed_second = second / (1 - beta_two**STEP)
    weight = weight - learn_rate * (
        fixed_first / (jnp.sqrt(fixed_second) + adam_eps) + weight_decay * weight
    )
    return (weight, first, second, weight.astype(low))


def per_device(
    inputs,
    out_queries,
    clip_lengths,
    labels,
    modality,
    labeled,
    head_params,
    head_first,
    head_second,
    common_params,
    common_first,
    common_second,
):
    n_head, n_blk = lax.axis_size("head"), lax.axis_size("blk")
    dims = grid_of(n_blk, n_head)
    head_rank = lax.axis_index("head")
    blk_rows = labels.shape[0]
    rows = blk_rows // n_head
    heads_here = HEADS // n_head
    n_h, n_c = head_params.shape[0], common_params.shape[0]
    shard_rows = n_h // LANES
    head_rows = round_up(shard_rows + 1, TILE)
    piece_rows = round_up(-(-(-(-n_c // LANES)) // n_head), TILE)

    marks = jnp.stack([labels, modality, labeled] + [jnp.zeros_like(labels)] * 5).astype(jnp.float32)
    mine = lax.dynamic_slice_in_dim(marks, head_rank * rows, rows, 1)
    member = (mine[1][None] == jnp.arange(MODES, dtype=jnp.float32)[:, None]) & (mine[2][None] == 1.0)
    counted = jnp.pad(jnp.sum(member.astype(jnp.float32), 1), (0, LANES - MODES)).astype(low)
    head_low = jnp.concatenate(
        [
            head_params.astype(low).reshape(shard_rows, LANES),
            jnp.broadcast_to(counted[None], (head_rows - shard_rows, LANES)),
        ]
    )
    common_low = jnp.pad(common_params.astype(low), (0, n_head * piece_rows * LANES - n_c))
    common_low = lax.dynamic_slice_in_dim(
        common_low.reshape(n_head * piece_rows, LANES), head_rank * piece_rows, piece_rows, 0
    )
    weights, common = gather_all(dims, (head_low, common_low), 0)
    label_counts = jnp.sum(weights[:, :, shard_rows, :MODES].astype(jnp.float32), (0, 1))
    if n_c % LANES == 0:
        common = common.reshape(n_blk, n_head * piece_rows, LANES)[:, : n_c // LANES]
    else:
        common = common.reshape(n_blk, n_head * piece_rows * LANES)[:, :n_c]
    common = common.reshape(-1, LANES)
    common = jnp.pad(common, ((0, -common.shape[0] % TILE), (0, 0)))

    finish = jnp.cumsum(clip_lengths)
    bounds = jnp.stack([finish - clip_lengths, finish])
    encoded = encode(bounds, weights, common, inputs, rows, n_head, shard_rows)
    gains, z_one = encoded[4], encoded[11]
    o_self, lse_self, out_self_t, q_all, kv_all = attend(
        dims, bounds, encoded[13], encoded[14], heads_here, 1
    )
    dout, d_two, tile, query_grad, gain_grads, grads = middle(
        label_counts, weights, common, z_one, o_self, out_queries, marks, gains, n_head, shard_rows
    )
    d_q, d_kv = attend_back(dims, bounds, q_all, kv_all, dout, out_self_t, lse_self, heads_here, 2)
    kept = encoded[:4] + encoded[5:13]
    grads, tail_grad = ending(
        bounds, grads, d_q, d_kv, d_two, gains, gain_grads, kept, n_head, shard_rows
    )
    common_grad = jnp.concatenate([query_grad, tail_grad])
    space = n_head * piece_rows * LANES
    if n_c % LANES == 0:
        common_grad = jnp.pad(
            common_grad.reshape(n_blk, n_c // LANES, LANES),
            ((0, 0), (0, (space - n_c) // LANES), (0, 0)),
        )
    else:
        common_grad = jnp.pad(common_grad.reshape(n_blk, n_c), ((0, 0), (0, space - n_c)))
    common_grad = common_grad.reshape(n_blk, n_head, piece_rows, LANES)
    head_share, unused, totals, common_share = reduce_all(
        dims, (grads, common_grad), (shard_rows, piece_rows), tile, 3
    )
    clip_norm = jnp.sqrt(totals[0, MODES])
    loss_sums = totals[0, :MODES]
    factor = jnp.minimum(1.0, clip_limit / clip_norm)
    head_share = head_share[:shard_rows].reshape(-1)
    common_share = common_share.reshape(-1)[:n_c].astype(jnp.float32)
    head_out = adam_step(head_params, head_first, head_second, head_share * factor)
    common_out = adam_step(common_params, common_first, common_second, common_share * factor)
    return head_out + common_out + (loss_sums, label_counts, clip_norm)


def solution(mesh):
    placed = (
        P("blk", None),
        P("blk", None),
        P(),
        P("blk"),
        P("blk"),
        P("blk"),
        P(("head", "blk")),
        P(("head", "blk")),
        P(("head", "blk")),
        P("blk"),
        P("blk"),
        P("blk"),
    )
    return jax.shard_map(
        per_device,
        mesh=mesh,
        in_specs=placed,
        out_specs=(
            P(("head", "blk")),
            P(("head", "blk")),
            P(("head", "blk")),
            P(("head", "blk")),
            P("blk"),
            P("blk"),
            P("blk"),
            P("blk"),
            P(),
            P(),
            P(),
        ),
        check_vma=False,
    )
```

```python
import functools

import jax
import jax.numpy as jnp
from jax import lax
from jax.experimental import pallas as pl
from jax.experimental.pallas import tpu as pltpu
from jax.sharding import PartitionSpec as P

D = 512
HEADS = 8
HD = 64
FF = 2048
DI = 704
DQ = 1026
C = 704
LAT = 784
MODES = 3
STEP = 10
LANES = 128
TILE = 16

norm_eps = 1e-05
learn_rate = 0.1
beta_one = 0.9
beta_two = 0.999
adam_eps = 1e-08
weight_decay = 0.01
clip_limit = 0.05
big_negative = -1e30
low = jnp.bfloat16
MESH = pl.DeviceIdType.MESH
MIB = 1 << 20
VMEM_SPEC = pl.BlockSpec(memory_space=pltpu.VMEM)
SMEM_SPEC = pl.BlockSpec(memory_space=pltpu.SMEM)
ANY_SPEC = pl.BlockSpec(memory_space=pl.ANY)


def shape_of(shape, dtype=low):
    return jax.ShapeDtypeStruct(shape, dtype)


def round_up(n, unit):
    return -(-n // unit) * unit


def grid_of(n_blk, n_head):
    cores = 2 if n_head % 2 == 0 else 1
    x = n_head // cores
    y = x if n_blk % x == 0 else 1
    return (n_blk // y, y, x, cores)


def my_place(dims):
    blk, head = lax.axis_index("blk"), lax.axis_index("head")
    return (blk // dims[1], lax.rem(blk, dims[1]), head // dims[3], lax.rem(head, dims[3]))


def shifted(dims, me, offset, sign):
    return tuple(
        m if o == 0 else lax.rem(m + (o if sign > 0 else n - o), n)
        for m, o, n in zip(me, offset, dims)
    )


def blk_of(dims, place):
    return place[0] * dims[1] + place[1]


def head_of(dims, place):
    return place[2] * dims[3] + place[3]


def device_of(dims, place):
    return {"blk": blk_of(dims, place), "head": head_of(dims, place)}


def along(axis, d):
    return tuple(d if a == axis else 0 for a in range(4))


def greet(dims, me, offsets):
    barrier = pltpu.get_barrier_semaphore()
    for offset in offsets:
        pl.semaphore_signal(
            barrier,
            inc=1,
            device_id=device_of(dims, shifted(dims, me, offset, 1)),
            device_id_type=MESH,
        )
    pl.semaphore_wait(barrier, len(offsets))


def axis_peers(dims, axes):
    return [along(axis, d) for axis in axes for d in range(1, dims[axis])]


def remote(src, dst, send_sem, recv_sem, place, dims):
    return pltpu.make_async_remote_copy(
        src_ref=src,
        dst_ref=dst,
        send_sem=send_sem,
        recv_sem=recv_sem,
        device_id=device_of(dims, place),
        device_id_type=MESH,
    )


AHEAD = 10
RING = 0


def in_order(first, follow, size_of, ahead, result):
    queues, busy, flight = {}, {}, {}
    now = 0.0

    def ready(messages):
        for message in messages:
            queues.setdefault(message[1], []).append(message)

    ready(first)
    while True:
        for axis in sorted(queues):
            queue, going = queues[axis], flight.setdefault(axis, [])
            while queue and (not going or busy[axis] < now + ahead):
                message = min(queue)
                queue.remove(message)
                busy[axis] = max(now, busy.get(axis, 0.0)) + size_of(message)
                going.append((busy[axis] + 1.5, message))
                result.append((True, message))
        arrivals = [min(going) for going in flight.values() if going]
        if not arrivals:
            return now
        arrival = min(arrivals)
        flight[arrival[1][1]].remove(arrival)
        now = max(now, arrival[0])
        result.append((False, arrival[1]))
        ready(follow(arrival[1]))


def time_of(rows, axis):
    return rows * LANES * 2 / (300e3 if axis == 3 else 45e3)


def with_at(offset, axis, d):
    return offset[:axis] + (d,) + offset[axis + 1 :]


def gather_order(dims, parts):
    def onward(p, offset, position):
        order = parts[p][3]
        result = []
        for k in range(max(position, 0), 4):
            axis = order[k]
            n = dims[axis]
            if k > position:
                steps = [1] if axis == RING else range(1, n)
                steps = [d for d in steps if d < n]
            else:
                steps = [offset[axis] + 1] if axis == RING and offset[axis] + 1 < n else []
            for d in steps:
                result.append(((k, sum(offset), p), axis, p, with_at(offset, axis, d)))
        return result

    def follow(message):
        rank, axis, p, offset = message
        return onward(p, offset, rank[0])

    first = [m for p in range(len(parts)) for m in onward(p, (0, 0, 0, 0), -1)]
    result = []
    now = in_order(first, follow, lambda m: time_of(parts[m[2]][2], m[1]), AHEAD, result)
    return result, now


def gather_kernel(
    dims,
    parts,
    labels,
    modality,
    labeled,
    head_params,
    common_params,
    head_all,
    common_all,
    head_low,
    common_low,
    common_wide,
    send_sem,
    recv_sem,
    own_sem,
):
    me = my_place(dims)
    my_head = head_of(dims, me)
    n_head = dims[2] * dims[3]
    shard_rows, common_rows = head_params.shape[0], common_params.shape[0]
    per_head = labels.shape[0] // n_head
    row = lax.broadcasted_iota(jnp.int32, labels.shape, 0)
    mine = (row >= my_head * per_head) & (row < (my_head + 1) * per_head) & (labeled[...] == 1)
    lane = lax.broadcasted_iota(jnp.int32, (1, LANES), 1)
    counts = jnp.zeros((1, LANES), jnp.float32)
    for m in range(MODES):
        member = jnp.where(mine & (modality[...] == m), 1.0, 0.0)
        counts = counts + jnp.where(lane == m, jnp.sum(member, (0, 1), keepdims=True), 0.0)
    padding = head_low.shape[0] - shard_rows
    tail = shard_rows // TILE * TILE
    head_low[:tail] = head_params[:tail].astype(low)
    last = [jnp.broadcast_to(counts, (padding, LANES))]
    if shard_rows > tail:
        last = [head_params[tail:]] + last
    head_low[tail:] = jnp.concatenate(last, 0).astype(low)
    common_wide[...] = jnp.zeros(common_wide.shape, jnp.float32)
    common_wide[:common_rows] = common_params[...]
    piece = common_low.shape[0]
    common_low[...] = common_wide[pl.ds(pl.multiple_of(my_head * piece, TILE), piece)].astype(low)

    greet(dims, me, ring_and_others(dims))
    srcs, outs = (head_low, common_low), (head_all, common_all)
    copies = {}

    def block(p, offset):
        place = shifted(dims, me, offset, -1)
        array, first, rows, order = parts[p]
        return outs[array].at[blk_of(dims, place), head_of(dims, place), pl.ds(first, rows)]

    own = []
    for is_send, (rank, axis, p, offset) in gather_order(dims, parts)[0]:
        if is_send:
            step = 1 if axis == RING else offset[axis]
            before = with_at(offset, axis, offset[axis] - step)
            array, first, rows, order = parts[p]
            source = block(p, before) if any(before) else srcs[array].at[pl.ds(first, rows)]
            i = len(copies)
            copies[(p, offset)] = remote(
                source,
                block(p, before),
                send_sem.at[i],
                recv_sem.at[i],
                shifted(dims, me, along(axis, step), 1),
                dims,
            )
            copies[(p, offset)].start()
        else:
            if not own:
                for array in range(2):
                    copy = pltpu.make_async_copy(
                        srcs[array], outs[array].at[blk_of(dims, me), my_head], own_sem.at[array]
                    )
                    copy.start()
                    own.append(copy)
            copies[(p, offset)].wait_recv()
    for copy in copies.values():
        copy.wait_send()
    for copy in own:
        copy.wait()


def ring_and_others(dims):
    ring = {along(RING, 1 % dims[RING]), along(RING, (dims[RING] - 1) % dims[RING])}
    return sorted(ring - {(0, 0, 0, 0)}) + axis_peers(dims, (1, 2, 3))


def cut(array, rows, shares):
    result = []
    first, so_far = 0, 0
    whole = sum(share for share, order in shares)
    for share, order in shares:
        so_far += share
        end = rows * so_far // whole // TILE * TILE if so_far < whole else rows
        if end > first:
            result.append((array, first, end - first, order))
        first = end
    return tuple(result)


ZYXC, ZXYC, YXZC, XYZC = (0, 1, 2, 3), (0, 2, 1, 3), (1, 2, 0, 3), (2, 1, 0, 3)
GATHER_SHARES = ((8, ZYXC), (6, ZXYC), (2, YXZC), (2, XYZC))
REDUCE_SHARES = ((7, ZYXC), (7, ZXYC), (2, YXZC), (2, XYZC))


def gather_all(dims, marks, params, rows, collective_id):
    z, y, x, cores = dims
    parts = cut(0, rows[0], GATHER_SHARES) + cut(1, rows[1], ((1, ZXYC),))
    count = len(parts) * (z * y * x * cores - 1)
    return pl.pallas_call(
        functools.partial(gather_kernel, dims, parts),
        out_shape=[shape_of((z * y, x * cores, n, LANES)) for n in rows],
        in_specs=[VMEM_SPEC] * 5,
        out_specs=[ANY_SPEC] * 2,
        scratch_shapes=[pltpu.VMEM((n, LANES), low) for n in rows]
        + [
            pltpu.VMEM((x * cores * rows[1], LANES), jnp.float32),
            pltpu.SemaphoreType.DMA((count,)),
            pltpu.SemaphoreType.DMA((count,)),
            pltpu.SemaphoreType.DMA((2,)),
        ],
        compiler_params=pltpu.CompilerParams(collective_id=collective_id, has_side_effects=True),
        name="gather_weights",
    )(*marks, *params)


def reduce_order(dims, parts):
    ready, arrived, order = set(), set(), []

    def message(p, position, offset):
        z = offset[RING]
        rank = (dims[RING] - z if z else dims[RING], position, tuple(-o for o in offset), p)
        return (rank, parts[p][3][position], p, position, offset)

    def done(p, position, offset):
        ready.add((p, position, offset))
        if position == 4:
            return []
        axis = parts[p][3][position]
        d = offset[axis]
        first = d != 0 and (axis != RING or d == dims[axis] - 1)
        return ([message(p, position, offset)] if first else []) + advance(p, position, offset)

    def advance(p, position, offset):
        axis = parts[p][3][position]
        n = dims[axis]
        start = with_at(offset, axis, 0)
        if axis == RING:
            here = (p, position, offset)
            if here in ready and here in arrived:
                order.append((None, here))
                if offset[axis]:
                    return [message(p, position, offset)]
                return done(p, position + 1, offset)
        elif (p, position, start) in ready and (p, position + 1, start) not in ready:
            if all((p, position, with_at(start, axis, d)) in arrived for d in range(1, n)):
                order.append((None, (p, position, start)))
                return done(p, position + 1, start)
        return []

    def follow(sent):
        rank, axis, p, position, offset = sent
        here = with_at(offset, axis, offset[axis] - 1) if axis == RING else offset
        arrived.add((p, position, here))
        return advance(p, position, here)

    first = []
    for p in range(len(parts)):
        for offset in all_offsets(dims, range(4)):
            first += done(p, 0, offset)
    now = in_order(first, follow, lambda m: time_of(parts[m[2]][2], m[1]), AHEAD, order)
    return order, now


def all_offsets(dims, axes):
    offsets = [(0, 0, 0, 0)]
    for a in axes:
        offsets = [with_at(o, a, d) for o in offsets for d in range(dims[a])]
    return offsets


def reduce_kernel(dims, parts, *refs):
    srcs, tile = refs[:2], refs[2]
    head_out, common_out, totals = refs[3:6]
    places = len(parts) * 4
    buffers = refs[6 : 6 + places]
    head_sum, common_sum, shares, send_sem, recv_sem, near_tiles, far_tiles = refs[6 + places :]
    sums = (head_sum, common_sum)
    me = my_place(dims)
    z, y, x, cores = dims
    across = peers_across(dims)
    others = [o for o in all_offsets(dims, (0, 1)) if any(o)]
    met = ring_and_others(dims)
    greet(dims, me, met + [o for o in across + others if o not in met])
    push = Pushes(dims, me, send_sem, recv_sem)
    copies = {}

    def slot(p, position, offset):
        order = parts[p][3]
        axis = order[position]
        rest = [o for o in all_offsets(dims, order[position + 1 :])]
        k = rest.index(with_at(offset, axis, 0))
        return buffers[p * 4 + position].at[k, max(offset[axis] - 1, 0)]

    def summed(p, position, offset):
        array, first, rows, order = parts[p]
        if position == 0:
            place = shifted(dims, me, offset, 1)
            return srcs[array].at[blk_of(dims, place), head_of(dims, place), pl.ds(first, rows)]
        return slot(p, position - 1, offset)

    def ring_slot(p, position, offset):
        axis = parts[p][3][position]
        return slot(p, position, with_at(offset, axis, offset[axis] + 1))

    def add(p, position, offset):
        array, first, rows, order = parts[p]
        axis = order[position]
        if axis == RING:
            arrivals = [ring_slot(p, position, offset)]
        else:
            arrivals = [slot(p, position, with_at(offset, axis, d)) for d in range(1, dims[axis])]
        mine = summed(p, position, offset)
        step = row_chunk(rows)

        @pl.loop(0, rows // step)
        def some_rows(n):
            at = pl.ds(pl.multiple_of(n * step, step), step)
            total = mine[at].astype(jnp.float32)
            for arrival in arrivals:
                total = total + arrival[at].astype(jnp.float32)
            if position == 3 and not any(offset):
                sums[array][pl.ds(pl.multiple_of(first + n * step, TILE), step)] = total
            else:
                arrivals[0][at] = total.astype(low)

    for is_send, what in reduce_order(dims, parts)[0]:
        if is_send is None:
            add(*what)
        elif is_send:
            rank, axis, p, position, offset = what
            d = offset[axis]
            started = axis != RING or d == dims[axis] - 1
            source = summed(p, position, offset) if started else ring_slot(p, position, offset)
            step = along(axis, 1 if axis == RING else d)
            copies[what] = push(source, slot(p, position, offset), step)
        else:
            copies[what].wait_recv()
    my_head, my_blk = head_of(dims, me), blk_of(dims, me)
    shares[my_head] = common_sum[...].astype(low)
    share_copies = [push(shares.at[my_head], shares.at[my_head], o) for o in across]
    amount = head_out.shape[0]
    head_out[...] = head_sum[:amount]
    squares = jnp.sum(head_sum[:amount] * head_sum[:amount], 0, keepdims=True)
    squares = squares + jnp.sum(common_sum[...] * common_sum[...], 0, keepdims=True)
    lane = lax.broadcasted_iota(jnp.int32, (1, LANES), 1)
    near_tiles[my_head] = tile[...] + jnp.where(
        lane == MODES, jnp.sum(squares, 1, keepdims=True), 0.0
    )
    near = [push(near_tiles.at[my_head], near_tiles.at[my_head], o) for o in across]
    for copy in near:
        copy.wait_recv()
    far_tiles[my_blk] = jnp.sum(near_tiles[...], 0)
    far = [push(far_tiles.at[my_blk], far_tiles.at[my_blk], o) for o in others]
    for copy in share_copies:
        copy.wait_recv()
    piece = shares.shape[1]
    for k in range(x * cores):
        amount = min(piece, common_out.shape[0] - k * piece)
        common_out[k * piece : k * piece + amount] = shares[k].astype(jnp.float32)[:amount]
    for copy in far:
        copy.wait_recv()
    totals[...] = jnp.sum(far_tiles[...], 0)
    push.finish()


def row_chunk(rows):
    for count in (4, 3, 2):
        if rows % (count * TILE) == 0:
            return rows // count
    return rows


def reduce_all(dims, arrays, valid, tile, collective_id):
    z, y, x, cores = dims
    rows = [array.shape[2] for array in arrays]
    parts = cut(0, rows[0], [(share, order[::-1]) for share, order in REDUCE_SHARES])
    parts = parts + cut(1, rows[1], ((1, ZXYC[::-1]),))
    scratch = []
    for array, first, amount, order in parts:
        for position, axis in enumerate(order):
            rest = len(all_offsets(dims, order[position + 1 :]))
            scratch.append(pltpu.VMEM((rest, dims[axis] - 1, amount, LANES), low))
    count = len(parts) * (z * y * x * cores - 1) + 2 * (x * cores - 1) + z * y - 1
    return pl.pallas_call(
        functools.partial(reduce_kernel, dims, parts),
        out_shape=[
            shape_of((valid[0], LANES), jnp.float32),
            shape_of((valid[1], LANES), jnp.float32),
            shape_of((8, LANES), jnp.float32),
        ],
        in_specs=[VMEM_SPEC] * 3,
        out_specs=[VMEM_SPEC] * 3,
        scratch_shapes=scratch
        + [pltpu.VMEM((n, LANES), jnp.float32) for n in rows]
        + [
            pltpu.VMEM((x * cores, rows[1], LANES), low),
            pltpu.SemaphoreType.DMA((count,)),
            pltpu.SemaphoreType.DMA((count,)),
            pltpu.VMEM((x * cores, 8, LANES), jnp.float32),
            pltpu.VMEM((z * y, 8, LANES), jnp.float32),
        ],
        compiler_params=pltpu.CompilerParams(
            collective_id=collective_id, has_side_effects=True, vmem_limit_bytes=60 * MIB
        ),
        name="reduce_gradients",
    )(*arrays, tile)


def contract_first(a, b):
    return lax.dot_general(a, b, (((0,), (0,)), ((), ())), preferred_element_type=jnp.float32)


def product(a, b):
    return jnp.dot(a, b, preferred_element_type=jnp.float32)


def against(a, b):
    return lax.dot_general(a, b, (((1,), (1,)), ((), ())), preferred_element_type=jnp.float32)


def clip_bounds(lengths):
    result, first = [], 0
    for clip in range(lengths.shape[0]):
        end = first + lengths[clip]
        result.append((first, end))
        first = end
    return result


def clip_borders(bounds, place):
    opening = jnp.zeros(place.shape, jnp.int32)
    ending = jnp.full(place.shape, 1 << 30, jnp.int32)
    for clip, (begin, end) in enumerate(bounds):
        here = place == clip
        opening = jnp.where(here, begin, opening)
        ending = jnp.where(here, end, ending)
    return opening, ending


def lane_of_tail(a):
    return HD if a % 2 == 0 else 0


def in_head(a, axis):
    shape = (1, LANES) if axis else (LANES, 1)
    lane = lax.broadcasted_iota(jnp.int32, shape, axis)
    return (lane >= a * HD) & (lane < (a + 1) * HD)


def all_lanes(block, first, width):
    piece = block[:, first : first + width]
    if width < LANES:
        piece = jnp.concatenate([piece, jnp.zeros((piece.shape[0], LANES - width), piece.dtype)], 1)
    return piece


def with_key_tail(bounds, a, first_row, columns):
    clips = len(bounds)
    place = lax.broadcasted_iota(jnp.int32, (1, LANES), 1) - lane_of_tail(a)
    opening, ending = clip_borders(bounds, place)
    ones = jnp.where((place >= clips) & (place < clips + 3), 1.0, 0.0)
    row = first_row + lax.broadcasted_iota(jnp.int32, columns.shape, 0)
    tail = jnp.where((row >= opening) & (row < ending), ones, big_negative)
    return jnp.where(in_head(a, 1), columns.astype(jnp.float32), tail).astype(low)


def in_three(place, value):
    top = value.astype(low).astype(jnp.float32)
    middle = (value - top).astype(low).astype(jnp.float32)
    bottom = value - top - middle
    return (
        jnp.where(place == 0, top, 0.0)
        + jnp.where(place == 1, middle, 0.0)
        + jnp.where(place == 2, bottom, 0.0)
    )


def with_tail(a, rows, tail):
    return jnp.concatenate([rows, tail] if lane_of_tail(a) else [tail, rows], 0)


def with_query_tail(bounds, a, first_row, rows, extra):
    clips = len(bounds)
    place = lax.broadcasted_iota(jnp.int32, (HD, 1), 0)
    opening, ending = clip_borders(bounds, place)
    row = first_row + lax.broadcasted_iota(jnp.int32, (1, rows.shape[1]), 1)
    inside = (place < clips) & (row >= opening) & (row < ending)
    tail = jnp.where(inside, 1.0, 0.0)
    if extra is not None:
        tail = tail + in_three(place - clips, -extra)
    return with_tail(a, rows * HD ** (-0.5), tail).astype(low)


class Pushes:
    def __init__(self, dims, me, send_sem, recv_sem):
        self.dims, self.me, self.send_sem, self.recv_sem = dims, me, send_sem, recv_sem
        self.started = []

    def __call__(self, src, dst, offset):
        i = len(self.started)
        place = shifted(self.dims, self.me, offset, 1)
        copy = remote(src, dst, self.send_sem.at[i], self.recv_sem.at[i], place, self.dims)
        copy.start()
        self.started.append(copy)
        return copy

    def finish(self):
        for copy in self.started:
            copy.wait_send()


def peers_across(dims):
    z, y, x, cores = dims
    across = [(0, 0, a, c) for a in range(x) for c in range(cores) if (a, c) != (0, 0)]
    return sorted(across, key=lambda o: (o[2] == 0, o[3]))


def ring_and_sides(dims):
    z = dims[0]
    ring = sorted({along(0, 1 % z), along(0, (z - 1) % z)} - {(0, 0, 0, 0)})
    return ring + axis_peers(dims, (1,))


def attend_kernel(
    dims,
    heads,
    key_step,
    query_step,
    lengths,
    q_in,
    kv_in,
    o_out,
    lse,
    out_t,
    q_all,
    kv_all,
    keys,
    values_t,
    queries,
    top,
    accum,
    o_mine,
    send_sem,
    recv_sem,
    own_sem,
):
    z, y, x, cores = dims
    me = my_place(dims)
    bounds = clip_bounds(lengths)
    n_head = x * cores
    rows, width = q_in.shape[1], heads * HD
    amount = n_head * rows
    my_blk, my_head = blk_of(dims, me), head_of(dims, me)
    across = peers_across(dims)
    sides = axis_peers(dims, (1,))
    greet(dims, me, across + ring_and_sides(dims))
    push = Pushes(dims, me, send_sem, recv_sem)
    own_kv = pltpu.make_async_copy(kv_in.at[my_head], kv_all.at[my_blk, my_head], own_sem.at[0])
    own_q = pltpu.make_async_copy(q_in.at[my_head], q_all.at[my_head], own_sem.at[1])
    own_kv.start()
    own_q.start()

    def to_head(src, dst, o):
        return push(src.at[head_of(dims, shifted(dims, me, o, 1))], dst, o)

    kv_copies = {o: to_head(kv_in, kv_all.at[my_blk, my_head], o) for o in across}
    q_copies = [to_head(q_in, q_all.at[my_head], o) for o in across]
    ring, side = {}, {}
    pieces = [(0, 0, 0, 0)] + across[::-1]

    def send_on(s, n):
        block = kv_all.at[
            blk_of(dims, shifted(dims, me, along(0, s), -1)),
            head_of(dims, shifted(dims, me, pieces[n], -1)),
        ]
        if s < z - 1:
            ring[(s + 1, n)] = push(block, block, along(0, 1))
        for o in sides:
            side[(s, n, o)] = push(block, block, o)

    def compute(offset):
        blk = blk_of(dims, shifted(dims, me, offset, -1))

        @pl.loop(0, n_head)
        def build(h):
            at = pl.ds(pl.multiple_of(h * rows, rows), rows)
            block = kv_all[blk, h]
            k_block, v_block = all_lanes(block, 0, width), all_lanes(block, width, width)
            v_t = v_block.astype(jnp.float32).T
            for a in range(heads):
                keys[a, at, :] = with_key_tail(bounds, a, blk * amount + h * rows, k_block)
                values_t[a, :HD, at] = v_t[a * HD : (a + 1) * HD].astype(low)

        @pl.loop(0, amount // query_step)
        def query_block(n):
            at = pl.ds(pl.multiple_of(n * query_step, query_step), query_step)
            for a in range(heads):
                query = queries[a, :, at]
                highest = jnp.full((8, query_step), -1e38, jnp.float32)
                for k in range(0, amount, key_step):
                    scores = product(keys[a, k : k + key_step, :], query)
                    highest = jnp.maximum(
                        highest, jnp.max(scores.reshape(key_step // 8, 8, query_step), 0)
                    )
                old = top[a, :, at]
                new = jnp.maximum(old, jnp.max(highest, 0, keepdims=True))
                top[a, :, at] = new
                total = accum[a, :, at] * jnp.exp(old - new)
                for k in range(0, amount, key_step):
                    scores = product(keys[a, k : k + key_step, :], query)
                    probs = jnp.exp(scores - new).astype(low)
                    total = total + product(values_t[a, :, k : k + key_step], probs)
                accum[a, :, at] = total

    for a in range(heads):
        values_t[a, HD:, :] = jnp.ones((values_t.shape[1] - HD, amount), low)
        top[a] = jnp.full((1, amount), -1e38, jnp.float32)
        accum[a] = jnp.zeros(accum.shape[1:], jnp.float32)
    own_kv.wait()
    send_on(0, 0)
    for n in range(1, n_head):
        kv_copies[pieces[n]].wait_recv()
        send_on(0, n)
    own_q.wait()
    for copy in q_copies:
        copy.wait_recv()
    for a in range(heads):
        for h in range(n_head):
            q_t = all_lanes(q_all[h], 0, width).astype(jnp.float32).T
            queries[a, :, h * rows : (h + 1) * rows] = with_query_tail(
                bounds, a, my_blk * amount + h * rows, q_t[a * HD : (a + 1) * HD], None
            )
    compute((0, 0, 0, 0))
    for s in range(1, z + 1):
        if s < z:
            for n in range(n_head):
                ring[(s, n)].wait_recv()
                send_on(s, n)
            compute(along(0, s))
        for o in sides:
            for n in range(n_head):
                side[(s - 1, n, o)].wait_recv()
            compute((s - 1, o[1], 0, 0))
    for a in range(heads):
        total = accum[a, HD : HD + 1, :]
        out_t[a * HD : (a + 1) * HD, :] = accum[a, :HD, :] / total
        lse[a : a + 1, :] = top[a] + jnp.log(total)
    for h in range(n_head):
        o_mine[h] = out_t[:, h * rows : (h + 1) * rows].T.astype(low)
    o_copies = [to_head(o_mine, o_out.at[my_head], o) for o in across]
    own_o = pltpu.make_async_copy(o_mine.at[my_head], o_out.at[my_head], own_sem.at[2])
    own_o.start()
    own_o.wait()
    for copy in o_copies:
        copy.wait_recv()
    push.finish()


def attend(dims, lengths, q, kv, heads, collective_id):
    z, y, x, cores = dims
    n_head, rows, width = q.shape
    amount = n_head * rows
    count = 3 * (n_head - 1) + n_head * (z - 1 + z * (y - 1))
    return pl.pallas_call(
        functools.partial(attend_kernel, dims, heads, 256, 256),
        out_shape=(
            jax.ShapeDtypeStruct(q.shape, low),
            jax.ShapeDtypeStruct((heads, amount), jnp.float32),
            jax.ShapeDtypeStruct((width, amount), jnp.float32),
            jax.ShapeDtypeStruct(q.shape, low),
            jax.ShapeDtypeStruct((z * y,) + kv.shape, low),
        ),
        in_specs=[SMEM_SPEC, VMEM_SPEC, VMEM_SPEC],
        out_specs=[VMEM_SPEC] * 5,
        scratch_shapes=[
            pltpu.VMEM((heads, amount, LANES), low),
            pltpu.VMEM((heads, HD + TILE, amount), low),
            pltpu.VMEM((heads, LANES, amount), low),
            pltpu.VMEM((heads, 1, amount), jnp.float32),
            pltpu.VMEM((heads, HD + TILE, amount), jnp.float32),
            pltpu.VMEM(q.shape, low),
            pltpu.SemaphoreType.DMA((count,)),
            pltpu.SemaphoreType.DMA((count,)),
            pltpu.SemaphoreType.DMA((3,)),
        ],
        compiler_params=pltpu.CompilerParams(
            collective_id=collective_id, has_side_effects=True, vmem_limit_bytes=56 * MIB
        ),
        name="attend",
    )(lengths, q, kv)


def attend_back_kernel(
    dims,
    heads,
    key_step,
    lengths,
    q_all,
    kv_all,
    do_in,
    out_t,
    lse,
    d_q_out,
    d_kv_out,
    do_all,
    keys,
    keys_t,
    values,
    queries,
    douts,
    d_q_t,
    q_rows,
    do_rows,
    side_out,
    side_in,
    ring_out,
    ring_in,
    mine,
    d_q_mine,
    d_kv_mine,
    send_sem,
    recv_sem,
    own_sem,
):
    z, y, x, cores = dims
    me = my_place(dims)
    bounds = clip_bounds(lengths)
    n_head, rows, width = q_all.shape
    amount = n_head * rows
    my_blk, my_head = blk_of(dims, me), head_of(dims, me)
    across = peers_across(dims)
    sides = axis_peers(dims, (1,))
    greet(dims, me, across + ring_and_sides(dims))
    push = Pushes(dims, me, send_sem, recv_sem)

    def to_head(src, dst, o):
        return push(src.at[head_of(dims, shifted(dims, me, o, 1))], dst, o)

    do_copies = [to_head(do_in, do_all.at[my_head], o) for o in across]
    own_do = pltpu.make_async_copy(do_in.at[my_head], do_all.at[my_head], own_sem.at[0])
    own_do.start()
    place = lax.broadcasted_iota(jnp.int32, (HD, 1), 0)

    def at_head(h):
        return slice(h * rows, (h + 1) * rows)

    for h in range(n_head):
        block = all_lanes(q_all[h], 0, width).astype(jnp.float32)
        q_t = block.T
        for a in range(heads):
            queries[a, :, at_head(h)] = with_query_tail(
                bounds,
                a,
                my_blk * amount + h * rows,
                q_t[a * HD : (a + 1) * HD],
                lse[a : a + 1, at_head(h)],
            )
            q_rows[a, at_head(h), :] = jnp.where(in_head(a, 1), block * HD ** (-0.5), 0.0).astype(low)
    for a in range(heads):
        d_q_t[a] = jnp.zeros(d_q_t.shape[1:], jnp.float32)
    own_do.wait()
    for copy in do_copies:
        copy.wait_recv()
    for h in range(n_head):
        block = all_lanes(do_all[h], 0, width).astype(jnp.float32)
        do_t = block.T
        for a in range(heads):
            part = do_t[a * HD : (a + 1) * HD]
            delta = jnp.sum(part * out_t[a * HD : (a + 1) * HD, at_head(h)], 0, keepdims=True)
            douts[a, :, at_head(h)] = with_tail(a, part, in_three(place, -delta)).astype(low)
            do_rows[a, at_head(h), :] = jnp.where(in_head(a, 1), block, 0.0).astype(low)

    def compute(offset, target):
        blk = blk_of(dims, shifted(dims, me, offset, 1))

        @pl.loop(0, n_head)
        def build(h):
            at = pl.ds(pl.multiple_of(h * rows, rows), rows)
            block = kv_all[blk, h]
            k_block, v_block = all_lanes(block, 0, width), all_lanes(block, width, width)
            k_t = k_block.astype(jnp.float32).T
            lane = lax.broadcasted_iota(jnp.int32, (1, LANES), 1)
            for a in range(heads):
                keys[a, at, :] = with_key_tail(bounds, a, blk * amount + h * rows, k_block)
                keys_t[a, :, at] = k_t[a * HD : (a + 1) * HD].astype(low)
                tail = lane - lane_of_tail(a)
                ones = jnp.where((tail >= 0) & (tail < 3), 1.0, 0.0)
                values[a, at, :] = jnp.where(
                    in_head(a, 1), v_block.astype(jnp.float32), ones
                ).astype(low)

        @pl.loop(0, amount // key_step)
        def key_block(k):
            at = pl.ds(pl.multiple_of(k * key_step, key_step), key_step)
            d_key = jnp.zeros((key_step, LANES), jnp.float32)
            d_value = jnp.zeros((key_step, LANES), jnp.float32)
            for a in range(heads):
                probs = jnp.exp(product(keys[a, at, :], queries[a]))
                d_probs = product(values[a, at, :], douts[a])
                d_scores = (probs * d_probs).astype(low)
                d_value = d_value + product(probs.astype(low), do_rows[a])
                d_key = d_key + product(d_scores, q_rows[a])
                d_q_t[a] = d_q_t[a] + product(keys_t[a, :, at], d_scores)
            target[at, :] = jnp.concatenate([d_key[:, :width], d_value[:, :width]], 1).astype(
                target.dtype
            )

    side, ring = {}, {}

    def send_sides(s):
        for o in sides:
            compute((z - s, o[1], 0, 0), side_out.at[s - 1, o[1] - 1])
            side[(s, o)] = push(side_out.at[s - 1, o[1] - 1], side_in.at[s - 1, o[1] - 1], o)

    def combine(s):
        for o in sides:
            side[(s, o)].wait_recv()
        if s > 1:
            ring[s - 1].wait_recv()

        for h in range(n_head):
            total = mine[(s - 1) % 2, at_head(h), :]
            for o in sides:
                total = total + side_in[s - 1, o[1] - 1, at_head(h), :].astype(jnp.float32)
            if s > 1:
                total = total + ring_in[s - 2, at_head(h), :].astype(jnp.float32)
            if s < z:
                ring_out[s - 1, at_head(h), :] = total.astype(low)
            else:
                d_kv_mine[h] = total.astype(low)
        if s < z:
            ring[s] = push(ring_out.at[s - 1], ring_in.at[s - 1], along(0, 1))

    for s in range(1, z + 1):
        send_sides(s)
        if s > 1:
            combine(s - 1)
        compute((z - s if s < z else 0, 0, 0, 0), mine.at[(s - 1) % 2])
    for h in range(n_head):
        block = jnp.concatenate([d_q_t[a, :, at_head(h)] for a in range(heads)], 0) * HD ** (-0.5)
        d_q_mine[h] = block.T.astype(low)
    copies = [to_head(d_q_mine, d_q_out.at[my_head], o) for o in across]
    own_q = pltpu.make_async_copy(d_q_mine.at[my_head], d_q_out.at[my_head], own_sem.at[1])
    own_q.start()
    combine(z)
    copies += [to_head(d_kv_mine, d_kv_out.at[my_head], o) for o in across]
    own_kv = pltpu.make_async_copy(d_kv_mine.at[my_head], d_kv_out.at[my_head], own_sem.at[2])
    own_kv.start()
    own_q.wait()
    own_kv.wait()
    for copy in copies:
        copy.wait_recv()
    push.finish()


def attend_back(dims, lengths, q, kv, dout, out_t, lse, heads, collective_id):
    z, y, x, cores = dims
    n_head, rows, width = q.shape
    amount = n_head * rows
    count = 3 * (n_head - 1) + z * (y - 1) + z - 1
    block = (amount, 2 * width)
    others = max(y - 1, 1)
    return pl.pallas_call(
        functools.partial(attend_back_kernel, dims, heads, 256),
        out_shape=(
            jax.ShapeDtypeStruct(q.shape, low),
            jax.ShapeDtypeStruct((n_head, rows, 2 * width), low),
        ),
        in_specs=[SMEM_SPEC] + [VMEM_SPEC] * 5,
        out_specs=[VMEM_SPEC] * 2,
        scratch_shapes=[
            pltpu.VMEM(q.shape, low),
            pltpu.VMEM((heads, amount, LANES), low),
            pltpu.VMEM((heads, HD, amount), low),
            pltpu.VMEM((heads, amount, LANES), low),
            pltpu.VMEM((heads, LANES, amount), low),
            pltpu.VMEM((heads, LANES, amount), low),
            pltpu.VMEM((heads, HD, amount), jnp.float32),
            pltpu.VMEM((heads, amount, LANES), low),
            pltpu.VMEM((heads, amount, LANES), low),
            pltpu.VMEM((z, others) + block, low),
            pltpu.VMEM((z, others) + block, low),
            pltpu.VMEM((max(z - 1, 1),) + block, low),
            pltpu.VMEM((max(z - 1, 1),) + block, low),
            pltpu.VMEM((2,) + block, jnp.float32),
            pltpu.VMEM(q.shape, low),
            pltpu.VMEM((n_head, rows, 2 * width), low),
            pltpu.SemaphoreType.DMA((count,)),
            pltpu.SemaphoreType.DMA((count,)),
            pltpu.SemaphoreType.DMA((3,)),
        ],
        compiler_params=pltpu.CompilerParams(
            collective_id=collective_id, has_side_effects=True, vmem_limit_bytes=60 * MIB
        ),
        name="attend_back",
    )(lengths, q, kv, dout, out_t, lse)


def part_shapes(n_head):
    width = HEADS // n_head * HD
    hidden = FF // n_head
    return (
        (D, width, True),
        (DI, 2 * width, True),
        (width, D, False),
        (D, 3 * width, True),
        (width, D, False),
        (D, hidden, True),
        (hidden, D, False),
        (D, C // n_head, True),
    )


def borders(n_head):
    result = [0]
    for rows, columns, joined in part_shapes(n_head):
        result.append(result[-1] + rows * columns // LANES)
    return result


def period(columns):
    amount = 1
    while amount * columns % LANES:
        amount *= 2
    return amount


def segments(start, amount, unit):
    result = []
    while amount > 0:
        which, at = divmod(start, unit)
        size = min(unit - at, amount)
        result.append((which, at, at + size))
        start, amount = start + size, amount - size
    return result


def joined_lanes(pieces):
    return pieces[0] if len(pieces) == 1 else jnp.concatenate(pieces, 1)


def lane_blocks(value):
    rows, columns = value.shape
    missing = -columns % LANES
    if missing:
        value = jnp.concatenate([value, jnp.zeros((rows, missing), value.dtype)], 1)
    return [value[:, i : i + LANES] for i in range(0, columns + missing, LANES)]


def every(first, amount, stride):
    return pl.ds(first, amount) if stride == 1 else pl.ds(first, amount, stride=stride)


def matrix_of(stage, first, rows, columns, line):
    if columns % LANES == 0:
        stride = columns // LANES
        for j in range(stride):
            yield j * LANES, stage[every(first + j, rows, stride), :]
        return
    height = period(columns)
    stride = height * columns // LANES
    for k in range(height):
        pieces = [
            stage[every(first + which, rows // height, stride), :][:, begin:end]
            for which, begin, end in segments(k * columns, columns, LANES)
        ]
        for i, piece in enumerate(lane_blocks(joined_lanes(pieces))):
            line[i, every(k, rows // height, height), :] = piece
    for i in range(-(-columns // LANES)):
        yield i * LANES, line[i, :rows, : min(columns - i * LANES, LANES)]


def matrix_into(stage, first, value, line):
    rows, columns = value.shape
    if columns % LANES == 0:
        stride = columns // LANES
        for j in range(stride):
            stage[every(first + j, rows, stride), :] = value[:, j * LANES : (j + 1) * LANES]
        return
    height = period(columns)
    stride = height * columns // LANES
    for i, piece in enumerate(lane_blocks(value)):
        line[i, :rows, :] = piece
    for i in range(stride):
        pieces = [
            line[which, every(k, rows // height, height), :][:, begin:end]
            for k, first_lane, last_lane in segments(i * LANES, LANES, columns)
            for which, begin, end in segments(first_lane, last_lane - first_lane, LANES)
        ]
        stage[every(first + i, rows // height, stride), :] = joined_lanes(pieces)


def load_stage(stage, held, first_shard, shard_rows, group):
    for b in range(held.shape[0]):
        stage[pl.ds(b * shard_rows, shard_rows), :] = held[b, group, :shard_rows, :].astype(jnp.float32)


def load_common(stage, held, valid):
    piece = held.shape[2]
    for b in range(held.shape[0]):
        for k in range(held.shape[1]):
            amount = min(piece, valid - k * piece)
            stage[b * valid + k * piece : b * valid + k * piece + amount, :] = held[b, k].astype(
                jnp.float32
            )[:amount]


def common_blocks(first_row, last_row, valid):
    return first_row // valid, -(-last_row // valid) - first_row // valid


def load_matrices(stage, first_row, n_head, group, which, targets, line):
    starts, shapes = borders(n_head), part_shapes(n_head)
    for m, target in zip(which, targets):
        rows, columns, joined = shapes[m]
        row = 0 if joined else group * rows
        column = group * columns if joined else 0
        for j, value in matrix_of(stage, starts[m] - first_row, rows, columns, line):
            size = value.shape[1]
            target[row : row + rows, column + j : column + j + size] = value.astype(target.dtype)


def normalized(x):
    centre = x - jnp.mean(x, -1, keepdims=True)
    rate = lax.rsqrt(jnp.mean(centre * centre, -1, keepdims=True) + norm_eps)
    return centre * rate, rate


def layer_norm(x, gain):
    return normalized(x)[0] * gain


def norm_pullback(x, gain, grad):
    unit, rate = normalized(x)
    inside = grad * gain
    both = jnp.mean(inside * unit, -1, keepdims=True)
    d_x = rate * (inside - jnp.mean(inside, -1, keepdims=True) - unit * both)
    return d_x, jnp.sum(grad * unit, 0, keepdims=True)


def head_lanes(group, heads, value):
    width = heads * HD
    block = value[:, group * width : (group + 1) * width]
    lane = lax.broadcasted_iota(jnp.int32, (1, width), 1)
    result = []
    for a in range(heads):
        here = (lane >= a * HD) & (lane < (a + 1) * HD)
        result.append((here, jnp.where(here, block, jnp.zeros_like(block))))
    return result


def place_of(bounds, first, amount):
    row = first + lax.broadcasted_iota(jnp.int32, (amount, 1), 0)
    opening = jnp.zeros((amount, 1), jnp.int32)
    for begin, end in bounds:
        opening = jnp.where((row >= begin) & (row < end), begin, opening)
    offset = row - opening
    turns = jnp.floor((offset.astype(jnp.float32) + 0.5) * (1.0 / LAT)).astype(jnp.int32)
    return offset - turns * LAT


def picked_rows(bounds, rows, n_head):
    first = lax.axis_index("blk") * (rows * n_head) + lax.axis_index("head") * rows
    lane = lax.broadcasted_iota(jnp.int32, (rows, LAT), 1)
    return jnp.where(lane == place_of(bounds, first, rows), 1.0, 0.0).astype(low)


def enc_scores(q_head, keys):
    return against(q_head, keys) * HD ** (-0.5)


def encode_kernel(
    n_head,
    shard_rows,
    valid,
    rows,
    lengths,
    weights,
    common,
    inputs_t,
    enc_query,
    enc_keyval,
    enc_output,
    self_project,
    gains,
    z_zero,
    h_zero,
    x_norm_t,
    q_enc,
    kv_enc,
    o_enc,
    z_one,
    h_one,
    q_self,
    kv_self,
    counts,
    held,
    held_common,
    held_counts,
    stage,
    stage_common,
    line,
    latent_table,
    sems,
):
    heads = HEADS // n_head
    width = heads * HD
    shards = held.shape[0]
    bounds = clip_bounds(lengths)
    first = DQ * D // LANES
    block, blocks = common_blocks(first, first + (LAT + 4) * D // LANES, valid)
    tail = shard_rows // TILE * TILE
    copies = [
        pltpu.make_async_copy(common.at[pl.ds(block, blocks)], held_common, sems.at[0]),
        pltpu.make_async_copy(weights.at[pl.ds(0, shards)], held, sems.at[1]),
        pltpu.make_async_copy(weights.at[:, :, pl.ds(tail, TILE)], held_counts, sems.at[2]),
    ]
    for copy in copies:
        copy.start()
    centre = inputs_t[...].astype(jnp.float32)
    centre = centre - jnp.mean(centre, 0, keepdims=True)
    rate = lax.rsqrt(jnp.mean(centre * centre, 0, keepdims=True) + norm_eps)
    x_norm_t[...] = (centre * rate).astype(low)
    copies[0].wait()
    load_common(stage_common, held_common, valid)
    first = first - block * valid
    for j, value in matrix_of(stage_common, first, LAT, D, line):
        latent_table[:, j : j + LANES] = value.astype(low)
    for j, value in matrix_of(stage_common, first + LAT * D // LANES, 4, D, line):
        gains[:, j : j + LANES] = value
    picked = picked_rows(bounds, rows, n_head)
    z_zero[...] = product(picked, latent_table[...])
    h_zero[...] = layer_norm(z_zero[...], gains[0:1, :]).astype(low)
    copies[2].wait()
    counted = held_counts[...].astype(jnp.float32)[:, :, shard_rows - tail : shard_rows - tail + 1]
    counts[...] = jnp.broadcast_to(jnp.sum(counted, (0, 1)), counts.shape)
    copies[1].wait()
    for g in range(n_head):
        load_stage(stage, held, 0, shard_rows, g)
        load_matrices(
            stage, 0, n_head, g, (0, 1, 2, 3), (enc_query, enc_keyval, enc_output, self_project), line
        )
    q_enc[...] = product(h_zero[...], enc_query[...]).astype(low)
    kv_enc[...] = contract_first(x_norm_t[...], enc_keyval[...]).astype(low)
    for g in range(n_head):
        keys = kv_enc[:, 2 * g * width : (2 * g + 1) * width]
        values = kv_enc[:, (2 * g + 1) * width : (2 * g + 2) * width]
        outcome = jnp.zeros((rows, width), jnp.float32)
        for here, q_head in head_lanes(g, heads, q_enc[...]):
            scores = enc_scores(q_head, keys)
            probs = jnp.exp(scores - jnp.max(scores, 1, keepdims=True))
            total = jnp.sum(probs, 1, keepdims=True)
            outcome = jnp.where(here, product(probs.astype(low), values) / total, outcome)
        o_enc[:, g * width : (g + 1) * width] = outcome.astype(low)
    z_one[...] = z_zero[...] + product(o_enc[...], enc_output[...])
    h_one[...] = layer_norm(z_one[...], gains[1:2, :]).astype(low)
    projected = product(h_one[...], self_project[...]).astype(low)
    for g in range(n_head):
        q_self[g] = projected[:, 3 * g * width : (3 * g + 1) * width]
        kv_self[g] = projected[:, (3 * g + 1) * width : (3 * g + 3) * width]


LINE = pltpu.VMEM((4, round_up(max(D, DI), 8), LANES), jnp.float32)


def shards_of(n_head, shard_rows, first, last):
    starts = borders(n_head)
    begin = starts[first] // shard_rows
    return begin, -(-starts[last] // shard_rows) - begin


def encode(lengths, weights, common, inputs_t, valid, rows, n_head, shard_rows):
    width = HEADS // n_head * HD
    begin, shards = shards_of(n_head, shard_rows, 0, 4)
    query_rows = DQ * D // LANES
    block, blocks = common_blocks(query_rows, query_rows + (LAT + 4) * D // LANES, valid)
    keys = inputs_t.shape[1]
    return pl.pallas_call(
        functools.partial(encode_kernel, n_head, shard_rows, valid, rows),
        out_shape=[
            shape_of((D, D)),
            shape_of((DI, 2 * D)),
            shape_of((D, D)),
            shape_of((D, 3 * D)),
            shape_of((4, D), jnp.float32),
            shape_of((rows, D), jnp.float32),
            shape_of((rows, D)),
            shape_of(inputs_t.shape),
            shape_of((rows, D)),
            shape_of((keys, 2 * D)),
            shape_of((rows, D)),
            shape_of((rows, D), jnp.float32),
            shape_of((rows, D)),
            shape_of((n_head, rows, width)),
            shape_of((n_head, rows, 2 * width)),
            shape_of((8, LANES), jnp.float32),
        ],
        in_specs=[SMEM_SPEC, ANY_SPEC, ANY_SPEC, VMEM_SPEC],
        out_specs=[VMEM_SPEC] * 16,
        scratch_shapes=[
            pltpu.VMEM((shards,) + weights.shape[1:], low),
            pltpu.VMEM((blocks,) + common.shape[1:], low),
            pltpu.VMEM(weights.shape[:2] + (TILE, LANES), low),
            pltpu.VMEM((shards * shard_rows, LANES), jnp.float32),
            pltpu.VMEM((blocks * valid, LANES), jnp.float32),
            LINE,
            pltpu.VMEM((LAT, D), low),
            pltpu.SemaphoreType.DMA((3,)),
        ],
        compiler_params=pltpu.CompilerParams(vmem_limit_bytes=56 * MIB),
        name="encode",
    )(lengths, weights, common, inputs_t)


def gelu_and_slope(x):
    rate = (2.0 / jnp.pi) ** 0.5
    cubic = 0.044715
    t = jnp.tanh(rate * (x + cubic * x * x * x))
    slope = 0.5 * (1.0 + t) + 0.5 * x * (1.0 - t * t) * rate * (1.0 + 3.0 * cubic * x * x)
    return 0.5 * x * (1.0 + t), slope


def my_column(marks, rows):
    turned = marks[...].astype(jnp.float32).T
    column = lax.broadcasted_iota(jnp.int32, turned.shape, 1)
    per_head = rows // LANES
    first = lax.axis_index("head") * per_head
    picked = [
        jnp.sum(jnp.where(column == first + k, turned, 0.0), 1, keepdims=True)
        for k in range(per_head)
    ]
    return jnp.concatenate(picked, 0) if per_head > 1 else picked[0]


def middle_kernel(
    n_head,
    shard_rows,
    valid,
    first_shard,
    rows,
    counts,
    weights,
    common,
    z_one,
    o_self,
    out_queries_t,
    labels,
    modality,
    labeled,
    gains,
    dout,
    d_two_out,
    tile,
    query_grad,
    gain_grads,
    grads,
    held,
    held_common,
    stage,
    stage_common,
    line,
    self_output,
    hidden_in,
    hidden_out,
    class_table,
    query_table,
    slope,
    activ,
    sems,
):
    heads = HEADS // n_head
    width, hidden, classes = heads * HD, FF // n_head, C // n_head
    shards = held.shape[0]
    first_row = first_shard * shard_rows
    starts = borders(n_head)
    copies = [
        pltpu.make_async_copy(common.at[pl.ds(0, held_common.shape[0])], held_common, sems.at[0]),
        pltpu.make_async_copy(weights.at[pl.ds(first_shard, shards)], held, sems.at[1]),
    ]
    for copy in copies:
        copy.start()
    copies[0].wait()
    load_common(stage_common, held_common, valid)
    for j, value in matrix_of(stage_common, 0, DQ, D, line):
        query_table[:, j : j + LANES] = value.astype(low)
    copies[1].wait()
    for g in range(n_head):
        load_stage(stage, held, first_shard, shard_rows, g)
        load_matrices(
            stage, first_row, n_head, g, (4, 5, 6, 7), (self_output, hidden_in, hidden_out, class_table), line
        )
    gain_two, gain_three = gains[2:3, :], gains[3:4, :]
    o_low = jnp.concatenate([o_self[g] for g in range(n_head)], 1)
    z_two = z_one[...] + product(o_low, self_output[...])
    h_two = layer_norm(z_two, gain_two).astype(low)
    value, bend = gelu_and_slope(product(h_two, hidden_in[...]))
    activ[...] = value.astype(low)
    slope[...] = bend
    z_three = z_two + product(activ[...], hidden_out[...])
    queries_t = out_queries_t[...]
    decoded = layer_norm(z_three, gain_three) + contract_first(queries_t, query_table[...])
    decoded = decoded.astype(low)
    logits = product(decoded, class_table[...])
    label, kind, counted = (my_column(marks, rows) for marks in (labels, modality, labeled))
    lane = lax.broadcasted_iota(jnp.int32, (rows, C), 1).astype(jnp.float32)
    is_target = jnp.where(lane == label, 1.0, 0.0)
    row_top = jnp.max(logits, 1, keepdims=True)
    row_lse = row_top + jnp.log(jnp.sum(jnp.exp(logits - row_top), 1, keepdims=True))
    loss = row_lse - jnp.sum(is_target * logits, 1, keepdims=True)
    weight = jnp.zeros((rows, 1), jnp.float32)
    place = lax.broadcasted_iota(jnp.int32, (1, LANES), 1)
    losses = jnp.zeros((1, LANES), jnp.float32)
    for m in range(MODES):
        member = jnp.where((kind == m) & (counted == 1.0), 1.0, 0.0)
        weight = weight + member / jnp.maximum(counts[0:1, m : m + 1], 1.0)
        losses = losses + jnp.where(place == m, jnp.sum(loss * member, 0, keepdims=True), 0.0)
    tile[...] = jnp.broadcast_to(losses, tile.shape)
    dlogits = (weight * (jnp.exp(logits - row_lse) - is_target)).astype(low)
    d_decoded = against(dlogits, class_table[...])
    matrix_into(query_grad, 0, product(queries_t, d_decoded.astype(low)), line)
    d_three, gain_three_grad = norm_pullback(z_three, gain_three, d_decoded)
    d_branch = d_three.astype(low)
    d_pre = (slope[...] * against(d_branch, hidden_out[...])).astype(low)
    d_middle, gain_two_grad = norm_pullback(z_two, gain_two, against(d_pre, hidden_in[...]))
    d_two = d_three + d_middle
    d_two_out[...] = d_two
    gain_grads[...] = jnp.concatenate([gain_two_grad, gain_three_grad], 0)
    d_two_low = d_two.astype(low)
    d_o = against(d_two_low, self_output[...]).astype(low)
    for g in range(n_head):
        dout[g] = d_o[:, g * width : (g + 1) * width]
    for g in range(n_head):
        results = (
            contract_first(o_self[g], d_two_low),
            contract_first(h_two, d_pre[:, g * hidden : (g + 1) * hidden]),
            contract_first(activ[:, g * hidden : (g + 1) * hidden], d_branch),
            contract_first(decoded, dlogits[:, g * classes : (g + 1) * classes]),
        )
        for m, result in zip((4, 5, 6, 7), results):
            matrix_into(stage, starts[m] - first_row, result, line)
        for b in range(shards):
            held[b, g, :shard_rows, :] = stage[pl.ds(b * shard_rows, shard_rows), :].astype(low)
    back = pltpu.make_async_copy(held, grads.at[pl.ds(first_shard, shards)], sems.at[2])
    back.start()
    back.wait()


def middle(counts, weights, common, z_one, o_self, out_queries_t, marks, gains, valid, n_head, shard_rows):
    rows = z_one.shape[0]
    begin, shards = shards_of(n_head, shard_rows, 4, 8)
    query_rows = DQ * D // LANES
    block, blocks = common_blocks(0, query_rows, valid)
    return pl.pallas_call(
        functools.partial(middle_kernel, n_head, shard_rows, valid, begin, rows),
        grid=(1,),
        out_shape=[
            shape_of(o_self.shape),
            shape_of((rows, D), jnp.float32),
            shape_of((8, LANES), jnp.float32),
            shape_of((query_rows, LANES), jnp.float32),
            shape_of((2, D), jnp.float32),
            shape_of(weights.shape),
        ],
        in_specs=[
            VMEM_SPEC,
            ANY_SPEC,
            ANY_SPEC,
            VMEM_SPEC,
            VMEM_SPEC,
            pl.BlockSpec((DQ, rows), lambda i: (0, lax.axis_index("head"))),
            VMEM_SPEC,
            VMEM_SPEC,
            VMEM_SPEC,
            VMEM_SPEC,
        ],
        out_specs=[VMEM_SPEC] * 5 + [ANY_SPEC],
        scratch_shapes=[
            pltpu.VMEM((shards,) + weights.shape[1:], low),
            pltpu.VMEM((blocks,) + common.shape[1:], low),
            pltpu.VMEM((shards * shard_rows, LANES), jnp.float32),
            pltpu.VMEM((blocks * valid, LANES), jnp.float32),
            LINE,
            pltpu.VMEM((D, D), low),
            pltpu.VMEM((D, FF), low),
            pltpu.VMEM((FF, D), low),
            pltpu.VMEM((D, C), low),
            pltpu.VMEM((DQ, D), low),
            pltpu.VMEM((rows, FF), jnp.float32),
            pltpu.VMEM((rows, FF), low),
            pltpu.SemaphoreType.DMA((3,)),
        ],
        compiler_params=pltpu.CompilerParams(vmem_limit_bytes=56 * MIB),
        name="middle",
    )(counts, weights, common, z_one, o_self, out_queries_t, *marks, gains)


def ending_kernel(
    n_head,
    shard_rows,
    valid,
    rows,
    lengths,
    grads_in,
    d_q_self,
    d_kv_self,
    d_two,
    gains,
    gain_grads,
    query_grad,
    enc_query,
    enc_keyval,
    enc_output,
    self_project,
    z_zero,
    h_zero,
    x_norm_t,
    q_enc,
    kv_enc,
    o_enc,
    z_one,
    h_one,
    grads,
    common_grad,
    held,
    stage,
    stage_common,
    line,
    d_q,
    d_kv,
    sems,
):
    heads = HEADS // n_head
    width = heads * HD
    shards = held.shape[0]
    starts = borders(n_head)
    shared = pltpu.make_async_copy(grads_in.at[pl.ds(shards - 1, 1)], held.at[pl.ds(shards - 1, 1)], sems.at[0])
    shared.start()
    d_projected = [jnp.concatenate([d_q_self[g], d_kv_self[g]], 1) for g in range(n_head)]
    whole = jnp.concatenate(d_projected, 1)
    d_middle, gain_one_grad = norm_pullback(
        z_one[...], gains[1:2, :], against(whole, self_project[...])
    )
    d_one = d_two[...] + d_middle
    d_one_low = d_one.astype(low)
    d_o = against(d_one_low, enc_output[...]).astype(low)
    for g in range(n_head):
        keys = kv_enc[:, 2 * g * width : (2 * g + 1) * width]
        values = kv_enc[:, (2 * g + 1) * width : (2 * g + 2) * width]
        d_key = jnp.zeros(keys.shape, jnp.float32)
        d_value = jnp.zeros(keys.shape, jnp.float32)
        d_query = jnp.zeros((rows, width), jnp.float32)
        for (here, q_head), (unused, do_head) in zip(
            head_lanes(g, heads, q_enc[...]), head_lanes(g, heads, d_o)
        ):
            scores = enc_scores(keys, q_head)
            probs = jnp.exp(scores - jnp.max(scores, 0, keepdims=True))
            probs = probs / jnp.sum(probs, 0, keepdims=True)
            d_probs = against(values, do_head)
            delta = jnp.sum(probs * d_probs, 0, keepdims=True)
            d_scores = (probs * (d_probs - delta)).astype(low)
            d_value = d_value + product(probs.astype(low), do_head)
            d_key = d_key + product(d_scores, q_head)
            d_query = jnp.where(here, contract_first(d_scores, keys), d_query)
        d_q[:, g * width : (g + 1) * width] = (d_query * HD ** (-0.5)).astype(low)
        d_kv[:, 2 * g * width : (2 * g + 1) * width] = (d_key * HD ** (-0.5)).astype(low)
        d_kv[:, (2 * g + 1) * width : (2 * g + 2) * width] = d_value.astype(low)
    d_middle, gain_zero_grad = norm_pullback(
        z_zero[...], gains[0:1, :], against(d_q[...], enc_query[...])
    )
    d_zero = d_one + d_middle
    d_zero_top = d_zero.astype(low)
    d_zero_rest = (d_zero - d_zero_top.astype(jnp.float32)).astype(low)
    picked = picked_rows(clip_bounds(lengths), rows, n_head)
    latent_grad = contract_first(picked, d_zero_top) + contract_first(picked, d_zero_rest)
    query_rows = query_grad.shape[0]
    stage_common[:query_rows] = query_grad[...]
    matrix_into(stage_common, query_rows, latent_grad, line)
    all_gains = jnp.concatenate([gain_zero_grad, gain_one_grad, gain_grads[...]], 0)
    matrix_into(stage_common, query_rows + LAT * D // LANES, all_gains, line)
    piece = common_grad.shape[2]
    for b in range(common_grad.shape[0]):
        for k in range(common_grad.shape[1]):
            amount = min(piece, valid - k * piece)
            block = stage_common[b * valid + k * piece : b * valid + k * piece + amount, :]
            if amount < piece:
                block = jnp.concatenate([block, jnp.zeros((piece - amount, LANES), jnp.float32)], 0)
            common_grad[b, k] = block.astype(low)
    shared.wait()
    kept = shards * shard_rows - starts[4]
    for g in range(n_head):
        results = (
            contract_first(h_zero[...], d_q[:, g * width : (g + 1) * width]),
            product(x_norm_t[...], d_kv[:, 2 * g * width : (2 * g + 2) * width]),
            contract_first(o_enc[:, g * width : (g + 1) * width], d_one_low),
            contract_first(h_one[...], d_projected[g]),
        )
        if kept:
            stage[pl.ds((shards - 1) * shard_rows, shard_rows), :] = held[
                shards - 1, g, :shard_rows, :
            ].astype(jnp.float32)
        for m, result in zip((0, 1, 2, 3), results):
            matrix_into(stage, starts[m], result, line)
        for b in range(shards):
            held[b, g, :shard_rows, :] = stage[pl.ds(b * shard_rows, shard_rows), :].astype(low)
    back = pltpu.make_async_copy(held, grads.at[pl.ds(0, shards)], sems.at[1])
    back.start()
    back.wait()


def ending(lengths, grads, d_self, d_two, gains, gain_grads, query_grad, kept, common_shape, valid, shard_rows):
    rows = d_two.shape[0]
    n_head = grads.shape[1]
    begin, shards = shards_of(n_head, shard_rows, 0, 4)
    keys = kept[6].shape[1]
    common_rows = (DQ + LAT + 4) * D // LANES
    return pl.pallas_call(
        functools.partial(ending_kernel, n_head, shard_rows, valid, rows),
        out_shape=[shape_of(grads.shape), shape_of(common_shape)],
        in_specs=[SMEM_SPEC, ANY_SPEC] + [VMEM_SPEC] * 18,
        out_specs=[ANY_SPEC, VMEM_SPEC],
        input_output_aliases={1: 0},
        scratch_shapes=[
            pltpu.VMEM((shards,) + grads.shape[1:], low),
            pltpu.VMEM((shards * shard_rows, LANES), jnp.float32),
            pltpu.VMEM((common_rows, LANES), jnp.float32),
            LINE,
            pltpu.VMEM((rows, D), low),
            pltpu.VMEM((keys, 2 * D), low),
            pltpu.SemaphoreType.DMA((2,)),
        ],
        compiler_params=pltpu.CompilerParams(vmem_limit_bytes=56 * MIB),
        name="ending",
    )(lengths, grads, *d_self, d_two, gains, gain_grads, query_grad, *kept)


def adam_step(weight, first, second, grad):
    first = beta_one * first + (1 - beta_one) * grad
    second = beta_two * second + (1 - beta_two) * grad * grad
    fixed_first = first / (1 - beta_one**STEP)
    fixed_second = second / (1 - beta_two**STEP)
    weight = weight - learn_rate * (
        fixed_first / (jnp.sqrt(fixed_second) + adam_eps) + weight_decay * weight
    )
    return (weight, first, second, weight.astype(low))


def per_device(
    inputs,
    out_queries,
    clip_lengths,
    labels,
    modality,
    labeled,
    head_params,
    head_first,
    head_second,
    common_params,
    common_first,
    common_second,
):
    n_head, n_blk = lax.axis_size("head"), lax.axis_size("blk")
    dims = grid_of(n_blk, n_head)
    rows = labels.shape[0] // n_head
    heads_here = HEADS // n_head
    n_h, n_c = head_params.shape[0], common_params.shape[0]
    shard_rows, common_rows = n_h // LANES, -(-n_c // LANES)
    head_rows = round_up(shard_rows + 1, TILE)
    piece_rows = round_up(-(-common_rows // n_head), TILE)
    marks = [x.reshape(-1, LANES) for x in (labels, modality, labeled)]
    head_wide = head_params.reshape(shard_rows, LANES)
    common_wide = jnp.pad(common_params, (0, common_rows * LANES - n_c)).reshape(common_rows, LANES)
    weights, common = gather_all(dims, marks, (head_wide, common_wide), (head_rows, piece_rows), 0)
    valid = common_rows
    if n_c % LANES:
        common = common.reshape(n_blk, -1)[:, :n_c].reshape(-1, LANES)
        valid = common.shape[0]
        common = jnp.pad(common, ((0, -valid % TILE), (0, 0)))[None, None]

    encoded = encode(clip_lengths, weights, common, inputs.T, valid, rows, n_head, shard_rows)
    gains, z_one, counts = encoded[4], encoded[11], encoded[15]
    o_self, lse_self, out_self_t, q_all, kv_all = attend(
        dims, clip_lengths, encoded[13], encoded[14], heads_here, 1
    )
    dout, d_two, tile, query_grad, gain_grads, grads = middle(
        counts, weights, common, z_one, o_self, out_queries.T, marks, gains, valid, n_head, shard_rows
    )
    d_self = attend_back(dims, clip_lengths, q_all, kv_all, dout, out_self_t, lse_self, heads_here, 2)
    kept = encoded[:4] + encoded[5:13]
    grads, common_grad = ending(
        clip_lengths,
        grads,
        d_self,
        d_two,
        gains,
        gain_grads,
        query_grad,
        kept,
        common.shape,
        valid,
        shard_rows,
    )
    if n_c % LANES:
        common_grad = common_grad[0, 0, :valid].reshape(n_blk, n_c)
        common_grad = jnp.pad(common_grad, ((0, 0), (0, n_head * piece_rows * LANES - n_c)))
        common_grad = common_grad.reshape(n_blk, n_head, piece_rows, LANES)
    head_share, common_share, totals = reduce_all(
        dims, (grads, common_grad), (shard_rows, common_rows), tile, 3
    )
    label_counts, loss_sums = counts[0, :MODES], totals[0, :MODES]
    clip_norm = jnp.sqrt(totals[0, MODES])
    factor = jnp.minimum(1.0, clip_limit / clip_norm)
    head_share, common_share = head_share.reshape(-1), common_share.reshape(-1)[:n_c]
    head_out = adam_step(head_params, head_first, head_second, head_share * factor)
    common_out = adam_step(common_params, common_first, common_second, common_share * factor)
    return head_out + common_out + (loss_sums, label_counts, clip_norm)


def solution(mesh):
    placed = (
        P("blk", None),
        P("blk", None),
        P(),
        P("blk"),
        P("blk"),
        P("blk"),
        P(("head", "blk")),
        P(("head", "blk")),
        P(("head", "blk")),
        P("blk"),
        P("blk"),
        P("blk"),
    )
    return jax.shard_map(
        per_device,
        mesh=mesh,
        in_specs=placed,
        out_specs=(
            P(("head", "blk")),
            P(("head", "blk")),
            P(("head", "blk")),
            P(("head", "blk")),
            P("blk"),
            P("blk"),
            P("blk"),
            P("blk"),
            P(),
            P(),
            P(),
        ),
        check_vma=False,
    )
```

```python
import functools

import jax
import jax.numpy as jnp
from jax import lax
from jax.experimental import pallas as pl
from jax.experimental.pallas import tpu as pltpu
from jax.sharding import PartitionSpec as P

D = 512
HEADS = 8
HD = 64
FF = 2048
DI = 704
DQ = 1026
C = 704
LAT = 784
MODES = 3
STEP = 10
LANES = 128
TILE = 16

norm_eps = 1e-05
learn_rate = 0.1
beta_one = 0.9
beta_two = 0.999
adam_eps = 1e-08
weight_decay = 0.01
clip_limit = 0.05
big_negative = -1e30
low = jnp.bfloat16
MESH = pl.DeviceIdType.MESH
MIB = 1 << 20
VMEM_SPEC = pl.BlockSpec(memory_space=pltpu.VMEM)
SMEM_SPEC = pl.BlockSpec(memory_space=pltpu.SMEM)
ANY_SPEC = pl.BlockSpec(memory_space=pl.ANY)


def shape_of(shape, dtype=low):
    return jax.ShapeDtypeStruct(shape, dtype)


def round_up(n, unit):
    return -(-n // unit) * unit


def grid_of(n_blk, n_head):
    cores = 2 if n_head % 2 == 0 else 1
    x = n_head // cores
    y = x if n_blk % x == 0 else 1
    return (n_blk // y, y, x, cores)


def my_place(dims):
    blk, head = lax.axis_index("blk"), lax.axis_index("head")
    return (blk // dims[1], lax.rem(blk, dims[1]), head // dims[3], lax.rem(head, dims[3]))


def shifted(dims, me, offset, sign):
    return tuple(
        m if o == 0 else lax.rem(m + (o if sign > 0 else n - o), n)
        for m, o, n in zip(me, offset, dims)
    )


def blk_of(dims, place):
    return place[0] * dims[1] + place[1]


def head_of(dims, place):
    return place[2] * dims[3] + place[3]


def device_of(dims, place):
    return {"blk": blk_of(dims, place), "head": head_of(dims, place)}


def along(axis, d):
    return tuple(d if a == axis else 0 for a in range(4))


def greet(dims, me, offsets):
    barrier = pltpu.get_barrier_semaphore()
    for offset in offsets:
        pl.semaphore_signal(
            barrier,
            inc=1,
            device_id=device_of(dims, shifted(dims, me, offset, 1)),
            device_id_type=MESH,
        )
    pl.semaphore_wait(barrier, len(offsets))


def axis_peers(dims, axes):
    return [along(axis, d) for axis in axes for d in range(1, dims[axis])]


def remote(src, dst, send_sem, recv_sem, place, dims):
    return pltpu.make_async_remote_copy(
        src_ref=src,
        dst_ref=dst,
        send_sem=send_sem,
        recv_sem=recv_sem,
        device_id=device_of(dims, place),
        device_id_type=MESH,
    )


AHEAD = 10
RING = 0


def in_order(first, follow, size_of, result):
    queues, busy, flight = {}, {}, {}
    now = 0.0

    def ready(messages):
        for message in messages:
            queues.setdefault(message[1], []).append(message)

    ready(first)
    while True:
        for axis in sorted(queues):
            queue, going = queues[axis], flight.setdefault(axis, [])
            while queue and (not going or busy[axis] < now + AHEAD):
                message = min(queue)
                queue.remove(message)
                busy[axis] = max(now, busy.get(axis, 0.0)) + size_of(message)
                going.append((busy[axis] + 1.5, message))
                result.append((now, True, message))
        arrivals = [min(going) for going in flight.values() if going]
        if not arrivals:
            return
        arrival = min(arrivals)
        flight[arrival[1][1]].remove(arrival)
        now = max(now, arrival[0])
        result.append((now, False, arrival[1]))
        ready(follow(arrival[1], now))


def time_of(rows, axis):
    return rows * LANES * 2 / (300e3 if axis == 3 else 45e3)


def with_at(offset, axis, d):
    return offset[:axis] + (d,) + offset[axis + 1 :]


def all_offsets(dims, axes):
    offsets = [(0, 0, 0, 0)]
    for a in axes:
        offsets = [with_at(o, a, d) for o in offsets for d in range(dims[a])]
    return offsets


def cut(array, rows, planes, orders):
    result = []
    first = 0
    for n, order in enumerate(orders):
        end = rows * (n + 1) // len(orders) // TILE * TILE if n + 1 < len(orders) else rows
        result.append((array, first, end - first, planes, order))
        first = end
    return tuple(result)


class Copies:
    def __init__(self, dims, me, send_sem, recv_sem):
        self.dims, self.me, self.send_sem, self.recv_sem = dims, me, send_sem, recv_sem
        self.made, self.always, self.maybe = 0, [], []

    def make(self, src, dst, offset):
        i = self.made
        self.made += 1
        place = shifted(self.dims, self.me, offset, 1)
        return remote(src, dst, self.send_sem.at[i], self.recv_sem.at[i], place, self.dims)

    def again(self, i, src, dst, offset):
        place = shifted(self.dims, self.me, offset, 1)
        return remote(src, dst, self.send_sem.at[i], self.recv_sem.at[i], place, self.dims)

    def __call__(self, src, dst, offset):
        copy = self.make(src, dst, offset)
        copy.start()
        self.always.append(copy)
        return copy

    def finish(self):
        for copy in self.always:
            copy.wait_send()
        for condition, copy in self.maybe:
            pl.when(condition)(copy.wait_send)


class InSteps:
    def __init__(self, events, stretch):
        self.events, self.stretch, self.at = events, stretch, 0

    def step(self, when):
        while self.at < len(self.events) and self.events[self.at][0] * self.stretch <= when:
            unused, kind, what = self.events[self.at]
            self.at += 1
            if kind is None:
                self.add(*what)
            elif kind:
                self.send(what)
            else:
                self.arrive(what)

    def rest(self):
        self.step(float("inf"))


class Gather(InSteps):
    def __init__(self, dims, parts, copies, outs, stretch=1.0):
        self.dims, self.parts, self.copies, self.outs = dims, parts, copies, outs
        self.flying = {}
        events = []

        def onward(p, plane, offset, position):
            order = parts[p][4]
            return [
                ((k, -plane, p, offset), axis, p, plane, with_at(offset, axis, d))
                for k, axis in enumerate(order)
                if k > position
                for d in range(1, dims[axis])
            ]

        def follow(message, now):
            rank, axis, p, plane, offset = message
            return onward(p, plane, offset, rank[0])

        first = [
            ((-1, -plane, p), 0, p, plane, (0, 0, 0, 0))
            for p, part in enumerate(parts)
            for plane in part[3]
        ]
        in_order(first, follow, lambda m: time_of(parts[m[2]][2], m[1]), events)
        super().__init__(events, stretch)

    def block(self, p, plane, offset):
        array, first, rows, planes, order = self.parts[p]
        place = (plane,) + shifted(self.dims, self.copies.me, offset, -1)[1:]
        at = (blk_of(self.dims, place), head_of(self.dims, place), pl.ds(first, rows))
        return self.outs[array].at[at]

    def send(self, message):
        rank, axis, p, plane, offset = message
        z, planes = self.copies.me[0], self.dims[0]
        if axis:
            block = self.block(p, plane, with_at(offset, axis, 0))
            self.flying[message[1:]] = self.copies(block, block, along(axis, offset[axis]))
            return
        block = self.block(p, plane, offset)
        up = self.copies.make(block, block, along(0, 1))
        down = self.copies.make(block, block, along(0, planes - 1))
        self.flying[message[1:]] = (up, down)
        for copy, there, here in ((up, z < planes - 1, z >= plane), (down, z > 0, z <= plane)):
            self.copies.maybe.append((there & here, copy))
            pl.when((z == plane) & there)(copy.start)

    def arrive(self, message):
        rank, axis, p, plane, offset = message
        flying = self.flying[message[1:]]
        if axis:
            flying.wait_recv()
            return
        up, down = flying
        z, planes = self.copies.me[0], self.dims[0]

        @pl.when(z > plane)
        def from_below():
            up.wait_recv()
            pl.when(z < planes - 1)(up.start)

        @pl.when(z < plane)
        def from_above():
            down.wait_recv()
            pl.when(z > 0)(down.start)


def gather_copies(dims, parts):
    z, y, x, cores = dims
    return sum(len(part[3]) * (y * x * cores - 1 + 2) for part in parts)


def lower_planes(dims, n_head, shard_rows):
    first, shards = shards_of(n_head, shard_rows, 0, 4)
    return -(-shards // dims[1])


YXC, XYC = (1, 2, 3), (2, 1, 3)
CXY, CYX = (3, 2, 1), (3, 1, 2)


def gather_kernel(
    dims,
    parts,
    labels,
    modality,
    labeled,
    head_params,
    common_params,
    head_all,
    common_all,
    head_low,
    common_low,
    common_wide,
    send_sem,
    recv_sem,
    own_sem,
):
    me = my_place(dims)
    my_blk, my_head = blk_of(dims, me), head_of(dims, me)
    shard_rows, common_rows = head_params.shape[0], common_params.shape[0]
    tail = shard_rows // TILE * TILE
    head_low[:tail] = head_params[:tail].astype(low)
    padding = jnp.zeros((head_low.shape[0] - shard_rows, LANES), jnp.float32)
    if shard_rows > tail:
        padding = jnp.concatenate([head_params[tail:], padding], 0)
    head_low[tail:] = padding.astype(low)
    own_head = pltpu.make_async_copy(head_low, head_all.at[my_blk, my_head], own_sem.at[0])
    own_head.start()
    lane = lax.broadcasted_iota(jnp.int32, (1, LANES), 1)
    counts = jnp.zeros(labels.shape, jnp.float32)
    for m in range(MODES):
        member = jnp.where((labeled[...] == 1) & (modality[...] == m), 1.0, 0.0)
        counts = counts + jnp.where(lane == m, jnp.sum(member, 1, keepdims=True), 0.0)
    common_wide[...] = jnp.zeros(common_wide.shape, jnp.float32)
    common_wide[:common_rows] = common_params[...]
    common_wide[common_rows : common_rows + labels.shape[0]] = counts
    piece = common_low.shape[0]
    common_low[...] = common_wide[pl.ds(pl.multiple_of(my_head * piece, TILE), piece)].astype(low)
    own_common = pltpu.make_async_copy(common_low, common_all.at[my_blk, my_head], own_sem.at[1])
    own_common.start()
    copies = Copies(dims, me, send_sem, recv_sem)
    greet(dims, me, ring_and_others(dims))
    own_head.wait()
    own_common.wait()
    gather = Gather(dims, parts, copies, (head_all, common_all))
    gather.rest()
    copies.finish()


def ring_and_others(dims):
    ring = {along(RING, 1 % dims[RING]), along(RING, (dims[RING] - 1) % dims[RING])}
    return sorted(ring - {(0, 0, 0, 0)}) + axis_peers(dims, (1, 2, 3))


def gather_all(dims, marks, params, rows, lower, collective_id):
    z, y, x, cores = dims
    parts = cut(0, rows[0], range(lower), (YXC, XYC, YXC, XYC))
    parts = parts + cut(1, rows[1], range(z), (XYC,))
    count = gather_copies(dims, parts)
    return pl.pallas_call(
        functools.partial(gather_kernel, dims, parts),
        out_shape=[shape_of((z * y, x * cores, n, LANES)) for n in rows],
        in_specs=[VMEM_SPEC] * 5,
        out_specs=[ANY_SPEC] * 2,
        scratch_shapes=[pltpu.VMEM((n, LANES), low) for n in rows]
        + [
            pltpu.VMEM((x * cores * rows[1], LANES), jnp.float32),
            pltpu.SemaphoreType.DMA((count,)),
            pltpu.SemaphoreType.DMA((count,)),
            pltpu.SemaphoreType.DMA((2,)),
        ],
        compiler_params=pltpu.CompilerParams(
            collective_id=collective_id, has_side_effects=True, vmem_limit_bytes=56 * MIB
        ),
        name="gather_weights",
    )(*marks, *params)


def row_chunk(rows):
    for count in (4, 3, 2):
        if rows % (count * TILE) == 0:
            return rows // count
    return rows


class Reduce(InSteps):
    def __init__(self, dims, parts, copies, srcs, buffers, outs, kept=None, stretch=1.0):
        self.dims, self.parts, self.copies, self.srcs, self.outs, self.kept = dims, parts, copies, srcs, outs, kept
        self.buffers, self.flying = {}, {}
        buffers = list(buffers)
        for p, part in enumerate(parts):
            for position in range(len(part[4])):
                self.buffers[(p, position)] = buffers.pop(0)
            if outs is not None:
                self.buffers[(p, 3)] = buffers.pop(0)
        ready, arrived, events = set(), set(), []

        def message(p, position, plane, offset):
            return ((position, plane, tuple(-o for o in offset), p), parts[p][4][position], p, position, plane, offset)

        def done(p, position, plane, offset, now):
            ready.add((p, position, plane, offset))
            order = parts[p][4]
            if position == len(order):
                return chain(p, plane, 1) if outs is not None else []
            first = offset[order[position]] != 0
            sent = [message(p, position, plane, offset)] if first else []
            return sent + advance(p, position, plane, offset, now)

        def chain(p, plane, k):
            return [((3, k, plane, p), 0, p, 3, plane, k)]

        def advance(p, position, plane, offset, now):
            axis = parts[p][4][position]
            start = with_at(offset, axis, 0)
            if (p, position, plane, start) not in ready or (p, position + 1, plane, start) in ready:
                return []
            for d in range(1, dims[axis]):
                if (p, position, plane, with_at(start, axis, d)) not in arrived:
                    return []
            events.append((now, None, (p, position, plane, start)))
            return done(p, position + 1, plane, start, now)

        def follow(sent, now):
            rank, axis, p, position, plane, offset = sent
            if position == 3:
                if offset < dims[0] - 1:
                    return chain(p, plane, offset + 1)
                events.append((now, None, (p, 3, plane, None)))
                return []
            arrived.add((p, position, plane, offset))
            return advance(p, position, plane, offset, now)

        first = []
        for p, part in enumerate(parts):
            for plane in part[3]:
                for offset in all_offsets(dims, part[4]):
                    first += done(p, 0, plane, offset, 0.0)
        in_order(first, follow, lambda m: time_of(parts[m[2]][2], m[1]), events)
        super().__init__(events, stretch)

    @staticmethod
    def scratch(dims, parts, chained):
        result = []
        for array, first, rows, planes, order in parts:
            for position, axis in enumerate(order):
                rest = len(all_offsets(dims, order[position + 1 :]))
                result.append(pltpu.VMEM((len(planes), rest, dims[axis] - 1, rows, LANES), low))
            if chained:
                result.append(pltpu.VMEM((len(planes), 2, rows, LANES), low))
        return result

    @staticmethod
    def count(dims, parts, chained):
        z, y, x, cores = dims
        return sum(
            len(planes) * ((y * x * cores - 1 if order else 0) + (2 if chained else 0))
            for array, first, rows, planes, order in parts
        )

    def slot(self, p, position, plane, offset):
        planes, order = self.parts[p][3:]
        axis = order[position]
        k = all_offsets(self.dims, order[position + 1 :]).index(with_at(offset, axis, 0))
        return self.buffers[(p, position)].at[plane - planes[0], k, max(offset[axis] - 1, 0)]

    def summed(self, p, position, plane, offset):
        array, first, rows, planes, order = self.parts[p]
        if position:
            return self.slot(p, position - 1, plane, offset)
        at = plane - planes[0]
        if not order:
            return self.srcs[array].at[at, pl.ds(first, rows)]
        place = shifted(self.dims, self.copies.me, offset, 1)
        place = (at,) + place[1:]
        return self.srcs[array].at[blk_of(self.dims, place), head_of(self.dims, place), pl.ds(first, rows)]

    def total(self, p, target, target_first, refs):
        rows = self.parts[p][2]
        step = row_chunk(rows)

        @pl.loop(0, rows // step)
        def some_rows(n):
            at = pl.ds(pl.multiple_of(n * step, step), step)
            total = refs[0][at].astype(jnp.float32)
            for ref in refs[1:]:
                total = total + ref[at].astype(jnp.float32)
            there = pl.ds(pl.multiple_of(target_first + n * step, TILE), step)
            target[there] = total.astype(target.dtype)

    def add(self, p, position, plane, offset):
        array, first, rows, planes, order = self.parts[p]
        if position == 3:
            self.last(p, plane)
            return
        axis = order[position]
        arrivals = [self.slot(p, position, plane, with_at(offset, axis, d)) for d in range(1, self.dims[axis])]
        refs = [self.summed(p, position, plane, offset)] + arrivals
        if self.outs is None and position == len(order) - 1:
            self.total(p, self.kept.at[plane - planes[0]], first, refs)
        else:
            self.total(p, arrivals[0], 0, refs)

    def send(self, message):
        rank, axis, p, position, plane, offset = message
        if position < 3:
            source = self.summed(p, position, plane, offset)
            target = self.slot(p, position, plane, offset)
            self.flying[message[1:]] = self.copies(source, target, along(axis, offset[axis]))
            return
        k, z, planes = offset, self.copies.me[0], self.dims[0]
        mine = self.summed(p, len(self.parts[p][4]), plane, (0, 0, 0, 0))
        if k == 1:
            made = []
            for side in range(2):
                number = self.copies.made
                away = along(0, 1 if side else planes - 1)
                made.append((number, away, self.copies.make(mine, self.arrived(p, plane, side), away)))
            self.flying[(p, plane)] = made
        for side in range(2):
            number, away, from_mine = self.flying[(p, plane)][side]
            sender = k - 1 if side else planes - k
            if not (sender < plane if side else sender > plane):
                continue
            arrived = self.arrived(p, plane, side)
            copy = from_mine if k == 1 else self.copies.again(number, arrived, arrived, away)
            self.copies.maybe.append((z == sender, copy))

            @pl.when(z == sender)
            def pass_on():
                if k > 1:
                    from_mine.wait_recv()
                    self.total(p, arrived, 0, [arrived, mine])
                copy.start()

    def arrived(self, p, plane, side):
        return self.buffers[(p, 3)].at[plane - self.parts[p][3][0], side]

    def arrive(self, message):
        if message[3] < 3:
            self.flying[message[1:]].wait_recv()

    def last(self, p, plane):
        array, first, rows, planes, order = self.parts[p]

        @pl.when(self.copies.me[0] == plane)
        def here():
            refs = [self.summed(p, len(order), plane, (0, 0, 0, 0))]
            for side in range(2):
                if plane > 0 if side else plane < self.dims[0] - 1:
                    self.flying[(p, plane)][side][2].wait_recv()
                    refs.append(self.arrived(p, plane, side))
            self.total(p, self.outs[array], first, refs)


def reduce_kernel(dims, parts, *refs):
    lower, upper, common, tile = refs[:4]
    head_out, common_out, totals = refs[4:7]
    places = len(Reduce.scratch(dims, parts, True))
    buffers = refs[7 : 7 + places]
    head_sum, common_sum, shares, send_sem, recv_sem, near_tiles, far_tiles = refs[7 + places :]
    me = my_place(dims)
    z, y, x, cores = dims
    across = peers_across(dims)
    others = [o for o in all_offsets(dims, (0, 1)) if any(o)]
    met = ring_and_others(dims)
    greet(dims, me, met + [o for o in across + others if o not in met])
    copies = Copies(dims, me, send_sem, recv_sem)
    reduction = Reduce(dims, parts, copies, (lower, upper, common), buffers, (head_sum, head_sum, common_sum))
    reduction.rest()
    my_head, my_blk = head_of(dims, me), blk_of(dims, me)
    shares[my_head] = common_sum[...].astype(low)
    share_copies = [copies(shares.at[my_head], shares.at[my_head], o) for o in across]
    amount = head_out.shape[0]
    head_out[...] = head_sum[:amount]
    squares = jnp.sum(head_sum[:amount] * head_sum[:amount], 0, keepdims=True)
    squares = squares + jnp.sum(common_sum[...] * common_sum[...], 0, keepdims=True)
    lane = lax.broadcasted_iota(jnp.int32, (1, LANES), 1)
    near_tiles[my_head] = tile[...] + jnp.where(
        lane == MODES, jnp.sum(squares, 1, keepdims=True), 0.0
    )
    near = [copies(near_tiles.at[my_head], near_tiles.at[my_head], o) for o in across]
    for copy in near:
        copy.wait_recv()
    far_tiles[my_blk] = jnp.sum(near_tiles[...], 0)
    far = [copies(far_tiles.at[my_blk], far_tiles.at[my_blk], o) for o in others]
    for copy in share_copies:
        copy.wait_recv()
    piece = shares.shape[1]
    for k in range(x * cores):
        amount = min(piece, common_out.shape[0] - k * piece)
        common_out[k * piece : k * piece + amount] = shares[k].astype(jnp.float32)[:amount]
    for copy in far:
        copy.wait_recv()
    totals[...] = jnp.sum(far_tiles[...], 0)
    copies.finish()


def reduce_all(dims, lower_grads, upper_sums, common_grads, valid, tile, collective_id):
    z, y, x, cores = dims
    lower = lower_grads.shape[0] // y
    rows = [lower_grads.shape[2], common_grads.shape[2]]
    parts = cut(1, rows[0], range(lower, z), ((), ()))
    parts = parts + cut(0, rows[0], range(lower), (CXY, CYX, CXY, CYX))
    parts = parts + cut(2, rows[1], range(z), (CXY,))
    count = Reduce.count(dims, parts, True) + 2 * (x * cores - 1) + z * y - 1
    return pl.pallas_call(
        functools.partial(reduce_kernel, dims, parts),
        out_shape=[
            shape_of((valid[0], LANES), jnp.float32),
            shape_of((valid[1], LANES), jnp.float32),
            shape_of((8, LANES), jnp.float32),
        ],
        in_specs=[VMEM_SPEC] * 4,
        out_specs=[VMEM_SPEC] * 3,
        scratch_shapes=Reduce.scratch(dims, parts, True)
        + [pltpu.VMEM((n, LANES), jnp.float32) for n in rows]
        + [
            pltpu.VMEM((x * cores, rows[1], LANES), low),
            pltpu.SemaphoreType.DMA((count,)),
            pltpu.SemaphoreType.DMA((count,)),
            pltpu.VMEM((x * cores, 8, LANES), jnp.float32),
            pltpu.VMEM((z * y, 8, LANES), jnp.float32),
        ],
        compiler_params=pltpu.CompilerParams(
            collective_id=collective_id, has_side_effects=True, vmem_limit_bytes=60 * MIB
        ),
        name="reduce_gradients",
    )(lower_grads, upper_sums, common_grads, tile)


def contract_first(a, b):
    return lax.dot_general(a, b, (((0,), (0,)), ((), ())), preferred_element_type=jnp.float32)


def product(a, b):
    return jnp.dot(a, b, preferred_element_type=jnp.float32)


def against(a, b):
    return lax.dot_general(a, b, (((1,), (1,)), ((), ())), preferred_element_type=jnp.float32)


def clip_bounds(lengths):
    result, first = [], 0
    for clip in range(lengths.shape[0]):
        end = first + lengths[clip]
        result.append((first, end))
        first = end
    return result


def clip_borders(bounds, place):
    opening = jnp.zeros(place.shape, jnp.int32)
    ending = jnp.full(place.shape, 1 << 30, jnp.int32)
    for clip, (begin, end) in enumerate(bounds):
        here = place == clip
        opening = jnp.where(here, begin, opening)
        ending = jnp.where(here, end, ending)
    return opening, ending


def lane_of_tail(a):
    return HD if a % 2 == 0 else 0


def in_head(a, axis):
    shape = (1, LANES) if axis else (LANES, 1)
    lane = lax.broadcasted_iota(jnp.int32, shape, axis)
    return (lane >= a * HD) & (lane < (a + 1) * HD)


def all_lanes(block, first, width):
    piece = block[:, first : first + width]
    if width < LANES:
        piece = jnp.concatenate([piece, jnp.zeros((piece.shape[0], LANES - width), piece.dtype)], 1)
    return piece


def with_key_tail(bounds, a, first_row, columns):
    clips = len(bounds)
    place = lax.broadcasted_iota(jnp.int32, (1, LANES), 1) - lane_of_tail(a)
    opening, ending = clip_borders(bounds, place)
    ones = jnp.where((place >= clips) & (place < clips + 3), 1.0, 0.0)
    row = first_row + lax.broadcasted_iota(jnp.int32, columns.shape, 0)
    tail = jnp.where((row >= opening) & (row < ending), ones, big_negative)
    return jnp.where(in_head(a, 1), columns.astype(jnp.float32), tail).astype(low)


def in_three(place, value):
    top = value.astype(low).astype(jnp.float32)
    middle = (value - top).astype(low).astype(jnp.float32)
    bottom = value - top - middle
    return (
        jnp.where(place == 0, top, 0.0)
        + jnp.where(place == 1, middle, 0.0)
        + jnp.where(place == 2, bottom, 0.0)
    )


def with_tail(a, rows, tail):
    return jnp.concatenate([rows, tail] if lane_of_tail(a) else [tail, rows], 0)


def with_query_tail(bounds, a, first_row, rows, extra):
    clips = len(bounds)
    place = lax.broadcasted_iota(jnp.int32, (HD, 1), 0)
    opening, ending = clip_borders(bounds, place)
    row = first_row + lax.broadcasted_iota(jnp.int32, (1, rows.shape[1]), 1)
    inside = (place < clips) & (row >= opening) & (row < ending)
    tail = jnp.where(inside, 1.0, 0.0)
    if extra is not None:
        tail = tail + in_three(place - clips, -extra)
    return with_tail(a, rows * HD ** (-0.5), tail).astype(low)


class Pushes:
    def __init__(self, dims, me, send_sem, recv_sem):
        self.dims, self.me, self.send_sem, self.recv_sem = dims, me, send_sem, recv_sem
        self.started = []

    def __call__(self, src, dst, offset):
        i = len(self.started)
        place = shifted(self.dims, self.me, offset, 1)
        copy = remote(src, dst, self.send_sem.at[i], self.recv_sem.at[i], place, self.dims)
        copy.start()
        self.started.append(copy)
        return copy

    def finish(self):
        for copy in self.started:
            copy.wait_send()


def peers_across(dims):
    z, y, x, cores = dims
    across = [(0, 0, a, c) for a in range(x) for c in range(cores) if (a, c) != (0, 0)]
    return sorted(across, key=lambda o: (o[2] == 0, o[3]))


def ring_and_sides(dims):
    z = dims[0]
    ring = sorted({along(0, 1 % z), along(0, (z - 1) % z)} - {(0, 0, 0, 0)})
    return ring + axis_peers(dims, (1,))


def attend_kernel(
    dims,
    heads,
    key_step,
    query_step,
    gather_parts,
    lengths,
    q_in,
    kv_in,
    weights_in,
    o_out,
    lse,
    out_t,
    q_all,
    kv_all,
    weights,
    keys,
    values_t,
    queries,
    top,
    accum,
    o_mine,
    send_sem,
    recv_sem,
    own_sem,
    gather_send_sem,
    gather_recv_sem,
):
    z, y, x, cores = dims
    me = my_place(dims)
    bounds = clip_bounds(lengths)
    n_head = x * cores
    rows, width = q_in.shape[1], heads * HD
    amount = n_head * rows
    my_blk, my_head = blk_of(dims, me), head_of(dims, me)
    across = peers_across(dims)
    sides = axis_peers(dims, (1,))
    greet(dims, me, across + ring_and_sides(dims))
    push = Pushes(dims, me, send_sem, recv_sem)
    own_kv = pltpu.make_async_copy(kv_in.at[my_head], kv_all.at[my_blk, my_head], own_sem.at[0])
    own_q = pltpu.make_async_copy(q_in.at[my_head], q_all.at[my_head], own_sem.at[1])
    own_kv.start()
    own_q.start()
    gather_copy = Copies(dims, me, gather_send_sem, gather_recv_sem)
    gather = Gather(dims, gather_parts, gather_copy, (weights,), 1.4)

    def to_head(src, dst, o):
        return push(src.at[head_of(dims, shifted(dims, me, o, 1))], dst, o)

    kv_copies = {o: to_head(kv_in, kv_all.at[my_blk, my_head], o) for o in across}
    q_copies = [to_head(q_in, q_all.at[my_head], o) for o in across]
    gather.step(1)
    ring, side = {}, {}
    pieces = [(0, 0, 0, 0)] + across[::-1]

    def send_on(s, n):
        block = kv_all.at[
            blk_of(dims, shifted(dims, me, along(0, s), -1)),
            head_of(dims, shifted(dims, me, pieces[n], -1)),
        ]
        if s < z - 1:
            ring[(s + 1, n)] = push(block, block, along(0, 1))
        for o in sides:
            side[(s, n, o)] = push(block, block, o)

    def compute(offset):
        blk = blk_of(dims, shifted(dims, me, offset, -1))

        @pl.loop(0, n_head)
        def build(h):
            at = pl.ds(pl.multiple_of(h * rows, rows), rows)
            block = kv_all[blk, h]
            k_block, v_block = all_lanes(block, 0, width), all_lanes(block, width, width)
            v_t = v_block.astype(jnp.float32).T
            for a in range(heads):
                keys[a, at, :] = with_key_tail(bounds, a, blk * amount + h * rows, k_block)
                values_t[a, :HD, at] = v_t[a * HD : (a + 1) * HD].astype(low)

        @pl.loop(0, amount // query_step)
        def query_block(n):
            at = pl.ds(pl.multiple_of(n * query_step, query_step), query_step)
            for a in range(heads):
                query = queries[a, :, at]
                highest = jnp.full((8, query_step), -1e38, jnp.float32)
                for k in range(0, amount, key_step):
                    scores = product(keys[a, k : k + key_step, :], query)
                    highest = jnp.maximum(
                        highest, jnp.max(scores.reshape(key_step // 8, 8, query_step), 0)
                    )
                old = top[a, :, at]
                new = jnp.maximum(old, jnp.max(highest, 0, keepdims=True))
                top[a, :, at] = new
                total = accum[a, :, at] * jnp.exp(old - new)
                for k in range(0, amount, key_step):
                    scores = product(keys[a, k : k + key_step, :], query)
                    probs = jnp.exp(scores - new).astype(low)
                    total = total + product(values_t[a, :, k : k + key_step], probs)
                accum[a, :, at] = total

    for a in range(heads):
        values_t[a, HD:, :] = jnp.ones((values_t.shape[1] - HD, amount), low)
        top[a] = jnp.full((1, amount), -1e38, jnp.float32)
        accum[a] = jnp.zeros(accum.shape[1:], jnp.float32)
    own_kv.wait()
    send_on(0, 0)
    for n in range(1, n_head):
        kv_copies[pieces[n]].wait_recv()
        send_on(0, n)
    own_q.wait()
    for copy in q_copies:
        copy.wait_recv()
    for a in range(heads):
        for h in range(n_head):
            q_t = all_lanes(q_all[h], 0, width).astype(jnp.float32).T
            queries[a, :, h * rows : (h + 1) * rows] = with_query_tail(
                bounds, a, my_blk * amount + h * rows, q_t[a * HD : (a + 1) * HD], None
            )
    gather.step(10)
    compute((0, 0, 0, 0))
    now = 17
    for s in range(1, z + 1):
        gather.step(now)
        if s < z:
            for n in range(n_head):
                ring[(s, n)].wait_recv()
                send_on(s, n)
            compute(along(0, s))
            now += 7
            gather.step(now)
        for o in sides:
            for n in range(n_head):
                side[(s - 1, n, o)].wait_recv()
            compute((s - 1, o[1], 0, 0))
            now += 7
    gather.rest()
    for a in range(heads):
        total = accum[a, HD : HD + 1, :]
        out_t[a * HD : (a + 1) * HD, :] = accum[a, :HD, :] / total
        lse[a : a + 1, :] = top[a] + jnp.log(total)
    for h in range(n_head):
        o_mine[h] = out_t[:, h * rows : (h + 1) * rows].T.astype(low)
    o_copies = [to_head(o_mine, o_out.at[my_head], o) for o in across]
    own_o = pltpu.make_async_copy(o_mine.at[my_head], o_out.at[my_head], own_sem.at[2])
    own_o.start()
    own_o.wait()
    for copy in o_copies:
        copy.wait_recv()
    push.finish()
    gather_copy.finish()


def attend(dims, lengths, q, kv, weights, lower, heads, collective_id):
    z, y, x, cores = dims
    n_head, rows, width = q.shape
    amount = n_head * rows
    count = 3 * (n_head - 1) + n_head * (z - 1 + z * (y - 1))
    parts = cut(0, weights.shape[2], range(lower, z), (YXC, YXC))
    gather_count = gather_copies(dims, parts)
    return pl.pallas_call(
        functools.partial(attend_kernel, dims, heads, 256, 256, parts),
        out_shape=(
            jax.ShapeDtypeStruct(q.shape, low),
            jax.ShapeDtypeStruct((heads, amount), jnp.float32),
            jax.ShapeDtypeStruct((width, amount), jnp.float32),
            jax.ShapeDtypeStruct(q.shape, low),
            jax.ShapeDtypeStruct((z * y,) + kv.shape, low),
            jax.ShapeDtypeStruct(weights.shape, low),
        ),
        in_specs=[SMEM_SPEC, VMEM_SPEC, VMEM_SPEC, ANY_SPEC],
        out_specs=[VMEM_SPEC] * 5 + [ANY_SPEC],
        input_output_aliases={3: 5},
        scratch_shapes=[
            pltpu.VMEM((heads, amount, LANES), low),
            pltpu.VMEM((heads, HD + TILE, amount), low),
            pltpu.VMEM((heads, LANES, amount), low),
            pltpu.VMEM((heads, 1, amount), jnp.float32),
            pltpu.VMEM((heads, HD + TILE, amount), jnp.float32),
            pltpu.VMEM(q.shape, low),
            pltpu.SemaphoreType.DMA((count,)),
            pltpu.SemaphoreType.DMA((count,)),
            pltpu.SemaphoreType.DMA((3,)),
            pltpu.SemaphoreType.DMA((gather_count,)),
            pltpu.SemaphoreType.DMA((gather_count,)),
        ],
        compiler_params=pltpu.CompilerParams(
            collective_id=collective_id, has_side_effects=True, vmem_limit_bytes=56 * MIB
        ),
        name="attend",
    )(lengths, q, kv, weights)


def attend_back_kernel(
    dims,
    heads,
    key_step,
    reduce_parts,
    lengths,
    q_all,
    kv_all,
    do_in,
    out_t,
    lse,
    grads,
    d_q_out,
    d_kv_out,
    grad_sums,
    do_all,
    keys,
    keys_t,
    values,
    queries,
    douts,
    d_q_t,
    q_rows,
    do_rows,
    side_out,
    side_in,
    ring_out,
    ring_in,
    mine,
    d_q_mine,
    d_kv_mine,
    send_sem,
    recv_sem,
    own_sem,
    reduce_send_sem,
    reduce_recv_sem,
    *buffers,
):
    z, y, x, cores = dims
    me = my_place(dims)
    bounds = clip_bounds(lengths)
    n_head, rows, width = q_all.shape
    amount = n_head * rows
    my_blk, my_head = blk_of(dims, me), head_of(dims, me)
    across = peers_across(dims)
    sides = axis_peers(dims, (1,))
    greet(dims, me, across + ring_and_sides(dims))
    push = Pushes(dims, me, send_sem, recv_sem)

    def to_head(src, dst, o):
        return push(src.at[head_of(dims, shifted(dims, me, o, 1))], dst, o)

    do_copies = [to_head(do_in, do_all.at[my_head], o) for o in across]
    own_do = pltpu.make_async_copy(do_in.at[my_head], do_all.at[my_head], own_sem.at[0])
    own_do.start()
    reduce_copy = Copies(dims, me, reduce_send_sem, reduce_recv_sem)
    reduction = Reduce(dims, reduce_parts, reduce_copy, (grads,), buffers, None, grad_sums, 1.5)
    reduction.step(1)
    place = lax.broadcasted_iota(jnp.int32, (HD, 1), 0)

    def at_head(h):
        return slice(h * rows, (h + 1) * rows)

    for h in range(n_head):
        block = all_lanes(q_all[h], 0, width).astype(jnp.float32)
        q_t = block.T
        for a in range(heads):
            queries[a, :, at_head(h)] = with_query_tail(
                bounds,
                a,
                my_blk * amount + h * rows,
                q_t[a * HD : (a + 1) * HD],
                lse[a : a + 1, at_head(h)],
            )
            q_rows[a, at_head(h), :] = jnp.where(in_head(a, 1), block * HD ** (-0.5), 0.0).astype(low)
    for a in range(heads):
        d_q_t[a] = jnp.zeros(d_q_t.shape[1:], jnp.float32)
    own_do.wait()
    for copy in do_copies:
        copy.wait_recv()
    for h in range(n_head):
        block = all_lanes(do_all[h], 0, width).astype(jnp.float32)
        do_t = block.T
        for a in range(heads):
            part = do_t[a * HD : (a + 1) * HD]
            delta = jnp.sum(part * out_t[a * HD : (a + 1) * HD, at_head(h)], 0, keepdims=True)
            douts[a, :, at_head(h)] = with_tail(a, part, in_three(place, -delta)).astype(low)
            do_rows[a, at_head(h), :] = jnp.where(in_head(a, 1), block, 0.0).astype(low)

    def compute(offset, target):
        blk = blk_of(dims, shifted(dims, me, offset, 1))

        @pl.loop(0, n_head)
        def build(h):
            at = pl.ds(pl.multiple_of(h * rows, rows), rows)
            block = kv_all[blk, h]
            k_block, v_block = all_lanes(block, 0, width), all_lanes(block, width, width)
            k_t = k_block.astype(jnp.float32).T
            lane = lax.broadcasted_iota(jnp.int32, (1, LANES), 1)
            for a in range(heads):
                keys[a, at, :] = with_key_tail(bounds, a, blk * amount + h * rows, k_block)
                keys_t[a, :, at] = k_t[a * HD : (a + 1) * HD].astype(low)
                tail = lane - lane_of_tail(a)
                ones = jnp.where((tail >= 0) & (tail < 3), 1.0, 0.0)
                values[a, at, :] = jnp.where(
                    in_head(a, 1), v_block.astype(jnp.float32), ones
                ).astype(low)

        @pl.loop(0, amount // key_step)
        def key_block(k):
            at = pl.ds(pl.multiple_of(k * key_step, key_step), key_step)
            d_key = jnp.zeros((key_step, LANES), jnp.float32)
            d_value = jnp.zeros((key_step, LANES), jnp.float32)
            for a in range(heads):
                probs = jnp.exp(product(keys[a, at, :], queries[a]))
                d_probs = product(values[a, at, :], douts[a])
                d_scores = (probs * d_probs).astype(low)
                d_value = d_value + product(probs.astype(low), do_rows[a])
                d_key = d_key + product(d_scores, q_rows[a])
                d_q_t[a] = d_q_t[a] + product(keys_t[a, :, at], d_scores)
            target[at, :] = jnp.concatenate([d_key[:, :width], d_value[:, :width]], 1).astype(
                target.dtype
            )

    side, ring = {}, {}

    def send_sides(s):
        for o in sides:
            compute((z - s, o[1], 0, 0), side_out.at[s - 1, o[1] - 1])
            side[(s, o)] = push(side_out.at[s - 1, o[1] - 1], side_in.at[s - 1, o[1] - 1], o)

    def combine(s):
        for o in sides:
            side[(s, o)].wait_recv()
        if s > 1:
            ring[s - 1].wait_recv()

        for h in range(n_head):
            total = mine[(s - 1) % 2, at_head(h), :]
            for o in sides:
                total = total + side_in[s - 1, o[1] - 1, at_head(h), :].astype(jnp.float32)
            if s > 1:
                total = total + ring_in[s - 2, at_head(h), :].astype(jnp.float32)
            if s < z:
                ring_out[s - 1, at_head(h), :] = total.astype(low)
            else:
                d_kv_mine[h] = total.astype(low)
        if s < z:
            ring[s] = push(ring_out.at[s - 1], ring_in.at[s - 1], along(0, 1))

    now = 7
    for s in range(1, z + 1):
        send_sides(s)
        now += 7 * len(sides)
        reduction.step(now)
        if s > 1:
            combine(s - 1)
        compute((z - s if s < z else 0, 0, 0, 0), mine.at[(s - 1) % 2])
        now += 7
        reduction.step(now)
    reduction.rest()
    for h in range(n_head):
        block = jnp.concatenate([d_q_t[a, :, at_head(h)] for a in range(heads)], 0) * HD ** (-0.5)
        d_q_mine[h] = block.T.astype(low)
    copies = [to_head(d_q_mine, d_q_out.at[my_head], o) for o in across]
    own_q = pltpu.make_async_copy(d_q_mine.at[my_head], d_q_out.at[my_head], own_sem.at[1])
    own_q.start()
    combine(z)
    copies += [to_head(d_kv_mine, d_kv_out.at[my_head], o) for o in across]
    own_kv = pltpu.make_async_copy(d_kv_mine.at[my_head], d_kv_out.at[my_head], own_sem.at[2])
    own_kv.start()
    own_q.wait()
    own_kv.wait()
    for copy in copies:
        copy.wait_recv()
    push.finish()
    reduce_copy.finish()


def attend_back(dims, lengths, q, kv, dout, out_t, lse, grads, lower, heads, collective_id):
    z, y, x, cores = dims
    n_head, rows, width = q.shape
    amount = n_head * rows
    count = 3 * (n_head - 1) + z * (y - 1) + z - 1
    block = (amount, 2 * width)
    others = max(y - 1, 1)
    parts = cut(0, grads.shape[2], range(lower, z), (CXY, CXY))
    reduce_count = Reduce.count(dims, parts, False)
    return pl.pallas_call(
        functools.partial(attend_back_kernel, dims, heads, 256, parts),
        out_shape=(
            jax.ShapeDtypeStruct(q.shape, low),
            jax.ShapeDtypeStruct((n_head, rows, 2 * width), low),
            jax.ShapeDtypeStruct((z - lower,) + grads.shape[2:], low),
        ),
        in_specs=[SMEM_SPEC] + [VMEM_SPEC] * 6,
        out_specs=[VMEM_SPEC] * 3,
        scratch_shapes=[
            pltpu.VMEM(q.shape, low),
            pltpu.VMEM((heads, amount, LANES), low),
            pltpu.VMEM((heads, HD, amount), low),
            pltpu.VMEM((heads, amount, LANES), low),
            pltpu.VMEM((heads, LANES, amount), low),
            pltpu.VMEM((heads, LANES, amount), low),
            pltpu.VMEM((heads, HD, amount), jnp.float32),
            pltpu.VMEM((heads, amount, LANES), low),
            pltpu.VMEM((heads, amount, LANES), low),
            pltpu.VMEM((z, others) + block, low),
            pltpu.VMEM((z, others) + block, low),
            pltpu.VMEM((max(z - 1, 1),) + block, low),
            pltpu.VMEM((max(z - 1, 1),) + block, low),
            pltpu.VMEM((2,) + block, jnp.float32),
            pltpu.VMEM(q.shape, low),
            pltpu.VMEM((n_head, rows, 2 * width), low),
            pltpu.SemaphoreType.DMA((count,)),
            pltpu.SemaphoreType.DMA((count,)),
            pltpu.SemaphoreType.DMA((3,)),
            pltpu.SemaphoreType.DMA((reduce_count,)),
            pltpu.SemaphoreType.DMA((reduce_count,)),
        ]
        + Reduce.scratch(dims, parts, False),
        compiler_params=pltpu.CompilerParams(
            collective_id=collective_id, has_side_effects=True, vmem_limit_bytes=60 * MIB
        ),
        name="attend_back",
    )(lengths, q, kv, dout, out_t, lse, grads)


def part_shapes(n_head):
    width = HEADS // n_head * HD
    hidden = FF // n_head
    return (
        (D, width, True),
        (DI, 2 * width, True),
        (width, D, False),
        (D, 3 * width, True),
        (width, D, False),
        (D, hidden, True),
        (hidden, D, False),
        (D, C // n_head, True),
    )


def borders(n_head):
    result = [0]
    for rows, columns, joined in part_shapes(n_head):
        result.append(result[-1] + rows * columns // LANES)
    return result


def period(columns):
    amount = 1
    while amount * columns % LANES:
        amount *= 2
    return amount


def segments(start, amount, unit):
    result = []
    while amount > 0:
        which, at = divmod(start, unit)
        size = min(unit - at, amount)
        result.append((which, at, at + size))
        start, amount = start + size, amount - size
    return result


def joined_lanes(pieces):
    return pieces[0] if len(pieces) == 1 else jnp.concatenate(pieces, 1)


def lane_blocks(value):
    rows, columns = value.shape
    missing = -columns % LANES
    if missing:
        value = jnp.concatenate([value, jnp.zeros((rows, missing), value.dtype)], 1)
    return [value[:, i : i + LANES] for i in range(0, columns + missing, LANES)]


def every(first, amount, stride):
    return pl.ds(first, amount) if stride == 1 else pl.ds(first, amount, stride=stride)


def matrix_of(stage, first, rows, columns, line):
    if columns % LANES == 0:
        stride = columns // LANES
        for j in range(stride):
            yield j * LANES, stage[every(first + j, rows, stride), :]
        return
    height = period(columns)
    stride = height * columns // LANES
    for k in range(height):
        pieces = [
            stage[every(first + which, rows // height, stride), :][:, begin:end]
            for which, begin, end in segments(k * columns, columns, LANES)
        ]
        for i, piece in enumerate(lane_blocks(joined_lanes(pieces))):
            line[i, every(k, rows // height, height), :] = piece
    for i in range(-(-columns // LANES)):
        yield i * LANES, line[i, :rows, : min(columns - i * LANES, LANES)]


def matrix_into(stage, first, value, line):
    rows, columns = value.shape
    if columns % LANES == 0:
        stride = columns // LANES
        for j in range(stride):
            stage[every(first + j, rows, stride), :] = value[:, j * LANES : (j + 1) * LANES]
        return
    height = period(columns)
    stride = height * columns // LANES
    for i, piece in enumerate(lane_blocks(value)):
        line[i, :rows, :] = piece
    for i in range(stride):
        pieces = [
            line[which, every(k, rows // height, height), :][:, begin:end]
            for k, first_lane, last_lane in segments(i * LANES, LANES, columns)
            for which, begin, end in segments(first_lane, last_lane - first_lane, LANES)
        ]
        stage[every(first + i, rows // height, stride), :] = joined_lanes(pieces)


def load_stage(stage, held, first_shard, shard_rows, group):
    for b in range(held.shape[0]):
        stage[pl.ds(b * shard_rows, shard_rows), :] = held[b, group, :shard_rows, :].astype(jnp.float32)


def load_common(stage, held, valid):
    piece = held.shape[2]
    for b in range(held.shape[0]):
        for k in range(held.shape[1]):
            amount = min(piece, valid - k * piece)
            stage[b * valid + k * piece : b * valid + k * piece + amount, :] = held[b, k].astype(
                jnp.float32
            )[:amount]


def common_blocks(first_row, last_row, valid):
    return first_row // valid, -(-last_row // valid) - first_row // valid


def load_matrices(stage, first_row, n_head, group, which, targets, line):
    starts, shapes = borders(n_head), part_shapes(n_head)
    for m, target in zip(which, targets):
        rows, columns, joined = shapes[m]
        row = 0 if joined else group * rows
        column = group * columns if joined else 0
        for j, value in matrix_of(stage, starts[m] - first_row, rows, columns, line):
            size = value.shape[1]
            target[row : row + rows, column + j : column + j + size] = value.astype(target.dtype)


def normalized(x):
    centre = x - jnp.mean(x, -1, keepdims=True)
    rate = lax.rsqrt(jnp.mean(centre * centre, -1, keepdims=True) + norm_eps)
    return centre * rate, rate


def layer_norm(x, gain):
    return normalized(x)[0] * gain


def norm_pullback(x, gain, grad):
    unit, rate = normalized(x)
    inside = grad * gain
    both = jnp.mean(inside * unit, -1, keepdims=True)
    d_x = rate * (inside - jnp.mean(inside, -1, keepdims=True) - unit * both)
    return d_x, jnp.sum(grad * unit, 0, keepdims=True)


def head_lanes(group, heads, value):
    width = heads * HD
    block = value[:, group * width : (group + 1) * width]
    lane = lax.broadcasted_iota(jnp.int32, (1, width), 1)
    result = []
    for a in range(heads):
        here = (lane >= a * HD) & (lane < (a + 1) * HD)
        result.append((here, jnp.where(here, block, jnp.zeros_like(block))))
    return result


def place_of(bounds, first, amount):
    row = first + lax.broadcasted_iota(jnp.int32, (amount, 1), 0)
    opening = jnp.zeros((amount, 1), jnp.int32)
    for begin, end in bounds:
        opening = jnp.where((row >= begin) & (row < end), begin, opening)
    offset = row - opening
    turns = jnp.floor((offset.astype(jnp.float32) + 0.5) * (1.0 / LAT)).astype(jnp.int32)
    return offset - turns * LAT


def picked_rows(bounds, rows, n_head):
    first = lax.axis_index("blk") * (rows * n_head) + lax.axis_index("head") * rows
    lane = lax.broadcasted_iota(jnp.int32, (rows, LAT), 1)
    return jnp.where(lane == place_of(bounds, first, rows), 1.0, 0.0).astype(low)


def enc_scores(q_head, keys):
    return against(q_head, keys) * HD ** (-0.5)


def encode_kernel(
    n_head,
    shard_rows,
    valid,
    rows,
    counts_at,
    lengths,
    weights,
    common,
    counted,
    inputs_t,
    enc_query,
    enc_keyval,
    enc_output,
    self_project,
    gains,
    z_zero,
    h_zero,
    x_norm_t,
    q_enc,
    kv_enc,
    o_enc,
    z_one,
    h_one,
    q_self,
    kv_self,
    counts,
    held,
    held_common,
    held_counts,
    stage,
    stage_common,
    line,
    latent_table,
    sems,
):
    heads = HEADS // n_head
    width = heads * HD
    shards = held.shape[0]
    bounds = clip_bounds(lengths)
    first = DQ * D // LANES
    block, blocks = common_blocks(first, first + (LAT + 4) * D // LANES, valid)
    piece, count_row, count_rows = counts_at
    count_tile = count_row // TILE * TILE
    copies = [
        pltpu.make_async_copy(common.at[pl.ds(block, blocks)], held_common, sems.at[0]),
        pltpu.make_async_copy(weights.at[pl.ds(0, shards)], held, sems.at[1]),
        pltpu.make_async_copy(
            counted.at[:, piece, pl.ds(count_tile, held_counts.shape[1])], held_counts, sems.at[2]
        ),
    ]
    for copy in copies:
        copy.start()
    centre = inputs_t[...].astype(jnp.float32)
    centre = centre - jnp.mean(centre, 0, keepdims=True)
    rate = lax.rsqrt(jnp.mean(centre * centre, 0, keepdims=True) + norm_eps)
    x_norm_t[...] = (centre * rate).astype(low)
    copies[0].wait()
    load_common(stage_common, held_common, valid)
    first = first - block * valid
    for j, value in matrix_of(stage_common, first, LAT, D, line):
        latent_table[:, j : j + LANES] = value.astype(low)
    for j, value in matrix_of(stage_common, first + LAT * D // LANES, 4, D, line):
        gains[:, j : j + LANES] = value
    picked = picked_rows(bounds, rows, n_head)
    z_zero[...] = product(picked, latent_table[...])
    h_zero[...] = layer_norm(z_zero[...], gains[0:1, :]).astype(low)
    copies[2].wait()
    begin = count_row - count_tile
    all_counts = jnp.sum(held_counts[...].astype(jnp.float32), 0)[begin : begin + count_rows]
    counts[...] = jnp.broadcast_to(jnp.sum(all_counts, 0, keepdims=True), counts.shape)
    copies[1].wait()
    for g in range(n_head):
        load_stage(stage, held, 0, shard_rows, g)
        load_matrices(
            stage, 0, n_head, g, (0, 1, 2, 3), (enc_query, enc_keyval, enc_output, self_project), line
        )
    q_enc[...] = product(h_zero[...], enc_query[...]).astype(low)
    kv_enc[...] = contract_first(x_norm_t[...], enc_keyval[...]).astype(low)
    for g in range(n_head):
        keys = kv_enc[:, 2 * g * width : (2 * g + 1) * width]
        values = kv_enc[:, (2 * g + 1) * width : (2 * g + 2) * width]
        outcome = jnp.zeros((rows, width), jnp.float32)
        for here, q_head in head_lanes(g, heads, q_enc[...]):
            scores = enc_scores(q_head, keys)
            probs = jnp.exp(scores - jnp.max(scores, 1, keepdims=True))
            total = jnp.sum(probs, 1, keepdims=True)
            outcome = jnp.where(here, product(probs.astype(low), values) / total, outcome)
        o_enc[:, g * width : (g + 1) * width] = outcome.astype(low)
    z_one[...] = z_zero[...] + product(o_enc[...], enc_output[...])
    h_one[...] = layer_norm(z_one[...], gains[1:2, :]).astype(low)
    projected = product(h_one[...], self_project[...]).astype(low)
    for g in range(n_head):
        q_self[g] = projected[:, 3 * g * width : (3 * g + 1) * width]
        kv_self[g] = projected[:, (3 * g + 1) * width : (3 * g + 3) * width]


LINE = pltpu.VMEM((4, round_up(max(D, DI), 8), LANES), jnp.float32)


def shards_of(n_head, shard_rows, first, last):
    starts = borders(n_head)
    begin = starts[first] // shard_rows
    return begin, -(-starts[last] // shard_rows) - begin


def encode(lengths, weights, common, counted, counts_at, inputs_t, valid, rows, n_head, shard_rows):
    width = HEADS // n_head * HD
    begin, shards = shards_of(n_head, shard_rows, 0, 4)
    query_rows = DQ * D // LANES
    block, blocks = common_blocks(query_rows, query_rows + (LAT + 4) * D // LANES, valid)
    keys = inputs_t.shape[1]
    return pl.pallas_call(
        functools.partial(encode_kernel, n_head, shard_rows, valid, rows, counts_at),
        out_shape=[
            shape_of((D, D)),
            shape_of((DI, 2 * D)),
            shape_of((D, D)),
            shape_of((D, 3 * D)),
            shape_of((4, D), jnp.float32),
            shape_of((rows, D), jnp.float32),
            shape_of((rows, D)),
            shape_of(inputs_t.shape),
            shape_of((rows, D)),
            shape_of((keys, 2 * D)),
            shape_of((rows, D)),
            shape_of((rows, D), jnp.float32),
            shape_of((rows, D)),
            shape_of((n_head, rows, width)),
            shape_of((n_head, rows, 2 * width)),
            shape_of((8, LANES), jnp.float32),
        ],
        in_specs=[SMEM_SPEC] + [ANY_SPEC] * 3 + [VMEM_SPEC],
        out_specs=[VMEM_SPEC] * 16,
        scratch_shapes=[
            pltpu.VMEM((shards,) + weights.shape[1:], low),
            pltpu.VMEM((blocks,) + common.shape[1:], low),
            pltpu.VMEM((counted.shape[0], round_up(counts_at[1] % TILE + counts_at[2], TILE), LANES), low),
            pltpu.VMEM((shards * shard_rows, LANES), jnp.float32),
            pltpu.VMEM((blocks * valid, LANES), jnp.float32),
            LINE,
            pltpu.VMEM((LAT, D), low),
            pltpu.SemaphoreType.DMA((3,)),
        ],
        compiler_params=pltpu.CompilerParams(vmem_limit_bytes=56 * MIB),
        name="encode",
    )(lengths, weights, common, counted, inputs_t)


def gelu_and_slope(x):
    rate = (2.0 / jnp.pi) ** 0.5
    cubic = 0.044715
    t = jnp.tanh(rate * (x + cubic * x * x * x))
    slope = 0.5 * (1.0 + t) + 0.5 * x * (1.0 - t * t) * rate * (1.0 + 3.0 * cubic * x * x)
    return 0.5 * x * (1.0 + t), slope


def my_column(marks, rows):
    turned = marks[...].astype(jnp.float32).T
    column = lax.broadcasted_iota(jnp.int32, turned.shape, 1)
    per_head = rows // LANES
    first = lax.axis_index("head") * per_head
    picked = [
        jnp.sum(jnp.where(column == first + k, turned, 0.0), 1, keepdims=True)
        for k in range(per_head)
    ]
    return jnp.concatenate(picked, 0) if per_head > 1 else picked[0]


def middle_kernel(
    n_head,
    shard_rows,
    valid,
    first_shard,
    rows,
    counts,
    weights,
    common,
    z_one,
    o_self,
    out_queries_t,
    labels,
    modality,
    labeled,
    gains,
    dout,
    d_two_out,
    tile,
    query_grad,
    gain_grads,
    lower_grads,
    upper_grads,
    held,
    held_common,
    stage,
    stage_common,
    line,
    self_output,
    hidden_in,
    hidden_out,
    class_table,
    query_table,
    slope,
    activ,
    sems,
):
    heads = HEADS // n_head
    width, hidden, classes = heads * HD, FF // n_head, C // n_head
    shards = held.shape[0]
    first_row = first_shard * shard_rows
    starts = borders(n_head)
    copies = [
        pltpu.make_async_copy(common.at[pl.ds(0, held_common.shape[0])], held_common, sems.at[0]),
        pltpu.make_async_copy(weights.at[pl.ds(first_shard, shards)], held, sems.at[1]),
    ]
    for copy in copies:
        copy.start()
    copies[0].wait()
    load_common(stage_common, held_common, valid)
    for j, value in matrix_of(stage_common, 0, DQ, D, line):
        query_table[:, j : j + LANES] = value.astype(low)
    copies[1].wait()
    for g in range(n_head):
        load_stage(stage, held, first_shard, shard_rows, g)
        load_matrices(
            stage, first_row, n_head, g, (4, 5, 6, 7), (self_output, hidden_in, hidden_out, class_table), line
        )
    gain_two, gain_three = gains[2:3, :], gains[3:4, :]
    o_low = jnp.concatenate([o_self[g] for g in range(n_head)], 1)
    z_two = z_one[...] + product(o_low, self_output[...])
    h_two = layer_norm(z_two, gain_two).astype(low)
    value, bend = gelu_and_slope(product(h_two, hidden_in[...]))
    activ[...] = value.astype(low)
    slope[...] = bend
    z_three = z_two + product(activ[...], hidden_out[...])
    queries_t = out_queries_t[...]
    decoded = layer_norm(z_three, gain_three) + contract_first(queries_t, query_table[...])
    decoded = decoded.astype(low)
    logits = product(decoded, class_table[...])
    label, kind, counted = (my_column(marks, rows) for marks in (labels, modality, labeled))
    lane = lax.broadcasted_iota(jnp.int32, (rows, C), 1).astype(jnp.float32)
    is_target = jnp.where(lane == label, 1.0, 0.0)
    row_top = jnp.max(logits, 1, keepdims=True)
    row_lse = row_top + jnp.log(jnp.sum(jnp.exp(logits - row_top), 1, keepdims=True))
    loss = row_lse - jnp.sum(is_target * logits, 1, keepdims=True)
    weight = jnp.zeros((rows, 1), jnp.float32)
    place = lax.broadcasted_iota(jnp.int32, (1, LANES), 1)
    losses = jnp.zeros((1, LANES), jnp.float32)
    for m in range(MODES):
        member = jnp.where((kind == m) & (counted == 1.0), 1.0, 0.0)
        weight = weight + member / jnp.maximum(counts[0:1, m : m + 1], 1.0)
        losses = losses + jnp.where(place == m, jnp.sum(loss * member, 0, keepdims=True), 0.0)
    tile[...] = jnp.broadcast_to(losses, tile.shape)
    dlogits = (weight * (jnp.exp(logits - row_lse) - is_target)).astype(low)
    d_decoded = against(dlogits, class_table[...])
    matrix_into(query_grad, 0, product(queries_t, d_decoded.astype(low)), line)
    d_three, gain_three_grad = norm_pullback(z_three, gain_three, d_decoded)
    d_branch = d_three.astype(low)
    d_pre = (slope[...] * against(d_branch, hidden_out[...])).astype(low)
    d_middle, gain_two_grad = norm_pullback(z_two, gain_two, against(d_pre, hidden_in[...]))
    d_two = d_three + d_middle
    d_two_out[...] = d_two
    gain_grads[...] = jnp.concatenate([gain_two_grad, gain_three_grad], 0)
    d_two_low = d_two.astype(low)
    d_o = against(d_two_low, self_output[...]).astype(low)
    for g in range(n_head):
        dout[g] = d_o[:, g * width : (g + 1) * width]
    for g in range(n_head):
        results = (
            contract_first(o_self[g], d_two_low),
            contract_first(h_two, d_pre[:, g * hidden : (g + 1) * hidden]),
            contract_first(activ[:, g * hidden : (g + 1) * hidden], d_branch),
            contract_first(decoded, dlogits[:, g * classes : (g + 1) * classes]),
        )
        for m, result in zip((4, 5, 6, 7), results):
            matrix_into(stage, starts[m] - first_row, result, line)
        for b in range(shards):
            held[b, g, :shard_rows, :] = stage[pl.ds(b * shard_rows, shard_rows), :].astype(low)
    split = lower_grads.shape[0] - first_shard
    copies = [
        pltpu.make_async_copy(held.at[pl.ds(split, shards - split)], upper_grads, sems.at[2]),
        pltpu.make_async_copy(
            held.at[pl.ds(0, split)], lower_grads.at[pl.ds(first_shard, split)], sems.at[3]
        ),
    ]
    for copy in copies:
        copy.start()
    for copy in copies:
        copy.wait()


def middle(counts, weights, common, z_one, o_self, out_queries_t, marks, gains, valid, split, n_head, shard_rows):
    rows = z_one.shape[0]
    begin, shards = shards_of(n_head, shard_rows, 4, 8)
    query_rows = DQ * D // LANES
    block, blocks = common_blocks(0, query_rows, valid)
    return pl.pallas_call(
        functools.partial(middle_kernel, n_head, shard_rows, valid, begin, rows),
        grid=(1,),
        out_shape=[
            shape_of(o_self.shape),
            shape_of((rows, D), jnp.float32),
            shape_of((8, LANES), jnp.float32),
            shape_of((query_rows, LANES), jnp.float32),
            shape_of((2, D), jnp.float32),
            shape_of((split,) + weights.shape[1:]),
            shape_of((weights.shape[0] - split,) + weights.shape[1:]),
        ],
        in_specs=[
            VMEM_SPEC,
            ANY_SPEC,
            ANY_SPEC,
            VMEM_SPEC,
            VMEM_SPEC,
            pl.BlockSpec((DQ, rows), lambda i: (0, lax.axis_index("head"))),
            VMEM_SPEC,
            VMEM_SPEC,
            VMEM_SPEC,
            VMEM_SPEC,
        ],
        out_specs=[VMEM_SPEC] * 5 + [ANY_SPEC] * 2,
        scratch_shapes=[
            pltpu.VMEM((shards,) + weights.shape[1:], low),
            pltpu.VMEM((blocks,) + common.shape[1:], low),
            pltpu.VMEM((shards * shard_rows, LANES), jnp.float32),
            pltpu.VMEM((blocks * valid, LANES), jnp.float32),
            LINE,
            pltpu.VMEM((D, D), low),
            pltpu.VMEM((D, FF), low),
            pltpu.VMEM((FF, D), low),
            pltpu.VMEM((D, C), low),
            pltpu.VMEM((DQ, D), low),
            pltpu.VMEM((rows, FF), jnp.float32),
            pltpu.VMEM((rows, FF), low),
            pltpu.SemaphoreType.DMA((4,)),
        ],
        compiler_params=pltpu.CompilerParams(vmem_limit_bytes=56 * MIB),
        name="middle",
    )(counts, weights, common, z_one, o_self, out_queries_t, *marks, gains)


def ending_kernel(
    n_head,
    shard_rows,
    valid,
    rows,
    lengths,
    grads_in,
    d_q_self,
    d_kv_self,
    d_two,
    gains,
    gain_grads,
    query_grad,
    enc_query,
    enc_keyval,
    enc_output,
    self_project,
    z_zero,
    h_zero,
    x_norm_t,
    q_enc,
    kv_enc,
    o_enc,
    z_one,
    h_one,
    grads,
    common_grad,
    held,
    stage,
    stage_common,
    line,
    d_q,
    d_kv,
    sems,
):
    heads = HEADS // n_head
    width = heads * HD
    shards = held.shape[0]
    starts = borders(n_head)
    shared = pltpu.make_async_copy(grads_in.at[pl.ds(shards - 1, 1)], held.at[pl.ds(shards - 1, 1)], sems.at[0])
    shared.start()
    d_projected = [jnp.concatenate([d_q_self[g], d_kv_self[g]], 1) for g in range(n_head)]
    whole = jnp.concatenate(d_projected, 1)
    d_middle, gain_one_grad = norm_pullback(
        z_one[...], gains[1:2, :], against(whole, self_project[...])
    )
    d_one = d_two[...] + d_middle
    d_one_low = d_one.astype(low)
    d_o = against(d_one_low, enc_output[...]).astype(low)
    for g in range(n_head):
        keys = kv_enc[:, 2 * g * width : (2 * g + 1) * width]
        values = kv_enc[:, (2 * g + 1) * width : (2 * g + 2) * width]
        d_key = jnp.zeros(keys.shape, jnp.float32)
        d_value = jnp.zeros(keys.shape, jnp.float32)
        d_query = jnp.zeros((rows, width), jnp.float32)
        for (here, q_head), (unused, do_head) in zip(
            head_lanes(g, heads, q_enc[...]), head_lanes(g, heads, d_o)
        ):
            scores = enc_scores(keys, q_head)
            probs = jnp.exp(scores - jnp.max(scores, 0, keepdims=True))
            probs = probs / jnp.sum(probs, 0, keepdims=True)
            d_probs = against(values, do_head)
            delta = jnp.sum(probs * d_probs, 0, keepdims=True)
            d_scores = (probs * (d_probs - delta)).astype(low)
            d_value = d_value + product(probs.astype(low), do_head)
            d_key = d_key + product(d_scores, q_head)
            d_query = jnp.where(here, contract_first(d_scores, keys), d_query)
        d_q[:, g * width : (g + 1) * width] = (d_query * HD ** (-0.5)).astype(low)
        d_kv[:, 2 * g * width : (2 * g + 1) * width] = (d_key * HD ** (-0.5)).astype(low)
        d_kv[:, (2 * g + 1) * width : (2 * g + 2) * width] = d_value.astype(low)
    d_middle, gain_zero_grad = norm_pullback(
        z_zero[...], gains[0:1, :], against(d_q[...], enc_query[...])
    )
    d_zero = d_one + d_middle
    d_zero_top = d_zero.astype(low)
    d_zero_rest = (d_zero - d_zero_top.astype(jnp.float32)).astype(low)
    picked = picked_rows(clip_bounds(lengths), rows, n_head)
    latent_grad = contract_first(picked, d_zero_top) + contract_first(picked, d_zero_rest)
    query_rows = query_grad.shape[0]
    stage_common[:query_rows] = query_grad[...]
    matrix_into(stage_common, query_rows, latent_grad, line)
    all_gains = jnp.concatenate([gain_zero_grad, gain_one_grad, gain_grads[...]], 0)
    matrix_into(stage_common, query_rows + LAT * D // LANES, all_gains, line)
    piece = common_grad.shape[2]
    for b in range(common_grad.shape[0]):
        for k in range(common_grad.shape[1]):
            amount = min(piece, valid - k * piece)
            block = stage_common[b * valid + k * piece : b * valid + k * piece + amount, :]
            if amount < piece:
                block = jnp.concatenate([block, jnp.zeros((piece - amount, LANES), jnp.float32)], 0)
            common_grad[b, k] = block.astype(low)
    shared.wait()
    kept = shards * shard_rows - starts[4]
    for g in range(n_head):
        results = (
            contract_first(h_zero[...], d_q[:, g * width : (g + 1) * width]),
            product(x_norm_t[...], d_kv[:, 2 * g * width : (2 * g + 2) * width]),
            contract_first(o_enc[:, g * width : (g + 1) * width], d_one_low),
            contract_first(h_one[...], d_projected[g]),
        )
        if kept:
            stage[pl.ds((shards - 1) * shard_rows, shard_rows), :] = held[
                shards - 1, g, :shard_rows, :
            ].astype(jnp.float32)
        for m, result in zip((0, 1, 2, 3), results):
            matrix_into(stage, starts[m], result, line)
        for b in range(shards):
            held[b, g, :shard_rows, :] = stage[pl.ds(b * shard_rows, shard_rows), :].astype(low)
    back = pltpu.make_async_copy(held, grads.at[pl.ds(0, shards)], sems.at[1])
    back.start()
    back.wait()


def ending(lengths, grads, d_self, d_two, gains, gain_grads, query_grad, kept, common_shape, valid, shard_rows):
    rows = d_two.shape[0]
    n_head = grads.shape[1]
    begin, shards = shards_of(n_head, shard_rows, 0, 4)
    keys = kept[6].shape[1]
    common_rows = (DQ + LAT + 4) * D // LANES
    return pl.pallas_call(
        functools.partial(ending_kernel, n_head, shard_rows, valid, rows),
        out_shape=[shape_of(grads.shape), shape_of(common_shape)],
        in_specs=[SMEM_SPEC, ANY_SPEC] + [VMEM_SPEC] * 18,
        out_specs=[ANY_SPEC, VMEM_SPEC],
        input_output_aliases={1: 0},
        scratch_shapes=[
            pltpu.VMEM((shards,) + grads.shape[1:], low),
            pltpu.VMEM((shards * shard_rows, LANES), jnp.float32),
            pltpu.VMEM((common_rows, LANES), jnp.float32),
            LINE,
            pltpu.VMEM((rows, D), low),
            pltpu.VMEM((keys, 2 * D), low),
            pltpu.SemaphoreType.DMA((2,)),
        ],
        compiler_params=pltpu.CompilerParams(vmem_limit_bytes=56 * MIB),
        name="ending",
    )(lengths, grads, *d_self, d_two, gains, gain_grads, query_grad, *kept)


def adam_step(weight, first, second, grad):
    first = beta_one * first + (1 - beta_one) * grad
    second = beta_two * second + (1 - beta_two) * grad * grad
    fixed_first = first / (1 - beta_one**STEP)
    fixed_second = second / (1 - beta_two**STEP)
    weight = weight - learn_rate * (
        fixed_first / (jnp.sqrt(fixed_second) + adam_eps) + weight_decay * weight
    )
    return (weight, first, second, weight.astype(low))


def per_device(
    inputs,
    out_queries,
    clip_lengths,
    labels,
    modality,
    labeled,
    head_params,
    head_first,
    head_second,
    common_params,
    common_first,
    common_second,
):
    n_head, n_blk = lax.axis_size("head"), lax.axis_size("blk")
    dims = grid_of(n_blk, n_head)
    rows = labels.shape[0] // n_head
    heads_here = HEADS // n_head
    n_h, n_c = head_params.shape[0], common_params.shape[0]
    shard_rows, common_rows = n_h // LANES, -(-n_c // LANES)
    marks = [x.reshape(-1, LANES) for x in (labels, modality, labeled)]
    count_rows = marks[0].shape[0]
    head_rows = round_up(shard_rows, TILE)
    piece_rows = round_up(-(-(common_rows + count_rows) // n_head), TILE)
    counts_at = (*divmod(common_rows, piece_rows), count_rows)
    lower = lower_planes(dims, n_head, shard_rows)
    head_wide = head_params.reshape(shard_rows, LANES)
    common_wide = jnp.pad(common_params, (0, common_rows * LANES - n_c)).reshape(common_rows, LANES)
    weights, counted = gather_all(
        dims, marks, (head_wide, common_wide), (head_rows, piece_rows), lower, 0
    )
    common, valid = counted, common_rows
    if n_c % LANES:
        common = common.reshape(n_blk, -1)[:, :n_c].reshape(-1, LANES)
        valid = common.shape[0]
        common = jnp.pad(common, ((0, -valid % TILE), (0, 0)))[None, None]

    encoded = encode(
        clip_lengths, weights, common, counted, counts_at, inputs.T, valid, rows, n_head, shard_rows
    )
    gains, z_one, counts = encoded[4], encoded[11], encoded[15]
    o_self, lse_self, out_self_t, q_all, kv_all, weights = attend(
        dims, clip_lengths, encoded[13], encoded[14], weights, lower, heads_here, 1
    )
    dout, d_two, tile, query_grad, gain_grads, lower_grads, upper_grads = middle(
        counts,
        weights,
        common,
        z_one,
        o_self,
        out_queries.T,
        marks,
        gains,
        valid,
        lower * dims[1],
        n_head,
        shard_rows,
    )
    d_q, d_kv, upper_sums = attend_back(
        dims,
        clip_lengths,
        q_all,
        kv_all,
        dout,
        out_self_t,
        lse_self,
        upper_grads,
        lower,
        heads_here,
        2,
    )
    kept = encoded[:4] + encoded[5:13]
    lower_grads, common_grad = ending(
        clip_lengths,
        lower_grads,
        (d_q, d_kv),
        d_two,
        gains,
        gain_grads,
        query_grad,
        kept,
        common.shape,
        valid,
        shard_rows,
    )
    if n_c % LANES:
        common_grad = common_grad[0, 0, :valid].reshape(n_blk, n_c)
        common_grad = jnp.pad(common_grad, ((0, 0), (0, n_head * piece_rows * LANES - n_c)))
        common_grad = common_grad.reshape(n_blk, n_head, piece_rows, LANES)
    head_share, common_share, totals = reduce_all(
        dims, lower_grads, upper_sums, common_grad, (shard_rows, common_rows), tile, 3
    )
    label_counts, loss_sums = counts[0, :MODES], totals[0, :MODES]
    clip_norm = jnp.sqrt(totals[0, MODES])
    factor = jnp.minimum(1.0, clip_limit / clip_norm)
    head_share, common_share = head_share.reshape(-1), common_share.reshape(-1)[:n_c]
    head_out = adam_step(head_params, head_first, head_second, head_share * factor)
    common_out = adam_step(common_params, common_first, common_second, common_share * factor)
    return head_out + common_out + (loss_sums, label_counts, clip_norm)


def solution(mesh):
    placed = (
        P("blk", None),
        P("blk", None),
        P(),
        P("blk"),
        P("blk"),
        P("blk"),
        P(("head", "blk")),
        P(("head", "blk")),
        P(("head", "blk")),
        P("blk"),
        P("blk"),
        P("blk"),
    )
    return jax.shard_map(
        per_device,
        mesh=mesh,
        in_specs=placed,
        out_specs=(
            P(("head", "blk")),
            P(("head", "blk")),
            P(("head", "blk")),
            P(("head", "blk")),
            P("blk"),
            P("blk"),
            P("blk"),
            P("blk"),
            P(),
            P(),
            P(),
        ),
        check_vma=False,
    )
```

```python
import functools

import jax
import jax.numpy as jnp
from jax import lax
from jax.experimental import pallas as pl
from jax.experimental.pallas import tpu as pltpu
from jax.sharding import PartitionSpec as P

D = 512
HEADS = 8
HD = 64
FF = 2048
DI = 704
DQ = 1026
C = 704
LAT = 784
MODES = 3
STEP = 10
LANES = 128
TILE = 16

norm_eps = 1e-05
learn_rate = 0.1
beta_one = 0.9
beta_two = 0.999
adam_eps = 1e-08
weight_decay = 0.01
clip_limit = 0.05
big_negative = -1e30
low = jnp.bfloat16
MESH = pl.DeviceIdType.MESH
MIB = 1 << 20
VMEM_SPEC = pl.BlockSpec(memory_space=pltpu.VMEM)
SMEM_SPEC = pl.BlockSpec(memory_space=pltpu.SMEM)
ANY_SPEC = pl.BlockSpec(memory_space=pl.ANY)


def shape_of(shape, dtype=low):
    return jax.ShapeDtypeStruct(shape, dtype)


def round_up(n, unit):
    return -(-n // unit) * unit


def grid_of(n_blk, n_head):
    cores = 2 if n_head % 2 == 0 else 1
    x = n_head // cores
    y = x if n_blk % x == 0 else 1
    return (n_blk // y, y, x, cores)


def my_place(dims):
    blk, head = lax.axis_index("blk"), lax.axis_index("head")
    return (blk // dims[1], lax.rem(blk, dims[1]), head // dims[3], lax.rem(head, dims[3]))


def shifted(dims, me, offset, sign):
    return tuple(
        m if o == 0 else lax.rem(m + (o if sign > 0 else n - o), n)
        for m, o, n in zip(me, offset, dims)
    )


def blk_of(dims, place):
    return place[0] * dims[1] + place[1]


def head_of(dims, place):
    return place[2] * dims[3] + place[3]


def device_of(dims, place):
    return {"blk": blk_of(dims, place), "head": head_of(dims, place)}


def along(axis, d):
    return tuple(d if a == axis else 0 for a in range(4))


def greet(dims, me, offsets):
    barrier = pltpu.get_barrier_semaphore()
    for offset in offsets:
        pl.semaphore_signal(
            barrier,
            inc=1,
            device_id=device_of(dims, shifted(dims, me, offset, 1)),
            device_id_type=MESH,
        )
    pl.semaphore_wait(barrier, len(offsets))


def axis_peers(dims, axes):
    return [along(axis, d) for axis in axes for d in range(1, dims[axis])]


def remote(src, dst, send_sem, recv_sem, place, dims):
    return pltpu.make_async_remote_copy(
        src_ref=src,
        dst_ref=dst,
        send_sem=send_sem,
        recv_sem=recv_sem,
        device_id=device_of(dims, place),
        device_id_type=MESH,
    )


AHEAD = 6.0
RING = 0


def in_order(first, follow, size_of, ahead, result):
    queues, busy, flight = {}, {}, {}
    now = 0.0

    def ready(messages):
        for message in messages:
            queues.setdefault(message[1], []).append(message)

    ready(first)
    while True:
        for axis in sorted(queues):
            queue, going = queues[axis], flight.setdefault(axis, [])
            while queue and (not going or busy[axis] < now + ahead):
                message = min(queue)
                queue.remove(message)
                busy[axis] = max(now, busy.get(axis, 0.0)) + size_of(message)
                going.append((busy[axis] + 1.5, message))
                result.append((True, message))
        arrivals = [min(going) for going in flight.values() if going]
        if not arrivals:
            return now
        arrival = min(arrivals)
        flight[arrival[1][1]].remove(arrival)
        now = max(now, arrival[0])
        result.append((False, arrival[1]))
        ready(follow(arrival[1]))


def time_of(rows, axis):
    return rows * LANES * 2 / (300e3 if axis == 3 else 45e3)


def with_at(offset, axis, d):
    return offset[:axis] + (d,) + offset[axis + 1 :]


def gather_order(dims, parts):
    def onward(p, offset, position):
        order = parts[p][3]
        result = []
        for k in range(max(position, 0), 4):
            axis = order[k]
            n = dims[axis]
            if k > position:
                steps = [1] if axis == RING else range(1, n)
                steps = [d for d in steps if d < n]
            else:
                steps = [offset[axis] + 1] if axis == RING and offset[axis] + 1 < n else []
            for d in steps:
                result.append(((k, sum(offset), p), axis, p, with_at(offset, axis, d)))
        return result

    def follow(message):
        rank, axis, p, offset = message
        return onward(p, offset, rank[0])

    first = [m for p in range(len(parts)) for m in onward(p, (0, 0, 0, 0), -1)]
    result = []
    now = in_order(first, follow, lambda m: time_of(parts[m[2]][2], m[1]), AHEAD, result)
    return result, now


def gather_kernel(
    dims,
    parts,
    labels,
    modality,
    labeled,
    head_params,
    common_params,
    head_all,
    common_all,
    head_low,
    common_low,
    common_wide,
    send_sem,
    recv_sem,
    own_sem,
):
    me = my_place(dims)
    my_head = head_of(dims, me)
    n_head = dims[2] * dims[3]
    shard_rows, common_rows = head_params.shape[0], common_params.shape[0]
    per_head = labels.shape[0] // n_head
    row = lax.broadcasted_iota(jnp.int32, labels.shape, 0)
    mine = (row >= my_head * per_head) & (row < (my_head + 1) * per_head) & (labeled[...] == 1)
    lane = lax.broadcasted_iota(jnp.int32, (1, LANES), 1)
    counts = jnp.zeros((1, LANES), jnp.float32)
    for m in range(MODES):
        member = jnp.where(mine & (modality[...] == m), 1.0, 0.0)
        counts = counts + jnp.where(lane == m, jnp.sum(member, (0, 1), keepdims=True), 0.0)
    padding = head_low.shape[0] - shard_rows
    tail = shard_rows // TILE * TILE
    head_low[:tail] = head_params[:tail].astype(low)
    last = [jnp.broadcast_to(counts, (padding, LANES))]
    if shard_rows > tail:
        last = [head_params[tail:]] + last
    head_low[tail:] = jnp.concatenate(last, 0).astype(low)
    common_wide[...] = jnp.zeros(common_wide.shape, jnp.float32)
    common_wide[:common_rows] = common_params[...]
    piece = common_low.shape[0]
    common_low[...] = common_wide[pl.ds(pl.multiple_of(my_head * piece, TILE), piece)].astype(low)

    greet(dims, me, ring_and_others(dims))
    srcs, outs = (head_low, common_low), (head_all, common_all)
    copies = {}

    def block(p, offset):
        place = shifted(dims, me, offset, -1)
        array, first, rows, order = parts[p]
        return outs[array].at[blk_of(dims, place), head_of(dims, place), pl.ds(first, rows)]

    own = []
    for is_send, (rank, axis, p, offset) in gather_order(dims, parts)[0]:
        if is_send:
            step = 1 if axis == RING else offset[axis]
            before = with_at(offset, axis, offset[axis] - step)
            array, first, rows, order = parts[p]
            source = block(p, before) if any(before) else srcs[array].at[pl.ds(first, rows)]
            i = len(copies)
            copies[(p, offset)] = remote(
                source,
                block(p, before),
                send_sem.at[i],
                recv_sem.at[i],
                shifted(dims, me, along(axis, step), 1),
                dims,
            )
            copies[(p, offset)].start()
        else:
            if not own:
                for array in range(2):
                    copy = pltpu.make_async_copy(
                        srcs[array], outs[array].at[blk_of(dims, me), my_head], own_sem.at[array]
                    )
                    copy.start()
                    own.append(copy)
            copies[(p, offset)].wait_recv()
    for copy in copies.values():
        copy.wait_send()
    for copy in own:
        copy.wait()


def ring_and_others(dims):
    ring = {along(RING, 1 % dims[RING]), along(RING, (dims[RING] - 1) % dims[RING])}
    return sorted(ring - {(0, 0, 0, 0)}) + axis_peers(dims, (1, 2, 3))


def cut(array, rows, shares):
    result = []
    first, so_far = 0, 0
    whole = sum(share for share, order in shares)
    for share, order in shares:
        so_far += share
        end = rows * so_far // whole // TILE * TILE if so_far < whole else rows
        if end > first:
            result.append((array, first, end - first, order))
        first = end
    return tuple(result)


ZYXC, ZXYC, YXZC, XYZC = (0, 1, 2, 3), (0, 2, 1, 3), (1, 2, 0, 3), (2, 1, 0, 3)
GATHER_SHARES = ((8, ZYXC), (6, ZXYC), (2, YXZC), (2, XYZC))
REDUCE_SHARES = ((7, ZYXC), (7, ZXYC), (2, YXZC), (2, XYZC))


def gather_all(dims, marks, params, rows, collective_id):
    z, y, x, cores = dims
    parts = cut(0, rows[0], GATHER_SHARES) + cut(1, rows[1], ((1, ZXYC),))
    count = len(parts) * (z * y * x * cores - 1)
    return pl.pallas_call(
        functools.partial(gather_kernel, dims, parts),
        out_shape=[shape_of((z * y, x * cores, n, LANES)) for n in rows],
        in_specs=[VMEM_SPEC] * 5,
        out_specs=[ANY_SPEC] * 2,
        scratch_shapes=[pltpu.VMEM((n, LANES), low) for n in rows]
        + [
            pltpu.VMEM((x * cores * rows[1], LANES), jnp.float32),
            pltpu.SemaphoreType.DMA((count,)),
            pltpu.SemaphoreType.DMA((count,)),
            pltpu.SemaphoreType.DMA((2,)),
        ],
        compiler_params=pltpu.CompilerParams(collective_id=collective_id, has_side_effects=True),
        name="gather_weights",
    )(*marks, *params)


def reduce_order(dims, parts):
    ready, arrived, order = set(), set(), []

    def message(p, position, offset):
        z = offset[RING]
        rank = (dims[RING] - z if z else dims[RING], position, tuple(-o for o in offset), p)
        return (rank, parts[p][3][position], p, position, offset)

    def done(p, position, offset):
        ready.add((p, position, offset))
        if position == 4:
            return []
        axis = parts[p][3][position]
        d = offset[axis]
        first = d != 0 and (axis != RING or d == dims[axis] - 1)
        return ([message(p, position, offset)] if first else []) + advance(p, position, offset)

    def advance(p, position, offset):
        axis = parts[p][3][position]
        n = dims[axis]
        start = with_at(offset, axis, 0)
        if axis == RING:
            here = (p, position, offset)
            if here in ready and here in arrived:
                order.append((None, here))
                if offset[axis]:
                    return [message(p, position, offset)]
                return done(p, position + 1, offset)
        elif (p, position, start) in ready and (p, position + 1, start) not in ready:
            if all((p, position, with_at(start, axis, d)) in arrived for d in range(1, n)):
                order.append((None, (p, position, start)))
                return done(p, position + 1, start)
        return []

    def follow(sent):
        rank, axis, p, position, offset = sent
        here = with_at(offset, axis, offset[axis] - 1) if axis == RING else offset
        arrived.add((p, position, here))
        return advance(p, position, here)

    first = []
    for p in range(len(parts)):
        for offset in all_offsets(dims, range(4)):
            first += done(p, 0, offset)
    now = in_order(first, follow, lambda m: time_of(parts[m[2]][2], m[1]), AHEAD, order)
    return order, now


def all_offsets(dims, axes):
    offsets = [(0, 0, 0, 0)]
    for a in axes:
        offsets = [with_at(o, a, d) for o in offsets for d in range(dims[a])]
    return offsets


def reduce_kernel(dims, parts, *refs):
    srcs, tile = refs[:2], refs[2]
    head_out, common_out, totals = refs[3:6]
    places = len(parts) * 4
    buffers = refs[6 : 6 + places]
    head_sum, common_sum, shares, send_sem, recv_sem, near_tiles, far_tiles = refs[6 + places :]
    sums = (head_sum, common_sum)
    me = my_place(dims)
    z, y, x, cores = dims
    across = peers_across(dims)
    others = [o for o in all_offsets(dims, (0, 1)) if any(o)]
    met = ring_and_others(dims)
    greet(dims, me, met + [o for o in across + others if o not in met])
    push = Pushes(dims, me, send_sem, recv_sem)
    copies = {}

    def slot(p, position, offset):
        order = parts[p][3]
        axis = order[position]
        rest = [o for o in all_offsets(dims, order[position + 1 :])]
        k = rest.index(with_at(offset, axis, 0))
        return buffers[p * 4 + position].at[k, max(offset[axis] - 1, 0)]

    def summed(p, position, offset):
        array, first, rows, order = parts[p]
        if position == 0:
            place = shifted(dims, me, offset, 1)
            return srcs[array].at[blk_of(dims, place), head_of(dims, place), pl.ds(first, rows)]
        return slot(p, position - 1, offset)

    def ring_slot(p, position, offset):
        axis = parts[p][3][position]
        return slot(p, position, with_at(offset, axis, offset[axis] + 1))

    def add(p, position, offset):
        array, first, rows, order = parts[p]
        axis = order[position]
        if axis == RING:
            arrivals = [ring_slot(p, position, offset)]
        else:
            arrivals = [slot(p, position, with_at(offset, axis, d)) for d in range(1, dims[axis])]
        mine = summed(p, position, offset)
        step = row_chunk(rows)

        @pl.loop(0, rows // step)
        def some_rows(n):
            at = pl.ds(pl.multiple_of(n * step, step), step)
            total = mine[at].astype(jnp.float32)
            for arrival in arrivals:
                total = total + arrival[at].astype(jnp.float32)
            if position == 3 and not any(offset):
                sums[array][pl.ds(pl.multiple_of(first + n * step, TILE), step)] = total
            else:
                arrivals[0][at] = total.astype(low)

    for is_send, what in reduce_order(dims, parts)[0]:
        if is_send is None:
            add(*what)
        elif is_send:
            rank, axis, p, position, offset = what
            d = offset[axis]
            started = axis != RING or d == dims[axis] - 1
            source = summed(p, position, offset) if started else ring_slot(p, position, offset)
            step = along(axis, 1 if axis == RING else d)
            copies[what] = push(source, slot(p, position, offset), step)
        else:
            copies[what].wait_recv()
    my_head, my_blk = head_of(dims, me), blk_of(dims, me)
    shares[my_head] = common_sum[...].astype(low)
    share_copies = [push(shares.at[my_head], shares.at[my_head], o) for o in across]
    amount = head_out.shape[0]
    head_out[...] = head_sum[:amount]
    squares = jnp.sum(head_sum[:amount] * head_sum[:amount], 0, keepdims=True)
    squares = squares + jnp.sum(common_sum[...] * common_sum[...], 0, keepdims=True)
    lane = lax.broadcasted_iota(jnp.int32, (1, LANES), 1)
    near_tiles[my_head] = tile[...] + jnp.where(
        lane == MODES, jnp.sum(squares, 1, keepdims=True), 0.0
    )
    near = [push(near_tiles.at[my_head], near_tiles.at[my_head], o) for o in across]
    for copy in near:
        copy.wait_recv()
    far_tiles[my_blk] = jnp.sum(near_tiles[...], 0)
    far = [push(far_tiles.at[my_blk], far_tiles.at[my_blk], o) for o in others]
    for copy in share_copies:
        copy.wait_recv()
    piece = shares.shape[1]
    for k in range(x * cores):
        amount = min(piece, common_out.shape[0] - k * piece)
        common_out[k * piece : k * piece + amount] = shares[k].astype(jnp.float32)[:amount]
    for copy in far:
        copy.wait_recv()
    totals[...] = jnp.sum(far_tiles[...], 0)
    push.finish()


def row_chunk(rows):
    for count in (4, 3, 2):
        if rows % (count * TILE) == 0:
            return rows // count
    return rows


def reduce_all(dims, arrays, valid, tile, collective_id):
    z, y, x, cores = dims
    rows = [array.shape[2] for array in arrays]
    parts = cut(0, rows[0], [(share, order[::-1]) for share, order in REDUCE_SHARES])
    parts = parts + cut(1, rows[1], ((1, ZXYC[::-1]),))
    scratch = []
    for array, first, amount, order in parts:
        for position, axis in enumerate(order):
            rest = len(all_offsets(dims, order[position + 1 :]))
            scratch.append(pltpu.VMEM((rest, dims[axis] - 1, amount, LANES), low))
    count = len(parts) * (z * y * x * cores - 1) + 2 * (x * cores - 1) + z * y - 1
    return pl.pallas_call(
        functools.partial(reduce_kernel, dims, parts),
        out_shape=[
            shape_of((valid[0], LANES), jnp.float32),
            shape_of((valid[1], LANES), jnp.float32),
            shape_of((8, LANES), jnp.float32),
        ],
        in_specs=[VMEM_SPEC] * 3,
        out_specs=[VMEM_SPEC] * 3,
        scratch_shapes=scratch
        + [pltpu.VMEM((n, LANES), jnp.float32) for n in rows]
        + [
            pltpu.VMEM((x * cores, rows[1], LANES), low),
            pltpu.SemaphoreType.DMA((count,)),
            pltpu.SemaphoreType.DMA((count,)),
            pltpu.VMEM((x * cores, 8, LANES), jnp.float32),
            pltpu.VMEM((z * y, 8, LANES), jnp.float32),
        ],
        compiler_params=pltpu.CompilerParams(
            collective_id=collective_id, has_side_effects=True, vmem_limit_bytes=60 * MIB
        ),
        name="reduce_gradients",
    )(*arrays, tile)


def contract_first(a, b):
    return lax.dot_general(a, b, (((0,), (0,)), ((), ())), preferred_element_type=jnp.float32)


def product(a, b):
    return jnp.dot(a, b, preferred_element_type=jnp.float32)


def against(a, b):
    return lax.dot_general(a, b, (((1,), (1,)), ((), ())), preferred_element_type=jnp.float32)


def clip_bounds(lengths):
    result, first = [], 0
    for clip in range(lengths.shape[0]):
        end = first + lengths[clip]
        result.append((first, end))
        first = end
    return result


def clip_borders(bounds, place):
    opening = jnp.zeros(place.shape, jnp.int32)
    ending = jnp.full(place.shape, 1 << 30, jnp.int32)
    for clip, (begin, end) in enumerate(bounds):
        here = place == clip
        opening = jnp.where(here, begin, opening)
        ending = jnp.where(here, end, ending)
    return opening, ending


def lane_of_tail(a):
    return HD if a % 2 == 0 else 0


def in_head(a, axis):
    shape = (1, LANES) if axis else (LANES, 1)
    lane = lax.broadcasted_iota(jnp.int32, shape, axis)
    return (lane >= a * HD) & (lane < (a + 1) * HD)


def all_lanes(block, first, width):
    piece = block[:, first : first + width]
    if width < LANES:
        piece = jnp.concatenate([piece, jnp.zeros((piece.shape[0], LANES - width), piece.dtype)], 1)
    return piece


def with_key_tail(bounds, a, first_row, columns):
    clips = len(bounds)
    place = lax.broadcasted_iota(jnp.int32, (1, LANES), 1) - lane_of_tail(a)
    opening, ending = clip_borders(bounds, place)
    ones = jnp.where((place >= clips) & (place < clips + 3), 1.0, 0.0)
    row = first_row + lax.broadcasted_iota(jnp.int32, columns.shape, 0)
    tail = jnp.where((row >= opening) & (row < ending), ones, big_negative)
    return jnp.where(in_head(a, 1), columns.astype(jnp.float32), tail).astype(low)


def in_three(place, value):
    top = value.astype(low).astype(jnp.float32)
    middle = (value - top).astype(low).astype(jnp.float32)
    bottom = value - top - middle
    return (
        jnp.where(place == 0, top, 0.0)
        + jnp.where(place == 1, middle, 0.0)
        + jnp.where(place == 2, bottom, 0.0)
    )


def with_tail(a, rows, tail):
    return jnp.concatenate([rows, tail] if lane_of_tail(a) else [tail, rows], 0)


def with_query_tail(bounds, a, first_row, rows, extra):
    clips = len(bounds)
    place = lax.broadcasted_iota(jnp.int32, (HD, 1), 0)
    opening, ending = clip_borders(bounds, place)
    row = first_row + lax.broadcasted_iota(jnp.int32, (1, rows.shape[1]), 1)
    inside = (place < clips) & (row >= opening) & (row < ending)
    tail = jnp.where(inside, 1.0, 0.0)
    if extra is not None:
        tail = tail + in_three(place - clips, -extra)
    return with_tail(a, rows * HD ** (-0.5), tail).astype(low)


class Pushes:
    def __init__(self, dims, me, send_sem, recv_sem):
        self.dims, self.me, self.send_sem, self.recv_sem = dims, me, send_sem, recv_sem
        self.started = []

    def __call__(self, src, dst, offset):
        i = len(self.started)
        place = shifted(self.dims, self.me, offset, 1)
        copy = remote(src, dst, self.send_sem.at[i], self.recv_sem.at[i], place, self.dims)
        copy.start()
        self.started.append(copy)
        return copy

    def finish(self):
        for copy in self.started:
            copy.wait_send()


def peers_across(dims):
    z, y, x, cores = dims
    across = [(0, 0, a, c) for a in range(x) for c in range(cores) if (a, c) != (0, 0)]
    return sorted(across, key=lambda o: (o[2] == 0, o[3]))


def ring_and_sides(dims):
    z = dims[0]
    ring = sorted({along(0, 1 % z), along(0, (z - 1) % z)} - {(0, 0, 0, 0)})
    return ring + axis_peers(dims, (1,))


def attend_kernel(
    dims,
    heads,
    query_step,
    lengths,
    q_in,
    kv_in,
    o_out,
    lse,
    out_t,
    q_all,
    kv_all,
    keys,
    values_t,
    queries,
    top,
    accum,
    o_mine,
    send_sem,
    recv_sem,
    own_sem,
):
    z, y, x, cores = dims
    me = my_place(dims)
    bounds = clip_bounds(lengths)
    n_head = x * cores
    rows, width = q_in.shape[1], heads * HD
    amount = n_head * rows
    my_blk, my_head = blk_of(dims, me), head_of(dims, me)
    across = peers_across(dims)
    sides = axis_peers(dims, (1,))
    greet(dims, me, across + ring_and_sides(dims))
    push = Pushes(dims, me, send_sem, recv_sem)
    own_kv = pltpu.make_async_copy(kv_in.at[my_head], kv_all.at[my_blk, my_head], own_sem.at[0])
    own_q = pltpu.make_async_copy(q_in.at[my_head], q_all.at[my_head], own_sem.at[1])
    own_kv.start()
    own_q.start()

    def to_head(src, dst, o):
        return push(src.at[head_of(dims, shifted(dims, me, o, 1))], dst, o)

    kv_copies = {o: to_head(kv_in, kv_all.at[my_blk, my_head], o) for o in across}
    q_copies = [to_head(q_in, q_all.at[my_head], o) for o in across]
    ring, side = {}, {}
    pieces = [(0, 0, 0, 0)] + across[::-1]

    def send_on(s, n):
        block = kv_all.at[
            blk_of(dims, shifted(dims, me, along(0, s), -1)),
            head_of(dims, shifted(dims, me, pieces[n], -1)),
        ]
        if s < z - 1:
            ring[(s + 1, n)] = push(block, block, along(0, 1))
        for o in sides:
            side[(s, n, o)] = push(block, block, o)

    def compute(offset):
        blk = blk_of(dims, shifted(dims, me, offset, -1))

        @pl.loop(0, n_head)
        def build(h):
            at = pl.ds(pl.multiple_of(h * rows, rows), rows)
            block = kv_all[blk, h]
            k_block, v_block = all_lanes(block, 0, width), all_lanes(block, width, width)
            v_t = v_block.astype(jnp.float32).T
            for a in range(heads):
                keys[a, at, :] = with_key_tail(bounds, a, blk * amount + h * rows, k_block)
                values_t[a, :HD, at] = v_t[a * HD : (a + 1) * HD].astype(low)

        @pl.loop(0, amount // query_step)
        def query_block(n):
            at = pl.ds(pl.multiple_of(n * query_step, query_step), query_step)
            for a in range(heads):
                scores = product(keys[a], queries[a, :, at])
                old = top[a, :, at]
                new = jnp.maximum(old, jnp.max(scores, 0, keepdims=True))
                top[a, :, at] = new
                probs = jnp.exp(scores - new).astype(low)
                total = accum[a, :, at] * jnp.exp(old - new) + product(values_t[a], probs)
                accum[a, :, at] = total

    for a in range(heads):
        values_t[a, HD:, :] = jnp.ones((values_t.shape[1] - HD, amount), low)
        top[a] = jnp.full((1, amount), -1e38, jnp.float32)
        accum[a] = jnp.zeros(accum.shape[1:], jnp.float32)
    own_kv.wait()
    send_on(0, 0)
    for n in range(1, n_head):
        kv_copies[pieces[n]].wait_recv()
        send_on(0, n)
    own_q.wait()
    for copy in q_copies:
        copy.wait_recv()
    for a in range(heads):
        for h in range(n_head):
            q_t = all_lanes(q_all[h], 0, width).astype(jnp.float32).T
            queries[a, :, h * rows : (h + 1) * rows] = with_query_tail(
                bounds, a, my_blk * amount + h * rows, q_t[a * HD : (a + 1) * HD], None
            )
    compute((0, 0, 0, 0))
    for s in range(1, z + 1):
        if s < z:
            for n in range(n_head):
                ring[(s, n)].wait_recv()
                send_on(s, n)
            compute(along(0, s))
        for o in sides:
            for n in range(n_head):
                side[(s - 1, n, o)].wait_recv()
            compute((s - 1, o[1], 0, 0))
    for a in range(heads):
        total = accum[a, HD : HD + 1, :]
        out_t[a * HD : (a + 1) * HD, :] = accum[a, :HD, :] / total
        lse[a : a + 1, :] = top[a] + jnp.log(total)
    for h in range(n_head):
        o_mine[h] = out_t[:, h * rows : (h + 1) * rows].T.astype(low)
    o_copies = [to_head(o_mine, o_out.at[my_head], o) for o in across]
    own_o = pltpu.make_async_copy(o_mine.at[my_head], o_out.at[my_head], own_sem.at[2])
    own_o.start()
    own_o.wait()
    for copy in o_copies:
        copy.wait_recv()
    push.finish()


def attend(dims, lengths, q, kv, heads, collective_id):
    z, y, x, cores = dims
    n_head, rows, width = q.shape
    amount = n_head * rows
    count = 3 * (n_head - 1) + n_head * (z - 1 + z * (y - 1))
    return pl.pallas_call(
        functools.partial(attend_kernel, dims, heads, 256),
        out_shape=(
            jax.ShapeDtypeStruct(q.shape, low),
            jax.ShapeDtypeStruct((heads, amount), jnp.float32),
            jax.ShapeDtypeStruct((width, amount), jnp.float32),
            jax.ShapeDtypeStruct(q.shape, low),
            jax.ShapeDtypeStruct((z * y,) + kv.shape, low),
        ),
        in_specs=[SMEM_SPEC, VMEM_SPEC, VMEM_SPEC],
        out_specs=[VMEM_SPEC] * 5,
        scratch_shapes=[
            pltpu.VMEM((heads, amount, LANES), low),
            pltpu.VMEM((heads, HD + TILE, amount), low),
            pltpu.VMEM((heads, LANES, amount), low),
            pltpu.VMEM((heads, 1, amount), jnp.float32),
            pltpu.VMEM((heads, HD + TILE, amount), jnp.float32),
            pltpu.VMEM(q.shape, low),
            pltpu.SemaphoreType.DMA((count,)),
            pltpu.SemaphoreType.DMA((count,)),
            pltpu.SemaphoreType.DMA((3,)),
        ],
        compiler_params=pltpu.CompilerParams(
            collective_id=collective_id, has_side_effects=True, vmem_limit_bytes=56 * MIB
        ),
        name="attend",
    )(lengths, q, kv)


def attend_back_kernel(
    dims,
    heads,
    key_step,
    lengths,
    q_all,
    kv_all,
    do_in,
    out_t,
    lse,
    d_q_out,
    d_kv_out,
    do_all,
    keys,
    keys_t,
    values,
    queries,
    douts,
    d_q_t,
    q_rows,
    do_rows,
    side_out,
    side_in,
    ring_out,
    ring_in,
    mine,
    d_q_mine,
    d_kv_mine,
    send_sem,
    recv_sem,
    own_sem,
):
    z, y, x, cores = dims
    me = my_place(dims)
    bounds = clip_bounds(lengths)
    n_head, rows, width = q_all.shape
    amount = n_head * rows
    my_blk, my_head = blk_of(dims, me), head_of(dims, me)
    across = peers_across(dims)
    sides = axis_peers(dims, (1,))
    greet(dims, me, across + ring_and_sides(dims))
    push = Pushes(dims, me, send_sem, recv_sem)

    def to_head(src, dst, o):
        return push(src.at[head_of(dims, shifted(dims, me, o, 1))], dst, o)

    do_copies = [to_head(do_in, do_all.at[my_head], o) for o in across]
    own_do = pltpu.make_async_copy(do_in.at[my_head], do_all.at[my_head], own_sem.at[0])
    own_do.start()
    place = lax.broadcasted_iota(jnp.int32, (HD, 1), 0)

    def at_head(h):
        return slice(h * rows, (h + 1) * rows)

    for h in range(n_head):
        block = all_lanes(q_all[h], 0, width).astype(jnp.float32)
        q_t = block.T
        for a in range(heads):
            queries[a, :, at_head(h)] = with_query_tail(
                bounds,
                a,
                my_blk * amount + h * rows,
                q_t[a * HD : (a + 1) * HD],
                lse[a : a + 1, at_head(h)],
            )
            q_rows[a, :, at_head(h)] = (q_t[a * HD : (a + 1) * HD] * HD ** (-0.5)).astype(low)
    for a in range(heads):
        d_q_t[a] = jnp.zeros(d_q_t.shape[1:], jnp.float32)
    own_do.wait()
    for copy in do_copies:
        copy.wait_recv()
    for h in range(n_head):
        block = all_lanes(do_all[h], 0, width).astype(jnp.float32)
        do_t = block.T
        for a in range(heads):
            part = do_t[a * HD : (a + 1) * HD]
            delta = jnp.sum(part * out_t[a * HD : (a + 1) * HD, at_head(h)], 0, keepdims=True)
            douts[a, :, at_head(h)] = with_tail(a, part, in_three(place, -delta)).astype(low)
            do_rows[a, :, at_head(h)] = part.astype(low)

    def compute(offset, target):
        blk = blk_of(dims, shifted(dims, me, offset, 1))

        @pl.loop(0, n_head)
        def build(h):
            at = pl.ds(pl.multiple_of(h * rows, rows), rows)
            block = kv_all[blk, h]
            k_block, v_block = all_lanes(block, 0, width), all_lanes(block, width, width)
            k_t = k_block.astype(jnp.float32).T
            lane = lax.broadcasted_iota(jnp.int32, (1, LANES), 1)
            for a in range(heads):
                keys[a, at, :] = with_key_tail(bounds, a, blk * amount + h * rows, k_block)
                keys_t[a, :, at] = k_t[a * HD : (a + 1) * HD].astype(low)
                tail = lane - lane_of_tail(a)
                ones = jnp.where((tail >= 0) & (tail < 3), 1.0, 0.0)
                values[a, at, :] = jnp.where(
                    in_head(a, 1), v_block.astype(jnp.float32), ones
                ).astype(low)

        @pl.loop(0, amount // key_step)
        def key_block(k):
            at = pl.ds(pl.multiple_of(k * key_step, key_step), key_step)
            d_keys, d_values = [], []
            for a in range(heads):
                probs = jnp.exp(product(keys[a, at, :], queries[a]))
                d_probs = product(values[a, at, :], douts[a])
                d_scores = (probs * d_probs).astype(low)
                d_values.append(against(do_rows[a], probs.astype(low)))
                d_keys.append(against(q_rows[a], d_scores))
                d_q_t[a] = d_q_t[a] + product(keys_t[a, :, at], d_scores)
            target[at, :] = jnp.concatenate(d_keys + d_values, 0).T.astype(target.dtype)

    side, ring = {}, {}

    def send_sides(s):
        for o in sides:
            compute((z - s, o[1], 0, 0), side_out.at[s - 1, o[1] - 1])
            side[(s, o)] = push(side_out.at[s - 1, o[1] - 1], side_in.at[s - 1, o[1] - 1], o)

    def combine(s):
        for o in sides:
            side[(s, o)].wait_recv()
        if s > 1:
            ring[s - 1].wait_recv()

        for h in range(n_head):
            total = mine[(s - 1) % 2, at_head(h), :]
            for o in sides:
                total = total + side_in[s - 1, o[1] - 1, at_head(h), :].astype(jnp.float32)
            if s > 1:
                total = total + ring_in[s - 2, at_head(h), :].astype(jnp.float32)
            if s < z:
                ring_out[s - 1, at_head(h), :] = total.astype(low)
            else:
                d_kv_mine[h] = total.astype(low)
        if s < z:
            ring[s] = push(ring_out.at[s - 1], ring_in.at[s - 1], along(0, 1))

    for s in range(1, z + 1):
        send_sides(s)
        if s > 1:
            combine(s - 1)
        compute((z - s if s < z else 0, 0, 0, 0), mine.at[(s - 1) % 2])
    for h in range(n_head):
        block = jnp.concatenate([d_q_t[a, :, at_head(h)] for a in range(heads)], 0) * HD ** (-0.5)
        d_q_mine[h] = block.T.astype(low)
    copies = [to_head(d_q_mine, d_q_out.at[my_head], o) for o in across]
    own_q = pltpu.make_async_copy(d_q_mine.at[my_head], d_q_out.at[my_head], own_sem.at[1])
    own_q.start()
    combine(z)
    copies += [to_head(d_kv_mine, d_kv_out.at[my_head], o) for o in across]
    own_kv = pltpu.make_async_copy(d_kv_mine.at[my_head], d_kv_out.at[my_head], own_sem.at[2])
    own_kv.start()
    own_q.wait()
    own_kv.wait()
    for copy in copies:
        copy.wait_recv()
    push.finish()


def attend_back(dims, lengths, q, kv, dout, out_t, lse, heads, collective_id):
    z, y, x, cores = dims
    n_head, rows, width = q.shape
    amount = n_head * rows
    count = 3 * (n_head - 1) + z * (y - 1) + z - 1
    block = (amount, 2 * width)
    others = max(y - 1, 1)
    return pl.pallas_call(
        functools.partial(attend_back_kernel, dims, heads, 256),
        out_shape=(
            jax.ShapeDtypeStruct(q.shape, low),
            jax.ShapeDtypeStruct((n_head, rows, 2 * width), low),
        ),
        in_specs=[SMEM_SPEC] + [VMEM_SPEC] * 5,
        out_specs=[VMEM_SPEC] * 2,
        scratch_shapes=[
            pltpu.VMEM(q.shape, low),
            pltpu.VMEM((heads, amount, LANES), low),
            pltpu.VMEM((heads, HD, amount), low),
            pltpu.VMEM((heads, amount, LANES), low),
            pltpu.VMEM((heads, LANES, amount), low),
            pltpu.VMEM((heads, LANES, amount), low),
            pltpu.VMEM((heads, HD, amount), jnp.float32),
            pltpu.VMEM((heads, HD, amount), low),
            pltpu.VMEM((heads, HD, amount), low),
            pltpu.VMEM((z, others) + block, low),
            pltpu.VMEM((z, others) + block, low),
            pltpu.VMEM((max(z - 1, 1),) + block, low),
            pltpu.VMEM((max(z - 1, 1),) + block, low),
            pltpu.VMEM((2,) + block, jnp.float32),
            pltpu.VMEM(q.shape, low),
            pltpu.VMEM((n_head, rows, 2 * width), low),
            pltpu.SemaphoreType.DMA((count,)),
            pltpu.SemaphoreType.DMA((count,)),
            pltpu.SemaphoreType.DMA((3,)),
        ],
        compiler_params=pltpu.CompilerParams(
            collective_id=collective_id, has_side_effects=True, vmem_limit_bytes=60 * MIB
        ),
        name="attend_back",
    )(lengths, q, kv, dout, out_t, lse)


def part_shapes(n_head):
    width = HEADS // n_head * HD
    hidden = FF // n_head
    return (
        (D, width, True),
        (DI, 2 * width, True),
        (width, D, False),
        (D, 3 * width, True),
        (width, D, False),
        (D, hidden, True),
        (hidden, D, False),
        (D, C // n_head, True),
    )


def borders(n_head):
    result = [0]
    for rows, columns, joined in part_shapes(n_head):
        result.append(result[-1] + rows * columns // LANES)
    return result


def period(columns):
    amount = 1
    while amount * columns % LANES:
        amount *= 2
    return amount


def segments(start, amount, unit):
    result = []
    while amount > 0:
        which, at = divmod(start, unit)
        size = min(unit - at, amount)
        result.append((which, at, at + size))
        start, amount = start + size, amount - size
    return result


def joined_lanes(pieces):
    return pieces[0] if len(pieces) == 1 else jnp.concatenate(pieces, 1)


def lane_blocks(value):
    rows, columns = value.shape
    missing = -columns % LANES
    if missing:
        value = jnp.concatenate([value, jnp.zeros((rows, missing), value.dtype)], 1)
    return [value[:, i : i + LANES] for i in range(0, columns + missing, LANES)]


def every(first, amount, stride):
    return pl.ds(first, amount) if stride == 1 else pl.ds(first, amount, stride=stride)


def matrix_of(stage, first, rows, columns, line):
    if columns % LANES == 0:
        stride = columns // LANES
        for j in range(stride):
            yield j * LANES, stage[every(first + j, rows, stride), :]
        return
    height = period(columns)
    stride = height * columns // LANES
    for k in range(height):
        pieces = [
            stage[every(first + which, rows // height, stride), :][:, begin:end]
            for which, begin, end in segments(k * columns, columns, LANES)
        ]
        for i, piece in enumerate(lane_blocks(joined_lanes(pieces))):
            line[i, every(k, rows // height, height), :] = piece
    for i in range(-(-columns // LANES)):
        yield i * LANES, line[i, :rows, : min(columns - i * LANES, LANES)]


def matrix_into(stage, first, value, line):
    rows, columns = value.shape
    if columns % LANES == 0:
        stride = columns // LANES
        for j in range(stride):
            stage[every(first + j, rows, stride), :] = value[:, j * LANES : (j + 1) * LANES]
        return
    height = period(columns)
    stride = height * columns // LANES
    for i, piece in enumerate(lane_blocks(value)):
        line[i, :rows, :] = piece
    for i in range(stride):
        pieces = [
            line[which, every(k, rows // height, height), :][:, begin:end]
            for k, first_lane, last_lane in segments(i * LANES, LANES, columns)
            for which, begin, end in segments(first_lane, last_lane - first_lane, LANES)
        ]
        stage[every(first + i, rows // height, stride), :] = joined_lanes(pieces)


def load_stage(stage, held, first_shard, shard_rows, group):
    for b in range(held.shape[0]):
        stage[pl.ds(b * shard_rows, shard_rows), :] = held[b, group, :shard_rows, :].astype(jnp.float32)


def load_common(stage, held, valid):
    piece = held.shape[2]
    for b in range(held.shape[0]):
        for k in range(held.shape[1]):
            amount = min(piece, valid - k * piece)
            stage[b * valid + k * piece : b * valid + k * piece + amount, :] = held[b, k].astype(
                jnp.float32
            )[:amount]


def common_blocks(first_row, last_row, valid):
    return first_row // valid, -(-last_row // valid) - first_row // valid


def load_matrices(stage, first_row, n_head, group, which, targets, line):
    starts, shapes = borders(n_head), part_shapes(n_head)
    for m, target in zip(which, targets):
        rows, columns, joined = shapes[m]
        row = 0 if joined else group * rows
        column = group * columns if joined else 0
        for j, value in matrix_of(stage, starts[m] - first_row, rows, columns, line):
            size = value.shape[1]
            target[row : row + rows, column + j : column + j + size] = value.astype(target.dtype)


def normalized(x):
    centre = x - jnp.mean(x, -1, keepdims=True)
    rate = lax.rsqrt(jnp.mean(centre * centre, -1, keepdims=True) + norm_eps)
    return centre * rate, rate


def layer_norm(x, gain):
    return normalized(x)[0] * gain


def norm_pullback(x, gain, grad):
    unit, rate = normalized(x)
    inside = grad * gain
    both = jnp.mean(inside * unit, -1, keepdims=True)
    d_x = rate * (inside - jnp.mean(inside, -1, keepdims=True) - unit * both)
    return d_x, jnp.sum(grad * unit, 0, keepdims=True)


def head_lanes(group, heads, value):
    width = heads * HD
    block = value[:, group * width : (group + 1) * width]
    lane = lax.broadcasted_iota(jnp.int32, (1, width), 1)
    result = []
    for a in range(heads):
        here = (lane >= a * HD) & (lane < (a + 1) * HD)
        result.append((here, jnp.where(here, block, jnp.zeros_like(block))))
    return result


def place_of(bounds, first, amount):
    row = first + lax.broadcasted_iota(jnp.int32, (amount, 1), 0)
    opening = jnp.zeros((amount, 1), jnp.int32)
    for begin, end in bounds:
        opening = jnp.where((row >= begin) & (row < end), begin, opening)
    offset = row - opening
    turns = jnp.floor((offset.astype(jnp.float32) + 0.5) * (1.0 / LAT)).astype(jnp.int32)
    return offset - turns * LAT


def picked_rows(bounds, rows, n_head):
    first = lax.axis_index("blk") * (rows * n_head) + lax.axis_index("head") * rows
    lane = lax.broadcasted_iota(jnp.int32, (rows, LAT), 1)
    return jnp.where(lane == place_of(bounds, first, rows), 1.0, 0.0).astype(low)


def enc_scores(q_head, keys):
    return against(q_head, keys) * HD ** (-0.5)


def encode_kernel(
    n_head,
    shard_rows,
    valid,
    rows,
    lengths,
    weights,
    common,
    inputs_t,
    enc_query,
    enc_keyval,
    enc_output,
    self_project,
    gains,
    z_zero,
    h_zero,
    x_norm_t,
    q_enc,
    kv_enc,
    o_enc,
    z_one,
    h_one,
    q_self,
    kv_self,
    counts,
    held,
    held_common,
    held_counts,
    stage,
    stage_common,
    line,
    latent_table,
    sems,
):
    heads = HEADS // n_head
    width = heads * HD
    shards = held.shape[0]
    bounds = clip_bounds(lengths)
    first = DQ * D // LANES
    block, blocks = common_blocks(first, first + (LAT + 4) * D // LANES, valid)
    tail = shard_rows // TILE * TILE
    copies = [
        pltpu.make_async_copy(common.at[pl.ds(block, blocks)], held_common, sems.at[0]),
        pltpu.make_async_copy(weights.at[pl.ds(0, shards)], held, sems.at[1]),
        pltpu.make_async_copy(weights.at[:, :, pl.ds(tail, TILE)], held_counts, sems.at[2]),
    ]
    for copy in copies:
        copy.start()
    centre = inputs_t[...].astype(jnp.float32)
    centre = centre - jnp.mean(centre, 0, keepdims=True)
    rate = lax.rsqrt(jnp.mean(centre * centre, 0, keepdims=True) + norm_eps)
    x_norm_t[...] = (centre * rate).astype(low)
    copies[0].wait()
    load_common(stage_common, held_common, valid)
    first = first - block * valid
    for j, value in matrix_of(stage_common, first, LAT, D, line):
        latent_table[:, j : j + LANES] = value.astype(low)
    for j, value in matrix_of(stage_common, first + LAT * D // LANES, 4, D, line):
        gains[:, j : j + LANES] = value
    picked = picked_rows(bounds, rows, n_head)
    z_zero[...] = product(picked, latent_table[...])
    h_zero[...] = layer_norm(z_zero[...], gains[0:1, :]).astype(low)
    copies[2].wait()
    counted = held_counts[...].astype(jnp.float32)[:, :, shard_rows - tail : shard_rows - tail + 1]
    counts[...] = jnp.broadcast_to(jnp.sum(counted, (0, 1)), counts.shape)
    copies[1].wait()
    for g in range(n_head):
        load_stage(stage, held, 0, shard_rows, g)
        load_matrices(
            stage, 0, n_head, g, (0, 1, 2, 3), (enc_query, enc_keyval, enc_output, self_project), line
        )
    q_enc[...] = product(h_zero[...], enc_query[...]).astype(low)
    kv_enc[...] = contract_first(x_norm_t[...], enc_keyval[...]).astype(low)
    for g in range(n_head):
        keys = kv_enc[:, 2 * g * width : (2 * g + 1) * width]
        values = kv_enc[:, (2 * g + 1) * width : (2 * g + 2) * width]
        outcome = jnp.zeros((rows, width), jnp.float32)
        for here, q_head in head_lanes(g, heads, q_enc[...]):
            scores = enc_scores(q_head, keys)
            probs = jnp.exp(scores - jnp.max(scores, 1, keepdims=True))
            total = jnp.sum(probs, 1, keepdims=True)
            outcome = jnp.where(here, product(probs.astype(low), values) / total, outcome)
        o_enc[:, g * width : (g + 1) * width] = outcome.astype(low)
    z_one[...] = z_zero[...] + product(o_enc[...], enc_output[...])
    h_one[...] = layer_norm(z_one[...], gains[1:2, :]).astype(low)
    projected = product(h_one[...], self_project[...]).astype(low)
    for g in range(n_head):
        q_self[g] = projected[:, 3 * g * width : (3 * g + 1) * width]
        kv_self[g] = projected[:, (3 * g + 1) * width : (3 * g + 3) * width]


LINE = pltpu.VMEM((4, round_up(max(D, DI), 8), LANES), jnp.float32)


def shards_of(n_head, shard_rows, first, last):
    starts = borders(n_head)
    begin = starts[first] // shard_rows
    return begin, -(-starts[last] // shard_rows) - begin


def encode(lengths, weights, common, inputs_t, valid, rows, n_head, shard_rows):
    width = HEADS // n_head * HD
    begin, shards = shards_of(n_head, shard_rows, 0, 4)
    query_rows = DQ * D // LANES
    block, blocks = common_blocks(query_rows, query_rows + (LAT + 4) * D // LANES, valid)
    keys = inputs_t.shape[1]
    return pl.pallas_call(
        functools.partial(encode_kernel, n_head, shard_rows, valid, rows),
        out_shape=[
            shape_of((D, D)),
            shape_of((DI, 2 * D)),
            shape_of((D, D)),
            shape_of((D, 3 * D)),
            shape_of((4, D), jnp.float32),
            shape_of((rows, D), jnp.float32),
            shape_of((rows, D)),
            shape_of(inputs_t.shape),
            shape_of((rows, D)),
            shape_of((keys, 2 * D)),
            shape_of((rows, D)),
            shape_of((rows, D), jnp.float32),
            shape_of((rows, D)),
            shape_of((n_head, rows, width)),
            shape_of((n_head, rows, 2 * width)),
            shape_of((8, LANES), jnp.float32),
        ],
        in_specs=[SMEM_SPEC, ANY_SPEC, ANY_SPEC, VMEM_SPEC],
        out_specs=[VMEM_SPEC] * 16,
        scratch_shapes=[
            pltpu.VMEM((shards,) + weights.shape[1:], low),
            pltpu.VMEM((blocks,) + common.shape[1:], low),
            pltpu.VMEM(weights.shape[:2] + (TILE, LANES), low),
            pltpu.VMEM((shards * shard_rows, LANES), jnp.float32),
            pltpu.VMEM((blocks * valid, LANES), jnp.float32),
            LINE,
            pltpu.VMEM((LAT, D), low),
            pltpu.SemaphoreType.DMA((3,)),
        ],
        compiler_params=pltpu.CompilerParams(vmem_limit_bytes=56 * MIB),
        name="encode",
    )(lengths, weights, common, inputs_t)


def gelu_and_slope(x):
    rate = (2.0 / jnp.pi) ** 0.5
    cubic = 0.044715
    t = jnp.tanh(rate * (x + cubic * x * x * x))
    slope = 0.5 * (1.0 + t) + 0.5 * x * (1.0 - t * t) * rate * (1.0 + 3.0 * cubic * x * x)
    return 0.5 * x * (1.0 + t), slope


def my_column(marks, rows):
    turned = marks[...].astype(jnp.float32).T
    column = lax.broadcasted_iota(jnp.int32, turned.shape, 1)
    per_head = rows // LANES
    first = lax.axis_index("head") * per_head
    picked = [
        jnp.sum(jnp.where(column == first + k, turned, 0.0), 1, keepdims=True)
        for k in range(per_head)
    ]
    return jnp.concatenate(picked, 0) if per_head > 1 else picked[0]


def middle_kernel(
    n_head,
    shard_rows,
    valid,
    first_shard,
    rows,
    counts,
    weights,
    common,
    z_one,
    o_self,
    out_queries_t,
    labels,
    modality,
    labeled,
    gains,
    dout,
    d_two_out,
    tile,
    query_grad,
    gain_grads,
    grads,
    held,
    held_common,
    stage,
    stage_common,
    line,
    self_output,
    hidden_in,
    hidden_out,
    class_table,
    query_table,
    slope,
    activ,
    sems,
):
    heads = HEADS // n_head
    width, hidden, classes = heads * HD, FF // n_head, C // n_head
    shards = held.shape[0]
    first_row = first_shard * shard_rows
    starts = borders(n_head)
    copies = [
        pltpu.make_async_copy(common.at[pl.ds(0, held_common.shape[0])], held_common, sems.at[0]),
        pltpu.make_async_copy(weights.at[pl.ds(first_shard, shards)], held, sems.at[1]),
    ]
    for copy in copies:
        copy.start()
    copies[0].wait()
    load_common(stage_common, held_common, valid)
    for j, value in matrix_of(stage_common, 0, DQ, D, line):
        query_table[:, j : j + LANES] = value.astype(low)
    copies[1].wait()
    for g in range(n_head):
        load_stage(stage, held, first_shard, shard_rows, g)
        load_matrices(
            stage, first_row, n_head, g, (4, 5, 6, 7), (self_output, hidden_in, hidden_out, class_table), line
        )
    gain_two, gain_three = gains[2:3, :], gains[3:4, :]
    o_low = jnp.concatenate([o_self[g] for g in range(n_head)], 1)
    z_two = z_one[...] + product(o_low, self_output[...])
    h_two = layer_norm(z_two, gain_two).astype(low)
    value, bend = gelu_and_slope(product(h_two, hidden_in[...]))
    activ[...] = value.astype(low)
    slope[...] = bend
    z_three = z_two + product(activ[...], hidden_out[...])
    queries_t = out_queries_t[...]
    decoded = layer_norm(z_three, gain_three) + contract_first(queries_t, query_table[...])
    decoded = decoded.astype(low)
    logits = product(decoded, class_table[...])
    label, kind, counted = (my_column(marks, rows) for marks in (labels, modality, labeled))
    lane = lax.broadcasted_iota(jnp.int32, (rows, C), 1).astype(jnp.float32)
    is_target = jnp.where(lane == label, 1.0, 0.0)
    row_top = jnp.max(logits, 1, keepdims=True)
    row_lse = row_top + jnp.log(jnp.sum(jnp.exp(logits - row_top), 1, keepdims=True))
    loss = row_lse - jnp.sum(is_target * logits, 1, keepdims=True)
    weight = jnp.zeros((rows, 1), jnp.float32)
    place = lax.broadcasted_iota(jnp.int32, (1, LANES), 1)
    losses = jnp.zeros((1, LANES), jnp.float32)
    for m in range(MODES):
        member = jnp.where((kind == m) & (counted == 1.0), 1.0, 0.0)
        weight = weight + member / jnp.maximum(counts[0:1, m : m + 1], 1.0)
        losses = losses + jnp.where(place == m, jnp.sum(loss * member, 0, keepdims=True), 0.0)
    tile[...] = jnp.broadcast_to(losses, tile.shape)
    dlogits = (weight * (jnp.exp(logits - row_lse) - is_target)).astype(low)
    d_decoded = against(dlogits, class_table[...])
    matrix_into(query_grad, 0, product(queries_t, d_decoded.astype(low)), line)
    d_three, gain_three_grad = norm_pullback(z_three, gain_three, d_decoded)
    d_branch = d_three.astype(low)
    d_pre = (slope[...] * against(d_branch, hidden_out[...])).astype(low)
    d_middle, gain_two_grad = norm_pullback(z_two, gain_two, against(d_pre, hidden_in[...]))
    d_two = d_three + d_middle
    d_two_out[...] = d_two
    gain_grads[...] = jnp.concatenate([gain_two_grad, gain_three_grad], 0)
    d_two_low = d_two.astype(low)
    d_o = against(d_two_low, self_output[...]).astype(low)
    for g in range(n_head):
        dout[g] = d_o[:, g * width : (g + 1) * width]
    for g in range(n_head):
        results = (
            contract_first(o_self[g], d_two_low),
            contract_first(h_two, d_pre[:, g * hidden : (g + 1) * hidden]),
            contract_first(activ[:, g * hidden : (g + 1) * hidden], d_branch),
            contract_first(decoded, dlogits[:, g * classes : (g + 1) * classes]),
        )
        for m, result in zip((4, 5, 6, 7), results):
            matrix_into(stage, starts[m] - first_row, result, line)
        for b in range(shards):
            held[b, g, :shard_rows, :] = stage[pl.ds(b * shard_rows, shard_rows), :].astype(low)
    back = pltpu.make_async_copy(held, grads.at[pl.ds(first_shard, shards)], sems.at[2])
    back.start()
    back.wait()


def middle(counts, weights, common, z_one, o_self, out_queries_t, marks, gains, valid, n_head, shard_rows):
    rows = z_one.shape[0]
    begin, shards = shards_of(n_head, shard_rows, 4, 8)
    query_rows = DQ * D // LANES
    block, blocks = common_blocks(0, query_rows, valid)
    return pl.pallas_call(
        functools.partial(middle_kernel, n_head, shard_rows, valid, begin, rows),
        grid=(1,),
        out_shape=[
            shape_of(o_self.shape),
            shape_of((rows, D), jnp.float32),
            shape_of((8, LANES), jnp.float32),
            shape_of((query_rows, LANES), jnp.float32),
            shape_of((2, D), jnp.float32),
            shape_of(weights.shape),
        ],
        in_specs=[
            VMEM_SPEC,
            ANY_SPEC,
            ANY_SPEC,
            VMEM_SPEC,
            VMEM_SPEC,
            pl.BlockSpec((DQ, rows), lambda i: (0, lax.axis_index("head"))),
            VMEM_SPEC,
            VMEM_SPEC,
            VMEM_SPEC,
            VMEM_SPEC,
        ],
        out_specs=[VMEM_SPEC] * 5 + [ANY_SPEC],
        scratch_shapes=[
            pltpu.VMEM((shards,) + weights.shape[1:], low),
            pltpu.VMEM((blocks,) + common.shape[1:], low),
            pltpu.VMEM((shards * shard_rows, LANES), jnp.float32),
            pltpu.VMEM((blocks * valid, LANES), jnp.float32),
            LINE,
            pltpu.VMEM((D, D), low),
            pltpu.VMEM((D, FF), low),
            pltpu.VMEM((FF, D), low),
            pltpu.VMEM((D, C), low),
            pltpu.VMEM((DQ, D), low),
            pltpu.VMEM((rows, FF), jnp.float32),
            pltpu.VMEM((rows, FF), low),
            pltpu.SemaphoreType.DMA((3,)),
        ],
        compiler_params=pltpu.CompilerParams(vmem_limit_bytes=56 * MIB),
        name="middle",
    )(counts, weights, common, z_one, o_self, out_queries_t, *marks, gains)


def ending_kernel(
    n_head,
    shard_rows,
    valid,
    rows,
    lengths,
    grads_in,
    d_q_self,
    d_kv_self,
    d_two,
    gains,
    gain_grads,
    query_grad,
    enc_query,
    enc_keyval,
    enc_output,
    self_project,
    z_zero,
    h_zero,
    x_norm_t,
    q_enc,
    kv_enc,
    o_enc,
    z_one,
    h_one,
    grads,
    common_grad,
    held,
    stage,
    stage_common,
    line,
    d_q,
    d_kv,
    sems,
):
    heads = HEADS // n_head
    width = heads * HD
    shards = held.shape[0]
    starts = borders(n_head)
    shared = pltpu.make_async_copy(grads_in.at[pl.ds(shards - 1, 1)], held.at[pl.ds(shards - 1, 1)], sems.at[0])
    shared.start()
    d_projected = [jnp.concatenate([d_q_self[g], d_kv_self[g]], 1) for g in range(n_head)]
    whole = jnp.concatenate(d_projected, 1)
    d_middle, gain_one_grad = norm_pullback(
        z_one[...], gains[1:2, :], against(whole, self_project[...])
    )
    d_one = d_two[...] + d_middle
    d_one_low = d_one.astype(low)
    d_o = against(d_one_low, enc_output[...]).astype(low)
    for g in range(n_head):
        keys = kv_enc[:, 2 * g * width : (2 * g + 1) * width]
        values = kv_enc[:, (2 * g + 1) * width : (2 * g + 2) * width]
        d_key = jnp.zeros(keys.shape, jnp.float32)
        d_value = jnp.zeros(keys.shape, jnp.float32)
        d_query = jnp.zeros((rows, width), jnp.float32)
        for (here, q_head), (unused, do_head) in zip(
            head_lanes(g, heads, q_enc[...]), head_lanes(g, heads, d_o)
        ):
            scores = enc_scores(keys, q_head)
            probs = jnp.exp(scores - jnp.max(scores, 0, keepdims=True))
            probs = probs / jnp.sum(probs, 0, keepdims=True)
            d_probs = against(values, do_head)
            delta = jnp.sum(probs * d_probs, 0, keepdims=True)
            d_scores = (probs * (d_probs - delta)).astype(low)
            d_value = d_value + product(probs.astype(low), do_head)
            d_key = d_key + product(d_scores, q_head)
            d_query = jnp.where(here, contract_first(d_scores, keys), d_query)
        d_q[:, g * width : (g + 1) * width] = (d_query * HD ** (-0.5)).astype(low)
        d_kv[:, 2 * g * width : (2 * g + 1) * width] = (d_key * HD ** (-0.5)).astype(low)
        d_kv[:, (2 * g + 1) * width : (2 * g + 2) * width] = d_value.astype(low)
    d_middle, gain_zero_grad = norm_pullback(
        z_zero[...], gains[0:1, :], against(d_q[...], enc_query[...])
    )
    d_zero = d_one + d_middle
    d_zero_top = d_zero.astype(low)
    d_zero_rest = (d_zero - d_zero_top.astype(jnp.float32)).astype(low)
    picked = picked_rows(clip_bounds(lengths), rows, n_head)
    latent_grad = contract_first(picked, d_zero_top) + contract_first(picked, d_zero_rest)
    query_rows = query_grad.shape[0]
    stage_common[:query_rows] = query_grad[...]
    matrix_into(stage_common, query_rows, latent_grad, line)
    all_gains = jnp.concatenate([gain_zero_grad, gain_one_grad, gain_grads[...]], 0)
    matrix_into(stage_common, query_rows + LAT * D // LANES, all_gains, line)
    piece = common_grad.shape[2]
    for b in range(common_grad.shape[0]):
        for k in range(common_grad.shape[1]):
            amount = min(piece, valid - k * piece)
            block = stage_common[b * valid + k * piece : b * valid + k * piece + amount, :]
            if amount < piece:
                block = jnp.concatenate([block, jnp.zeros((piece - amount, LANES), jnp.float32)], 0)
            common_grad[b, k] = block.astype(low)
    shared.wait()
    kept = shards * shard_rows - starts[4]
    for g in range(n_head):
        results = (
            contract_first(h_zero[...], d_q[:, g * width : (g + 1) * width]),
            product(x_norm_t[...], d_kv[:, 2 * g * width : (2 * g + 2) * width]),
            contract_first(o_enc[:, g * width : (g + 1) * width], d_one_low),
            contract_first(h_one[...], d_projected[g]),
        )
        if kept:
            stage[pl.ds((shards - 1) * shard_rows, shard_rows), :] = held[
                shards - 1, g, :shard_rows, :
            ].astype(jnp.float32)
        for m, result in zip((0, 1, 2, 3), results):
            matrix_into(stage, starts[m], result, line)
        for b in range(shards):
            held[b, g, :shard_rows, :] = stage[pl.ds(b * shard_rows, shard_rows), :].astype(low)
    back = pltpu.make_async_copy(held, grads.at[pl.ds(0, shards)], sems.at[1])
    back.start()
    back.wait()


def ending(lengths, grads, d_self, d_two, gains, gain_grads, query_grad, kept, common_shape, valid, shard_rows):
    rows = d_two.shape[0]
    n_head = grads.shape[1]
    begin, shards = shards_of(n_head, shard_rows, 0, 4)
    keys = kept[6].shape[1]
    common_rows = (DQ + LAT + 4) * D // LANES
    return pl.pallas_call(
        functools.partial(ending_kernel, n_head, shard_rows, valid, rows),
        out_shape=[shape_of(grads.shape), shape_of(common_shape)],
        in_specs=[SMEM_SPEC, ANY_SPEC] + [VMEM_SPEC] * 18,
        out_specs=[ANY_SPEC, VMEM_SPEC],
        input_output_aliases={1: 0},
        scratch_shapes=[
            pltpu.VMEM((shards,) + grads.shape[1:], low),
            pltpu.VMEM((shards * shard_rows, LANES), jnp.float32),
            pltpu.VMEM((common_rows, LANES), jnp.float32),
            LINE,
            pltpu.VMEM((rows, D), low),
            pltpu.VMEM((keys, 2 * D), low),
            pltpu.SemaphoreType.DMA((2,)),
        ],
        compiler_params=pltpu.CompilerParams(vmem_limit_bytes=56 * MIB),
        name="ending",
    )(lengths, grads, *d_self, d_two, gains, gain_grads, query_grad, *kept)


def adam_step(weight, first, second, grad):
    first = beta_one * first + (1 - beta_one) * grad
    second = beta_two * second + (1 - beta_two) * grad * grad
    fixed_first = first / (1 - beta_one**STEP)
    fixed_second = second / (1 - beta_two**STEP)
    weight = weight - learn_rate * (
        fixed_first / (jnp.sqrt(fixed_second) + adam_eps) + weight_decay * weight
    )
    return (weight, first, second, weight.astype(low))


def per_device(
    inputs,
    out_queries,
    clip_lengths,
    labels,
    modality,
    labeled,
    head_params,
    head_first,
    head_second,
    common_params,
    common_first,
    common_second,
):
    n_head, n_blk = lax.axis_size("head"), lax.axis_size("blk")
    dims = grid_of(n_blk, n_head)
    rows = labels.shape[0] // n_head
    heads_here = HEADS // n_head
    n_h, n_c = head_params.shape[0], common_params.shape[0]
    shard_rows, common_rows = n_h // LANES, -(-n_c // LANES)
    head_rows = round_up(shard_rows + 1, TILE)
    piece_rows = round_up(-(-common_rows // n_head), TILE)
    marks = [x.reshape(-1, LANES) for x in (labels, modality, labeled)]
    head_wide = head_params.reshape(shard_rows, LANES)
    common_wide = jnp.pad(common_params, (0, common_rows * LANES - n_c)).reshape(common_rows, LANES)
    weights, common = gather_all(dims, marks, (head_wide, common_wide), (head_rows, piece_rows), 0)
    valid = common_rows
    if n_c % LANES:
        common = common.reshape(n_blk, -1)[:, :n_c].reshape(-1, LANES)
        valid = common.shape[0]
        common = jnp.pad(common, ((0, -valid % TILE), (0, 0)))[None, None]

    encoded = encode(clip_lengths, weights, common, inputs.T, valid, rows, n_head, shard_rows)
    gains, z_one, counts = encoded[4], encoded[11], encoded[15]
    o_self, lse_self, out_self_t, q_all, kv_all = attend(
        dims, clip_lengths, encoded[13], encoded[14], heads_here, 1
    )
    dout, d_two, tile, query_grad, gain_grads, grads = middle(
        counts, weights, common, z_one, o_self, out_queries.T, marks, gains, valid, n_head, shard_rows
    )
    d_self = attend_back(dims, clip_lengths, q_all, kv_all, dout, out_self_t, lse_self, heads_here, 2)
    kept = encoded[:4] + encoded[5:13]
    grads, common_grad = ending(
        clip_lengths,
        grads,
        d_self,
        d_two,
        gains,
        gain_grads,
        query_grad,
        kept,
        common.shape,
        valid,
        shard_rows,
    )
    if n_c % LANES:
        common_grad = common_grad[0, 0, :valid].reshape(n_blk, n_c)
        common_grad = jnp.pad(common_grad, ((0, 0), (0, n_head * piece_rows * LANES - n_c)))
        common_grad = common_grad.reshape(n_blk, n_head, piece_rows, LANES)
    head_share, common_share, totals = reduce_all(
        dims, (grads, common_grad), (shard_rows, common_rows), tile, 3
    )
    label_counts, loss_sums = counts[0, :MODES], totals[0, :MODES]
    clip_norm = jnp.sqrt(totals[0, MODES])
    factor = jnp.minimum(1.0, clip_limit / clip_norm)
    head_share, common_share = head_share.reshape(-1), common_share.reshape(-1)[:n_c]
    head_out = adam_step(head_params, head_first, head_second, head_share * factor)
    common_out = adam_step(common_params, common_first, common_second, common_share * factor)
    return head_out + common_out + (loss_sums, label_counts, clip_norm)


def solution(mesh):
    placed = (
        P("blk", None),
        P("blk", None),
        P(),
        P("blk"),
        P("blk"),
        P("blk"),
        P(("head", "blk")),
        P(("head", "blk")),
        P(("head", "blk")),
        P("blk"),
        P("blk"),
        P("blk"),
    )
    return jax.shard_map(
        per_device,
        mesh=mesh,
        in_specs=placed,
        out_specs=(
            P(("head", "blk")),
            P(("head", "blk")),
            P(("head", "blk")),
            P(("head", "blk")),
            P("blk"),
            P("blk"),
            P("blk"),
            P("blk"),
            P(),
            P(),
            P(),
        ),
        check_vma=False,
    )
```

```python
import functools

import jax
import jax.numpy as jnp
from jax import lax
from jax.experimental import pallas as pl
from jax.experimental.pallas import tpu as pltpu
from jax.sharding import PartitionSpec as P

D = 512
HEADS = 8
HD = 64
FF = 2048
DI = 704
DQ = 1026
C = 704
LAT = 784
MODES = 3
STEP = 10
LANES = 128
TILE = 16

norm_eps = 1e-05
learn_rate = 0.1
beta_one = 0.9
beta_two = 0.999
adam_eps = 1e-08
weight_decay = 0.01
clip_limit = 0.05
big_negative = -1e30
low = jnp.bfloat16
MESH = pl.DeviceIdType.MESH
MIB = 1 << 20
VMEM_SPEC = pl.BlockSpec(memory_space=pltpu.VMEM)
SMEM_SPEC = pl.BlockSpec(memory_space=pltpu.SMEM)
ANY_SPEC = pl.BlockSpec(memory_space=pl.ANY)


def shape_of(shape, dtype=low):
    return jax.ShapeDtypeStruct(shape, dtype)


def round_up(n, unit):
    return -(-n // unit) * unit


def grid_of(n_blk, n_head):
    cores = 2 if n_head % 2 == 0 else 1
    x = n_head // cores
    y = x if n_blk % x == 0 else 1
    return (n_blk // y, y, x, cores)


def my_place(dims):
    blk, head = lax.axis_index("blk"), lax.axis_index("head")
    return (blk // dims[1], lax.rem(blk, dims[1]), head // dims[3], lax.rem(head, dims[3]))


def shifted(dims, me, offset, sign):
    return tuple(
        m if o == 0 else lax.rem(m + (o if sign > 0 else n - o), n)
        for m, o, n in zip(me, offset, dims)
    )


def blk_of(dims, place):
    return place[0] * dims[1] + place[1]


def head_of(dims, place):
    return place[2] * dims[3] + place[3]


def device_of(dims, place):
    return {"blk": blk_of(dims, place), "head": head_of(dims, place)}


def along(axis, d):
    return tuple(d if a == axis else 0 for a in range(4))


def greet(dims, me, offsets):
    barrier = pltpu.get_barrier_semaphore()
    for offset in offsets:
        pl.semaphore_signal(
            barrier,
            inc=1,
            device_id=device_of(dims, shifted(dims, me, offset, 1)),
            device_id_type=MESH,
        )
    pl.semaphore_wait(barrier, len(offsets))


def axis_peers(dims, axes):
    return [along(axis, d) for axis in axes for d in range(1, dims[axis])]


def remote(src, dst, send_sem, recv_sem, place, dims):
    return pltpu.make_async_remote_copy(
        src_ref=src,
        dst_ref=dst,
        send_sem=send_sem,
        recv_sem=recv_sem,
        device_id=device_of(dims, place),
        device_id_type=MESH,
    )


AHEAD = 6.0
RING = 0


def in_order(first, follow, size_of, ahead, result):
    queues, busy, flight = {}, {}, {}
    now = 0.0

    def ready(messages):
        for message in messages:
            queues.setdefault(message[1], []).append(message)

    ready(first)
    while True:
        for axis in sorted(queues):
            queue, going = queues[axis], flight.setdefault(axis, [])
            while queue and (not going or busy[axis] < now + ahead):
                message = min(queue)
                queue.remove(message)
                busy[axis] = max(now, busy.get(axis, 0.0)) + size_of(message)
                going.append((busy[axis] + 1.5, message))
                result.append((True, message))
        arrivals = [min(going) for going in flight.values() if going]
        if not arrivals:
            return now
        arrival = min(arrivals)
        flight[arrival[1][1]].remove(arrival)
        now = max(now, arrival[0])
        result.append((False, arrival[1]))
        ready(follow(arrival[1]))


def time_of(rows, axis):
    return rows * LANES * 2 / (300e3 if axis == 3 else 45e3)


def with_at(offset, axis, d):
    return offset[:axis] + (d,) + offset[axis + 1 :]


def gather_order(dims, parts):
    def onward(p, offset, position):
        order = parts[p][3]
        result = []
        for k in range(max(position, 0), 4):
            axis = order[k]
            n = dims[axis]
            if k > position:
                steps = [1] if axis == RING else range(1, n)
                steps = [d for d in steps if d < n]
            else:
                steps = [offset[axis] + 1] if axis == RING and offset[axis] + 1 < n else []
            for d in steps:
                result.append(((k, sum(offset), p), axis, p, with_at(offset, axis, d)))
        return result

    def follow(message):
        rank, axis, p, offset = message
        return onward(p, offset, rank[0])

    first = [m for p in range(len(parts)) for m in onward(p, (0, 0, 0, 0), -1)]
    result = []
    now = in_order(first, follow, lambda m: time_of(parts[m[2]][2], m[1]), AHEAD, result)
    return result, now


def gather_kernel(
    dims,
    parts,
    labels,
    modality,
    labeled,
    head_params,
    common_params,
    head_all,
    common_all,
    head_low,
    common_low,
    common_wide,
    send_sem,
    recv_sem,
    own_sem,
):
    me = my_place(dims)
    my_head = head_of(dims, me)
    n_head = dims[2] * dims[3]
    shard_rows, common_rows = head_params.shape[0], common_params.shape[0]
    per_head = labels.shape[0] // n_head
    row = lax.broadcasted_iota(jnp.int32, labels.shape, 0)
    mine = (row >= my_head * per_head) & (row < (my_head + 1) * per_head) & (labeled[...] == 1)
    lane = lax.broadcasted_iota(jnp.int32, (1, LANES), 1)
    counts = jnp.zeros((1, LANES), jnp.float32)
    for m in range(MODES):
        member = jnp.where(mine & (modality[...] == m), 1.0, 0.0)
        counts = counts + jnp.where(lane == m, jnp.sum(member, (0, 1), keepdims=True), 0.0)
    padding = head_low.shape[0] - shard_rows
    tail = shard_rows // TILE * TILE
    head_low[:tail] = head_params[:tail].astype(low)
    last = [jnp.broadcast_to(counts, (padding, LANES))]
    if shard_rows > tail:
        last = [head_params[tail:]] + last
    head_low[tail:] = jnp.concatenate(last, 0).astype(low)
    common_wide[...] = jnp.zeros(common_wide.shape, jnp.float32)
    common_wide[:common_rows] = common_params[...]
    piece = common_low.shape[0]
    common_low[...] = common_wide[pl.ds(pl.multiple_of(my_head * piece, TILE), piece)].astype(low)

    greet(dims, me, ring_and_others(dims))
    srcs, outs = (head_low, common_low), (head_all, common_all)
    copies = {}

    def block(p, offset):
        place = shifted(dims, me, offset, -1)
        array, first, rows, order = parts[p]
        return outs[array].at[blk_of(dims, place), head_of(dims, place), pl.ds(first, rows)]

    own = []
    for is_send, (rank, axis, p, offset) in gather_order(dims, parts)[0]:
        if is_send:
            step = 1 if axis == RING else offset[axis]
            before = with_at(offset, axis, offset[axis] - step)
            array, first, rows, order = parts[p]
            source = block(p, before) if any(before) else srcs[array].at[pl.ds(first, rows)]
            i = len(copies)
            copies[(p, offset)] = remote(
                source,
                block(p, before),
                send_sem.at[i],
                recv_sem.at[i],
                shifted(dims, me, along(axis, step), 1),
                dims,
            )
            copies[(p, offset)].start()
        else:
            if not own:
                for array in range(2):
                    copy = pltpu.make_async_copy(
                        srcs[array], outs[array].at[blk_of(dims, me), my_head], own_sem.at[array]
                    )
                    copy.start()
                    own.append(copy)
            copies[(p, offset)].wait_recv()
    for copy in copies.values():
        copy.wait_send()
    for copy in own:
        copy.wait()


def ring_and_others(dims):
    ring = {along(RING, 1 % dims[RING]), along(RING, (dims[RING] - 1) % dims[RING])}
    return sorted(ring - {(0, 0, 0, 0)}) + axis_peers(dims, (1, 2, 3))


def cut(array, rows, shares):
    result = []
    first, so_far = 0, 0
    whole = sum(share for share, order in shares)
    for share, order in shares:
        so_far += share
        end = rows * so_far // whole // TILE * TILE if so_far < whole else rows
        if end > first:
            result.append((array, first, end - first, order))
        first = end
    return tuple(result)


ZYXC, ZXYC, YXZC, XYZC = (0, 1, 2, 3), (0, 2, 1, 3), (1, 2, 0, 3), (2, 1, 0, 3)
GATHER_SHARES = ((8, ZYXC), (6, ZXYC), (2, YXZC), (2, XYZC))
REDUCE_SHARES = ((7, ZYXC), (7, ZXYC), (2, YXZC), (2, XYZC))


def gather_all(dims, marks, params, rows, collective_id):
    z, y, x, cores = dims
    parts = cut(0, rows[0], GATHER_SHARES) + cut(1, rows[1], ((1, ZXYC),))
    count = len(parts) * (z * y * x * cores - 1)
    return pl.pallas_call(
        functools.partial(gather_kernel, dims, parts),
        out_shape=[shape_of((z * y, x * cores, n, LANES)) for n in rows],
        in_specs=[VMEM_SPEC] * 5,
        out_specs=[ANY_SPEC] * 2,
        scratch_shapes=[pltpu.VMEM((n, LANES), low) for n in rows]
        + [
            pltpu.VMEM((x * cores * rows[1], LANES), jnp.float32),
            pltpu.SemaphoreType.DMA((count,)),
            pltpu.SemaphoreType.DMA((count,)),
            pltpu.SemaphoreType.DMA((2,)),
        ],
        compiler_params=pltpu.CompilerParams(collective_id=collective_id, has_side_effects=True),
        name="gather_weights",
    )(*marks, *params)


def reduce_order(dims, parts):
    ready, arrived, order = set(), set(), []

    def message(p, position, offset):
        z = offset[RING]
        rank = (dims[RING] - z if z else dims[RING], position, tuple(-o for o in offset), p)
        return (rank, parts[p][3][position], p, position, offset)

    def done(p, position, offset):
        ready.add((p, position, offset))
        if position == 4:
            return []
        axis = parts[p][3][position]
        d = offset[axis]
        first = d != 0 and (axis != RING or d == dims[axis] - 1)
        return ([message(p, position, offset)] if first else []) + advance(p, position, offset)

    def advance(p, position, offset):
        axis = parts[p][3][position]
        n = dims[axis]
        start = with_at(offset, axis, 0)
        if axis == RING:
            here = (p, position, offset)
            if here in ready and here in arrived:
                order.append((None, here))
                if offset[axis]:
                    return [message(p, position, offset)]
                return done(p, position + 1, offset)
        elif (p, position, start) in ready and (p, position + 1, start) not in ready:
            if all((p, position, with_at(start, axis, d)) in arrived for d in range(1, n)):
                order.append((None, (p, position, start)))
                return done(p, position + 1, start)
        return []

    def follow(sent):
        rank, axis, p, position, offset = sent
        here = with_at(offset, axis, offset[axis] - 1) if axis == RING else offset
        arrived.add((p, position, here))
        return advance(p, position, here)

    first = []
    for p in range(len(parts)):
        for offset in all_offsets(dims, range(4)):
            first += done(p, 0, offset)
    now = in_order(first, follow, lambda m: time_of(parts[m[2]][2], m[1]), AHEAD, order)
    return order, now


def all_offsets(dims, axes):
    offsets = [(0, 0, 0, 0)]
    for a in axes:
        offsets = [with_at(o, a, d) for o in offsets for d in range(dims[a])]
    return offsets


def reduce_kernel(dims, parts, *refs):
    srcs, tile = refs[:2], refs[2]
    head_out, common_out, totals = refs[3:6]
    places = len(parts) * 4
    buffers = refs[6 : 6 + places]
    head_sum, common_sum, shares, send_sem, recv_sem, near_tiles, far_tiles = refs[6 + places :]
    sums = (head_sum, common_sum)
    me = my_place(dims)
    z, y, x, cores = dims
    across = peers_across(dims)
    others = [o for o in all_offsets(dims, (0, 1)) if any(o)]
    met = ring_and_others(dims)
    greet(dims, me, met + [o for o in across + others if o not in met])
    push = Pushes(dims, me, send_sem, recv_sem)
    copies = {}

    def slot(p, position, offset):
        order = parts[p][3]
        axis = order[position]
        rest = [o for o in all_offsets(dims, order[position + 1 :])]
        k = rest.index(with_at(offset, axis, 0))
        return buffers[p * 4 + position].at[k, max(offset[axis] - 1, 0)]

    def summed(p, position, offset):
        array, first, rows, order = parts[p]
        if position == 0:
            place = shifted(dims, me, offset, 1)
            return srcs[array].at[blk_of(dims, place), head_of(dims, place), pl.ds(first, rows)]
        return slot(p, position - 1, offset)

    def ring_slot(p, position, offset):
        axis = parts[p][3][position]
        return slot(p, position, with_at(offset, axis, offset[axis] + 1))

    def add(p, position, offset):
        array, first, rows, order = parts[p]
        axis = order[position]
        if axis == RING:
            arrivals = [ring_slot(p, position, offset)]
        else:
            arrivals = [slot(p, position, with_at(offset, axis, d)) for d in range(1, dims[axis])]
        mine = summed(p, position, offset)
        step = row_chunk(rows)

        @pl.loop(0, rows // step)
        def some_rows(n):
            at = pl.ds(pl.multiple_of(n * step, step), step)
            total = mine[at].astype(jnp.float32)
            for arrival in arrivals:
                total = total + arrival[at].astype(jnp.float32)
            if position == 3 and not any(offset):
                sums[array][pl.ds(pl.multiple_of(first + n * step, TILE), step)] = total
            else:
                arrivals[0][at] = total.astype(low)

    for is_send, what in reduce_order(dims, parts)[0]:
        if is_send is None:
            add(*what)
        elif is_send:
            rank, axis, p, position, offset = what
            d = offset[axis]
            started = axis != RING or d == dims[axis] - 1
            source = summed(p, position, offset) if started else ring_slot(p, position, offset)
            step = along(axis, 1 if axis == RING else d)
            copies[what] = push(source, slot(p, position, offset), step)
        else:
            copies[what].wait_recv()
    my_head, my_blk = head_of(dims, me), blk_of(dims, me)
    shares[my_head] = common_sum[...].astype(low)
    share_copies = [push(shares.at[my_head], shares.at[my_head], o) for o in across]
    amount = head_out.shape[0]
    head_out[...] = head_sum[:amount]
    squares = jnp.sum(head_sum[:amount] * head_sum[:amount], 0, keepdims=True)
    squares = squares + jnp.sum(common_sum[...] * common_sum[...], 0, keepdims=True)
    lane = lax.broadcasted_iota(jnp.int32, (1, LANES), 1)
    near_tiles[my_head] = tile[...] + jnp.where(
        lane == MODES, jnp.sum(squares, 1, keepdims=True), 0.0
    )
    near = [push(near_tiles.at[my_head], near_tiles.at[my_head], o) for o in across]
    for copy in near:
        copy.wait_recv()
    far_tiles[my_blk] = jnp.sum(near_tiles[...], 0)
    far = [push(far_tiles.at[my_blk], far_tiles.at[my_blk], o) for o in others]
    for copy in share_copies:
        copy.wait_recv()
    piece = shares.shape[1]
    for k in range(x * cores):
        amount = min(piece, common_out.shape[0] - k * piece)
        common_out[k * piece : k * piece + amount] = shares[k].astype(jnp.float32)[:amount]
    for copy in far:
        copy.wait_recv()
    totals[...] = jnp.sum(far_tiles[...], 0)
    push.finish()


def row_chunk(rows):
    for count in (4, 3, 2):
        if rows % (count * TILE) == 0:
            return rows // count
    return rows


def reduce_all(dims, arrays, valid, tile, collective_id):
    z, y, x, cores = dims
    rows = [array.shape[2] for array in arrays]
    parts = cut(0, rows[0], [(share, order[::-1]) for share, order in REDUCE_SHARES])
    parts = parts + cut(1, rows[1], ((1, ZXYC[::-1]),))
    scratch = []
    for array, first, amount, order in parts:
        for position, axis in enumerate(order):
            rest = len(all_offsets(dims, order[position + 1 :]))
            scratch.append(pltpu.VMEM((rest, dims[axis] - 1, amount, LANES), low))
    count = len(parts) * (z * y * x * cores - 1) + 2 * (x * cores - 1) + z * y - 1
    return pl.pallas_call(
        functools.partial(reduce_kernel, dims, parts),
        out_shape=[
            shape_of((valid[0], LANES), jnp.float32),
            shape_of((valid[1], LANES), jnp.float32),
            shape_of((8, LANES), jnp.float32),
        ],
        in_specs=[VMEM_SPEC] * 3,
        out_specs=[VMEM_SPEC] * 3,
        scratch_shapes=scratch
        + [pltpu.VMEM((n, LANES), jnp.float32) for n in rows]
        + [
            pltpu.VMEM((x * cores, rows[1], LANES), low),
            pltpu.SemaphoreType.DMA((count,)),
            pltpu.SemaphoreType.DMA((count,)),
            pltpu.VMEM((x * cores, 8, LANES), jnp.float32),
            pltpu.VMEM((z * y, 8, LANES), jnp.float32),
        ],
        compiler_params=pltpu.CompilerParams(
            collective_id=collective_id, has_side_effects=True, vmem_limit_bytes=60 * MIB
        ),
        name="reduce_gradients",
    )(*arrays, tile)


def contract_first(a, b):
    return lax.dot_general(a, b, (((0,), (0,)), ((), ())), preferred_element_type=jnp.float32)


def product(a, b):
    return jnp.dot(a, b, preferred_element_type=jnp.float32)


def against(a, b):
    return lax.dot_general(a, b, (((1,), (1,)), ((), ())), preferred_element_type=jnp.float32)


def clip_bounds(lengths):
    result, first = [], 0
    for clip in range(lengths.shape[0]):
        end = first + lengths[clip]
        result.append((first, end))
        first = end
    return result


def clip_borders(bounds, place):
    opening = jnp.zeros(place.shape, jnp.int32)
    ending = jnp.full(place.shape, 1 << 30, jnp.int32)
    for clip, (begin, end) in enumerate(bounds):
        here = place == clip
        opening = jnp.where(here, begin, opening)
        ending = jnp.where(here, end, ending)
    return opening, ending


def low_half(axis):
    return lax.broadcasted_iota(jnp.int32, (1, LANES) if axis else (LANES, 1), axis) < HD


def with_key_tail(bounds, first_row, kv):
    clips = len(bounds)
    place = lax.broadcasted_iota(jnp.int32, (1, LANES), 1) - HD
    opening, ending = clip_borders(bounds, place)
    ones = jnp.where((place >= clips) & (place < clips + 3), 1.0, 0.0)
    row = first_row + lax.broadcasted_iota(jnp.int32, kv.shape, 0)
    tail = jnp.where((row >= opening) & (row < ending), ones, big_negative)
    return jnp.where(low_half(1), kv.astype(jnp.float32), tail).astype(low)


def with_value_tail(kv):
    place = lax.broadcasted_iota(jnp.int32, (1, LANES), 1)
    ones = jnp.where(place < 3, 1.0, 0.0)
    return jnp.where(low_half(1), ones, kv.astype(jnp.float32)).astype(low)


def in_three(place, value):
    top = value.astype(low).astype(jnp.float32)
    middle = (value - top).astype(low).astype(jnp.float32)
    bottom = value - top - middle
    return (
        jnp.where(place == 0, top, 0.0)
        + jnp.where(place == 1, middle, 0.0)
        + jnp.where(place == 2, bottom, 0.0)
    )


def with_query_tail(bounds, first_row, rows, extra):
    clips = len(bounds)
    place = lax.broadcasted_iota(jnp.int32, (HD, 1), 0)
    opening, ending = clip_borders(bounds, place)
    row = first_row + lax.broadcasted_iota(jnp.int32, (1, rows.shape[1]), 1)
    inside = (place < clips) & (row >= opening) & (row < ending)
    tail = jnp.where(inside, 1.0, 0.0)
    if extra is not None:
        tail = tail + in_three(place - clips, -extra)
    return jnp.concatenate([rows * HD ** (-0.5), tail], 0).astype(low)


def pack(rows):
    half = rows.shape[0] // 2
    return jnp.concatenate([rows[:half], rows[half:]], 1)


def unpack(packed):
    return jnp.concatenate([packed[:, :HD], packed[:, HD:]], 0)


def unpack_t(packed):
    turned = packed.astype(jnp.float32).T
    return jnp.concatenate([turned[:HD], turned[HD:]], 1)


def pack_t(columns):
    half = columns.shape[1] // 2
    return jnp.concatenate([columns[:, :half], columns[:, half:]], 0).T


class Team:
    def __init__(self, dims):
        z, y, x, cores = dims
        self.dims = dims
        self.wide = HEADS // (x * cores) == y
        self.size = x * cores * (y if self.wide else 1)
        self.groups = z if self.wide else z * y
        axes = (1, 2, 3) if self.wide else (2, 3)
        offsets = [o for o in all_offsets(dims, axes) if any(o)]
        self.others = sorted(offsets, key=lambda o: (o[1] + o[2], o))
        self.sides = [] if self.wide else axis_peers(dims, (1,))

    def slot(self, place):
        head = head_of(self.dims, place)
        return place[1] * self.dims[2] * self.dims[3] + head if self.wide else head

    def group(self, place):
        return place[0] if self.wide else blk_of(self.dims, place)


def heads_of(n_head, slots):
    return [(s % n_head, s // n_head) for s in range(slots)]


class Pushes:
    def __init__(self, dims, me, send_sem, recv_sem):
        self.dims, self.me, self.send_sem, self.recv_sem = dims, me, send_sem, recv_sem
        self.started = []

    def __call__(self, src, dst, offset):
        i = len(self.started)
        place = shifted(self.dims, self.me, offset, 1)
        copy = remote(src, dst, self.send_sem.at[i], self.recv_sem.at[i], place, self.dims)
        copy.start()
        self.started.append(copy)
        return copy

    def finish(self):
        for copy in self.started:
            copy.wait_send()


def peers_across(dims):
    z, y, x, cores = dims
    across = [(0, 0, a, c) for a in range(x) for c in range(cores) if (a, c) != (0, 0)]
    return sorted(across, key=lambda o: (o[2] == 0, o[3]))


def attend_kernel(
    team,
    query_step,
    key_step,
    lengths,
    q_in,
    kv_in,
    o_out,
    lse,
    out_t,
    q_all,
    kv_all,
    keys,
    values_t,
    queries,
    top,
    accum,
    o_mine,
    send_sem,
    recv_sem,
    own_sem,
):
    dims = team.dims
    z = dims[0]
    me = my_place(dims)
    bounds = clip_bounds(lengths)
    rows = kv_in.shape[1]
    amount = team.size * rows
    my_group, my_slot = team.group(me), team.slot(me)
    ring_ends = sorted({along(0, 1 % z), along(0, (z - 1) % z)} - {(0, 0, 0, 0)})
    greet(dims, me, team.others + ring_ends + team.sides)
    push = Pushes(dims, me, send_sem, recv_sem)
    own_kv = pltpu.make_async_copy(kv_in.at[my_slot], kv_all.at[my_group, my_slot], own_sem.at[0])
    own_q = pltpu.make_async_copy(q_in.at[my_slot], q_all.at[my_slot], own_sem.at[1])
    own_kv.start()
    own_q.start()

    def to_team(src, dst, o):
        return push(src.at[team.slot(shifted(dims, me, o, 1))], dst, o)

    kv_copies = {o: to_team(kv_in, kv_all.at[my_group, my_slot], o) for o in team.others}
    q_copies = [to_team(q_in, q_all.at[my_slot], o) for o in team.others]
    ring, side = {}, {}

    def group_at(offset):
        return team.group(shifted(dims, me, offset, -1))

    def send_piece(o):
        block = kv_all.at[my_group, team.slot(shifted(dims, me, o, -1))]
        if z > 1:
            ring.setdefault(1, []).append(push(block, block, along(0, 1)))

    def send_on(s):
        block = kv_all.at[group_at(along(0, s))]
        if 0 < s < z - 1:
            ring[s + 1] = [push(block, block, along(0, 1))]
        for o in team.sides:
            side[(s, o)] = push(block, block, o)

    def compute(offset):
        group = group_at(offset)

        @pl.loop(0, team.size)
        def build(n):
            at = pl.ds(pl.multiple_of(n * rows, rows), rows)
            block = kv_all[group, n]
            keys[at, :] = with_key_tail(bounds, group * amount + n * rows, block)
            values_t[:HD, at] = block.astype(jnp.float32).T[HD:].astype(low)

        @pl.loop(0, amount // (2 * query_step))
        def query_blocks(n):
            for half in range(2):
                at = pl.ds(pl.multiple_of((2 * n + half) * query_step, query_step), query_step)
                query = queries[:, at]
                old, total = top[:, at], accum[:, at]
                for k in range(0, amount, key_step):
                    scores = product(keys[k : k + key_step, :], query)
                    new = jnp.maximum(old, jnp.max(scores, 0, keepdims=True))
                    probs = jnp.exp(scores - new).astype(low)
                    total = total * jnp.exp(old - new) + product(values_t[:, k : k + key_step], probs)
                    old = new
                top[:, at] = old
                accum[:, at] = total

    values_t[HD:, :] = jnp.ones((TILE, amount), low)
    top[...] = jnp.full(top.shape, -1e38, jnp.float32)
    accum[...] = jnp.zeros(accum.shape, jnp.float32)
    own_kv.wait()
    send_piece((0, 0, 0, 0))
    for o in team.others:
        kv_copies[o].wait_recv()
        send_piece(o)
    send_on(0)
    own_q.wait()
    for copy in q_copies:
        copy.wait_recv()
    for n in range(team.size):
        queries[:, n * rows : (n + 1) * rows] = with_query_tail(
            bounds, my_group * amount + n * rows, unpack_t(q_all[n]), None
        )
    compute((0, 0, 0, 0))
    for s in range(1, z + 1):
        if s < z:
            for copy in ring[s]:
                copy.wait_recv()
            send_on(s)
            compute(along(0, s))
        for o in team.sides:
            side[(s - 1, o)].wait_recv()
            compute((s - 1, o[1], 0, 0))
    total = accum[HD : HD + 1, :]
    out_t[...] = accum[:HD, :] / total
    lse[...] = top[...] + jnp.log(total)
    for n in range(team.size):
        o_mine[n] = pack_t(out_t[:, n * rows : (n + 1) * rows]).astype(low)
    o_copies = [to_team(o_mine, o_out.at[my_slot], o) for o in team.others]
    own_o = pltpu.make_async_copy(o_mine.at[my_slot], o_out.at[my_slot], own_sem.at[2])
    own_o.start()
    own_o.wait()
    for copy in o_copies:
        copy.wait_recv()
    push.finish()


def attend(dims, lengths, q, kv, collective_id):
    team = Team(dims)
    z = dims[0]
    amount = team.size * kv.shape[1]
    count = 3 * (team.size - 1) + team.size + z + z * len(team.sides)
    return pl.pallas_call(
        functools.partial(attend_kernel, team, 256, 1024),
        out_shape=(
            jax.ShapeDtypeStruct(q.shape, low),
            jax.ShapeDtypeStruct((1, amount), jnp.float32),
            jax.ShapeDtypeStruct((HD, amount), jnp.float32),
            jax.ShapeDtypeStruct(q.shape, low),
            jax.ShapeDtypeStruct((team.groups,) + kv.shape, low),
        ),
        in_specs=[SMEM_SPEC, VMEM_SPEC, VMEM_SPEC],
        out_specs=[VMEM_SPEC] * 5,
        scratch_shapes=[
            pltpu.VMEM((amount, LANES), low),
            pltpu.VMEM((HD + TILE, amount), low),
            pltpu.VMEM((LANES, amount), low),
            pltpu.VMEM((1, amount), jnp.float32),
            pltpu.VMEM((HD + TILE, amount), jnp.float32),
            pltpu.VMEM(q.shape, low),
            pltpu.SemaphoreType.DMA((count,)),
            pltpu.SemaphoreType.DMA((count,)),
            pltpu.SemaphoreType.DMA((3,)),
        ],
        compiler_params=pltpu.CompilerParams(
            collective_id=collective_id, has_side_effects=True, vmem_limit_bytes=56 * MIB
        ),
        name="attend",
    )(lengths, q, kv)


def attend_back_kernel(
    team,
    key_step,
    pieces,
    lengths,
    q_all,
    kv_all,
    do_in,
    out_t,
    lse,
    d_q_out,
    d_kv_out,
    do_all,
    keys,
    keys_t,
    values,
    queries,
    douts,
    d_q_t,
    q_rows,
    do_rows,
    side_out,
    side_in,
    ring_out,
    ring_in,
    mine,
    d_q_mine,
    d_kv_mine,
    send_sem,
    recv_sem,
    own_sem,
):
    dims = team.dims
    z = dims[0]
    me = my_place(dims)
    bounds = clip_bounds(lengths)
    rows = kv_all.shape[2]
    amount = team.size * rows
    slots = team.size // pieces
    piece_rows = slots * rows
    my_group, my_slot = team.group(me), team.slot(me)
    ring_ends = sorted({along(0, 1 % z), along(0, (z - 1) % z)} - {(0, 0, 0, 0)})
    greet(dims, me, team.others + ring_ends + team.sides)
    push = Pushes(dims, me, send_sem, recv_sem)

    def to_team(src, dst, o):
        return push(src.at[team.slot(shifted(dims, me, o, 1))], dst, o)

    do_copies = [to_team(do_in, do_all.at[my_slot], o) for o in team.others]
    own_do = pltpu.make_async_copy(do_in.at[my_slot], do_all.at[my_slot], own_sem.at[0])
    own_do.start()
    place = lax.broadcasted_iota(jnp.int32, (HD, 1), 0)
    for n in range(team.size):
        at = slice(n * rows, (n + 1) * rows)
        q_t = unpack_t(q_all[n])
        queries[:, at] = with_query_tail(bounds, my_group * amount + n * rows, q_t, lse[:, at])
        q_rows[:, at] = (q_t * HD ** (-0.5)).astype(low)
    d_q_t[...] = jnp.zeros(d_q_t.shape, jnp.float32)
    own_do.wait()
    for copy in do_copies:
        copy.wait_recv()
    for n in range(team.size):
        at = slice(n * rows, (n + 1) * rows)
        do_t = unpack_t(do_all[n])
        delta = jnp.sum(do_t * out_t[:, at], 0, keepdims=True)
        douts[:, at] = jnp.concatenate([in_three(place, -delta), do_t], 0).astype(low)
        do_rows[:, at] = do_t.astype(low)

    def compute(offset, piece, target):
        group = team.group(shifted(dims, me, offset, 1))

        @pl.loop(0, slots)
        def build(n):
            at = pl.ds(pl.multiple_of(n * rows, rows), rows)
            slot = piece * slots + n
            block = kv_all[group, slot]
            keys[at, :] = with_key_tail(bounds, group * amount + slot * rows, block)
            keys_t[:, at] = block.astype(jnp.float32).T[:HD].astype(low)
            values[at, :] = with_value_tail(block)

        @pl.loop(0, piece_rows // key_step)
        def key_block(k):
            at = pl.ds(pl.multiple_of(k * key_step, key_step), key_step)
            d_key = jnp.zeros((HD, key_step), jnp.float32)
            d_value = jnp.zeros((HD, key_step), jnp.float32)
            for half in (slice(0, amount // 2), slice(amount // 2, amount)):
                probs = jnp.exp(product(keys[at, :], queries[:, half]))
                d_probs = product(values[at, :], douts[:, half])
                d_scores = (probs * d_probs).astype(low)
                d_value = d_value + against(do_rows[:, half], probs.astype(low))
                d_key = d_key + against(q_rows[:, half], d_scores)
                d_q_t[:, half] = d_q_t[:, half] + product(keys_t[:, at], d_scores)
            target[at, :] = jnp.concatenate([d_key, d_value], 0).T.astype(target.dtype)

    side, ring = {}, {}

    def send_sides(s, piece):
        for o in team.sides:
            target = side_out.at[s - 1, o[1] - 1, piece]
            compute((z - s, o[1], 0, 0), piece, target)
            side[(s, o, piece)] = push(target, side_in.at[s - 1, o[1] - 1, piece], o)

    def combine(s, piece):
        for o in team.sides:
            side[(s, o, piece)].wait_recv()
        if s > 1:
            ring[(s - 1, piece)].wait_recv()
        for n in range(slots):
            at = slice(n * rows, (n + 1) * rows)
            total = mine[piece, at, :]
            for o in team.sides:
                total = total + side_in[s - 1, o[1] - 1, piece, at, :].astype(jnp.float32)
            if s > 1:
                total = total + ring_in[s - 2, piece, at, :].astype(jnp.float32)
            if s < z:
                ring_out[s - 1, piece, at, :] = total.astype(low)
            else:
                d_kv_mine[piece * slots + n] = total.astype(low)
        if s < z:
            ring[(s, piece)] = push(ring_out.at[s - 1, piece], ring_in.at[s - 1, piece], along(0, 1))

    for s in range(1, z + 1):
        for piece in range(pieces):
            send_sides(s, piece)
            compute((z - s if s < z else 0, 0, 0, 0), piece, mine.at[piece])
            if team.sides or s < z:
                combine(s, piece)
    for n in range(team.size):
        at = slice(n * rows, (n + 1) * rows)
        d_q_mine[n] = pack_t(d_q_t[:, at] * HD ** (-0.5)).astype(low)
    copies = [to_team(d_q_mine, d_q_out.at[my_slot], o) for o in team.others]
    own_q = pltpu.make_async_copy(d_q_mine.at[my_slot], d_q_out.at[my_slot], own_sem.at[1])
    own_q.start()
    if not team.sides:
        for piece in range(pieces):
            combine(z, piece)
    copies += [to_team(d_kv_mine, d_kv_out.at[my_slot], o) for o in team.others]
    own_kv = pltpu.make_async_copy(d_kv_mine.at[my_slot], d_kv_out.at[my_slot], own_sem.at[2])
    own_kv.start()
    own_q.wait()
    own_kv.wait()
    for copy in copies:
        copy.wait_recv()
    push.finish()


def attend_back(dims, lengths, q, kv, dout, out_t, lse, collective_id):
    team = Team(dims)
    z = dims[0]
    rows = kv.shape[2]
    amount = team.size * rows
    pieces = 2
    piece = (pieces, amount // pieces, LANES)
    count = 3 * (team.size - 1) + pieces * (z + z * len(team.sides))
    others = max(len(team.sides), 1)
    ring_steps, side_steps = max(z - 1, 1), z if team.sides else 1
    return pl.pallas_call(
        functools.partial(attend_back_kernel, team, 256, pieces),
        out_shape=(
            jax.ShapeDtypeStruct(q.shape, low),
            jax.ShapeDtypeStruct(kv.shape[1:], low),
        ),
        in_specs=[SMEM_SPEC] + [VMEM_SPEC] * 5,
        out_specs=[VMEM_SPEC] * 2,
        scratch_shapes=[
            pltpu.VMEM(q.shape, low),
            pltpu.VMEM((amount // pieces, LANES), low),
            pltpu.VMEM((HD, amount // pieces), low),
            pltpu.VMEM((amount // pieces, LANES), low),
            pltpu.VMEM((LANES, amount), low),
            pltpu.VMEM((LANES, amount), low),
            pltpu.VMEM((HD, amount), jnp.float32),
            pltpu.VMEM((HD, amount), low),
            pltpu.VMEM((HD, amount), low),
            pltpu.VMEM((side_steps, others) + piece, low),
            pltpu.VMEM((side_steps, others) + piece, low),
            pltpu.VMEM((ring_steps,) + piece, low),
            pltpu.VMEM((ring_steps,) + piece, low),
            pltpu.VMEM(piece, jnp.float32),
            pltpu.VMEM(q.shape, low),
            pltpu.VMEM(kv.shape[1:], low),
            pltpu.SemaphoreType.DMA((count,)),
            pltpu.SemaphoreType.DMA((count,)),
            pltpu.SemaphoreType.DMA((3,)),
        ],
        compiler_params=pltpu.CompilerParams(
            collective_id=collective_id, has_side_effects=True, vmem_limit_bytes=60 * MIB
        ),
        name="attend_back",
    )(lengths, q, kv, dout, out_t, lse)


def part_shapes(n_head):
    width = HEADS // n_head * HD
    hidden = FF // n_head
    return (
        (D, width, True),
        (DI, 2 * width, True),
        (width, D, False),
        (D, 3 * width, True),
        (width, D, False),
        (D, hidden, True),
        (hidden, D, False),
        (D, C // n_head, True),
    )


def borders(n_head):
    result = [0]
    for rows, columns, joined in part_shapes(n_head):
        result.append(result[-1] + rows * columns // LANES)
    return result


def period(columns):
    amount = 1
    while amount * columns % LANES:
        amount *= 2
    return amount


def segments(start, amount, unit):
    result = []
    while amount > 0:
        which, at = divmod(start, unit)
        size = min(unit - at, amount)
        result.append((which, at, at + size))
        start, amount = start + size, amount - size
    return result


def joined_lanes(pieces):
    return pieces[0] if len(pieces) == 1 else jnp.concatenate(pieces, 1)


def lane_blocks(value):
    rows, columns = value.shape
    missing = -columns % LANES
    if missing:
        value = jnp.concatenate([value, jnp.zeros((rows, missing), value.dtype)], 1)
    return [value[:, i : i + LANES] for i in range(0, columns + missing, LANES)]


def every(first, amount, stride):
    return pl.ds(first, amount) if stride == 1 else pl.ds(first, amount, stride=stride)


def matrix_of(stage, first, rows, columns, line):
    if columns % LANES == 0:
        stride = columns // LANES
        for j in range(stride):
            yield j * LANES, stage[every(first + j, rows, stride), :]
        return
    height = period(columns)
    stride = height * columns // LANES
    for k in range(height):
        pieces = [
            stage[every(first + which, rows // height, stride), :][:, begin:end]
            for which, begin, end in segments(k * columns, columns, LANES)
        ]
        for i, piece in enumerate(lane_blocks(joined_lanes(pieces))):
            line[i, every(k, rows // height, height), :] = piece
    for i in range(-(-columns // LANES)):
        yield i * LANES, line[i, :rows, : min(columns - i * LANES, LANES)]


def matrix_into(stage, first, value, line):
    rows, columns = value.shape
    if columns % LANES == 0:
        stride = columns // LANES
        for j in range(stride):
            stage[every(first + j, rows, stride), :] = value[:, j * LANES : (j + 1) * LANES]
        return
    height = period(columns)
    stride = height * columns // LANES
    for i, piece in enumerate(lane_blocks(value)):
        line[i, :rows, :] = piece
    for i in range(stride):
        pieces = [
            line[which, every(k, rows // height, height), :][:, begin:end]
            for k, first_lane, last_lane in segments(i * LANES, LANES, columns)
            for which, begin, end in segments(first_lane, last_lane - first_lane, LANES)
        ]
        stage[every(first + i, rows // height, stride), :] = joined_lanes(pieces)


def load_stage(stage, held, first_shard, shard_rows, group):
    for b in range(held.shape[0]):
        stage[pl.ds(b * shard_rows, shard_rows), :] = held[b, group, :shard_rows, :].astype(jnp.float32)


def load_common(stage, held, valid):
    piece = held.shape[2]
    for b in range(held.shape[0]):
        for k in range(held.shape[1]):
            amount = min(piece, valid - k * piece)
            stage[b * valid + k * piece : b * valid + k * piece + amount, :] = held[b, k].astype(
                jnp.float32
            )[:amount]


def common_blocks(first_row, last_row, valid):
    return first_row // valid, -(-last_row // valid) - first_row // valid


def load_matrices(stage, first_row, n_head, group, which, targets, line):
    starts, shapes = borders(n_head), part_shapes(n_head)
    for m, target in zip(which, targets):
        rows, columns, joined = shapes[m]
        row = 0 if joined else group * rows
        column = group * columns if joined else 0
        for j, value in matrix_of(stage, starts[m] - first_row, rows, columns, line):
            size = value.shape[1]
            target[row : row + rows, column + j : column + j + size] = value.astype(target.dtype)


def normalized(x):
    centre = x - jnp.mean(x, -1, keepdims=True)
    rate = lax.rsqrt(jnp.mean(centre * centre, -1, keepdims=True) + norm_eps)
    return centre * rate, rate


def layer_norm(x, gain):
    return normalized(x)[0] * gain


def norm_pullback(x, gain, grad):
    unit, rate = normalized(x)
    inside = grad * gain
    both = jnp.mean(inside * unit, -1, keepdims=True)
    d_x = rate * (inside - jnp.mean(inside, -1, keepdims=True) - unit * both)
    return d_x, jnp.sum(grad * unit, 0, keepdims=True)


def head_lanes(group, heads, value):
    width = heads * HD
    block = value[:, group * width : (group + 1) * width]
    lane = lax.broadcasted_iota(jnp.int32, (1, width), 1)
    result = []
    for a in range(heads):
        here = (lane >= a * HD) & (lane < (a + 1) * HD)
        result.append((here, jnp.where(here, block, jnp.zeros_like(block))))
    return result


def place_of(bounds, first, amount):
    row = first + lax.broadcasted_iota(jnp.int32, (amount, 1), 0)
    opening = jnp.zeros((amount, 1), jnp.int32)
    for begin, end in bounds:
        opening = jnp.where((row >= begin) & (row < end), begin, opening)
    offset = row - opening
    turns = jnp.floor((offset.astype(jnp.float32) + 0.5) * (1.0 / LAT)).astype(jnp.int32)
    return offset - turns * LAT


def picked_rows(bounds, rows, n_head):
    first = lax.axis_index("blk") * (rows * n_head) + lax.axis_index("head") * rows
    lane = lax.broadcasted_iota(jnp.int32, (rows, LAT), 1)
    return jnp.where(lane == place_of(bounds, first, rows), 1.0, 0.0).astype(low)


def enc_scores(q_head, keys):
    return against(q_head, keys) * HD ** (-0.5)


def encode_kernel(
    n_head,
    shard_rows,
    valid,
    rows,
    lengths,
    weights,
    common,
    inputs_t,
    enc_query,
    enc_keyval,
    enc_output,
    self_project,
    gains,
    z_zero,
    h_zero,
    x_norm_t,
    q_enc,
    kv_enc,
    o_enc,
    z_one,
    h_one,
    q_self,
    kv_self,
    counts,
    held,
    held_common,
    held_counts,
    stage,
    stage_common,
    line,
    latent_table,
    sems,
):
    heads = HEADS // n_head
    width = heads * HD
    shards = held.shape[0]
    bounds = clip_bounds(lengths)
    first = DQ * D // LANES
    block, blocks = common_blocks(first, first + (LAT + 4) * D // LANES, valid)
    tail = shard_rows // TILE * TILE
    copies = [
        pltpu.make_async_copy(common.at[pl.ds(block, blocks)], held_common, sems.at[0]),
        pltpu.make_async_copy(weights.at[pl.ds(0, shards)], held, sems.at[1]),
        pltpu.make_async_copy(weights.at[:, :, pl.ds(tail, TILE)], held_counts, sems.at[2]),
    ]
    for copy in copies:
        copy.start()
    centre = inputs_t[...].astype(jnp.float32)
    centre = centre - jnp.mean(centre, 0, keepdims=True)
    rate = lax.rsqrt(jnp.mean(centre * centre, 0, keepdims=True) + norm_eps)
    x_norm_t[...] = (centre * rate).astype(low)
    copies[0].wait()
    load_common(stage_common, held_common, valid)
    first = first - block * valid
    for j, value in matrix_of(stage_common, first, LAT, D, line):
        latent_table[:, j : j + LANES] = value.astype(low)
    for j, value in matrix_of(stage_common, first + LAT * D // LANES, 4, D, line):
        gains[:, j : j + LANES] = value
    picked = picked_rows(bounds, rows, n_head)
    z_zero[...] = product(picked, latent_table[...])
    h_zero[...] = layer_norm(z_zero[...], gains[0:1, :]).astype(low)
    copies[2].wait()
    counted = held_counts[...].astype(jnp.float32)[:, :, shard_rows - tail : shard_rows - tail + 1]
    counts[...] = jnp.broadcast_to(jnp.sum(counted, (0, 1)), counts.shape)
    copies[1].wait()
    for g in range(n_head):
        load_stage(stage, held, 0, shard_rows, g)
        load_matrices(
            stage, 0, n_head, g, (0, 1, 2, 3), (enc_query, enc_keyval, enc_output, self_project), line
        )
    q_enc[...] = product(h_zero[...], enc_query[...]).astype(low)
    kv_enc[...] = contract_first(x_norm_t[...], enc_keyval[...]).astype(low)
    for g in range(n_head):
        keys = kv_enc[:, 2 * g * width : (2 * g + 1) * width]
        values = kv_enc[:, (2 * g + 1) * width : (2 * g + 2) * width]
        outcome = jnp.zeros((rows, width), jnp.float32)
        for here, q_head in head_lanes(g, heads, q_enc[...]):
            scores = enc_scores(q_head, keys)
            probs = jnp.exp(scores - jnp.max(scores, 1, keepdims=True))
            total = jnp.sum(probs, 1, keepdims=True)
            outcome = jnp.where(here, product(probs.astype(low), values) / total, outcome)
        o_enc[:, g * width : (g + 1) * width] = outcome.astype(low)
    z_one[...] = z_zero[...] + product(o_enc[...], enc_output[...])
    h_one[...] = layer_norm(z_one[...], gains[1:2, :]).astype(low)
    projected = product(h_one[...], self_project[...]).astype(low)
    for slot, (g, a) in enumerate(heads_of(n_head, q_self.shape[0])):
        query, key, value = (
            projected[:, (3 * g + i) * width + a * HD : (3 * g + i) * width + (a + 1) * HD]
            for i in range(3)
        )
        q_self[slot] = pack(query)
        kv_self[slot] = jnp.concatenate([key, value], 1)


LINE = pltpu.VMEM((4, round_up(max(D, DI), 8), LANES), jnp.float32)


def shards_of(n_head, shard_rows, first, last):
    starts = borders(n_head)
    begin = starts[first] // shard_rows
    return begin, -(-starts[last] // shard_rows) - begin


def encode(lengths, weights, common, inputs_t, valid, rows, slots, n_head, shard_rows):
    begin, shards = shards_of(n_head, shard_rows, 0, 4)
    query_rows = DQ * D // LANES
    block, blocks = common_blocks(query_rows, query_rows + (LAT + 4) * D // LANES, valid)
    keys = inputs_t.shape[1]
    return pl.pallas_call(
        functools.partial(encode_kernel, n_head, shard_rows, valid, rows),
        out_shape=[
            shape_of((D, D)),
            shape_of((DI, 2 * D)),
            shape_of((D, D)),
            shape_of((D, 3 * D)),
            shape_of((4, D), jnp.float32),
            shape_of((rows, D), jnp.float32),
            shape_of((rows, D)),
            shape_of(inputs_t.shape),
            shape_of((rows, D)),
            shape_of((keys, 2 * D)),
            shape_of((rows, D)),
            shape_of((rows, D), jnp.float32),
            shape_of((rows, D)),
            shape_of((slots, rows // 2, LANES)),
            shape_of((slots, rows, LANES)),
            shape_of((8, LANES), jnp.float32),
        ],
        in_specs=[SMEM_SPEC, ANY_SPEC, ANY_SPEC, VMEM_SPEC],
        out_specs=[VMEM_SPEC] * 16,
        scratch_shapes=[
            pltpu.VMEM((shards,) + weights.shape[1:], low),
            pltpu.VMEM((blocks,) + common.shape[1:], low),
            pltpu.VMEM(weights.shape[:2] + (TILE, LANES), low),
            pltpu.VMEM((shards * shard_rows, LANES), jnp.float32),
            pltpu.VMEM((blocks * valid, LANES), jnp.float32),
            LINE,
            pltpu.VMEM((LAT, D), low),
            pltpu.SemaphoreType.DMA((3,)),
        ],
        compiler_params=pltpu.CompilerParams(vmem_limit_bytes=56 * MIB),
        name="encode",
    )(lengths, weights, common, inputs_t)


def gelu_and_slope(x):
    rate = (2.0 / jnp.pi) ** 0.5
    cubic = 0.044715
    t = jnp.tanh(rate * (x + cubic * x * x * x))
    slope = 0.5 * (1.0 + t) + 0.5 * x * (1.0 - t * t) * rate * (1.0 + 3.0 * cubic * x * x)
    return 0.5 * x * (1.0 + t), slope


def my_column(marks, rows):
    turned = marks[...].astype(jnp.float32).T
    column = lax.broadcasted_iota(jnp.int32, turned.shape, 1)
    per_head = rows // LANES
    first = lax.axis_index("head") * per_head
    picked = [
        jnp.sum(jnp.where(column == first + k, turned, 0.0), 1, keepdims=True)
        for k in range(per_head)
    ]
    return jnp.concatenate(picked, 0) if per_head > 1 else picked[0]


def middle_kernel(
    n_head,
    shard_rows,
    valid,
    first_shard,
    rows,
    counts,
    weights,
    common,
    z_one,
    o_self,
    out_queries_t,
    labels,
    modality,
    labeled,
    gains,
    dout,
    d_two_out,
    tile,
    query_grad,
    gain_grads,
    grads,
    held,
    held_common,
    stage,
    stage_common,
    line,
    self_output,
    hidden_in,
    hidden_out,
    class_table,
    query_table,
    slope,
    activ,
    sems,
):
    heads = HEADS // n_head
    width, hidden, classes = heads * HD, FF // n_head, C // n_head
    shards = held.shape[0]
    first_row = first_shard * shard_rows
    starts = borders(n_head)
    copies = [
        pltpu.make_async_copy(common.at[pl.ds(0, held_common.shape[0])], held_common, sems.at[0]),
        pltpu.make_async_copy(weights.at[pl.ds(first_shard, shards)], held, sems.at[1]),
    ]
    for copy in copies:
        copy.start()
    copies[0].wait()
    load_common(stage_common, held_common, valid)
    for j, value in matrix_of(stage_common, 0, DQ, D, line):
        query_table[:, j : j + LANES] = value.astype(low)
    copies[1].wait()
    for g in range(n_head):
        load_stage(stage, held, first_shard, shard_rows, g)
        load_matrices(
            stage, first_row, n_head, g, (4, 5, 6, 7), (self_output, hidden_in, hidden_out, class_table), line
        )
    gain_two, gain_three = gains[2:3, :], gains[3:4, :]
    o_heads = {head: unpack(o_self[s]) for s, head in enumerate(heads_of(n_head, o_self.shape[0]))}
    o_groups = [joined_lanes([o_heads[(g, a)] for a in range(heads)]) for g in range(n_head)]
    o_low = jnp.concatenate(o_groups, 1)
    z_two = z_one[...] + product(o_low, self_output[...])
    h_two = layer_norm(z_two, gain_two).astype(low)
    value, bend = gelu_and_slope(product(h_two, hidden_in[...]))
    activ[...] = value.astype(low)
    slope[...] = bend
    z_three = z_two + product(activ[...], hidden_out[...])
    queries_t = out_queries_t[...]
    decoded = layer_norm(z_three, gain_three) + contract_first(queries_t, query_table[...])
    decoded = decoded.astype(low)
    logits = product(decoded, class_table[...])
    label, kind, counted = (my_column(marks, rows) for marks in (labels, modality, labeled))
    lane = lax.broadcasted_iota(jnp.int32, (rows, C), 1).astype(jnp.float32)
    is_target = jnp.where(lane == label, 1.0, 0.0)
    row_top = jnp.max(logits, 1, keepdims=True)
    row_lse = row_top + jnp.log(jnp.sum(jnp.exp(logits - row_top), 1, keepdims=True))
    loss = row_lse - jnp.sum(is_target * logits, 1, keepdims=True)
    weight = jnp.zeros((rows, 1), jnp.float32)
    place = lax.broadcasted_iota(jnp.int32, (1, LANES), 1)
    losses = jnp.zeros((1, LANES), jnp.float32)
    for m in range(MODES):
        member = jnp.where((kind == m) & (counted == 1.0), 1.0, 0.0)
        weight = weight + member / jnp.maximum(counts[0:1, m : m + 1], 1.0)
        losses = losses + jnp.where(place == m, jnp.sum(loss * member, 0, keepdims=True), 0.0)
    tile[...] = jnp.broadcast_to(losses, tile.shape)
    dlogits = (weight * (jnp.exp(logits - row_lse) - is_target)).astype(low)
    d_decoded = against(dlogits, class_table[...])
    matrix_into(query_grad, 0, product(queries_t, d_decoded.astype(low)), line)
    d_three, gain_three_grad = norm_pullback(z_three, gain_three, d_decoded)
    d_branch = d_three.astype(low)
    d_pre = (slope[...] * against(d_branch, hidden_out[...])).astype(low)
    d_middle, gain_two_grad = norm_pullback(z_two, gain_two, against(d_pre, hidden_in[...]))
    d_two = d_three + d_middle
    d_two_out[...] = d_two
    gain_grads[...] = jnp.concatenate([gain_two_grad, gain_three_grad], 0)
    d_two_low = d_two.astype(low)
    d_o = against(d_two_low, self_output[...]).astype(low)
    for slot, (g, a) in enumerate(heads_of(n_head, o_self.shape[0])):
        dout[slot] = pack(d_o[:, g * width + a * HD : g * width + (a + 1) * HD])
    for g in range(n_head):
        results = (
            contract_first(o_groups[g], d_two_low),
            contract_first(h_two, d_pre[:, g * hidden : (g + 1) * hidden]),
            contract_first(activ[:, g * hidden : (g + 1) * hidden], d_branch),
            contract_first(decoded, dlogits[:, g * classes : (g + 1) * classes]),
        )
        for m, result in zip((4, 5, 6, 7), results):
            matrix_into(stage, starts[m] - first_row, result, line)
        for b in range(shards):
            held[b, g, :shard_rows, :] = stage[pl.ds(b * shard_rows, shard_rows), :].astype(low)
    back = pltpu.make_async_copy(held, grads.at[pl.ds(first_shard, shards)], sems.at[2])
    back.start()
    back.wait()


def middle(counts, weights, common, z_one, o_self, out_queries_t, marks, gains, valid, n_head, shard_rows):
    rows = z_one.shape[0]
    begin, shards = shards_of(n_head, shard_rows, 4, 8)
    query_rows = DQ * D // LANES
    block, blocks = common_blocks(0, query_rows, valid)
    return pl.pallas_call(
        functools.partial(middle_kernel, n_head, shard_rows, valid, begin, rows),
        grid=(1,),
        out_shape=[
            shape_of(o_self.shape),
            shape_of((rows, D), jnp.float32),
            shape_of((8, LANES), jnp.float32),
            shape_of((query_rows, LANES), jnp.float32),
            shape_of((2, D), jnp.float32),
            shape_of(weights.shape),
        ],
        in_specs=[
            VMEM_SPEC,
            ANY_SPEC,
            ANY_SPEC,
            VMEM_SPEC,
            VMEM_SPEC,
            pl.BlockSpec((DQ, rows), lambda i: (0, lax.axis_index("head"))),
            VMEM_SPEC,
            VMEM_SPEC,
            VMEM_SPEC,
            VMEM_SPEC,
        ],
        out_specs=[VMEM_SPEC] * 5 + [ANY_SPEC],
        scratch_shapes=[
            pltpu.VMEM((shards,) + weights.shape[1:], low),
            pltpu.VMEM((blocks,) + common.shape[1:], low),
            pltpu.VMEM((shards * shard_rows, LANES), jnp.float32),
            pltpu.VMEM((blocks * valid, LANES), jnp.float32),
            LINE,
            pltpu.VMEM((D, D), low),
            pltpu.VMEM((D, FF), low),
            pltpu.VMEM((FF, D), low),
            pltpu.VMEM((D, C), low),
            pltpu.VMEM((DQ, D), low),
            pltpu.VMEM((rows, FF), jnp.float32),
            pltpu.VMEM((rows, FF), low),
            pltpu.SemaphoreType.DMA((3,)),
        ],
        compiler_params=pltpu.CompilerParams(vmem_limit_bytes=56 * MIB),
        name="middle",
    )(counts, weights, common, z_one, o_self, out_queries_t, *marks, gains)


def ending_kernel(
    n_head,
    shard_rows,
    valid,
    rows,
    lengths,
    grads_in,
    d_q_self,
    d_kv_self,
    d_two,
    gains,
    gain_grads,
    query_grad,
    enc_query,
    enc_keyval,
    enc_output,
    self_project,
    z_zero,
    h_zero,
    x_norm_t,
    q_enc,
    kv_enc,
    o_enc,
    z_one,
    h_one,
    grads,
    common_grad,
    held,
    stage,
    stage_common,
    line,
    d_q,
    d_kv,
    sems,
):
    heads = HEADS // n_head
    width = heads * HD
    shards = held.shape[0]
    starts = borders(n_head)
    shared = pltpu.make_async_copy(grads_in.at[pl.ds(shards - 1, 1)], held.at[pl.ds(shards - 1, 1)], sems.at[0])
    shared.start()
    d_heads = {}
    for slot, head in enumerate(heads_of(n_head, d_kv_self.shape[0])):
        d_kv_head = d_kv_self[slot]
        d_heads[head] = (unpack(d_q_self[slot]), d_kv_head[:, :HD], d_kv_head[:, HD:])
    d_projected = [
        jnp.concatenate([d_heads[(g, a)][i] for i in range(3) for a in range(heads)], 1)
        for g in range(n_head)
    ]
    whole = jnp.concatenate(d_projected, 1)
    d_middle, gain_one_grad = norm_pullback(
        z_one[...], gains[1:2, :], against(whole, self_project[...])
    )
    d_one = d_two[...] + d_middle
    d_one_low = d_one.astype(low)
    d_o = against(d_one_low, enc_output[...]).astype(low)
    for g in range(n_head):
        keys = kv_enc[:, 2 * g * width : (2 * g + 1) * width]
        values = kv_enc[:, (2 * g + 1) * width : (2 * g + 2) * width]
        d_key = jnp.zeros(keys.shape, jnp.float32)
        d_value = jnp.zeros(keys.shape, jnp.float32)
        d_query = jnp.zeros((rows, width), jnp.float32)
        for (here, q_head), (unused, do_head) in zip(
            head_lanes(g, heads, q_enc[...]), head_lanes(g, heads, d_o)
        ):
            scores = enc_scores(keys, q_head)
            probs = jnp.exp(scores - jnp.max(scores, 0, keepdims=True))
            probs = probs / jnp.sum(probs, 0, keepdims=True)
            d_probs = against(values, do_head)
            delta = jnp.sum(probs * d_probs, 0, keepdims=True)
            d_scores = (probs * (d_probs - delta)).astype(low)
            d_value = d_value + product(probs.astype(low), do_head)
            d_key = d_key + product(d_scores, q_head)
            d_query = jnp.where(here, contract_first(d_scores, keys), d_query)
        d_q[:, g * width : (g + 1) * width] = (d_query * HD ** (-0.5)).astype(low)
        d_kv[:, 2 * g * width : (2 * g + 1) * width] = (d_key * HD ** (-0.5)).astype(low)
        d_kv[:, (2 * g + 1) * width : (2 * g + 2) * width] = d_value.astype(low)
    d_middle, gain_zero_grad = norm_pullback(
        z_zero[...], gains[0:1, :], against(d_q[...], enc_query[...])
    )
    d_zero = d_one + d_middle
    d_zero_top = d_zero.astype(low)
    d_zero_rest = (d_zero - d_zero_top.astype(jnp.float32)).astype(low)
    picked = picked_rows(clip_bounds(lengths), rows, n_head)
    latent_grad = contract_first(picked, d_zero_top) + contract_first(picked, d_zero_rest)
    query_rows = query_grad.shape[0]
    stage_common[:query_rows] = query_grad[...]
    matrix_into(stage_common, query_rows, latent_grad, line)
    all_gains = jnp.concatenate([gain_zero_grad, gain_one_grad, gain_grads[...]], 0)
    matrix_into(stage_common, query_rows + LAT * D // LANES, all_gains, line)
    piece = common_grad.shape[2]
    for b in range(common_grad.shape[0]):
        for k in range(common_grad.shape[1]):
            amount = min(piece, valid - k * piece)
            block = stage_common[b * valid + k * piece : b * valid + k * piece + amount, :]
            if amount < piece:
                block = jnp.concatenate([block, jnp.zeros((piece - amount, LANES), jnp.float32)], 0)
            common_grad[b, k] = block.astype(low)
    shared.wait()
    kept = shards * shard_rows - starts[4]
    for g in range(n_head):
        results = (
            contract_first(h_zero[...], d_q[:, g * width : (g + 1) * width]),
            product(x_norm_t[...], d_kv[:, 2 * g * width : (2 * g + 2) * width]),
            contract_first(o_enc[:, g * width : (g + 1) * width], d_one_low),
            contract_first(h_one[...], d_projected[g]),
        )
        if kept:
            stage[pl.ds((shards - 1) * shard_rows, shard_rows), :] = held[
                shards - 1, g, :shard_rows, :
            ].astype(jnp.float32)
        for m, result in zip((0, 1, 2, 3), results):
            matrix_into(stage, starts[m], result, line)
        for b in range(shards):
            held[b, g, :shard_rows, :] = stage[pl.ds(b * shard_rows, shard_rows), :].astype(low)
    back = pltpu.make_async_copy(held, grads.at[pl.ds(0, shards)], sems.at[1])
    back.start()
    back.wait()


def ending(lengths, grads, d_self, d_two, gains, gain_grads, query_grad, kept, common_shape, valid, shard_rows):
    rows = d_two.shape[0]
    n_head = grads.shape[1]
    begin, shards = shards_of(n_head, shard_rows, 0, 4)
    keys = kept[6].shape[1]
    common_rows = (DQ + LAT + 4) * D // LANES
    return pl.pallas_call(
        functools.partial(ending_kernel, n_head, shard_rows, valid, rows),
        out_shape=[shape_of(grads.shape), shape_of(common_shape)],
        in_specs=[SMEM_SPEC, ANY_SPEC] + [VMEM_SPEC] * 18,
        out_specs=[ANY_SPEC, VMEM_SPEC],
        input_output_aliases={1: 0},
        scratch_shapes=[
            pltpu.VMEM((shards,) + grads.shape[1:], low),
            pltpu.VMEM((shards * shard_rows, LANES), jnp.float32),
            pltpu.VMEM((common_rows, LANES), jnp.float32),
            LINE,
            pltpu.VMEM((rows, D), low),
            pltpu.VMEM((keys, 2 * D), low),
            pltpu.SemaphoreType.DMA((2,)),
        ],
        compiler_params=pltpu.CompilerParams(vmem_limit_bytes=56 * MIB),
        name="ending",
    )(lengths, grads, *d_self, d_two, gains, gain_grads, query_grad, *kept)


def adam_step(weight, first, second, grad):
    first = beta_one * first + (1 - beta_one) * grad
    second = beta_two * second + (1 - beta_two) * grad * grad
    fixed_first = first / (1 - beta_one**STEP)
    fixed_second = second / (1 - beta_two**STEP)
    weight = weight - learn_rate * (
        fixed_first / (jnp.sqrt(fixed_second) + adam_eps) + weight_decay * weight
    )
    return (weight, first, second, weight.astype(low))


def per_device(
    inputs,
    out_queries,
    clip_lengths,
    labels,
    modality,
    labeled,
    head_params,
    head_first,
    head_second,
    common_params,
    common_first,
    common_second,
):
    n_head, n_blk = lax.axis_size("head"), lax.axis_size("blk")
    dims = grid_of(n_blk, n_head)
    rows = labels.shape[0] // n_head
    n_h, n_c = head_params.shape[0], common_params.shape[0]
    shard_rows, common_rows = n_h // LANES, -(-n_c // LANES)
    head_rows = round_up(shard_rows + 1, TILE)
    piece_rows = round_up(-(-common_rows // n_head), TILE)
    marks = [x.reshape(-1, LANES) for x in (labels, modality, labeled)]
    head_wide = head_params.reshape(shard_rows, LANES)
    common_wide = jnp.pad(common_params, (0, common_rows * LANES - n_c)).reshape(common_rows, LANES)
    weights, common = gather_all(dims, marks, (head_wide, common_wide), (head_rows, piece_rows), 0)
    valid = common_rows
    if n_c % LANES:
        common = common.reshape(n_blk, -1)[:, :n_c].reshape(-1, LANES)
        valid = common.shape[0]
        common = jnp.pad(common, ((0, -valid % TILE), (0, 0)))[None, None]

    encoded = encode(
        clip_lengths, weights, common, inputs.T, valid, rows, Team(dims).size, n_head, shard_rows
    )
    gains, z_one, counts = encoded[4], encoded[11], encoded[15]
    o_self, lse_self, out_self_t, q_all, kv_all = attend(
        dims, clip_lengths, encoded[13], encoded[14], 1
    )
    dout, d_two, tile, query_grad, gain_grads, grads = middle(
        counts, weights, common, z_one, o_self, out_queries.T, marks, gains, valid, n_head, shard_rows
    )
    d_self = attend_back(dims, clip_lengths, q_all, kv_all, dout, out_self_t, lse_self, 2)
    kept = encoded[:4] + encoded[5:13]
    grads, common_grad = ending(
        clip_lengths,
        grads,
        d_self,
        d_two,
        gains,
        gain_grads,
        query_grad,
        kept,
        common.shape,
        valid,
        shard_rows,
    )
    if n_c % LANES:
        common_grad = common_grad[0, 0, :valid].reshape(n_blk, n_c)
        common_grad = jnp.pad(common_grad, ((0, 0), (0, n_head * piece_rows * LANES - n_c)))
        common_grad = common_grad.reshape(n_blk, n_head, piece_rows, LANES)
    head_share, common_share, totals = reduce_all(
        dims, (grads, common_grad), (shard_rows, common_rows), tile, 3
    )
    label_counts, loss_sums = counts[0, :MODES], totals[0, :MODES]
    clip_norm = jnp.sqrt(totals[0, MODES])
    factor = jnp.minimum(1.0, clip_limit / clip_norm)
    head_share, common_share = head_share.reshape(-1), common_share.reshape(-1)[:n_c]
    head_out = adam_step(head_params, head_first, head_second, head_share * factor)
    common_out = adam_step(common_params, common_first, common_second, common_share * factor)
    return head_out + common_out + (loss_sums, label_counts, clip_norm)


def solution(mesh):
    placed = (
        P("blk", None),
        P("blk", None),
        P(),
        P("blk"),
        P("blk"),
        P("blk"),
        P(("head", "blk")),
        P(("head", "blk")),
        P(("head", "blk")),
        P("blk"),
        P("blk"),
        P("blk"),
    )
    return jax.shard_map(
        per_device,
        mesh=mesh,
        in_specs=placed,
        out_specs=(
            P(("head", "blk")),
            P(("head", "blk")),
            P(("head", "blk")),
            P(("head", "blk")),
            P("blk"),
            P("blk"),
            P("blk"),
            P("blk"),
            P(),
            P(),
            P(),
        ),
        check_vma=False,
    )
```

```python
import functools

import jax
import jax.numpy as jnp
from jax import lax
from jax.experimental import pallas as pl
from jax.experimental.pallas import tpu as pltpu
from jax.sharding import PartitionSpec as P

D = 512
HEADS = 8
HD = 64
FF = 2048
DI = 704
DQ = 1026
C = 704
LAT = 784
MODES = 3
STEP = 10
LANES = 128
TILE = 16

norm_eps = 1e-05
learn_rate = 0.1
beta_one = 0.9
beta_two = 0.999
adam_eps = 1e-08
weight_decay = 0.01
clip_limit = 0.05
big_negative = -1e30
low = jnp.bfloat16
LOG2E = 1.4426950408889634
SCORE_SCALE = HD ** (-0.5)
MESH = pl.DeviceIdType.MESH
MIB = 1 << 20
VMEM_SPEC = pl.BlockSpec(memory_space=pltpu.VMEM)
SMEM_SPEC = pl.BlockSpec(memory_space=pltpu.SMEM)
ANY_SPEC = pl.BlockSpec(memory_space=pl.ANY)


def shape_of(shape, dtype=low):
    return jax.ShapeDtypeStruct(shape, dtype)


def round_up(n, unit):
    return -(-n // unit) * unit


def grid_of(n_blk, n_head):
    cores = 2 if n_head % 2 == 0 else 1
    x = n_head // cores
    y = x if n_blk % x == 0 else 1
    return (n_blk // y, y, x, cores)


def my_place(dims):
    blk, head = lax.axis_index("blk"), lax.axis_index("head")
    return (blk // dims[1], lax.rem(blk, dims[1]), head // dims[3], lax.rem(head, dims[3]))


def shifted(dims, me, offset, sign):
    return tuple(
        m if o == 0 else lax.rem(m + (o if sign > 0 else n - o), n)
        for m, o, n in zip(me, offset, dims)
    )


def blk_of(dims, place):
    return place[0] * dims[1] + place[1]


def head_of(dims, place):
    return place[2] * dims[3] + place[3]


def device_of(dims, place):
    return {"blk": blk_of(dims, place), "head": head_of(dims, place)}


def along(axis, d):
    return tuple(d if a == axis else 0 for a in range(4))


def greet(dims, me, offsets):
    barrier = pltpu.get_barrier_semaphore()
    for offset in offsets:
        pl.semaphore_signal(
            barrier,
            inc=1,
            device_id=device_of(dims, shifted(dims, me, offset, 1)),
            device_id_type=MESH,
        )
    pl.semaphore_wait(barrier, len(offsets))


def axis_peers(dims, axes):
    return [along(axis, d) for axis in axes for d in range(1, dims[axis])]


def remote(src, dst, send_sem, recv_sem, place, dims):
    return pltpu.make_async_remote_copy(
        src_ref=src,
        dst_ref=dst,
        send_sem=send_sem,
        recv_sem=recv_sem,
        device_id=device_of(dims, place),
        device_id_type=MESH,
    )


AHEAD = 6.0
RING = 0


def in_order(first, follow, size_of, ahead, result):
    queues, busy, flight = {}, {}, {}
    now = 0.0

    def ready(messages):
        for message in messages:
            queues.setdefault(message[1], []).append(message)

    ready(first)
    while True:
        for axis in sorted(queues):
            queue, going = queues[axis], flight.setdefault(axis, [])
            while queue and (not going or busy[axis] < now + ahead):
                message = min(queue)
                queue.remove(message)
                busy[axis] = max(now, busy.get(axis, 0.0)) + size_of(message)
                going.append((busy[axis] + 1.5, message))
                result.append((True, message))
        arrivals = [min(going) for going in flight.values() if going]
        if not arrivals:
            return now
        arrival = min(arrivals)
        flight[arrival[1][1]].remove(arrival)
        now = max(now, arrival[0])
        result.append((False, arrival[1]))
        ready(follow(arrival[1]))


def time_of(rows, axis):
    return rows * LANES * 2 / (300e3 if axis == 3 else 45e3)


def with_at(offset, axis, d):
    return offset[:axis] + (d,) + offset[axis + 1 :]


def gather_order(dims, parts):
    def onward(p, offset, position):
        order = parts[p][3]
        result = []
        for k in range(max(position, 0), 4):
            axis = order[k]
            n = dims[axis]
            if k > position:
                steps = [1] if axis == RING else range(1, n)
                steps = [d for d in steps if d < n]
            else:
                steps = [offset[axis] + 1] if axis == RING and offset[axis] + 1 < n else []
            for d in steps:
                result.append(((k, sum(offset), p), axis, p, with_at(offset, axis, d)))
        return result

    def follow(message):
        rank, axis, p, offset = message
        return onward(p, offset, rank[0])

    first = [m for p in range(len(parts)) for m in onward(p, (0, 0, 0, 0), -1)]
    result = []
    now = in_order(first, follow, lambda m: time_of(parts[m[2]][2], m[1]), AHEAD, result)
    return result, now


def gather_kernel(
    dims,
    parts,
    labels,
    modality,
    labeled,
    head_params,
    common_params,
    head_all,
    common_all,
    head_low,
    common_low,
    common_wide,
    send_sem,
    recv_sem,
    own_sem,
):
    me = my_place(dims)
    my_head = head_of(dims, me)
    n_head = dims[2] * dims[3]
    shard_rows, common_rows = head_params.shape[0], common_params.shape[0]
    per_head = labels.shape[0] // n_head
    row = lax.broadcasted_iota(jnp.int32, labels.shape, 0)
    mine = (row >= my_head * per_head) & (row < (my_head + 1) * per_head) & (labeled[...] == 1)
    lane = lax.broadcasted_iota(jnp.int32, (1, LANES), 1)
    counts = jnp.zeros((1, LANES), jnp.float32)
    for m in range(MODES):
        member = jnp.where(mine & (modality[...] == m), 1.0, 0.0)
        counts = counts + jnp.where(lane == m, jnp.sum(member, (0, 1), keepdims=True), 0.0)
    padding = head_low.shape[0] - shard_rows
    tail = shard_rows // TILE * TILE
    head_low[:tail] = head_params[:tail].astype(low)
    last = [jnp.broadcast_to(counts, (padding, LANES))]
    if shard_rows > tail:
        last = [head_params[tail:]] + last
    head_low[tail:] = jnp.concatenate(last, 0).astype(low)
    common_wide[...] = jnp.zeros(common_wide.shape, jnp.float32)
    common_wide[:common_rows] = common_params[...]
    piece = common_low.shape[0]
    common_low[...] = common_wide[pl.ds(pl.multiple_of(my_head * piece, TILE), piece)].astype(low)

    greet(dims, me, ring_and_others(dims))
    srcs, outs = (head_low, common_low), (head_all, common_all)
    copies = {}

    def block(p, offset):
        place = shifted(dims, me, offset, -1)
        array, first, rows, order = parts[p]
        return outs[array].at[blk_of(dims, place), head_of(dims, place), pl.ds(first, rows)]

    own = []
    for is_send, (rank, axis, p, offset) in gather_order(dims, parts)[0]:
        if is_send:
            step = 1 if axis == RING else offset[axis]
            before = with_at(offset, axis, offset[axis] - step)
            array, first, rows, order = parts[p]
            source = block(p, before) if any(before) else srcs[array].at[pl.ds(first, rows)]
            i = len(copies)
            copies[(p, offset)] = remote(
                source,
                block(p, before),
                send_sem.at[i],
                recv_sem.at[i],
                shifted(dims, me, along(axis, step), 1),
                dims,
            )
            copies[(p, offset)].start()
        else:
            if not own:
                for array in range(2):
                    copy = pltpu.make_async_copy(
                        srcs[array], outs[array].at[blk_of(dims, me), my_head], own_sem.at[array]
                    )
                    copy.start()
                    own.append(copy)
            copies[(p, offset)].wait_recv()
    for copy in copies.values():
        copy.wait_send()
    for copy in own:
        copy.wait()


def ring_and_others(dims):
    ring = {along(RING, 1 % dims[RING]), along(RING, (dims[RING] - 1) % dims[RING])}
    return sorted(ring - {(0, 0, 0, 0)}) + axis_peers(dims, (1, 2, 3))


def cut(array, rows, shares):
    result = []
    first, so_far = 0, 0
    whole = sum(share for share, order in shares)
    for share, order in shares:
        so_far += share
        end = rows * so_far // whole // TILE * TILE if so_far < whole else rows
        if end > first:
            result.append((array, first, end - first, order))
        first = end
    return tuple(result)


ZYXC, ZXYC, YXZC, XYZC = (0, 1, 2, 3), (0, 2, 1, 3), (1, 2, 0, 3), (2, 1, 0, 3)
GATHER_SHARES = ((8, ZYXC), (6, ZXYC), (2, YXZC), (2, XYZC))
REDUCE_SHARES = ((7, ZYXC), (7, ZXYC), (2, YXZC), (2, XYZC))


def gather_all(dims, marks, params, rows, collective_id):
    z, y, x, cores = dims
    parts = cut(0, rows[0], GATHER_SHARES) + cut(1, rows[1], ((1, ZXYC),))
    count = len(parts) * (z * y * x * cores - 1)
    return pl.pallas_call(
        functools.partial(gather_kernel, dims, parts),
        out_shape=[shape_of((z * y, x * cores, n, LANES)) for n in rows],
        in_specs=[VMEM_SPEC] * 5,
        out_specs=[ANY_SPEC] * 2,
        scratch_shapes=[pltpu.VMEM((n, LANES), low) for n in rows]
        + [
            pltpu.VMEM((x * cores * rows[1], LANES), jnp.float32),
            pltpu.SemaphoreType.DMA((count,)),
            pltpu.SemaphoreType.DMA((count,)),
            pltpu.SemaphoreType.DMA((2,)),
        ],
        compiler_params=pltpu.CompilerParams(collective_id=collective_id, has_side_effects=True),
        name="gather_weights",
    )(*marks, *params)


def reduce_order(dims, parts):
    ready, arrived, order = set(), set(), []

    def message(p, position, offset):
        z = offset[RING]
        rank = (dims[RING] - z if z else dims[RING], position, tuple(-o for o in offset), p)
        return (rank, parts[p][3][position], p, position, offset)

    def done(p, position, offset):
        ready.add((p, position, offset))
        if position == 4:
            return []
        axis = parts[p][3][position]
        d = offset[axis]
        first = d != 0 and (axis != RING or d == dims[axis] - 1)
        return ([message(p, position, offset)] if first else []) + advance(p, position, offset)

    def advance(p, position, offset):
        axis = parts[p][3][position]
        n = dims[axis]
        start = with_at(offset, axis, 0)
        if axis == RING:
            here = (p, position, offset)
            if here in ready and here in arrived:
                order.append((None, here))
                if offset[axis]:
                    return [message(p, position, offset)]
                return done(p, position + 1, offset)
        elif (p, position, start) in ready and (p, position + 1, start) not in ready:
            if all((p, position, with_at(start, axis, d)) in arrived for d in range(1, n)):
                order.append((None, (p, position, start)))
                return done(p, position + 1, start)
        return []

    def follow(sent):
        rank, axis, p, position, offset = sent
        here = with_at(offset, axis, offset[axis] - 1) if axis == RING else offset
        arrived.add((p, position, here))
        return advance(p, position, here)

    first = []
    for p in range(len(parts)):
        for offset in all_offsets(dims, range(4)):
            first += done(p, 0, offset)
    now = in_order(first, follow, lambda m: time_of(parts[m[2]][2], m[1]), AHEAD, order)
    return order, now


def all_offsets(dims, axes):
    offsets = [(0, 0, 0, 0)]
    for a in axes:
        offsets = [with_at(o, a, d) for o in offsets for d in range(dims[a])]
    return offsets


def reduce_kernel(dims, parts, *refs):
    srcs, tile = refs[:2], refs[2]
    head_out, common_out, losses, norm, factor = refs[3:8]
    places = len(parts) * 4
    buffers = refs[8 : 8 + places]
    head_sum, common_sum, shares, send_sem, recv_sem, near_tiles, far_tiles = refs[8 + places :]
    sums = (head_sum, common_sum)
    me = my_place(dims)
    z, y, x, cores = dims
    across = peers_across(dims)
    others = [o for o in all_offsets(dims, (0, 1)) if any(o)]
    met = ring_and_others(dims)
    greet(dims, me, met + [o for o in across + others if o not in met])
    push = Pushes(dims, me, send_sem, recv_sem)
    copies = {}

    def slot(p, position, offset):
        order = parts[p][3]
        axis = order[position]
        rest = [o for o in all_offsets(dims, order[position + 1 :])]
        k = rest.index(with_at(offset, axis, 0))
        return buffers[p * 4 + position].at[k, max(offset[axis] - 1, 0)]

    def summed(p, position, offset):
        array, first, rows, order = parts[p]
        if position == 0:
            place = shifted(dims, me, offset, 1)
            return srcs[array].at[blk_of(dims, place), head_of(dims, place), pl.ds(first, rows)]
        return slot(p, position - 1, offset)

    def ring_slot(p, position, offset):
        axis = parts[p][3][position]
        return slot(p, position, with_at(offset, axis, offset[axis] + 1))

    def add(p, position, offset):
        array, first, rows, order = parts[p]
        axis = order[position]
        if axis == RING:
            arrivals = [ring_slot(p, position, offset)]
        else:
            arrivals = [slot(p, position, with_at(offset, axis, d)) for d in range(1, dims[axis])]
        mine = summed(p, position, offset)
        step = row_chunk(rows)

        @pl.loop(0, rows // step)
        def some_rows(n):
            at = pl.ds(pl.multiple_of(n * step, step), step)
            total = mine[at].astype(jnp.float32)
            for arrival in arrivals:
                total = total + arrival[at].astype(jnp.float32)
            if position == 3 and not any(offset):
                sums[array][pl.ds(pl.multiple_of(first + n * step, TILE), step)] = total
            else:
                arrivals[0][at] = total.astype(low)

    for is_send, what in reduce_order(dims, parts)[0]:
        if is_send is None:
            add(*what)
        elif is_send:
            rank, axis, p, position, offset = what
            d = offset[axis]
            started = axis != RING or d == dims[axis] - 1
            source = summed(p, position, offset) if started else ring_slot(p, position, offset)
            step = along(axis, 1 if axis == RING else d)
            copies[what] = push(source, slot(p, position, offset), step)
        else:
            copies[what].wait_recv()
    my_head, my_blk = head_of(dims, me), blk_of(dims, me)
    shares[my_head] = common_sum[...].astype(low)
    share_copies = [push(shares.at[my_head], shares.at[my_head], o) for o in across]
    amount = head_out.shape[0]
    head_out[...] = head_sum[:amount]
    squares = jnp.sum(head_sum[:amount] * head_sum[:amount], 0, keepdims=True)
    squares = squares + jnp.sum(common_sum[...] * common_sum[...], 0, keepdims=True)
    lane = lax.broadcasted_iota(jnp.int32, (1, LANES), 1)
    near_tiles[my_head] = tile[...] + jnp.where(
        lane == MODES, jnp.sum(squares, 1, keepdims=True), 0.0
    )
    near = [push(near_tiles.at[my_head], near_tiles.at[my_head], o) for o in across]
    for copy in near:
        copy.wait_recv()
    far_tiles[my_blk] = jnp.sum(near_tiles[...], 0)
    far = [push(far_tiles.at[my_blk], far_tiles.at[my_blk], o) for o in others]
    for copy in share_copies:
        copy.wait_recv()
    piece = shares.shape[1]
    for k in range(x * cores):
        amount = min(piece, common_out.shape[0] - k * piece)
        common_out[k * piece : k * piece + amount] = shares[k].astype(jnp.float32)[:amount]
    for copy in far:
        copy.wait_recv()
    totals = jnp.sum(far_tiles[...], 0)[:1]
    losses[...] = totals[:, :MODES]
    norm[...] = jnp.sqrt(totals[:, MODES : MODES + 1])
    factor[...] = jnp.minimum(1.0, clip_limit / norm[...])
    push.finish()


def row_chunk(rows):
    for count in (4, 3, 2):
        if rows % (count * TILE) == 0:
            return rows // count
    return rows


def reduce_all(dims, arrays, valid, tile, collective_id):
    z, y, x, cores = dims
    rows = [array.shape[2] for array in arrays]
    parts = cut(0, rows[0], [(share, order[::-1]) for share, order in REDUCE_SHARES])
    parts = parts + cut(1, rows[1], ((1, ZXYC[::-1]),))
    scratch = []
    for array, first, amount, order in parts:
        for position, axis in enumerate(order):
            rest = len(all_offsets(dims, order[position + 1 :]))
            scratch.append(pltpu.VMEM((rest, dims[axis] - 1, amount, LANES), low))
    count = len(parts) * (z * y * x * cores - 1) + 2 * (x * cores - 1) + z * y - 1
    return pl.pallas_call(
        functools.partial(reduce_kernel, dims, parts),
        out_shape=[
            shape_of((valid[0], LANES), jnp.float32),
            shape_of((valid[1], LANES), jnp.float32),
            shape_of((1, MODES), jnp.float32),
            shape_of((1, 1), jnp.float32),
            shape_of((1, 1), jnp.float32),
        ],
        in_specs=[VMEM_SPEC] * 3,
        out_specs=[VMEM_SPEC] * 5,
        scratch_shapes=scratch
        + [pltpu.VMEM((n, LANES), jnp.float32) for n in rows]
        + [
            pltpu.VMEM((x * cores, rows[1], LANES), low),
            pltpu.SemaphoreType.DMA((count,)),
            pltpu.SemaphoreType.DMA((count,)),
            pltpu.VMEM((x * cores, 8, LANES), jnp.float32),
            pltpu.VMEM((z * y, 8, LANES), jnp.float32),
        ],
        compiler_params=pltpu.CompilerParams(
            collective_id=collective_id, has_side_effects=True, vmem_limit_bytes=60 * MIB
        ),
        name="reduce_gradients",
    )(*arrays, tile)


def contract_first(a, b):
    return lax.dot_general(a, b, (((0,), (0,)), ((), ())), preferred_element_type=jnp.float32)


def product(a, b):
    return jnp.dot(a, b, preferred_element_type=jnp.float32)


def against(a, b):
    return lax.dot_general(a, b, (((1,), (1,)), ((), ())), preferred_element_type=jnp.float32)


def clip_bounds(lengths):
    result, first = [], 0
    for clip in range(lengths.shape[0]):
        end = first + lengths[clip]
        result.append((first, end))
        first = end
    return result


def clip_borders(bounds, place):
    opening = jnp.zeros(place.shape, jnp.int32)
    ending = jnp.full(place.shape, 1 << 30, jnp.int32)
    for clip, (begin, end) in enumerate(bounds):
        here = place == clip
        opening = jnp.where(here, begin, opening)
        ending = jnp.where(here, end, ending)
    return opening, ending


def low_half(axis):
    return lax.broadcasted_iota(jnp.int32, (1, LANES) if axis else (LANES, 1), axis) < HD


def with_key_tail(bounds, first_row, kv):
    clips = len(bounds)
    place = lax.broadcasted_iota(jnp.int32, (1, LANES), 1) - HD
    opening, ending = clip_borders(bounds, place)
    ones = jnp.where((place >= clips) & (place < clips + 3), 1.0, 0.0)
    row = first_row + lax.broadcasted_iota(jnp.int32, kv.shape, 0)
    tail = jnp.where((row >= opening) & (row < ending), ones, big_negative)
    return jnp.where(low_half(1), kv.astype(jnp.float32), tail).astype(low)


def with_value_tail(kv):
    place = lax.broadcasted_iota(jnp.int32, (1, LANES), 1)
    ones = jnp.where(place < 3, 1.0, 0.0)
    return jnp.where(low_half(1), ones, kv.astype(jnp.float32)).astype(low)


def in_three(place, value):
    top = value.astype(low).astype(jnp.float32)
    middle = (value - top).astype(low).astype(jnp.float32)
    bottom = value - top - middle
    return (
        jnp.where(place == 0, top, 0.0)
        + jnp.where(place == 1, middle, 0.0)
        + jnp.where(place == 2, bottom, 0.0)
    )


def with_query_tail(bounds, first_row, rows, extra):
    clips = len(bounds)
    place = lax.broadcasted_iota(jnp.int32, (HD, 1), 0)
    opening, ending = clip_borders(bounds, place)
    row = first_row + lax.broadcasted_iota(jnp.int32, (1, rows.shape[1]), 1)
    inside = (place < clips) & (row >= opening) & (row < ending)
    tail = jnp.where(inside, 1.0, 0.0)
    if extra is not None:
        tail = tail + in_three(place - clips, -extra)
    return jnp.concatenate([rows * (SCORE_SCALE * LOG2E), tail], 0).astype(low)


def pack(rows):
    half = rows.shape[0] // 2
    return jnp.concatenate([rows[:half], rows[half:]], 1)


def unpack(packed):
    return jnp.concatenate([packed[:, :HD], packed[:, HD:]], 0)


def unpack_t(packed):
    turned = packed.astype(jnp.float32).T
    return jnp.concatenate([turned[:HD], turned[HD:]], 1)


def pack_t(columns):
    half = columns.shape[1] // 2
    return jnp.concatenate([columns[:, :half], columns[:, half:]], 0).T


class Team:
    def __init__(self, dims):
        z, y, x, cores = dims
        self.dims = dims
        self.wide = HEADS // (x * cores) == y
        self.size = x * cores * (y if self.wide else 1)
        self.groups = z if self.wide else z * y
        axes = (1, 2, 3) if self.wide else (2, 3)
        offsets = [o for o in all_offsets(dims, axes) if any(o)]
        self.others = sorted(offsets, key=lambda o: (o[1] + o[2], o))
        self.sides = [] if self.wide else axis_peers(dims, (1,))

    def slot(self, place):
        head = head_of(self.dims, place)
        return place[1] * self.dims[2] * self.dims[3] + head if self.wide else head

    def group(self, place):
        return place[0] if self.wide else blk_of(self.dims, place)


def heads_of(n_head, slots):
    return [(s % n_head, s // n_head) for s in range(slots)]


class Pushes:
    def __init__(self, dims, me, send_sem, recv_sem):
        self.dims, self.me, self.send_sem, self.recv_sem = dims, me, send_sem, recv_sem
        self.started = []

    def __call__(self, src, dst, offset):
        i = len(self.started)
        place = shifted(self.dims, self.me, offset, 1)
        copy = remote(src, dst, self.send_sem.at[i], self.recv_sem.at[i], place, self.dims)
        copy.start()
        self.started.append(copy)
        return copy

    def finish(self):
        for copy in self.started:
            copy.wait_send()


def peers_across(dims):
    z, y, x, cores = dims
    across = [(0, 0, a, c) for a in range(x) for c in range(cores) if (a, c) != (0, 0)]
    return sorted(across, key=lambda o: (o[2] == 0, o[3]))


def attend_kernel(
    team,
    query_step,
    key_step,
    lengths,
    q_in,
    kv_in,
    o_out,
    lse,
    out_t,
    q_all,
    kv_all,
    keys,
    values_t,
    queries,
    top,
    accum,
    o_mine,
    send_sem,
    recv_sem,
    own_sem,
):
    dims = team.dims
    z = dims[0]
    me = my_place(dims)
    bounds = clip_bounds(lengths)
    rows = kv_in.shape[1]
    amount = team.size * rows
    my_group, my_slot = team.group(me), team.slot(me)
    ring_ends = sorted({along(0, 1 % z), along(0, (z - 1) % z)} - {(0, 0, 0, 0)})
    greet(dims, me, team.others + ring_ends + team.sides)
    push = Pushes(dims, me, send_sem, recv_sem)
    own_kv = pltpu.make_async_copy(kv_in.at[my_slot], kv_all.at[my_group, my_slot], own_sem.at[0])
    own_q = pltpu.make_async_copy(q_in.at[my_slot], q_all.at[my_slot], own_sem.at[1])
    own_kv.start()
    own_q.start()

    def to_team(src, dst, o):
        return push(src.at[team.slot(shifted(dims, me, o, 1))], dst, o)

    kv_copies = {o: to_team(kv_in, kv_all.at[my_group, my_slot], o) for o in team.others}
    q_copies = [to_team(q_in, q_all.at[my_slot], o) for o in team.others]
    ring, side = {}, {}

    def group_at(offset):
        return team.group(shifted(dims, me, offset, -1))

    def send_piece(o):
        block = kv_all.at[my_group, team.slot(shifted(dims, me, o, -1))]
        if z > 1:
            ring.setdefault(1, []).append(push(block, block, along(0, 1)))

    def send_on(s):
        block = kv_all.at[group_at(along(0, s))]
        if 0 < s < z - 1:
            ring[s + 1] = [push(block, block, along(0, 1))]
        for o in team.sides:
            side[(s, o)] = push(block, block, o)

    def compute(offset):
        group = group_at(offset)

        @pl.loop(0, team.size)
        def build(n):
            at = pl.ds(pl.multiple_of(n * rows, rows), rows)
            block = kv_all[group, n]
            keys[at, :] = with_key_tail(bounds, group * amount + n * rows, block)
            values_t[:HD, at] = block.astype(jnp.float32).T[HD:].astype(low)

        @pl.loop(0, amount // (2 * query_step))
        def query_blocks(n):
            for half in range(2):
                at = pl.ds(pl.multiple_of((2 * n + half) * query_step, query_step), query_step)
                query = queries[:, at]
                old, total = top[:, at], accum[:, at]
                for k in range(0, amount, key_step):
                    scores = product(keys[k : k + key_step, :], query)
                    new = jnp.maximum(old, jnp.max(scores, 0, keepdims=True))
                    probs = jnp.exp2(scores - new).astype(low)
                    total = total * jnp.exp2(old - new) + product(values_t[:, k : k + key_step], probs)
                    old = new
                top[:, at] = old
                accum[:, at] = total

    values_t[HD:, :] = jnp.ones((TILE, amount), low)
    top[...] = jnp.full(top.shape, -1e38, jnp.float32)
    accum[...] = jnp.zeros(accum.shape, jnp.float32)
    own_kv.wait()
    send_piece((0, 0, 0, 0))
    for o in team.others:
        kv_copies[o].wait_recv()
        send_piece(o)
    send_on(0)
    own_q.wait()
    for copy in q_copies:
        copy.wait_recv()
    for n in range(team.size):
        queries[:, n * rows : (n + 1) * rows] = with_query_tail(
            bounds, my_group * amount + n * rows, unpack_t(q_all[n]), None
        )
    compute((0, 0, 0, 0))
    for s in range(1, z + 1):
        if s < z:
            for copy in ring[s]:
                copy.wait_recv()
            send_on(s)
            compute(along(0, s))
        for o in team.sides:
            side[(s - 1, o)].wait_recv()
            compute((s - 1, o[1], 0, 0))
    total = accum[HD : HD + 1, :]
    out_t[...] = accum[:HD, :] / total
    lse[...] = top[...] + jnp.log(total) * LOG2E
    for n in range(team.size):
        o_mine[n] = pack_t(out_t[:, n * rows : (n + 1) * rows]).astype(low)
    o_copies = [to_team(o_mine, o_out.at[my_slot], o) for o in team.others]
    own_o = pltpu.make_async_copy(o_mine.at[my_slot], o_out.at[my_slot], own_sem.at[2])
    own_o.start()
    own_o.wait()
    for copy in o_copies:
        copy.wait_recv()
    push.finish()


def attend(dims, lengths, q, kv, collective_id):
    team = Team(dims)
    z = dims[0]
    amount = team.size * kv.shape[1]
    count = 3 * (team.size - 1) + team.size + z + z * len(team.sides)
    return pl.pallas_call(
        functools.partial(attend_kernel, team, 256, 1024),
        out_shape=(
            jax.ShapeDtypeStruct(q.shape, low),
            jax.ShapeDtypeStruct((1, amount), jnp.float32),
            jax.ShapeDtypeStruct((HD, amount), jnp.float32),
            jax.ShapeDtypeStruct(q.shape, low),
            jax.ShapeDtypeStruct((team.groups,) + kv.shape, low),
        ),
        in_specs=[SMEM_SPEC, VMEM_SPEC, VMEM_SPEC],
        out_specs=[VMEM_SPEC] * 5,
        scratch_shapes=[
            pltpu.VMEM((amount, LANES), low),
            pltpu.VMEM((HD + TILE, amount), low),
            pltpu.VMEM((LANES, amount), low),
            pltpu.VMEM((1, amount), jnp.float32),
            pltpu.VMEM((HD + TILE, amount), jnp.float32),
            pltpu.VMEM(q.shape, low),
            pltpu.SemaphoreType.DMA((count,)),
            pltpu.SemaphoreType.DMA((count,)),
            pltpu.SemaphoreType.DMA((3,)),
        ],
        compiler_params=pltpu.CompilerParams(
            collective_id=collective_id, has_side_effects=True, vmem_limit_bytes=56 * MIB
        ),
        name="attend",
    )(lengths, q, kv)


def attend_back_kernel(
    team,
    key_step,
    pieces,
    lengths,
    q_all,
    kv_all,
    do_in,
    out_t,
    lse,
    d_q_out,
    d_kv_out,
    do_all,
    keys,
    keys_t,
    values,
    queries,
    douts,
    d_q_t,
    q_rows,
    do_rows,
    side_out,
    side_in,
    ring_out,
    ring_in,
    mine,
    d_q_mine,
    d_kv_mine,
    send_sem,
    recv_sem,
    own_sem,
):
    dims = team.dims
    z = dims[0]
    me = my_place(dims)
    bounds = clip_bounds(lengths)
    rows = kv_all.shape[2]
    amount = team.size * rows
    slots = team.size // pieces
    piece_rows = slots * rows
    my_group, my_slot = team.group(me), team.slot(me)
    ring_ends = sorted({along(0, 1 % z), along(0, (z - 1) % z)} - {(0, 0, 0, 0)})
    greet(dims, me, team.others + ring_ends + team.sides)
    push = Pushes(dims, me, send_sem, recv_sem)

    def to_team(src, dst, o):
        return push(src.at[team.slot(shifted(dims, me, o, 1))], dst, o)

    do_copies = [to_team(do_in, do_all.at[my_slot], o) for o in team.others]
    own_do = pltpu.make_async_copy(do_in.at[my_slot], do_all.at[my_slot], own_sem.at[0])
    own_do.start()
    place = lax.broadcasted_iota(jnp.int32, (HD, 1), 0)
    for n in range(team.size):
        at = slice(n * rows, (n + 1) * rows)
        q_t = unpack_t(q_all[n])
        queries[:, at] = with_query_tail(bounds, my_group * amount + n * rows, q_t, lse[:, at])
        q_rows[:, at] = (q_t * SCORE_SCALE).astype(low)
    d_q_t[...] = jnp.zeros(d_q_t.shape, jnp.float32)
    own_do.wait()
    for copy in do_copies:
        copy.wait_recv()
    for n in range(team.size):
        at = slice(n * rows, (n + 1) * rows)
        do_t = unpack_t(do_all[n])
        delta = jnp.sum(do_t * out_t[:, at], 0, keepdims=True)
        douts[:, at] = jnp.concatenate([in_three(place, -delta), do_t], 0).astype(low)
        do_rows[:, at] = do_t.astype(low)

    def compute(offset, piece, target):
        group = team.group(shifted(dims, me, offset, 1))

        @pl.loop(0, slots)
        def build(n):
            at = pl.ds(pl.multiple_of(n * rows, rows), rows)
            slot = piece * slots + n
            block = kv_all[group, slot]
            keys[at, :] = with_key_tail(bounds, group * amount + slot * rows, block)
            keys_t[:, at] = block.astype(jnp.float32).T[:HD].astype(low)
            values[at, :] = with_value_tail(block)

        @pl.loop(0, piece_rows // key_step)
        def key_block(k):
            at = pl.ds(pl.multiple_of(k * key_step, key_step), key_step)
            d_key = jnp.zeros((HD, key_step), jnp.float32)
            d_value = jnp.zeros((HD, key_step), jnp.float32)
            for half in (slice(0, amount // 2), slice(amount // 2, amount)):
                probs = jnp.exp2(product(keys[at, :], queries[:, half]))
                d_probs = product(values[at, :], douts[:, half])
                d_scores = (probs * d_probs).astype(low)
                d_value = d_value + against(do_rows[:, half], probs.astype(low))
                d_key = d_key + against(q_rows[:, half], d_scores)
                d_q_t[:, half] = d_q_t[:, half] + product(keys_t[:, at], d_scores)
            target[at, :] = jnp.concatenate([d_key, d_value], 0).T.astype(target.dtype)

    side, ring = {}, {}

    def send_sides(s, piece):
        for o in team.sides:
            target = side_out.at[s - 1, o[1] - 1, piece]
            compute((z - s, o[1], 0, 0), piece, target)
            side[(s, o, piece)] = push(target, side_in.at[s - 1, o[1] - 1, piece], o)

    def combine(s, piece):
        for o in team.sides:
            side[(s, o, piece)].wait_recv()
        if s > 1:
            ring[(s - 1, piece)].wait_recv()
        for n in range(slots):
            at = slice(n * rows, (n + 1) * rows)
            total = mine[piece, at, :]
            for o in team.sides:
                total = total + side_in[s - 1, o[1] - 1, piece, at, :].astype(jnp.float32)
            if s > 1:
                total = total + ring_in[s - 2, piece, at, :].astype(jnp.float32)
            if s < z:
                ring_out[s - 1, piece, at, :] = total.astype(low)
            else:
                d_kv_mine[piece * slots + n] = total.astype(low)
        if s < z:
            ring[(s, piece)] = push(ring_out.at[s - 1, piece], ring_in.at[s - 1, piece], along(0, 1))

    for s in range(1, z + 1):
        for piece in range(pieces):
            send_sides(s, piece)
            compute((z - s if s < z else 0, 0, 0, 0), piece, mine.at[piece])
            if team.sides or s < z:
                combine(s, piece)
    for n in range(team.size):
        at = slice(n * rows, (n + 1) * rows)
        d_q_mine[n] = pack_t(d_q_t[:, at] * SCORE_SCALE).astype(low)
    copies = [to_team(d_q_mine, d_q_out.at[my_slot], o) for o in team.others]
    own_q = pltpu.make_async_copy(d_q_mine.at[my_slot], d_q_out.at[my_slot], own_sem.at[1])
    own_q.start()
    if not team.sides:
        for piece in range(pieces):
            combine(z, piece)
    copies += [to_team(d_kv_mine, d_kv_out.at[my_slot], o) for o in team.others]
    own_kv = pltpu.make_async_copy(d_kv_mine.at[my_slot], d_kv_out.at[my_slot], own_sem.at[2])
    own_kv.start()
    own_q.wait()
    own_kv.wait()
    for copy in copies:
        copy.wait_recv()
    push.finish()


def attend_back(dims, lengths, q, kv, dout, out_t, lse, collective_id):
    team = Team(dims)
    z = dims[0]
    rows = kv.shape[2]
    amount = team.size * rows
    pieces = 2
    piece = (pieces, amount // pieces, LANES)
    count = 3 * (team.size - 1) + pieces * (z + z * len(team.sides))
    others = max(len(team.sides), 1)
    ring_steps, side_steps = max(z - 1, 1), z if team.sides else 1
    return pl.pallas_call(
        functools.partial(attend_back_kernel, team, 256, pieces),
        out_shape=(
            jax.ShapeDtypeStruct(q.shape, low),
            jax.ShapeDtypeStruct(kv.shape[1:], low),
        ),
        in_specs=[SMEM_SPEC] + [VMEM_SPEC] * 5,
        out_specs=[VMEM_SPEC] * 2,
        scratch_shapes=[
            pltpu.VMEM(q.shape, low),
            pltpu.VMEM((amount // pieces, LANES), low),
            pltpu.VMEM((HD, amount // pieces), low),
            pltpu.VMEM((amount // pieces, LANES), low),
            pltpu.VMEM((LANES, amount), low),
            pltpu.VMEM((LANES, amount), low),
            pltpu.VMEM((HD, amount), jnp.float32),
            pltpu.VMEM((HD, amount), low),
            pltpu.VMEM((HD, amount), low),
            pltpu.VMEM((side_steps, others) + piece, low),
            pltpu.VMEM((side_steps, others) + piece, low),
            pltpu.VMEM((ring_steps,) + piece, low),
            pltpu.VMEM((ring_steps,) + piece, low),
            pltpu.VMEM(piece, jnp.float32),
            pltpu.VMEM(q.shape, low),
            pltpu.VMEM(kv.shape[1:], low),
            pltpu.SemaphoreType.DMA((count,)),
            pltpu.SemaphoreType.DMA((count,)),
            pltpu.SemaphoreType.DMA((3,)),
        ],
        compiler_params=pltpu.CompilerParams(
            collective_id=collective_id, has_side_effects=True, vmem_limit_bytes=60 * MIB
        ),
        name="attend_back",
    )(lengths, q, kv, dout, out_t, lse)


def part_shapes(n_head):
    width = HEADS // n_head * HD
    hidden = FF // n_head
    return (
        (D, width, True),
        (DI, 2 * width, True),
        (width, D, False),
        (D, 3 * width, True),
        (width, D, False),
        (D, hidden, True),
        (hidden, D, False),
        (D, C // n_head, True),
    )


def borders(n_head):
    result = [0]
    for rows, columns, joined in part_shapes(n_head):
        result.append(result[-1] + rows * columns // LANES)
    return result


def period(columns):
    amount = 1
    while amount * columns % LANES:
        amount *= 2
    return amount


def segments(start, amount, unit):
    result = []
    while amount > 0:
        which, at = divmod(start, unit)
        size = min(unit - at, amount)
        result.append((which, at, at + size))
        start, amount = start + size, amount - size
    return result


def joined_lanes(pieces):
    return pieces[0] if len(pieces) == 1 else jnp.concatenate(pieces, 1)


def lane_blocks(value):
    rows, columns = value.shape
    missing = -columns % LANES
    if missing:
        value = jnp.concatenate([value, jnp.zeros((rows, missing), value.dtype)], 1)
    return [value[:, i : i + LANES] for i in range(0, columns + missing, LANES)]


def every(first, amount, stride):
    return pl.ds(first, amount) if stride == 1 else pl.ds(first, amount, stride=stride)


def matrix_of(stage, first, rows, columns, line):
    if columns % LANES == 0:
        stride = columns // LANES
        for j in range(stride):
            yield j * LANES, stage[every(first + j, rows, stride), :]
        return
    height = period(columns)
    stride = height * columns // LANES
    for k in range(height):
        pieces = [
            stage[every(first + which, rows // height, stride), :][:, begin:end]
            for which, begin, end in segments(k * columns, columns, LANES)
        ]
        for i, piece in enumerate(lane_blocks(joined_lanes(pieces))):
            line[i, every(k, rows // height, height), :] = piece
    for i in range(-(-columns // LANES)):
        yield i * LANES, line[i, :rows, : min(columns - i * LANES, LANES)]


def matrix_into(stage, first, value, line):
    rows, columns = value.shape
    if columns % LANES == 0:
        stride = columns // LANES
        for j in range(stride):
            stage[every(first + j, rows, stride), :] = value[:, j * LANES : (j + 1) * LANES]
        return
    height = period(columns)
    stride = height * columns // LANES
    for i, piece in enumerate(lane_blocks(value)):
        line[i, :rows, :] = piece
    for i in range(stride):
        pieces = [
            line[which, every(k, rows // height, height), :][:, begin:end]
            for k, first_lane, last_lane in segments(i * LANES, LANES, columns)
            for which, begin, end in segments(first_lane, last_lane - first_lane, LANES)
        ]
        stage[every(first + i, rows // height, stride), :] = joined_lanes(pieces)


def load_stage(stage, held, first_shard, shard_rows, group):
    for b in range(held.shape[0]):
        stage[pl.ds(b * shard_rows, shard_rows), :] = held[b, group, :shard_rows, :].astype(jnp.float32)


def load_common(stage, held, valid):
    piece = held.shape[2]
    for b in range(held.shape[0]):
        for k in range(held.shape[1]):
            amount = min(piece, valid - k * piece)
            stage[b * valid + k * piece : b * valid + k * piece + amount, :] = held[b, k].astype(
                jnp.float32
            )[:amount]


def common_blocks(first_row, last_row, valid):
    return first_row // valid, -(-last_row // valid) - first_row // valid


def load_matrices(stage, first_row, n_head, group, which, targets, line):
    starts, shapes = borders(n_head), part_shapes(n_head)
    for m, target in zip(which, targets):
        rows, columns, joined = shapes[m]
        row = 0 if joined else group * rows
        column = group * columns if joined else 0
        for j, value in matrix_of(stage, starts[m] - first_row, rows, columns, line):
            size = value.shape[1]
            target[row : row + rows, column + j : column + j + size] = value.astype(target.dtype)


def normalized(x):
    centre = x - jnp.mean(x, -1, keepdims=True)
    rate = lax.rsqrt(jnp.mean(centre * centre, -1, keepdims=True) + norm_eps)
    return centre * rate, rate


def layer_norm(x, gain):
    return normalized(x)[0] * gain


def norm_pullback(x, gain, grad):
    unit, rate = normalized(x)
    inside = grad * gain
    both = jnp.mean(inside * unit, -1, keepdims=True)
    d_x = rate * (inside - jnp.mean(inside, -1, keepdims=True) - unit * both)
    return d_x, jnp.sum(grad * unit, 0, keepdims=True)


def head_lanes(group, heads, value):
    width = heads * HD
    block = value[:, group * width : (group + 1) * width]
    lane = lax.broadcasted_iota(jnp.int32, (1, width), 1)
    result = []
    for a in range(heads):
        here = (lane >= a * HD) & (lane < (a + 1) * HD)
        result.append((here, jnp.where(here, block, jnp.zeros_like(block))))
    return result


def place_of(bounds, first, amount):
    row = first + lax.broadcasted_iota(jnp.int32, (amount, 1), 0)
    opening = jnp.zeros((amount, 1), jnp.int32)
    for begin, end in bounds:
        opening = jnp.where((row >= begin) & (row < end), begin, opening)
    offset = row - opening
    turns = jnp.floor((offset.astype(jnp.float32) + 0.5) * (1.0 / LAT)).astype(jnp.int32)
    return offset - turns * LAT


def picked_rows(bounds, rows, n_head):
    first = lax.axis_index("blk") * (rows * n_head) + lax.axis_index("head") * rows
    lane = lax.broadcasted_iota(jnp.int32, (rows, LAT), 1)
    return jnp.where(lane == place_of(bounds, first, rows), 1.0, 0.0).astype(low)


def enc_scores(q_head, keys):
    return against(q_head, keys) * (SCORE_SCALE * LOG2E)


def encode_kernel(
    n_head,
    shard_rows,
    valid,
    rows,
    lengths,
    weights,
    common,
    inputs_t,
    enc_query,
    enc_keyval,
    enc_output,
    self_project,
    gains,
    z_zero,
    h_zero,
    x_norm_t,
    q_enc,
    kv_enc,
    o_enc,
    z_one,
    h_one,
    q_self,
    kv_self,
    counts,
    label_counts,
    held,
    held_common,
    held_counts,
    stage,
    stage_common,
    line,
    latent_table,
    sems,
):
    heads = HEADS // n_head
    width = heads * HD
    shards = held.shape[0]
    bounds = clip_bounds(lengths)
    first = DQ * D // LANES
    block, blocks = common_blocks(first, first + (LAT + 4) * D // LANES, valid)
    tail = shard_rows // TILE * TILE
    copies = [
        pltpu.make_async_copy(common.at[pl.ds(block, blocks)], held_common, sems.at[0]),
        pltpu.make_async_copy(weights.at[pl.ds(0, shards)], held, sems.at[1]),
        pltpu.make_async_copy(weights.at[:, :, pl.ds(tail, TILE)], held_counts, sems.at[2]),
    ]
    for copy in copies:
        copy.start()
    centre = inputs_t[...].astype(jnp.float32)
    centre = centre - jnp.mean(centre, 0, keepdims=True)
    rate = lax.rsqrt(jnp.mean(centre * centre, 0, keepdims=True) + norm_eps)
    x_norm_t[...] = (centre * rate).astype(low)
    copies[0].wait()
    load_common(stage_common, held_common, valid)
    first = first - block * valid
    for j, value in matrix_of(stage_common, first, LAT, D, line):
        latent_table[:, j : j + LANES] = value.astype(low)
    for j, value in matrix_of(stage_common, first + LAT * D // LANES, 4, D, line):
        gains[:, j : j + LANES] = value
    picked = picked_rows(bounds, rows, n_head)
    z_zero[...] = product(picked, latent_table[...])
    h_zero[...] = layer_norm(z_zero[...], gains[0:1, :]).astype(low)
    copies[2].wait()
    counted = held_counts[...].astype(jnp.float32)[:, :, shard_rows - tail : shard_rows - tail + 1]
    counts[...] = jnp.broadcast_to(jnp.sum(counted, (0, 1)), counts.shape)
    label_counts[...] = counts[:1, :MODES]
    copies[1].wait()
    for g in range(n_head):
        load_stage(stage, held, 0, shard_rows, g)
        load_matrices(
            stage, 0, n_head, g, (0, 1, 2, 3), (enc_query, enc_keyval, enc_output, self_project), line
        )
    q_enc[...] = product(h_zero[...], enc_query[...]).astype(low)
    kv_enc[...] = contract_first(x_norm_t[...], enc_keyval[...]).astype(low)
    for g in range(n_head):
        keys = kv_enc[:, 2 * g * width : (2 * g + 1) * width]
        values = kv_enc[:, (2 * g + 1) * width : (2 * g + 2) * width]
        outcome = jnp.zeros((rows, width), jnp.float32)
        for here, q_head in head_lanes(g, heads, q_enc[...]):
            scores = enc_scores(q_head, keys)
            probs = jnp.exp2(scores - jnp.max(scores, 1, keepdims=True))
            total = jnp.sum(probs, 1, keepdims=True)
            outcome = jnp.where(here, product(probs.astype(low), values) / total, outcome)
        o_enc[:, g * width : (g + 1) * width] = outcome.astype(low)
    z_one[...] = z_zero[...] + product(o_enc[...], enc_output[...])
    h_one[...] = layer_norm(z_one[...], gains[1:2, :]).astype(low)
    projected = product(h_one[...], self_project[...]).astype(low)
    for slot, (g, a) in enumerate(heads_of(n_head, q_self.shape[0])):
        query, key, value = (
            projected[:, (3 * g + i) * width + a * HD : (3 * g + i) * width + (a + 1) * HD]
            for i in range(3)
        )
        q_self[slot] = pack(query)
        kv_self[slot] = jnp.concatenate([key, value], 1)


LINE = pltpu.VMEM((4, round_up(max(D, DI), 8), LANES), jnp.float32)


def shards_of(n_head, shard_rows, first, last):
    starts = borders(n_head)
    begin = starts[first] // shard_rows
    return begin, -(-starts[last] // shard_rows) - begin


def encode(lengths, weights, common, inputs_t, valid, rows, slots, n_head, shard_rows):
    begin, shards = shards_of(n_head, shard_rows, 0, 4)
    query_rows = DQ * D // LANES
    block, blocks = common_blocks(query_rows, query_rows + (LAT + 4) * D // LANES, valid)
    keys = inputs_t.shape[1]
    return pl.pallas_call(
        functools.partial(encode_kernel, n_head, shard_rows, valid, rows),
        out_shape=[
            shape_of((D, D)),
            shape_of((DI, 2 * D)),
            shape_of((D, D)),
            shape_of((D, 3 * D)),
            shape_of((4, D), jnp.float32),
            shape_of((rows, D), jnp.float32),
            shape_of((rows, D)),
            shape_of(inputs_t.shape),
            shape_of((rows, D)),
            shape_of((keys, 2 * D)),
            shape_of((rows, D)),
            shape_of((rows, D), jnp.float32),
            shape_of((rows, D)),
            shape_of((slots, rows // 2, LANES)),
            shape_of((slots, rows, LANES)),
            shape_of((8, LANES), jnp.float32),
            shape_of((1, MODES), jnp.float32),
        ],
        in_specs=[SMEM_SPEC, ANY_SPEC, ANY_SPEC, VMEM_SPEC],
        out_specs=[VMEM_SPEC] * 17,
        scratch_shapes=[
            pltpu.VMEM((shards,) + weights.shape[1:], low),
            pltpu.VMEM((blocks,) + common.shape[1:], low),
            pltpu.VMEM(weights.shape[:2] + (TILE, LANES), low),
            pltpu.VMEM((shards * shard_rows, LANES), jnp.float32),
            pltpu.VMEM((blocks * valid, LANES), jnp.float32),
            LINE,
            pltpu.VMEM((LAT, D), low),
            pltpu.SemaphoreType.DMA((3,)),
        ],
        compiler_params=pltpu.CompilerParams(vmem_limit_bytes=56 * MIB),
        name="encode",
    )(lengths, weights, common, inputs_t)


def gelu_and_slope(x):
    rate = (2.0 / jnp.pi) ** 0.5
    cubic = 0.044715
    t = jnp.tanh(rate * (x + cubic * x * x * x))
    slope = 0.5 * (1.0 + t) + 0.5 * x * (1.0 - t * t) * rate * (1.0 + 3.0 * cubic * x * x)
    return 0.5 * x * (1.0 + t), slope


def my_column(marks, rows):
    turned = marks[...].astype(jnp.float32).T
    column = lax.broadcasted_iota(jnp.int32, turned.shape, 1)
    per_head = rows // LANES
    first = lax.axis_index("head") * per_head
    picked = [
        jnp.sum(jnp.where(column == first + k, turned, 0.0), 1, keepdims=True)
        for k in range(per_head)
    ]
    return jnp.concatenate(picked, 0) if per_head > 1 else picked[0]


def middle_kernel(
    n_head,
    shard_rows,
    valid,
    first_shard,
    rows,
    counts,
    weights,
    common,
    z_one,
    o_self,
    out_queries_t,
    labels,
    modality,
    labeled,
    gains,
    dout,
    d_two_out,
    tile,
    query_grad,
    gain_grads,
    grads,
    held,
    held_common,
    stage,
    stage_common,
    line,
    self_output,
    hidden_in,
    hidden_out,
    class_table,
    query_table,
    slope,
    activ,
    sems,
):
    heads = HEADS // n_head
    width, hidden, classes = heads * HD, FF // n_head, C // n_head
    shards = held.shape[0]
    first_row = first_shard * shard_rows
    starts = borders(n_head)
    copies = [
        pltpu.make_async_copy(common.at[pl.ds(0, held_common.shape[0])], held_common, sems.at[0]),
        pltpu.make_async_copy(weights.at[pl.ds(first_shard, shards)], held, sems.at[1]),
    ]
    for copy in copies:
        copy.start()
    copies[0].wait()
    load_common(stage_common, held_common, valid)
    for j, value in matrix_of(stage_common, 0, DQ, D, line):
        query_table[:, j : j + LANES] = value.astype(low)
    copies[1].wait()
    for g in range(n_head):
        load_stage(stage, held, first_shard, shard_rows, g)
        load_matrices(
            stage, first_row, n_head, g, (4, 5, 6, 7), (self_output, hidden_in, hidden_out, class_table), line
        )
    gain_two, gain_three = gains[2:3, :], gains[3:4, :]
    o_heads = {head: unpack(o_self[s]) for s, head in enumerate(heads_of(n_head, o_self.shape[0]))}
    o_groups = [joined_lanes([o_heads[(g, a)] for a in range(heads)]) for g in range(n_head)]
    o_low = jnp.concatenate(o_groups, 1)
    z_two = z_one[...] + product(o_low, self_output[...])
    h_two = layer_norm(z_two, gain_two).astype(low)
    value, bend = gelu_and_slope(product(h_two, hidden_in[...]))
    activ[...] = value.astype(low)
    slope[...] = bend
    z_three = z_two + product(activ[...], hidden_out[...])
    queries_t = out_queries_t[...]
    decoded = layer_norm(z_three, gain_three) + contract_first(queries_t, query_table[...])
    decoded = decoded.astype(low)
    logits = product(decoded, class_table[...])
    label, kind, counted = (my_column(marks, rows) for marks in (labels, modality, labeled))
    lane = lax.broadcasted_iota(jnp.int32, (rows, C), 1).astype(jnp.float32)
    is_target = jnp.where(lane == label, 1.0, 0.0)
    row_top = jnp.max(logits, 1, keepdims=True)
    row_lse = row_top + jnp.log(jnp.sum(jnp.exp2((logits - row_top) * LOG2E), 1, keepdims=True))
    loss = row_lse - jnp.sum(is_target * logits, 1, keepdims=True)
    weight = jnp.zeros((rows, 1), jnp.float32)
    place = lax.broadcasted_iota(jnp.int32, (1, LANES), 1)
    losses = jnp.zeros((1, LANES), jnp.float32)
    for m in range(MODES):
        member = jnp.where((kind == m) & (counted == 1.0), 1.0, 0.0)
        weight = weight + member / jnp.maximum(counts[0:1, m : m + 1], 1.0)
        losses = losses + jnp.where(place == m, jnp.sum(loss * member, 0, keepdims=True), 0.0)
    tile[...] = jnp.broadcast_to(losses, tile.shape)
    dlogits = (weight * (jnp.exp2((logits - row_lse) * LOG2E) - is_target)).astype(low)
    d_decoded = against(dlogits, class_table[...])
    matrix_into(query_grad, 0, product(queries_t, d_decoded.astype(low)), line)
    d_three, gain_three_grad = norm_pullback(z_three, gain_three, d_decoded)
    d_branch = d_three.astype(low)
    d_pre = (slope[...] * against(d_branch, hidden_out[...])).astype(low)
    d_middle, gain_two_grad = norm_pullback(z_two, gain_two, against(d_pre, hidden_in[...]))
    d_two = d_three + d_middle
    d_two_out[...] = d_two
    gain_grads[...] = jnp.concatenate([gain_two_grad, gain_three_grad], 0)
    d_two_low = d_two.astype(low)
    d_o = against(d_two_low, self_output[...]).astype(low)
    for slot, (g, a) in enumerate(heads_of(n_head, o_self.shape[0])):
        dout[slot] = pack(d_o[:, g * width + a * HD : g * width + (a + 1) * HD])
    for g in range(n_head):
        results = (
            contract_first(o_groups[g], d_two_low),
            contract_first(h_two, d_pre[:, g * hidden : (g + 1) * hidden]),
            contract_first(activ[:, g * hidden : (g + 1) * hidden], d_branch),
            contract_first(decoded, dlogits[:, g * classes : (g + 1) * classes]),
        )
        for m, result in zip((4, 5, 6, 7), results):
            matrix_into(stage, starts[m] - first_row, result, line)
        for b in range(shards):
            held[b, g, :shard_rows, :] = stage[pl.ds(b * shard_rows, shard_rows), :].astype(low)
    back = pltpu.make_async_copy(held, grads.at[pl.ds(first_shard, shards)], sems.at[2])
    back.start()
    back.wait()


def middle(counts, weights, common, z_one, o_self, out_queries_t, marks, gains, valid, n_head, shard_rows):
    rows = z_one.shape[0]
    begin, shards = shards_of(n_head, shard_rows, 4, 8)
    query_rows = DQ * D // LANES
    block, blocks = common_blocks(0, query_rows, valid)
    return pl.pallas_call(
        functools.partial(middle_kernel, n_head, shard_rows, valid, begin, rows),
        grid=(1,),
        out_shape=[
            shape_of(o_self.shape),
            shape_of((rows, D), jnp.float32),
            shape_of((8, LANES), jnp.float32),
            shape_of((query_rows, LANES), jnp.float32),
            shape_of((2, D), jnp.float32),
            shape_of(weights.shape),
        ],
        in_specs=[
            VMEM_SPEC,
            ANY_SPEC,
            ANY_SPEC,
            VMEM_SPEC,
            VMEM_SPEC,
            pl.BlockSpec((DQ, rows), lambda i: (0, lax.axis_index("head"))),
            VMEM_SPEC,
            VMEM_SPEC,
            VMEM_SPEC,
            VMEM_SPEC,
        ],
        out_specs=[VMEM_SPEC] * 5 + [ANY_SPEC],
        scratch_shapes=[
            pltpu.VMEM((shards,) + weights.shape[1:], low),
            pltpu.VMEM((blocks,) + common.shape[1:], low),
            pltpu.VMEM((shards * shard_rows, LANES), jnp.float32),
            pltpu.VMEM((blocks * valid, LANES), jnp.float32),
            LINE,
            pltpu.VMEM((D, D), low),
            pltpu.VMEM((D, FF), low),
            pltpu.VMEM((FF, D), low),
            pltpu.VMEM((D, C), low),
            pltpu.VMEM((DQ, D), low),
            pltpu.VMEM((rows, FF), jnp.float32),
            pltpu.VMEM((rows, FF), low),
            pltpu.SemaphoreType.DMA((3,)),
        ],
        compiler_params=pltpu.CompilerParams(vmem_limit_bytes=56 * MIB),
        name="middle",
    )(counts, weights, common, z_one, o_self, out_queries_t, *marks, gains)


def ending_kernel(
    n_head,
    shard_rows,
    valid,
    rows,
    lengths,
    grads_in,
    d_q_self,
    d_kv_self,
    d_two,
    gains,
    gain_grads,
    query_grad,
    enc_query,
    enc_keyval,
    enc_output,
    self_project,
    z_zero,
    h_zero,
    x_norm_t,
    q_enc,
    kv_enc,
    o_enc,
    z_one,
    h_one,
    grads,
    common_grad,
    held,
    stage,
    stage_common,
    line,
    d_q,
    d_kv,
    sems,
):
    heads = HEADS // n_head
    width = heads * HD
    shards = held.shape[0]
    starts = borders(n_head)
    shared = pltpu.make_async_copy(grads_in.at[pl.ds(shards - 1, 1)], held.at[pl.ds(shards - 1, 1)], sems.at[0])
    shared.start()
    d_heads = {}
    for slot, head in enumerate(heads_of(n_head, d_kv_self.shape[0])):
        d_kv_head = d_kv_self[slot]
        d_heads[head] = (unpack(d_q_self[slot]), d_kv_head[:, :HD], d_kv_head[:, HD:])
    d_projected = [
        jnp.concatenate([d_heads[(g, a)][i] for i in range(3) for a in range(heads)], 1)
        for g in range(n_head)
    ]
    whole = jnp.concatenate(d_projected, 1)
    d_middle, gain_one_grad = norm_pullback(
        z_one[...], gains[1:2, :], against(whole, self_project[...])
    )
    d_one = d_two[...] + d_middle
    d_one_low = d_one.astype(low)
    d_o = against(d_one_low, enc_output[...]).astype(low)
    for g in range(n_head):
        keys = kv_enc[:, 2 * g * width : (2 * g + 1) * width]
        values = kv_enc[:, (2 * g + 1) * width : (2 * g + 2) * width]
        d_key = jnp.zeros(keys.shape, jnp.float32)
        d_value = jnp.zeros(keys.shape, jnp.float32)
        d_query = jnp.zeros((rows, width), jnp.float32)
        for (here, q_head), (unused, do_head) in zip(
            head_lanes(g, heads, q_enc[...]), head_lanes(g, heads, d_o)
        ):
            scores = enc_scores(keys, q_head)
            probs = jnp.exp2(scores - jnp.max(scores, 0, keepdims=True))
            probs = probs / jnp.sum(probs, 0, keepdims=True)
            d_probs = against(values, do_head)
            delta = jnp.sum(probs * d_probs, 0, keepdims=True)
            d_scores = (probs * (d_probs - delta)).astype(low)
            d_value = d_value + product(probs.astype(low), do_head)
            d_key = d_key + product(d_scores, q_head)
            d_query = jnp.where(here, contract_first(d_scores, keys), d_query)
        d_q[:, g * width : (g + 1) * width] = (d_query * SCORE_SCALE).astype(low)
        d_kv[:, 2 * g * width : (2 * g + 1) * width] = (d_key * SCORE_SCALE).astype(low)
        d_kv[:, (2 * g + 1) * width : (2 * g + 2) * width] = d_value.astype(low)
    d_middle, gain_zero_grad = norm_pullback(
        z_zero[...], gains[0:1, :], against(d_q[...], enc_query[...])
    )
    d_zero = d_one + d_middle
    d_zero_top = d_zero.astype(low)
    d_zero_rest = (d_zero - d_zero_top.astype(jnp.float32)).astype(low)
    picked = picked_rows(clip_bounds(lengths), rows, n_head)
    latent_grad = contract_first(picked, d_zero_top) + contract_first(picked, d_zero_rest)
    query_rows = query_grad.shape[0]
    stage_common[:query_rows] = query_grad[...]
    matrix_into(stage_common, query_rows, latent_grad, line)
    all_gains = jnp.concatenate([gain_zero_grad, gain_one_grad, gain_grads[...]], 0)
    matrix_into(stage_common, query_rows + LAT * D // LANES, all_gains, line)
    piece = common_grad.shape[2]
    for b in range(common_grad.shape[0]):
        for k in range(common_grad.shape[1]):
            amount = min(piece, valid - k * piece)
            block = stage_common[b * valid + k * piece : b * valid + k * piece + amount, :]
            if amount < piece:
                block = jnp.concatenate([block, jnp.zeros((piece - amount, LANES), jnp.float32)], 0)
            common_grad[b, k] = block.astype(low)
    shared.wait()
    kept = shards * shard_rows - starts[4]
    for g in range(n_head):
        results = (
            contract_first(h_zero[...], d_q[:, g * width : (g + 1) * width]),
            product(x_norm_t[...], d_kv[:, 2 * g * width : (2 * g + 2) * width]),
            contract_first(o_enc[:, g * width : (g + 1) * width], d_one_low),
            contract_first(h_one[...], d_projected[g]),
        )
        if kept:
            stage[pl.ds((shards - 1) * shard_rows, shard_rows), :] = held[
                shards - 1, g, :shard_rows, :
            ].astype(jnp.float32)
        for m, result in zip((0, 1, 2, 3), results):
            matrix_into(stage, starts[m], result, line)
        for b in range(shards):
            held[b, g, :shard_rows, :] = stage[pl.ds(b * shard_rows, shard_rows), :].astype(low)
    back = pltpu.make_async_copy(held, grads.at[pl.ds(0, shards)], sems.at[1])
    back.start()
    back.wait()


def ending(lengths, grads, d_self, d_two, gains, gain_grads, query_grad, kept, common_shape, valid, shard_rows):
    rows = d_two.shape[0]
    n_head = grads.shape[1]
    begin, shards = shards_of(n_head, shard_rows, 0, 4)
    keys = kept[6].shape[1]
    common_rows = (DQ + LAT + 4) * D // LANES
    return pl.pallas_call(
        functools.partial(ending_kernel, n_head, shard_rows, valid, rows),
        out_shape=[shape_of(grads.shape), shape_of(common_shape)],
        in_specs=[SMEM_SPEC, ANY_SPEC] + [VMEM_SPEC] * 18,
        out_specs=[ANY_SPEC, VMEM_SPEC],
        input_output_aliases={1: 0},
        scratch_shapes=[
            pltpu.VMEM((shards,) + grads.shape[1:], low),
            pltpu.VMEM((shards * shard_rows, LANES), jnp.float32),
            pltpu.VMEM((common_rows, LANES), jnp.float32),
            LINE,
            pltpu.VMEM((rows, D), low),
            pltpu.VMEM((keys, 2 * D), low),
            pltpu.SemaphoreType.DMA((2,)),
        ],
        compiler_params=pltpu.CompilerParams(vmem_limit_bytes=56 * MIB),
        name="ending",
    )(lengths, grads, *d_self, d_two, gains, gain_grads, query_grad, *kept)


def adam_step(weight, first, second, grad):
    first = beta_one * first + (1 - beta_one) * grad
    second = beta_two * second + (1 - beta_two) * grad * grad
    fixed_first = first / (1 - beta_one**STEP)
    fixed_second = second / (1 - beta_two**STEP)
    weight = weight - learn_rate * (
        fixed_first / (jnp.sqrt(fixed_second) + adam_eps) + weight_decay * weight
    )
    return (weight, first, second, weight.astype(low))


def per_device(
    inputs,
    out_queries,
    clip_lengths,
    labels,
    modality,
    labeled,
    head_params,
    head_first,
    head_second,
    common_params,
    common_first,
    common_second,
):
    n_head, n_blk = lax.axis_size("head"), lax.axis_size("blk")
    dims = grid_of(n_blk, n_head)
    rows = labels.shape[0] // n_head
    n_h, n_c = head_params.shape[0], common_params.shape[0]
    shard_rows, common_rows = n_h // LANES, -(-n_c // LANES)
    head_rows = round_up(shard_rows + 1, TILE)
    piece_rows = round_up(-(-common_rows // n_head), TILE)
    marks = [x.reshape(-1, LANES) for x in (labels, modality, labeled)]
    head_wide = head_params.reshape(shard_rows, LANES)
    common_wide = jnp.pad(common_params, (0, common_rows * LANES - n_c)).reshape(common_rows, LANES)
    weights, common = gather_all(dims, marks, (head_wide, common_wide), (head_rows, piece_rows), 0)
    valid = common_rows
    if n_c % LANES:
        common = common.reshape(n_blk, -1)[:, :n_c].reshape(-1, LANES)
        valid = common.shape[0]
        common = jnp.pad(common, ((0, -valid % TILE), (0, 0)))[None, None]

    encoded = encode(
        clip_lengths, weights, common, inputs.T, valid, rows, Team(dims).size, n_head, shard_rows
    )
    gains, z_one, counts = encoded[4], encoded[11], encoded[15]
    o_self, lse_self, out_self_t, q_all, kv_all = attend(
        dims, clip_lengths, encoded[13], encoded[14], 1
    )
    dout, d_two, tile, query_grad, gain_grads, grads = middle(
        counts, weights, common, z_one, o_self, out_queries.T, marks, gains, valid, n_head, shard_rows
    )
    d_self = attend_back(dims, clip_lengths, q_all, kv_all, dout, out_self_t, lse_self, 2)
    kept = encoded[:4] + encoded[5:13]
    grads, common_grad = ending(
        clip_lengths,
        grads,
        d_self,
        d_two,
        gains,
        gain_grads,
        query_grad,
        kept,
        common.shape,
        valid,
        shard_rows,
    )
    if n_c % LANES:
        common_grad = common_grad[0, 0, :valid].reshape(n_blk, n_c)
        common_grad = jnp.pad(common_grad, ((0, 0), (0, n_head * piece_rows * LANES - n_c)))
        common_grad = common_grad.reshape(n_blk, n_head, piece_rows, LANES)
    head_share, common_share, loss_sums, clip_norm, factor = reduce_all(
        dims, (grads, common_grad), (shard_rows, common_rows), tile, 3
    )
    label_counts, loss_sums = encoded[16].reshape(MODES), loss_sums.reshape(MODES)
    clip_norm, factor = clip_norm.reshape(()), factor.reshape(())
    head_share, common_share = head_share.reshape(-1), common_share.reshape(-1)[:n_c]
    head_out = adam_step(head_params, head_first, head_second, head_share * factor)
    common_out = adam_step(common_params, common_first, common_second, common_share * factor)
    return head_out + common_out + (loss_sums, label_counts, clip_norm)


def solution(mesh):
    placed = (
        P("blk", None),
        P("blk", None),
        P(),
        P("blk"),
        P("blk"),
        P("blk"),
        P(("head", "blk")),
        P(("head", "blk")),
        P(("head", "blk")),
        P("blk"),
        P("blk"),
        P("blk"),
    )
    return jax.shard_map(
        per_device,
        mesh=mesh,
        in_specs=placed,
        out_specs=(
            P(("head", "blk")),
            P(("head", "blk")),
            P(("head", "blk")),
            P(("head", "blk")),
            P("blk"),
            P("blk"),
            P("blk"),
            P("blk"),
            P(),
            P(),
            P(),
        ),
        check_vma=False,
    )
```

```python
import functools

import jax
import jax.numpy as jnp
from jax import lax
from jax.experimental import pallas as pl
from jax.experimental.pallas import tpu as pltpu
from jax.sharding import PartitionSpec as P

D = 512
HEADS = 8
HD = 64
FF = 2048
DI = 704
DQ = 1026
C = 704
LAT = 784
MODES = 3
STEP = 10
LANES = 128
TILE = 16

norm_eps = 1e-05
learn_rate = 0.1
beta_one = 0.9
beta_two = 0.999
adam_eps = 1e-08
weight_decay = 0.01
clip_limit = 0.05
big_negative = -1e30
low = jnp.bfloat16
LOG2E = 1.4426950408889634
SCORE_SCALE = HD ** (-0.5)
MESH = pl.DeviceIdType.MESH
MIB = 1 << 20
VMEM_SPEC = pl.BlockSpec(memory_space=pltpu.VMEM)
SMEM_SPEC = pl.BlockSpec(memory_space=pltpu.SMEM)
ANY_SPEC = pl.BlockSpec(memory_space=pl.ANY)


def shape_of(shape, dtype=low):
    return jax.ShapeDtypeStruct(shape, dtype)


def round_up(n, unit):
    return -(-n // unit) * unit


def grid_of(n_blk, n_head):
    cores = 2 if n_head % 2 == 0 else 1
    x = n_head // cores
    y = x if n_blk % x == 0 else 1
    return (n_blk // y, y, x, cores)


def my_place(dims):
    blk, head = lax.axis_index("blk"), lax.axis_index("head")
    return (blk // dims[1], lax.rem(blk, dims[1]), head // dims[3], lax.rem(head, dims[3]))


def shifted(dims, me, offset, sign):
    return tuple(
        m if o == 0 else lax.rem(m + (o if sign > 0 else n - o), n)
        for m, o, n in zip(me, offset, dims)
    )


def blk_of(dims, place):
    return place[0] * dims[1] + place[1]


def head_of(dims, place):
    return place[2] * dims[3] + place[3]


def device_of(dims, place):
    return {"blk": blk_of(dims, place), "head": head_of(dims, place)}


def along(axis, d):
    return tuple(d if a == axis else 0 for a in range(4))


def greet(dims, me, offsets):
    barrier = pltpu.get_barrier_semaphore()
    for offset in offsets:
        pl.semaphore_signal(
            barrier,
            inc=1,
            device_id=device_of(dims, shifted(dims, me, offset, 1)),
            device_id_type=MESH,
        )
    pl.semaphore_wait(barrier, len(offsets))


def axis_peers(dims, axes):
    return [along(axis, d) for axis in axes for d in range(1, dims[axis])]


def remote(src, dst, send_sem, recv_sem, place, dims):
    return pltpu.make_async_remote_copy(
        src_ref=src,
        dst_ref=dst,
        send_sem=send_sem,
        recv_sem=recv_sem,
        device_id=device_of(dims, place),
        device_id_type=MESH,
    )


AHEAD = 6.0
RING = 0


def in_order(first, follow, size_of, ahead, result):
    queues, busy, flight = {}, {}, {}
    now = 0.0

    def ready(messages):
        for message in messages:
            queues.setdefault(message[1], []).append(message)

    ready(first)
    while True:
        for axis in sorted(queues):
            queue, going = queues[axis], flight.setdefault(axis, [])
            while queue and (not going or busy[axis] < now + ahead):
                message = min(queue)
                queue.remove(message)
                busy[axis] = max(now, busy.get(axis, 0.0)) + size_of(message)
                going.append((busy[axis] + 1.5, message))
                result.append((True, message))
        arrivals = [min(going) for going in flight.values() if going]
        if not arrivals:
            return now
        arrival = min(arrivals)
        flight[arrival[1][1]].remove(arrival)
        now = max(now, arrival[0])
        result.append((False, arrival[1]))
        ready(follow(arrival[1]))


def time_of(rows, axis):
    return rows * LANES * 2 / (300e3 if axis == 3 else 45e3)


def with_at(offset, axis, d):
    return offset[:axis] + (d,) + offset[axis + 1 :]


def gather_order(dims, parts):
    def onward(p, offset, position):
        order = parts[p][3]
        result = []
        for k in range(max(position, 0), 4):
            axis = order[k]
            n = dims[axis]
            if k > position:
                steps = [1] if axis == RING else range(1, n)
                steps = [d for d in steps if d < n]
            else:
                steps = [offset[axis] + 1] if axis == RING and offset[axis] + 1 < n else []
            for d in steps:
                result.append(((k, sum(offset), p), axis, p, with_at(offset, axis, d)))
        return result

    def follow(message):
        rank, axis, p, offset = message
        return onward(p, offset, rank[0])

    first = [m for p in range(len(parts)) for m in onward(p, (0, 0, 0, 0), -1)]
    result = []
    now = in_order(first, follow, lambda m: time_of(parts[m[2]][2], m[1]), AHEAD, result)
    return result, now


def gather_kernel(
    dims,
    parts,
    labels,
    modality,
    labeled,
    head_params,
    common_params,
    head_all,
    common_all,
    head_low,
    common_low,
    common_wide,
    send_sem,
    recv_sem,
    own_sem,
):
    me = my_place(dims)
    my_head = head_of(dims, me)
    n_head = dims[2] * dims[3]
    shard_rows, common_rows = head_params.shape[0], common_params.shape[0]
    per_head = labels.shape[0] // n_head
    row = lax.broadcasted_iota(jnp.int32, labels.shape, 0)
    mine = (row >= my_head * per_head) & (row < (my_head + 1) * per_head) & (labeled[...] == 1)
    lane = lax.broadcasted_iota(jnp.int32, (1, LANES), 1)
    counts = jnp.zeros((1, LANES), jnp.float32)
    for m in range(MODES):
        member = jnp.where(mine & (modality[...] == m), 1.0, 0.0)
        counts = counts + jnp.where(lane == m, jnp.sum(member, (0, 1), keepdims=True), 0.0)
    padding = head_low.shape[0] - shard_rows
    tail = shard_rows // TILE * TILE
    head_low[:tail] = head_params[:tail].astype(low)
    last = [jnp.broadcast_to(counts, (padding, LANES))]
    if shard_rows > tail:
        last = [head_params[tail:]] + last
    head_low[tail:] = jnp.concatenate(last, 0).astype(low)
    common_wide[...] = jnp.zeros(common_wide.shape, jnp.float32)
    common_wide[:common_rows] = common_params[...]
    piece = common_low.shape[0]
    common_low[...] = common_wide[pl.ds(pl.multiple_of(my_head * piece, TILE), piece)].astype(low)

    greet(dims, me, ring_and_others(dims))
    srcs, outs = (head_low, common_low), (head_all, common_all)
    copies = {}

    def block(p, offset):
        place = shifted(dims, me, offset, -1)
        array, first, rows, order = parts[p]
        return outs[array].at[blk_of(dims, place), head_of(dims, place), pl.ds(first, rows)]

    own = []
    for is_send, (rank, axis, p, offset) in gather_order(dims, parts)[0]:
        if is_send:
            step = 1 if axis == RING else offset[axis]
            before = with_at(offset, axis, offset[axis] - step)
            array, first, rows, order = parts[p]
            source = block(p, before) if any(before) else srcs[array].at[pl.ds(first, rows)]
            i = len(copies)
            copies[(p, offset)] = remote(
                source,
                block(p, before),
                send_sem.at[i],
                recv_sem.at[i],
                shifted(dims, me, along(axis, step), 1),
                dims,
            )
            copies[(p, offset)].start()
        else:
            if not own:
                for array in range(2):
                    copy = pltpu.make_async_copy(
                        srcs[array], outs[array].at[blk_of(dims, me), my_head], own_sem.at[array]
                    )
                    copy.start()
                    own.append(copy)
            copies[(p, offset)].wait_recv()
    for copy in copies.values():
        copy.wait_send()
    for copy in own:
        copy.wait()


def ring_and_others(dims):
    ring = {along(RING, 1 % dims[RING]), along(RING, (dims[RING] - 1) % dims[RING])}
    return sorted(ring - {(0, 0, 0, 0)}) + axis_peers(dims, (1, 2, 3))


def cut(array, rows, shares):
    result = []
    first, so_far = 0, 0
    whole = sum(share for share, order in shares)
    for share, order in shares:
        so_far += share
        end = rows * so_far // whole // TILE * TILE if so_far < whole else rows
        if end > first:
            result.append((array, first, end - first, order))
        first = end
    return tuple(result)


ZYXC, ZXYC, YXZC, XYZC = (0, 1, 2, 3), (0, 2, 1, 3), (1, 2, 0, 3), (2, 1, 0, 3)
GATHER_SHARES = ((8, ZYXC), (6, ZXYC), (2, YXZC), (2, XYZC))
REDUCE_SHARES = ((7, ZYXC), (7, ZXYC), (2, YXZC), (2, XYZC))


def gather_all(dims, marks, params, rows, collective_id):
    z, y, x, cores = dims
    parts = cut(0, rows[0], GATHER_SHARES) + cut(1, rows[1], ((1, ZXYC),))
    count = len(parts) * (z * y * x * cores - 1)
    return pl.pallas_call(
        functools.partial(gather_kernel, dims, parts),
        out_shape=[shape_of((z * y, x * cores, n, LANES)) for n in rows],
        in_specs=[VMEM_SPEC] * 5,
        out_specs=[ANY_SPEC] * 2,
        scratch_shapes=[pltpu.VMEM((n, LANES), low) for n in rows]
        + [
            pltpu.VMEM((x * cores * rows[1], LANES), jnp.float32),
            pltpu.SemaphoreType.DMA((count,)),
            pltpu.SemaphoreType.DMA((count,)),
            pltpu.SemaphoreType.DMA((2,)),
        ],
        compiler_params=pltpu.CompilerParams(collective_id=collective_id, has_side_effects=True),
        name="gather_weights",
    )(*marks, *params)


def reduce_order(dims, parts):
    ready, arrived, order = set(), set(), []

    def message(p, position, offset):
        z = offset[RING]
        rank = (dims[RING] - z if z else dims[RING], position, tuple(-o for o in offset), p)
        return (rank, parts[p][3][position], p, position, offset)

    def done(p, position, offset):
        ready.add((p, position, offset))
        if position == 4:
            return []
        axis = parts[p][3][position]
        d = offset[axis]
        first = d != 0 and (axis != RING or d == dims[axis] - 1)
        return ([message(p, position, offset)] if first else []) + advance(p, position, offset)

    def advance(p, position, offset):
        axis = parts[p][3][position]
        n = dims[axis]
        start = with_at(offset, axis, 0)
        if axis == RING:
            here = (p, position, offset)
            if here in ready and here in arrived:
                order.append((None, here))
                if offset[axis]:
                    return [message(p, position, offset)]
                return done(p, position + 1, offset)
        elif (p, position, start) in ready and (p, position + 1, start) not in ready:
            if all((p, position, with_at(start, axis, d)) in arrived for d in range(1, n)):
                order.append((None, (p, position, start)))
                return done(p, position + 1, start)
        return []

    def follow(sent):
        rank, axis, p, position, offset = sent
        here = with_at(offset, axis, offset[axis] - 1) if axis == RING else offset
        arrived.add((p, position, here))
        return advance(p, position, here)

    first = []
    for p in range(len(parts)):
        for offset in all_offsets(dims, range(4)):
            first += done(p, 0, offset)
    now = in_order(first, follow, lambda m: time_of(parts[m[2]][2], m[1]), AHEAD, order)
    return order, now


def all_offsets(dims, axes):
    offsets = [(0, 0, 0, 0)]
    for a in axes:
        offsets = [with_at(o, a, d) for o in offsets for d in range(dims[a])]
    return offsets


def reduce_kernel(dims, parts, *refs):
    srcs, tile = refs[:2], refs[2]
    head_out, common_out, losses, norm, factor = refs[3:8]
    places = len(parts) * 4
    buffers = refs[8 : 8 + places]
    head_sum, common_sum, shares, send_sem, recv_sem, near_tiles, far_tiles = refs[8 + places :]
    sums = (head_sum, common_sum)
    me = my_place(dims)
    z, y, x, cores = dims
    across = peers_across(dims)
    others = [o for o in all_offsets(dims, (0, 1)) if any(o)]
    met = ring_and_others(dims)
    greet(dims, me, met + [o for o in across + others if o not in met])
    push = Pushes(dims, me, send_sem, recv_sem)
    copies = {}

    def slot(p, position, offset):
        order = parts[p][3]
        axis = order[position]
        rest = [o for o in all_offsets(dims, order[position + 1 :])]
        k = rest.index(with_at(offset, axis, 0))
        return buffers[p * 4 + position].at[k, max(offset[axis] - 1, 0)]

    def summed(p, position, offset):
        array, first, rows, order = parts[p]
        if position == 0:
            place = shifted(dims, me, offset, 1)
            return srcs[array].at[blk_of(dims, place), head_of(dims, place), pl.ds(first, rows)]
        return slot(p, position - 1, offset)

    def ring_slot(p, position, offset):
        axis = parts[p][3][position]
        return slot(p, position, with_at(offset, axis, offset[axis] + 1))

    def add(p, position, offset):
        array, first, rows, order = parts[p]
        axis = order[position]
        if axis == RING:
            arrivals = [ring_slot(p, position, offset)]
        else:
            arrivals = [slot(p, position, with_at(offset, axis, d)) for d in range(1, dims[axis])]
        mine = summed(p, position, offset)
        step = row_chunk(rows)

        @pl.loop(0, rows // step)
        def some_rows(n):
            at = pl.ds(pl.multiple_of(n * step, step), step)
            total = mine[at].astype(jnp.float32)
            for arrival in arrivals:
                total = total + arrival[at].astype(jnp.float32)
            if position == 3 and not any(offset):
                sums[array][pl.ds(pl.multiple_of(first + n * step, TILE), step)] = total
            else:
                arrivals[0][at] = total.astype(low)

    for is_send, what in reduce_order(dims, parts)[0]:
        if is_send is None:
            add(*what)
        elif is_send:
            rank, axis, p, position, offset = what
            d = offset[axis]
            started = axis != RING or d == dims[axis] - 1
            source = summed(p, position, offset) if started else ring_slot(p, position, offset)
            step = along(axis, 1 if axis == RING else d)
            copies[what] = push(source, slot(p, position, offset), step)
        else:
            copies[what].wait_recv()
    my_head, my_blk = head_of(dims, me), blk_of(dims, me)
    shares[my_head] = common_sum[...].astype(low)
    share_copies = [push(shares.at[my_head], shares.at[my_head], o) for o in across]
    amount = head_out.shape[0]
    head_out[...] = head_sum[:amount]
    squares = jnp.sum(head_sum[:amount] * head_sum[:amount], 0, keepdims=True)
    squares = squares + jnp.sum(common_sum[...] * common_sum[...], 0, keepdims=True)
    lane = lax.broadcasted_iota(jnp.int32, (1, LANES), 1)
    near_tiles[my_head] = tile[...] + jnp.where(
        lane == MODES, jnp.sum(squares, 1, keepdims=True), 0.0
    )
    near = [push(near_tiles.at[my_head], near_tiles.at[my_head], o) for o in across]
    for copy in near:
        copy.wait_recv()
    far_tiles[my_blk] = jnp.sum(near_tiles[...], 0)
    far = [push(far_tiles.at[my_blk], far_tiles.at[my_blk], o) for o in others]
    for copy in share_copies:
        copy.wait_recv()
    piece = shares.shape[1]
    for k in range(x * cores):
        amount = min(piece, common_out.shape[0] - k * piece)
        common_out[k * piece : k * piece + amount] = shares[k].astype(jnp.float32)[:amount]
    for copy in far:
        copy.wait_recv()
    totals = jnp.sum(far_tiles[...], 0)[:1]
    losses[...] = totals[:, :MODES]
    norm[...] = jnp.sqrt(totals[:, MODES : MODES + 1])
    factor[...] = jnp.minimum(1.0, clip_limit / norm[...])
    push.finish()


def row_chunk(rows):
    for count in (4, 3, 2):
        if rows % (count * TILE) == 0:
            return rows // count
    return rows


def reduce_all(dims, arrays, valid, tile, collective_id):
    z, y, x, cores = dims
    rows = [array.shape[2] for array in arrays]
    parts = cut(0, rows[0], [(share, order[::-1]) for share, order in REDUCE_SHARES])
    parts = parts + cut(1, rows[1], ((1, ZXYC[::-1]),))
    scratch = []
    for array, first, amount, order in parts:
        for position, axis in enumerate(order):
            rest = len(all_offsets(dims, order[position + 1 :]))
            scratch.append(pltpu.VMEM((rest, dims[axis] - 1, amount, LANES), low))
    count = len(parts) * (z * y * x * cores - 1) + 2 * (x * cores - 1) + z * y - 1
    return pl.pallas_call(
        functools.partial(reduce_kernel, dims, parts),
        out_shape=[
            shape_of((valid[0], LANES), jnp.float32),
            shape_of((valid[1], LANES), jnp.float32),
            shape_of((1, MODES), jnp.float32),
            shape_of((1, 1), jnp.float32),
            shape_of((1, 1), jnp.float32),
        ],
        in_specs=[VMEM_SPEC] * 3,
        out_specs=[VMEM_SPEC] * 5,
        scratch_shapes=scratch
        + [pltpu.VMEM((n, LANES), jnp.float32) for n in rows]
        + [
            pltpu.VMEM((x * cores, rows[1], LANES), low),
            pltpu.SemaphoreType.DMA((count,)),
            pltpu.SemaphoreType.DMA((count,)),
            pltpu.VMEM((x * cores, 8, LANES), jnp.float32),
            pltpu.VMEM((z * y, 8, LANES), jnp.float32),
        ],
        compiler_params=pltpu.CompilerParams(
            collective_id=collective_id, has_side_effects=True, vmem_limit_bytes=60 * MIB
        ),
        name="reduce_gradients",
    )(*arrays, tile)


def contract_first(a, b):
    return lax.dot_general(a, b, (((0,), (0,)), ((), ())), preferred_element_type=jnp.float32)


def product(a, b):
    return jnp.dot(a, b, preferred_element_type=jnp.float32)


def against(a, b):
    return lax.dot_general(a, b, (((1,), (1,)), ((), ())), preferred_element_type=jnp.float32)


def clip_bounds(lengths):
    result, first = [], 0
    for clip in range(lengths.shape[0]):
        end = first + lengths[clip]
        result.append((first, end))
        first = end
    return result


def clip_borders(bounds, place):
    opening = jnp.zeros(place.shape, jnp.int32)
    ending = jnp.full(place.shape, 1 << 30, jnp.int32)
    for clip, (begin, end) in enumerate(bounds):
        here = place == clip
        opening = jnp.where(here, begin, opening)
        ending = jnp.where(here, end, ending)
    return opening, ending


def low_half(axis):
    return lax.broadcasted_iota(jnp.int32, (1, LANES) if axis else (LANES, 1), axis) < HD


def with_key_tail(bounds, first_row, kv):
    clips = len(bounds)
    place = lax.broadcasted_iota(jnp.int32, (1, LANES), 1) - HD
    opening, ending = clip_borders(bounds, place)
    ones = jnp.where((place >= clips) & (place < clips + 3), 1.0, 0.0)
    row = first_row + lax.broadcasted_iota(jnp.int32, kv.shape, 0)
    tail = jnp.where((row >= opening) & (row < ending), ones, big_negative)
    return jnp.where(low_half(1), kv.astype(jnp.float32), tail).astype(low)


def with_value_tail(kv):
    place = lax.broadcasted_iota(jnp.int32, (1, LANES), 1)
    ones = jnp.where(place < 3, 1.0, 0.0)
    return jnp.where(low_half(1), ones, kv.astype(jnp.float32)).astype(low)


def in_three(place, value):
    top = value.astype(low).astype(jnp.float32)
    middle = (value - top).astype(low).astype(jnp.float32)
    bottom = value - top - middle
    return (
        jnp.where(place == 0, top, 0.0)
        + jnp.where(place == 1, middle, 0.0)
        + jnp.where(place == 2, bottom, 0.0)
    )


def with_query_tail(bounds, first_row, rows, extra):
    clips = len(bounds)
    place = lax.broadcasted_iota(jnp.int32, (HD, 1), 0)
    opening, ending = clip_borders(bounds, place)
    row = first_row + lax.broadcasted_iota(jnp.int32, (1, rows.shape[1]), 1)
    inside = (place < clips) & (row >= opening) & (row < ending)
    tail = jnp.where(inside, 1.0, 0.0)
    if extra is not None:
        tail = tail + in_three(place - clips, -extra)
    return jnp.concatenate([rows * (SCORE_SCALE * LOG2E), tail], 0).astype(low)


def pack(rows):
    half = rows.shape[0] // 2
    return jnp.concatenate([rows[:half], rows[half:]], 1)


def unpack(packed):
    return jnp.concatenate([packed[:, :HD], packed[:, HD:]], 0)


def unpack_t(packed):
    turned = packed.astype(jnp.float32).T
    return jnp.concatenate([turned[:HD], turned[HD:]], 1)


def pack_t(columns):
    half = columns.shape[1] // 2
    return jnp.concatenate([columns[:, :half], columns[:, half:]], 0).T


class Team:
    def __init__(self, dims):
        z, y, x, cores = dims
        self.dims = dims
        self.wide = HEADS // (x * cores) == y
        self.size = x * cores * (y if self.wide else 1)
        self.groups = z if self.wide else z * y
        axes = (1, 2, 3) if self.wide else (2, 3)
        offsets = [o for o in all_offsets(dims, axes) if any(o)]
        self.others = sorted(offsets, key=lambda o: (o[1] + o[2], o))
        self.sides = [] if self.wide else axis_peers(dims, (1,))

    def slot(self, place):
        head = head_of(self.dims, place)
        return place[1] * self.dims[2] * self.dims[3] + head if self.wide else head

    def group(self, place):
        return place[0] if self.wide else blk_of(self.dims, place)


def heads_of(n_head, slots):
    return [(s % n_head, s // n_head) for s in range(slots)]


class Pushes:
    def __init__(self, dims, me, send_sem, recv_sem):
        self.dims, self.me, self.send_sem, self.recv_sem = dims, me, send_sem, recv_sem
        self.started = []

    def __call__(self, src, dst, offset):
        i = len(self.started)
        place = shifted(self.dims, self.me, offset, 1)
        copy = remote(src, dst, self.send_sem.at[i], self.recv_sem.at[i], place, self.dims)
        copy.start()
        self.started.append(copy)
        return copy

    def finish(self):
        for copy in self.started:
            copy.wait_send()


def peers_across(dims):
    z, y, x, cores = dims
    across = [(0, 0, a, c) for a in range(x) for c in range(cores) if (a, c) != (0, 0)]
    return sorted(across, key=lambda o: (o[2] == 0, o[3]))


def attend_kernel(
    team,
    query_step,
    key_step,
    pieces,
    lengths,
    q_in,
    kv_in,
    o_out,
    lse,
    out_t,
    q_all,
    kv_all,
    keys,
    values_t,
    queries,
    top,
    accum,
    o_mine,
    send_sem,
    recv_sem,
    own_sem,
):
    dims = team.dims
    z = dims[0]
    me = my_place(dims)
    bounds = clip_bounds(lengths)
    rows = kv_in.shape[1]
    amount = team.size * rows
    slots = team.size // pieces
    my_group, my_slot = team.group(me), team.slot(me)
    ring_ends = sorted({along(0, 1 % z), along(0, (z - 1) % z)} - {(0, 0, 0, 0)})
    greet(dims, me, team.others + ring_ends + team.sides)
    push = Pushes(dims, me, send_sem, recv_sem)
    own_kv = pltpu.make_async_copy(kv_in.at[my_slot], kv_all.at[my_group, my_slot], own_sem.at[0])
    own_q = pltpu.make_async_copy(q_in.at[my_slot], q_all.at[my_slot], own_sem.at[1])
    own_kv.start()
    own_q.start()

    def to_team(src, dst, o):
        return push(src.at[team.slot(shifted(dims, me, o, 1))], dst, o)

    kv_copies = {o: to_team(kv_in, kv_all.at[my_group, my_slot], o) for o in team.others}
    q_copies = [to_team(q_in, q_all.at[my_slot], o) for o in team.others]
    ring, side = {}, {}

    def group_at(offset):
        return team.group(shifted(dims, me, offset, -1))

    def send_on(s, piece):
        block = kv_all.at[group_at(along(0, s)), pl.ds(piece * slots, slots)]
        if s < z - 1:
            ring[(s + 1, piece)] = push(block, block, along(0, 1))
        for o in team.sides:
            side[(s, o, piece)] = push(block, block, o)

    def compute(offset, piece):
        group = group_at(offset)

        @pl.loop(0, slots)
        def build(n):
            at = pl.ds(pl.multiple_of(n * rows, rows), rows)
            slot = piece * slots + n
            block = kv_all[group, slot]
            keys[at, :] = with_key_tail(bounds, group * amount + slot * rows, block)
            values_t[:HD, at] = block.astype(jnp.float32).T[HD:].astype(low)

        @pl.loop(0, amount // (2 * query_step))
        def query_blocks(n):
            for half in range(2):
                at = pl.ds(pl.multiple_of((2 * n + half) * query_step, query_step), query_step)
                query = queries[:, at]
                old, total = top[:, at], accum[:, at]
                for k in range(0, slots * rows, key_step):
                    scores = product(keys[k : k + key_step, :], query)
                    new = jnp.maximum(old, jnp.max(scores, 0, keepdims=True))
                    probs = jnp.exp2((scores - new).astype(low))
                    total = total * jnp.exp2(old - new) + product(values_t[:, k : k + key_step], probs)
                    old = new
                top[:, at] = old
                accum[:, at] = total

    values_t[HD:, :] = jnp.ones((TILE, slots * rows), low)
    top[...] = jnp.full(top.shape, -1e38, jnp.float32)
    accum[...] = jnp.zeros(accum.shape, jnp.float32)
    own_kv.wait()
    for o in team.others:
        kv_copies[o].wait_recv()
    for piece in range(pieces):
        send_on(0, piece)
    own_q.wait()
    for copy in q_copies:
        copy.wait_recv()
    for n in range(team.size):
        queries[:, n * rows : (n + 1) * rows] = with_query_tail(
            bounds, my_group * amount + n * rows, unpack_t(q_all[n]), None
        )
    for s in range(z):
        for piece in range(pieces):
            compute(along(0, s), piece)
            if s < z - 1:
                ring[(s + 1, piece)].wait_recv()
                send_on(s + 1, piece)
            for o in team.sides:
                side[(s, o, piece)].wait_recv()
                compute((s, o[1], 0, 0), piece)
    total = accum[HD : HD + 1, :]
    out_t[...] = accum[:HD, :] / total
    lse[...] = top[...] + jnp.log(total) * LOG2E
    for n in range(team.size):
        o_mine[n] = pack_t(out_t[:, n * rows : (n + 1) * rows]).astype(low)
    o_copies = [to_team(o_mine, o_out.at[my_slot], o) for o in team.others]
    own_o = pltpu.make_async_copy(o_mine.at[my_slot], o_out.at[my_slot], own_sem.at[2])
    own_o.start()
    own_o.wait()
    for copy in o_copies:
        copy.wait_recv()
    push.finish()


def attend(dims, lengths, q, kv, collective_id):
    team = Team(dims)
    z = dims[0]
    amount = team.size * kv.shape[1]
    pieces = 2
    count = 3 * (team.size - 1) + pieces * (z + z * len(team.sides))
    return pl.pallas_call(
        functools.partial(attend_kernel, team, 256, min(1024, amount // pieces), pieces),
        out_shape=(
            jax.ShapeDtypeStruct(q.shape, low),
            jax.ShapeDtypeStruct((1, amount), jnp.float32),
            jax.ShapeDtypeStruct((HD, amount), jnp.float32),
            jax.ShapeDtypeStruct(q.shape, low),
            jax.ShapeDtypeStruct((team.groups,) + kv.shape, low),
        ),
        in_specs=[SMEM_SPEC, VMEM_SPEC, VMEM_SPEC],
        out_specs=[VMEM_SPEC] * 5,
        scratch_shapes=[
            pltpu.VMEM((amount // pieces, LANES), low),
            pltpu.VMEM((HD + TILE, amount // pieces), low),
            pltpu.VMEM((LANES, amount), low),
            pltpu.VMEM((1, amount), jnp.float32),
            pltpu.VMEM((HD + TILE, amount), jnp.float32),
            pltpu.VMEM(q.shape, low),
            pltpu.SemaphoreType.DMA((count,)),
            pltpu.SemaphoreType.DMA((count,)),
            pltpu.SemaphoreType.DMA((3,)),
        ],
        compiler_params=pltpu.CompilerParams(
            collective_id=collective_id, has_side_effects=True, vmem_limit_bytes=56 * MIB
        ),
        name="attend",
    )(lengths, q, kv)


def attend_back_kernel(
    team,
    key_step,
    pieces,
    lengths,
    q_all,
    kv_all,
    do_in,
    out_t,
    lse,
    d_q_out,
    d_kv_out,
    do_all,
    keys,
    keys_t,
    values,
    queries,
    douts,
    d_q_t,
    q_rows,
    do_rows,
    side_out,
    side_in,
    ring_out,
    ring_in,
    mine,
    d_q_mine,
    d_kv_mine,
    send_sem,
    recv_sem,
    own_sem,
):
    dims = team.dims
    z = dims[0]
    me = my_place(dims)
    bounds = clip_bounds(lengths)
    rows = kv_all.shape[2]
    amount = team.size * rows
    slots = team.size // pieces
    piece_rows = slots * rows
    my_group, my_slot = team.group(me), team.slot(me)
    ring_ends = sorted({along(0, 1 % z), along(0, (z - 1) % z)} - {(0, 0, 0, 0)})
    greet(dims, me, team.others + ring_ends + team.sides)
    push = Pushes(dims, me, send_sem, recv_sem)

    def to_team(src, dst, o):
        return push(src.at[team.slot(shifted(dims, me, o, 1))], dst, o)

    do_copies = [to_team(do_in, do_all.at[my_slot], o) for o in team.others]
    own_do = pltpu.make_async_copy(do_in.at[my_slot], do_all.at[my_slot], own_sem.at[0])
    own_do.start()
    place = lax.broadcasted_iota(jnp.int32, (HD, 1), 0)
    for n in range(team.size):
        at = slice(n * rows, (n + 1) * rows)
        q_t = unpack_t(q_all[n])
        queries[:, at] = with_query_tail(bounds, my_group * amount + n * rows, q_t, lse[:, at])
        q_rows[:, at] = (q_t * SCORE_SCALE).astype(low)
    d_q_t[...] = jnp.zeros(d_q_t.shape, jnp.float32)
    own_do.wait()
    for copy in do_copies:
        copy.wait_recv()
    for n in range(team.size):
        at = slice(n * rows, (n + 1) * rows)
        do_t = unpack_t(do_all[n])
        delta = jnp.sum(do_t * out_t[:, at], 0, keepdims=True)
        douts[:, at] = jnp.concatenate([in_three(place, -delta), do_t], 0).astype(low)
        do_rows[:, at] = do_t.astype(low)

    def compute(offset, piece, target):
        group = team.group(shifted(dims, me, offset, 1))

        @pl.loop(0, slots)
        def build(n):
            at = pl.ds(pl.multiple_of(n * rows, rows), rows)
            slot = piece * slots + n
            block = kv_all[group, slot]
            keys[at, :] = with_key_tail(bounds, group * amount + slot * rows, block)
            keys_t[:, at] = block.astype(jnp.float32).T[:HD].astype(low)
            values[at, :] = with_value_tail(block)

        @pl.loop(0, piece_rows // key_step)
        def key_block(k):
            at = pl.ds(pl.multiple_of(k * key_step, key_step), key_step)
            d_key = jnp.zeros((HD, key_step), jnp.float32)
            d_value = jnp.zeros((HD, key_step), jnp.float32)
            for half in (slice(0, amount // 2), slice(amount // 2, amount)):
                probs = jnp.exp2(product(keys[at, :], queries[:, half]).astype(low))
                d_probs = product(values[at, :], douts[:, half])
                d_scores = (probs.astype(jnp.float32) * d_probs).astype(low)
                d_value = d_value + against(do_rows[:, half], probs)
                d_key = d_key + against(q_rows[:, half], d_scores)
                d_q_t[:, half] = d_q_t[:, half] + product(keys_t[:, at], d_scores)
            target[at, :] = jnp.concatenate([d_key, d_value], 0).T.astype(target.dtype)

    side, ring = {}, {}

    def send_sides(s, piece):
        for o in team.sides:
            target = side_out.at[s - 1, o[1] - 1, piece]
            compute((z - s, o[1], 0, 0), piece, target)
            side[(s, o, piece)] = push(target, side_in.at[s - 1, o[1] - 1, piece], o)

    def combine(s, piece):
        for o in team.sides:
            side[(s, o, piece)].wait_recv()
        if s > 1:
            ring[(s - 1, piece)].wait_recv()
        for n in range(slots):
            at = slice(n * rows, (n + 1) * rows)
            total = mine[piece, at, :]
            for o in team.sides:
                total = total + side_in[s - 1, o[1] - 1, piece, at, :].astype(jnp.float32)
            if s > 1:
                total = total + ring_in[s - 2, piece, at, :].astype(jnp.float32)
            if s < z:
                ring_out[s - 1, piece, at, :] = total.astype(low)
            else:
                d_kv_mine[piece * slots + n] = total.astype(low)
        if s < z:
            ring[(s, piece)] = push(ring_out.at[s - 1, piece], ring_in.at[s - 1, piece], along(0, 1))

    for s in range(1, z + 1):
        for piece in range(pieces):
            send_sides(s, piece)
            compute((z - s if s < z else 0, 0, 0, 0), piece, mine.at[piece])
            if team.sides or s < z:
                combine(s, piece)
    for n in range(team.size):
        at = slice(n * rows, (n + 1) * rows)
        d_q_mine[n] = pack_t(d_q_t[:, at] * SCORE_SCALE).astype(low)
    copies = [to_team(d_q_mine, d_q_out.at[my_slot], o) for o in team.others]
    own_q = pltpu.make_async_copy(d_q_mine.at[my_slot], d_q_out.at[my_slot], own_sem.at[1])
    own_q.start()
    if not team.sides:
        for piece in range(pieces):
            combine(z, piece)
    copies += [to_team(d_kv_mine, d_kv_out.at[my_slot], o) for o in team.others]
    own_kv = pltpu.make_async_copy(d_kv_mine.at[my_slot], d_kv_out.at[my_slot], own_sem.at[2])
    own_kv.start()
    own_q.wait()
    own_kv.wait()
    for copy in copies:
        copy.wait_recv()
    push.finish()


def attend_back(dims, lengths, q, kv, dout, out_t, lse, collective_id):
    team = Team(dims)
    z = dims[0]
    rows = kv.shape[2]
    amount = team.size * rows
    pieces = 2
    piece = (pieces, amount // pieces, LANES)
    count = 3 * (team.size - 1) + pieces * (z + z * len(team.sides))
    others = max(len(team.sides), 1)
    ring_steps, side_steps = max(z - 1, 1), z if team.sides else 1
    return pl.pallas_call(
        functools.partial(attend_back_kernel, team, 256, pieces),
        out_shape=(
            jax.ShapeDtypeStruct(q.shape, low),
            jax.ShapeDtypeStruct(kv.shape[1:], low),
        ),
        in_specs=[SMEM_SPEC] + [VMEM_SPEC] * 5,
        out_specs=[VMEM_SPEC] * 2,
        scratch_shapes=[
            pltpu.VMEM(q.shape, low),
            pltpu.VMEM((amount // pieces, LANES), low),
            pltpu.VMEM((HD, amount // pieces), low),
            pltpu.VMEM((amount // pieces, LANES), low),
            pltpu.VMEM((LANES, amount), low),
            pltpu.VMEM((LANES, amount), low),
            pltpu.VMEM((HD, amount), jnp.float32),
            pltpu.VMEM((HD, amount), low),
            pltpu.VMEM((HD, amount), low),
            pltpu.VMEM((side_steps, others) + piece, low),
            pltpu.VMEM((side_steps, others) + piece, low),
            pltpu.VMEM((ring_steps,) + piece, low),
            pltpu.VMEM((ring_steps,) + piece, low),
            pltpu.VMEM(piece, jnp.float32),
            pltpu.VMEM(q.shape, low),
            pltpu.VMEM(kv.shape[1:], low),
            pltpu.SemaphoreType.DMA((count,)),
            pltpu.SemaphoreType.DMA((count,)),
            pltpu.SemaphoreType.DMA((3,)),
        ],
        compiler_params=pltpu.CompilerParams(
            collective_id=collective_id, has_side_effects=True, vmem_limit_bytes=60 * MIB
        ),
        name="attend_back",
    )(lengths, q, kv, dout, out_t, lse)


def part_shapes(n_head):
    width = HEADS // n_head * HD
    hidden = FF // n_head
    return (
        (D, width, True),
        (DI, 2 * width, True),
        (width, D, False),
        (D, 3 * width, True),
        (width, D, False),
        (D, hidden, True),
        (hidden, D, False),
        (D, C // n_head, True),
    )


def borders(n_head):
    result = [0]
    for rows, columns, joined in part_shapes(n_head):
        result.append(result[-1] + rows * columns // LANES)
    return result


def period(columns):
    amount = 1
    while amount * columns % LANES:
        amount *= 2
    return amount


def segments(start, amount, unit):
    result = []
    while amount > 0:
        which, at = divmod(start, unit)
        size = min(unit - at, amount)
        result.append((which, at, at + size))
        start, amount = start + size, amount - size
    return result


def joined_lanes(pieces):
    return pieces[0] if len(pieces) == 1 else jnp.concatenate(pieces, 1)


def lane_blocks(value):
    rows, columns = value.shape
    missing = -columns % LANES
    if missing:
        value = jnp.concatenate([value, jnp.zeros((rows, missing), value.dtype)], 1)
    return [value[:, i : i + LANES] for i in range(0, columns + missing, LANES)]


def every(first, amount, stride):
    return pl.ds(first, amount) if stride == 1 else pl.ds(first, amount, stride=stride)


def matrix_of(stage, first, rows, columns, line):
    if columns % LANES == 0:
        stride = columns // LANES
        for j in range(stride):
            yield j * LANES, stage[every(first + j, rows, stride), :]
        return
    height = period(columns)
    stride = height * columns // LANES
    for k in range(height):
        pieces = [
            stage[every(first + which, rows // height, stride), :][:, begin:end]
            for which, begin, end in segments(k * columns, columns, LANES)
        ]
        for i, piece in enumerate(lane_blocks(joined_lanes(pieces))):
            line[i, every(k, rows // height, height), :] = piece
    for i in range(-(-columns // LANES)):
        yield i * LANES, line[i, :rows, : min(columns - i * LANES, LANES)]


def matrix_into(stage, first, value, line):
    rows, columns = value.shape
    if columns % LANES == 0:
        stride = columns // LANES
        for j in range(stride):
            stage[every(first + j, rows, stride), :] = value[:, j * LANES : (j + 1) * LANES]
        return
    height = period(columns)
    stride = height * columns // LANES
    for i, piece in enumerate(lane_blocks(value)):
        line[i, :rows, :] = piece
    for i in range(stride):
        pieces = [
            line[which, every(k, rows // height, height), :][:, begin:end]
            for k, first_lane, last_lane in segments(i * LANES, LANES, columns)
            for which, begin, end in segments(first_lane, last_lane - first_lane, LANES)
        ]
        stage[every(first + i, rows // height, stride), :] = joined_lanes(pieces)


def load_stage(stage, held, first_shard, shard_rows, group):
    for b in range(held.shape[0]):
        stage[pl.ds(b * shard_rows, shard_rows), :] = held[b, group, :shard_rows, :].astype(jnp.float32)


def load_common(stage, held, valid):
    piece = held.shape[2]
    for b in range(held.shape[0]):
        for k in range(held.shape[1]):
            amount = min(piece, valid - k * piece)
            stage[b * valid + k * piece : b * valid + k * piece + amount, :] = held[b, k].astype(
                jnp.float32
            )[:amount]


def common_blocks(first_row, last_row, valid):
    return first_row // valid, -(-last_row // valid) - first_row // valid


def load_matrices(stage, first_row, n_head, group, which, targets, line):
    starts, shapes = borders(n_head), part_shapes(n_head)
    for m, target in zip(which, targets):
        rows, columns, joined = shapes[m]
        row = 0 if joined else group * rows
        column = group * columns if joined else 0
        for j, value in matrix_of(stage, starts[m] - first_row, rows, columns, line):
            size = value.shape[1]
            target[row : row + rows, column + j : column + j + size] = value.astype(target.dtype)


def normalized(x):
    centre = x - jnp.mean(x, -1, keepdims=True)
    rate = lax.rsqrt(jnp.mean(centre * centre, -1, keepdims=True) + norm_eps)
    return centre * rate, rate


def layer_norm(x, gain):
    return normalized(x)[0] * gain


def norm_pullback(x, gain, grad):
    unit, rate = normalized(x)
    inside = grad * gain
    both = jnp.mean(inside * unit, -1, keepdims=True)
    d_x = rate * (inside - jnp.mean(inside, -1, keepdims=True) - unit * both)
    return d_x, jnp.sum(grad * unit, 0, keepdims=True)


def head_lanes(group, heads, value):
    width = heads * HD
    block = value[:, group * width : (group + 1) * width]
    lane = lax.broadcasted_iota(jnp.int32, (1, width), 1)
    result = []
    for a in range(heads):
        here = (lane >= a * HD) & (lane < (a + 1) * HD)
        result.append((here, jnp.where(here, block, jnp.zeros_like(block))))
    return result


def place_of(bounds, first, amount):
    row = first + lax.broadcasted_iota(jnp.int32, (amount, 1), 0)
    opening = jnp.zeros((amount, 1), jnp.int32)
    for begin, end in bounds:
        opening = jnp.where((row >= begin) & (row < end), begin, opening)
    offset = row - opening
    turns = jnp.floor((offset.astype(jnp.float32) + 0.5) * (1.0 / LAT)).astype(jnp.int32)
    return offset - turns * LAT


def picked_rows(bounds, rows, n_head):
    first = lax.axis_index("blk") * (rows * n_head) + lax.axis_index("head") * rows
    lane = lax.broadcasted_iota(jnp.int32, (rows, LAT), 1)
    return jnp.where(lane == place_of(bounds, first, rows), 1.0, 0.0).astype(low)


def enc_scores(q_head, keys):
    return against(q_head, keys) * (SCORE_SCALE * LOG2E)


def encode_kernel(
    n_head,
    shard_rows,
    valid,
    rows,
    lengths,
    weights,
    common,
    inputs_t,
    enc_query,
    enc_keyval,
    enc_output,
    self_project,
    gains,
    z_zero,
    h_zero,
    x_norm_t,
    q_enc,
    kv_enc,
    o_enc,
    z_one,
    h_one,
    q_self,
    kv_self,
    counts,
    label_counts,
    held,
    held_common,
    held_counts,
    stage,
    stage_common,
    line,
    latent_table,
    sems,
):
    heads = HEADS // n_head
    width = heads * HD
    shards = held.shape[0]
    bounds = clip_bounds(lengths)
    first = DQ * D // LANES
    block, blocks = common_blocks(first, first + (LAT + 4) * D // LANES, valid)
    tail = shard_rows // TILE * TILE
    copies = [
        pltpu.make_async_copy(common.at[pl.ds(block, blocks)], held_common, sems.at[0]),
        pltpu.make_async_copy(weights.at[pl.ds(0, shards)], held, sems.at[1]),
        pltpu.make_async_copy(weights.at[:, :, pl.ds(tail, TILE)], held_counts, sems.at[2]),
    ]
    for copy in copies:
        copy.start()
    centre = inputs_t[...].astype(jnp.float32)
    centre = centre - jnp.mean(centre, 0, keepdims=True)
    rate = lax.rsqrt(jnp.mean(centre * centre, 0, keepdims=True) + norm_eps)
    x_norm_t[...] = (centre * rate).astype(low)
    copies[0].wait()
    load_common(stage_common, held_common, valid)
    first = first - block * valid
    for j, value in matrix_of(stage_common, first, LAT, D, line):
        latent_table[:, j : j + LANES] = value.astype(low)
    for j, value in matrix_of(stage_common, first + LAT * D // LANES, 4, D, line):
        gains[:, j : j + LANES] = value
    picked = picked_rows(bounds, rows, n_head)
    z_zero[...] = product(picked, latent_table[...])
    h_zero[...] = layer_norm(z_zero[...], gains[0:1, :]).astype(low)
    copies[2].wait()
    counted = held_counts[...].astype(jnp.float32)[:, :, shard_rows - tail : shard_rows - tail + 1]
    counts[...] = jnp.broadcast_to(jnp.sum(counted, (0, 1)), counts.shape)
    label_counts[...] = counts[:1, :MODES]
    copies[1].wait()
    for g in range(n_head):
        load_stage(stage, held, 0, shard_rows, g)
        load_matrices(
            stage, 0, n_head, g, (0, 1, 2, 3), (enc_query, enc_keyval, enc_output, self_project), line
        )
    q_enc[...] = product(h_zero[...], enc_query[...]).astype(low)
    kv_enc[...] = contract_first(x_norm_t[...], enc_keyval[...]).astype(low)
    for g in range(n_head):
        keys = kv_enc[:, 2 * g * width : (2 * g + 1) * width]
        values = kv_enc[:, (2 * g + 1) * width : (2 * g + 2) * width]
        outcome = jnp.zeros((rows, width), jnp.float32)
        for here, q_head in head_lanes(g, heads, q_enc[...]):
            scores = enc_scores(q_head, keys)
            probs = jnp.exp2((scores - jnp.max(scores, 1, keepdims=True)).astype(low))
            total = jnp.sum(probs.astype(jnp.float32), 1, keepdims=True)
            outcome = jnp.where(here, product(probs, values) / total, outcome)
        o_enc[:, g * width : (g + 1) * width] = outcome.astype(low)
    z_one[...] = z_zero[...] + product(o_enc[...], enc_output[...])
    h_one[...] = layer_norm(z_one[...], gains[1:2, :]).astype(low)
    projected = product(h_one[...], self_project[...]).astype(low)
    for slot, (g, a) in enumerate(heads_of(n_head, q_self.shape[0])):
        query, key, value = (
            projected[:, (3 * g + i) * width + a * HD : (3 * g + i) * width + (a + 1) * HD]
            for i in range(3)
        )
        q_self[slot] = pack(query)
        kv_self[slot] = jnp.concatenate([key, value], 1)


LINE = pltpu.VMEM((4, round_up(max(D, DI), 8), LANES), jnp.float32)


def shards_of(n_head, shard_rows, first, last):
    starts = borders(n_head)
    begin = starts[first] // shard_rows
    return begin, -(-starts[last] // shard_rows) - begin


def encode(lengths, weights, common, inputs_t, valid, rows, slots, n_head, shard_rows):
    begin, shards = shards_of(n_head, shard_rows, 0, 4)
    query_rows = DQ * D // LANES
    block, blocks = common_blocks(query_rows, query_rows + (LAT + 4) * D // LANES, valid)
    keys = inputs_t.shape[1]
    return pl.pallas_call(
        functools.partial(encode_kernel, n_head, shard_rows, valid, rows),
        out_shape=[
            shape_of((D, D)),
            shape_of((DI, 2 * D)),
            shape_of((D, D)),
            shape_of((D, 3 * D)),
            shape_of((4, D), jnp.float32),
            shape_of((rows, D), jnp.float32),
            shape_of((rows, D)),
            shape_of(inputs_t.shape),
            shape_of((rows, D)),
            shape_of((keys, 2 * D)),
            shape_of((rows, D)),
            shape_of((rows, D), jnp.float32),
            shape_of((rows, D)),
            shape_of((slots, rows // 2, LANES)),
            shape_of((slots, rows, LANES)),
            shape_of((8, LANES), jnp.float32),
            shape_of((1, MODES), jnp.float32),
        ],
        in_specs=[SMEM_SPEC, ANY_SPEC, ANY_SPEC, VMEM_SPEC],
        out_specs=[VMEM_SPEC] * 17,
        scratch_shapes=[
            pltpu.VMEM((shards,) + weights.shape[1:], low),
            pltpu.VMEM((blocks,) + common.shape[1:], low),
            pltpu.VMEM(weights.shape[:2] + (TILE, LANES), low),
            pltpu.VMEM((shards * shard_rows, LANES), jnp.float32),
            pltpu.VMEM((blocks * valid, LANES), jnp.float32),
            LINE,
            pltpu.VMEM((LAT, D), low),
            pltpu.SemaphoreType.DMA((3,)),
        ],
        compiler_params=pltpu.CompilerParams(vmem_limit_bytes=56 * MIB),
        name="encode",
    )(lengths, weights, common, inputs_t)


def gelu_and_slope(x):
    rate = (2.0 / jnp.pi) ** 0.5
    cubic = 0.044715
    t = jnp.tanh(rate * (x + cubic * x * x * x))
    slope = 0.5 * (1.0 + t) + 0.5 * x * (1.0 - t * t) * rate * (1.0 + 3.0 * cubic * x * x)
    return 0.5 * x * (1.0 + t), slope


def my_column(marks, rows):
    turned = marks[...].astype(jnp.float32).T
    column = lax.broadcasted_iota(jnp.int32, turned.shape, 1)
    per_head = rows // LANES
    first = lax.axis_index("head") * per_head
    picked = [
        jnp.sum(jnp.where(column == first + k, turned, 0.0), 1, keepdims=True)
        for k in range(per_head)
    ]
    return jnp.concatenate(picked, 0) if per_head > 1 else picked[0]


def middle_kernel(
    n_head,
    shard_rows,
    valid,
    first_shard,
    rows,
    counts,
    weights,
    common,
    z_one,
    o_self,
    out_queries_t,
    labels,
    modality,
    labeled,
    gains,
    dout,
    d_two_out,
    tile,
    query_grad,
    gain_grads,
    grads,
    held,
    held_common,
    stage,
    stage_common,
    line,
    self_output,
    hidden_in,
    hidden_out,
    class_table,
    query_table,
    slope,
    activ,
    sems,
):
    heads = HEADS // n_head
    width, hidden, classes = heads * HD, FF // n_head, C // n_head
    shards = held.shape[0]
    first_row = first_shard * shard_rows
    starts = borders(n_head)
    copies = [
        pltpu.make_async_copy(common.at[pl.ds(0, held_common.shape[0])], held_common, sems.at[0]),
        pltpu.make_async_copy(weights.at[pl.ds(first_shard, shards)], held, sems.at[1]),
    ]
    for copy in copies:
        copy.start()
    copies[0].wait()
    load_common(stage_common, held_common, valid)
    for j, value in matrix_of(stage_common, 0, DQ, D, line):
        query_table[:, j : j + LANES] = value.astype(low)
    copies[1].wait()
    for g in range(n_head):
        load_stage(stage, held, first_shard, shard_rows, g)
        load_matrices(
            stage, first_row, n_head, g, (4, 5, 6, 7), (self_output, hidden_in, hidden_out, class_table), line
        )
    gain_two, gain_three = gains[2:3, :], gains[3:4, :]
    o_heads = {head: unpack(o_self[s]) for s, head in enumerate(heads_of(n_head, o_self.shape[0]))}
    o_groups = [joined_lanes([o_heads[(g, a)] for a in range(heads)]) for g in range(n_head)]
    o_low = jnp.concatenate(o_groups, 1)
    z_two = z_one[...] + product(o_low, self_output[...])
    h_two = layer_norm(z_two, gain_two).astype(low)
    value, bend = gelu_and_slope(product(h_two, hidden_in[...]))
    activ[...] = value.astype(low)
    slope[...] = bend
    z_three = z_two + product(activ[...], hidden_out[...])
    queries_t = out_queries_t[...]
    decoded = layer_norm(z_three, gain_three) + contract_first(queries_t, query_table[...])
    decoded = decoded.astype(low)
    logits = product(decoded, class_table[...])
    label, kind, counted = (my_column(marks, rows) for marks in (labels, modality, labeled))
    lane = lax.broadcasted_iota(jnp.int32, (rows, C), 1).astype(jnp.float32)
    is_target = jnp.where(lane == label, 1.0, 0.0)
    row_top = jnp.max(logits, 1, keepdims=True)
    row_lse = row_top + jnp.log(jnp.sum(jnp.exp2((logits - row_top) * LOG2E), 1, keepdims=True))
    loss = row_lse - jnp.sum(is_target * logits, 1, keepdims=True)
    weight = jnp.zeros((rows, 1), jnp.float32)
    place = lax.broadcasted_iota(jnp.int32, (1, LANES), 1)
    losses = jnp.zeros((1, LANES), jnp.float32)
    for m in range(MODES):
        member = jnp.where((kind == m) & (counted == 1.0), 1.0, 0.0)
        weight = weight + member / jnp.maximum(counts[0:1, m : m + 1], 1.0)
        losses = losses + jnp.where(place == m, jnp.sum(loss * member, 0, keepdims=True), 0.0)
    tile[...] = jnp.broadcast_to(losses, tile.shape)
    dlogits = (weight * (jnp.exp2((logits - row_lse) * LOG2E) - is_target)).astype(low)
    d_decoded = against(dlogits, class_table[...])
    matrix_into(query_grad, 0, product(queries_t, d_decoded.astype(low)), line)
    d_three, gain_three_grad = norm_pullback(z_three, gain_three, d_decoded)
    d_branch = d_three.astype(low)
    d_pre = (slope[...] * against(d_branch, hidden_out[...])).astype(low)
    d_middle, gain_two_grad = norm_pullback(z_two, gain_two, against(d_pre, hidden_in[...]))
    d_two = d_three + d_middle
    d_two_out[...] = d_two
    gain_grads[...] = jnp.concatenate([gain_two_grad, gain_three_grad], 0)
    d_two_low = d_two.astype(low)
    d_o = against(d_two_low, self_output[...]).astype(low)
    for slot, (g, a) in enumerate(heads_of(n_head, o_self.shape[0])):
        dout[slot] = pack(d_o[:, g * width + a * HD : g * width + (a + 1) * HD])
    for g in range(n_head):
        results = (
            contract_first(o_groups[g], d_two_low),
            contract_first(h_two, d_pre[:, g * hidden : (g + 1) * hidden]),
            contract_first(activ[:, g * hidden : (g + 1) * hidden], d_branch),
            contract_first(decoded, dlogits[:, g * classes : (g + 1) * classes]),
        )
        for m, result in zip((4, 5, 6, 7), results):
            matrix_into(stage, starts[m] - first_row, result, line)
        for b in range(shards):
            held[b, g, :shard_rows, :] = stage[pl.ds(b * shard_rows, shard_rows), :].astype(low)
    back = pltpu.make_async_copy(held, grads.at[pl.ds(first_shard, shards)], sems.at[2])
    back.start()
    back.wait()


def middle(counts, weights, common, z_one, o_self, out_queries_t, marks, gains, valid, n_head, shard_rows):
    rows = z_one.shape[0]
    begin, shards = shards_of(n_head, shard_rows, 4, 8)
    query_rows = DQ * D // LANES
    block, blocks = common_blocks(0, query_rows, valid)
    return pl.pallas_call(
        functools.partial(middle_kernel, n_head, shard_rows, valid, begin, rows),
        grid=(1,),
        out_shape=[
            shape_of(o_self.shape),
            shape_of((rows, D), jnp.float32),
            shape_of((8, LANES), jnp.float32),
            shape_of((query_rows, LANES), jnp.float32),
            shape_of((2, D), jnp.float32),
            shape_of(weights.shape),
        ],
        in_specs=[
            VMEM_SPEC,
            ANY_SPEC,
            ANY_SPEC,
            VMEM_SPEC,
            VMEM_SPEC,
            pl.BlockSpec((DQ, rows), lambda i: (0, lax.axis_index("head"))),
            VMEM_SPEC,
            VMEM_SPEC,
            VMEM_SPEC,
            VMEM_SPEC,
        ],
        out_specs=[VMEM_SPEC] * 5 + [ANY_SPEC],
        scratch_shapes=[
            pltpu.VMEM((shards,) + weights.shape[1:], low),
            pltpu.VMEM((blocks,) + common.shape[1:], low),
            pltpu.VMEM((shards * shard_rows, LANES), jnp.float32),
            pltpu.VMEM((blocks * valid, LANES), jnp.float32),
            LINE,
            pltpu.VMEM((D, D), low),
            pltpu.VMEM((D, FF), low),
            pltpu.VMEM((FF, D), low),
            pltpu.VMEM((D, C), low),
            pltpu.VMEM((DQ, D), low),
            pltpu.VMEM((rows, FF), jnp.float32),
            pltpu.VMEM((rows, FF), low),
            pltpu.SemaphoreType.DMA((3,)),
        ],
        compiler_params=pltpu.CompilerParams(vmem_limit_bytes=56 * MIB),
        name="middle",
    )(counts, weights, common, z_one, o_self, out_queries_t, *marks, gains)


def ending_kernel(
    n_head,
    shard_rows,
    valid,
    rows,
    lengths,
    grads_in,
    d_q_self,
    d_kv_self,
    d_two,
    gains,
    gain_grads,
    query_grad,
    enc_query,
    enc_keyval,
    enc_output,
    self_project,
    z_zero,
    h_zero,
    x_norm_t,
    q_enc,
    kv_enc,
    o_enc,
    z_one,
    h_one,
    grads,
    common_grad,
    held,
    stage,
    stage_common,
    line,
    d_q,
    d_kv,
    sems,
):
    heads = HEADS // n_head
    width = heads * HD
    shards = held.shape[0]
    starts = borders(n_head)
    shared = pltpu.make_async_copy(grads_in.at[pl.ds(shards - 1, 1)], held.at[pl.ds(shards - 1, 1)], sems.at[0])
    shared.start()
    d_heads = {}
    for slot, head in enumerate(heads_of(n_head, d_kv_self.shape[0])):
        d_kv_head = d_kv_self[slot]
        d_heads[head] = (unpack(d_q_self[slot]), d_kv_head[:, :HD], d_kv_head[:, HD:])
    d_projected = [
        jnp.concatenate([d_heads[(g, a)][i] for i in range(3) for a in range(heads)], 1)
        for g in range(n_head)
    ]
    whole = jnp.concatenate(d_projected, 1)
    d_middle, gain_one_grad = norm_pullback(
        z_one[...], gains[1:2, :], against(whole, self_project[...])
    )
    d_one = d_two[...] + d_middle
    d_one_low = d_one.astype(low)
    d_o = against(d_one_low, enc_output[...]).astype(low)
    for g in range(n_head):
        keys = kv_enc[:, 2 * g * width : (2 * g + 1) * width]
        values = kv_enc[:, (2 * g + 1) * width : (2 * g + 2) * width]
        d_key = jnp.zeros(keys.shape, jnp.float32)
        d_value = jnp.zeros(keys.shape, jnp.float32)
        d_query = jnp.zeros((rows, width), jnp.float32)
        for (here, q_head), (unused, do_head) in zip(
            head_lanes(g, heads, q_enc[...]), head_lanes(g, heads, d_o)
        ):
            scores = enc_scores(keys, q_head)
            probs = jnp.exp2((scores - jnp.max(scores, 0, keepdims=True)).astype(low))
            probs = probs.astype(jnp.float32)
            probs = probs / jnp.sum(probs, 0, keepdims=True)
            d_probs = against(values, do_head)
            delta = jnp.sum(probs * d_probs, 0, keepdims=True)
            d_scores = (probs * (d_probs - delta)).astype(low)
            d_value = d_value + product(probs.astype(low), do_head)
            d_key = d_key + product(d_scores, q_head)
            d_query = jnp.where(here, contract_first(d_scores, keys), d_query)
        d_q[:, g * width : (g + 1) * width] = (d_query * SCORE_SCALE).astype(low)
        d_kv[:, 2 * g * width : (2 * g + 1) * width] = (d_key * SCORE_SCALE).astype(low)
        d_kv[:, (2 * g + 1) * width : (2 * g + 2) * width] = d_value.astype(low)
    d_middle, gain_zero_grad = norm_pullback(
        z_zero[...], gains[0:1, :], against(d_q[...], enc_query[...])
    )
    d_zero = d_one + d_middle
    d_zero_top = d_zero.astype(low)
    d_zero_rest = (d_zero - d_zero_top.astype(jnp.float32)).astype(low)
    picked = picked_rows(clip_bounds(lengths), rows, n_head)
    latent_grad = contract_first(picked, d_zero_top) + contract_first(picked, d_zero_rest)
    query_rows = query_grad.shape[0]
    stage_common[:query_rows] = query_grad[...]
    matrix_into(stage_common, query_rows, latent_grad, line)
    all_gains = jnp.concatenate([gain_zero_grad, gain_one_grad, gain_grads[...]], 0)
    matrix_into(stage_common, query_rows + LAT * D // LANES, all_gains, line)
    piece = common_grad.shape[2]
    for b in range(common_grad.shape[0]):
        for k in range(common_grad.shape[1]):
            amount = min(piece, valid - k * piece)
            block = stage_common[b * valid + k * piece : b * valid + k * piece + amount, :]
            if amount < piece:
                block = jnp.concatenate([block, jnp.zeros((piece - amount, LANES), jnp.float32)], 0)
            common_grad[b, k] = block.astype(low)
    shared.wait()
    kept = shards * shard_rows - starts[4]
    for g in range(n_head):
        results = (
            contract_first(h_zero[...], d_q[:, g * width : (g + 1) * width]),
            product(x_norm_t[...], d_kv[:, 2 * g * width : (2 * g + 2) * width]),
            contract_first(o_enc[:, g * width : (g + 1) * width], d_one_low),
            contract_first(h_one[...], d_projected[g]),
        )
        if kept:
            stage[pl.ds((shards - 1) * shard_rows, shard_rows), :] = held[
                shards - 1, g, :shard_rows, :
            ].astype(jnp.float32)
        for m, result in zip((0, 1, 2, 3), results):
            matrix_into(stage, starts[m], result, line)
        for b in range(shards):
            held[b, g, :shard_rows, :] = stage[pl.ds(b * shard_rows, shard_rows), :].astype(low)
    back = pltpu.make_async_copy(held, grads.at[pl.ds(0, shards)], sems.at[1])
    back.start()
    back.wait()


def ending(lengths, grads, d_self, d_two, gains, gain_grads, query_grad, kept, common_shape, valid, shard_rows):
    rows = d_two.shape[0]
    n_head = grads.shape[1]
    begin, shards = shards_of(n_head, shard_rows, 0, 4)
    keys = kept[6].shape[1]
    common_rows = (DQ + LAT + 4) * D // LANES
    return pl.pallas_call(
        functools.partial(ending_kernel, n_head, shard_rows, valid, rows),
        out_shape=[shape_of(grads.shape), shape_of(common_shape)],
        in_specs=[SMEM_SPEC, ANY_SPEC] + [VMEM_SPEC] * 18,
        out_specs=[ANY_SPEC, VMEM_SPEC],
        input_output_aliases={1: 0},
        scratch_shapes=[
            pltpu.VMEM((shards,) + grads.shape[1:], low),
            pltpu.VMEM((shards * shard_rows, LANES), jnp.float32),
            pltpu.VMEM((common_rows, LANES), jnp.float32),
            LINE,
            pltpu.VMEM((rows, D), low),
            pltpu.VMEM((keys, 2 * D), low),
            pltpu.SemaphoreType.DMA((2,)),
        ],
        compiler_params=pltpu.CompilerParams(vmem_limit_bytes=56 * MIB),
        name="ending",
    )(lengths, grads, *d_self, d_two, gains, gain_grads, query_grad, *kept)


def adam_step(weight, first, second, grad):
    first = beta_one * first + (1 - beta_one) * grad
    second = beta_two * second + (1 - beta_two) * grad * grad
    fixed_first = first / (1 - beta_one**STEP)
    fixed_second = second / (1 - beta_two**STEP)
    weight = weight - learn_rate * (
        fixed_first / (jnp.sqrt(fixed_second) + adam_eps) + weight_decay * weight
    )
    return (weight, first, second, weight.astype(low))


def per_device(
    inputs,
    out_queries,
    clip_lengths,
    labels,
    modality,
    labeled,
    head_params,
    head_first,
    head_second,
    common_params,
    common_first,
    common_second,
):
    n_head, n_blk = lax.axis_size("head"), lax.axis_size("blk")
    dims = grid_of(n_blk, n_head)
    rows = labels.shape[0] // n_head
    n_h, n_c = head_params.shape[0], common_params.shape[0]
    shard_rows, common_rows = n_h // LANES, -(-n_c // LANES)
    head_rows = round_up(shard_rows + 1, TILE)
    piece_rows = round_up(-(-common_rows // n_head), TILE)
    marks = [x.reshape(-1, LANES) for x in (labels, modality, labeled)]
    head_wide = head_params.reshape(shard_rows, LANES)
    common_wide = jnp.pad(common_params, (0, common_rows * LANES - n_c)).reshape(common_rows, LANES)
    weights, common = gather_all(dims, marks, (head_wide, common_wide), (head_rows, piece_rows), 0)
    valid = common_rows
    if n_c % LANES:
        common = common.reshape(n_blk, -1)[:, :n_c].reshape(-1, LANES)
        valid = common.shape[0]
        common = jnp.pad(common, ((0, -valid % TILE), (0, 0)))[None, None]

    encoded = encode(
        clip_lengths, weights, common, inputs.T, valid, rows, Team(dims).size, n_head, shard_rows
    )
    gains, z_one, counts = encoded[4], encoded[11], encoded[15]
    o_self, lse_self, out_self_t, q_all, kv_all = attend(
        dims, clip_lengths, encoded[13], encoded[14], 1
    )
    dout, d_two, tile, query_grad, gain_grads, grads = middle(
        counts, weights, common, z_one, o_self, out_queries.T, marks, gains, valid, n_head, shard_rows
    )
    d_self = attend_back(dims, clip_lengths, q_all, kv_all, dout, out_self_t, lse_self, 2)
    kept = encoded[:4] + encoded[5:13]
    grads, common_grad = ending(
        clip_lengths,
        grads,
        d_self,
        d_two,
        gains,
        gain_grads,
        query_grad,
        kept,
        common.shape,
        valid,
        shard_rows,
    )
    if n_c % LANES:
        common_grad = common_grad[0, 0, :valid].reshape(n_blk, n_c)
        common_grad = jnp.pad(common_grad, ((0, 0), (0, n_head * piece_rows * LANES - n_c)))
        common_grad = common_grad.reshape(n_blk, n_head, piece_rows, LANES)
    head_share, common_share, loss_sums, clip_norm, factor = reduce_all(
        dims, (grads, common_grad), (shard_rows, common_rows), tile, 3
    )
    label_counts, loss_sums = encoded[16].reshape(MODES), loss_sums.reshape(MODES)
    clip_norm, factor = clip_norm.reshape(()), factor.reshape(())
    head_share, common_share = head_share.reshape(-1), common_share.reshape(-1)[:n_c]
    head_out = adam_step(head_params, head_first, head_second, head_share * factor)
    common_out = adam_step(common_params, common_first, common_second, common_share * factor)
    return head_out + common_out + (loss_sums, label_counts, clip_norm)


def solution(mesh):
    placed = (
        P("blk", None),
        P("blk", None),
        P(),
        P("blk"),
        P("blk"),
        P("blk"),
        P(("head", "blk")),
        P(("head", "blk")),
        P(("head", "blk")),
        P("blk"),
        P("blk"),
        P("blk"),
    )
    return jax.shard_map(
        per_device,
        mesh=mesh,
        in_specs=placed,
        out_specs=(
            P(("head", "blk")),
            P(("head", "blk")),
            P(("head", "blk")),
            P(("head", "blk")),
            P("blk"),
            P("blk"),
            P("blk"),
            P("blk"),
            P(),
            P(),
            P(),
        ),
        check_vma=False,
    )
```

```python
import functools

import jax
import jax.numpy as jnp
from jax import lax
from jax.experimental import pallas as pl
from jax.experimental.pallas import tpu as pltpu
from jax.sharding import PartitionSpec as P

D = 512
HEADS = 8
HD = 64
FF = 2048
DI = 704
DQ = 1026
C = 704
LAT = 784
MODES = 3
STEP = 10
LANES = 128
TILE = 16

norm_eps = 1e-05
learn_rate = 0.1
beta_one = 0.9
beta_two = 0.999
adam_eps = 1e-08
weight_decay = 0.01
clip_limit = 0.05
big_negative = -1e30
low = jnp.bfloat16
LOG2E = 1.4426950408889634
SCORE_SCALE = HD ** (-0.5)
MESH = pl.DeviceIdType.MESH
MIB = 1 << 20
VMEM_SPEC = pl.BlockSpec(memory_space=pltpu.VMEM)
SMEM_SPEC = pl.BlockSpec(memory_space=pltpu.SMEM)
ANY_SPEC = pl.BlockSpec(memory_space=pl.ANY)


def shape_of(shape, dtype=low):
    return jax.ShapeDtypeStruct(shape, dtype)


def round_up(n, unit):
    return -(-n // unit) * unit


def grid_of(n_blk, n_head):
    cores = 2 if n_head % 2 == 0 else 1
    x = n_head // cores
    y = x if n_blk % x == 0 else 1
    return (n_blk // y, y, x, cores)


def my_place(dims):
    blk, head = lax.axis_index("blk"), lax.axis_index("head")
    return (blk // dims[1], lax.rem(blk, dims[1]), head // dims[3], lax.rem(head, dims[3]))


def shifted(dims, me, offset, sign):
    return tuple(
        m if o == 0 else lax.rem(m + (o if sign > 0 else n - o), n)
        for m, o, n in zip(me, offset, dims)
    )


def blk_of(dims, place):
    return place[0] * dims[1] + place[1]


def head_of(dims, place):
    return place[2] * dims[3] + place[3]


def device_of(dims, place):
    return {"blk": blk_of(dims, place), "head": head_of(dims, place)}


def along(axis, d):
    return tuple(d if a == axis else 0 for a in range(4))


def greet(dims, me, offsets):
    barrier = pltpu.get_barrier_semaphore()
    for offset in offsets:
        pl.semaphore_signal(
            barrier,
            inc=1,
            device_id=device_of(dims, shifted(dims, me, offset, 1)),
            device_id_type=MESH,
        )
    pl.semaphore_wait(barrier, len(offsets))


def axis_peers(dims, axes):
    return [along(axis, d) for axis in axes for d in range(1, dims[axis])]


def remote(src, dst, send_sem, recv_sem, place, dims):
    return pltpu.make_async_remote_copy(
        src_ref=src,
        dst_ref=dst,
        send_sem=send_sem,
        recv_sem=recv_sem,
        device_id=device_of(dims, place),
        device_id_type=MESH,
    )


AHEAD = 6.0
RING = 0


def in_order(first, follow, size_of, ahead, result):
    queues, busy, flight = {}, {}, {}
    now = 0.0

    def ready(messages):
        for message in messages:
            queues.setdefault(message[1], []).append(message)

    ready(first)
    while True:
        for axis in sorted(queues):
            queue, going = queues[axis], flight.setdefault(axis, [])
            while queue and (not going or busy[axis] < now + ahead):
                message = min(queue)
                queue.remove(message)
                busy[axis] = max(now, busy.get(axis, 0.0)) + size_of(message)
                going.append((busy[axis] + 1.5, message))
                result.append((True, message))
        arrivals = [min(going) for going in flight.values() if going]
        if not arrivals:
            return now
        arrival = min(arrivals)
        flight[arrival[1][1]].remove(arrival)
        now = max(now, arrival[0])
        result.append((False, arrival[1]))
        ready(follow(arrival[1]))


def time_of(rows, axis):
    return rows * LANES * 2 / (300e3 if axis == 3 else 45e3)


def with_at(offset, axis, d):
    return offset[:axis] + (d,) + offset[axis + 1 :]


def gather_order(dims, parts):
    def onward(p, offset, position):
        order = parts[p][3]
        result = []
        for k in range(max(position, 0), 4):
            axis = order[k]
            n = dims[axis]
            if k > position:
                steps = [1] if axis == RING else range(1, n)
                steps = [d for d in steps if d < n]
            else:
                steps = [offset[axis] + 1] if axis == RING and offset[axis] + 1 < n else []
            for d in steps:
                result.append(((k, sum(offset), p), axis, p, with_at(offset, axis, d)))
        return result

    def follow(message):
        rank, axis, p, offset = message
        return onward(p, offset, rank[0])

    first = [m for p in range(len(parts)) for m in onward(p, (0, 0, 0, 0), -1)]
    result = []
    now = in_order(first, follow, lambda m: time_of(parts[m[2]][2], m[1]), AHEAD, result)
    return result, now


def gather_kernel(
    dims,
    parts,
    labels,
    modality,
    labeled,
    head_params,
    common_params,
    head_all,
    common_all,
    head_low,
    common_low,
    common_wide,
    send_sem,
    recv_sem,
    own_sem,
):
    me = my_place(dims)
    my_head = head_of(dims, me)
    n_head = dims[2] * dims[3]
    shard_rows, common_rows = head_params.shape[0], common_params.shape[0]
    per_head = labels.shape[0] // n_head
    row = lax.broadcasted_iota(jnp.int32, labels.shape, 0)
    mine = (row >= my_head * per_head) & (row < (my_head + 1) * per_head) & (labeled[...] == 1)
    lane = lax.broadcasted_iota(jnp.int32, (1, LANES), 1)
    counts = jnp.zeros((1, LANES), jnp.float32)
    for m in range(MODES):
        member = jnp.where(mine & (modality[...] == m), 1.0, 0.0)
        counts = counts + jnp.where(lane == m, jnp.sum(member, (0, 1), keepdims=True), 0.0)
    padding = head_low.shape[0] - shard_rows
    tail = shard_rows // TILE * TILE
    head_low[:tail] = head_params[:tail].astype(low)
    last = [jnp.broadcast_to(counts, (padding, LANES))]
    if shard_rows > tail:
        last = [head_params[tail:]] + last
    head_low[tail:] = jnp.concatenate(last, 0).astype(low)
    common_wide[...] = jnp.zeros(common_wide.shape, jnp.float32)
    common_wide[:common_rows] = common_params[...]
    piece = common_low.shape[0]
    common_low[...] = common_wide[pl.ds(pl.multiple_of(my_head * piece, TILE), piece)].astype(low)

    greet(dims, me, ring_and_others(dims))
    srcs, outs = (head_low, common_low), (head_all, common_all)
    copies = {}

    def block(p, offset):
        place = shifted(dims, me, offset, -1)
        array, first, rows, order = parts[p]
        return outs[array].at[blk_of(dims, place), head_of(dims, place), pl.ds(first, rows)]

    own = []
    for is_send, (rank, axis, p, offset) in gather_order(dims, parts)[0]:
        if is_send:
            step = 1 if axis == RING else offset[axis]
            before = with_at(offset, axis, offset[axis] - step)
            array, first, rows, order = parts[p]
            source = block(p, before) if any(before) else srcs[array].at[pl.ds(first, rows)]
            i = len(copies)
            copies[(p, offset)] = remote(
                source,
                block(p, before),
                send_sem.at[i],
                recv_sem.at[i],
                shifted(dims, me, along(axis, step), 1),
                dims,
            )
            copies[(p, offset)].start()
        else:
            if not own:
                for array in range(2):
                    copy = pltpu.make_async_copy(
                        srcs[array], outs[array].at[blk_of(dims, me), my_head], own_sem.at[array]
                    )
                    copy.start()
                    own.append(copy)
            copies[(p, offset)].wait_recv()
    for copy in copies.values():
        copy.wait_send()
    for copy in own:
        copy.wait()


def ring_and_others(dims):
    ring = {along(RING, 1 % dims[RING]), along(RING, (dims[RING] - 1) % dims[RING])}
    return sorted(ring - {(0, 0, 0, 0)}) + axis_peers(dims, (1, 2, 3))


def cut(array, rows, shares):
    result = []
    first, so_far = 0, 0
    whole = sum(share for share, order in shares)
    for share, order in shares:
        so_far += share
        end = rows * so_far // whole // TILE * TILE if so_far < whole else rows
        if end > first:
            result.append((array, first, end - first, order))
        first = end
    return tuple(result)


ZYXC, ZXYC, YXZC, XYZC = (0, 1, 2, 3), (0, 2, 1, 3), (1, 2, 0, 3), (2, 1, 0, 3)
GATHER_SHARES = ((8, ZYXC), (6, ZXYC), (2, YXZC), (2, XYZC))
REDUCE_SHARES = ((7, ZYXC), (7, ZXYC), (2, YXZC), (2, XYZC))


def gather_all(dims, marks, params, rows, collective_id):
    z, y, x, cores = dims
    parts = cut(0, rows[0], GATHER_SHARES) + cut(1, rows[1], ((1, ZXYC),))
    count = len(parts) * (z * y * x * cores - 1)
    return pl.pallas_call(
        functools.partial(gather_kernel, dims, parts),
        out_shape=[shape_of((z * y, x * cores, n, LANES)) for n in rows],
        in_specs=[VMEM_SPEC] * 5,
        out_specs=[ANY_SPEC] * 2,
        scratch_shapes=[pltpu.VMEM((n, LANES), low) for n in rows]
        + [
            pltpu.VMEM((x * cores * rows[1], LANES), jnp.float32),
            pltpu.SemaphoreType.DMA((count,)),
            pltpu.SemaphoreType.DMA((count,)),
            pltpu.SemaphoreType.DMA((2,)),
        ],
        compiler_params=pltpu.CompilerParams(collective_id=collective_id, has_side_effects=True),
        name="gather_weights",
    )(*marks, *params)


def reduce_order(dims, parts):
    ready, arrived, order = set(), set(), []

    def message(p, position, offset):
        z = offset[RING]
        rank = (dims[RING] - z if z else dims[RING], position, tuple(-o for o in offset), p)
        return (rank, parts[p][3][position], p, position, offset)

    def done(p, position, offset):
        ready.add((p, position, offset))
        if position == 4:
            return []
        axis = parts[p][3][position]
        d = offset[axis]
        first = d != 0 and (axis != RING or d == dims[axis] - 1)
        return ([message(p, position, offset)] if first else []) + advance(p, position, offset)

    def advance(p, position, offset):
        axis = parts[p][3][position]
        n = dims[axis]
        start = with_at(offset, axis, 0)
        if axis == RING:
            here = (p, position, offset)
            if here in ready and here in arrived:
                order.append((None, here))
                if offset[axis]:
                    return [message(p, position, offset)]
                return done(p, position + 1, offset)
        elif (p, position, start) in ready and (p, position + 1, start) not in ready:
            if all((p, position, with_at(start, axis, d)) in arrived for d in range(1, n)):
                order.append((None, (p, position, start)))
                return done(p, position + 1, start)
        return []

    def follow(sent):
        rank, axis, p, position, offset = sent
        here = with_at(offset, axis, offset[axis] - 1) if axis == RING else offset
        arrived.add((p, position, here))
        return advance(p, position, here)

    first = []
    for p in range(len(parts)):
        for offset in all_offsets(dims, range(4)):
            first += done(p, 0, offset)
    now = in_order(first, follow, lambda m: time_of(parts[m[2]][2], m[1]), AHEAD, order)
    return order, now


def all_offsets(dims, axes):
    offsets = [(0, 0, 0, 0)]
    for a in axes:
        offsets = [with_at(o, a, d) for o in offsets for d in range(dims[a])]
    return offsets


def reduce_kernel(dims, parts, *refs):
    srcs, tile = refs[:2], refs[2]
    head_out, common_out, losses, norm, factor = refs[3:8]
    places = len(parts) * 4
    buffers = refs[8 : 8 + places]
    head_sum, common_sum, shares, send_sem, recv_sem, near_tiles, far_tiles = refs[8 + places :]
    sums = (head_sum, common_sum)
    me = my_place(dims)
    z, y, x, cores = dims
    across = peers_across(dims)
    others = [o for o in all_offsets(dims, (0, 1)) if any(o)]
    met = ring_and_others(dims)
    greet(dims, me, met + [o for o in across + others if o not in met])
    push = Pushes(dims, me, send_sem, recv_sem)
    copies = {}

    def slot(p, position, offset):
        order = parts[p][3]
        axis = order[position]
        rest = [o for o in all_offsets(dims, order[position + 1 :])]
        k = rest.index(with_at(offset, axis, 0))
        return buffers[p * 4 + position].at[k, max(offset[axis] - 1, 0)]

    def summed(p, position, offset):
        array, first, rows, order = parts[p]
        if position == 0:
            place = shifted(dims, me, offset, 1)
            return srcs[array].at[blk_of(dims, place), head_of(dims, place), pl.ds(first, rows)]
        return slot(p, position - 1, offset)

    def ring_slot(p, position, offset):
        axis = parts[p][3][position]
        return slot(p, position, with_at(offset, axis, offset[axis] + 1))

    def add(p, position, offset):
        array, first, rows, order = parts[p]
        axis = order[position]
        if axis == RING:
            arrivals = [ring_slot(p, position, offset)]
        else:
            arrivals = [slot(p, position, with_at(offset, axis, d)) for d in range(1, dims[axis])]
        mine = summed(p, position, offset)
        step = row_chunk(rows)

        @pl.loop(0, rows // step)
        def some_rows(n):
            at = pl.ds(pl.multiple_of(n * step, step), step)
            total = mine[at].astype(jnp.float32)
            for arrival in arrivals:
                total = total + arrival[at].astype(jnp.float32)
            if position == 3 and not any(offset):
                sums[array][pl.ds(pl.multiple_of(first + n * step, TILE), step)] = total
            else:
                arrivals[0][at] = total.astype(low)

    for is_send, what in reduce_order(dims, parts)[0]:
        if is_send is None:
            add(*what)
        elif is_send:
            rank, axis, p, position, offset = what
            d = offset[axis]
            started = axis != RING or d == dims[axis] - 1
            source = summed(p, position, offset) if started else ring_slot(p, position, offset)
            step = along(axis, 1 if axis == RING else d)
            copies[what] = push(source, slot(p, position, offset), step)
        else:
            copies[what].wait_recv()
    my_head, my_blk = head_of(dims, me), blk_of(dims, me)
    shares[my_head] = common_sum[...].astype(low)
    share_copies = [push(shares.at[my_head], shares.at[my_head], o) for o in across]
    amount = head_out.shape[0]
    head_out[...] = head_sum[:amount]
    squares = jnp.sum(head_sum[:amount] * head_sum[:amount], 0, keepdims=True)
    squares = squares + jnp.sum(common_sum[...] * common_sum[...], 0, keepdims=True)
    lane = lax.broadcasted_iota(jnp.int32, (1, LANES), 1)
    near_tiles[my_head] = tile[...] + jnp.where(
        lane == MODES, jnp.sum(squares, 1, keepdims=True), 0.0
    )
    near = [push(near_tiles.at[my_head], near_tiles.at[my_head], o) for o in across]
    for copy in near:
        copy.wait_recv()
    far_tiles[my_blk] = jnp.sum(near_tiles[...], 0)
    far = [push(far_tiles.at[my_blk], far_tiles.at[my_blk], o) for o in others]
    for copy in share_copies:
        copy.wait_recv()
    piece = shares.shape[1]
    for k in range(x * cores):
        amount = min(piece, common_out.shape[0] - k * piece)
        common_out[k * piece : k * piece + amount] = shares[k].astype(jnp.float32)[:amount]
    for copy in far:
        copy.wait_recv()
    totals = jnp.sum(far_tiles[...], 0)[:1]
    losses[...] = totals[:, :MODES]
    norm[...] = jnp.sqrt(totals[:, MODES : MODES + 1])
    factor[...] = jnp.minimum(1.0, clip_limit / norm[...])
    push.finish()


def row_chunk(rows):
    for count in (4, 3, 2):
        if rows % (count * TILE) == 0:
            return rows // count
    return rows


def reduce_all(dims, arrays, valid, tile, collective_id):
    z, y, x, cores = dims
    rows = [array.shape[2] for array in arrays]
    parts = cut(0, rows[0], [(share, order[::-1]) for share, order in REDUCE_SHARES])
    parts = parts + cut(1, rows[1], ((1, ZXYC[::-1]),))
    scratch = []
    for array, first, amount, order in parts:
        for position, axis in enumerate(order):
            rest = len(all_offsets(dims, order[position + 1 :]))
            scratch.append(pltpu.VMEM((rest, dims[axis] - 1, amount, LANES), low))
    count = len(parts) * (z * y * x * cores - 1) + 2 * (x * cores - 1) + z * y - 1
    return pl.pallas_call(
        functools.partial(reduce_kernel, dims, parts),
        out_shape=[
            shape_of((valid[0], LANES), jnp.float32),
            shape_of((valid[1], LANES), jnp.float32),
            shape_of((1, MODES), jnp.float32),
            shape_of((1, 1), jnp.float32),
            shape_of((1, 1), jnp.float32),
        ],
        in_specs=[VMEM_SPEC] * 3,
        out_specs=[VMEM_SPEC] * 5,
        scratch_shapes=scratch
        + [pltpu.VMEM((n, LANES), jnp.float32) for n in rows]
        + [
            pltpu.VMEM((x * cores, rows[1], LANES), low),
            pltpu.SemaphoreType.DMA((count,)),
            pltpu.SemaphoreType.DMA((count,)),
            pltpu.VMEM((x * cores, 8, LANES), jnp.float32),
            pltpu.VMEM((z * y, 8, LANES), jnp.float32),
        ],
        compiler_params=pltpu.CompilerParams(
            collective_id=collective_id, has_side_effects=True, vmem_limit_bytes=60 * MIB
        ),
        name="reduce_gradients",
    )(*arrays, tile)


def contract_first(a, b):
    return lax.dot_general(a, b, (((0,), (0,)), ((), ())), preferred_element_type=jnp.float32)


def product(a, b):
    return jnp.dot(a, b, preferred_element_type=jnp.float32)


def against(a, b):
    return lax.dot_general(a, b, (((1,), (1,)), ((), ())), preferred_element_type=jnp.float32)


def clip_bounds(lengths):
    result, first = [], 0
    for clip in range(lengths.shape[0]):
        end = first + lengths[clip]
        result.append((first, end))
        first = end
    return result


def clip_borders(bounds, place):
    opening = jnp.zeros(place.shape, jnp.int32)
    ending = jnp.full(place.shape, 1 << 30, jnp.int32)
    for clip, (begin, end) in enumerate(bounds):
        here = place == clip
        opening = jnp.where(here, begin, opening)
        ending = jnp.where(here, end, ending)
    return opening, ending


def low_half(axis):
    return lax.broadcasted_iota(jnp.int32, (1, LANES) if axis else (LANES, 1), axis) < HD


def with_key_tail(bounds, first_row, kv):
    clips = len(bounds)
    place = lax.broadcasted_iota(jnp.int32, (1, LANES), 1) - HD
    opening, ending = clip_borders(bounds, place)
    ones = jnp.where((place >= clips) & (place < clips + 3), 1.0, 0.0)
    row = first_row + lax.broadcasted_iota(jnp.int32, kv.shape, 0)
    tail = jnp.where((row >= opening) & (row < ending), ones, big_negative)
    return jnp.where(low_half(1), kv.astype(jnp.float32), tail).astype(low)


def with_value_tail(kv):
    place = lax.broadcasted_iota(jnp.int32, (1, LANES), 1)
    ones = jnp.where(place < 3, 1.0, 0.0)
    return jnp.where(low_half(1), ones, kv.astype(jnp.float32)).astype(low)


def in_three(place, value):
    top = value.astype(low).astype(jnp.float32)
    middle = (value - top).astype(low).astype(jnp.float32)
    bottom = value - top - middle
    return (
        jnp.where(place == 0, top, 0.0)
        + jnp.where(place == 1, middle, 0.0)
        + jnp.where(place == 2, bottom, 0.0)
    )


def with_query_tail(bounds, first_row, rows, extra):
    clips = len(bounds)
    place = lax.broadcasted_iota(jnp.int32, (HD, 1), 0)
    opening, ending = clip_borders(bounds, place)
    row = first_row + lax.broadcasted_iota(jnp.int32, (1, rows.shape[1]), 1)
    inside = (place < clips) & (row >= opening) & (row < ending)
    tail = jnp.where(inside, 1.0, 0.0)
    if extra is not None:
        tail = tail + in_three(place - clips, -extra)
    return jnp.concatenate([rows * (SCORE_SCALE * LOG2E), tail], 0).astype(low)


def pack(rows):
    half = rows.shape[0] // 2
    return jnp.concatenate([rows[:half], rows[half:]], 1)


def unpack(packed):
    return jnp.concatenate([packed[:, :HD], packed[:, HD:]], 0)


def unpack_t(packed):
    turned = packed.astype(jnp.float32).T
    return jnp.concatenate([turned[:HD], turned[HD:]], 1)


def pack_t(columns):
    half = columns.shape[1] // 2
    return jnp.concatenate([columns[:, :half], columns[:, half:]], 0).T


class Team:
    def __init__(self, dims):
        z, y, x, cores = dims
        self.dims = dims
        self.wide = HEADS // (x * cores) == y
        self.size = x * cores * (y if self.wide else 1)
        self.groups = z if self.wide else z * y
        axes = (1, 2, 3) if self.wide else (2, 3)
        offsets = [o for o in all_offsets(dims, axes) if any(o)]
        self.others = sorted(offsets, key=lambda o: (o[1] + o[2], o))
        self.sides = [] if self.wide else axis_peers(dims, (1,))

    def slot(self, place):
        head = head_of(self.dims, place)
        return place[1] * self.dims[2] * self.dims[3] + head if self.wide else head

    def group(self, place):
        return place[0] if self.wide else blk_of(self.dims, place)


def heads_of(n_head, slots):
    return [(s % n_head, s // n_head) for s in range(slots)]


class Pushes:
    def __init__(self, dims, me, send_sem, recv_sem):
        self.dims, self.me, self.send_sem, self.recv_sem = dims, me, send_sem, recv_sem
        self.started = []

    def __call__(self, src, dst, offset):
        i = len(self.started)
        place = shifted(self.dims, self.me, offset, 1)
        copy = remote(src, dst, self.send_sem.at[i], self.recv_sem.at[i], place, self.dims)
        copy.start()
        self.started.append(copy)
        return copy

    def finish(self):
        for copy in self.started:
            copy.wait_send()


def peers_across(dims):
    z, y, x, cores = dims
    across = [(0, 0, a, c) for a in range(x) for c in range(cores) if (a, c) != (0, 0)]
    return sorted(across, key=lambda o: (o[2] == 0, o[3]))


def attend_kernel(
    team,
    query_step,
    key_step,
    pieces,
    lengths,
    q_in,
    kv_in,
    o_out,
    lse,
    out_t,
    q_all,
    kv_all,
    keys,
    values_t,
    queries,
    top,
    accum,
    even_scores,
    odd_scores,
    even_top,
    odd_top,
    o_mine,
    send_sem,
    recv_sem,
    own_sem,
):
    dims = team.dims
    z = dims[0]
    me = my_place(dims)
    bounds = clip_bounds(lengths)
    rows = kv_in.shape[1]
    amount = team.size * rows
    slots = team.size // pieces
    my_group, my_slot = team.group(me), team.slot(me)
    ring_ends = sorted({along(0, 1 % z), along(0, (z - 1) % z)} - {(0, 0, 0, 0)})
    greet(dims, me, team.others + ring_ends + team.sides)
    push = Pushes(dims, me, send_sem, recv_sem)
    own_kv = pltpu.make_async_copy(kv_in.at[my_slot], kv_all.at[my_group, my_slot], own_sem.at[0])
    own_q = pltpu.make_async_copy(q_in.at[my_slot], q_all.at[my_slot], own_sem.at[1])
    own_kv.start()
    own_q.start()

    def to_team(src, dst, o):
        return push(src.at[team.slot(shifted(dims, me, o, 1))], dst, o)

    kv_copies = {o: to_team(kv_in, kv_all.at[my_group, my_slot], o) for o in team.others}
    q_copies = [to_team(q_in, q_all.at[my_slot], o) for o in team.others]
    ring, side = {}, {}

    def group_at(offset):
        return team.group(shifted(dims, me, offset, -1))

    def send_on(s, piece):
        block = kv_all.at[group_at(along(0, s)), pl.ds(piece * slots, slots)]
        if s < z - 1:
            ring[(s + 1, piece)] = push(block, block, along(0, 1))
        for o in team.sides:
            side[(s, o, piece)] = push(block, block, o)

    def compute(offset, piece):
        group = group_at(offset)

        @pl.loop(0, slots)
        def build(n):
            at = pl.ds(pl.multiple_of(n * rows, rows), rows)
            slot = piece * slots + n
            block = kv_all[group, slot]
            keys[at, :] = with_key_tail(bounds, group * amount + slot * rows, block)
            values_t[:HD, at] = block.astype(jnp.float32).T[HD:].astype(low)

        def both(now, now_scores, now_top, later, later_scores, later_top):
            if now is not None:
                at = tile(now)
                old = top[:, at]
                new = jnp.maximum(old, jnp.max(now_top[...], 0, keepdims=True))
                top[:, at] = new
                total = accum[:, at] * jnp.exp2(old - new)
            query = queries[:, tile(later)]
            highest = jnp.full(later_top.shape, -1e38, jnp.float32)
            for k in range(0, slots * rows, key_step):
                scores = product(keys[k : k + key_step, :], query)
                later_scores[k : k + key_step, :] = scores
                highest = jnp.maximum(
                    highest, jnp.max(scores.reshape(key_step // 8, 8, query_step), 0)
                )
                if now is not None:
                    probs = jnp.exp2((now_scores[k : k + key_step, :] - new).astype(low))
                    total = total + product(values_t[:, k : k + key_step], probs)
            later_top[...] = highest
            if now is not None:
                accum[:, at] = total

        def tile(n):
            return pl.ds(pl.multiple_of(n * query_step, query_step), query_step)

        tiles = amount // query_step
        both(None, None, None, 0, even_scores, even_top)

        @pl.loop(0, tiles // 2)
        def query_blocks(n):
            last = jnp.minimum(2 * n + 2, tiles - 1)
            both(2 * n, even_scores, even_top, 2 * n + 1, odd_scores, odd_top)
            both(2 * n + 1, odd_scores, odd_top, last, even_scores, even_top)

    values_t[HD:, :] = jnp.ones((TILE, slots * rows), low)
    top[...] = jnp.full(top.shape, -1e38, jnp.float32)
    accum[...] = jnp.zeros(accum.shape, jnp.float32)
    own_kv.wait()
    for o in team.others:
        kv_copies[o].wait_recv()
    for piece in range(pieces):
        send_on(0, piece)
    own_q.wait()
    for copy in q_copies:
        copy.wait_recv()
    for n in range(team.size):
        queries[:, n * rows : (n + 1) * rows] = with_query_tail(
            bounds, my_group * amount + n * rows, unpack_t(q_all[n]), None
        )
    for s in range(z):
        for piece in range(pieces):
            compute(along(0, s), piece)
            if s < z - 1:
                ring[(s + 1, piece)].wait_recv()
                send_on(s + 1, piece)
            for o in team.sides:
                side[(s, o, piece)].wait_recv()
                compute((s, o[1], 0, 0), piece)
    total = accum[HD : HD + 1, :]
    out_t[...] = accum[:HD, :] / total
    lse[...] = top[...] + jnp.log(total) * LOG2E
    for n in range(team.size):
        o_mine[n] = pack_t(out_t[:, n * rows : (n + 1) * rows]).astype(low)
    o_copies = [to_team(o_mine, o_out.at[my_slot], o) for o in team.others]
    own_o = pltpu.make_async_copy(o_mine.at[my_slot], o_out.at[my_slot], own_sem.at[2])
    own_o.start()
    own_o.wait()
    for copy in o_copies:
        copy.wait_recv()
    push.finish()


def attend(dims, lengths, q, kv, collective_id):
    team = Team(dims)
    z = dims[0]
    amount = team.size * kv.shape[1]
    pieces, query_step = 2, 256
    count = 3 * (team.size - 1) + pieces * (z + z * len(team.sides))
    return pl.pallas_call(
        functools.partial(attend_kernel, team, query_step, 256, pieces),
        out_shape=(
            jax.ShapeDtypeStruct(q.shape, low),
            jax.ShapeDtypeStruct((1, amount), jnp.float32),
            jax.ShapeDtypeStruct((HD, amount), jnp.float32),
            jax.ShapeDtypeStruct(q.shape, low),
            jax.ShapeDtypeStruct((team.groups,) + kv.shape, low),
        ),
        in_specs=[SMEM_SPEC, VMEM_SPEC, VMEM_SPEC],
        out_specs=[VMEM_SPEC] * 5,
        scratch_shapes=[
            pltpu.VMEM((amount // pieces, LANES), low),
            pltpu.VMEM((HD + TILE, amount // pieces), low),
            pltpu.VMEM((LANES, amount), low),
            pltpu.VMEM((1, amount), jnp.float32),
            pltpu.VMEM((HD + TILE, amount), jnp.float32),
            pltpu.VMEM((amount // pieces, query_step), jnp.float32),
            pltpu.VMEM((amount // pieces, query_step), jnp.float32),
            pltpu.VMEM((8, query_step), jnp.float32),
            pltpu.VMEM((8, query_step), jnp.float32),
            pltpu.VMEM(q.shape, low),
            pltpu.SemaphoreType.DMA((count,)),
            pltpu.SemaphoreType.DMA((count,)),
            pltpu.SemaphoreType.DMA((3,)),
        ],
        compiler_params=pltpu.CompilerParams(
            collective_id=collective_id, has_side_effects=True, vmem_limit_bytes=56 * MIB
        ),
        name="attend",
    )(lengths, q, kv)


def attend_back_kernel(
    team,
    key_step,
    query_step,
    pieces,
    lengths,
    q_all,
    kv_all,
    do_in,
    out_t,
    lse,
    d_q_out,
    d_kv_out,
    do_all,
    keys,
    keys_t,
    values,
    queries,
    douts,
    d_q_t,
    q_rows,
    do_rows,
    even_probs,
    odd_probs,
    even_scores,
    odd_scores,
    side_out,
    side_in,
    ring_out,
    ring_in,
    mine,
    d_q_mine,
    d_kv_mine,
    send_sem,
    recv_sem,
    own_sem,
):
    dims = team.dims
    z = dims[0]
    me = my_place(dims)
    bounds = clip_bounds(lengths)
    rows = kv_all.shape[2]
    amount = team.size * rows
    slots = team.size // pieces
    piece_rows = slots * rows
    my_group, my_slot = team.group(me), team.slot(me)
    ring_ends = sorted({along(0, 1 % z), along(0, (z - 1) % z)} - {(0, 0, 0, 0)})
    greet(dims, me, team.others + ring_ends + team.sides)
    push = Pushes(dims, me, send_sem, recv_sem)

    def to_team(src, dst, o):
        return push(src.at[team.slot(shifted(dims, me, o, 1))], dst, o)

    do_copies = [to_team(do_in, do_all.at[my_slot], o) for o in team.others]
    own_do = pltpu.make_async_copy(do_in.at[my_slot], do_all.at[my_slot], own_sem.at[0])
    own_do.start()
    place = lax.broadcasted_iota(jnp.int32, (HD, 1), 0)
    for n in range(team.size):
        at = slice(n * rows, (n + 1) * rows)
        q_t = unpack_t(q_all[n])
        queries[:, at] = with_query_tail(bounds, my_group * amount + n * rows, q_t, lse[:, at])
        q_rows[at, :] = jnp.concatenate([q_t * SCORE_SCALE, jnp.zeros_like(q_t)], 0).T.astype(low)
    d_q_t[...] = jnp.zeros(d_q_t.shape, jnp.float32)
    own_do.wait()
    for copy in do_copies:
        copy.wait_recv()
    for n in range(team.size):
        at = slice(n * rows, (n + 1) * rows)
        do_t = unpack_t(do_all[n])
        delta = jnp.sum(do_t * out_t[:, at], 0, keepdims=True)
        douts[:, at] = jnp.concatenate([in_three(place, -delta), do_t], 0).astype(low)
        do_rows[at, :] = jnp.concatenate([jnp.zeros_like(do_t), do_t], 0).T.astype(low)

    def compute(offset, piece, target):
        group = team.group(shifted(dims, me, offset, 1))

        @pl.loop(0, slots)
        def build(n):
            at = pl.ds(pl.multiple_of(n * rows, rows), rows)
            slot = piece * slots + n
            block = kv_all[group, slot]
            keys[at, :] = with_key_tail(bounds, group * amount + slot * rows, block)
            keys_t[:, at] = block.astype(jnp.float32).T[:HD].astype(low)
            values[at, :] = with_value_tail(block)

        def both(now, now_probs, now_scores, later, later_probs, later_scores):
            at = rows_of(later)
            if now is not None:
                now_at = rows_of(now)
                total = jnp.zeros((key_step, LANES), jnp.float32)
            for first in range(0, amount, query_step):
                part = slice(first, first + query_step)
                probs = jnp.exp2(product(keys[at, :], queries[:, part]).astype(low))
                d_probs = product(values[at, :], douts[:, part])
                later_probs[:, part] = probs
                later_scores[:, part] = (probs.astype(jnp.float32) * d_probs).astype(low)
                if now is not None:
                    d_scores = now_scores[:, part]
                    total = total + product(now_probs[:, part], do_rows[part, :])
                    total = total + product(d_scores, q_rows[part, :])
                    d_q_t[:, part] = d_q_t[:, part] + product(keys_t[:, now_at], d_scores)
            if now is not None:
                target[now_at, :] = total.astype(target.dtype)

        def rows_of(k):
            return pl.ds(pl.multiple_of(k * key_step, key_step), key_step)

        steps = piece_rows // key_step
        both(None, None, None, 0, even_probs, even_scores)

        @pl.loop(0, steps // 2)
        def key_blocks(k):
            last = jnp.minimum(2 * k + 2, steps - 1)
            both(2 * k, even_probs, even_scores, 2 * k + 1, odd_probs, odd_scores)
            both(2 * k + 1, odd_probs, odd_scores, last, even_probs, even_scores)

    side, ring = {}, {}

    def send_sides(s, piece):
        for o in team.sides:
            target = side_out.at[s - 1, o[1] - 1, piece]
            compute((z - s, o[1], 0, 0), piece, target)
            side[(s, o, piece)] = push(target, side_in.at[s - 1, o[1] - 1, piece], o)

    def combine(s, piece):
        for o in team.sides:
            side[(s, o, piece)].wait_recv()
        if s > 1:
            ring[(s - 1, piece)].wait_recv()
        for n in range(slots):
            at = slice(n * rows, (n + 1) * rows)
            total = mine[piece, at, :]
            for o in team.sides:
                total = total + side_in[s - 1, o[1] - 1, piece, at, :].astype(jnp.float32)
            if s > 1:
                total = total + ring_in[s - 2, piece, at, :].astype(jnp.float32)
            if s < z:
                ring_out[s - 1, piece, at, :] = total.astype(low)
            else:
                d_kv_mine[piece * slots + n] = total.astype(low)
        if s < z:
            ring[(s, piece)] = push(ring_out.at[s - 1, piece], ring_in.at[s - 1, piece], along(0, 1))

    for s in range(1, z + 1):
        for piece in range(pieces):
            send_sides(s, piece)
            compute((z - s if s < z else 0, 0, 0, 0), piece, mine.at[piece])
            if team.sides or s < z:
                combine(s, piece)
    for n in range(team.size):
        at = slice(n * rows, (n + 1) * rows)
        d_q_mine[n] = pack_t(d_q_t[:, at] * SCORE_SCALE).astype(low)
    copies = [to_team(d_q_mine, d_q_out.at[my_slot], o) for o in team.others]
    own_q = pltpu.make_async_copy(d_q_mine.at[my_slot], d_q_out.at[my_slot], own_sem.at[1])
    own_q.start()
    if not team.sides:
        for piece in range(pieces):
            combine(z, piece)
    copies += [to_team(d_kv_mine, d_kv_out.at[my_slot], o) for o in team.others]
    own_kv = pltpu.make_async_copy(d_kv_mine.at[my_slot], d_kv_out.at[my_slot], own_sem.at[2])
    own_kv.start()
    own_q.wait()
    own_kv.wait()
    for copy in copies:
        copy.wait_recv()
    push.finish()


def attend_back(dims, lengths, q, kv, dout, out_t, lse, collective_id):
    team = Team(dims)
    z = dims[0]
    rows = kv.shape[2]
    amount = team.size * rows
    pieces, key_step = 2, 256
    piece = (pieces, amount // pieces, LANES)
    count = 3 * (team.size - 1) + pieces * (z + z * len(team.sides))
    others = max(len(team.sides), 1)
    ring_steps, side_steps = max(z - 1, 1), z if team.sides else 1
    return pl.pallas_call(
        functools.partial(attend_back_kernel, team, key_step, 512, pieces),
        out_shape=(
            jax.ShapeDtypeStruct(q.shape, low),
            jax.ShapeDtypeStruct(kv.shape[1:], low),
        ),
        in_specs=[SMEM_SPEC] + [VMEM_SPEC] * 5,
        out_specs=[VMEM_SPEC] * 2,
        scratch_shapes=[
            pltpu.VMEM(q.shape, low),
            pltpu.VMEM((amount // pieces, LANES), low),
            pltpu.VMEM((HD, amount // pieces), low),
            pltpu.VMEM((amount // pieces, LANES), low),
            pltpu.VMEM((LANES, amount), low),
            pltpu.VMEM((LANES, amount), low),
            pltpu.VMEM((HD, amount), jnp.float32),
            pltpu.VMEM((amount, LANES), low),
            pltpu.VMEM((amount, LANES), low),
            pltpu.VMEM((key_step, amount), low),
            pltpu.VMEM((key_step, amount), low),
            pltpu.VMEM((key_step, amount), low),
            pltpu.VMEM((key_step, amount), low),
            pltpu.VMEM((side_steps, others) + piece, low),
            pltpu.VMEM((side_steps, others) + piece, low),
            pltpu.VMEM((ring_steps,) + piece, low),
            pltpu.VMEM((ring_steps,) + piece, low),
            pltpu.VMEM(piece, jnp.float32),
            pltpu.VMEM(q.shape, low),
            pltpu.VMEM(kv.shape[1:], low),
            pltpu.SemaphoreType.DMA((count,)),
            pltpu.SemaphoreType.DMA((count,)),
            pltpu.SemaphoreType.DMA((3,)),
        ],
        compiler_params=pltpu.CompilerParams(
            collective_id=collective_id, has_side_effects=True, vmem_limit_bytes=60 * MIB
        ),
        name="attend_back",
    )(lengths, q, kv, dout, out_t, lse)


def part_shapes(n_head):
    width = HEADS // n_head * HD
    hidden = FF // n_head
    return (
        (D, width, True),
        (DI, 2 * width, True),
        (width, D, False),
        (D, 3 * width, True),
        (width, D, False),
        (D, hidden, True),
        (hidden, D, False),
        (D, C // n_head, True),
    )


def borders(n_head):
    result = [0]
    for rows, columns, joined in part_shapes(n_head):
        result.append(result[-1] + rows * columns // LANES)
    return result


def period(columns):
    amount = 1
    while amount * columns % LANES:
        amount *= 2
    return amount


def segments(start, amount, unit):
    result = []
    while amount > 0:
        which, at = divmod(start, unit)
        size = min(unit - at, amount)
        result.append((which, at, at + size))
        start, amount = start + size, amount - size
    return result


def joined_lanes(pieces):
    return pieces[0] if len(pieces) == 1 else jnp.concatenate(pieces, 1)


def lane_blocks(value):
    rows, columns = value.shape
    missing = -columns % LANES
    if missing:
        value = jnp.concatenate([value, jnp.zeros((rows, missing), value.dtype)], 1)
    return [value[:, i : i + LANES] for i in range(0, columns + missing, LANES)]


def every(first, amount, stride):
    return pl.ds(first, amount) if stride == 1 else pl.ds(first, amount, stride=stride)


def matrix_of(stage, first, rows, columns, line):
    if columns % LANES == 0:
        stride = columns // LANES
        for j in range(stride):
            yield j * LANES, stage[every(first + j, rows, stride), :]
        return
    height = period(columns)
    stride = height * columns // LANES
    for k in range(height):
        pieces = [
            stage[every(first + which, rows // height, stride), :][:, begin:end]
            for which, begin, end in segments(k * columns, columns, LANES)
        ]
        for i, piece in enumerate(lane_blocks(joined_lanes(pieces))):
            line[i, every(k, rows // height, height), :] = piece
    for i in range(-(-columns // LANES)):
        yield i * LANES, line[i, :rows, : min(columns - i * LANES, LANES)]


def matrix_into(stage, first, value, line):
    rows, columns = value.shape
    if columns % LANES == 0:
        stride = columns // LANES
        for j in range(stride):
            stage[every(first + j, rows, stride), :] = value[:, j * LANES : (j + 1) * LANES]
        return
    height = period(columns)
    stride = height * columns // LANES
    for i, piece in enumerate(lane_blocks(value)):
        line[i, :rows, :] = piece
    for i in range(stride):
        pieces = [
            line[which, every(k, rows // height, height), :][:, begin:end]
            for k, first_lane, last_lane in segments(i * LANES, LANES, columns)
            for which, begin, end in segments(first_lane, last_lane - first_lane, LANES)
        ]
        stage[every(first + i, rows // height, stride), :] = joined_lanes(pieces)


def load_stage(stage, held, first_shard, shard_rows, group):
    for b in range(held.shape[0]):
        stage[pl.ds(b * shard_rows, shard_rows), :] = held[b, group, :shard_rows, :].astype(jnp.float32)


def load_common(stage, held, valid):
    piece = held.shape[2]
    for b in range(held.shape[0]):
        for k in range(held.shape[1]):
            amount = min(piece, valid - k * piece)
            stage[b * valid + k * piece : b * valid + k * piece + amount, :] = held[b, k].astype(
                jnp.float32
            )[:amount]


def common_blocks(first_row, last_row, valid):
    return first_row // valid, -(-last_row // valid) - first_row // valid


def load_matrices(stage, first_row, n_head, group, which, targets, line):
    starts, shapes = borders(n_head), part_shapes(n_head)
    for m, target in zip(which, targets):
        rows, columns, joined = shapes[m]
        row = 0 if joined else group * rows
        column = group * columns if joined else 0
        for j, value in matrix_of(stage, starts[m] - first_row, rows, columns, line):
            size = value.shape[1]
            target[row : row + rows, column + j : column + j + size] = value.astype(target.dtype)


def normalized(x):
    centre = x - jnp.mean(x, -1, keepdims=True)
    rate = lax.rsqrt(jnp.mean(centre * centre, -1, keepdims=True) + norm_eps)
    return centre * rate, rate


def layer_norm(x, gain):
    return normalized(x)[0] * gain


def norm_pullback(x, gain, grad):
    unit, rate = normalized(x)
    inside = grad * gain
    both = jnp.mean(inside * unit, -1, keepdims=True)
    d_x = rate * (inside - jnp.mean(inside, -1, keepdims=True) - unit * both)
    return d_x, jnp.sum(grad * unit, 0, keepdims=True)


def head_lanes(group, heads, value):
    width = heads * HD
    block = value[:, group * width : (group + 1) * width]
    lane = lax.broadcasted_iota(jnp.int32, (1, width), 1)
    result = []
    for a in range(heads):
        here = (lane >= a * HD) & (lane < (a + 1) * HD)
        result.append((here, jnp.where(here, block, jnp.zeros_like(block))))
    return result


def place_of(bounds, first, amount):
    row = first + lax.broadcasted_iota(jnp.int32, (amount, 1), 0)
    opening = jnp.zeros((amount, 1), jnp.int32)
    for begin, end in bounds:
        opening = jnp.where((row >= begin) & (row < end), begin, opening)
    offset = row - opening
    turns = jnp.floor((offset.astype(jnp.float32) + 0.5) * (1.0 / LAT)).astype(jnp.int32)
    return offset - turns * LAT


def picked_rows(bounds, rows, n_head):
    first = lax.axis_index("blk") * (rows * n_head) + lax.axis_index("head") * rows
    lane = lax.broadcasted_iota(jnp.int32, (rows, LAT), 1)
    return jnp.where(lane == place_of(bounds, first, rows), 1.0, 0.0).astype(low)


def enc_scores(q_head, keys):
    return against(q_head, keys) * (SCORE_SCALE * LOG2E)


def encode_kernel(
    n_head,
    shard_rows,
    valid,
    rows,
    lengths,
    weights,
    common,
    inputs_t,
    enc_query,
    enc_keyval,
    enc_output,
    self_project,
    gains,
    z_zero,
    h_zero,
    x_norm_t,
    q_enc,
    kv_enc,
    o_enc,
    z_one,
    h_one,
    q_self,
    kv_self,
    counts,
    label_counts,
    held,
    held_common,
    held_counts,
    stage,
    stage_common,
    line,
    latent_table,
    sems,
):
    heads = HEADS // n_head
    width = heads * HD
    shards = held.shape[0]
    bounds = clip_bounds(lengths)
    first = DQ * D // LANES
    block, blocks = common_blocks(first, first + (LAT + 4) * D // LANES, valid)
    tail = shard_rows // TILE * TILE
    copies = [
        pltpu.make_async_copy(common.at[pl.ds(block, blocks)], held_common, sems.at[0]),
        pltpu.make_async_copy(weights.at[pl.ds(0, shards)], held, sems.at[1]),
        pltpu.make_async_copy(weights.at[:, :, pl.ds(tail, TILE)], held_counts, sems.at[2]),
    ]
    for copy in copies:
        copy.start()
    centre = inputs_t[...].astype(jnp.float32)
    centre = centre - jnp.mean(centre, 0, keepdims=True)
    rate = lax.rsqrt(jnp.mean(centre * centre, 0, keepdims=True) + norm_eps)
    x_norm_t[...] = (centre * rate).astype(low)
    copies[0].wait()
    load_common(stage_common, held_common, valid)
    first = first - block * valid
    for j, value in matrix_of(stage_common, first, LAT, D, line):
        latent_table[:, j : j + LANES] = value.astype(low)
    for j, value in matrix_of(stage_common, first + LAT * D // LANES, 4, D, line):
        gains[:, j : j + LANES] = value
    picked = picked_rows(bounds, rows, n_head)
    z_zero[...] = product(picked, latent_table[...])
    h_zero[...] = layer_norm(z_zero[...], gains[0:1, :]).astype(low)
    copies[2].wait()
    counted = held_counts[...].astype(jnp.float32)[:, :, shard_rows - tail : shard_rows - tail + 1]
    counts[...] = jnp.broadcast_to(jnp.sum(counted, (0, 1)), counts.shape)
    label_counts[...] = counts[:1, :MODES]
    copies[1].wait()
    for g in range(n_head):
        load_stage(stage, held, 0, shard_rows, g)
        load_matrices(
            stage, 0, n_head, g, (0, 1, 2, 3), (enc_query, enc_keyval, enc_output, self_project), line
        )
    q_enc[...] = product(h_zero[...], enc_query[...]).astype(low)
    kv_enc[...] = contract_first(x_norm_t[...], enc_keyval[...]).astype(low)
    for g in range(n_head):
        keys = kv_enc[:, 2 * g * width : (2 * g + 1) * width]
        values = kv_enc[:, (2 * g + 1) * width : (2 * g + 2) * width]
        outcome = jnp.zeros((rows, width), jnp.float32)
        for here, q_head in head_lanes(g, heads, q_enc[...]):
            scores = enc_scores(q_head, keys)
            probs = jnp.exp2((scores - jnp.max(scores, 1, keepdims=True)).astype(low))
            total = jnp.sum(probs.astype(jnp.float32), 1, keepdims=True)
            outcome = jnp.where(here, product(probs, values) / total, outcome)
        o_enc[:, g * width : (g + 1) * width] = outcome.astype(low)
    z_one[...] = z_zero[...] + product(o_enc[...], enc_output[...])
    h_one[...] = layer_norm(z_one[...], gains[1:2, :]).astype(low)
    projected = product(h_one[...], self_project[...]).astype(low)
    for slot, (g, a) in enumerate(heads_of(n_head, q_self.shape[0])):
        query, key, value = (
            projected[:, (3 * g + i) * width + a * HD : (3 * g + i) * width + (a + 1) * HD]
            for i in range(3)
        )
        q_self[slot] = pack(query)
        kv_self[slot] = jnp.concatenate([key, value], 1)


LINE = pltpu.VMEM((4, round_up(max(D, DI), 8), LANES), jnp.float32)


def shards_of(n_head, shard_rows, first, last):
    starts = borders(n_head)
    begin = starts[first] // shard_rows
    return begin, -(-starts[last] // shard_rows) - begin


def encode(lengths, weights, common, inputs_t, valid, rows, slots, n_head, shard_rows):
    begin, shards = shards_of(n_head, shard_rows, 0, 4)
    query_rows = DQ * D // LANES
    block, blocks = common_blocks(query_rows, query_rows + (LAT + 4) * D // LANES, valid)
    keys = inputs_t.shape[1]
    return pl.pallas_call(
        functools.partial(encode_kernel, n_head, shard_rows, valid, rows),
        out_shape=[
            shape_of((D, D)),
            shape_of((DI, 2 * D)),
            shape_of((D, D)),
            shape_of((D, 3 * D)),
            shape_of((4, D), jnp.float32),
            shape_of((rows, D), jnp.float32),
            shape_of((rows, D)),
            shape_of(inputs_t.shape),
            shape_of((rows, D)),
            shape_of((keys, 2 * D)),
            shape_of((rows, D)),
            shape_of((rows, D), jnp.float32),
            shape_of((rows, D)),
            shape_of((slots, rows // 2, LANES)),
            shape_of((slots, rows, LANES)),
            shape_of((8, LANES), jnp.float32),
            shape_of((1, MODES), jnp.float32),
        ],
        in_specs=[SMEM_SPEC, ANY_SPEC, ANY_SPEC, VMEM_SPEC],
        out_specs=[VMEM_SPEC] * 17,
        scratch_shapes=[
            pltpu.VMEM((shards,) + weights.shape[1:], low),
            pltpu.VMEM((blocks,) + common.shape[1:], low),
            pltpu.VMEM(weights.shape[:2] + (TILE, LANES), low),
            pltpu.VMEM((shards * shard_rows, LANES), jnp.float32),
            pltpu.VMEM((blocks * valid, LANES), jnp.float32),
            LINE,
            pltpu.VMEM((LAT, D), low),
            pltpu.SemaphoreType.DMA((3,)),
        ],
        compiler_params=pltpu.CompilerParams(vmem_limit_bytes=56 * MIB),
        name="encode",
    )(lengths, weights, common, inputs_t)


def gelu_and_slope(x):
    rate = (2.0 / jnp.pi) ** 0.5
    cubic = 0.044715
    t = jnp.tanh(rate * (x + cubic * x * x * x))
    slope = 0.5 * (1.0 + t) + 0.5 * x * (1.0 - t * t) * rate * (1.0 + 3.0 * cubic * x * x)
    return 0.5 * x * (1.0 + t), slope


def my_column(marks, rows):
    turned = marks[...].astype(jnp.float32).T
    column = lax.broadcasted_iota(jnp.int32, turned.shape, 1)
    per_head = rows // LANES
    first = lax.axis_index("head") * per_head
    picked = [
        jnp.sum(jnp.where(column == first + k, turned, 0.0), 1, keepdims=True)
        for k in range(per_head)
    ]
    return jnp.concatenate(picked, 0) if per_head > 1 else picked[0]


def middle_kernel(
    n_head,
    shard_rows,
    valid,
    first_shard,
    rows,
    counts,
    weights,
    common,
    z_one,
    o_self,
    out_queries_t,
    labels,
    modality,
    labeled,
    gains,
    dout,
    d_two_out,
    tile,
    query_grad,
    gain_grads,
    grads,
    held,
    held_common,
    stage,
    stage_common,
    line,
    self_output,
    hidden_in,
    hidden_out,
    class_table,
    query_table,
    slope,
    activ,
    sems,
):
    heads = HEADS // n_head
    width, hidden, classes = heads * HD, FF // n_head, C // n_head
    shards = held.shape[0]
    first_row = first_shard * shard_rows
    starts = borders(n_head)
    copies = [
        pltpu.make_async_copy(common.at[pl.ds(0, held_common.shape[0])], held_common, sems.at[0]),
        pltpu.make_async_copy(weights.at[pl.ds(first_shard, shards)], held, sems.at[1]),
    ]
    for copy in copies:
        copy.start()
    copies[0].wait()
    load_common(stage_common, held_common, valid)
    for j, value in matrix_of(stage_common, 0, DQ, D, line):
        query_table[:, j : j + LANES] = value.astype(low)
    copies[1].wait()
    for g in range(n_head):
        load_stage(stage, held, first_shard, shard_rows, g)
        load_matrices(
            stage, first_row, n_head, g, (4, 5, 6, 7), (self_output, hidden_in, hidden_out, class_table), line
        )
    gain_two, gain_three = gains[2:3, :], gains[3:4, :]
    o_heads = {head: unpack(o_self[s]) for s, head in enumerate(heads_of(n_head, o_self.shape[0]))}
    o_groups = [joined_lanes([o_heads[(g, a)] for a in range(heads)]) for g in range(n_head)]
    o_low = jnp.concatenate(o_groups, 1)
    z_two = z_one[...] + product(o_low, self_output[...])
    h_two = layer_norm(z_two, gain_two).astype(low)
    value, bend = gelu_and_slope(product(h_two, hidden_in[...]))
    activ[...] = value.astype(low)
    slope[...] = bend
    z_three = z_two + product(activ[...], hidden_out[...])
    queries_t = out_queries_t[...]
    decoded = layer_norm(z_three, gain_three) + contract_first(queries_t, query_table[...])
    decoded = decoded.astype(low)
    logits = product(decoded, class_table[...])
    label, kind, counted = (my_column(marks, rows) for marks in (labels, modality, labeled))
    lane = lax.broadcasted_iota(jnp.int32, (rows, C), 1).astype(jnp.float32)
    is_target = jnp.where(lane == label, 1.0, 0.0)
    row_top = jnp.max(logits, 1, keepdims=True)
    row_lse = row_top + jnp.log(jnp.sum(jnp.exp2((logits - row_top) * LOG2E), 1, keepdims=True))
    loss = row_lse - jnp.sum(is_target * logits, 1, keepdims=True)
    weight = jnp.zeros((rows, 1), jnp.float32)
    place = lax.broadcasted_iota(jnp.int32, (1, LANES), 1)
    losses = jnp.zeros((1, LANES), jnp.float32)
    for m in range(MODES):
        member = jnp.where((kind == m) & (counted == 1.0), 1.0, 0.0)
        weight = weight + member / jnp.maximum(counts[0:1, m : m + 1], 1.0)
        losses = losses + jnp.where(place == m, jnp.sum(loss * member, 0, keepdims=True), 0.0)
    tile[...] = jnp.broadcast_to(losses, tile.shape)
    dlogits = (weight * (jnp.exp2((logits - row_lse) * LOG2E) - is_target)).astype(low)
    d_decoded = against(dlogits, class_table[...])
    matrix_into(query_grad, 0, product(queries_t, d_decoded.astype(low)), line)
    d_three, gain_three_grad = norm_pullback(z_three, gain_three, d_decoded)
    d_branch = d_three.astype(low)
    d_pre = (slope[...] * against(d_branch, hidden_out[...])).astype(low)
    d_middle, gain_two_grad = norm_pullback(z_two, gain_two, against(d_pre, hidden_in[...]))
    d_two = d_three + d_middle
    d_two_out[...] = d_two
    gain_grads[...] = jnp.concatenate([gain_two_grad, gain_three_grad], 0)
    d_two_low = d_two.astype(low)
    d_o = against(d_two_low, self_output[...]).astype(low)
    for slot, (g, a) in enumerate(heads_of(n_head, o_self.shape[0])):
        dout[slot] = pack(d_o[:, g * width + a * HD : g * width + (a + 1) * HD])
    for g in range(n_head):
        results = (
            contract_first(o_groups[g], d_two_low),
            contract_first(h_two, d_pre[:, g * hidden : (g + 1) * hidden]),
            contract_first(activ[:, g * hidden : (g + 1) * hidden], d_branch),
            contract_first(decoded, dlogits[:, g * classes : (g + 1) * classes]),
        )
        for m, result in zip((4, 5, 6, 7), results):
            matrix_into(stage, starts[m] - first_row, result, line)
        for b in range(shards):
            held[b, g, :shard_rows, :] = stage[pl.ds(b * shard_rows, shard_rows), :].astype(low)
    back = pltpu.make_async_copy(held, grads.at[pl.ds(first_shard, shards)], sems.at[2])
    back.start()
    back.wait()


def middle(counts, weights, common, z_one, o_self, out_queries_t, marks, gains, valid, n_head, shard_rows):
    rows = z_one.shape[0]
    begin, shards = shards_of(n_head, shard_rows, 4, 8)
    query_rows = DQ * D // LANES
    block, blocks = common_blocks(0, query_rows, valid)
    return pl.pallas_call(
        functools.partial(middle_kernel, n_head, shard_rows, valid, begin, rows),
        grid=(1,),
        out_shape=[
            shape_of(o_self.shape),
            shape_of((rows, D), jnp.float32),
            shape_of((8, LANES), jnp.float32),
            shape_of((query_rows, LANES), jnp.float32),
            shape_of((2, D), jnp.float32),
            shape_of(weights.shape),
        ],
        in_specs=[
            VMEM_SPEC,
            ANY_SPEC,
            ANY_SPEC,
            VMEM_SPEC,
            VMEM_SPEC,
            pl.BlockSpec((DQ, rows), lambda i: (0, lax.axis_index("head"))),
            VMEM_SPEC,
            VMEM_SPEC,
            VMEM_SPEC,
            VMEM_SPEC,
        ],
        out_specs=[VMEM_SPEC] * 5 + [ANY_SPEC],
        scratch_shapes=[
            pltpu.VMEM((shards,) + weights.shape[1:], low),
            pltpu.VMEM((blocks,) + common.shape[1:], low),
            pltpu.VMEM((shards * shard_rows, LANES), jnp.float32),
            pltpu.VMEM((blocks * valid, LANES), jnp.float32),
            LINE,
            pltpu.VMEM((D, D), low),
            pltpu.VMEM((D, FF), low),
            pltpu.VMEM((FF, D), low),
            pltpu.VMEM((D, C), low),
            pltpu.VMEM((DQ, D), low),
            pltpu.VMEM((rows, FF), jnp.float32),
            pltpu.VMEM((rows, FF), low),
            pltpu.SemaphoreType.DMA((3,)),
        ],
        compiler_params=pltpu.CompilerParams(vmem_limit_bytes=56 * MIB),
        name="middle",
    )(counts, weights, common, z_one, o_self, out_queries_t, *marks, gains)


def ending_kernel(
    n_head,
    shard_rows,
    valid,
    rows,
    lengths,
    grads_in,
    d_q_self,
    d_kv_self,
    d_two,
    gains,
    gain_grads,
    query_grad,
    enc_query,
    enc_keyval,
    enc_output,
    self_project,
    z_zero,
    h_zero,
    x_norm_t,
    q_enc,
    kv_enc,
    o_enc,
    z_one,
    h_one,
    grads,
    common_grad,
    held,
    stage,
    stage_common,
    line,
    d_q,
    d_kv,
    sems,
):
    heads = HEADS // n_head
    width = heads * HD
    shards = held.shape[0]
    starts = borders(n_head)
    shared = pltpu.make_async_copy(grads_in.at[pl.ds(shards - 1, 1)], held.at[pl.ds(shards - 1, 1)], sems.at[0])
    shared.start()
    d_heads = {}
    for slot, head in enumerate(heads_of(n_head, d_kv_self.shape[0])):
        d_kv_head = d_kv_self[slot]
        d_heads[head] = (unpack(d_q_self[slot]), d_kv_head[:, :HD], d_kv_head[:, HD:])
    d_projected = [
        jnp.concatenate([d_heads[(g, a)][i] for i in range(3) for a in range(heads)], 1)
        for g in range(n_head)
    ]
    whole = jnp.concatenate(d_projected, 1)
    d_middle, gain_one_grad = norm_pullback(
        z_one[...], gains[1:2, :], against(whole, self_project[...])
    )
    d_one = d_two[...] + d_middle
    d_one_low = d_one.astype(low)
    d_o = against(d_one_low, enc_output[...]).astype(low)
    for g in range(n_head):
        keys = kv_enc[:, 2 * g * width : (2 * g + 1) * width]
        values = kv_enc[:, (2 * g + 1) * width : (2 * g + 2) * width]
        d_key = jnp.zeros(keys.shape, jnp.float32)
        d_value = jnp.zeros(keys.shape, jnp.float32)
        d_query = jnp.zeros((rows, width), jnp.float32)
        for (here, q_head), (unused, do_head) in zip(
            head_lanes(g, heads, q_enc[...]), head_lanes(g, heads, d_o)
        ):
            scores = enc_scores(keys, q_head)
            probs = jnp.exp2((scores - jnp.max(scores, 0, keepdims=True)).astype(low))
            probs = probs.astype(jnp.float32)
            probs = probs / jnp.sum(probs, 0, keepdims=True)
            d_probs = against(values, do_head)
            delta = jnp.sum(probs * d_probs, 0, keepdims=True)
            d_scores = (probs * (d_probs - delta)).astype(low)
            d_value = d_value + product(probs.astype(low), do_head)
            d_key = d_key + product(d_scores, q_head)
            d_query = jnp.where(here, contract_first(d_scores, keys), d_query)
        d_q[:, g * width : (g + 1) * width] = (d_query * SCORE_SCALE).astype(low)
        d_kv[:, 2 * g * width : (2 * g + 1) * width] = (d_key * SCORE_SCALE).astype(low)
        d_kv[:, (2 * g + 1) * width : (2 * g + 2) * width] = d_value.astype(low)
    d_middle, gain_zero_grad = norm_pullback(
        z_zero[...], gains[0:1, :], against(d_q[...], enc_query[...])
    )
    d_zero = d_one + d_middle
    d_zero_top = d_zero.astype(low)
    d_zero_rest = (d_zero - d_zero_top.astype(jnp.float32)).astype(low)
    picked = picked_rows(clip_bounds(lengths), rows, n_head)
    latent_grad = contract_first(picked, d_zero_top) + contract_first(picked, d_zero_rest)
    query_rows = query_grad.shape[0]
    stage_common[:query_rows] = query_grad[...]
    matrix_into(stage_common, query_rows, latent_grad, line)
    all_gains = jnp.concatenate([gain_zero_grad, gain_one_grad, gain_grads[...]], 0)
    matrix_into(stage_common, query_rows + LAT * D // LANES, all_gains, line)
    piece = common_grad.shape[2]
    for b in range(common_grad.shape[0]):
        for k in range(common_grad.shape[1]):
            amount = min(piece, valid - k * piece)
            block = stage_common[b * valid + k * piece : b * valid + k * piece + amount, :]
            if amount < piece:
                block = jnp.concatenate([block, jnp.zeros((piece - amount, LANES), jnp.float32)], 0)
            common_grad[b, k] = block.astype(low)
    shared.wait()
    kept = shards * shard_rows - starts[4]
    for g in range(n_head):
        results = (
            contract_first(h_zero[...], d_q[:, g * width : (g + 1) * width]),
            product(x_norm_t[...], d_kv[:, 2 * g * width : (2 * g + 2) * width]),
            contract_first(o_enc[:, g * width : (g + 1) * width], d_one_low),
            contract_first(h_one[...], d_projected[g]),
        )
        if kept:
            stage[pl.ds((shards - 1) * shard_rows, shard_rows), :] = held[
                shards - 1, g, :shard_rows, :
            ].astype(jnp.float32)
        for m, result in zip((0, 1, 2, 3), results):
            matrix_into(stage, starts[m], result, line)
        for b in range(shards):
            held[b, g, :shard_rows, :] = stage[pl.ds(b * shard_rows, shard_rows), :].astype(low)
    back = pltpu.make_async_copy(held, grads.at[pl.ds(0, shards)], sems.at[1])
    back.start()
    back.wait()


def ending(lengths, grads, d_self, d_two, gains, gain_grads, query_grad, kept, common_shape, valid, shard_rows):
    rows = d_two.shape[0]
    n_head = grads.shape[1]
    begin, shards = shards_of(n_head, shard_rows, 0, 4)
    keys = kept[6].shape[1]
    common_rows = (DQ + LAT + 4) * D // LANES
    return pl.pallas_call(
        functools.partial(ending_kernel, n_head, shard_rows, valid, rows),
        out_shape=[shape_of(grads.shape), shape_of(common_shape)],
        in_specs=[SMEM_SPEC, ANY_SPEC] + [VMEM_SPEC] * 18,
        out_specs=[ANY_SPEC, VMEM_SPEC],
        input_output_aliases={1: 0},
        scratch_shapes=[
            pltpu.VMEM((shards,) + grads.shape[1:], low),
            pltpu.VMEM((shards * shard_rows, LANES), jnp.float32),
            pltpu.VMEM((common_rows, LANES), jnp.float32),
            LINE,
            pltpu.VMEM((rows, D), low),
            pltpu.VMEM((keys, 2 * D), low),
            pltpu.SemaphoreType.DMA((2,)),
        ],
        compiler_params=pltpu.CompilerParams(vmem_limit_bytes=56 * MIB),
        name="ending",
    )(lengths, grads, *d_self, d_two, gains, gain_grads, query_grad, *kept)


def adam_step(weight, first, second, grad):
    first = beta_one * first + (1 - beta_one) * grad
    second = beta_two * second + (1 - beta_two) * grad * grad
    fixed_first = first / (1 - beta_one**STEP)
    fixed_second = second / (1 - beta_two**STEP)
    weight = weight - learn_rate * (
        fixed_first / (jnp.sqrt(fixed_second) + adam_eps) + weight_decay * weight
    )
    return (weight, first, second, weight.astype(low))


def per_device(
    inputs,
    out_queries,
    clip_lengths,
    labels,
    modality,
    labeled,
    head_params,
    head_first,
    head_second,
    common_params,
    common_first,
    common_second,
):
    n_head, n_blk = lax.axis_size("head"), lax.axis_size("blk")
    dims = grid_of(n_blk, n_head)
    rows = labels.shape[0] // n_head
    n_h, n_c = head_params.shape[0], common_params.shape[0]
    shard_rows, common_rows = n_h // LANES, -(-n_c // LANES)
    head_rows = round_up(shard_rows + 1, TILE)
    piece_rows = round_up(-(-common_rows // n_head), TILE)
    marks = [x.reshape(-1, LANES) for x in (labels, modality, labeled)]
    head_wide = head_params.reshape(shard_rows, LANES)
    common_wide = jnp.pad(common_params, (0, common_rows * LANES - n_c)).reshape(common_rows, LANES)
    weights, common = gather_all(dims, marks, (head_wide, common_wide), (head_rows, piece_rows), 0)
    valid = common_rows
    if n_c % LANES:
        common = common.reshape(n_blk, -1)[:, :n_c].reshape(-1, LANES)
        valid = common.shape[0]
        common = jnp.pad(common, ((0, -valid % TILE), (0, 0)))[None, None]

    encoded = encode(
        clip_lengths, weights, common, inputs.T, valid, rows, Team(dims).size, n_head, shard_rows
    )
    gains, z_one, counts = encoded[4], encoded[11], encoded[15]
    o_self, lse_self, out_self_t, q_all, kv_all = attend(
        dims, clip_lengths, encoded[13], encoded[14], 1
    )
    dout, d_two, tile, query_grad, gain_grads, grads = middle(
        counts, weights, common, z_one, o_self, out_queries.T, marks, gains, valid, n_head, shard_rows
    )
    d_self = attend_back(dims, clip_lengths, q_all, kv_all, dout, out_self_t, lse_self, 2)
    kept = encoded[:4] + encoded[5:13]
    grads, common_grad = ending(
        clip_lengths,
        grads,
        d_self,
        d_two,
        gains,
        gain_grads,
        query_grad,
        kept,
        common.shape,
        valid,
        shard_rows,
    )
    if n_c % LANES:
        common_grad = common_grad[0, 0, :valid].reshape(n_blk, n_c)
        common_grad = jnp.pad(common_grad, ((0, 0), (0, n_head * piece_rows * LANES - n_c)))
        common_grad = common_grad.reshape(n_blk, n_head, piece_rows, LANES)
    head_share, common_share, loss_sums, clip_norm, factor = reduce_all(
        dims, (grads, common_grad), (shard_rows, common_rows), tile, 3
    )
    label_counts, loss_sums = encoded[16].reshape(MODES), loss_sums.reshape(MODES)
    clip_norm, factor = clip_norm.reshape(()), factor.reshape(())
    head_share, common_share = head_share.reshape(-1), common_share.reshape(-1)[:n_c]
    head_out = adam_step(head_params, head_first, head_second, head_share * factor)
    common_out = adam_step(common_params, common_first, common_second, common_share * factor)
    return head_out + common_out + (loss_sums, label_counts, clip_norm)


def solution(mesh):
    placed = (
        P("blk", None),
        P("blk", None),
        P(),
        P("blk"),
        P("blk"),
        P("blk"),
        P(("head", "blk")),
        P(("head", "blk")),
        P(("head", "blk")),
        P("blk"),
        P("blk"),
        P("blk"),
    )
    return jax.shard_map(
        per_device,
        mesh=mesh,
        in_specs=placed,
        out_specs=(
            P(("head", "blk")),
            P(("head", "blk")),
            P(("head", "blk")),
            P(("head", "blk")),
            P("blk"),
            P("blk"),
            P("blk"),
            P("blk"),
            P(),
            P(),
            P(),
        ),
        check_vma=False,
    )
```

```python
import functools

import jax
import jax.numpy as jnp
from jax import lax
from jax.experimental import pallas as pl
from jax.experimental.pallas import tpu as pltpu
from jax.sharding import PartitionSpec as P

D = 512
HEADS = 8
HD = 64
FF = 2048
DI = 704
DQ = 1026
C = 704
LAT = 784
MODES = 3
STEP = 10
LANES = 128
TILE = 16

norm_eps = 1e-05
learn_rate = 0.1
beta_one = 0.9
beta_two = 0.999
adam_eps = 1e-08
weight_decay = 0.01
clip_limit = 0.05
big_negative = -1e30
low = jnp.bfloat16
LOG2E = 1.4426950408889634
SCORE_SCALE = HD ** (-0.5)
MESH = pl.DeviceIdType.MESH
MIB = 1 << 20
VMEM_SPEC = pl.BlockSpec(memory_space=pltpu.VMEM)
SMEM_SPEC = pl.BlockSpec(memory_space=pltpu.SMEM)
ANY_SPEC = pl.BlockSpec(memory_space=pl.ANY)


def shape_of(shape, dtype=low):
    return jax.ShapeDtypeStruct(shape, dtype)


def round_up(n, unit):
    return -(-n // unit) * unit


def grid_of(n_blk, n_head):
    cores = 2 if n_head % 2 == 0 else 1
    x = n_head // cores
    y = x if n_blk % x == 0 else 1
    return (n_blk // y, y, x, cores)


def my_place(dims):
    blk, head = lax.axis_index("blk"), lax.axis_index("head")
    return (blk // dims[1], lax.rem(blk, dims[1]), head // dims[3], lax.rem(head, dims[3]))


def shifted(dims, me, offset, sign):
    return tuple(
        m if o == 0 else lax.rem(m + (o if sign > 0 else n - o), n)
        for m, o, n in zip(me, offset, dims)
    )


def blk_of(dims, place):
    return place[0] * dims[1] + place[1]


def head_of(dims, place):
    return place[2] * dims[3] + place[3]


def device_of(dims, place):
    return {"blk": blk_of(dims, place), "head": head_of(dims, place)}


def along(axis, d):
    return tuple(d if a == axis else 0 for a in range(4))


def greet(dims, me, offsets):
    barrier = pltpu.get_barrier_semaphore()
    for offset in offsets:
        pl.semaphore_signal(
            barrier,
            inc=1,
            device_id=device_of(dims, shifted(dims, me, offset, 1)),
            device_id_type=MESH,
        )
    pl.semaphore_wait(barrier, len(offsets))


def axis_peers(dims, axes):
    return [along(axis, d) for axis in axes for d in range(1, dims[axis])]


def remote(src, dst, send_sem, recv_sem, place, dims):
    return pltpu.make_async_remote_copy(
        src_ref=src,
        dst_ref=dst,
        send_sem=send_sem,
        recv_sem=recv_sem,
        device_id=device_of(dims, place),
        device_id_type=MESH,
    )


AHEAD = 6.0
RING = 0


def in_order(first, follow, size_of, ahead, result):
    queues, busy, flight = {}, {}, {}
    now = 0.0

    def ready(messages):
        for message in messages:
            queues.setdefault(message[1], []).append(message)

    ready(first)
    while True:
        for axis in sorted(queues):
            queue, going = queues[axis], flight.setdefault(axis, [])
            while queue and (not going or busy[axis] < now + ahead):
                message = min(queue)
                queue.remove(message)
                busy[axis] = max(now, busy.get(axis, 0.0)) + size_of(message)
                going.append((busy[axis] + 1.5, message))
                result.append((True, message))
        arrivals = [min(going) for going in flight.values() if going]
        if not arrivals:
            return now
        arrival = min(arrivals)
        flight[arrival[1][1]].remove(arrival)
        now = max(now, arrival[0])
        result.append((False, arrival[1]))
        ready(follow(arrival[1]))


def time_of(rows, axis):
    return rows * LANES * 2 / (300e3 if axis == 3 else 45e3)


def with_at(offset, axis, d):
    return offset[:axis] + (d,) + offset[axis + 1 :]


def gather_order(dims, parts):
    def onward(p, offset, position):
        order = parts[p][3]
        result = []
        for k in range(max(position, 0), 4):
            axis = order[k]
            n = dims[axis]
            if k > position:
                steps = [1] if axis == RING else range(1, n)
                steps = [d for d in steps if d < n]
            else:
                steps = [offset[axis] + 1] if axis == RING and offset[axis] + 1 < n else []
            for d in steps:
                result.append(((k, sum(offset), p), axis, p, with_at(offset, axis, d)))
        return result

    def follow(message):
        rank, axis, p, offset = message
        return onward(p, offset, rank[0])

    first = [m for p in range(len(parts)) for m in onward(p, (0, 0, 0, 0), -1)]
    result = []
    now = in_order(first, follow, lambda m: time_of(parts[m[2]][2], m[1]), AHEAD, result)
    return result, now


def gather_kernel(
    dims,
    parts,
    labels,
    modality,
    labeled,
    head_params,
    common_params,
    head_all,
    common_all,
    head_low,
    common_low,
    common_wide,
    send_sem,
    recv_sem,
    own_sem,
):
    me = my_place(dims)
    my_head = head_of(dims, me)
    n_head = dims[2] * dims[3]
    shard_rows, common_rows = head_params.shape[0], common_params.shape[0]
    per_head = labels.shape[0] // n_head
    row = lax.broadcasted_iota(jnp.int32, labels.shape, 0)
    mine = (row >= my_head * per_head) & (row < (my_head + 1) * per_head) & (labeled[...] == 1)
    lane = lax.broadcasted_iota(jnp.int32, (1, LANES), 1)
    counts = jnp.zeros((1, LANES), jnp.float32)
    for m in range(MODES):
        member = jnp.where(mine & (modality[...] == m), 1.0, 0.0)
        counts = counts + jnp.where(lane == m, jnp.sum(member, (0, 1), keepdims=True), 0.0)
    padding = head_low.shape[0] - shard_rows
    tail = shard_rows // TILE * TILE
    head_low[:tail] = head_params[:tail].astype(low)
    last = [jnp.broadcast_to(counts, (padding, LANES))]
    if shard_rows > tail:
        last = [head_params[tail:]] + last
    head_low[tail:] = jnp.concatenate(last, 0).astype(low)
    common_wide[...] = jnp.zeros(common_wide.shape, jnp.float32)
    common_wide[:common_rows] = common_params[...]
    piece = common_low.shape[0]
    common_low[...] = common_wide[pl.ds(pl.multiple_of(my_head * piece, TILE), piece)].astype(low)

    greet(dims, me, ring_and_others(dims))
    srcs, outs = (head_low, common_low), (head_all, common_all)
    copies = {}

    def block(p, offset):
        place = shifted(dims, me, offset, -1)
        array, first, rows, order = parts[p]
        return outs[array].at[blk_of(dims, place), head_of(dims, place), pl.ds(first, rows)]

    own = []
    for is_send, (rank, axis, p, offset) in gather_order(dims, parts)[0]:
        if is_send:
            step = 1 if axis == RING else offset[axis]
            before = with_at(offset, axis, offset[axis] - step)
            array, first, rows, order = parts[p]
            source = block(p, before) if any(before) else srcs[array].at[pl.ds(first, rows)]
            i = len(copies)
            copies[(p, offset)] = remote(
                source,
                block(p, before),
                send_sem.at[i],
                recv_sem.at[i],
                shifted(dims, me, along(axis, step), 1),
                dims,
            )
            copies[(p, offset)].start()
        else:
            if not own:
                for array in range(2):
                    copy = pltpu.make_async_copy(
                        srcs[array], outs[array].at[blk_of(dims, me), my_head], own_sem.at[array]
                    )
                    copy.start()
                    own.append(copy)
            copies[(p, offset)].wait_recv()
    for copy in copies.values():
        copy.wait_send()
    for copy in own:
        copy.wait()


def ring_and_others(dims):
    ring = {along(RING, 1 % dims[RING]), along(RING, (dims[RING] - 1) % dims[RING])}
    return sorted(ring - {(0, 0, 0, 0)}) + axis_peers(dims, (1, 2, 3))


def cut(array, rows, shares):
    result = []
    first, so_far = 0, 0
    whole = sum(share for share, order in shares)
    for share, order in shares:
        so_far += share
        end = rows * so_far // whole // TILE * TILE if so_far < whole else rows
        if end > first:
            result.append((array, first, end - first, order))
        first = end
    return tuple(result)


ZYXC, ZXYC, YXZC, XYZC = (0, 1, 2, 3), (0, 2, 1, 3), (1, 2, 0, 3), (2, 1, 0, 3)
GATHER_SHARES = ((8, ZYXC), (6, ZXYC), (2, YXZC), (2, XYZC))
REDUCE_SHARES = ((7, ZYXC), (7, ZXYC), (2, YXZC), (2, XYZC))


def gather_all(dims, marks, params, rows, collective_id):
    z, y, x, cores = dims
    parts = cut(0, rows[0], GATHER_SHARES) + cut(1, rows[1], ((1, ZXYC),))
    count = len(parts) * (z * y * x * cores - 1)
    return pl.pallas_call(
        functools.partial(gather_kernel, dims, parts),
        out_shape=[shape_of((z * y, x * cores, n, LANES)) for n in rows],
        in_specs=[VMEM_SPEC] * 5,
        out_specs=[ANY_SPEC] * 2,
        scratch_shapes=[pltpu.VMEM((n, LANES), low) for n in rows]
        + [
            pltpu.VMEM((x * cores * rows[1], LANES), jnp.float32),
            pltpu.SemaphoreType.DMA((count,)),
            pltpu.SemaphoreType.DMA((count,)),
            pltpu.SemaphoreType.DMA((2,)),
        ],
        compiler_params=pltpu.CompilerParams(collective_id=collective_id, has_side_effects=True),
        name="gather_weights",
    )(*marks, *params)


def reduce_order(dims, parts):
    ready, arrived, order = set(), set(), []

    def message(p, position, offset):
        z = offset[RING]
        rank = (dims[RING] - z if z else dims[RING], position, tuple(-o for o in offset), p)
        return (rank, parts[p][3][position], p, position, offset)

    def done(p, position, offset):
        ready.add((p, position, offset))
        if position == 4:
            return []
        axis = parts[p][3][position]
        d = offset[axis]
        first = d != 0 and (axis != RING or d == dims[axis] - 1)
        return ([message(p, position, offset)] if first else []) + advance(p, position, offset)

    def advance(p, position, offset):
        axis = parts[p][3][position]
        n = dims[axis]
        start = with_at(offset, axis, 0)
        if axis == RING:
            here = (p, position, offset)
            if here in ready and here in arrived:
                order.append((None, here))
                if offset[axis]:
                    return [message(p, position, offset)]
                return done(p, position + 1, offset)
        elif (p, position, start) in ready and (p, position + 1, start) not in ready:
            if all((p, position, with_at(start, axis, d)) in arrived for d in range(1, n)):
                order.append((None, (p, position, start)))
                return done(p, position + 1, start)
        return []

    def follow(sent):
        rank, axis, p, position, offset = sent
        here = with_at(offset, axis, offset[axis] - 1) if axis == RING else offset
        arrived.add((p, position, here))
        return advance(p, position, here)

    first = []
    for p in range(len(parts)):
        for offset in all_offsets(dims, range(4)):
            first += done(p, 0, offset)
    now = in_order(first, follow, lambda m: time_of(parts[m[2]][2], m[1]), AHEAD, order)
    return order, now


def all_offsets(dims, axes):
    offsets = [(0, 0, 0, 0)]
    for a in axes:
        offsets = [with_at(o, a, d) for o in offsets for d in range(dims[a])]
    return offsets


def reduce_kernel(dims, parts, *refs):
    srcs, tile = refs[:2], refs[2]
    head_out, common_out, losses, norm, factor = refs[3:8]
    places = len(parts) * 4
    buffers = refs[8 : 8 + places]
    head_sum, common_sum, shares, send_sem, recv_sem, near_tiles, far_tiles = refs[8 + places :]
    sums = (head_sum, common_sum)
    me = my_place(dims)
    z, y, x, cores = dims
    across = peers_across(dims)
    others = [o for o in all_offsets(dims, (0, 1)) if any(o)]
    met = ring_and_others(dims)
    greet(dims, me, met + [o for o in across + others if o not in met])
    push = Pushes(dims, me, send_sem, recv_sem)
    copies = {}

    def slot(p, position, offset):
        order = parts[p][3]
        axis = order[position]
        rest = [o for o in all_offsets(dims, order[position + 1 :])]
        k = rest.index(with_at(offset, axis, 0))
        return buffers[p * 4 + position].at[k, max(offset[axis] - 1, 0)]

    def summed(p, position, offset):
        array, first, rows, order = parts[p]
        if position == 0:
            place = shifted(dims, me, offset, 1)
            return srcs[array].at[blk_of(dims, place), head_of(dims, place), pl.ds(first, rows)]
        return slot(p, position - 1, offset)

    def ring_slot(p, position, offset):
        axis = parts[p][3][position]
        return slot(p, position, with_at(offset, axis, offset[axis] + 1))

    def add(p, position, offset):
        array, first, rows, order = parts[p]
        axis = order[position]
        if axis == RING:
            arrivals = [ring_slot(p, position, offset)]
        else:
            arrivals = [slot(p, position, with_at(offset, axis, d)) for d in range(1, dims[axis])]
        mine = summed(p, position, offset)
        step = row_chunk(rows)

        @pl.loop(0, rows // step)
        def some_rows(n):
            at = pl.ds(pl.multiple_of(n * step, step), step)
            total = mine[at].astype(jnp.float32)
            for arrival in arrivals:
                total = total + arrival[at].astype(jnp.float32)
            if position == 3 and not any(offset):
                sums[array][pl.ds(pl.multiple_of(first + n * step, TILE), step)] = total
            else:
                arrivals[0][at] = total.astype(low)

    for is_send, what in reduce_order(dims, parts)[0]:
        if is_send is None:
            add(*what)
        elif is_send:
            rank, axis, p, position, offset = what
            d = offset[axis]
            started = axis != RING or d == dims[axis] - 1
            source = summed(p, position, offset) if started else ring_slot(p, position, offset)
            step = along(axis, 1 if axis == RING else d)
            copies[what] = push(source, slot(p, position, offset), step)
        else:
            copies[what].wait_recv()
    my_head, my_blk = head_of(dims, me), blk_of(dims, me)
    shares[my_head] = common_sum[...].astype(low)
    share_copies = [push(shares.at[my_head], shares.at[my_head], o) for o in across]
    amount = head_out.shape[0]
    head_out[...] = head_sum[:amount]
    squares = jnp.sum(head_sum[:amount] * head_sum[:amount], 0, keepdims=True)
    squares = squares + jnp.sum(common_sum[...] * common_sum[...], 0, keepdims=True)
    lane = lax.broadcasted_iota(jnp.int32, (1, LANES), 1)
    near_tiles[my_head] = tile[...] + jnp.where(
        lane == MODES, jnp.sum(squares, 1, keepdims=True), 0.0
    )
    near = [push(near_tiles.at[my_head], near_tiles.at[my_head], o) for o in across]
    for copy in near:
        copy.wait_recv()
    far_tiles[my_blk] = jnp.sum(near_tiles[...], 0)
    far = [push(far_tiles.at[my_blk], far_tiles.at[my_blk], o) for o in others]
    for copy in share_copies:
        copy.wait_recv()
    piece = shares.shape[1]
    for k in range(x * cores):
        amount = min(piece, common_out.shape[0] - k * piece)
        common_out[k * piece : k * piece + amount] = shares[k].astype(jnp.float32)[:amount]
    for copy in far:
        copy.wait_recv()
    totals = jnp.sum(far_tiles[...], 0)[:1]
    losses[...] = totals[:, :MODES]
    norm[...] = jnp.sqrt(totals[:, MODES : MODES + 1])
    factor[...] = jnp.minimum(1.0, clip_limit / norm[...])
    push.finish()


def row_chunk(rows):
    for count in (4, 3, 2):
        if rows % (count * TILE) == 0:
            return rows // count
    return rows


def reduce_all(dims, arrays, valid, tile, collective_id):
    z, y, x, cores = dims
    rows = [array.shape[2] for array in arrays]
    parts = cut(0, rows[0], [(share, order[::-1]) for share, order in REDUCE_SHARES])
    parts = parts + cut(1, rows[1], ((1, ZXYC[::-1]),))
    scratch = []
    for array, first, amount, order in parts:
        for position, axis in enumerate(order):
            rest = len(all_offsets(dims, order[position + 1 :]))
            scratch.append(pltpu.VMEM((rest, dims[axis] - 1, amount, LANES), low))
    count = len(parts) * (z * y * x * cores - 1) + 2 * (x * cores - 1) + z * y - 1
    return pl.pallas_call(
        functools.partial(reduce_kernel, dims, parts),
        out_shape=[
            shape_of((valid[0], LANES), jnp.float32),
            shape_of((valid[1], LANES), jnp.float32),
            shape_of((1, MODES), jnp.float32),
            shape_of((1, 1), jnp.float32),
            shape_of((1, 1), jnp.float32),
        ],
        in_specs=[VMEM_SPEC] * 3,
        out_specs=[VMEM_SPEC] * 5,
        scratch_shapes=scratch
        + [pltpu.VMEM((n, LANES), jnp.float32) for n in rows]
        + [
            pltpu.VMEM((x * cores, rows[1], LANES), low),
            pltpu.SemaphoreType.DMA((count,)),
            pltpu.SemaphoreType.DMA((count,)),
            pltpu.VMEM((x * cores, 8, LANES), jnp.float32),
            pltpu.VMEM((z * y, 8, LANES), jnp.float32),
        ],
        compiler_params=pltpu.CompilerParams(
            collective_id=collective_id, has_side_effects=True, vmem_limit_bytes=60 * MIB
        ),
        name="reduce_gradients",
    )(*arrays, tile)


def contract_first(a, b):
    return lax.dot_general(a, b, (((0,), (0,)), ((), ())), preferred_element_type=jnp.float32)


def product(a, b):
    return jnp.dot(a, b, preferred_element_type=jnp.float32)


def against(a, b):
    return lax.dot_general(a, b, (((1,), (1,)), ((), ())), preferred_element_type=jnp.float32)


def clip_bounds(lengths):
    result, first = [], 0
    for clip in range(lengths.shape[0]):
        end = first + lengths[clip]
        result.append((first, end))
        first = end
    return result


def clip_borders(bounds, place):
    opening = jnp.zeros(place.shape, jnp.int32)
    ending = jnp.full(place.shape, 1 << 30, jnp.int32)
    for clip, (begin, end) in enumerate(bounds):
        here = place == clip
        opening = jnp.where(here, begin, opening)
        ending = jnp.where(here, end, ending)
    return opening, ending


def low_half(axis):
    return lax.broadcasted_iota(jnp.int32, (1, LANES) if axis else (LANES, 1), axis) < HD


def with_key_tail(bounds, first_row, kv):
    clips = len(bounds)
    place = lax.broadcasted_iota(jnp.int32, (1, LANES), 1) - HD
    opening, ending = clip_borders(bounds, place)
    ones = jnp.where((place >= clips) & (place < clips + 3), 1.0, 0.0)
    row = first_row + lax.broadcasted_iota(jnp.int32, kv.shape, 0)
    tail = jnp.where((row >= opening) & (row < ending), ones, big_negative)
    return jnp.where(low_half(1), kv.astype(jnp.float32), tail).astype(low)


def with_value_tail(kv):
    place = lax.broadcasted_iota(jnp.int32, (1, LANES), 1)
    ones = jnp.where(place < 3, 1.0, 0.0)
    return jnp.where(low_half(1), ones, kv.astype(jnp.float32)).astype(low)


def in_three(place, value):
    top = value.astype(low).astype(jnp.float32)
    middle = (value - top).astype(low).astype(jnp.float32)
    bottom = value - top - middle
    return (
        jnp.where(place == 0, top, 0.0)
        + jnp.where(place == 1, middle, 0.0)
        + jnp.where(place == 2, bottom, 0.0)
    )


def with_query_tail(bounds, first_row, rows, extra):
    clips = len(bounds)
    place = lax.broadcasted_iota(jnp.int32, (HD, 1), 0)
    opening, ending = clip_borders(bounds, place)
    row = first_row + lax.broadcasted_iota(jnp.int32, (1, rows.shape[1]), 1)
    inside = (place < clips) & (row >= opening) & (row < ending)
    tail = jnp.where(inside, 1.0, 0.0)
    if extra is not None:
        tail = tail + in_three(place - clips, -extra)
    return jnp.concatenate([rows * (SCORE_SCALE * LOG2E), tail], 0).astype(low)


def pack(rows):
    half = rows.shape[0] // 2
    return jnp.concatenate([rows[:half], rows[half:]], 1)


def unpack(packed):
    return jnp.concatenate([packed[:, :HD], packed[:, HD:]], 0)


def unpack_t(packed):
    turned = packed.astype(jnp.float32).T
    return jnp.concatenate([turned[:HD], turned[HD:]], 1)


def pack_t(columns):
    half = columns.shape[1] // 2
    return jnp.concatenate([columns[:, :half], columns[:, half:]], 0).T


class Team:
    def __init__(self, dims):
        z, y, x, cores = dims
        self.dims = dims
        self.wide = HEADS // (x * cores) == y
        self.size = x * cores * (y if self.wide else 1)
        self.groups = z if self.wide else z * y
        axes = (1, 2, 3) if self.wide else (2, 3)
        offsets = [o for o in all_offsets(dims, axes) if any(o)]
        self.others = sorted(offsets, key=lambda o: (o[1] + o[2], o))
        self.sides = [] if self.wide else axis_peers(dims, (1,))

    def slot(self, place):
        head = head_of(self.dims, place)
        return place[1] * self.dims[2] * self.dims[3] + head if self.wide else head

    def group(self, place):
        return place[0] if self.wide else blk_of(self.dims, place)


def heads_of(n_head, slots):
    return [(s % n_head, s // n_head) for s in range(slots)]


class Pushes:
    def __init__(self, dims, me, send_sem, recv_sem):
        self.dims, self.me, self.send_sem, self.recv_sem = dims, me, send_sem, recv_sem
        self.started = []

    def __call__(self, src, dst, offset):
        i = len(self.started)
        place = shifted(self.dims, self.me, offset, 1)
        copy = remote(src, dst, self.send_sem.at[i], self.recv_sem.at[i], place, self.dims)
        copy.start()
        self.started.append(copy)
        return copy

    def finish(self):
        for copy in self.started:
            copy.wait_send()


def peers_across(dims):
    z, y, x, cores = dims
    across = [(0, 0, a, c) for a in range(x) for c in range(cores) if (a, c) != (0, 0)]
    return sorted(across, key=lambda o: (o[2] == 0, o[3]))


def attend_kernel(
    team,
    query_step,
    key_step,
    pieces,
    lengths,
    q_in,
    kv_in,
    o_out,
    lse,
    out_t,
    q_all,
    kv_all,
    even_keys,
    even_values_t,
    odd_keys,
    odd_values_t,
    queries,
    top,
    accum,
    even_scores,
    odd_scores,
    even_top,
    odd_top,
    o_mine,
    send_sem,
    recv_sem,
    own_sem,
):
    dims = team.dims
    z = dims[0]
    me = my_place(dims)
    bounds = clip_bounds(lengths)
    rows = kv_in.shape[1]
    amount = team.size * rows
    slots = team.size // pieces
    my_group, my_slot = team.group(me), team.slot(me)
    ring_ends = sorted({along(0, 1 % z), along(0, (z - 1) % z)} - {(0, 0, 0, 0)})
    greet(dims, me, team.others + ring_ends + team.sides)
    push = Pushes(dims, me, send_sem, recv_sem)
    own_kv = pltpu.make_async_copy(kv_in.at[my_slot], kv_all.at[my_group, my_slot], own_sem.at[0])
    own_q = pltpu.make_async_copy(q_in.at[my_slot], q_all.at[my_slot], own_sem.at[1])
    own_kv.start()
    own_q.start()

    def to_team(src, dst, o):
        return push(src.at[team.slot(shifted(dims, me, o, 1))], dst, o)

    kv_copies = {o: to_team(kv_in, kv_all.at[my_group, my_slot], o) for o in team.others}
    q_copies = [to_team(q_in, q_all.at[my_slot], o) for o in team.others]
    ring, side = {}, {}

    def group_at(offset):
        return team.group(shifted(dims, me, offset, -1))

    def send_on(s, piece):
        block = kv_all.at[group_at(along(0, s)), pl.ds(piece * slots, slots)]
        if s < z - 1:
            ring[(s + 1, piece)] = push(block, block, along(0, 1))
        for o in team.sides:
            side[(s, o, piece)] = push(block, block, o)

    def both(now, later):
        if now is not None:
            n, unused, now_values, now_scores, now_top = now
            at = tile(n)
            old = top[:, at]
            new = jnp.maximum(old, jnp.max(now_top[...], 0, keepdims=True))
            top[:, at] = new
            total = accum[:, at] * jnp.exp2(old - new)
        if later is not None:
            n, later_keys, unused, later_scores, later_top = later
            query = queries[:, tile(n)]
            highest = jnp.full(later_top.shape, -1e38, jnp.float32)
        for k in range(0, slots * rows, key_step):
            if later is not None:
                scores = product(later_keys[k : k + key_step, :], query)
                later_scores[k : k + key_step, :] = scores
                highest = jnp.maximum(
                    highest, jnp.max(scores.reshape(key_step // 8, 8, query_step), 0)
                )
            if now is not None:
                probs = jnp.exp2((now_scores[k : k + key_step, :] - new).astype(low))
                total = total + product(now_values[:, k : k + key_step], probs)
        if later is not None:
            later_top[...] = highest
        if now is not None:
            accum[:, at] = total

    def tile(n):
        return pl.ds(pl.multiple_of(n * query_step, query_step), query_step)

    computed, pending = [], [None]

    def compute(offset, piece):
        group = group_at(offset)
        keys, values_t = sides_of_keys[len(computed) % 2]
        computed.append(offset)

        @pl.loop(0, slots)
        def build(n):
            at = pl.ds(pl.multiple_of(n * rows, rows), rows)
            slot = piece * slots + n
            block = kv_all[group, slot]
            keys[at, :] = with_key_tail(bounds, group * amount + slot * rows, block)
            values_t[:HD, at] = block.astype(jnp.float32).T[HD:].astype(low)

        def even(n):
            return (n, keys, values_t, even_scores, even_top)

        def odd(n):
            return (n, keys, values_t, odd_scores, odd_top)

        tiles = amount // query_step
        both(pending[0], even(0))

        @pl.loop(0, tiles // 2 - 1)
        def query_blocks(n):
            both(even(2 * n), odd(2 * n + 1))
            both(odd(2 * n + 1), even(2 * n + 2))

        both(even(tiles - 2), odd(tiles - 1))
        pending[0] = odd(tiles - 1)

    sides_of_keys = ((even_keys, even_values_t), (odd_keys, odd_values_t))
    for unused, values_t in sides_of_keys:
        values_t[HD:, :] = jnp.ones((TILE, slots * rows), low)
    top[...] = jnp.full(top.shape, -1e38, jnp.float32)
    accum[...] = jnp.zeros(accum.shape, jnp.float32)
    own_kv.wait()
    for o in team.others:
        kv_copies[o].wait_recv()
    for piece in range(pieces):
        send_on(0, piece)
    own_q.wait()
    for copy in q_copies:
        copy.wait_recv()
    for n in range(team.size):
        queries[:, n * rows : (n + 1) * rows] = with_query_tail(
            bounds, my_group * amount + n * rows, unpack_t(q_all[n]), None
        )
    for s in range(z):
        for piece in range(pieces):
            compute(along(0, s), piece)
            if s < z - 1:
                ring[(s + 1, piece)].wait_recv()
                send_on(s + 1, piece)
            for o in team.sides:
                side[(s, o, piece)].wait_recv()
                compute((s, o[1], 0, 0), piece)
    both(pending[0], None)
    total = accum[HD : HD + 1, :]
    out_t[...] = accum[:HD, :] / total
    lse[...] = top[...] + jnp.log(total) * LOG2E
    for n in range(team.size):
        o_mine[n] = pack_t(out_t[:, n * rows : (n + 1) * rows]).astype(low)
    o_copies = [to_team(o_mine, o_out.at[my_slot], o) for o in team.others]
    own_o = pltpu.make_async_copy(o_mine.at[my_slot], o_out.at[my_slot], own_sem.at[2])
    own_o.start()
    own_o.wait()
    for copy in o_copies:
        copy.wait_recv()
    push.finish()


def attend(dims, lengths, q, kv, collective_id):
    team = Team(dims)
    z = dims[0]
    amount = team.size * kv.shape[1]
    pieces, query_step = 2, 256
    count = 3 * (team.size - 1) + pieces * (z + z * len(team.sides))
    return pl.pallas_call(
        functools.partial(attend_kernel, team, query_step, 256, pieces),
        out_shape=(
            jax.ShapeDtypeStruct(q.shape, low),
            jax.ShapeDtypeStruct((1, amount), jnp.float32),
            jax.ShapeDtypeStruct((HD, amount), jnp.float32),
            jax.ShapeDtypeStruct(q.shape, low),
            jax.ShapeDtypeStruct((team.groups,) + kv.shape, low),
        ),
        in_specs=[SMEM_SPEC, VMEM_SPEC, VMEM_SPEC],
        out_specs=[VMEM_SPEC] * 5,
        scratch_shapes=[
            pltpu.VMEM((amount // pieces, LANES), low),
            pltpu.VMEM((HD + TILE, amount // pieces), low),
            pltpu.VMEM((amount // pieces, LANES), low),
            pltpu.VMEM((HD + TILE, amount // pieces), low),
            pltpu.VMEM((LANES, amount), low),
            pltpu.VMEM((1, amount), jnp.float32),
            pltpu.VMEM((HD + TILE, amount), jnp.float32),
            pltpu.VMEM((amount // pieces, query_step), jnp.float32),
            pltpu.VMEM((amount // pieces, query_step), jnp.float32),
            pltpu.VMEM((8, query_step), jnp.float32),
            pltpu.VMEM((8, query_step), jnp.float32),
            pltpu.VMEM(q.shape, low),
            pltpu.SemaphoreType.DMA((count,)),
            pltpu.SemaphoreType.DMA((count,)),
            pltpu.SemaphoreType.DMA((3,)),
        ],
        compiler_params=pltpu.CompilerParams(
            collective_id=collective_id, has_side_effects=True, vmem_limit_bytes=56 * MIB
        ),
        name="attend",
    )(lengths, q, kv)


def attend_back_kernel(
    team,
    key_step,
    query_step,
    pieces,
    lengths,
    q_all,
    kv_all,
    do_in,
    out_t,
    lse,
    d_q_out,
    d_kv_out,
    do_all,
    even_keys_t,
    even_values_t,
    even_rows,
    odd_keys_t,
    odd_values_t,
    odd_rows,
    queries,
    douts,
    d_q_sum,
    q_rows,
    do_rows,
    even_probs,
    odd_probs,
    even_scores,
    odd_scores,
    side_out,
    side_in,
    ring_out,
    ring_in,
    mine,
    d_q_mine,
    d_kv_mine,
    send_sem,
    recv_sem,
    own_sem,
):
    dims = team.dims
    z = dims[0]
    me = my_place(dims)
    bounds = clip_bounds(lengths)
    rows = kv_all.shape[2]
    amount = team.size * rows
    slots = team.size // pieces
    piece_rows = slots * rows
    my_group, my_slot = team.group(me), team.slot(me)
    ring_ends = sorted({along(0, 1 % z), along(0, (z - 1) % z)} - {(0, 0, 0, 0)})
    greet(dims, me, team.others + ring_ends + team.sides)
    push = Pushes(dims, me, send_sem, recv_sem)

    def to_team(src, dst, o):
        return push(src.at[team.slot(shifted(dims, me, o, 1))], dst, o)

    do_copies = [to_team(do_in, do_all.at[my_slot], o) for o in team.others]
    own_do = pltpu.make_async_copy(do_in.at[my_slot], do_all.at[my_slot], own_sem.at[0])
    own_do.start()
    place = lax.broadcasted_iota(jnp.int32, (HD, 1), 0)
    for n in range(team.size):
        at = slice(n * rows, (n + 1) * rows)
        q_t = unpack_t(q_all[n])
        extended = with_query_tail(bounds, my_group * amount + n * rows, q_t, lse[:, at])
        queries[at, :] = extended.astype(jnp.float32).T.astype(low)
        q_rows[:, at] = (q_t * SCORE_SCALE).astype(low)
    d_q_sum[...] = jnp.zeros(d_q_sum.shape, jnp.float32)
    own_do.wait()
    for copy in do_copies:
        copy.wait_recv()
    for n in range(team.size):
        at = slice(n * rows, (n + 1) * rows)
        do_t = unpack_t(do_all[n])
        delta = jnp.sum(do_t * out_t[:, at], 0, keepdims=True)
        extended = jnp.concatenate([in_three(place, -delta), do_t], 0).astype(low)
        douts[at, :] = extended.astype(jnp.float32).T.astype(low)
        do_rows[:, at] = do_t.astype(low)

    def both(now, later):
        if now is not None:
            n, (unused, unused, now_rows), now_probs, now_scores, target = now
            now_at = rows_of(n)
        if later is not None:
            n, (keys_t, values_t, unused), later_probs, later_scores, unused = later
            at = rows_of(n)
        for first in range(0, amount, query_step):
            part = slice(first, first + query_step)
            if later is not None:
                probs = jnp.exp2(product(queries[part, :], keys_t[:, at]).astype(low))
                d_probs = product(douts[part, :], values_t[:, at])
                later_probs[part, :] = probs
                later_scores[part, :] = (probs.astype(jnp.float32) * d_probs).astype(low)
            if now is not None:
                if first == 0:
                    d_value = product(do_rows[...], now_probs[...])
                if first == amount // 2:
                    d_key = product(q_rows[...], now_scores[...])
                d_q_sum[part, :] = d_q_sum[part, :] + product(now_scores[part, :], now_rows[now_at, :])
        if now is not None:
            target[now_at, :] = jnp.concatenate([d_key, d_value], 0).T.astype(target.dtype)

    def rows_of(k):
        return slice(k * key_step, (k + 1) * key_step)

    computed, pending = [], []

    def flush(later=None):
        if pending:
            now, after = pending.pop()
            both(now, later)
            after()
        elif later is not None:
            both(None, later)

    def compute(offset, piece, target, after):
        group = team.group(shifted(dims, me, offset, 1))
        keys = sides_of_keys[len(computed) % 2]
        computed.append(offset)

        @pl.loop(0, slots)
        def build(n):
            at = pl.ds(pl.multiple_of(n * rows, rows), rows)
            slot = piece * slots + n
            block = kv_all[group, slot]
            extended = with_key_tail(bounds, group * amount + slot * rows, block)
            keys[0][:, at] = extended.astype(jnp.float32).T.astype(low)
            keys[1][:, at] = with_value_tail(block).astype(jnp.float32).T.astype(low)
            keys[2][at, :] = block

        steps = [
            (k, keys) + ((odd_probs, odd_scores) if k % 2 else (even_probs, even_scores)) + (target,)
            for k in range(piece_rows // key_step)
        ]
        flush(steps[0])
        for now, later in zip(steps[:-1], steps[1:]):
            both(now, later)
        pending.append((steps[-1], after))

    sides_of_keys = (
        (even_keys_t, even_values_t, even_rows),
        (odd_keys_t, odd_values_t, odd_rows),
    )
    side, ring = {}, {}

    def send_sides(s, piece):
        for o in team.sides:
            target = side_out.at[s - 1, o[1] - 1, piece]

            def send(o=o, target=target):
                side[(s, o, piece)] = push(target, side_in.at[s - 1, o[1] - 1, piece], o)

            compute((z - s, o[1], 0, 0), piece, target, send)

    def combine(s, piece):
        for o in team.sides:
            side[(s, o, piece)].wait_recv()
        if s > 1:
            ring[(s - 1, piece)].wait_recv()
        for n in range(slots):
            at = slice(n * rows, (n + 1) * rows)
            total = mine[piece, at, :]
            for o in team.sides:
                total = total + side_in[s - 1, o[1] - 1, piece, at, :].astype(jnp.float32)
            if s > 1:
                total = total + ring_in[s - 2, piece, at, :].astype(jnp.float32)
            if s < z:
                ring_out[s - 1, piece, at, :] = total.astype(low)
            else:
                d_kv_mine[piece * slots + n] = total.astype(low)
        if s < z:
            ring[(s, piece)] = push(ring_out.at[s - 1, piece], ring_in.at[s - 1, piece], along(0, 1))

    for s in range(1, z + 1):
        for piece in range(pieces):
            send_sides(s, piece)
            after = functools.partial(combine, s, piece) if s < z else lambda: None
            compute((z - s if s < z else 0, 0, 0, 0), piece, mine.at[piece], after)
    flush()
    for n in range(team.size):
        at = slice(n * rows, (n + 1) * rows)
        d_q_mine[n] = pack(d_q_sum[at, :HD] * SCORE_SCALE).astype(low)
    copies = [to_team(d_q_mine, d_q_out.at[my_slot], o) for o in team.others]
    own_q = pltpu.make_async_copy(d_q_mine.at[my_slot], d_q_out.at[my_slot], own_sem.at[1])
    own_q.start()
    for piece in range(pieces):
        combine(z, piece)
    copies += [to_team(d_kv_mine, d_kv_out.at[my_slot], o) for o in team.others]
    own_kv = pltpu.make_async_copy(d_kv_mine.at[my_slot], d_kv_out.at[my_slot], own_sem.at[2])
    own_kv.start()
    own_q.wait()
    own_kv.wait()
    for copy in copies:
        copy.wait_recv()
    push.finish()


def attend_back(dims, lengths, q, kv, dout, out_t, lse, collective_id):
    team = Team(dims)
    z = dims[0]
    rows = kv.shape[2]
    amount = team.size * rows
    pieces, key_step = 2, 256
    piece = (pieces, amount // pieces, LANES)
    count = 3 * (team.size - 1) + pieces * (z + z * len(team.sides))
    others = max(len(team.sides), 1)
    ring_steps, side_steps = max(z - 1, 1), z if team.sides else 1
    return pl.pallas_call(
        functools.partial(attend_back_kernel, team, key_step, 512, pieces),
        out_shape=(
            jax.ShapeDtypeStruct(q.shape, low),
            jax.ShapeDtypeStruct(kv.shape[1:], low),
        ),
        in_specs=[SMEM_SPEC] + [VMEM_SPEC] * 5,
        out_specs=[VMEM_SPEC] * 2,
        scratch_shapes=[
            pltpu.VMEM(q.shape, low),
            pltpu.VMEM((LANES, amount // pieces), low),
            pltpu.VMEM((LANES, amount // pieces), low),
            pltpu.VMEM((amount // pieces, LANES), low),
            pltpu.VMEM((LANES, amount // pieces), low),
            pltpu.VMEM((LANES, amount // pieces), low),
            pltpu.VMEM((amount // pieces, LANES), low),
            pltpu.VMEM((amount, LANES), low),
            pltpu.VMEM((amount, LANES), low),
            pltpu.VMEM((amount, LANES), jnp.float32),
            pltpu.VMEM((HD, amount), low),
            pltpu.VMEM((HD, amount), low),
            pltpu.VMEM((amount, key_step), low),
            pltpu.VMEM((amount, key_step), low),
            pltpu.VMEM((amount, key_step), low),
            pltpu.VMEM((amount, key_step), low),
            pltpu.VMEM((side_steps, others) + piece, low),
            pltpu.VMEM((side_steps, others) + piece, low),
            pltpu.VMEM((ring_steps,) + piece, low),
            pltpu.VMEM((ring_steps,) + piece, low),
            pltpu.VMEM(piece, jnp.float32),
            pltpu.VMEM(q.shape, low),
            pltpu.VMEM(kv.shape[1:], low),
            pltpu.SemaphoreType.DMA((count,)),
            pltpu.SemaphoreType.DMA((count,)),
            pltpu.SemaphoreType.DMA((3,)),
        ],
        compiler_params=pltpu.CompilerParams(
            collective_id=collective_id, has_side_effects=True, vmem_limit_bytes=60 * MIB
        ),
        name="attend_back",
    )(lengths, q, kv, dout, out_t, lse)


def part_shapes(n_head):
    width = HEADS // n_head * HD
    hidden = FF // n_head
    return (
        (D, width, True),
        (DI, 2 * width, True),
        (width, D, False),
        (D, 3 * width, True),
        (width, D, False),
        (D, hidden, True),
        (hidden, D, False),
        (D, C // n_head, True),
    )


def borders(n_head):
    result = [0]
    for rows, columns, joined in part_shapes(n_head):
        result.append(result[-1] + rows * columns // LANES)
    return result


def period(columns):
    amount = 1
    while amount * columns % LANES:
        amount *= 2
    return amount


def segments(start, amount, unit):
    result = []
    while amount > 0:
        which, at = divmod(start, unit)
        size = min(unit - at, amount)
        result.append((which, at, at + size))
        start, amount = start + size, amount - size
    return result


def joined_lanes(pieces):
    return pieces[0] if len(pieces) == 1 else jnp.concatenate(pieces, 1)


def lane_blocks(value):
    rows, columns = value.shape
    missing = -columns % LANES
    if missing:
        value = jnp.concatenate([value, jnp.zeros((rows, missing), value.dtype)], 1)
    return [value[:, i : i + LANES] for i in range(0, columns + missing, LANES)]


def every(first, amount, stride):
    return pl.ds(first, amount) if stride == 1 else pl.ds(first, amount, stride=stride)


def matrix_of(stage, first, rows, columns, line):
    if columns % LANES == 0:
        stride = columns // LANES
        for j in range(stride):
            yield j * LANES, stage[every(first + j, rows, stride), :]
        return
    height = period(columns)
    stride = height * columns // LANES
    for k in range(height):
        pieces = [
            stage[every(first + which, rows // height, stride), :][:, begin:end]
            for which, begin, end in segments(k * columns, columns, LANES)
        ]
        for i, piece in enumerate(lane_blocks(joined_lanes(pieces))):
            line[i, every(k, rows // height, height), :] = piece
    for i in range(-(-columns // LANES)):
        yield i * LANES, line[i, :rows, : min(columns - i * LANES, LANES)]


def matrix_into(stage, first, value, line):
    rows, columns = value.shape
    if columns % LANES == 0:
        stride = columns // LANES
        for j in range(stride):
            stage[every(first + j, rows, stride), :] = value[:, j * LANES : (j + 1) * LANES]
        return
    height = period(columns)
    stride = height * columns // LANES
    for i, piece in enumerate(lane_blocks(value)):
        line[i, :rows, :] = piece
    for i in range(stride):
        pieces = [
            line[which, every(k, rows // height, height), :][:, begin:end]
            for k, first_lane, last_lane in segments(i * LANES, LANES, columns)
            for which, begin, end in segments(first_lane, last_lane - first_lane, LANES)
        ]
        stage[every(first + i, rows // height, stride), :] = joined_lanes(pieces)


def load_stage(stage, held, first_shard, shard_rows, group):
    for b in range(held.shape[0]):
        stage[pl.ds(b * shard_rows, shard_rows), :] = held[b, group, :shard_rows, :].astype(jnp.float32)


def load_common(stage, held, valid):
    piece = held.shape[2]
    for b in range(held.shape[0]):
        for k in range(held.shape[1]):
            amount = min(piece, valid - k * piece)
            stage[b * valid + k * piece : b * valid + k * piece + amount, :] = held[b, k].astype(
                jnp.float32
            )[:amount]


def common_blocks(first_row, last_row, valid):
    return first_row // valid, -(-last_row // valid) - first_row // valid


def load_matrices(stage, first_row, n_head, group, which, targets, line):
    starts, shapes = borders(n_head), part_shapes(n_head)
    for m, target in zip(which, targets):
        rows, columns, joined = shapes[m]
        row = 0 if joined else group * rows
        column = group * columns if joined else 0
        for j, value in matrix_of(stage, starts[m] - first_row, rows, columns, line):
            size = value.shape[1]
            target[row : row + rows, column + j : column + j + size] = value.astype(target.dtype)


def normalized(x):
    centre = x - jnp.mean(x, -1, keepdims=True)
    rate = lax.rsqrt(jnp.mean(centre * centre, -1, keepdims=True) + norm_eps)
    return centre * rate, rate


def layer_norm(x, gain):
    return normalized(x)[0] * gain


def norm_pullback(x, gain, grad):
    unit, rate = normalized(x)
    inside = grad * gain
    both = jnp.mean(inside * unit, -1, keepdims=True)
    d_x = rate * (inside - jnp.mean(inside, -1, keepdims=True) - unit * both)
    return d_x, jnp.sum(grad * unit, 0, keepdims=True)


def head_lanes(group, heads, value):
    width = heads * HD
    block = value[:, group * width : (group + 1) * width]
    lane = lax.broadcasted_iota(jnp.int32, (1, width), 1)
    result = []
    for a in range(heads):
        here = (lane >= a * HD) & (lane < (a + 1) * HD)
        result.append((here, jnp.where(here, block, jnp.zeros_like(block))))
    return result


def place_of(bounds, first, amount):
    row = first + lax.broadcasted_iota(jnp.int32, (amount, 1), 0)
    opening = jnp.zeros((amount, 1), jnp.int32)
    for begin, end in bounds:
        opening = jnp.where((row >= begin) & (row < end), begin, opening)
    offset = row - opening
    turns = jnp.floor((offset.astype(jnp.float32) + 0.5) * (1.0 / LAT)).astype(jnp.int32)
    return offset - turns * LAT


def picked_rows(bounds, rows, n_head):
    first = lax.axis_index("blk") * (rows * n_head) + lax.axis_index("head") * rows
    lane = lax.broadcasted_iota(jnp.int32, (rows, LAT), 1)
    return jnp.where(lane == place_of(bounds, first, rows), 1.0, 0.0).astype(low)


def enc_scores(q_head, keys):
    return against(q_head, keys) * (SCORE_SCALE * LOG2E)


def encode_kernel(
    n_head,
    shard_rows,
    valid,
    rows,
    lengths,
    weights,
    common,
    inputs_t,
    enc_query,
    enc_keyval,
    enc_output,
    self_project,
    gains,
    z_zero,
    h_zero,
    x_norm_t,
    q_enc,
    kv_enc,
    o_enc,
    z_one,
    h_one,
    q_self,
    kv_self,
    counts,
    label_counts,
    held,
    held_common,
    held_counts,
    stage,
    stage_common,
    line,
    latent_table,
    sems,
):
    heads = HEADS // n_head
    width = heads * HD
    shards = held.shape[0]
    bounds = clip_bounds(lengths)
    first = DQ * D // LANES
    block, blocks = common_blocks(first, first + (LAT + 4) * D // LANES, valid)
    tail = shard_rows // TILE * TILE
    copies = [
        pltpu.make_async_copy(common.at[pl.ds(block, blocks)], held_common, sems.at[0]),
        pltpu.make_async_copy(weights.at[pl.ds(0, shards)], held, sems.at[1]),
        pltpu.make_async_copy(weights.at[:, :, pl.ds(tail, TILE)], held_counts, sems.at[2]),
    ]
    for copy in copies:
        copy.start()
    centre = inputs_t[...].astype(jnp.float32)
    centre = centre - jnp.mean(centre, 0, keepdims=True)
    rate = lax.rsqrt(jnp.mean(centre * centre, 0, keepdims=True) + norm_eps)
    x_norm_t[...] = (centre * rate).astype(low)
    copies[0].wait()
    load_common(stage_common, held_common, valid)
    first = first - block * valid
    for j, value in matrix_of(stage_common, first, LAT, D, line):
        latent_table[:, j : j + LANES] = value.astype(low)
    for j, value in matrix_of(stage_common, first + LAT * D // LANES, 4, D, line):
        gains[:, j : j + LANES] = value
    picked = picked_rows(bounds, rows, n_head)
    z_zero[...] = product(picked, latent_table[...])
    h_zero[...] = layer_norm(z_zero[...], gains[0:1, :]).astype(low)
    copies[2].wait()
    counted = held_counts[...].astype(jnp.float32)[:, :, shard_rows - tail : shard_rows - tail + 1]
    counts[...] = jnp.broadcast_to(jnp.sum(counted, (0, 1)), counts.shape)
    label_counts[...] = counts[:1, :MODES]
    copies[1].wait()
    for g in range(n_head):
        load_stage(stage, held, 0, shard_rows, g)
        load_matrices(
            stage, 0, n_head, g, (0, 1, 2, 3), (enc_query, enc_keyval, enc_output, self_project), line
        )
    q_enc[...] = product(h_zero[...], enc_query[...]).astype(low)
    kv_enc[...] = contract_first(x_norm_t[...], enc_keyval[...]).astype(low)
    for g in range(n_head):
        keys = kv_enc[:, 2 * g * width : (2 * g + 1) * width]
        values = kv_enc[:, (2 * g + 1) * width : (2 * g + 2) * width]
        outcome = jnp.zeros((rows, width), jnp.float32)
        for here, q_head in head_lanes(g, heads, q_enc[...]):
            scores = enc_scores(q_head, keys)
            probs = jnp.exp2((scores - jnp.max(scores, 1, keepdims=True)).astype(low))
            total = jnp.sum(probs.astype(jnp.float32), 1, keepdims=True)
            outcome = jnp.where(here, product(probs, values) / total, outcome)
        o_enc[:, g * width : (g + 1) * width] = outcome.astype(low)
    z_one[...] = z_zero[...] + product(o_enc[...], enc_output[...])
    h_one[...] = layer_norm(z_one[...], gains[1:2, :]).astype(low)
    projected = product(h_one[...], self_project[...]).astype(low)
    for slot, (g, a) in enumerate(heads_of(n_head, q_self.shape[0])):
        query, key, value = (
            projected[:, (3 * g + i) * width + a * HD : (3 * g + i) * width + (a + 1) * HD]
            for i in range(3)
        )
        q_self[slot] = pack(query)
        kv_self[slot] = jnp.concatenate([key, value], 1)


LINE = pltpu.VMEM((4, round_up(max(D, DI), 8), LANES), jnp.float32)


def shards_of(n_head, shard_rows, first, last):
    starts = borders(n_head)
    begin = starts[first] // shard_rows
    return begin, -(-starts[last] // shard_rows) - begin


def encode(lengths, weights, common, inputs_t, valid, rows, slots, n_head, shard_rows):
    begin, shards = shards_of(n_head, shard_rows, 0, 4)
    query_rows = DQ * D // LANES
    block, blocks = common_blocks(query_rows, query_rows + (LAT + 4) * D // LANES, valid)
    keys = inputs_t.shape[1]
    return pl.pallas_call(
        functools.partial(encode_kernel, n_head, shard_rows, valid, rows),
        out_shape=[
            shape_of((D, D)),
            shape_of((DI, 2 * D)),
            shape_of((D, D)),
            shape_of((D, 3 * D)),
            shape_of((4, D), jnp.float32),
            shape_of((rows, D), jnp.float32),
            shape_of((rows, D)),
            shape_of(inputs_t.shape),
            shape_of((rows, D)),
            shape_of((keys, 2 * D)),
            shape_of((rows, D)),
            shape_of((rows, D), jnp.float32),
            shape_of((rows, D)),
            shape_of((slots, rows // 2, LANES)),
            shape_of((slots, rows, LANES)),
            shape_of((8, LANES), jnp.float32),
            shape_of((1, MODES), jnp.float32),
        ],
        in_specs=[SMEM_SPEC, ANY_SPEC, ANY_SPEC, VMEM_SPEC],
        out_specs=[VMEM_SPEC] * 17,
        scratch_shapes=[
            pltpu.VMEM((shards,) + weights.shape[1:], low),
            pltpu.VMEM((blocks,) + common.shape[1:], low),
            pltpu.VMEM(weights.shape[:2] + (TILE, LANES), low),
            pltpu.VMEM((shards * shard_rows, LANES), jnp.float32),
            pltpu.VMEM((blocks * valid, LANES), jnp.float32),
            LINE,
            pltpu.VMEM((LAT, D), low),
            pltpu.SemaphoreType.DMA((3,)),
        ],
        compiler_params=pltpu.CompilerParams(vmem_limit_bytes=56 * MIB),
        name="encode",
    )(lengths, weights, common, inputs_t)


def gelu_and_slope(x):
    rate = (2.0 / jnp.pi) ** 0.5
    cubic = 0.044715
    t = jnp.tanh(rate * (x + cubic * x * x * x))
    slope = 0.5 * (1.0 + t) + 0.5 * x * (1.0 - t * t) * rate * (1.0 + 3.0 * cubic * x * x)
    return 0.5 * x * (1.0 + t), slope


def my_column(marks, rows):
    turned = marks[...].astype(jnp.float32).T
    column = lax.broadcasted_iota(jnp.int32, turned.shape, 1)
    per_head = rows // LANES
    first = lax.axis_index("head") * per_head
    picked = [
        jnp.sum(jnp.where(column == first + k, turned, 0.0), 1, keepdims=True)
        for k in range(per_head)
    ]
    return jnp.concatenate(picked, 0) if per_head > 1 else picked[0]


def middle_kernel(
    n_head,
    shard_rows,
    valid,
    first_shard,
    rows,
    counts,
    weights,
    common,
    z_one,
    o_self,
    out_queries_t,
    labels,
    modality,
    labeled,
    gains,
    dout,
    d_two_out,
    tile,
    query_grad,
    gain_grads,
    grads,
    held,
    held_common,
    stage,
    stage_common,
    line,
    self_output,
    hidden_in,
    hidden_out,
    class_table,
    query_table,
    slope,
    activ,
    sems,
):
    heads = HEADS // n_head
    width, hidden, classes = heads * HD, FF // n_head, C // n_head
    shards = held.shape[0]
    first_row = first_shard * shard_rows
    starts = borders(n_head)
    copies = [
        pltpu.make_async_copy(common.at[pl.ds(0, held_common.shape[0])], held_common, sems.at[0]),
        pltpu.make_async_copy(weights.at[pl.ds(first_shard, shards)], held, sems.at[1]),
    ]
    for copy in copies:
        copy.start()
    copies[0].wait()
    load_common(stage_common, held_common, valid)
    for j, value in matrix_of(stage_common, 0, DQ, D, line):
        query_table[:, j : j + LANES] = value.astype(low)
    copies[1].wait()
    for g in range(n_head):
        load_stage(stage, held, first_shard, shard_rows, g)
        load_matrices(
            stage, first_row, n_head, g, (4, 5, 6, 7), (self_output, hidden_in, hidden_out, class_table), line
        )
    gain_two, gain_three = gains[2:3, :], gains[3:4, :]
    o_heads = {head: unpack(o_self[s]) for s, head in enumerate(heads_of(n_head, o_self.shape[0]))}
    o_groups = [joined_lanes([o_heads[(g, a)] for a in range(heads)]) for g in range(n_head)]
    o_low = jnp.concatenate(o_groups, 1)
    z_two = z_one[...] + product(o_low, self_output[...])
    h_two = layer_norm(z_two, gain_two).astype(low)
    value, bend = gelu_and_slope(product(h_two, hidden_in[...]))
    activ[...] = value.astype(low)
    slope[...] = bend
    z_three = z_two + product(activ[...], hidden_out[...])
    queries_t = out_queries_t[...]
    decoded = layer_norm(z_three, gain_three) + contract_first(queries_t, query_table[...])
    decoded = decoded.astype(low)
    logits = product(decoded, class_table[...])
    label, kind, counted = (my_column(marks, rows) for marks in (labels, modality, labeled))
    lane = lax.broadcasted_iota(jnp.int32, (rows, C), 1).astype(jnp.float32)
    is_target = jnp.where(lane == label, 1.0, 0.0)
    row_top = jnp.max(logits, 1, keepdims=True)
    row_lse = row_top + jnp.log(jnp.sum(jnp.exp2((logits - row_top) * LOG2E), 1, keepdims=True))
    loss = row_lse - jnp.sum(is_target * logits, 1, keepdims=True)
    weight = jnp.zeros((rows, 1), jnp.float32)
    place = lax.broadcasted_iota(jnp.int32, (1, LANES), 1)
    losses = jnp.zeros((1, LANES), jnp.float32)
    for m in range(MODES):
        member = jnp.where((kind == m) & (counted == 1.0), 1.0, 0.0)
        weight = weight + member / jnp.maximum(counts[0:1, m : m + 1], 1.0)
        losses = losses + jnp.where(place == m, jnp.sum(loss * member, 0, keepdims=True), 0.0)
    tile[...] = jnp.broadcast_to(losses, tile.shape)
    dlogits = (weight * (jnp.exp2((logits - row_lse) * LOG2E) - is_target)).astype(low)
    d_decoded = against(dlogits, class_table[...])
    matrix_into(query_grad, 0, product(queries_t, d_decoded.astype(low)), line)
    d_three, gain_three_grad = norm_pullback(z_three, gain_three, d_decoded)
    d_branch = d_three.astype(low)
    d_pre = (slope[...] * against(d_branch, hidden_out[...])).astype(low)
    d_middle, gain_two_grad = norm_pullback(z_two, gain_two, against(d_pre, hidden_in[...]))
    d_two = d_three + d_middle
    d_two_out[...] = d_two
    gain_grads[...] = jnp.concatenate([gain_two_grad, gain_three_grad], 0)
    d_two_low = d_two.astype(low)
    d_o = against(d_two_low, self_output[...]).astype(low)
    for slot, (g, a) in enumerate(heads_of(n_head, o_self.shape[0])):
        dout[slot] = pack(d_o[:, g * width + a * HD : g * width + (a + 1) * HD])
    for g in range(n_head):
        results = (
            contract_first(o_groups[g], d_two_low),
            contract_first(h_two, d_pre[:, g * hidden : (g + 1) * hidden]),
            contract_first(activ[:, g * hidden : (g + 1) * hidden], d_branch),
            contract_first(decoded, dlogits[:, g * classes : (g + 1) * classes]),
        )
        for m, result in zip((4, 5, 6, 7), results):
            matrix_into(stage, starts[m] - first_row, result, line)
        for b in range(shards):
            held[b, g, :shard_rows, :] = stage[pl.ds(b * shard_rows, shard_rows), :].astype(low)
    back = pltpu.make_async_copy(held, grads.at[pl.ds(first_shard, shards)], sems.at[2])
    back.start()
    back.wait()


def middle(counts, weights, common, z_one, o_self, out_queries_t, marks, gains, valid, n_head, shard_rows):
    rows = z_one.shape[0]
    begin, shards = shards_of(n_head, shard_rows, 4, 8)
    query_rows = DQ * D // LANES
    block, blocks = common_blocks(0, query_rows, valid)
    return pl.pallas_call(
        functools.partial(middle_kernel, n_head, shard_rows, valid, begin, rows),
        grid=(1,),
        out_shape=[
            shape_of(o_self.shape),
            shape_of((rows, D), jnp.float32),
            shape_of((8, LANES), jnp.float32),
            shape_of((query_rows, LANES), jnp.float32),
            shape_of((2, D), jnp.float32),
            shape_of(weights.shape),
        ],
        in_specs=[
            VMEM_SPEC,
            ANY_SPEC,
            ANY_SPEC,
            VMEM_SPEC,
            VMEM_SPEC,
            pl.BlockSpec((DQ, rows), lambda i: (0, lax.axis_index("head"))),
            VMEM_SPEC,
            VMEM_SPEC,
            VMEM_SPEC,
            VMEM_SPEC,
        ],
        out_specs=[VMEM_SPEC] * 5 + [ANY_SPEC],
        scratch_shapes=[
            pltpu.VMEM((shards,) + weights.shape[1:], low),
            pltpu.VMEM((blocks,) + common.shape[1:], low),
            pltpu.VMEM((shards * shard_rows, LANES), jnp.float32),
            pltpu.VMEM((blocks * valid, LANES), jnp.float32),
            LINE,
            pltpu.VMEM((D, D), low),
            pltpu.VMEM((D, FF), low),
            pltpu.VMEM((FF, D), low),
            pltpu.VMEM((D, C), low),
            pltpu.VMEM((DQ, D), low),
            pltpu.VMEM((rows, FF), jnp.float32),
            pltpu.VMEM((rows, FF), low),
            pltpu.SemaphoreType.DMA((3,)),
        ],
        compiler_params=pltpu.CompilerParams(vmem_limit_bytes=56 * MIB),
        name="middle",
    )(counts, weights, common, z_one, o_self, out_queries_t, *marks, gains)


def ending_kernel(
    n_head,
    shard_rows,
    valid,
    rows,
    lengths,
    grads_in,
    d_q_self,
    d_kv_self,
    d_two,
    gains,
    gain_grads,
    query_grad,
    enc_query,
    enc_keyval,
    enc_output,
    self_project,
    z_zero,
    h_zero,
    x_norm_t,
    q_enc,
    kv_enc,
    o_enc,
    z_one,
    h_one,
    grads,
    common_grad,
    held,
    stage,
    stage_common,
    line,
    d_q,
    d_kv,
    sems,
):
    heads = HEADS // n_head
    width = heads * HD
    shards = held.shape[0]
    starts = borders(n_head)
    shared = pltpu.make_async_copy(grads_in.at[pl.ds(shards - 1, 1)], held.at[pl.ds(shards - 1, 1)], sems.at[0])
    shared.start()
    d_heads = {}
    for slot, head in enumerate(heads_of(n_head, d_kv_self.shape[0])):
        d_kv_head = d_kv_self[slot]
        d_heads[head] = (unpack(d_q_self[slot]), d_kv_head[:, :HD], d_kv_head[:, HD:])
    d_projected = [
        jnp.concatenate([d_heads[(g, a)][i] for i in range(3) for a in range(heads)], 1)
        for g in range(n_head)
    ]
    whole = jnp.concatenate(d_projected, 1)
    d_middle, gain_one_grad = norm_pullback(
        z_one[...], gains[1:2, :], against(whole, self_project[...])
    )
    d_one = d_two[...] + d_middle
    d_one_low = d_one.astype(low)
    d_o = against(d_one_low, enc_output[...]).astype(low)
    for g in range(n_head):
        keys = kv_enc[:, 2 * g * width : (2 * g + 1) * width]
        values = kv_enc[:, (2 * g + 1) * width : (2 * g + 2) * width]
        d_key = jnp.zeros(keys.shape, jnp.float32)
        d_value = jnp.zeros(keys.shape, jnp.float32)
        d_query = jnp.zeros((rows, width), jnp.float32)
        for (here, q_head), (unused, do_head) in zip(
            head_lanes(g, heads, q_enc[...]), head_lanes(g, heads, d_o)
        ):
            scores = enc_scores(keys, q_head)
            probs = jnp.exp2((scores - jnp.max(scores, 0, keepdims=True)).astype(low))
            probs = probs.astype(jnp.float32)
            probs = probs / jnp.sum(probs, 0, keepdims=True)
            d_probs = against(values, do_head)
            delta = jnp.sum(probs * d_probs, 0, keepdims=True)
            d_scores = (probs * (d_probs - delta)).astype(low)
            d_value = d_value + product(probs.astype(low), do_head)
            d_key = d_key + product(d_scores, q_head)
            d_query = jnp.where(here, contract_first(d_scores, keys), d_query)
        d_q[:, g * width : (g + 1) * width] = (d_query * SCORE_SCALE).astype(low)
        d_kv[:, 2 * g * width : (2 * g + 1) * width] = (d_key * SCORE_SCALE).astype(low)
        d_kv[:, (2 * g + 1) * width : (2 * g + 2) * width] = d_value.astype(low)
    d_middle, gain_zero_grad = norm_pullback(
        z_zero[...], gains[0:1, :], against(d_q[...], enc_query[...])
    )
    d_zero = d_one + d_middle
    d_zero_top = d_zero.astype(low)
    d_zero_rest = (d_zero - d_zero_top.astype(jnp.float32)).astype(low)
    picked = picked_rows(clip_bounds(lengths), rows, n_head)
    latent_grad = contract_first(picked, d_zero_top) + contract_first(picked, d_zero_rest)
    query_rows = query_grad.shape[0]
    stage_common[:query_rows] = query_grad[...]
    matrix_into(stage_common, query_rows, latent_grad, line)
    all_gains = jnp.concatenate([gain_zero_grad, gain_one_grad, gain_grads[...]], 0)
    matrix_into(stage_common, query_rows + LAT * D // LANES, all_gains, line)
    piece = common_grad.shape[2]
    for b in range(common_grad.shape[0]):
        for k in range(common_grad.shape[1]):
            amount = min(piece, valid - k * piece)
            block = stage_common[b * valid + k * piece : b * valid + k * piece + amount, :]
            if amount < piece:
                block = jnp.concatenate([block, jnp.zeros((piece - amount, LANES), jnp.float32)], 0)
            common_grad[b, k] = block.astype(low)
    shared.wait()
    kept = shards * shard_rows - starts[4]
    for g in range(n_head):
        results = (
            contract_first(h_zero[...], d_q[:, g * width : (g + 1) * width]),
            product(x_norm_t[...], d_kv[:, 2 * g * width : (2 * g + 2) * width]),
            contract_first(o_enc[:, g * width : (g + 1) * width], d_one_low),
            contract_first(h_one[...], d_projected[g]),
        )
        if kept:
            stage[pl.ds((shards - 1) * shard_rows, shard_rows), :] = held[
                shards - 1, g, :shard_rows, :
            ].astype(jnp.float32)
        for m, result in zip((0, 1, 2, 3), results):
            matrix_into(stage, starts[m], result, line)
        for b in range(shards):
            held[b, g, :shard_rows, :] = stage[pl.ds(b * shard_rows, shard_rows), :].astype(low)
    back = pltpu.make_async_copy(held, grads.at[pl.ds(0, shards)], sems.at[1])
    back.start()
    back.wait()


def ending(lengths, grads, d_self, d_two, gains, gain_grads, query_grad, kept, common_shape, valid, shard_rows):
    rows = d_two.shape[0]
    n_head = grads.shape[1]
    begin, shards = shards_of(n_head, shard_rows, 0, 4)
    keys = kept[6].shape[1]
    common_rows = (DQ + LAT + 4) * D // LANES
    return pl.pallas_call(
        functools.partial(ending_kernel, n_head, shard_rows, valid, rows),
        out_shape=[shape_of(grads.shape), shape_of(common_shape)],
        in_specs=[SMEM_SPEC, ANY_SPEC] + [VMEM_SPEC] * 18,
        out_specs=[ANY_SPEC, VMEM_SPEC],
        input_output_aliases={1: 0},
        scratch_shapes=[
            pltpu.VMEM((shards,) + grads.shape[1:], low),
            pltpu.VMEM((shards * shard_rows, LANES), jnp.float32),
            pltpu.VMEM((common_rows, LANES), jnp.float32),
            LINE,
            pltpu.VMEM((rows, D), low),
            pltpu.VMEM((keys, 2 * D), low),
            pltpu.SemaphoreType.DMA((2,)),
        ],
        compiler_params=pltpu.CompilerParams(vmem_limit_bytes=56 * MIB),
        name="ending",
    )(lengths, grads, *d_self, d_two, gains, gain_grads, query_grad, *kept)


def adam_step(weight, first, second, grad):
    first = beta_one * first + (1 - beta_one) * grad
    second = beta_two * second + (1 - beta_two) * grad * grad
    fixed_first = first / (1 - beta_one**STEP)
    fixed_second = second / (1 - beta_two**STEP)
    weight = weight - learn_rate * (
        fixed_first / (jnp.sqrt(fixed_second) + adam_eps) + weight_decay * weight
    )
    return (weight, first, second, weight.astype(low))


def per_device(
    inputs,
    out_queries,
    clip_lengths,
    labels,
    modality,
    labeled,
    head_params,
    head_first,
    head_second,
    common_params,
    common_first,
    common_second,
):
    n_head, n_blk = lax.axis_size("head"), lax.axis_size("blk")
    dims = grid_of(n_blk, n_head)
    rows = labels.shape[0] // n_head
    n_h, n_c = head_params.shape[0], common_params.shape[0]
    shard_rows, common_rows = n_h // LANES, -(-n_c // LANES)
    head_rows = round_up(shard_rows + 1, TILE)
    piece_rows = round_up(-(-common_rows // n_head), TILE)
    marks = [x.reshape(-1, LANES) for x in (labels, modality, labeled)]
    head_wide = head_params.reshape(shard_rows, LANES)
    common_wide = jnp.pad(common_params, (0, common_rows * LANES - n_c)).reshape(common_rows, LANES)
    weights, common = gather_all(dims, marks, (head_wide, common_wide), (head_rows, piece_rows), 0)
    valid = common_rows
    if n_c % LANES:
        common = common.reshape(n_blk, -1)[:, :n_c].reshape(-1, LANES)
        valid = common.shape[0]
        common = jnp.pad(common, ((0, -valid % TILE), (0, 0)))[None, None]

    encoded = encode(
        clip_lengths, weights, common, inputs.T, valid, rows, Team(dims).size, n_head, shard_rows
    )
    gains, z_one, counts = encoded[4], encoded[11], encoded[15]
    o_self, lse_self, out_self_t, q_all, kv_all = attend(
        dims, clip_lengths, encoded[13], encoded[14], 1
    )
    dout, d_two, tile, query_grad, gain_grads, grads = middle(
        counts, weights, common, z_one, o_self, out_queries.T, marks, gains, valid, n_head, shard_rows
    )
    d_self = attend_back(dims, clip_lengths, q_all, kv_all, dout, out_self_t, lse_self, 2)
    kept = encoded[:4] + encoded[5:13]
    grads, common_grad = ending(
        clip_lengths,
        grads,
        d_self,
        d_two,
        gains,
        gain_grads,
        query_grad,
        kept,
        common.shape,
        valid,
        shard_rows,
    )
    if n_c % LANES:
        common_grad = common_grad[0, 0, :valid].reshape(n_blk, n_c)
        common_grad = jnp.pad(common_grad, ((0, 0), (0, n_head * piece_rows * LANES - n_c)))
        common_grad = common_grad.reshape(n_blk, n_head, piece_rows, LANES)
    head_share, common_share, loss_sums, clip_norm, factor = reduce_all(
        dims, (grads, common_grad), (shard_rows, common_rows), tile, 3
    )
    label_counts, loss_sums = encoded[16].reshape(MODES), loss_sums.reshape(MODES)
    clip_norm, factor = clip_norm.reshape(()), factor.reshape(())
    head_share, common_share = head_share.reshape(-1), common_share.reshape(-1)[:n_c]
    head_out = adam_step(head_params, head_first, head_second, head_share * factor)
    common_out = adam_step(common_params, common_first, common_second, common_share * factor)
    return head_out + common_out + (loss_sums, label_counts, clip_norm)


def solution(mesh):
    placed = (
        P("blk", None),
        P("blk", None),
        P(),
        P("blk"),
        P("blk"),
        P("blk"),
        P(("head", "blk")),
        P(("head", "blk")),
        P(("head", "blk")),
        P("blk"),
        P("blk"),
        P("blk"),
    )
    return jax.shard_map(
        per_device,
        mesh=mesh,
        in_specs=placed,
        out_specs=(
            P(("head", "blk")),
            P(("head", "blk")),
            P(("head", "blk")),
            P(("head", "blk")),
            P("blk"),
            P("blk"),
            P("blk"),
            P("blk"),
            P(),
            P(),
            P(),
        ),
        check_vma=False,
    )
```

```python
import functools

import jax
import jax.numpy as jnp
from jax import lax
from jax.experimental import pallas as pl
from jax.experimental.pallas import tpu as pltpu
from jax.sharding import PartitionSpec as P

D = 512
HEADS = 8
HD = 64
FF = 2048
DI = 704
DQ = 1026
C = 704
LAT = 784
MODES = 3
STEP = 10
LANES = 128
TILE = 16

norm_eps = 1e-05
learn_rate = 0.1
beta_one = 0.9
beta_two = 0.999
adam_eps = 1e-08
weight_decay = 0.01
clip_limit = 0.05
big_negative = -1e30
low = jnp.bfloat16
LOG2E = 1.4426950408889634
SCORE_SCALE = HD ** (-0.5)
MESH = pl.DeviceIdType.MESH
MIB = 1 << 20
VMEM_SPEC = pl.BlockSpec(memory_space=pltpu.VMEM)
SMEM_SPEC = pl.BlockSpec(memory_space=pltpu.SMEM)
ANY_SPEC = pl.BlockSpec(memory_space=pl.ANY)


def shape_of(shape, dtype=low):
    return jax.ShapeDtypeStruct(shape, dtype)


def round_up(n, unit):
    return -(-n // unit) * unit


def grid_of(n_blk, n_head):
    cores = 2 if n_head % 2 == 0 else 1
    x = n_head // cores
    y = x if n_blk % x == 0 else 1
    return (n_blk // y, y, x, cores)


def my_place(dims):
    blk, head = lax.axis_index("blk"), lax.axis_index("head")
    return (blk // dims[1], lax.rem(blk, dims[1]), head // dims[3], lax.rem(head, dims[3]))


def shifted(dims, me, offset, sign):
    return tuple(
        m if o == 0 else lax.rem(m + (o if sign > 0 else n - o), n)
        for m, o, n in zip(me, offset, dims)
    )


def blk_of(dims, place):
    return place[0] * dims[1] + place[1]


def head_of(dims, place):
    return place[2] * dims[3] + place[3]


def device_of(dims, place):
    return {"blk": blk_of(dims, place), "head": head_of(dims, place)}


def along(axis, d):
    return tuple(d if a == axis else 0 for a in range(4))


def greet(dims, me, offsets):
    barrier = pltpu.get_barrier_semaphore()
    for offset in offsets:
        pl.semaphore_signal(
            barrier,
            inc=1,
            device_id=device_of(dims, shifted(dims, me, offset, 1)),
            device_id_type=MESH,
        )
    pl.semaphore_wait(barrier, len(offsets))


def axis_peers(dims, axes):
    return [along(axis, d) for axis in axes for d in range(1, dims[axis])]


def remote(src, dst, send_sem, recv_sem, place, dims):
    return pltpu.make_async_remote_copy(
        src_ref=src,
        dst_ref=dst,
        send_sem=send_sem,
        recv_sem=recv_sem,
        device_id=device_of(dims, place),
        device_id_type=MESH,
    )


AHEAD = 6.0
RING = 0


def in_order(first, follow, size_of, ahead, result):
    queues, busy, flight = {}, {}, {}
    now = 0.0

    def ready(messages):
        for message in messages:
            queues.setdefault(message[1], []).append(message)

    ready(first)
    while True:
        for axis in sorted(queues):
            queue, going = queues[axis], flight.setdefault(axis, [])
            while queue and (not going or busy[axis] < now + ahead):
                message = min(queue)
                queue.remove(message)
                busy[axis] = max(now, busy.get(axis, 0.0)) + size_of(message)
                going.append((busy[axis] + 1.5, message))
                result.append((True, message))
        arrivals = [min(going) for going in flight.values() if going]
        if not arrivals:
            return now
        arrival = min(arrivals)
        flight[arrival[1][1]].remove(arrival)
        now = max(now, arrival[0])
        result.append((False, arrival[1]))
        ready(follow(arrival[1]))


def time_of(rows, axis):
    return rows * LANES * 2 / (300e3 if axis == 3 else 45e3)


def with_at(offset, axis, d):
    return offset[:axis] + (d,) + offset[axis + 1 :]


def gather_order(dims, parts):
    def onward(p, offset, position):
        order = parts[p][3]
        result = []
        for k in range(max(position, 0), 4):
            axis = order[k]
            n = dims[axis]
            if k > position:
                steps = [1] if axis == RING else range(1, n)
                steps = [d for d in steps if d < n]
            else:
                steps = [offset[axis] + 1] if axis == RING and offset[axis] + 1 < n else []
            for d in steps:
                result.append(((k, sum(offset), p), axis, p, with_at(offset, axis, d)))
        return result

    def follow(message):
        rank, axis, p, offset = message
        return onward(p, offset, rank[0])

    first = [m for p in range(len(parts)) for m in onward(p, (0, 0, 0, 0), -1)]
    result = []
    now = in_order(first, follow, lambda m: time_of(parts[m[2]][2], m[1]), AHEAD, result)
    return result, now


def gather_kernel(
    dims,
    parts,
    labels,
    modality,
    labeled,
    head_params,
    common_params,
    head_all,
    common_all,
    head_low,
    common_low,
    common_wide,
    send_sem,
    recv_sem,
    own_sem,
):
    me = my_place(dims)
    my_head = head_of(dims, me)
    n_head = dims[2] * dims[3]
    shard_rows, common_rows = head_params.shape[0], common_params.shape[0]
    per_head = labels.shape[0] // n_head
    row = lax.broadcasted_iota(jnp.int32, labels.shape, 0)
    mine = (row >= my_head * per_head) & (row < (my_head + 1) * per_head) & (labeled[...] == 1)
    lane = lax.broadcasted_iota(jnp.int32, (1, LANES), 1)
    counts = jnp.zeros((1, LANES), jnp.float32)
    for m in range(MODES):
        member = jnp.where(mine & (modality[...] == m), 1.0, 0.0)
        counts = counts + jnp.where(lane == m, jnp.sum(member, (0, 1), keepdims=True), 0.0)
    padding = head_low.shape[0] - shard_rows
    tail = shard_rows // TILE * TILE
    head_low[:tail] = head_params[:tail].astype(low)
    last = [jnp.broadcast_to(counts, (padding, LANES))]
    if shard_rows > tail:
        last = [head_params[tail:]] + last
    head_low[tail:] = jnp.concatenate(last, 0).astype(low)
    common_wide[...] = jnp.zeros(common_wide.shape, jnp.float32)
    common_wide[:common_rows] = common_params[...]
    piece = common_low.shape[0]
    common_low[...] = common_wide[pl.ds(pl.multiple_of(my_head * piece, TILE), piece)].astype(low)

    greet(dims, me, ring_and_others(dims))
    srcs, outs = (head_low, common_low), (head_all, common_all)
    copies = {}

    def block(p, offset):
        place = shifted(dims, me, offset, -1)
        array, first, rows, order = parts[p]
        return outs[array].at[blk_of(dims, place), head_of(dims, place), pl.ds(first, rows)]

    own = []
    for is_send, (rank, axis, p, offset) in gather_order(dims, parts)[0]:
        if is_send:
            step = 1 if axis == RING else offset[axis]
            before = with_at(offset, axis, offset[axis] - step)
            array, first, rows, order = parts[p]
            source = block(p, before) if any(before) else srcs[array].at[pl.ds(first, rows)]
            i = len(copies)
            copies[(p, offset)] = remote(
                source,
                block(p, before),
                send_sem.at[i],
                recv_sem.at[i],
                shifted(dims, me, along(axis, step), 1),
                dims,
            )
            copies[(p, offset)].start()
        else:
            if not own:
                for array in range(2):
                    copy = pltpu.make_async_copy(
                        srcs[array], outs[array].at[blk_of(dims, me), my_head], own_sem.at[array]
                    )
                    copy.start()
                    own.append(copy)
            copies[(p, offset)].wait_recv()
    for copy in copies.values():
        copy.wait_send()
    for copy in own:
        copy.wait()


def ring_and_others(dims):
    ring = {along(RING, 1 % dims[RING]), along(RING, (dims[RING] - 1) % dims[RING])}
    return sorted(ring - {(0, 0, 0, 0)}) + axis_peers(dims, (1, 2, 3))


def cut(array, rows, shares):
    result = []
    first, so_far = 0, 0
    whole = sum(share for share, order in shares)
    for share, order in shares:
        so_far += share
        end = rows * so_far // whole // TILE * TILE if so_far < whole else rows
        if end > first:
            result.append((array, first, end - first, order))
        first = end
    return tuple(result)


ZYXC, ZXYC, YXZC, XYZC = (0, 1, 2, 3), (0, 2, 1, 3), (1, 2, 0, 3), (2, 1, 0, 3)
GATHER_SHARES = ((8, ZYXC), (6, ZXYC), (2, YXZC), (2, XYZC))
REDUCE_SHARES = ((7, ZYXC), (7, ZXYC), (2, YXZC), (2, XYZC))


def gather_all(dims, marks, params, rows, collective_id):
    z, y, x, cores = dims
    parts = cut(0, rows[0], GATHER_SHARES) + cut(1, rows[1], ((1, ZXYC),))
    count = len(parts) * (z * y * x * cores - 1)
    return pl.pallas_call(
        functools.partial(gather_kernel, dims, parts),
        out_shape=[shape_of((z * y, x * cores, n, LANES)) for n in rows],
        in_specs=[VMEM_SPEC] * 5,
        out_specs=[ANY_SPEC] * 2,
        scratch_shapes=[pltpu.VMEM((n, LANES), low) for n in rows]
        + [
            pltpu.VMEM((x * cores * rows[1], LANES), jnp.float32),
            pltpu.SemaphoreType.DMA((count,)),
            pltpu.SemaphoreType.DMA((count,)),
            pltpu.SemaphoreType.DMA((2,)),
        ],
        compiler_params=pltpu.CompilerParams(collective_id=collective_id, has_side_effects=True),
        name="gather_weights",
    )(*marks, *params)


def reduce_order(dims, parts):
    ready, arrived, order = set(), set(), []

    def message(p, position, offset):
        z = offset[RING]
        rank = (dims[RING] - z if z else dims[RING], position, tuple(-o for o in offset), p)
        return (rank, parts[p][3][position], p, position, offset)

    def done(p, position, offset):
        ready.add((p, position, offset))
        if position == 4:
            return []
        axis = parts[p][3][position]
        d = offset[axis]
        first = d != 0 and (axis != RING or d == dims[axis] - 1)
        return ([message(p, position, offset)] if first else []) + advance(p, position, offset)

    def advance(p, position, offset):
        axis = parts[p][3][position]
        n = dims[axis]
        start = with_at(offset, axis, 0)
        if axis == RING:
            here = (p, position, offset)
            if here in ready and here in arrived:
                order.append((None, here))
                if offset[axis]:
                    return [message(p, position, offset)]
                return done(p, position + 1, offset)
        elif (p, position, start) in ready and (p, position + 1, start) not in ready:
            if all((p, position, with_at(start, axis, d)) in arrived for d in range(1, n)):
                order.append((None, (p, position, start)))
                return done(p, position + 1, start)
        return []

    def follow(sent):
        rank, axis, p, position, offset = sent
        here = with_at(offset, axis, offset[axis] - 1) if axis == RING else offset
        arrived.add((p, position, here))
        return advance(p, position, here)

    first = []
    for p in range(len(parts)):
        for offset in all_offsets(dims, range(4)):
            first += done(p, 0, offset)
    now = in_order(first, follow, lambda m: time_of(parts[m[2]][2], m[1]), AHEAD, order)
    return order, now


def all_offsets(dims, axes):
    offsets = [(0, 0, 0, 0)]
    for a in axes:
        offsets = [with_at(o, a, d) for o in offsets for d in range(dims[a])]
    return offsets


def reduce_kernel(dims, parts, *refs):
    srcs, tile = refs[:2], refs[2]
    head_out, common_out, losses, norm, factor = refs[3:8]
    places = len(parts) * 4
    buffers = refs[8 : 8 + places]
    head_sum, common_sum, shares, send_sem, recv_sem, near_tiles, far_tiles = refs[8 + places :]
    sums = (head_sum, common_sum)
    me = my_place(dims)
    z, y, x, cores = dims
    across = peers_across(dims)
    others = [o for o in all_offsets(dims, (0, 1)) if any(o)]
    met = ring_and_others(dims)
    greet(dims, me, met + [o for o in across + others if o not in met])
    push = Pushes(dims, me, send_sem, recv_sem)
    copies = {}

    def slot(p, position, offset):
        order = parts[p][3]
        axis = order[position]
        rest = [o for o in all_offsets(dims, order[position + 1 :])]
        k = rest.index(with_at(offset, axis, 0))
        return buffers[p * 4 + position].at[k, max(offset[axis] - 1, 0)]

    def summed(p, position, offset):
        array, first, rows, order = parts[p]
        if position == 0:
            place = shifted(dims, me, offset, 1)
            return srcs[array].at[blk_of(dims, place), head_of(dims, place), pl.ds(first, rows)]
        return slot(p, position - 1, offset)

    def ring_slot(p, position, offset):
        axis = parts[p][3][position]
        return slot(p, position, with_at(offset, axis, offset[axis] + 1))

    def add(p, position, offset):
        array, first, rows, order = parts[p]
        axis = order[position]
        if axis == RING:
            arrivals = [ring_slot(p, position, offset)]
        else:
            arrivals = [slot(p, position, with_at(offset, axis, d)) for d in range(1, dims[axis])]
        mine = summed(p, position, offset)
        step = row_chunk(rows)

        @pl.loop(0, rows // step)
        def some_rows(n):
            at = pl.ds(pl.multiple_of(n * step, step), step)
            total = mine[at].astype(jnp.float32)
            for arrival in arrivals:
                total = total + arrival[at].astype(jnp.float32)
            if position == 3 and not any(offset):
                sums[array][pl.ds(pl.multiple_of(first + n * step, TILE), step)] = total
            else:
                arrivals[0][at] = total.astype(low)

    for is_send, what in reduce_order(dims, parts)[0]:
        if is_send is None:
            add(*what)
        elif is_send:
            rank, axis, p, position, offset = what
            d = offset[axis]
            started = axis != RING or d == dims[axis] - 1
            source = summed(p, position, offset) if started else ring_slot(p, position, offset)
            step = along(axis, 1 if axis == RING else d)
            copies[what] = push(source, slot(p, position, offset), step)
        else:
            copies[what].wait_recv()
    my_head, my_blk = head_of(dims, me), blk_of(dims, me)
    shares[my_head] = common_sum[...].astype(low)
    share_copies = [push(shares.at[my_head], shares.at[my_head], o) for o in across]
    amount = head_out.shape[0]
    head_out[...] = head_sum[:amount]
    squares = jnp.sum(head_sum[:amount] * head_sum[:amount], 0, keepdims=True)
    squares = squares + jnp.sum(common_sum[...] * common_sum[...], 0, keepdims=True)
    lane = lax.broadcasted_iota(jnp.int32, (1, LANES), 1)
    near_tiles[my_head] = tile[...] + jnp.where(
        lane == MODES, jnp.sum(squares, 1, keepdims=True), 0.0
    )
    near = [push(near_tiles.at[my_head], near_tiles.at[my_head], o) for o in across]
    for copy in near:
        copy.wait_recv()
    far_tiles[my_blk] = jnp.sum(near_tiles[...], 0)
    far = [push(far_tiles.at[my_blk], far_tiles.at[my_blk], o) for o in others]
    for copy in share_copies:
        copy.wait_recv()
    piece = shares.shape[1]
    for k in range(x * cores):
        amount = min(piece, common_out.shape[0] - k * piece)
        common_out[k * piece : k * piece + amount] = shares[k].astype(jnp.float32)[:amount]
    for copy in far:
        copy.wait_recv()
    totals = jnp.sum(far_tiles[...], 0)[:1]
    losses[...] = totals[:, :MODES]
    norm[...] = jnp.sqrt(totals[:, MODES : MODES + 1])
    factor[...] = jnp.minimum(1.0, clip_limit / norm[...])
    push.finish()


def row_chunk(rows):
    for count in (4, 3, 2):
        if rows % (count * TILE) == 0:
            return rows // count
    return rows


def reduce_all(dims, arrays, valid, tile, collective_id):
    z, y, x, cores = dims
    rows = [array.shape[2] for array in arrays]
    parts = cut(0, rows[0], [(share, order[::-1]) for share, order in REDUCE_SHARES])
    parts = parts + cut(1, rows[1], ((1, ZXYC[::-1]),))
    scratch = []
    for array, first, amount, order in parts:
        for position, axis in enumerate(order):
            rest = len(all_offsets(dims, order[position + 1 :]))
            scratch.append(pltpu.VMEM((rest, dims[axis] - 1, amount, LANES), low))
    count = len(parts) * (z * y * x * cores - 1) + 2 * (x * cores - 1) + z * y - 1
    return pl.pallas_call(
        functools.partial(reduce_kernel, dims, parts),
        out_shape=[
            shape_of((valid[0], LANES), jnp.float32),
            shape_of((valid[1], LANES), jnp.float32),
            shape_of((1, MODES), jnp.float32),
            shape_of((1, 1), jnp.float32),
            shape_of((1, 1), jnp.float32),
        ],
        in_specs=[VMEM_SPEC] * 3,
        out_specs=[VMEM_SPEC] * 5,
        scratch_shapes=scratch
        + [pltpu.VMEM((n, LANES), jnp.float32) for n in rows]
        + [
            pltpu.VMEM((x * cores, rows[1], LANES), low),
            pltpu.SemaphoreType.DMA((count,)),
            pltpu.SemaphoreType.DMA((count,)),
            pltpu.VMEM((x * cores, 8, LANES), jnp.float32),
            pltpu.VMEM((z * y, 8, LANES), jnp.float32),
        ],
        compiler_params=pltpu.CompilerParams(
            collective_id=collective_id, has_side_effects=True, vmem_limit_bytes=60 * MIB
        ),
        name="reduce_gradients",
    )(*arrays, tile)


def contract_first(a, b):
    return lax.dot_general(a, b, (((0,), (0,)), ((), ())), preferred_element_type=jnp.float32)


def product(a, b):
    return jnp.dot(a, b, preferred_element_type=jnp.float32)


def against(a, b):
    return lax.dot_general(a, b, (((1,), (1,)), ((), ())), preferred_element_type=jnp.float32)


def clip_bounds(lengths):
    result, first = [], 0
    for clip in range(lengths.shape[0]):
        end = first + lengths[clip]
        result.append((first, end))
        first = end
    return result


def clip_borders(bounds, place):
    opening = jnp.zeros(place.shape, jnp.int32)
    ending = jnp.full(place.shape, 1 << 30, jnp.int32)
    for clip, (begin, end) in enumerate(bounds):
        here = place == clip
        opening = jnp.where(here, begin, opening)
        ending = jnp.where(here, end, ending)
    return opening, ending


def low_half(axis):
    return lax.broadcasted_iota(jnp.int32, (1, LANES) if axis else (LANES, 1), axis) < HD


def with_key_tail(bounds, first_row, kv):
    clips = len(bounds)
    place = lax.broadcasted_iota(jnp.int32, (1, LANES), 1) - HD
    opening, ending = clip_borders(bounds, place)
    ones = jnp.where((place >= clips) & (place < clips + 3), 1.0, 0.0)
    row = first_row + lax.broadcasted_iota(jnp.int32, kv.shape, 0)
    tail = jnp.where((row >= opening) & (row < ending), ones, big_negative)
    return jnp.where(low_half(1), kv.astype(jnp.float32), tail).astype(low)


def with_value_tail(kv):
    place = lax.broadcasted_iota(jnp.int32, (1, LANES), 1)
    ones = jnp.where(place < 3, 1.0, 0.0)
    return jnp.where(low_half(1), ones, kv.astype(jnp.float32)).astype(low)


def in_three(place, value):
    top = value.astype(low).astype(jnp.float32)
    middle = (value - top).astype(low).astype(jnp.float32)
    bottom = value - top - middle
    return (
        jnp.where(place == 0, top, 0.0)
        + jnp.where(place == 1, middle, 0.0)
        + jnp.where(place == 2, bottom, 0.0)
    )


def with_query_tail(bounds, first_row, rows, extra):
    clips = len(bounds)
    place = lax.broadcasted_iota(jnp.int32, (HD, 1), 0)
    opening, ending = clip_borders(bounds, place)
    row = first_row + lax.broadcasted_iota(jnp.int32, (1, rows.shape[1]), 1)
    inside = (place < clips) & (row >= opening) & (row < ending)
    tail = jnp.where(inside, 1.0, 0.0)
    if extra is not None:
        tail = tail + in_three(place - clips, -extra)
    return jnp.concatenate([rows * (SCORE_SCALE * LOG2E), tail], 0).astype(low)


def pack(rows):
    half = rows.shape[0] // 2
    return jnp.concatenate([rows[:half], rows[half:]], 1)


def unpack(packed):
    return jnp.concatenate([packed[:, :HD], packed[:, HD:]], 0)


def unpack_t(packed):
    turned = packed.astype(jnp.float32).T
    return jnp.concatenate([turned[:HD], turned[HD:]], 1)


def pack_t(columns):
    half = columns.shape[1] // 2
    return jnp.concatenate([columns[:, :half], columns[:, half:]], 0).T


class Team:
    def __init__(self, dims):
        z, y, x, cores = dims
        self.dims = dims
        self.wide = HEADS // (x * cores) == y
        self.size = x * cores * (y if self.wide else 1)
        self.groups = z if self.wide else z * y
        axes = (1, 2, 3) if self.wide else (2, 3)
        offsets = [o for o in all_offsets(dims, axes) if any(o)]
        self.others = sorted(offsets, key=lambda o: (o[1] + o[2], o))
        self.sides = [] if self.wide else axis_peers(dims, (1,))

    def slot(self, place):
        head = head_of(self.dims, place)
        return place[1] * self.dims[2] * self.dims[3] + head if self.wide else head

    def group(self, place):
        return place[0] if self.wide else blk_of(self.dims, place)


def heads_of(n_head, slots):
    return [(s % n_head, s // n_head) for s in range(slots)]


class Pushes:
    def __init__(self, dims, me, send_sem, recv_sem):
        self.dims, self.me, self.send_sem, self.recv_sem = dims, me, send_sem, recv_sem
        self.started = []

    def later(self, src, dst, offset):
        i = len(self.started)
        place = shifted(self.dims, self.me, offset, 1)
        copy = remote(src, dst, self.send_sem.at[i], self.recv_sem.at[i], place, self.dims)
        self.started.append(copy)
        return copy

    def __call__(self, src, dst, offset):
        copy = self.later(src, dst, offset)
        copy.start()
        return copy

    def finish(self):
        for copy in self.started:
            copy.wait_send()


def peers_across(dims):
    z, y, x, cores = dims
    across = [(0, 0, a, c) for a in range(x) for c in range(cores) if (a, c) != (0, 0)]
    return sorted(across, key=lambda o: (o[2] == 0, o[3]))


def attend_kernel(
    team,
    query_step,
    key_step,
    pieces,
    lengths,
    q_in,
    kv_in,
    o_out,
    lse,
    out_t,
    q_all,
    kv_out,
    kv_all,
    even_keys,
    even_values_t,
    odd_keys,
    odd_values_t,
    queries,
    top,
    accum,
    even_scores,
    odd_scores,
    even_top,
    odd_top,
    o_mine,
    send_sem,
    recv_sem,
    own_sem,
):
    dims = team.dims
    z = dims[0]
    me = my_place(dims)
    bounds = clip_bounds(lengths)
    rows = kv_in.shape[1]
    amount = team.size * rows
    slots = team.size // pieces
    my_group, my_slot = team.group(me), team.slot(me)
    ring_ends = sorted({along(0, 1 % z), along(0, (z - 1) % z)} - {(0, 0, 0, 0)})
    greet(dims, me, team.others + ring_ends + team.sides)
    push = Pushes(dims, me, send_sem, recv_sem)
    own_kv = pltpu.make_async_copy(kv_in.at[my_slot], kv_all.at[my_group, my_slot], own_sem.at[0])
    own_q = pltpu.make_async_copy(q_in.at[my_slot], q_all.at[my_slot], own_sem.at[1])
    own_kv.start()
    own_q.start()

    def to_team(src, dst, o):
        return push(src.at[team.slot(shifted(dims, me, o, 1))], dst, o)

    kv_copies = {o: to_team(kv_in, kv_all.at[my_group, my_slot], o) for o in team.others}
    q_copies = [to_team(q_in, q_all.at[my_slot], o) for o in team.others]
    ring, side, slot_copies = {}, {}, []

    def group_at(offset):
        return team.group(shifted(dims, me, offset, -1))

    def send_slot(o):
        if z > 1:
            block = kv_all.at[my_group, team.slot(shifted(dims, me, o, -1))]
            slot_copies.append(push(block, block, along(0, 1)))

    def slot_arrived():
        for copy in slot_copies:
            copy.wait_recv()

    def send_on(s, piece):
        block = kv_all.at[group_at(along(0, s)), pl.ds(piece * slots, slots)]
        if 0 < s < z - 1:
            ring[(s + 1, piece)] = push(block, block, along(0, 1))
        for o in team.sides:
            side[(s, o, piece)] = push(block, block, o)

    def both(now, later):
        if now is not None:
            n, unused, now_values, now_scores, now_top = now
            at = tile(n)
            old = top[:, at]
            new = jnp.maximum(old, jnp.max(now_top[...], 0, keepdims=True))
            top[:, at] = new
            total = accum[:, at] * jnp.exp2(old - new)
        if later is not None:
            n, later_keys, unused, later_scores, later_top = later
            query = queries[:, tile(n)]
            highest = jnp.full(later_top.shape, -1e38, jnp.float32)
        for k in range(0, slots * rows, key_step):
            if later is not None:
                scores = product(later_keys[k : k + key_step, :], query)
                later_scores[k : k + key_step, :] = scores
                highest = jnp.maximum(
                    highest, jnp.max(scores.reshape(key_step // 8, 8, query_step), 0)
                )
            if now is not None:
                probs = jnp.exp2((now_scores[k : k + key_step, :] - new).astype(low))
                total = total + product(now_values[:, k : k + key_step], probs)
        if later is not None:
            later_top[...] = highest
        if now is not None:
            accum[:, at] = total

    def tile(n):
        return pl.ds(pl.multiple_of(n * query_step, query_step), query_step)

    computed, pending = [], [None]

    def compute(offset, piece):
        group = group_at(offset)
        keys, values_t = sides_of_keys[len(computed) % 2]
        computed.append(offset)

        @pl.loop(0, slots)
        def build(n):
            at = pl.ds(pl.multiple_of(n * rows, rows), rows)
            slot = piece * slots + n
            block = kv_all[group, slot]
            keys[at, :] = with_key_tail(bounds, group * amount + slot * rows, block)
            values_t[:HD, at] = block.astype(jnp.float32).T[HD:].astype(low)

        def even(n):
            return (n, keys, values_t, even_scores, even_top)

        def odd(n):
            return (n, keys, values_t, odd_scores, odd_top)

        tiles = amount // query_step
        both(pending[0], even(0))

        @pl.loop(0, tiles // 2 - 1)
        def query_blocks(n):
            both(even(2 * n), odd(2 * n + 1))
            both(odd(2 * n + 1), even(2 * n + 2))

        both(even(tiles - 2), odd(tiles - 1))
        pending[0] = odd(tiles - 1)

    sides_of_keys = ((even_keys, even_values_t), (odd_keys, odd_values_t))
    for unused, values_t in sides_of_keys:
        values_t[HD:, :] = jnp.ones((TILE, slots * rows), low)
    top[...] = jnp.full(top.shape, -1e38, jnp.float32)
    accum[...] = jnp.zeros(accum.shape, jnp.float32)
    own_kv.wait()
    send_slot((0, 0, 0, 0))
    for o in team.others:
        kv_copies[o].wait_recv()
        send_slot(o)
    for piece in range(pieces):
        send_on(0, piece)
    own_q.wait()
    for copy in q_copies:
        copy.wait_recv()
    for n in range(team.size):
        queries[:, n * rows : (n + 1) * rows] = with_query_tail(
            bounds, my_group * amount + n * rows, unpack_t(q_all[n]), None
        )
    stores = []

    def store(offset):
        group = group_at(offset)
        copy = pltpu.make_async_copy(kv_all.at[group], kv_out.at[group], own_sem.at[3 + len(stores)])
        copy.start()
        stores.append(copy)

    for s in range(z):
        store(along(0, s))
        for piece in range(pieces):
            compute(along(0, s), piece)
            if s < z - 1:
                if s:
                    ring[(s + 1, piece)].wait_recv()
                elif piece == 0:
                    slot_arrived()
                send_on(s + 1, piece)
            for o in team.sides:
                side[(s, o, piece)].wait_recv()
                compute((s, o[1], 0, 0), piece)
        for o in team.sides:
            store((s, o[1], 0, 0))
    both(pending[0], None)
    total = accum[HD : HD + 1, :]
    out_t[...] = accum[:HD, :] / total
    lse[...] = top[...] + jnp.log(total) * LOG2E
    for n in range(team.size):
        o_mine[n] = pack_t(out_t[:, n * rows : (n + 1) * rows]).astype(low)
    o_copies = [to_team(o_mine, o_out.at[my_slot], o) for o in team.others]
    own_o = pltpu.make_async_copy(o_mine.at[my_slot], o_out.at[my_slot], own_sem.at[2])
    own_o.start()
    own_o.wait()
    for copy in o_copies:
        copy.wait_recv()
    for copy in stores:
        copy.wait()
    push.finish()


def attend(dims, lengths, q, kv, collective_id):
    team = Team(dims)
    z = dims[0]
    amount = team.size * kv.shape[1]
    pieces, query_step = 2, 256
    count = 4 * team.size + pieces * (z + z * len(team.sides))
    return pl.pallas_call(
        functools.partial(attend_kernel, team, query_step, 256, pieces),
        out_shape=(
            jax.ShapeDtypeStruct(q.shape, low),
            jax.ShapeDtypeStruct((1, amount), jnp.float32),
            jax.ShapeDtypeStruct((HD, amount), jnp.float32),
            jax.ShapeDtypeStruct(q.shape, low),
            jax.ShapeDtypeStruct((team.groups,) + kv.shape, low),
        ),
        in_specs=[SMEM_SPEC, VMEM_SPEC, VMEM_SPEC],
        out_specs=[VMEM_SPEC] * 4 + [ANY_SPEC],
        scratch_shapes=[
            pltpu.VMEM((team.groups,) + kv.shape, low),
            pltpu.VMEM((amount // pieces, LANES), low),
            pltpu.VMEM((HD + TILE, amount // pieces), low),
            pltpu.VMEM((amount // pieces, LANES), low),
            pltpu.VMEM((HD + TILE, amount // pieces), low),
            pltpu.VMEM((LANES, amount), low),
            pltpu.VMEM((1, amount), jnp.float32),
            pltpu.VMEM((HD + TILE, amount), jnp.float32),
            pltpu.VMEM((amount // pieces, query_step), jnp.float32),
            pltpu.VMEM((amount // pieces, query_step), jnp.float32),
            pltpu.VMEM((8, query_step), jnp.float32),
            pltpu.VMEM((8, query_step), jnp.float32),
            pltpu.VMEM(q.shape, low),
            pltpu.SemaphoreType.DMA((count,)),
            pltpu.SemaphoreType.DMA((count,)),
            pltpu.SemaphoreType.DMA((3 + team.groups,)),
        ],
        compiler_params=pltpu.CompilerParams(
            collective_id=collective_id, has_side_effects=True, vmem_limit_bytes=56 * MIB
        ),
        name="attend",
    )(lengths, q, kv)


def attend_back_kernel(
    team,
    key_step,
    query_step,
    pieces,
    lengths,
    q_all,
    kv_in,
    do_in,
    out_t,
    lse,
    d_q_out,
    d_kv_out,
    kv_all,
    do_all,
    even_keys_t,
    even_values_t,
    even_rows,
    odd_keys_t,
    odd_values_t,
    odd_rows,
    queries,
    douts,
    d_q_sum,
    q_rows,
    do_rows,
    even_probs,
    odd_probs,
    even_scores,
    odd_scores,
    side_out,
    side_in,
    ring_out,
    ring_in,
    mine,
    d_q_mine,
    d_kv_mine,
    send_sem,
    recv_sem,
    own_sem,
):
    dims = team.dims
    z = dims[0]
    me = my_place(dims)
    bounds = clip_bounds(lengths)
    rows = kv_all.shape[2]
    amount = team.size * rows
    loads = {}
    for s in range(1, z + 1):
        for o in team.sides + [(0, 0, 0, 0)]:
            offset = ((z - s) % z, o[1], 0, 0)
            group = team.group(shifted(dims, me, offset, 1))
            loads[offset] = pltpu.make_async_copy(
                kv_in.at[group], kv_all.at[group], own_sem.at[3 + len(loads)]
            )
            loads[offset].start()
    slots = team.size // pieces
    piece_rows = slots * rows
    my_group, my_slot = team.group(me), team.slot(me)
    ring_ends = sorted({along(0, 1 % z), along(0, (z - 1) % z)} - {(0, 0, 0, 0)})
    greet(dims, me, team.others + ring_ends + team.sides)
    push = Pushes(dims, me, send_sem, recv_sem)

    def to_team(src, dst, o):
        return push(src.at[team.slot(shifted(dims, me, o, 1))], dst, o)

    do_copies = [to_team(do_in, do_all.at[my_slot], o) for o in team.others]
    own_do = pltpu.make_async_copy(do_in.at[my_slot], do_all.at[my_slot], own_sem.at[0])
    own_do.start()
    place = lax.broadcasted_iota(jnp.int32, (HD, 1), 0)
    for n in range(team.size):
        at = slice(n * rows, (n + 1) * rows)
        q_t = unpack_t(q_all[n])
        extended = with_query_tail(bounds, my_group * amount + n * rows, q_t, lse[:, at])
        queries[at, :] = extended.astype(jnp.float32).T.astype(low)
        q_rows[:, at] = (q_t * SCORE_SCALE).astype(low)
    d_q_sum[...] = jnp.zeros(d_q_sum.shape, jnp.float32)
    own_do.wait()
    for copy in do_copies:
        copy.wait_recv()
    for n in range(team.size):
        at = slice(n * rows, (n + 1) * rows)
        do_t = unpack_t(do_all[n])
        delta = jnp.sum(do_t * out_t[:, at], 0, keepdims=True)
        extended = jnp.concatenate([in_three(place, -delta), do_t], 0).astype(low)
        douts[at, :] = extended.astype(jnp.float32).T.astype(low)
        do_rows[:, at] = do_t.astype(low)

    def both(now, later):
        if now is not None:
            n, (unused, unused, now_rows), now_probs, now_scores, target = now
            now_at = rows_of(n)
        if later is not None:
            n, (keys_t, values_t, unused), later_probs, later_scores, unused = later
            at = rows_of(n)
        for first in range(0, amount, query_step):
            part = slice(first, first + query_step)
            if later is not None:
                probs = jnp.exp2(product(queries[part, :], keys_t[:, at]).astype(low))
                d_probs = product(douts[part, :], values_t[:, at])
                later_probs[part, :] = probs
                later_scores[part, :] = (probs.astype(jnp.float32) * d_probs).astype(low)
            if now is not None:
                if first == 0:
                    d_value = product(do_rows[...], now_probs[...])
                if first == amount // 2:
                    d_key = product(q_rows[...], now_scores[...])
                d_q_sum[part, :] = d_q_sum[part, :] + product(now_scores[part, :], now_rows[now_at, :])
        if now is not None:
            target[now_at, :] = jnp.concatenate([d_key, d_value], 0).T.astype(target.dtype)

    def rows_of(k):
        return slice(k * key_step, (k + 1) * key_step)

    computed, pending = [], []

    def flush(later=None):
        if pending:
            now, after = pending.pop()
            both(now, later)
            after()
        elif later is not None:
            both(None, later)

    def compute(offset, piece, target, after):
        group = team.group(shifted(dims, me, offset, 1))
        keys = sides_of_keys[len(computed) % 2]
        computed.append(offset)
        if offset in loads:
            loads.pop(offset).wait()

        @pl.loop(0, slots)
        def build(n):
            at = pl.ds(pl.multiple_of(n * rows, rows), rows)
            slot = piece * slots + n
            block = kv_all[group, slot]
            extended = with_key_tail(bounds, group * amount + slot * rows, block)
            keys[0][:, at] = extended.astype(jnp.float32).T.astype(low)
            keys[1][:, at] = with_value_tail(block).astype(jnp.float32).T.astype(low)
            keys[2][at, :] = block

        steps = [
            (k, keys) + ((odd_probs, odd_scores) if k % 2 else (even_probs, even_scores)) + (target,)
            for k in range(piece_rows // key_step)
        ]
        flush(steps[0])
        for now, later in zip(steps[:-1], steps[1:]):
            both(now, later)
        pending.append((steps[-1], after))

    sides_of_keys = (
        (even_keys_t, even_values_t, even_rows),
        (odd_keys_t, odd_values_t, odd_rows),
    )
    side, ring = {}, {}

    def send_sides(s, piece):
        for o in team.sides:
            target = side_out.at[s - 1, o[1] - 1, piece]

            def send(o=o, target=target):
                side[(s, o, piece)] = push(target, side_in.at[s - 1, o[1] - 1, piece], o)

            compute(((z - s) % z, o[1], 0, 0), piece, target, send)

    def combine(s, piece):
        for o in team.sides:
            side[(s, o, piece)].wait_recv()
        if s > 1:
            ring[(s - 1, piece)].wait_recv()
        for n in range(slots):
            at = slice(n * rows, (n + 1) * rows)
            total = mine[piece, at, :]
            for o in team.sides:
                total = total + side_in[s - 1, o[1] - 1, piece, at, :].astype(jnp.float32)
            if s > 1:
                total = total + ring_in[s - 2, piece, at, :].astype(jnp.float32)
            if s < z:
                ring_out[s - 1, piece, at, :] = total.astype(low)
            else:
                d_kv_mine[piece * slots + n] = total.astype(low)
        if s == z:
            for copy, slot in d_kv_copies:
                pl.when((slot >= piece * slots) & (slot < (piece + 1) * slots))(copy.start)
        if s < z:
            ring[(s, piece)] = push(ring_out.at[s - 1, piece], ring_in.at[s - 1, piece], along(0, 1))

    d_kv_copies = []
    for o in team.others:
        slot = team.slot(shifted(dims, me, o, 1))
        d_kv_copies.append((push.later(d_kv_mine.at[slot], d_kv_out.at[my_slot], o), slot))
    for s in range(1, z + 1):
        for piece in range(pieces):
            send_sides(s, piece)
            after = functools.partial(combine, s, piece)
            compute((z - s if s < z else 0, 0, 0, 0), piece, mine.at[piece], after)
    flush()
    for n in range(team.size):
        at = slice(n * rows, (n + 1) * rows)
        d_q_mine[n] = pack(d_q_sum[at, :HD] * SCORE_SCALE).astype(low)
    copies = [to_team(d_q_mine, d_q_out.at[my_slot], o) for o in team.others]
    own_q = pltpu.make_async_copy(d_q_mine.at[my_slot], d_q_out.at[my_slot], own_sem.at[1])
    own_q.start()
    copies += [copy for copy, slot in d_kv_copies]
    own_kv = pltpu.make_async_copy(d_kv_mine.at[my_slot], d_kv_out.at[my_slot], own_sem.at[2])
    own_kv.start()
    own_q.wait()
    own_kv.wait()
    for copy in copies:
        copy.wait_recv()
    push.finish()


def attend_back(dims, lengths, q, kv, dout, out_t, lse, collective_id):
    team = Team(dims)
    z = dims[0]
    rows = kv.shape[2]
    amount = team.size * rows
    pieces, key_step = 2, 256
    piece = (pieces, amount // pieces, LANES)
    count = 3 * (team.size - 1) + pieces * (z + z * len(team.sides))
    others = max(len(team.sides), 1)
    ring_steps, side_steps = max(z - 1, 1), z if team.sides else 1
    return pl.pallas_call(
        functools.partial(attend_back_kernel, team, key_step, 512, pieces),
        out_shape=(
            jax.ShapeDtypeStruct(q.shape, low),
            jax.ShapeDtypeStruct(kv.shape[1:], low),
        ),
        in_specs=[SMEM_SPEC, VMEM_SPEC, ANY_SPEC] + [VMEM_SPEC] * 3,
        out_specs=[VMEM_SPEC] * 2,
        scratch_shapes=[
            pltpu.VMEM(kv.shape, low),
            pltpu.VMEM(q.shape, low),
            pltpu.VMEM((LANES, amount // pieces), low),
            pltpu.VMEM((LANES, amount // pieces), low),
            pltpu.VMEM((amount // pieces, LANES), low),
            pltpu.VMEM((LANES, amount // pieces), low),
            pltpu.VMEM((LANES, amount // pieces), low),
            pltpu.VMEM((amount // pieces, LANES), low),
            pltpu.VMEM((amount, LANES), low),
            pltpu.VMEM((amount, LANES), low),
            pltpu.VMEM((amount, LANES), jnp.float32),
            pltpu.VMEM((HD, amount), low),
            pltpu.VMEM((HD, amount), low),
            pltpu.VMEM((amount, key_step), low),
            pltpu.VMEM((amount, key_step), low),
            pltpu.VMEM((amount, key_step), low),
            pltpu.VMEM((amount, key_step), low),
            pltpu.VMEM((side_steps, others) + piece, low),
            pltpu.VMEM((side_steps, others) + piece, low),
            pltpu.VMEM((ring_steps,) + piece, low),
            pltpu.VMEM((ring_steps,) + piece, low),
            pltpu.VMEM(piece, jnp.float32),
            pltpu.VMEM(q.shape, low),
            pltpu.VMEM(kv.shape[1:], low),
            pltpu.SemaphoreType.DMA((count,)),
            pltpu.SemaphoreType.DMA((count,)),
            pltpu.SemaphoreType.DMA((3 + team.groups,)),
        ],
        compiler_params=pltpu.CompilerParams(
            collective_id=collective_id, has_side_effects=True, vmem_limit_bytes=60 * MIB
        ),
        name="attend_back",
    )(lengths, q, kv, dout, out_t, lse)


def part_shapes(n_head):
    width = HEADS // n_head * HD
    hidden = FF // n_head
    return (
        (D, width, True),
        (DI, 2 * width, True),
        (width, D, False),
        (D, 3 * width, True),
        (width, D, False),
        (D, hidden, True),
        (hidden, D, False),
        (D, C // n_head, True),
    )


def borders(n_head):
    result = [0]
    for rows, columns, joined in part_shapes(n_head):
        result.append(result[-1] + rows * columns // LANES)
    return result


def period(columns):
    amount = 1
    while amount * columns % LANES:
        amount *= 2
    return amount


def segments(start, amount, unit):
    result = []
    while amount > 0:
        which, at = divmod(start, unit)
        size = min(unit - at, amount)
        result.append((which, at, at + size))
        start, amount = start + size, amount - size
    return result


def joined_lanes(pieces):
    return pieces[0] if len(pieces) == 1 else jnp.concatenate(pieces, 1)


def lane_blocks(value):
    rows, columns = value.shape
    missing = -columns % LANES
    if missing:
        value = jnp.concatenate([value, jnp.zeros((rows, missing), value.dtype)], 1)
    return [value[:, i : i + LANES] for i in range(0, columns + missing, LANES)]


def every(first, amount, stride):
    return pl.ds(first, amount) if stride == 1 else pl.ds(first, amount, stride=stride)


def matrix_of(stage, first, rows, columns, line):
    if columns % LANES == 0:
        stride = columns // LANES
        for j in range(stride):
            yield j * LANES, stage[every(first + j, rows, stride), :]
        return
    height = period(columns)
    stride = height * columns // LANES
    for k in range(height):
        pieces = [
            stage[every(first + which, rows // height, stride), :][:, begin:end]
            for which, begin, end in segments(k * columns, columns, LANES)
        ]
        for i, piece in enumerate(lane_blocks(joined_lanes(pieces))):
            line[i, every(k, rows // height, height), :] = piece
    for i in range(-(-columns // LANES)):
        yield i * LANES, line[i, :rows, : min(columns - i * LANES, LANES)]


def matrix_into(stage, first, value, line):
    rows, columns = value.shape
    if columns % LANES == 0:
        stride = columns // LANES
        for j in range(stride):
            stage[every(first + j, rows, stride), :] = value[:, j * LANES : (j + 1) * LANES]
        return
    height = period(columns)
    stride = height * columns // LANES
    for i, piece in enumerate(lane_blocks(value)):
        line[i, :rows, :] = piece
    for i in range(stride):
        pieces = [
            line[which, every(k, rows // height, height), :][:, begin:end]
            for k, first_lane, last_lane in segments(i * LANES, LANES, columns)
            for which, begin, end in segments(first_lane, last_lane - first_lane, LANES)
        ]
        stage[every(first + i, rows // height, stride), :] = joined_lanes(pieces)


def load_stage(stage, held, first_shard, shard_rows, group):
    for b in range(held.shape[0]):
        stage[pl.ds(b * shard_rows, shard_rows), :] = held[b, group, :shard_rows, :].astype(jnp.float32)


def load_common(stage, held, valid):
    piece = held.shape[2]
    for b in range(held.shape[0]):
        for k in range(held.shape[1]):
            amount = min(piece, valid - k * piece)
            stage[b * valid + k * piece : b * valid + k * piece + amount, :] = held[b, k].astype(
                jnp.float32
            )[:amount]


def common_blocks(first_row, last_row, valid):
    return first_row // valid, -(-last_row // valid) - first_row // valid


def load_matrices(stage, first_row, n_head, group, which, targets, line):
    starts, shapes = borders(n_head), part_shapes(n_head)
    for m, target in zip(which, targets):
        rows, columns, joined = shapes[m]
        row = 0 if joined else group * rows
        column = group * columns if joined else 0
        for j, value in matrix_of(stage, starts[m] - first_row, rows, columns, line):
            size = value.shape[1]
            target[row : row + rows, column + j : column + j + size] = value.astype(target.dtype)


class Moves:
    def __init__(self, sems):
        self.sems, self.going = sems, []

    def __call__(self, src, dst):
        copy = pltpu.make_async_copy(src, dst, self.sems.at[len(self.going)])
        copy.start()
        self.going.append(copy)
        return copy


def normalized(x):
    centre = x - jnp.mean(x, -1, keepdims=True)
    rate = lax.rsqrt(jnp.mean(centre * centre, -1, keepdims=True) + norm_eps)
    return centre * rate, rate


def layer_norm(x, gain):
    return normalized(x)[0] * gain


def norm_pullback(x, gain, grad):
    unit, rate = normalized(x)
    inside = grad * gain
    both = jnp.mean(inside * unit, -1, keepdims=True)
    d_x = rate * (inside - jnp.mean(inside, -1, keepdims=True) - unit * both)
    return d_x, jnp.sum(grad * unit, 0, keepdims=True)


def head_lanes(group, heads, value):
    width = heads * HD
    block = value[:, group * width : (group + 1) * width]
    lane = lax.broadcasted_iota(jnp.int32, (1, width), 1)
    result = []
    for a in range(heads):
        here = (lane >= a * HD) & (lane < (a + 1) * HD)
        result.append((here, jnp.where(here, block, jnp.zeros_like(block))))
    return result


def place_of(bounds, first, amount):
    row = first + lax.broadcasted_iota(jnp.int32, (amount, 1), 0)
    opening = jnp.zeros((amount, 1), jnp.int32)
    for begin, end in bounds:
        opening = jnp.where((row >= begin) & (row < end), begin, opening)
    offset = row - opening
    turns = jnp.floor((offset.astype(jnp.float32) + 0.5) * (1.0 / LAT)).astype(jnp.int32)
    return offset - turns * LAT


def picked_rows(bounds, rows, n_head):
    first = lax.axis_index("blk") * (rows * n_head) + lax.axis_index("head") * rows
    lane = lax.broadcasted_iota(jnp.int32, (rows, LAT), 1)
    return jnp.where(lane == place_of(bounds, first, rows), 1.0, 0.0).astype(low)


def enc_scores(q_head, keys):
    return against(q_head, keys) * (SCORE_SCALE * LOG2E)


def encode_kernel(
    n_head,
    shard_rows,
    valid,
    rows,
    lengths,
    weights,
    common,
    inputs_t,
    enc_query_out,
    enc_keyval_out,
    enc_output_out,
    self_project_out,
    gains,
    z_zero_out,
    h_zero_out,
    x_norm_out,
    q_enc_out,
    kv_enc_out,
    o_enc_out,
    z_one_out,
    h_one_out,
    q_self,
    kv_self,
    counts,
    label_counts,
    enc_query,
    enc_keyval,
    enc_output,
    self_project,
    z_zero,
    h_zero,
    x_norm_t,
    q_enc,
    kv_enc,
    o_enc,
    z_one,
    h_one,
    held,
    held_common,
    held_counts,
    stage,
    stage_common,
    line,
    latent_table,
    sems,
):
    heads = HEADS // n_head
    width = heads * HD
    shards = held.shape[0]
    bounds = clip_bounds(lengths)
    first = DQ * D // LANES
    block, blocks = common_blocks(first, first + (LAT + 4) * D // LANES, valid)
    tail = shard_rows // TILE * TILE
    move = Moves(sems)
    common_here = move(common.at[pl.ds(block, blocks)], held_common)
    counts_here = move(weights.at[:, :, pl.ds(tail, TILE)], held_counts)
    weights_here = [move(weights.at[pl.ds(0, shards), g], held.at[:, g]) for g in range(n_head)]
    centre = inputs_t[...].astype(jnp.float32)
    centre = centre - jnp.mean(centre, 0, keepdims=True)
    rate = lax.rsqrt(jnp.mean(centre * centre, 0, keepdims=True) + norm_eps)
    x_norm_t[...] = (centre * rate).astype(low)
    stored = [move(x_norm_t, x_norm_out)]
    common_here.wait()
    load_common(stage_common, held_common, valid)
    first = first - block * valid
    for j, value in matrix_of(stage_common, first, LAT, D, line):
        latent_table[:, j : j + LANES] = value.astype(low)
    for j, value in matrix_of(stage_common, first + LAT * D // LANES, 4, D, line):
        gains[:, j : j + LANES] = value
    picked = picked_rows(bounds, rows, n_head)
    z_zero[...] = product(picked, latent_table[...])
    h_zero[...] = layer_norm(z_zero[...], gains[0:1, :]).astype(low)
    stored += [move(z_zero, z_zero_out), move(h_zero, h_zero_out)]
    counts_here.wait()
    counted = held_counts[...].astype(jnp.float32)[:, :, shard_rows - tail : shard_rows - tail + 1]
    counts[...] = jnp.broadcast_to(jnp.sum(counted, (0, 1)), counts.shape)
    label_counts[...] = counts[:1, :MODES]
    for g in range(n_head):
        weights_here[g].wait()
        load_stage(stage, held, 0, shard_rows, g)
        load_matrices(
            stage, 0, n_head, g, (0, 1, 2, 3), (enc_query, enc_keyval, enc_output, self_project), line
        )
    stored += [move(enc_query, enc_query_out), move(enc_keyval, enc_keyval_out)]
    stored += [move(enc_output, enc_output_out), move(self_project, self_project_out)]
    q_enc[...] = product(h_zero[...], enc_query[...]).astype(low)
    kv_enc[...] = contract_first(x_norm_t[...], enc_keyval[...]).astype(low)
    stored += [move(q_enc, q_enc_out), move(kv_enc, kv_enc_out)]
    for g in range(n_head):
        keys = kv_enc[:, 2 * g * width : (2 * g + 1) * width]
        values = kv_enc[:, (2 * g + 1) * width : (2 * g + 2) * width]
        outcome = jnp.zeros((rows, width), jnp.float32)
        for here, q_head in head_lanes(g, heads, q_enc[...]):
            scores = enc_scores(q_head, keys)
            probs = jnp.exp2((scores - jnp.max(scores, 1, keepdims=True)).astype(low))
            total = jnp.sum(probs.astype(jnp.float32), 1, keepdims=True)
            outcome = jnp.where(here, product(probs, values) / total, outcome)
        o_enc[:, g * width : (g + 1) * width] = outcome.astype(low)
    z_one[...] = z_zero[...] + product(o_enc[...], enc_output[...])
    h_one[...] = layer_norm(z_one[...], gains[1:2, :]).astype(low)
    stored += [move(o_enc, o_enc_out), move(z_one, z_one_out), move(h_one, h_one_out)]
    projected = product(h_one[...], self_project[...]).astype(low)
    for slot, (g, a) in enumerate(heads_of(n_head, q_self.shape[0])):
        query, key, value = (
            projected[:, (3 * g + i) * width + a * HD : (3 * g + i) * width + (a + 1) * HD]
            for i in range(3)
        )
        q_self[slot] = pack(query)
        kv_self[slot] = jnp.concatenate([key, value], 1)
    for copy in stored:
        copy.wait()


LINE = pltpu.VMEM((4, round_up(max(D, DI), 8), LANES), jnp.float32)


def shards_of(n_head, shard_rows, first, last):
    starts = borders(n_head)
    begin = starts[first] // shard_rows
    return begin, -(-starts[last] // shard_rows) - begin


def encode(lengths, weights, common, inputs_t, valid, rows, slots, n_head, shard_rows):
    begin, shards = shards_of(n_head, shard_rows, 0, 4)
    query_rows = DQ * D // LANES
    block, blocks = common_blocks(query_rows, query_rows + (LAT + 4) * D // LANES, valid)
    keys = inputs_t.shape[1]
    kept = [
        shape_of((D, D)),
        shape_of((DI, 2 * D)),
        shape_of((D, D)),
        shape_of((D, 3 * D)),
        shape_of((rows, D), jnp.float32),
        shape_of((rows, D)),
        shape_of(inputs_t.shape),
        shape_of((rows, D)),
        shape_of((keys, 2 * D)),
        shape_of((rows, D)),
        shape_of((rows, D), jnp.float32),
        shape_of((rows, D)),
    ]
    return pl.pallas_call(
        functools.partial(encode_kernel, n_head, shard_rows, valid, rows),
        out_shape=kept[:4]
        + [shape_of((4, D), jnp.float32)]
        + kept[4:]
        + [
            shape_of((slots, rows // 2, LANES)),
            shape_of((slots, rows, LANES)),
            shape_of((8, LANES), jnp.float32),
            shape_of((1, MODES), jnp.float32),
        ],
        in_specs=[SMEM_SPEC, ANY_SPEC, ANY_SPEC, VMEM_SPEC],
        out_specs=[ANY_SPEC] * 4 + [VMEM_SPEC] + [ANY_SPEC] * 8 + [VMEM_SPEC] * 4,
        scratch_shapes=[pltpu.VMEM(a.shape, a.dtype) for a in kept]
        + [
            pltpu.VMEM((shards,) + weights.shape[1:], low),
            pltpu.VMEM((blocks,) + common.shape[1:], low),
            pltpu.VMEM(weights.shape[:2] + (TILE, LANES), low),
            pltpu.VMEM((shards * shard_rows, LANES), jnp.float32),
            pltpu.VMEM((blocks * valid, LANES), jnp.float32),
            LINE,
            pltpu.VMEM((LAT, D), low),
            pltpu.SemaphoreType.DMA((2 + n_head + len(kept),)),
        ],
        compiler_params=pltpu.CompilerParams(vmem_limit_bytes=56 * MIB),
        name="encode",
    )(lengths, weights, common, inputs_t)


def gelu_and_slope(x):
    rate = (2.0 / jnp.pi) ** 0.5
    cubic = 0.044715
    t = jnp.tanh(rate * (x + cubic * x * x * x))
    slope = 0.5 * (1.0 + t) + 0.5 * x * (1.0 - t * t) * rate * (1.0 + 3.0 * cubic * x * x)
    return 0.5 * x * (1.0 + t), slope


def my_column(marks, rows):
    turned = marks[...].astype(jnp.float32).T
    column = lax.broadcasted_iota(jnp.int32, turned.shape, 1)
    per_head = rows // LANES
    first = lax.axis_index("head") * per_head
    picked = [
        jnp.sum(jnp.where(column == first + k, turned, 0.0), 1, keepdims=True)
        for k in range(per_head)
    ]
    return jnp.concatenate(picked, 0) if per_head > 1 else picked[0]


def middle_kernel(
    n_head,
    shard_rows,
    valid,
    first_shard,
    rows,
    counts,
    weights,
    common,
    z_one,
    o_self,
    out_queries_t,
    labels,
    modality,
    labeled,
    gains,
    dout,
    d_two_out,
    tile,
    query_grad_out,
    gain_grads,
    grads,
    held,
    held_common,
    stage,
    stage_common,
    line,
    query_grad,
    self_output,
    hidden_in,
    hidden_out,
    class_table,
    query_table,
    slope,
    activ,
    sems,
):
    heads = HEADS // n_head
    width, hidden, classes = heads * HD, FF // n_head, C // n_head
    shards = held.shape[0]
    first_row = first_shard * shard_rows
    starts = borders(n_head)
    move = Moves(sems)
    shards_here = pl.ds(first_shard, shards)
    common_here = move(common.at[pl.ds(0, held_common.shape[0])], held_common)
    weights_here = [move(weights.at[shards_here, g], held.at[:, g]) for g in range(n_head)]
    common_here.wait()
    load_common(stage_common, held_common, valid)
    for j, value in matrix_of(stage_common, 0, DQ, D, line):
        query_table[:, j : j + LANES] = value.astype(low)
    for g in range(n_head):
        weights_here[g].wait()
        load_stage(stage, held, first_shard, shard_rows, g)
        load_matrices(
            stage, first_row, n_head, g, (4, 5, 6, 7), (self_output, hidden_in, hidden_out, class_table), line
        )
    gain_two, gain_three = gains[2:3, :], gains[3:4, :]
    o_heads = {head: unpack(o_self[s]) for s, head in enumerate(heads_of(n_head, o_self.shape[0]))}
    o_groups = [joined_lanes([o_heads[(g, a)] for a in range(heads)]) for g in range(n_head)]
    o_low = jnp.concatenate(o_groups, 1)
    z_two = z_one[...] + product(o_low, self_output[...])
    h_two = layer_norm(z_two, gain_two).astype(low)
    value, bend = gelu_and_slope(product(h_two, hidden_in[...]))
    activ[...] = value.astype(low)
    slope[...] = bend
    z_three = z_two + product(activ[...], hidden_out[...])
    queries_t = out_queries_t[...]
    decoded = layer_norm(z_three, gain_three) + contract_first(queries_t, query_table[...])
    decoded = decoded.astype(low)
    logits = product(decoded, class_table[...])
    label, kind, counted = (my_column(marks, rows) for marks in (labels, modality, labeled))
    lane = lax.broadcasted_iota(jnp.int32, (rows, C), 1).astype(jnp.float32)
    is_target = jnp.where(lane == label, 1.0, 0.0)
    row_top = jnp.max(logits, 1, keepdims=True)
    row_lse = row_top + jnp.log(jnp.sum(jnp.exp2((logits - row_top) * LOG2E), 1, keepdims=True))
    loss = row_lse - jnp.sum(is_target * logits, 1, keepdims=True)
    weight = jnp.zeros((rows, 1), jnp.float32)
    place = lax.broadcasted_iota(jnp.int32, (1, LANES), 1)
    losses = jnp.zeros((1, LANES), jnp.float32)
    for m in range(MODES):
        member = jnp.where((kind == m) & (counted == 1.0), 1.0, 0.0)
        weight = weight + member / jnp.maximum(counts[0:1, m : m + 1], 1.0)
        losses = losses + jnp.where(place == m, jnp.sum(loss * member, 0, keepdims=True), 0.0)
    tile[...] = jnp.broadcast_to(losses, tile.shape)
    dlogits = (weight * (jnp.exp2((logits - row_lse) * LOG2E) - is_target)).astype(low)
    d_decoded = against(dlogits, class_table[...])
    matrix_into(query_grad, 0, product(queries_t, d_decoded.astype(low)), line)
    stored = [move(query_grad, query_grad_out)]
    d_three, gain_three_grad = norm_pullback(z_three, gain_three, d_decoded)
    d_branch = d_three.astype(low)
    d_pre = (slope[...] * against(d_branch, hidden_out[...])).astype(low)
    d_middle, gain_two_grad = norm_pullback(z_two, gain_two, against(d_pre, hidden_in[...]))
    d_two = d_three + d_middle
    d_two_out[...] = d_two
    gain_grads[...] = jnp.concatenate([gain_two_grad, gain_three_grad], 0)
    d_two_low = d_two.astype(low)
    d_o = against(d_two_low, self_output[...]).astype(low)
    for slot, (g, a) in enumerate(heads_of(n_head, o_self.shape[0])):
        dout[slot] = pack(d_o[:, g * width + a * HD : g * width + (a + 1) * HD])
    for g in range(n_head):
        results = (
            contract_first(o_groups[g], d_two_low),
            contract_first(h_two, d_pre[:, g * hidden : (g + 1) * hidden]),
            contract_first(activ[:, g * hidden : (g + 1) * hidden], d_branch),
            contract_first(decoded, dlogits[:, g * classes : (g + 1) * classes]),
        )
        for m, result in zip((4, 5, 6, 7), results):
            matrix_into(stage, starts[m] - first_row, result, line)
        for b in range(shards):
            held[b, g, :shard_rows, :] = stage[pl.ds(b * shard_rows, shard_rows), :].astype(low)
        stored.append(move(held.at[:, g], grads.at[shards_here, g]))
    for copy in stored:
        copy.wait()


def middle(counts, weights, common, z_one, o_self, out_queries_t, marks, gains, valid, n_head, shard_rows):
    rows = z_one.shape[0]
    begin, shards = shards_of(n_head, shard_rows, 4, 8)
    query_rows = DQ * D // LANES
    block, blocks = common_blocks(0, query_rows, valid)
    return pl.pallas_call(
        functools.partial(middle_kernel, n_head, shard_rows, valid, begin, rows),
        grid=(1,),
        out_shape=[
            shape_of(o_self.shape),
            shape_of((rows, D), jnp.float32),
            shape_of((8, LANES), jnp.float32),
            shape_of((query_rows, LANES), jnp.float32),
            shape_of((2, D), jnp.float32),
            shape_of(weights.shape),
        ],
        in_specs=[
            VMEM_SPEC,
            ANY_SPEC,
            ANY_SPEC,
            VMEM_SPEC,
            VMEM_SPEC,
            pl.BlockSpec((DQ, rows), lambda i: (0, lax.axis_index("head"))),
            VMEM_SPEC,
            VMEM_SPEC,
            VMEM_SPEC,
            VMEM_SPEC,
        ],
        out_specs=[VMEM_SPEC] * 3 + [ANY_SPEC, VMEM_SPEC, ANY_SPEC],
        scratch_shapes=[
            pltpu.VMEM((shards,) + weights.shape[1:], low),
            pltpu.VMEM((blocks,) + common.shape[1:], low),
            pltpu.VMEM((shards * shard_rows, LANES), jnp.float32),
            pltpu.VMEM((blocks * valid, LANES), jnp.float32),
            LINE,
            pltpu.VMEM((query_rows, LANES), jnp.float32),
            pltpu.VMEM((D, D), low),
            pltpu.VMEM((D, FF), low),
            pltpu.VMEM((FF, D), low),
            pltpu.VMEM((D, C), low),
            pltpu.VMEM((DQ, D), low),
            pltpu.VMEM((rows, FF), jnp.float32),
            pltpu.VMEM((rows, FF), low),
            pltpu.SemaphoreType.DMA((2 + 2 * n_head,)),
        ],
        compiler_params=pltpu.CompilerParams(vmem_limit_bytes=56 * MIB),
        name="middle",
    )(counts, weights, common, z_one, o_self, out_queries_t, *marks, gains)


def ending_kernel(
    n_head,
    shard_rows,
    valid,
    rows,
    lengths,
    grads_in,
    d_q_self,
    d_kv_self,
    gains,
    gain_grads,
    *refs,
):
    kept_in, (grads, common_grad), kept = refs[:14], refs[14:16], refs[16:30]
    held, stage, stage_common, line, d_q, d_kv, sems = refs[30:]
    (
        d_two,
        query_grad,
        enc_query,
        enc_keyval,
        enc_output,
        self_project,
        z_zero,
        h_zero,
        x_norm_t,
        q_enc,
        kv_enc,
        o_enc,
        z_one,
        h_one,
    ) = kept
    move = Moves(sems)
    first_used = (12, 5, 0, 4, 10, 9, 2, 6, 1, 7, 8, 11, 3, 13)
    loads = {i: move(kept_in[i], kept[i]) for i in first_used}

    def need(*which):
        for i in which:
            loads[i].wait()

    heads = HEADS // n_head
    width = heads * HD
    shards = held.shape[0]
    starts = borders(n_head)
    shared = move(grads_in.at[pl.ds(shards - 1, 1)], held.at[pl.ds(shards - 1, 1)])
    d_heads = {}
    for slot, head in enumerate(heads_of(n_head, d_kv_self.shape[0])):
        d_kv_head = d_kv_self[slot]
        d_heads[head] = (unpack(d_q_self[slot]), d_kv_head[:, :HD], d_kv_head[:, HD:])
    d_projected = [
        jnp.concatenate([d_heads[(g, a)][i] for i in range(3) for a in range(heads)], 1)
        for g in range(n_head)
    ]
    whole = jnp.concatenate(d_projected, 1)
    need(12, 5, 0)
    d_middle, gain_one_grad = norm_pullback(
        z_one[...], gains[1:2, :], against(whole, self_project[...])
    )
    d_one = d_two[...] + d_middle
    d_one_low = d_one.astype(low)
    need(4, 10, 9)
    d_o = against(d_one_low, enc_output[...]).astype(low)
    for g in range(n_head):
        keys = kv_enc[:, 2 * g * width : (2 * g + 1) * width]
        values = kv_enc[:, (2 * g + 1) * width : (2 * g + 2) * width]
        d_key = jnp.zeros(keys.shape, jnp.float32)
        d_value = jnp.zeros(keys.shape, jnp.float32)
        d_query = jnp.zeros((rows, width), jnp.float32)
        for (here, q_head), (unused, do_head) in zip(
            head_lanes(g, heads, q_enc[...]), head_lanes(g, heads, d_o)
        ):
            scores = enc_scores(keys, q_head)
            probs = jnp.exp2((scores - jnp.max(scores, 0, keepdims=True)).astype(low))
            probs = probs.astype(jnp.float32)
            probs = probs / jnp.sum(probs, 0, keepdims=True)
            d_probs = against(values, do_head)
            delta = jnp.sum(probs * d_probs, 0, keepdims=True)
            d_scores = (probs * (d_probs - delta)).astype(low)
            d_value = d_value + product(probs.astype(low), do_head)
            d_key = d_key + product(d_scores, q_head)
            d_query = jnp.where(here, contract_first(d_scores, keys), d_query)
        d_q[:, g * width : (g + 1) * width] = (d_query * SCORE_SCALE).astype(low)
        d_kv[:, 2 * g * width : (2 * g + 1) * width] = (d_key * SCORE_SCALE).astype(low)
        d_kv[:, (2 * g + 1) * width : (2 * g + 2) * width] = d_value.astype(low)
    need(2, 6)
    d_middle, gain_zero_grad = norm_pullback(
        z_zero[...], gains[0:1, :], against(d_q[...], enc_query[...])
    )
    d_zero = d_one + d_middle
    d_zero_top = d_zero.astype(low)
    d_zero_rest = (d_zero - d_zero_top.astype(jnp.float32)).astype(low)
    picked = picked_rows(clip_bounds(lengths), rows, n_head)
    latent_grad = contract_first(picked, d_zero_top) + contract_first(picked, d_zero_rest)
    need(1, 7, 8, 11, 3, 13)
    query_rows = query_grad.shape[0]
    stage_common[:query_rows] = query_grad[...]
    matrix_into(stage_common, query_rows, latent_grad, line)
    all_gains = jnp.concatenate([gain_zero_grad, gain_one_grad, gain_grads[...]], 0)
    matrix_into(stage_common, query_rows + LAT * D // LANES, all_gains, line)
    piece = common_grad.shape[2]
    for b in range(common_grad.shape[0]):
        for k in range(common_grad.shape[1]):
            amount = min(piece, valid - k * piece)
            block = stage_common[b * valid + k * piece : b * valid + k * piece + amount, :]
            if amount < piece:
                block = jnp.concatenate([block, jnp.zeros((piece - amount, LANES), jnp.float32)], 0)
            common_grad[b, k] = block.astype(low)
    shared.wait()
    shared_rows = shards * shard_rows - starts[4]
    stored = []
    for g in range(n_head):
        results = (
            contract_first(h_zero[...], d_q[:, g * width : (g + 1) * width]),
            product(x_norm_t[...], d_kv[:, 2 * g * width : (2 * g + 2) * width]),
            contract_first(o_enc[:, g * width : (g + 1) * width], d_one_low),
            contract_first(h_one[...], d_projected[g]),
        )
        if shared_rows:
            stage[pl.ds((shards - 1) * shard_rows, shard_rows), :] = held[
                shards - 1, g, :shard_rows, :
            ].astype(jnp.float32)
        for m, result in zip((0, 1, 2, 3), results):
            matrix_into(stage, starts[m], result, line)
        for b in range(shards):
            held[b, g, :shard_rows, :] = stage[pl.ds(b * shard_rows, shard_rows), :].astype(low)
        stored.append(move(held.at[:, g], grads.at[pl.ds(0, shards), g]))
    for copy in stored:
        copy.wait()


def ending(lengths, grads, d_self, d_two, gains, gain_grads, query_grad, kept, common_shape, valid, shard_rows):
    rows = d_two.shape[0]
    n_head = grads.shape[1]
    begin, shards = shards_of(n_head, shard_rows, 0, 4)
    kept = (d_two, query_grad) + tuple(kept)
    keys = kept[8].shape[1]
    common_rows = (DQ + LAT + 4) * D // LANES
    return pl.pallas_call(
        functools.partial(ending_kernel, n_head, shard_rows, valid, rows),
        out_shape=[shape_of(grads.shape), shape_of(common_shape)],
        in_specs=[SMEM_SPEC, ANY_SPEC] + [VMEM_SPEC] * 4 + [ANY_SPEC] * len(kept),
        out_specs=[ANY_SPEC, VMEM_SPEC],
        input_output_aliases={1: 0},
        scratch_shapes=[pltpu.VMEM(a.shape, a.dtype) for a in kept]
        + [
            pltpu.VMEM((shards,) + grads.shape[1:], low),
            pltpu.VMEM((shards * shard_rows, LANES), jnp.float32),
            pltpu.VMEM((common_rows, LANES), jnp.float32),
            LINE,
            pltpu.VMEM((rows, D), low),
            pltpu.VMEM((keys, 2 * D), low),
            pltpu.SemaphoreType.DMA((len(kept) + 1 + n_head,)),
        ],
        compiler_params=pltpu.CompilerParams(vmem_limit_bytes=56 * MIB),
        name="ending",
    )(lengths, grads, *d_self, gains, gain_grads, *kept)


def adam_step(weight, first, second, grad):
    first = beta_one * first + (1 - beta_one) * grad
    second = beta_two * second + (1 - beta_two) * grad * grad
    fixed_first = first / (1 - beta_one**STEP)
    fixed_second = second / (1 - beta_two**STEP)
    weight = weight - learn_rate * (
        fixed_first / (jnp.sqrt(fixed_second) + adam_eps) + weight_decay * weight
    )
    return (weight, first, second, weight.astype(low))


def per_device(
    inputs,
    out_queries,
    clip_lengths,
    labels,
    modality,
    labeled,
    head_params,
    head_first,
    head_second,
    common_params,
    common_first,
    common_second,
):
    n_head, n_blk = lax.axis_size("head"), lax.axis_size("blk")
    dims = grid_of(n_blk, n_head)
    rows = labels.shape[0] // n_head
    n_h, n_c = head_params.shape[0], common_params.shape[0]
    shard_rows, common_rows = n_h // LANES, -(-n_c // LANES)
    head_rows = round_up(shard_rows + 1, TILE)
    piece_rows = round_up(-(-common_rows // n_head), TILE)
    marks = [x.reshape(-1, LANES) for x in (labels, modality, labeled)]
    head_wide = head_params.reshape(shard_rows, LANES)
    common_wide = jnp.pad(common_params, (0, common_rows * LANES - n_c)).reshape(common_rows, LANES)
    weights, common = gather_all(dims, marks, (head_wide, common_wide), (head_rows, piece_rows), 0)
    valid = common_rows
    if n_c % LANES:
        common = common.reshape(n_blk, -1)[:, :n_c].reshape(-1, LANES)
        valid = common.shape[0]
        common = jnp.pad(common, ((0, -valid % TILE), (0, 0)))[None, None]

    encoded = encode(
        clip_lengths, weights, common, inputs.T, valid, rows, Team(dims).size, n_head, shard_rows
    )
    gains, z_one, counts = encoded[4], encoded[11], encoded[15]
    o_self, lse_self, out_self_t, q_all, kv_all = attend(
        dims, clip_lengths, encoded[13], encoded[14], 1
    )
    dout, d_two, tile, query_grad, gain_grads, grads = middle(
        counts, weights, common, z_one, o_self, out_queries.T, marks, gains, valid, n_head, shard_rows
    )
    d_self = attend_back(dims, clip_lengths, q_all, kv_all, dout, out_self_t, lse_self, 2)
    kept = encoded[:4] + encoded[5:13]
    grads, common_grad = ending(
        clip_lengths,
        grads,
        d_self,
        d_two,
        gains,
        gain_grads,
        query_grad,
        kept,
        common.shape,
        valid,
        shard_rows,
    )
    if n_c % LANES:
        common_grad = common_grad[0, 0, :valid].reshape(n_blk, n_c)
        common_grad = jnp.pad(common_grad, ((0, 0), (0, n_head * piece_rows * LANES - n_c)))
        common_grad = common_grad.reshape(n_blk, n_head, piece_rows, LANES)
    head_share, common_share, loss_sums, clip_norm, factor = reduce_all(
        dims, (grads, common_grad), (shard_rows, common_rows), tile, 3
    )
    label_counts, loss_sums = encoded[16].reshape(MODES), loss_sums.reshape(MODES)
    clip_norm, factor = clip_norm.reshape(()), factor.reshape(())
    head_share, common_share = head_share.reshape(-1), common_share.reshape(-1)[:n_c]
    head_out = adam_step(head_params, head_first, head_second, head_share * factor)
    common_out = adam_step(common_params, common_first, common_second, common_share * factor)
    return head_out + common_out + (loss_sums, label_counts, clip_norm)


def solution(mesh):
    placed = (
        P("blk", None),
        P("blk", None),
        P(),
        P("blk"),
        P("blk"),
        P("blk"),
        P(("head", "blk")),
        P(("head", "blk")),
        P(("head", "blk")),
        P("blk"),
        P("blk"),
        P("blk"),
    )
    return jax.shard_map(
        per_device,
        mesh=mesh,
        in_specs=placed,
        out_specs=(
            P(("head", "blk")),
            P(("head", "blk")),
            P(("head", "blk")),
            P(("head", "blk")),
            P("blk"),
            P("blk"),
            P("blk"),
            P("blk"),
            P(),
            P(),
            P(),
        ),
        check_vma=False,
    )
```

```python
import functools

import jax
import jax.numpy as jnp
from jax import lax
from jax.experimental import pallas as pl
from jax.experimental.pallas import tpu as pltpu
from jax.sharding import PartitionSpec as P

D = 512
HEADS = 8
HD = 64
FF = 2048
DI = 704
DQ = 1026
C = 704
LAT = 784
MODES = 3
STEP = 10
LANES = 128
TILE = 16

norm_eps = 1e-05
learn_rate = 0.1
beta_one = 0.9
beta_two = 0.999
adam_eps = 1e-08
weight_decay = 0.01
clip_limit = 0.05
big_negative = -1e30
low = jnp.bfloat16
LOG2E = 1.4426950408889634
SCORE_SCALE = HD ** (-0.5)
MESH = pl.DeviceIdType.MESH
MIB = 1 << 20
VMEM_SPEC = pl.BlockSpec(memory_space=pltpu.VMEM)
SMEM_SPEC = pl.BlockSpec(memory_space=pltpu.SMEM)
ANY_SPEC = pl.BlockSpec(memory_space=pl.ANY)


def shape_of(shape, dtype=low):
    return jax.ShapeDtypeStruct(shape, dtype)


def round_up(n, unit):
    return -(-n // unit) * unit


def grid_of(n_blk, n_head):
    cores = 2 if n_head % 2 == 0 else 1
    x = n_head // cores
    y = x if n_blk % x == 0 else 1
    return (n_blk // y, y, x, cores)


def my_place(dims):
    blk, head = lax.axis_index("blk"), lax.axis_index("head")
    return (blk // dims[1], lax.rem(blk, dims[1]), head // dims[3], lax.rem(head, dims[3]))


def shifted(dims, me, offset, sign):
    return tuple(
        m if o == 0 else lax.rem(m + (o if sign > 0 else n - o), n)
        for m, o, n in zip(me, offset, dims)
    )


def blk_of(dims, place):
    return place[0] * dims[1] + place[1]


def head_of(dims, place):
    return place[2] * dims[3] + place[3]


def device_of(dims, place):
    return {"blk": blk_of(dims, place), "head": head_of(dims, place)}


def along(axis, d):
    return tuple(d if a == axis else 0 for a in range(4))


def greet(dims, me, offsets):
    barrier = pltpu.get_barrier_semaphore()
    for offset in offsets:
        pl.semaphore_signal(
            barrier,
            inc=1,
            device_id=device_of(dims, shifted(dims, me, offset, 1)),
            device_id_type=MESH,
        )
    pl.semaphore_wait(barrier, len(offsets))


def axis_peers(dims, axes):
    return [along(axis, d) for axis in axes for d in range(1, dims[axis])]


def remote(src, dst, send_sem, recv_sem, place, dims):
    return pltpu.make_async_remote_copy(
        src_ref=src,
        dst_ref=dst,
        send_sem=send_sem,
        recv_sem=recv_sem,
        device_id=device_of(dims, place),
        device_id_type=MESH,
    )


AHEAD = 6.0
RING = 0


def in_order(first, follow, size_of, ahead, result):
    queues, busy, flight = {}, {}, {}
    now = 0.0

    def ready(messages):
        for message in messages:
            queues.setdefault(message[1], []).append(message)

    ready(first)
    while True:
        for axis in sorted(queues):
            queue, going = queues[axis], flight.setdefault(axis, [])
            while queue and (not going or busy[axis] < now + ahead):
                message = min(queue)
                queue.remove(message)
                busy[axis] = max(now, busy.get(axis, 0.0)) + size_of(message)
                going.append((busy[axis] + 1.5, message))
                result.append((True, message))
        arrivals = [min(going) for going in flight.values() if going]
        if not arrivals:
            return now
        arrival = min(arrivals)
        flight[arrival[1][1]].remove(arrival)
        now = max(now, arrival[0])
        result.append((False, arrival[1]))
        ready(follow(arrival[1]))


def time_of(rows, axis):
    return rows * LANES * 2 / (300e3 if axis == 3 else 45e3)


def with_at(offset, axis, d):
    return offset[:axis] + (d,) + offset[axis + 1 :]


def gather_order(dims, parts):
    def onward(p, offset, position):
        order = parts[p][3]
        result = []
        for k in range(max(position, 0), 4):
            axis = order[k]
            n = dims[axis]
            if k > position:
                steps = [1] if axis == RING else range(1, n)
                steps = [d for d in steps if d < n]
            else:
                steps = [offset[axis] + 1] if axis == RING and offset[axis] + 1 < n else []
            for d in steps:
                result.append(((k, sum(offset), p), axis, p, with_at(offset, axis, d)))
        return result

    def follow(message):
        rank, axis, p, offset = message
        return onward(p, offset, rank[0])

    first = [m for p in range(len(parts)) for m in onward(p, (0, 0, 0, 0), -1)]
    result = []
    now = in_order(first, follow, lambda m: time_of(parts[m[2]][2], m[1]), AHEAD, result)
    return result, now


def gather_kernel(
    dims,
    parts,
    labels,
    modality,
    labeled,
    head_params,
    common_params,
    head_all,
    common_all,
    head_low,
    common_low,
    common_wide,
    send_sem,
    recv_sem,
    own_sem,
):
    me = my_place(dims)
    my_head = head_of(dims, me)
    n_head = dims[2] * dims[3]
    shard_rows, common_rows = head_params.shape[0], common_params.shape[0]
    per_head = labels.shape[0] // n_head
    row = lax.broadcasted_iota(jnp.int32, labels.shape, 0)
    mine = (row >= my_head * per_head) & (row < (my_head + 1) * per_head) & (labeled[...] == 1)
    lane = lax.broadcasted_iota(jnp.int32, (1, LANES), 1)
    counts = jnp.zeros((1, LANES), jnp.float32)
    for m in range(MODES):
        member = jnp.where(mine & (modality[...] == m), 1.0, 0.0)
        counts = counts + jnp.where(lane == m, jnp.sum(member, (0, 1), keepdims=True), 0.0)
    padding = head_low.shape[0] - shard_rows
    tail = shard_rows // TILE * TILE
    head_low[:tail] = head_params[:tail].astype(low)
    last = [jnp.broadcast_to(counts, (padding, LANES))]
    if shard_rows > tail:
        last = [head_params[tail:]] + last
    head_low[tail:] = jnp.concatenate(last, 0).astype(low)
    common_wide[...] = jnp.zeros(common_wide.shape, jnp.float32)
    common_wide[:common_rows] = common_params[...]
    piece = common_low.shape[0]
    common_low[...] = common_wide[pl.ds(pl.multiple_of(my_head * piece, TILE), piece)].astype(low)

    greet(dims, me, ring_and_others(dims))
    srcs, outs = (head_low, common_low), (head_all, common_all)
    copies = {}

    def block(p, offset):
        place = shifted(dims, me, offset, -1)
        array, first, rows, order = parts[p]
        return outs[array].at[blk_of(dims, place), head_of(dims, place), pl.ds(first, rows)]

    own = []
    for is_send, (rank, axis, p, offset) in gather_order(dims, parts)[0]:
        if is_send:
            step = 1 if axis == RING else offset[axis]
            before = with_at(offset, axis, offset[axis] - step)
            array, first, rows, order = parts[p]
            source = block(p, before) if any(before) else srcs[array].at[pl.ds(first, rows)]
            i = len(copies)
            copies[(p, offset)] = remote(
                source,
                block(p, before),
                send_sem.at[i],
                recv_sem.at[i],
                shifted(dims, me, along(axis, step), 1),
                dims,
            )
            copies[(p, offset)].start()
        else:
            if not own:
                for array in range(2):
                    copy = pltpu.make_async_copy(
                        srcs[array], outs[array].at[blk_of(dims, me), my_head], own_sem.at[array]
                    )
                    copy.start()
                    own.append(copy)
            copies[(p, offset)].wait_recv()
    for copy in copies.values():
        copy.wait_send()
    for copy in own:
        copy.wait()


def ring_and_others(dims):
    ring = {along(RING, 1 % dims[RING]), along(RING, (dims[RING] - 1) % dims[RING])}
    return sorted(ring - {(0, 0, 0, 0)}) + axis_peers(dims, (1, 2, 3))


def cut(array, rows, shares):
    result = []
    first, so_far = 0, 0
    whole = sum(share for share, order in shares)
    for share, order in shares:
        so_far += share
        end = rows * so_far // whole // TILE * TILE if so_far < whole else rows
        if end > first:
            result.append((array, first, end - first, order))
        first = end
    return tuple(result)


ZYXC, ZXYC, YXZC, XYZC = (0, 1, 2, 3), (0, 2, 1, 3), (1, 2, 0, 3), (2, 1, 0, 3)
HEAD_SHARES = ((15, ZYXC), (13, ZXYC), (4, YXZC), (5, XYZC))
COMMON_SHARES = ((1, ZYXC), (1, ZXYC))


def gather_all(dims, marks, params, rows, collective_id):
    z, y, x, cores = dims
    parts = cut(0, rows[0], HEAD_SHARES) + cut(1, rows[1], COMMON_SHARES)
    count = len(parts) * (z * y * x * cores - 1)
    return pl.pallas_call(
        functools.partial(gather_kernel, dims, parts),
        out_shape=[shape_of((z * y, x * cores, n, LANES)) for n in rows],
        in_specs=[VMEM_SPEC] * 5,
        out_specs=[ANY_SPEC] * 2,
        scratch_shapes=[pltpu.VMEM((n, LANES), low) for n in rows]
        + [
            pltpu.VMEM((x * cores * rows[1], LANES), jnp.float32),
            pltpu.SemaphoreType.DMA((count,)),
            pltpu.SemaphoreType.DMA((count,)),
            pltpu.SemaphoreType.DMA((2,)),
        ],
        compiler_params=pltpu.CompilerParams(collective_id=collective_id, has_side_effects=True),
        name="gather_weights",
    )(*marks, *params)


def reduce_order(dims, parts):
    ready, arrived, order = set(), set(), []

    def message(p, position, offset):
        z = offset[RING]
        rank = (dims[RING] - z if z else dims[RING], position, tuple(-o for o in offset), p)
        return (rank, parts[p][3][position], p, position, offset)

    def done(p, position, offset):
        ready.add((p, position, offset))
        if position == 4:
            return []
        axis = parts[p][3][position]
        d = offset[axis]
        first = d != 0 and (axis != RING or d == dims[axis] - 1)
        return ([message(p, position, offset)] if first else []) + advance(p, position, offset)

    def advance(p, position, offset):
        axis = parts[p][3][position]
        n = dims[axis]
        start = with_at(offset, axis, 0)
        if axis == RING:
            here = (p, position, offset)
            if here in ready and here in arrived:
                order.append((None, here))
                if offset[axis]:
                    return [message(p, position, offset)]
                return done(p, position + 1, offset)
        elif (p, position, start) in ready and (p, position + 1, start) not in ready:
            if all((p, position, with_at(start, axis, d)) in arrived for d in range(1, n)):
                order.append((None, (p, position, start)))
                return done(p, position + 1, start)
        return []

    def follow(sent):
        rank, axis, p, position, offset = sent
        here = with_at(offset, axis, offset[axis] - 1) if axis == RING else offset
        arrived.add((p, position, here))
        return advance(p, position, here)

    first = []
    for p in range(len(parts)):
        for offset in all_offsets(dims, range(4)):
            first += done(p, 0, offset)
    now = in_order(first, follow, lambda m: time_of(parts[m[2]][2], m[1]), AHEAD, order)
    return order, now


def all_offsets(dims, axes):
    offsets = [(0, 0, 0, 0)]
    for a in axes:
        offsets = [with_at(o, a, d) for o in offsets for d in range(dims[a])]
    return offsets


def reduce_kernel(dims, parts, *refs):
    srcs, tile = refs[:2], refs[2]
    head_out, common_out, losses, norm, factor = refs[3:8]
    places = len(parts) * 4
    buffers = refs[8 : 8 + places]
    head_sum, common_sum, shares, send_sem, recv_sem, near_tiles, far_tiles = refs[8 + places : 15 + places]
    held, held_sem = refs[15 + places : 17 + places], refs[17 + places]
    sums = (head_sum, common_sum)
    me = my_place(dims)
    z, y, x, cores = dims
    loads = [
        pltpu.make_async_copy(srcs[k].at[:, :, me[3]], held[k], held_sem.at[k]) for k in range(2)
    ]
    for load in loads:
        load.start()
    across = peers_across(dims)
    others = [o for o in all_offsets(dims, (0, 1)) if any(o)]
    met = ring_and_others(dims)
    greet(dims, me, met + [o for o in across + others if o not in met])
    push = Pushes(dims, me, send_sem, recv_sem)
    copies = {}

    def slot(p, position, offset):
        order = parts[p][3]
        axis = order[position]
        rest = [o for o in all_offsets(dims, order[position + 1 :])]
        k = rest.index(with_at(offset, axis, 0))
        return buffers[p * 4 + position].at[k, max(offset[axis] - 1, 0)]

    def summed(p, position, offset):
        array, first, rows, order = parts[p]
        if position == 0:
            place = shifted(dims, me, offset, 1)
            at = (blk_of(dims, place), place[2])
            if offset[3]:
                return srcs[array].at[(*at, place[3], pl.ds(first, rows))]
            if loads[array] is not None:
                loads[array].wait()
                loads[array] = None
            return held[array].at[(*at, pl.ds(first, rows))]
        return slot(p, position - 1, offset)

    def ring_slot(p, position, offset):
        axis = parts[p][3][position]
        return slot(p, position, with_at(offset, axis, offset[axis] + 1))

    def add(p, position, offset):
        array, first, rows, order = parts[p]
        axis = order[position]
        if axis == RING:
            arrivals = [ring_slot(p, position, offset)]
        else:
            arrivals = [slot(p, position, with_at(offset, axis, d)) for d in range(1, dims[axis])]
        mine = summed(p, position, offset)
        step = row_chunk(rows)

        @pl.loop(0, rows // step)
        def some_rows(n):
            at = pl.ds(pl.multiple_of(n * step, step), step)
            last = position == 3 and not any(offset)
            if len(arrivals) == 1 and not last:
                arrivals[0][at] = mine[at] + arrivals[0][at]
                return
            total = mine[at].astype(jnp.float32)
            for arrival in arrivals:
                total = total + arrival[at].astype(jnp.float32)
            if last:
                sums[array][pl.ds(pl.multiple_of(first + n * step, TILE), step)] = total
            else:
                arrivals[0][at] = total.astype(low)

    for is_send, what in reduce_order(dims, parts)[0]:
        if is_send is None:
            add(*what)
        elif is_send:
            rank, axis, p, position, offset = what
            d = offset[axis]
            started = axis != RING or d == dims[axis] - 1
            source = summed(p, position, offset) if started else ring_slot(p, position, offset)
            step = along(axis, 1 if axis == RING else d)
            copies[what] = push(source, slot(p, position, offset), step)
        else:
            copies[what].wait_recv()
    my_head, my_blk = head_of(dims, me), blk_of(dims, me)
    shares[my_head] = common_sum[...].astype(low)
    share_copies = [push(shares.at[my_head], shares.at[my_head], o) for o in across]
    amount = head_out.shape[0]
    head_out[...] = head_sum[:amount]
    squares = jnp.sum(head_sum[:amount] * head_sum[:amount], 0, keepdims=True)
    squares = squares + jnp.sum(common_sum[...] * common_sum[...], 0, keepdims=True)
    lane = lax.broadcasted_iota(jnp.int32, (1, LANES), 1)
    near_tiles[my_head] = tile[...] + jnp.where(
        lane == MODES, jnp.sum(squares, 1, keepdims=True), 0.0
    )
    near = [push(near_tiles.at[my_head], near_tiles.at[my_head], o) for o in across]
    for copy in near:
        copy.wait_recv()
    far_tiles[my_blk] = jnp.sum(near_tiles[...], 0)
    far = [push(far_tiles.at[my_blk], far_tiles.at[my_blk], o) for o in others]
    for copy in share_copies:
        copy.wait_recv()
    piece = shares.shape[1]
    for k in range(x * cores):
        amount = min(piece, common_out.shape[0] - k * piece)
        common_out[k * piece : k * piece + amount] = shares[k].astype(jnp.float32)[:amount]
    for copy in far:
        copy.wait_recv()
    totals = jnp.sum(far_tiles[...], 0)[:1]
    losses[...] = totals[:, :MODES]
    norm[...] = jnp.sqrt(totals[:, MODES : MODES + 1])
    factor[...] = jnp.minimum(1.0, clip_limit / norm[...])
    push.finish()


def row_chunk(rows):
    for count in (4, 3, 2):
        if rows % (count * TILE) == 0:
            return rows // count
    return rows


def reduce_all(dims, arrays, valid, tile, collective_id):
    z, y, x, cores = dims
    rows = [array.shape[2] for array in arrays]
    arrays = [array.reshape(z * y, x, cores, *array.shape[2:]) for array in arrays]
    parts = ()
    for array, shares in enumerate((HEAD_SHARES, COMMON_SHARES)):
        parts += cut(array, rows[array], [(share, order[::-1]) for share, order in shares])
    scratch = []
    for array, first, amount, order in parts:
        for position, axis in enumerate(order):
            rest = len(all_offsets(dims, order[position + 1 :]))
            scratch.append(pltpu.VMEM((rest, dims[axis] - 1, amount, LANES), low))
    count = len(parts) * (z * y * x * cores - 1) + 2 * (x * cores - 1) + z * y - 1
    return pl.pallas_call(
        functools.partial(reduce_kernel, dims, parts),
        out_shape=[
            shape_of((valid[0], LANES), jnp.float32),
            shape_of((valid[1], LANES), jnp.float32),
            shape_of((1, MODES), jnp.float32),
            shape_of((1, 1), jnp.float32),
            shape_of((1, 1), jnp.float32),
        ],
        in_specs=[ANY_SPEC] * 2 + [VMEM_SPEC],
        out_specs=[VMEM_SPEC] * 5,
        scratch_shapes=scratch
        + [pltpu.VMEM((n, LANES), jnp.float32) for n in rows]
        + [
            pltpu.VMEM((x * cores, rows[1], LANES), low),
            pltpu.SemaphoreType.DMA((count,)),
            pltpu.SemaphoreType.DMA((count,)),
            pltpu.VMEM((x * cores, 8, LANES), jnp.float32),
            pltpu.VMEM((z * y, 8, LANES), jnp.float32),
        ]
        + [pltpu.VMEM((z * y, x, n, LANES), low) for n in rows]
        + [pltpu.SemaphoreType.DMA((2,))],
        compiler_params=pltpu.CompilerParams(
            collective_id=collective_id, has_side_effects=True, vmem_limit_bytes=60 * MIB
        ),
        name="reduce_gradients",
    )(*arrays, tile)


def contract_first(a, b):
    return lax.dot_general(a, b, (((0,), (0,)), ((), ())), preferred_element_type=jnp.float32)


def product(a, b):
    return jnp.dot(a, b, preferred_element_type=jnp.float32)


def against(a, b):
    return lax.dot_general(a, b, (((1,), (1,)), ((), ())), preferred_element_type=jnp.float32)


def clip_bounds(lengths):
    result, first = [], 0
    for clip in range(lengths.shape[0]):
        end = first + lengths[clip]
        result.append((first, end))
        first = end
    return result


def clip_borders(bounds, place):
    opening = jnp.zeros(place.shape, jnp.int32)
    ending = jnp.full(place.shape, 1 << 30, jnp.int32)
    for clip, (begin, end) in enumerate(bounds):
        here = place == clip
        opening = jnp.where(here, begin, opening)
        ending = jnp.where(here, end, ending)
    return opening, ending


def low_half(axis):
    return lax.broadcasted_iota(jnp.int32, (1, LANES) if axis else (LANES, 1), axis) < HD


def with_key_tail(bounds, first_row, kv):
    clips = len(bounds)
    place = lax.broadcasted_iota(jnp.int32, (1, LANES), 1) - HD
    opening, ending = clip_borders(bounds, place)
    ones = jnp.where((place >= clips) & (place < clips + 3), 1.0, 0.0)
    row = first_row + lax.broadcasted_iota(jnp.int32, kv.shape, 0)
    tail = jnp.where((row >= opening) & (row < ending), ones, big_negative)
    return jnp.where(low_half(1), kv.astype(jnp.float32), tail).astype(low)


def with_value_tail(kv):
    place = lax.broadcasted_iota(jnp.int32, (1, LANES), 1)
    ones = jnp.where(place < 3, 1.0, 0.0)
    return jnp.where(low_half(1), ones, kv.astype(jnp.float32)).astype(low)


def in_three(place, value):
    top = value.astype(low).astype(jnp.float32)
    middle = (value - top).astype(low).astype(jnp.float32)
    bottom = value - top - middle
    return (
        jnp.where(place == 0, top, 0.0)
        + jnp.where(place == 1, middle, 0.0)
        + jnp.where(place == 2, bottom, 0.0)
    )


def with_query_tail(bounds, first_row, rows, extra):
    clips = len(bounds)
    place = lax.broadcasted_iota(jnp.int32, (HD, 1), 0)
    opening, ending = clip_borders(bounds, place)
    row = first_row + lax.broadcasted_iota(jnp.int32, (1, rows.shape[1]), 1)
    inside = (place < clips) & (row >= opening) & (row < ending)
    tail = jnp.where(inside, 1.0, 0.0)
    if extra is not None:
        tail = tail + in_three(place - clips, -extra)
    return jnp.concatenate([rows * (SCORE_SCALE * LOG2E), tail], 0).astype(low)


def pack(rows):
    half = rows.shape[0] // 2
    return jnp.concatenate([rows[:half], rows[half:]], 1)


def unpack(packed):
    return jnp.concatenate([packed[:, :HD], packed[:, HD:]], 0)


def unpack_t(packed):
    turned = packed.astype(jnp.float32).T
    return jnp.concatenate([turned[:HD], turned[HD:]], 1)


def pack_t(columns):
    half = columns.shape[1] // 2
    return jnp.concatenate([columns[:, :half], columns[:, half:]], 0).T


class Team:
    def __init__(self, dims):
        z, y, x, cores = dims
        self.dims = dims
        self.wide = HEADS // (x * cores) == y
        self.size = x * cores * (y if self.wide else 1)
        self.groups = z if self.wide else z * y
        axes = (1, 2, 3) if self.wide else (2, 3)
        offsets = [o for o in all_offsets(dims, axes) if any(o)]
        self.others = sorted(offsets, key=lambda o: (o[1] + o[2], o))
        self.sides = [] if self.wide else axis_peers(dims, (1,))

    def slot(self, place):
        head = head_of(self.dims, place)
        return place[1] * self.dims[2] * self.dims[3] + head if self.wide else head

    def group(self, place):
        return place[0] if self.wide else blk_of(self.dims, place)


def heads_of(n_head, slots):
    return [(s % n_head, s // n_head) for s in range(slots)]


class Pushes:
    def __init__(self, dims, me, send_sem, recv_sem):
        self.dims, self.me, self.send_sem, self.recv_sem = dims, me, send_sem, recv_sem
        self.started = []

    def later(self, src, dst, offset):
        i = len(self.started)
        place = shifted(self.dims, self.me, offset, 1)
        copy = remote(src, dst, self.send_sem.at[i], self.recv_sem.at[i], place, self.dims)
        self.started.append(copy)
        return copy

    def __call__(self, src, dst, offset):
        copy = self.later(src, dst, offset)
        copy.start()
        return copy

    def finish(self):
        for copy in self.started:
            copy.wait_send()


def peers_across(dims):
    z, y, x, cores = dims
    across = [(0, 0, a, c) for a in range(x) for c in range(cores) if (a, c) != (0, 0)]
    return sorted(across, key=lambda o: (o[2] == 0, o[3]))


def attend_kernel(
    team,
    query_step,
    key_step,
    pieces,
    lengths,
    q_in,
    kv_in,
    o_out,
    lse,
    out_t,
    q_all,
    kv_out,
    kv_all,
    even_keys,
    even_values_t,
    odd_keys,
    odd_values_t,
    queries,
    top,
    accum,
    even_scores,
    odd_scores,
    even_top,
    odd_top,
    o_mine,
    send_sem,
    recv_sem,
    own_sem,
):
    dims = team.dims
    z = dims[0]
    me = my_place(dims)
    bounds = clip_bounds(lengths)
    rows = kv_in.shape[1]
    amount = team.size * rows
    slots = team.size // pieces
    my_group, my_slot = team.group(me), team.slot(me)
    ring_ends = sorted({along(0, 1 % z), along(0, (z - 1) % z)} - {(0, 0, 0, 0)})
    greet(dims, me, team.others + ring_ends + team.sides)
    push = Pushes(dims, me, send_sem, recv_sem)
    own_kv = pltpu.make_async_copy(kv_in.at[my_slot], kv_all.at[my_group, my_slot], own_sem.at[0])
    own_q = pltpu.make_async_copy(q_in.at[my_slot], q_all.at[my_slot], own_sem.at[1])
    own_kv.start()
    own_q.start()

    def to_team(src, dst, o):
        return push(src.at[team.slot(shifted(dims, me, o, 1))], dst, o)

    kv_copies = {o: to_team(kv_in, kv_all.at[my_group, my_slot], o) for o in team.others}
    q_copies = [to_team(q_in, q_all.at[my_slot], o) for o in team.others]
    ring, side, slot_copies = {}, {}, []

    def group_at(offset):
        return team.group(shifted(dims, me, offset, -1))

    def send_slot(o):
        if z > 1:
            block = kv_all.at[my_group, team.slot(shifted(dims, me, o, -1))]
            slot_copies.append(push(block, block, along(0, 1)))

    def slot_arrived():
        for copy in slot_copies:
            copy.wait_recv()

    def send_on(s, piece):
        block = kv_all.at[group_at(along(0, s)), pl.ds(piece * slots, slots)]
        if 0 < s < z - 1:
            ring[(s + 1, piece)] = push(block, block, along(0, 1))
        for o in team.sides:
            side[(s, o, piece)] = push(block, block, o)

    def both(now, later):
        if now is not None:
            n, unused, now_values, now_scores, now_top = now
            at = tile(n)
            old = top[:, at]
            new = jnp.maximum(old, jnp.max(now_top[...], 0, keepdims=True))
            top[:, at] = new
            total = accum[:, at] * jnp.exp2(old - new)
        if later is not None:
            n, later_keys, unused, later_scores, later_top = later
            query = queries[:, tile(n)]
            highest = jnp.full(later_top.shape, -1e38, jnp.float32)
        for k in range(0, slots * rows, key_step):
            if later is not None:
                scores = product(later_keys[k : k + key_step, :], query)
                later_scores[k : k + key_step, :] = scores
                highest = jnp.maximum(
                    highest, jnp.max(scores.reshape(key_step // 8, 8, query_step), 0)
                )
            if now is not None:
                probs = jnp.exp2((now_scores[k : k + key_step, :] - new).astype(low))
                total = total + product(now_values[:, k : k + key_step], probs)
        if later is not None:
            later_top[...] = highest
        if now is not None:
            accum[:, at] = total

    def tile(n):
        return pl.ds(pl.multiple_of(n * query_step, query_step), query_step)

    computed, pending = [], [None]

    def compute(offset, piece):
        group = group_at(offset)
        keys, values_t = sides_of_keys[len(computed) % 2]
        computed.append(offset)

        @pl.loop(0, slots)
        def build(n):
            at = pl.ds(pl.multiple_of(n * rows, rows), rows)
            slot = piece * slots + n
            block = kv_all[group, slot]
            keys[at, :] = with_key_tail(bounds, group * amount + slot * rows, block)
            values_t[:HD, at] = block.astype(jnp.float32).T[HD:].astype(low)

        def even(n):
            return (n, keys, values_t, even_scores, even_top)

        def odd(n):
            return (n, keys, values_t, odd_scores, odd_top)

        tiles = amount // query_step
        both(pending[0], even(0))

        @pl.loop(0, tiles // 2 - 1)
        def query_blocks(n):
            both(even(2 * n), odd(2 * n + 1))
            both(odd(2 * n + 1), even(2 * n + 2))

        both(even(tiles - 2), odd(tiles - 1))
        pending[0] = odd(tiles - 1)

    sides_of_keys = ((even_keys, even_values_t), (odd_keys, odd_values_t))
    for unused, values_t in sides_of_keys:
        values_t[HD:, :] = jnp.ones((TILE, slots * rows), low)
    top[...] = jnp.full(top.shape, -1e38, jnp.float32)
    accum[...] = jnp.zeros(accum.shape, jnp.float32)
    own_kv.wait()
    send_slot((0, 0, 0, 0))
    for o in team.others:
        kv_copies[o].wait_recv()
        send_slot(o)
    for piece in range(pieces):
        send_on(0, piece)
    own_q.wait()
    for copy in q_copies:
        copy.wait_recv()
    for n in range(team.size):
        queries[:, n * rows : (n + 1) * rows] = with_query_tail(
            bounds, my_group * amount + n * rows, unpack_t(q_all[n]), None
        )
    stores = []

    def store(offset):
        group = group_at(offset)
        copy = pltpu.make_async_copy(kv_all.at[group], kv_out.at[group], own_sem.at[3 + len(stores)])
        copy.start()
        stores.append(copy)

    for s in range(z):
        store(along(0, s))
        for piece in range(pieces):
            compute(along(0, s), piece)
            if s < z - 1:
                if s:
                    ring[(s + 1, piece)].wait_recv()
                elif piece == 0:
                    slot_arrived()
                send_on(s + 1, piece)
            for o in team.sides:
                side[(s, o, piece)].wait_recv()
                compute((s, o[1], 0, 0), piece)
        for o in team.sides:
            store((s, o[1], 0, 0))
    both(pending[0], None)
    total = accum[HD : HD + 1, :]
    out_t[...] = accum[:HD, :] / total
    lse[...] = top[...] + jnp.log(total) * LOG2E
    for n in range(team.size):
        o_mine[n] = pack_t(out_t[:, n * rows : (n + 1) * rows]).astype(low)
    o_copies = [to_team(o_mine, o_out.at[my_slot], o) for o in team.others]
    own_o = pltpu.make_async_copy(o_mine.at[my_slot], o_out.at[my_slot], own_sem.at[2])
    own_o.start()
    own_o.wait()
    for copy in o_copies:
        copy.wait_recv()
    for copy in stores:
        copy.wait()
    push.finish()


def attend(dims, lengths, q, kv, collective_id):
    team = Team(dims)
    z = dims[0]
    amount = team.size * kv.shape[1]
    pieces, query_step = 2, 256
    count = 4 * team.size + pieces * (z + z * len(team.sides))
    return pl.pallas_call(
        functools.partial(attend_kernel, team, query_step, 256, pieces),
        out_shape=(
            jax.ShapeDtypeStruct(q.shape, low),
            jax.ShapeDtypeStruct((1, amount), jnp.float32),
            jax.ShapeDtypeStruct((HD, amount), jnp.float32),
            jax.ShapeDtypeStruct(q.shape, low),
            jax.ShapeDtypeStruct((team.groups,) + kv.shape, low),
        ),
        in_specs=[SMEM_SPEC, VMEM_SPEC, VMEM_SPEC],
        out_specs=[VMEM_SPEC] * 4 + [ANY_SPEC],
        scratch_shapes=[
            pltpu.VMEM((team.groups,) + kv.shape, low),
            pltpu.VMEM((amount // pieces, LANES), low),
            pltpu.VMEM((HD + TILE, amount // pieces), low),
            pltpu.VMEM((amount // pieces, LANES), low),
            pltpu.VMEM((HD + TILE, amount // pieces), low),
            pltpu.VMEM((LANES, amount), low),
            pltpu.VMEM((1, amount), jnp.float32),
            pltpu.VMEM((HD + TILE, amount), jnp.float32),
            pltpu.VMEM((amount // pieces, query_step), jnp.float32),
            pltpu.VMEM((amount // pieces, query_step), jnp.float32),
            pltpu.VMEM((8, query_step), jnp.float32),
            pltpu.VMEM((8, query_step), jnp.float32),
            pltpu.VMEM(q.shape, low),
            pltpu.SemaphoreType.DMA((count,)),
            pltpu.SemaphoreType.DMA((count,)),
            pltpu.SemaphoreType.DMA((3 + team.groups,)),
        ],
        compiler_params=pltpu.CompilerParams(
            collective_id=collective_id, has_side_effects=True, vmem_limit_bytes=56 * MIB
        ),
        name="attend",
    )(lengths, q, kv)


def attend_back_kernel(
    team,
    key_step,
    query_step,
    pieces,
    lengths,
    q_all,
    kv_in,
    do_in,
    out_t,
    lse,
    d_q_out,
    d_kv_out,
    kv_all,
    do_all,
    even_keys_t,
    even_values_t,
    even_rows,
    odd_keys_t,
    odd_values_t,
    odd_rows,
    queries,
    douts,
    d_q_sum,
    q_rows,
    do_rows,
    even_probs,
    odd_probs,
    even_scores,
    odd_scores,
    side_out,
    side_in,
    ring_out,
    ring_in,
    mine,
    d_q_mine,
    d_kv_mine,
    send_sem,
    recv_sem,
    own_sem,
):
    dims = team.dims
    z = dims[0]
    me = my_place(dims)
    bounds = clip_bounds(lengths)
    rows = kv_all.shape[2]
    amount = team.size * rows
    loads = {}
    for s in range(1, z + 1):
        for o in team.sides + [(0, 0, 0, 0)]:
            offset = ((z - s) % z, o[1], 0, 0)
            group = team.group(shifted(dims, me, offset, 1))
            loads[offset] = pltpu.make_async_copy(
                kv_in.at[group], kv_all.at[group], own_sem.at[3 + len(loads)]
            )
            loads[offset].start()
    slots = team.size // pieces
    piece_rows = slots * rows
    my_group, my_slot = team.group(me), team.slot(me)
    ring_ends = sorted({along(0, 1 % z), along(0, (z - 1) % z)} - {(0, 0, 0, 0)})
    greet(dims, me, team.others + ring_ends + team.sides)
    push = Pushes(dims, me, send_sem, recv_sem)

    def to_team(src, dst, o):
        return push(src.at[team.slot(shifted(dims, me, o, 1))], dst, o)

    do_copies = [to_team(do_in, do_all.at[my_slot], o) for o in team.others]
    own_do = pltpu.make_async_copy(do_in.at[my_slot], do_all.at[my_slot], own_sem.at[0])
    own_do.start()
    place = lax.broadcasted_iota(jnp.int32, (HD, 1), 0)
    for n in range(team.size):
        at = slice(n * rows, (n + 1) * rows)
        q_t = unpack_t(q_all[n])
        extended = with_query_tail(bounds, my_group * amount + n * rows, q_t, lse[:, at])
        queries[at, :] = extended.astype(jnp.float32).T.astype(low)
        q_rows[:, at] = (q_t * SCORE_SCALE).astype(low)
    d_q_sum[...] = jnp.zeros(d_q_sum.shape, jnp.float32)
    own_do.wait()
    for copy in do_copies:
        copy.wait_recv()
    for n in range(team.size):
        at = slice(n * rows, (n + 1) * rows)
        do_t = unpack_t(do_all[n])
        delta = jnp.sum(do_t * out_t[:, at], 0, keepdims=True)
        extended = jnp.concatenate([in_three(place, -delta), do_t], 0).astype(low)
        douts[at, :] = extended.astype(jnp.float32).T.astype(low)
        do_rows[:, at] = do_t.astype(low)

    def both(now, later):
        if now is not None:
            n, (unused, unused, now_rows), now_probs, now_scores, target = now
            now_at = rows_of(n)
        if later is not None:
            n, (keys_t, values_t, unused), later_probs, later_scores, unused = later
            at = rows_of(n)
        for first in range(0, amount, query_step):
            part = slice(first, first + query_step)
            if later is not None:
                probs = jnp.exp2(product(queries[part, :], keys_t[:, at]).astype(low))
                d_probs = product(douts[part, :], values_t[:, at])
                later_probs[part, :] = probs
                later_scores[part, :] = (probs.astype(jnp.float32) * d_probs).astype(low)
            if now is not None:
                if first == 0:
                    d_value = product(do_rows[...], now_probs[...])
                if first == amount // 2:
                    d_key = product(q_rows[...], now_scores[...])
                d_q_sum[part, :] = d_q_sum[part, :] + product(now_scores[part, :], now_rows[now_at, :])
        if now is not None:
            target[now_at, :] = jnp.concatenate([d_key, d_value], 0).T.astype(target.dtype)

    def rows_of(k):
        return slice(k * key_step, (k + 1) * key_step)

    computed, pending = [], []

    def flush(later=None):
        if pending:
            now, after = pending.pop()
            both(now, later)
            after()
        elif later is not None:
            both(None, later)

    def compute(offset, piece, target, after):
        group = team.group(shifted(dims, me, offset, 1))
        keys = sides_of_keys[len(computed) % 2]
        computed.append(offset)
        if offset in loads:
            loads.pop(offset).wait()

        @pl.loop(0, slots)
        def build(n):
            at = pl.ds(pl.multiple_of(n * rows, rows), rows)
            slot = piece * slots + n
            block = kv_all[group, slot]
            extended = with_key_tail(bounds, group * amount + slot * rows, block)
            keys[0][:, at] = extended.astype(jnp.float32).T.astype(low)
            keys[1][:, at] = with_value_tail(block).astype(jnp.float32).T.astype(low)
            keys[2][at, :] = block

        steps = [
            (k, keys) + ((odd_probs, odd_scores) if k % 2 else (even_probs, even_scores)) + (target,)
            for k in range(piece_rows // key_step)
        ]
        flush(steps[0])
        for now, later in zip(steps[:-1], steps[1:]):
            both(now, later)
        pending.append((steps[-1], after))

    sides_of_keys = (
        (even_keys_t, even_values_t, even_rows),
        (odd_keys_t, odd_values_t, odd_rows),
    )
    side, ring = {}, {}

    def send_sides(s, piece):
        for o in team.sides:
            target = side_out.at[s - 1, o[1] - 1, piece]

            def send(o=o, target=target):
                side[(s, o, piece)] = push(target, side_in.at[s - 1, o[1] - 1, piece], o)

            compute(((z - s) % z, o[1], 0, 0), piece, target, send)

    def combine(s, piece):
        for o in team.sides:
            side[(s, o, piece)].wait_recv()
        if s > 1:
            ring[(s - 1, piece)].wait_recv()
        for n in range(slots):
            at = slice(n * rows, (n + 1) * rows)
            total = mine[piece, at, :]
            for o in team.sides:
                total = total + side_in[s - 1, o[1] - 1, piece, at, :].astype(jnp.float32)
            if s > 1:
                total = total + ring_in[s - 2, piece, at, :].astype(jnp.float32)
            if s < z:
                ring_out[s - 1, piece, at, :] = total.astype(low)
            else:
                d_kv_mine[piece * slots + n] = total.astype(low)
        if s == z:
            for copy, slot in d_kv_copies:
                pl.when((slot >= piece * slots) & (slot < (piece + 1) * slots))(copy.start)
        if s < z:
            ring[(s, piece)] = push(ring_out.at[s - 1, piece], ring_in.at[s - 1, piece], along(0, 1))

    d_kv_copies = []
    for o in team.others:
        slot = team.slot(shifted(dims, me, o, 1))
        d_kv_copies.append((push.later(d_kv_mine.at[slot], d_kv_out.at[my_slot], o), slot))
    for s in range(1, z + 1):
        for piece in range(pieces):
            send_sides(s, piece)
            after = functools.partial(combine, s, piece)
            compute((z - s if s < z else 0, 0, 0, 0), piece, mine.at[piece], after)
    flush()
    for n in range(team.size):
        at = slice(n * rows, (n + 1) * rows)
        d_q_mine[n] = pack(d_q_sum[at, :HD] * SCORE_SCALE).astype(low)
    copies = [to_team(d_q_mine, d_q_out.at[my_slot], o) for o in team.others]
    own_q = pltpu.make_async_copy(d_q_mine.at[my_slot], d_q_out.at[my_slot], own_sem.at[1])
    own_q.start()
    copies += [copy for copy, slot in d_kv_copies]
    own_kv = pltpu.make_async_copy(d_kv_mine.at[my_slot], d_kv_out.at[my_slot], own_sem.at[2])
    own_kv.start()
    own_q.wait()
    own_kv.wait()
    for copy in copies:
        copy.wait_recv()
    push.finish()


def attend_back(dims, lengths, q, kv, dout, out_t, lse, collective_id):
    team = Team(dims)
    z = dims[0]
    rows = kv.shape[2]
    amount = team.size * rows
    pieces, key_step = 2, 256
    piece = (pieces, amount // pieces, LANES)
    count = 3 * (team.size - 1) + pieces * (z + z * len(team.sides))
    others = max(len(team.sides), 1)
    ring_steps, side_steps = max(z - 1, 1), z if team.sides else 1
    return pl.pallas_call(
        functools.partial(attend_back_kernel, team, key_step, 512, pieces),
        out_shape=(
            jax.ShapeDtypeStruct(q.shape, low),
            jax.ShapeDtypeStruct(kv.shape[1:], low),
        ),
        in_specs=[SMEM_SPEC, VMEM_SPEC, ANY_SPEC] + [VMEM_SPEC] * 3,
        out_specs=[VMEM_SPEC] * 2,
        scratch_shapes=[
            pltpu.VMEM(kv.shape, low),
            pltpu.VMEM(q.shape, low),
            pltpu.VMEM((LANES, amount // pieces), low),
            pltpu.VMEM((LANES, amount // pieces), low),
            pltpu.VMEM((amount // pieces, LANES), low),
            pltpu.VMEM((LANES, amount // pieces), low),
            pltpu.VMEM((LANES, amount // pieces), low),
            pltpu.VMEM((amount // pieces, LANES), low),
            pltpu.VMEM((amount, LANES), low),
            pltpu.VMEM((amount, LANES), low),
            pltpu.VMEM((amount, LANES), jnp.float32),
            pltpu.VMEM((HD, amount), low),
            pltpu.VMEM((HD, amount), low),
            pltpu.VMEM((amount, key_step), low),
            pltpu.VMEM((amount, key_step), low),
            pltpu.VMEM((amount, key_step), low),
            pltpu.VMEM((amount, key_step), low),
            pltpu.VMEM((side_steps, others) + piece, low),
            pltpu.VMEM((side_steps, others) + piece, low),
            pltpu.VMEM((ring_steps,) + piece, low),
            pltpu.VMEM((ring_steps,) + piece, low),
            pltpu.VMEM(piece, jnp.float32),
            pltpu.VMEM(q.shape, low),
            pltpu.VMEM(kv.shape[1:], low),
            pltpu.SemaphoreType.DMA((count,)),
            pltpu.SemaphoreType.DMA((count,)),
            pltpu.SemaphoreType.DMA((3 + team.groups,)),
        ],
        compiler_params=pltpu.CompilerParams(
            collective_id=collective_id, has_side_effects=True, vmem_limit_bytes=60 * MIB
        ),
        name="attend_back",
    )(lengths, q, kv, dout, out_t, lse)


def part_shapes(n_head):
    width = HEADS // n_head * HD
    hidden = FF // n_head
    return (
        (D, width, True),
        (DI, 2 * width, True),
        (width, D, False),
        (D, 3 * width, True),
        (width, D, False),
        (D, hidden, True),
        (hidden, D, False),
        (D, C // n_head, True),
    )


def borders(n_head):
    result = [0]
    for rows, columns, joined in part_shapes(n_head):
        result.append(result[-1] + rows * columns // LANES)
    return result


def period(columns):
    amount = 1
    while amount * columns % LANES:
        amount *= 2
    return amount


def segments(start, amount, unit):
    result = []
    while amount > 0:
        which, at = divmod(start, unit)
        size = min(unit - at, amount)
        result.append((which, at, at + size))
        start, amount = start + size, amount - size
    return result


def joined_lanes(pieces):
    return pieces[0] if len(pieces) == 1 else jnp.concatenate(pieces, 1)


def lane_blocks(value):
    rows, columns = value.shape
    missing = -columns % LANES
    if missing:
        value = jnp.concatenate([value, jnp.zeros((rows, missing), value.dtype)], 1)
    return [value[:, i : i + LANES] for i in range(0, columns + missing, LANES)]


def every(first, amount, stride):
    return pl.ds(first, amount) if stride == 1 else pl.ds(first, amount, stride=stride)


def matrix_of(stage, first, rows, columns, line):
    if columns % LANES == 0:
        stride = columns // LANES
        for j in range(stride):
            yield j * LANES, stage[every(first + j, rows, stride), :]
        return
    height = period(columns)
    stride = height * columns // LANES
    for k in range(height):
        pieces = [
            stage[every(first + which, rows // height, stride), :][:, begin:end]
            for which, begin, end in segments(k * columns, columns, LANES)
        ]
        for i, piece in enumerate(lane_blocks(joined_lanes(pieces))):
            line[i, every(k, rows // height, height), :] = piece
    for i in range(-(-columns // LANES)):
        yield i * LANES, line[i, :rows, : min(columns - i * LANES, LANES)]


def matrix_into(stage, first, value, line):
    rows, columns = value.shape
    if columns % LANES == 0:
        stride = columns // LANES
        for j in range(stride):
            stage[every(first + j, rows, stride), :] = value[:, j * LANES : (j + 1) * LANES]
        return
    height = period(columns)
    stride = height * columns // LANES
    for i, piece in enumerate(lane_blocks(value)):
        line[i, :rows, :] = piece
    for i in range(stride):
        pieces = [
            line[which, every(k, rows // height, height), :][:, begin:end]
            for k, first_lane, last_lane in segments(i * LANES, LANES, columns)
            for which, begin, end in segments(first_lane, last_lane - first_lane, LANES)
        ]
        stage[every(first + i, rows // height, stride), :] = joined_lanes(pieces)


def load_stage(stage, held, first_shard, shard_rows, group):
    for b in range(held.shape[0]):
        stage[pl.ds(b * shard_rows, shard_rows), :] = held[b, group, :shard_rows, :].astype(jnp.float32)


def load_common(stage, held, valid):
    piece = held.shape[2]
    for b in range(held.shape[0]):
        for k in range(held.shape[1]):
            amount = min(piece, valid - k * piece)
            stage[b * valid + k * piece : b * valid + k * piece + amount, :] = held[b, k].astype(
                jnp.float32
            )[:amount]


def common_blocks(first_row, last_row, valid):
    return first_row // valid, -(-last_row // valid) - first_row // valid


def load_matrices(stage, first_row, n_head, group, which, targets, line):
    starts, shapes = borders(n_head), part_shapes(n_head)
    for m, target in zip(which, targets):
        rows, columns, joined = shapes[m]
        row = 0 if joined else group * rows
        column = group * columns if joined else 0
        for j, value in matrix_of(stage, starts[m] - first_row, rows, columns, line):
            size = value.shape[1]
            target[row : row + rows, column + j : column + j + size] = value.astype(target.dtype)


class Moves:
    def __init__(self, sems):
        self.sems, self.going = sems, []

    def __call__(self, src, dst):
        copy = pltpu.make_async_copy(src, dst, self.sems.at[len(self.going)])
        copy.start()
        self.going.append(copy)
        return copy


def normalized(x):
    centre = x - jnp.mean(x, -1, keepdims=True)
    rate = lax.rsqrt(jnp.mean(centre * centre, -1, keepdims=True) + norm_eps)
    return centre * rate, rate


def layer_norm(x, gain):
    return normalized(x)[0] * gain


def norm_pullback(x, gain, grad):
    unit, rate = normalized(x)
    inside = grad * gain
    both = jnp.mean(inside * unit, -1, keepdims=True)
    d_x = rate * (inside - jnp.mean(inside, -1, keepdims=True) - unit * both)
    return d_x, jnp.sum(grad * unit, 0, keepdims=True)


def head_lanes(group, heads, value):
    width = heads * HD
    block = value[:, group * width : (group + 1) * width]
    lane = lax.broadcasted_iota(jnp.int32, (1, width), 1)
    result = []
    for a in range(heads):
        here = (lane >= a * HD) & (lane < (a + 1) * HD)
        result.append((here, jnp.where(here, block, jnp.zeros_like(block))))
    return result


def place_of(bounds, first, amount):
    row = first + lax.broadcasted_iota(jnp.int32, (amount, 1), 0)
    opening = jnp.zeros((amount, 1), jnp.int32)
    for begin, end in bounds:
        opening = jnp.where((row >= begin) & (row < end), begin, opening)
    offset = row - opening
    turns = jnp.floor((offset.astype(jnp.float32) + 0.5) * (1.0 / LAT)).astype(jnp.int32)
    return offset - turns * LAT


def picked_rows(bounds, rows, n_head):
    first = lax.axis_index("blk") * (rows * n_head) + lax.axis_index("head") * rows
    lane = lax.broadcasted_iota(jnp.int32, (rows, LAT), 1)
    return jnp.where(lane == place_of(bounds, first, rows), 1.0, 0.0).astype(low)


def enc_scores(q_head, keys):
    return against(q_head, keys) * (SCORE_SCALE * LOG2E)


def encode_kernel(
    n_head,
    shard_rows,
    valid,
    rows,
    lengths,
    weights,
    common,
    inputs_t,
    enc_query,
    enc_keyval,
    enc_output,
    self_project,
    gains,
    z_zero,
    h_zero,
    x_norm_t,
    q_enc,
    kv_enc,
    o_enc,
    z_one,
    h_one,
    q_self,
    kv_self,
    counts,
    label_counts,
    held,
    held_common,
    held_counts,
    stage,
    stage_common,
    line,
    latent_table,
    sems,
):
    heads = HEADS // n_head
    width = heads * HD
    shards = held.shape[0]
    bounds = clip_bounds(lengths)
    first = DQ * D // LANES
    block, blocks = common_blocks(first, first + (LAT + 4) * D // LANES, valid)
    tail = shard_rows // TILE * TILE
    copies = [
        pltpu.make_async_copy(common.at[pl.ds(block, blocks)], held_common, sems.at[0]),
        pltpu.make_async_copy(weights.at[pl.ds(0, shards)], held, sems.at[1]),
        pltpu.make_async_copy(weights.at[:, :, pl.ds(tail, TILE)], held_counts, sems.at[2]),
    ]
    for copy in copies:
        copy.start()
    centre = inputs_t[...].astype(jnp.float32)
    centre = centre - jnp.mean(centre, 0, keepdims=True)
    rate = lax.rsqrt(jnp.mean(centre * centre, 0, keepdims=True) + norm_eps)
    x_norm_t[...] = (centre * rate).astype(low)
    copies[0].wait()
    load_common(stage_common, held_common, valid)
    first = first - block * valid
    for j, value in matrix_of(stage_common, first, LAT, D, line):
        latent_table[:, j : j + LANES] = value.astype(low)
    for j, value in matrix_of(stage_common, first + LAT * D // LANES, 4, D, line):
        gains[:, j : j + LANES] = value
    picked = picked_rows(bounds, rows, n_head)
    z_zero[...] = product(picked, latent_table[...])
    h_zero[...] = layer_norm(z_zero[...], gains[0:1, :]).astype(low)
    copies[2].wait()
    counted = held_counts[...].astype(jnp.float32)[:, :, shard_rows - tail : shard_rows - tail + 1]
    counts[...] = jnp.broadcast_to(jnp.sum(counted, (0, 1)), counts.shape)
    label_counts[...] = counts[:1, :MODES]
    copies[1].wait()
    for g in range(n_head):
        load_stage(stage, held, 0, shard_rows, g)
        load_matrices(
            stage, 0, n_head, g, (0, 1, 2, 3), (enc_query, enc_keyval, enc_output, self_project), line
        )
    q_enc[...] = product(h_zero[...], enc_query[...]).astype(low)
    kv_enc[...] = contract_first(x_norm_t[...], enc_keyval[...]).astype(low)
    for g in range(n_head):
        keys = kv_enc[:, 2 * g * width : (2 * g + 1) * width]
        values = kv_enc[:, (2 * g + 1) * width : (2 * g + 2) * width]
        outcome = jnp.zeros((rows, width), jnp.float32)
        for here, q_head in head_lanes(g, heads, q_enc[...]):
            scores = enc_scores(q_head, keys)
            probs = jnp.exp2((scores - jnp.max(scores, 1, keepdims=True)).astype(low))
            total = jnp.sum(probs.astype(jnp.float32), 1, keepdims=True)
            outcome = jnp.where(here, product(probs, values) / total, outcome)
        o_enc[:, g * width : (g + 1) * width] = outcome.astype(low)
    z_one[...] = z_zero[...] + product(o_enc[...], enc_output[...])
    h_one[...] = layer_norm(z_one[...], gains[1:2, :]).astype(low)
    projected = product(h_one[...], self_project[...]).astype(low)
    for slot, (g, a) in enumerate(heads_of(n_head, q_self.shape[0])):
        query, key, value = (
            projected[:, (3 * g + i) * width + a * HD : (3 * g + i) * width + (a + 1) * HD]
            for i in range(3)
        )
        q_self[slot] = pack(query)
        kv_self[slot] = jnp.concatenate([key, value], 1)


LINE = pltpu.VMEM((4, round_up(max(D, DI), 8), LANES), jnp.float32)


def shards_of(n_head, shard_rows, first, last):
    starts = borders(n_head)
    begin = starts[first] // shard_rows
    return begin, -(-starts[last] // shard_rows) - begin


def encode(lengths, weights, common, inputs_t, valid, rows, slots, n_head, shard_rows):
    begin, shards = shards_of(n_head, shard_rows, 0, 4)
    query_rows = DQ * D // LANES
    block, blocks = common_blocks(query_rows, query_rows + (LAT + 4) * D // LANES, valid)
    keys = inputs_t.shape[1]
    return pl.pallas_call(
        functools.partial(encode_kernel, n_head, shard_rows, valid, rows),
        out_shape=[
            shape_of((D, D)),
            shape_of((DI, 2 * D)),
            shape_of((D, D)),
            shape_of((D, 3 * D)),
            shape_of((4, D), jnp.float32),
            shape_of((rows, D), jnp.float32),
            shape_of((rows, D)),
            shape_of(inputs_t.shape),
            shape_of((rows, D)),
            shape_of((keys, 2 * D)),
            shape_of((rows, D)),
            shape_of((rows, D), jnp.float32),
            shape_of((rows, D)),
            shape_of((slots, rows // 2, LANES)),
            shape_of((slots, rows, LANES)),
            shape_of((8, LANES), jnp.float32),
            shape_of((1, MODES), jnp.float32),
        ],
        in_specs=[SMEM_SPEC, ANY_SPEC, ANY_SPEC, VMEM_SPEC],
        out_specs=[VMEM_SPEC] * 17,
        scratch_shapes=[
            pltpu.VMEM((shards,) + weights.shape[1:], low),
            pltpu.VMEM((blocks,) + common.shape[1:], low),
            pltpu.VMEM(weights.shape[:2] + (TILE, LANES), low),
            pltpu.VMEM((shards * shard_rows, LANES), jnp.float32),
            pltpu.VMEM((blocks * valid, LANES), jnp.float32),
            LINE,
            pltpu.VMEM((LAT, D), low),
            pltpu.SemaphoreType.DMA((3,)),
        ],
        compiler_params=pltpu.CompilerParams(vmem_limit_bytes=56 * MIB),
        name="encode",
    )(lengths, weights, common, inputs_t)


def gelu_and_slope(x):
    rate = (2.0 / jnp.pi) ** 0.5
    cubic = 0.044715
    t = jnp.tanh(rate * (x + cubic * x * x * x))
    slope = 0.5 * (1.0 + t) + 0.5 * x * (1.0 - t * t) * rate * (1.0 + 3.0 * cubic * x * x)
    return 0.5 * x * (1.0 + t), slope


def my_column(marks, rows):
    turned = marks[...].astype(jnp.float32).T
    column = lax.broadcasted_iota(jnp.int32, turned.shape, 1)
    per_head = rows // LANES
    first = lax.axis_index("head") * per_head
    picked = [
        jnp.sum(jnp.where(column == first + k, turned, 0.0), 1, keepdims=True)
        for k in range(per_head)
    ]
    return jnp.concatenate(picked, 0) if per_head > 1 else picked[0]


def middle_kernel(
    n_head,
    shard_rows,
    valid,
    first_shard,
    rows,
    counts,
    weights,
    common,
    z_one,
    o_self,
    out_queries_t,
    labels,
    modality,
    labeled,
    gains,
    dout,
    d_two_out,
    tile,
    query_grad_out,
    gain_grads,
    grads,
    held,
    held_common,
    stage,
    stage_common,
    line,
    query_grad,
    self_output,
    hidden_in,
    hidden_out,
    class_table,
    query_table,
    slope,
    activ,
    sems,
):
    heads = HEADS // n_head
    width, hidden, classes = heads * HD, FF // n_head, C // n_head
    shards = held.shape[0]
    first_row = first_shard * shard_rows
    starts = borders(n_head)
    move = Moves(sems)
    shards_here = pl.ds(first_shard, shards)
    common_here = move(common.at[pl.ds(0, held_common.shape[0])], held_common)
    weights_here = [move(weights.at[shards_here, g], held.at[:, g]) for g in range(n_head)]
    common_here.wait()
    load_common(stage_common, held_common, valid)
    for j, value in matrix_of(stage_common, 0, DQ, D, line):
        query_table[:, j : j + LANES] = value.astype(low)
    for g in range(n_head):
        weights_here[g].wait()
        load_stage(stage, held, first_shard, shard_rows, g)
        load_matrices(
            stage, first_row, n_head, g, (4, 5, 6, 7), (self_output, hidden_in, hidden_out, class_table), line
        )
    gain_two, gain_three = gains[2:3, :], gains[3:4, :]
    o_heads = {head: unpack(o_self[s]) for s, head in enumerate(heads_of(n_head, o_self.shape[0]))}
    o_groups = [joined_lanes([o_heads[(g, a)] for a in range(heads)]) for g in range(n_head)]
    o_low = jnp.concatenate(o_groups, 1)
    z_two = z_one[...] + product(o_low, self_output[...])
    h_two = layer_norm(z_two, gain_two).astype(low)
    value, bend = gelu_and_slope(product(h_two, hidden_in[...]))
    activ[...] = value.astype(low)
    slope[...] = bend
    z_three = z_two + product(activ[...], hidden_out[...])
    queries_t = out_queries_t[...]
    decoded = layer_norm(z_three, gain_three) + contract_first(queries_t, query_table[...])
    decoded = decoded.astype(low)
    logits = product(decoded, class_table[...])
    label, kind, counted = (my_column(marks, rows) for marks in (labels, modality, labeled))
    lane = lax.broadcasted_iota(jnp.int32, (rows, C), 1).astype(jnp.float32)
    is_target = jnp.where(lane == label, 1.0, 0.0)
    row_top = jnp.max(logits, 1, keepdims=True)
    row_lse = row_top + jnp.log(jnp.sum(jnp.exp2((logits - row_top) * LOG2E), 1, keepdims=True))
    loss = row_lse - jnp.sum(is_target * logits, 1, keepdims=True)
    weight = jnp.zeros((rows, 1), jnp.float32)
    place = lax.broadcasted_iota(jnp.int32, (1, LANES), 1)
    losses = jnp.zeros((1, LANES), jnp.float32)
    for m in range(MODES):
        member = jnp.where((kind == m) & (counted == 1.0), 1.0, 0.0)
        weight = weight + member / jnp.maximum(counts[0:1, m : m + 1], 1.0)
        losses = losses + jnp.where(place == m, jnp.sum(loss * member, 0, keepdims=True), 0.0)
    tile[...] = jnp.broadcast_to(losses, tile.shape)
    dlogits = (weight * (jnp.exp2((logits - row_lse) * LOG2E) - is_target)).astype(low)
    d_decoded = against(dlogits, class_table[...])
    matrix_into(query_grad, 0, product(queries_t, d_decoded.astype(low)), line)
    stored = [move(query_grad, query_grad_out)]
    d_three, gain_three_grad = norm_pullback(z_three, gain_three, d_decoded)
    d_branch = d_three.astype(low)
    d_pre = (slope[...] * against(d_branch, hidden_out[...])).astype(low)
    d_middle, gain_two_grad = norm_pullback(z_two, gain_two, against(d_pre, hidden_in[...]))
    d_two = d_three + d_middle
    d_two_out[...] = d_two
    gain_grads[...] = jnp.concatenate([gain_two_grad, gain_three_grad], 0)
    d_two_low = d_two.astype(low)
    d_o = against(d_two_low, self_output[...]).astype(low)
    for slot, (g, a) in enumerate(heads_of(n_head, o_self.shape[0])):
        dout[slot] = pack(d_o[:, g * width + a * HD : g * width + (a + 1) * HD])
    for g in range(n_head):
        results = (
            contract_first(o_groups[g], d_two_low),
            contract_first(h_two, d_pre[:, g * hidden : (g + 1) * hidden]),
            contract_first(activ[:, g * hidden : (g + 1) * hidden], d_branch),
            contract_first(decoded, dlogits[:, g * classes : (g + 1) * classes]),
        )
        for m, result in zip((4, 5, 6, 7), results):
            matrix_into(stage, starts[m] - first_row, result, line)
        for b in range(shards):
            held[b, g, :shard_rows, :] = stage[pl.ds(b * shard_rows, shard_rows), :].astype(low)
        stored.append(move(held.at[:, g], grads.at[shards_here, g]))
    for copy in stored:
        copy.wait()


def middle(counts, weights, common, z_one, o_self, out_queries_t, marks, gains, valid, n_head, shard_rows):
    rows = z_one.shape[0]
    begin, shards = shards_of(n_head, shard_rows, 4, 8)
    query_rows = DQ * D // LANES
    block, blocks = common_blocks(0, query_rows, valid)
    return pl.pallas_call(
        functools.partial(middle_kernel, n_head, shard_rows, valid, begin, rows),
        grid=(1,),
        out_shape=[
            shape_of(o_self.shape),
            shape_of((rows, D), jnp.float32),
            shape_of((8, LANES), jnp.float32),
            shape_of((query_rows, LANES), jnp.float32),
            shape_of((2, D), jnp.float32),
            shape_of(weights.shape),
        ],
        in_specs=[
            VMEM_SPEC,
            ANY_SPEC,
            ANY_SPEC,
            VMEM_SPEC,
            VMEM_SPEC,
            pl.BlockSpec((DQ, rows), lambda i: (0, lax.axis_index("head"))),
            VMEM_SPEC,
            VMEM_SPEC,
            VMEM_SPEC,
            VMEM_SPEC,
        ],
        out_specs=[VMEM_SPEC] * 3 + [ANY_SPEC, VMEM_SPEC, ANY_SPEC],
        scratch_shapes=[
            pltpu.VMEM((shards,) + weights.shape[1:], low),
            pltpu.VMEM((blocks,) + common.shape[1:], low),
            pltpu.VMEM((shards * shard_rows, LANES), jnp.float32),
            pltpu.VMEM((blocks * valid, LANES), jnp.float32),
            LINE,
            pltpu.VMEM((query_rows, LANES), jnp.float32),
            pltpu.VMEM((D, D), low),
            pltpu.VMEM((D, FF), low),
            pltpu.VMEM((FF, D), low),
            pltpu.VMEM((D, C), low),
            pltpu.VMEM((DQ, D), low),
            pltpu.VMEM((rows, FF), jnp.float32),
            pltpu.VMEM((rows, FF), low),
            pltpu.SemaphoreType.DMA((2 + 2 * n_head,)),
        ],
        compiler_params=pltpu.CompilerParams(vmem_limit_bytes=56 * MIB),
        name="middle",
    )(counts, weights, common, z_one, o_self, out_queries_t, *marks, gains)


def ending_kernel(
    n_head,
    shard_rows,
    valid,
    rows,
    lengths,
    grads_in,
    d_q_self,
    d_kv_self,
    gains,
    gain_grads,
    *refs,
):
    kept_in, (grads, common_grad), kept = refs[:14], refs[14:16], refs[16:30]
    held, stage, stage_common, line, d_q, d_kv, sems = refs[30:]
    (
        d_two,
        query_grad,
        enc_query,
        enc_keyval,
        enc_output,
        self_project,
        z_zero,
        h_zero,
        x_norm_t,
        q_enc,
        kv_enc,
        o_enc,
        z_one,
        h_one,
    ) = kept
    move = Moves(sems)
    first_used = (12, 5, 0, 4, 10, 9, 2, 6, 1, 7, 8, 11, 3, 13)
    loads = {i: move(kept_in[i], kept[i]) for i in first_used}

    def need(*which):
        for i in which:
            loads[i].wait()

    heads = HEADS // n_head
    width = heads * HD
    shards = held.shape[0]
    starts = borders(n_head)
    shared = move(grads_in.at[pl.ds(shards - 1, 1)], held.at[pl.ds(shards - 1, 1)])
    d_heads = {}
    for slot, head in enumerate(heads_of(n_head, d_kv_self.shape[0])):
        d_kv_head = d_kv_self[slot]
        d_heads[head] = (unpack(d_q_self[slot]), d_kv_head[:, :HD], d_kv_head[:, HD:])
    d_projected = [
        jnp.concatenate([d_heads[(g, a)][i] for i in range(3) for a in range(heads)], 1)
        for g in range(n_head)
    ]
    whole = jnp.concatenate(d_projected, 1)
    need(12, 5, 0)
    d_middle, gain_one_grad = norm_pullback(
        z_one[...], gains[1:2, :], against(whole, self_project[...])
    )
    d_one = d_two[...] + d_middle
    d_one_low = d_one.astype(low)
    need(4, 10, 9)
    d_o = against(d_one_low, enc_output[...]).astype(low)
    for g in range(n_head):
        keys = kv_enc[:, 2 * g * width : (2 * g + 1) * width]
        values = kv_enc[:, (2 * g + 1) * width : (2 * g + 2) * width]
        d_key = jnp.zeros(keys.shape, jnp.float32)
        d_value = jnp.zeros(keys.shape, jnp.float32)
        d_query = jnp.zeros((rows, width), jnp.float32)
        for (here, q_head), (unused, do_head) in zip(
            head_lanes(g, heads, q_enc[...]), head_lanes(g, heads, d_o)
        ):
            scores = enc_scores(keys, q_head)
            probs = jnp.exp2((scores - jnp.max(scores, 0, keepdims=True)).astype(low))
            probs = probs.astype(jnp.float32)
            probs = probs / jnp.sum(probs, 0, keepdims=True)
            d_probs = against(values, do_head)
            delta = jnp.sum(probs * d_probs, 0, keepdims=True)
            d_scores = (probs * (d_probs - delta)).astype(low)
            d_value = d_value + product(probs.astype(low), do_head)
            d_key = d_key + product(d_scores, q_head)
            d_query = jnp.where(here, contract_first(d_scores, keys), d_query)
        d_q[:, g * width : (g + 1) * width] = (d_query * SCORE_SCALE).astype(low)
        d_kv[:, 2 * g * width : (2 * g + 1) * width] = (d_key * SCORE_SCALE).astype(low)
        d_kv[:, (2 * g + 1) * width : (2 * g + 2) * width] = d_value.astype(low)
    need(2, 6)
    d_middle, gain_zero_grad = norm_pullback(
        z_zero[...], gains[0:1, :], against(d_q[...], enc_query[...])
    )
    d_zero = d_one + d_middle
    d_zero_top = d_zero.astype(low)
    d_zero_rest = (d_zero - d_zero_top.astype(jnp.float32)).astype(low)
    picked = picked_rows(clip_bounds(lengths), rows, n_head)
    latent_grad = contract_first(picked, d_zero_top) + contract_first(picked, d_zero_rest)
    need(1, 7, 8, 11, 3, 13)
    query_rows = query_grad.shape[0]
    stage_common[:query_rows] = query_grad[...]
    matrix_into(stage_common, query_rows, latent_grad, line)
    all_gains = jnp.concatenate([gain_zero_grad, gain_one_grad, gain_grads[...]], 0)
    matrix_into(stage_common, query_rows + LAT * D // LANES, all_gains, line)
    piece = common_grad.shape[2]
    for b in range(common_grad.shape[0]):
        for k in range(common_grad.shape[1]):
            amount = min(piece, valid - k * piece)
            block = stage_common[b * valid + k * piece : b * valid + k * piece + amount, :]
            if amount < piece:
                block = jnp.concatenate([block, jnp.zeros((piece - amount, LANES), jnp.float32)], 0)
            common_grad[b, k] = block.astype(low)
    shared.wait()
    shared_rows = shards * shard_rows - starts[4]
    stored = []
    for g in range(n_head):
        results = (
            contract_first(h_zero[...], d_q[:, g * width : (g + 1) * width]),
            product(x_norm_t[...], d_kv[:, 2 * g * width : (2 * g + 2) * width]),
            contract_first(o_enc[:, g * width : (g + 1) * width], d_one_low),
            contract_first(h_one[...], d_projected[g]),
        )
        if shared_rows:
            stage[pl.ds((shards - 1) * shard_rows, shard_rows), :] = held[
                shards - 1, g, :shard_rows, :
            ].astype(jnp.float32)
        for m, result in zip((0, 1, 2, 3), results):
            matrix_into(stage, starts[m], result, line)
        for b in range(shards):
            held[b, g, :shard_rows, :] = stage[pl.ds(b * shard_rows, shard_rows), :].astype(low)
        stored.append(move(held.at[:, g], grads.at[pl.ds(0, shards), g]))
    for copy in stored:
        copy.wait()


def ending(lengths, grads, d_self, d_two, gains, gain_grads, query_grad, kept, common_shape, valid, shard_rows):
    rows = d_two.shape[0]
    n_head = grads.shape[1]
    begin, shards = shards_of(n_head, shard_rows, 0, 4)
    kept = (d_two, query_grad) + tuple(kept)
    keys = kept[8].shape[1]
    common_rows = (DQ + LAT + 4) * D // LANES
    return pl.pallas_call(
        functools.partial(ending_kernel, n_head, shard_rows, valid, rows),
        out_shape=[shape_of(grads.shape), shape_of(common_shape)],
        in_specs=[SMEM_SPEC, ANY_SPEC] + [VMEM_SPEC] * 4 + [ANY_SPEC] * len(kept),
        out_specs=[ANY_SPEC, VMEM_SPEC],
        input_output_aliases={1: 0},
        scratch_shapes=[pltpu.VMEM(a.shape, a.dtype) for a in kept]
        + [
            pltpu.VMEM((shards,) + grads.shape[1:], low),
            pltpu.VMEM((shards * shard_rows, LANES), jnp.float32),
            pltpu.VMEM((common_rows, LANES), jnp.float32),
            LINE,
            pltpu.VMEM((rows, D), low),
            pltpu.VMEM((keys, 2 * D), low),
            pltpu.SemaphoreType.DMA((len(kept) + 1 + n_head,)),
        ],
        compiler_params=pltpu.CompilerParams(vmem_limit_bytes=56 * MIB),
        name="ending",
    )(lengths, grads, *d_self, gains, gain_grads, *kept)


def adam_step(weight, first, second, grad):
    first = beta_one * first + (1 - beta_one) * grad
    second = beta_two * second + (1 - beta_two) * grad * grad
    fixed_first = first / (1 - beta_one**STEP)
    fixed_second = second / (1 - beta_two**STEP)
    weight = weight - learn_rate * (
        fixed_first / (jnp.sqrt(fixed_second) + adam_eps) + weight_decay * weight
    )
    return (weight, first, second, weight.astype(low))


def per_device(
    inputs,
    out_queries,
    clip_lengths,
    labels,
    modality,
    labeled,
    head_params,
    head_first,
    head_second,
    common_params,
    common_first,
    common_second,
):
    n_head, n_blk = lax.axis_size("head"), lax.axis_size("blk")
    dims = grid_of(n_blk, n_head)
    rows = labels.shape[0] // n_head
    n_h, n_c = head_params.shape[0], common_params.shape[0]
    shard_rows, common_rows = n_h // LANES, -(-n_c // LANES)
    head_rows = round_up(shard_rows + 1, TILE)
    piece_rows = round_up(-(-common_rows // n_head), TILE)
    marks = [x.reshape(-1, LANES) for x in (labels, modality, labeled)]
    head_wide = head_params.reshape(shard_rows, LANES)
    common_wide = jnp.pad(common_params, (0, common_rows * LANES - n_c)).reshape(common_rows, LANES)
    weights, common = gather_all(dims, marks, (head_wide, common_wide), (head_rows, piece_rows), 0)
    valid = common_rows
    if n_c % LANES:
        common = common.reshape(n_blk, -1)[:, :n_c].reshape(-1, LANES)
        valid = common.shape[0]
        common = jnp.pad(common, ((0, -valid % TILE), (0, 0)))[None, None]

    encoded = encode(
        clip_lengths, weights, common, inputs.T, valid, rows, Team(dims).size, n_head, shard_rows
    )
    gains, z_one, counts = encoded[4], encoded[11], encoded[15]
    o_self, lse_self, out_self_t, q_all, kv_all = attend(
        dims, clip_lengths, encoded[13], encoded[14], 1
    )
    dout, d_two, tile, query_grad, gain_grads, grads = middle(
        counts, weights, common, z_one, o_self, out_queries.T, marks, gains, valid, n_head, shard_rows
    )
    d_self = attend_back(dims, clip_lengths, q_all, kv_all, dout, out_self_t, lse_self, 2)
    kept = encoded[:4] + encoded[5:13]
    grads, common_grad = ending(
        clip_lengths,
        grads,
        d_self,
        d_two,
        gains,
        gain_grads,
        query_grad,
        kept,
        common.shape,
        valid,
        shard_rows,
    )
    if n_c % LANES:
        common_grad = common_grad[0, 0, :valid].reshape(n_blk, n_c)
        common_grad = jnp.pad(common_grad, ((0, 0), (0, n_head * piece_rows * LANES - n_c)))
        common_grad = common_grad.reshape(n_blk, n_head, piece_rows, LANES)
    head_share, common_share, loss_sums, clip_norm, factor = reduce_all(
        dims, (grads, common_grad), (shard_rows, common_rows), tile, 3
    )
    label_counts, loss_sums = encoded[16].reshape(MODES), loss_sums.reshape(MODES)
    clip_norm, factor = clip_norm.reshape(()), factor.reshape(())
    head_share, common_share = head_share.reshape(-1), common_share.reshape(-1)[:n_c]
    head_out = adam_step(head_params, head_first, head_second, head_share * factor)
    common_out = adam_step(common_params, common_first, common_second, common_share * factor)
    return head_out + common_out + (loss_sums, label_counts, clip_norm)


def solution(mesh):
    placed = (
        P("blk", None),
        P("blk", None),
        P(),
        P("blk"),
        P("blk"),
        P("blk"),
        P(("head", "blk")),
        P(("head", "blk")),
        P(("head", "blk")),
        P("blk"),
        P("blk"),
        P("blk"),
    )
    return jax.shard_map(
        per_device,
        mesh=mesh,
        in_specs=placed,
        out_specs=(
            P(("head", "blk")),
            P(("head", "blk")),
            P(("head", "blk")),
            P(("head", "blk")),
            P("blk"),
            P("blk"),
            P("blk"),
            P("blk"),
            P(),
            P(),
            P(),
        ),
        check_vma=False,
    )
```

```python
import functools

import jax
import jax.numpy as jnp
from jax import lax
from jax.experimental import pallas as pl
from jax.experimental.pallas import tpu as pltpu
from jax.sharding import PartitionSpec as P

D = 512
HEADS = 8
HD = 64
FF = 2048
DI = 704
DQ = 1026
C = 704
LAT = 784
MODES = 3
STEP = 10
LANES = 128
TILE = 16

norm_eps = 1e-05
learn_rate = 0.1
beta_one = 0.9
beta_two = 0.999
adam_eps = 1e-08
weight_decay = 0.01
clip_limit = 0.05
big_negative = -1e30
low = jnp.bfloat16
LOG2E = 1.4426950408889634
SCORE_SCALE = HD ** (-0.5)
MESH = pl.DeviceIdType.MESH
MIB = 1 << 20
VMEM_SPEC = pl.BlockSpec(memory_space=pltpu.VMEM)
SMEM_SPEC = pl.BlockSpec(memory_space=pltpu.SMEM)
ANY_SPEC = pl.BlockSpec(memory_space=pl.ANY)


def shape_of(shape, dtype=low):
    return jax.ShapeDtypeStruct(shape, dtype)


def round_up(n, unit):
    return -(-n // unit) * unit


def grid_of(n_blk, n_head):
    cores = 2 if n_head % 2 == 0 else 1
    x = n_head // cores
    y = x if n_blk % x == 0 else 1
    return (n_blk // y, y, x, cores)


def my_place(dims):
    blk, head = lax.axis_index("blk"), lax.axis_index("head")
    return (blk // dims[1], lax.rem(blk, dims[1]), head // dims[3], lax.rem(head, dims[3]))


def shifted(dims, me, offset, sign):
    return tuple(
        m if o == 0 else lax.rem(m + (o if sign > 0 else n - o), n)
        for m, o, n in zip(me, offset, dims)
    )


def blk_of(dims, place):
    return place[0] * dims[1] + place[1]


def head_of(dims, place):
    return place[2] * dims[3] + place[3]


def device_of(dims, place):
    return {"blk": blk_of(dims, place), "head": head_of(dims, place)}


def along(axis, d):
    return tuple(d if a == axis else 0 for a in range(4))


def greet(dims, me, offsets):
    barrier = pltpu.get_barrier_semaphore()
    for offset in offsets:
        pl.semaphore_signal(
            barrier,
            inc=1,
            device_id=device_of(dims, shifted(dims, me, offset, 1)),
            device_id_type=MESH,
        )
    pl.semaphore_wait(barrier, len(offsets))


def axis_peers(dims, axes):
    return [along(axis, d) for axis in axes for d in range(1, dims[axis])]


def remote(src, dst, send_sem, recv_sem, place, dims):
    return pltpu.make_async_remote_copy(
        src_ref=src,
        dst_ref=dst,
        send_sem=send_sem,
        recv_sem=recv_sem,
        device_id=device_of(dims, place),
        device_id_type=MESH,
    )


AHEAD = 6.0
RING = 0


def in_order(first, follow, size_of, ahead, result):
    queues, busy, flight = {}, {}, {}
    now = 0.0

    def ready(messages):
        for message in messages:
            queues.setdefault(message[1], []).append(message)

    ready(first)
    while True:
        for axis in sorted(queues):
            queue, going = queues[axis], flight.setdefault(axis, [])
            while queue and (not going or busy[axis] < now + ahead):
                message = min(queue)
                queue.remove(message)
                busy[axis] = max(now, busy.get(axis, 0.0)) + size_of(message)
                going.append((busy[axis] + 1.5, message))
                result.append((True, message))
        arrivals = [min(going) for going in flight.values() if going]
        if not arrivals:
            return now
        arrival = min(arrivals)
        flight[arrival[1][1]].remove(arrival)
        now = max(now, arrival[0])
        result.append((False, arrival[1]))
        ready(follow(arrival[1]))


def time_of(rows, axis):
    return rows * LANES * 2 / (300e3 if axis == 3 else 45e3)


def with_at(offset, axis, d):
    return offset[:axis] + (d,) + offset[axis + 1 :]


def gather_order(dims, parts):
    def onward(p, offset, position):
        order = parts[p][3]
        result = []
        for k in range(max(position, 0), 4):
            axis = order[k]
            n = dims[axis]
            if k > position:
                steps = [1] if axis == RING else range(1, n)
                steps = [d for d in steps if d < n]
            else:
                steps = [offset[axis] + 1] if axis == RING and offset[axis] + 1 < n else []
            for d in steps:
                result.append(((k, sum(offset), p), axis, p, with_at(offset, axis, d)))
        return result

    def follow(message):
        rank, axis, p, offset = message
        return onward(p, offset, rank[0])

    first = [m for p in range(len(parts)) for m in onward(p, (0, 0, 0, 0), -1)]
    result = []
    now = in_order(first, follow, lambda m: time_of(parts[m[2]][2], m[1]), AHEAD, result)
    return result, now


def gather_kernel(
    dims,
    parts,
    labels,
    modality,
    labeled,
    head_params,
    common_params,
    head_all,
    common_all,
    head_low,
    common_low,
    common_wide,
    send_sem,
    recv_sem,
    own_sem,
):
    me = my_place(dims)
    my_head = head_of(dims, me)
    n_head = dims[2] * dims[3]
    shard_rows, common_rows = head_params.shape[0], common_params.shape[0]
    per_head = labels.shape[0] // n_head
    row = lax.broadcasted_iota(jnp.int32, labels.shape, 0)
    mine = (row >= my_head * per_head) & (row < (my_head + 1) * per_head) & (labeled[...] == 1)
    lane = lax.broadcasted_iota(jnp.int32, (1, LANES), 1)
    counts = jnp.zeros((1, LANES), jnp.float32)
    for m in range(MODES):
        member = jnp.where(mine & (modality[...] == m), 1.0, 0.0)
        counts = counts + jnp.where(lane == m, jnp.sum(member, (0, 1), keepdims=True), 0.0)
    padding = head_low.shape[0] - shard_rows
    tail = shard_rows // TILE * TILE
    head_low[:tail] = head_params[:tail].astype(low)
    last = [jnp.broadcast_to(counts, (padding, LANES))]
    if shard_rows > tail:
        last = [head_params[tail:]] + last
    head_low[tail:] = jnp.concatenate(last, 0).astype(low)
    common_wide[...] = jnp.zeros(common_wide.shape, jnp.float32)
    common_wide[:common_rows] = common_params[...]
    piece = common_low.shape[0]
    common_low[...] = common_wide[pl.ds(pl.multiple_of(my_head * piece, TILE), piece)].astype(low)

    greet(dims, me, ring_and_others(dims))
    srcs, outs = (head_low, common_low), (head_all, common_all)
    copies = {}

    def block(p, offset):
        place = shifted(dims, me, offset, -1)
        array, first, rows, order = parts[p]
        return outs[array].at[blk_of(dims, place), head_of(dims, place), pl.ds(first, rows)]

    own = []
    for is_send, (rank, axis, p, offset) in gather_order(dims, parts)[0]:
        if is_send:
            step = 1 if axis == RING else offset[axis]
            before = with_at(offset, axis, offset[axis] - step)
            array, first, rows, order = parts[p]
            source = block(p, before) if any(before) else srcs[array].at[pl.ds(first, rows)]
            i = len(copies)
            copies[(p, offset)] = remote(
                source,
                block(p, before),
                send_sem.at[i],
                recv_sem.at[i],
                shifted(dims, me, along(axis, step), 1),
                dims,
            )
            copies[(p, offset)].start()
        else:
            if not own:
                for array in range(2):
                    copy = pltpu.make_async_copy(
                        srcs[array], outs[array].at[blk_of(dims, me), my_head], own_sem.at[array]
                    )
                    copy.start()
                    own.append(copy)
            copies[(p, offset)].wait_recv()
    for copy in copies.values():
        copy.wait_send()
    for copy in own:
        copy.wait()


def ring_and_others(dims):
    ring = {along(RING, 1 % dims[RING]), along(RING, (dims[RING] - 1) % dims[RING])}
    return sorted(ring - {(0, 0, 0, 0)}) + axis_peers(dims, (1, 2, 3))


def cut(array, rows, shares):
    result = []
    first, so_far = 0, 0
    whole = sum(share for share, order in shares)
    for share, order in shares:
        so_far += share
        end = rows * so_far // whole // TILE * TILE if so_far < whole else rows
        if end > first:
            result.append((array, first, end - first, order))
        first = end
    return tuple(result)


ZYXC, ZXYC, YXZC, XYZC = (0, 1, 2, 3), (0, 2, 1, 3), (1, 2, 0, 3), (2, 1, 0, 3)
HEAD_SHARES = ((15, ZYXC), (13, ZXYC), (4, YXZC), (5, XYZC))
COMMON_SHARES = ((1, ZYXC), (1, ZXYC))


def gather_all(dims, marks, params, rows, collective_id):
    z, y, x, cores = dims
    parts = cut(0, rows[0], HEAD_SHARES) + cut(1, rows[1], COMMON_SHARES)
    count = len(parts) * (z * y * x * cores - 1)
    return pl.pallas_call(
        functools.partial(gather_kernel, dims, parts),
        out_shape=[shape_of((z * y, x * cores, n, LANES)) for n in rows],
        in_specs=[VMEM_SPEC] * 5,
        out_specs=[ANY_SPEC] * 2,
        scratch_shapes=[pltpu.VMEM((n, LANES), low) for n in rows]
        + [
            pltpu.VMEM((x * cores * rows[1], LANES), jnp.float32),
            pltpu.SemaphoreType.DMA((count,)),
            pltpu.SemaphoreType.DMA((count,)),
            pltpu.SemaphoreType.DMA((2,)),
        ],
        compiler_params=pltpu.CompilerParams(collective_id=collective_id, has_side_effects=True),
        name="gather_weights",
    )(*marks, *params)


def reduce_order(dims, parts):
    ready, arrived, order = set(), set(), []

    def message(p, position, offset):
        z = offset[RING]
        rank = (dims[RING] - z if z else dims[RING], position, tuple(-o for o in offset), p)
        return (rank, parts[p][3][position], p, position, offset)

    def done(p, position, offset):
        ready.add((p, position, offset))
        if position == 4:
            return []
        axis = parts[p][3][position]
        d = offset[axis]
        first = d != 0 and (axis != RING or d == dims[axis] - 1)
        return ([message(p, position, offset)] if first else []) + advance(p, position, offset)

    def advance(p, position, offset):
        axis = parts[p][3][position]
        n = dims[axis]
        start = with_at(offset, axis, 0)
        if axis == RING:
            here = (p, position, offset)
            if here in ready and here in arrived:
                order.append((None, here))
                if offset[axis]:
                    return [message(p, position, offset)]
                return done(p, position + 1, offset)
        elif (p, position, start) in ready and (p, position + 1, start) not in ready:
            if all((p, position, with_at(start, axis, d)) in arrived for d in range(1, n)):
                order.append((None, (p, position, start)))
                return done(p, position + 1, start)
        return []

    def follow(sent):
        rank, axis, p, position, offset = sent
        here = with_at(offset, axis, offset[axis] - 1) if axis == RING else offset
        arrived.add((p, position, here))
        return advance(p, position, here)

    first = []
    for p in range(len(parts)):
        for offset in all_offsets(dims, range(4)):
            first += done(p, 0, offset)
    now = in_order(first, follow, lambda m: time_of(parts[m[2]][2], m[1]), AHEAD, order)
    return order, now


def all_offsets(dims, axes):
    offsets = [(0, 0, 0, 0)]
    for a in axes:
        offsets = [with_at(o, a, d) for o in offsets for d in range(dims[a])]
    return offsets


def reduce_kernel(dims, parts, *refs):
    srcs, tile = refs[:2], refs[2]
    head_out, common_out, losses, norm, factor = refs[3:8]
    places = len(parts) * 4
    buffers = refs[8 : 8 + places]
    head_sum, common_sum, shares, send_sem, recv_sem, near_tiles, far_tiles = refs[8 + places : 15 + places]
    held, held_sem = refs[15 + places : 17 + places], refs[17 + places]
    sums = (head_sum, common_sum)
    me = my_place(dims)
    z, y, x, cores = dims
    loads = [
        pltpu.make_async_copy(srcs[k].at[:, :, me[3]], held[k], held_sem.at[k]) for k in range(2)
    ]
    for load in loads:
        load.start()
    across = peers_across(dims)
    others = [o for o in all_offsets(dims, (0, 1)) if any(o)]
    met = ring_and_others(dims)
    greet(dims, me, met + [o for o in across + others if o not in met])
    push = Pushes(dims, me, send_sem, recv_sem)
    copies = {}

    def slot(p, position, offset):
        order = parts[p][3]
        axis = order[position]
        rest = [o for o in all_offsets(dims, order[position + 1 :])]
        k = rest.index(with_at(offset, axis, 0))
        return buffers[p * 4 + position].at[k, max(offset[axis] - 1, 0)]

    def summed(p, position, offset):
        array, first, rows, order = parts[p]
        if position == 0:
            place = shifted(dims, me, offset, 1)
            at = (blk_of(dims, place), place[2])
            if offset[3]:
                return srcs[array].at[(*at, place[3], pl.ds(first, rows))]
            if loads[array] is not None:
                loads[array].wait()
                loads[array] = None
            return held[array].at[(*at, pl.ds(first, rows))]
        return slot(p, position - 1, offset)

    def ring_slot(p, position, offset):
        axis = parts[p][3][position]
        return slot(p, position, with_at(offset, axis, offset[axis] + 1))

    def add(p, position, offset):
        array, first, rows, order = parts[p]
        axis = order[position]
        if axis == RING:
            arrivals = [ring_slot(p, position, offset)]
        else:
            arrivals = [slot(p, position, with_at(offset, axis, d)) for d in range(1, dims[axis])]
        mine = summed(p, position, offset)
        step = row_chunk(rows)

        @pl.loop(0, rows // step)
        def some_rows(n):
            at = pl.ds(pl.multiple_of(n * step, step), step)
            last = position == 3 and not any(offset)
            if len(arrivals) == 1 and not last:
                arrivals[0][at] = mine[at] + arrivals[0][at]
                return
            total = mine[at].astype(jnp.float32)
            for arrival in arrivals:
                total = total + arrival[at].astype(jnp.float32)
            if last:
                sums[array][pl.ds(pl.multiple_of(first + n * step, TILE), step)] = total
            else:
                arrivals[0][at] = total.astype(low)

    for is_send, what in reduce_order(dims, parts)[0]:
        if is_send is None:
            add(*what)
        elif is_send:
            rank, axis, p, position, offset = what
            d = offset[axis]
            started = axis != RING or d == dims[axis] - 1
            source = summed(p, position, offset) if started else ring_slot(p, position, offset)
            step = along(axis, 1 if axis == RING else d)
            copies[what] = push(source, slot(p, position, offset), step)
        else:
            copies[what].wait_recv()
    my_head, my_blk = head_of(dims, me), blk_of(dims, me)
    shares[my_head] = common_sum[...].astype(low)
    share_copies = [push(shares.at[my_head], shares.at[my_head], o) for o in across]
    amount = head_out.shape[0]
    head_out[...] = head_sum[:amount]
    squares = jnp.sum(head_sum[:amount] * head_sum[:amount], 0, keepdims=True)
    squares = squares + jnp.sum(common_sum[...] * common_sum[...], 0, keepdims=True)
    lane = lax.broadcasted_iota(jnp.int32, (1, LANES), 1)
    near_tiles[my_head] = tile[...] + jnp.where(
        lane == MODES, jnp.sum(squares, 1, keepdims=True), 0.0
    )
    near = [push(near_tiles.at[my_head], near_tiles.at[my_head], o) for o in across]
    for copy in near:
        copy.wait_recv()
    far_tiles[my_blk] = jnp.sum(near_tiles[...], 0)
    far = [push(far_tiles.at[my_blk], far_tiles.at[my_blk], o) for o in others]
    for copy in share_copies:
        copy.wait_recv()
    piece = shares.shape[1]
    for k in range(x * cores):
        amount = min(piece, common_out.shape[0] - k * piece)
        common_out[k * piece : k * piece + amount] = shares[k].astype(jnp.float32)[:amount]
    for copy in far:
        copy.wait_recv()
    totals = jnp.sum(far_tiles[...], 0)[:1]
    losses[...] = totals[:, :MODES]
    norm[...] = jnp.sqrt(totals[:, MODES : MODES + 1])
    factor[...] = jnp.minimum(1.0, clip_limit / norm[...])
    push.finish()


def row_chunk(rows):
    for count in (4, 3, 2):
        if rows % (count * TILE) == 0:
            return rows // count
    return rows


def reduce_all(dims, arrays, valid, tile, collective_id):
    z, y, x, cores = dims
    rows = [array.shape[2] for array in arrays]
    arrays = [array.reshape(z * y, x, cores, *array.shape[2:]) for array in arrays]
    parts = ()
    for array, shares in enumerate((HEAD_SHARES, COMMON_SHARES)):
        parts += cut(array, rows[array], [(share, order[::-1]) for share, order in shares])
    scratch = []
    for array, first, amount, order in parts:
        for position, axis in enumerate(order):
            rest = len(all_offsets(dims, order[position + 1 :]))
            scratch.append(pltpu.VMEM((rest, dims[axis] - 1, amount, LANES), low))
    count = len(parts) * (z * y * x * cores - 1) + 2 * (x * cores - 1) + z * y - 1
    return pl.pallas_call(
        functools.partial(reduce_kernel, dims, parts),
        out_shape=[
            shape_of((valid[0], LANES), jnp.float32),
            shape_of((valid[1], LANES), jnp.float32),
            shape_of((1, MODES), jnp.float32),
            shape_of((1, 1), jnp.float32),
            shape_of((1, 1), jnp.float32),
        ],
        in_specs=[ANY_SPEC] * 2 + [VMEM_SPEC],
        out_specs=[VMEM_SPEC] * 5,
        scratch_shapes=scratch
        + [pltpu.VMEM((n, LANES), jnp.float32) for n in rows]
        + [
            pltpu.VMEM((x * cores, rows[1], LANES), low),
            pltpu.SemaphoreType.DMA((count,)),
            pltpu.SemaphoreType.DMA((count,)),
            pltpu.VMEM((x * cores, 8, LANES), jnp.float32),
            pltpu.VMEM((z * y, 8, LANES), jnp.float32),
        ]
        + [pltpu.VMEM((z * y, x, n, LANES), low) for n in rows]
        + [pltpu.SemaphoreType.DMA((2,))],
        compiler_params=pltpu.CompilerParams(
            collective_id=collective_id, has_side_effects=True, vmem_limit_bytes=60 * MIB
        ),
        name="reduce_gradients",
    )(*arrays, tile)


def contract_first(a, b):
    return lax.dot_general(a, b, (((0,), (0,)), ((), ())), preferred_element_type=jnp.float32)


def product(a, b):
    return jnp.dot(a, b, preferred_element_type=jnp.float32)


def against(a, b):
    return lax.dot_general(a, b, (((1,), (1,)), ((), ())), preferred_element_type=jnp.float32)


def clip_bounds(lengths):
    result, first = [], 0
    for clip in range(lengths.shape[0]):
        end = first + lengths[clip]
        result.append((first, end))
        first = end
    return result


def clip_borders(bounds, place):
    opening = jnp.zeros(place.shape, jnp.int32)
    ending = jnp.full(place.shape, 1 << 30, jnp.int32)
    for clip, (begin, end) in enumerate(bounds):
        here = place == clip
        opening = jnp.where(here, begin, opening)
        ending = jnp.where(here, end, ending)
    return opening, ending


def low_half(axis):
    return lax.broadcasted_iota(jnp.int32, (1, LANES) if axis else (LANES, 1), axis) < HD


def with_key_tail(bounds, first_row, kv):
    clips = len(bounds)
    place = lax.broadcasted_iota(jnp.int32, (1, LANES), 1) - HD
    opening, ending = clip_borders(bounds, place)
    ones = jnp.where((place >= clips) & (place < clips + 3), 1.0, 0.0)
    row = first_row + lax.broadcasted_iota(jnp.int32, kv.shape, 0)
    tail = jnp.where((row >= opening) & (row < ending), ones, big_negative)
    return jnp.where(low_half(1), kv.astype(jnp.float32), tail).astype(low)


def with_value_tail(kv):
    place = lax.broadcasted_iota(jnp.int32, (1, LANES), 1)
    ones = jnp.where(place < 3, 1.0, 0.0)
    return jnp.where(low_half(1), ones, kv.astype(jnp.float32)).astype(low)


def in_three(place, value):
    top = value.astype(low).astype(jnp.float32)
    middle = (value - top).astype(low).astype(jnp.float32)
    bottom = value - top - middle
    return (
        jnp.where(place == 0, top, 0.0)
        + jnp.where(place == 1, middle, 0.0)
        + jnp.where(place == 2, bottom, 0.0)
    )


def with_query_tail(bounds, first_row, rows, extra):
    clips = len(bounds)
    place = lax.broadcasted_iota(jnp.int32, (HD, 1), 0)
    opening, ending = clip_borders(bounds, place)
    row = first_row + lax.broadcasted_iota(jnp.int32, (1, rows.shape[1]), 1)
    inside = (place < clips) & (row >= opening) & (row < ending)
    tail = jnp.where(inside, 1.0, 0.0)
    if extra is not None:
        tail = tail + in_three(place - clips, -extra)
    return jnp.concatenate([rows * (SCORE_SCALE * LOG2E), tail], 0).astype(low)


def pack(rows):
    half = rows.shape[0] // 2
    return jnp.concatenate([rows[:half], rows[half:]], 1)


def unpack(packed):
    return jnp.concatenate([packed[:, :HD], packed[:, HD:]], 0)


def unpack_t(packed):
    turned = packed.astype(jnp.float32).T
    return jnp.concatenate([turned[:HD], turned[HD:]], 1)


def pack_t(columns):
    half = columns.shape[1] // 2
    return jnp.concatenate([columns[:, :half], columns[:, half:]], 0).T


class Team:
    def __init__(self, dims):
        z, y, x, cores = dims
        self.dims = dims
        self.wide = HEADS // (x * cores) == y
        self.size = x * cores * (y if self.wide else 1)
        self.groups = z if self.wide else z * y
        axes = (1, 2, 3) if self.wide else (2, 3)
        offsets = [o for o in all_offsets(dims, axes) if any(o)]
        self.others = sorted(offsets, key=lambda o: (o[1] + o[2], o))
        self.sides = [] if self.wide else axis_peers(dims, (1,))

    def slot(self, place):
        head = head_of(self.dims, place)
        return place[1] * self.dims[2] * self.dims[3] + head if self.wide else head

    def group(self, place):
        return place[0] if self.wide else blk_of(self.dims, place)


def heads_of(n_head, slots):
    return [(s % n_head, s // n_head) for s in range(slots)]


class Pushes:
    def __init__(self, dims, me, send_sem, recv_sem):
        self.dims, self.me, self.send_sem, self.recv_sem = dims, me, send_sem, recv_sem
        self.started = []

    def later(self, src, dst, offset):
        i = len(self.started)
        place = shifted(self.dims, self.me, offset, 1)
        copy = remote(src, dst, self.send_sem.at[i], self.recv_sem.at[i], place, self.dims)
        self.started.append(copy)
        return copy

    def __call__(self, src, dst, offset):
        copy = self.later(src, dst, offset)
        copy.start()
        return copy

    def finish(self):
        for copy in self.started:
            copy.wait_send()


def peers_across(dims):
    z, y, x, cores = dims
    across = [(0, 0, a, c) for a in range(x) for c in range(cores) if (a, c) != (0, 0)]
    return sorted(across, key=lambda o: (o[2] == 0, o[3]))


def attend_kernel(
    team,
    query_step,
    key_step,
    pieces,
    lengths,
    q_in,
    kv_in,
    o_out,
    lse,
    out_t,
    q_all,
    kv_out,
    kv_all,
    even_keys,
    even_values_t,
    odd_keys,
    odd_values_t,
    queries,
    top,
    accum,
    even_scores,
    odd_scores,
    even_top,
    odd_top,
    o_mine,
    send_sem,
    recv_sem,
    own_sem,
):
    dims = team.dims
    z = dims[0]
    me = my_place(dims)
    bounds = clip_bounds(lengths)
    rows = kv_in.shape[1]
    amount = team.size * rows
    slots = team.size // pieces
    my_group, my_slot = team.group(me), team.slot(me)
    ring_ends = sorted({along(0, 1 % z), along(0, (z - 1) % z)} - {(0, 0, 0, 0)})
    greet(dims, me, team.others + ring_ends + team.sides)
    push = Pushes(dims, me, send_sem, recv_sem)
    own_kv = pltpu.make_async_copy(kv_in.at[my_slot], kv_all.at[my_group, my_slot], own_sem.at[0])
    own_q = pltpu.make_async_copy(q_in.at[my_slot], q_all.at[my_slot], own_sem.at[1])
    own_kv.start()
    own_q.start()

    def to_team(src, dst, o):
        return push(src.at[team.slot(shifted(dims, me, o, 1))], dst, o)

    kv_copies = {o: to_team(kv_in, kv_all.at[my_group, my_slot], o) for o in team.others}
    q_copies = [to_team(q_in, q_all.at[my_slot], o) for o in team.others]
    ring, side, slot_copies = {}, {}, []

    def group_at(offset):
        return team.group(shifted(dims, me, offset, -1))

    def send_slot(o):
        if z > 1:
            block = kv_all.at[my_group, team.slot(shifted(dims, me, o, -1))]
            slot_copies.append(push(block, block, along(0, 1)))

    def slot_arrived():
        for copy in slot_copies:
            copy.wait_recv()

    def send_on(s, piece):
        block = kv_all.at[group_at(along(0, s)), pl.ds(piece * slots, slots)]
        if 0 < s < z - 1:
            ring[(s + 1, piece)] = push(block, block, along(0, 1))
        for o in team.sides:
            side[(s, o, piece)] = push(block, block, o)

    def both(now, later):
        if now is not None:
            n, unused, now_values, now_scores, now_top = now
            at = tile(n)
            old = top[:, at]
            new = jnp.maximum(old, jnp.max(now_top[...], 0, keepdims=True))
            top[:, at] = new
            total = accum[:, at] * jnp.exp2(old - new)
        if later is not None:
            n, later_keys, unused, later_scores, later_top = later
            query = queries[:, tile(n)]
            highest = jnp.full(later_top.shape, -1e38, jnp.float32)
        for k in range(0, slots * rows, key_step):
            if later is not None:
                scores = product(later_keys[k : k + key_step, :], query)
                later_scores[k : k + key_step, :] = scores
                highest = jnp.maximum(
                    highest, jnp.max(scores.reshape(key_step // 8, 8, query_step), 0)
                )
            if now is not None:
                probs = jnp.exp2((now_scores[k : k + key_step, :] - new).astype(low))
                total = total + product(now_values[:, k : k + key_step], probs)
        if later is not None:
            later_top[...] = highest
        if now is not None:
            accum[:, at] = total

    def tile(n):
        return pl.ds(pl.multiple_of(n * query_step, query_step), query_step)

    computed, pending = [], [None]

    def compute(offset, piece):
        group = group_at(offset)
        keys, values_t = sides_of_keys[len(computed) % 2]
        computed.append(offset)

        @pl.loop(0, slots)
        def build(n):
            at = pl.ds(pl.multiple_of(n * rows, rows), rows)
            slot = piece * slots + n
            block = kv_all[group, slot]
            keys[at, :] = with_key_tail(bounds, group * amount + slot * rows, block)
            values_t[:HD, at] = block.astype(jnp.float32).T[HD:].astype(low)

        def even(n):
            return (n, keys, values_t, even_scores, even_top)

        def odd(n):
            return (n, keys, values_t, odd_scores, odd_top)

        tiles = amount // query_step
        both(pending[0], even(0))

        @pl.loop(0, tiles // 2 - 1)
        def query_blocks(n):
            both(even(2 * n), odd(2 * n + 1))
            both(odd(2 * n + 1), even(2 * n + 2))

        both(even(tiles - 2), odd(tiles - 1))
        pending[0] = odd(tiles - 1)

    sides_of_keys = ((even_keys, even_values_t), (odd_keys, odd_values_t))
    for unused, values_t in sides_of_keys:
        values_t[HD:, :] = jnp.ones((TILE, slots * rows), low)
    top[...] = jnp.full(top.shape, -1e38, jnp.float32)
    accum[...] = jnp.zeros(accum.shape, jnp.float32)
    own_kv.wait()
    send_slot((0, 0, 0, 0))
    for o in team.others:
        kv_copies[o].wait_recv()
        send_slot(o)
    for piece in range(pieces):
        send_on(0, piece)
    own_q.wait()
    for copy in q_copies:
        copy.wait_recv()
    for n in range(team.size):
        queries[:, n * rows : (n + 1) * rows] = with_query_tail(
            bounds, my_group * amount + n * rows, unpack_t(q_all[n]), None
        )
    stores = []

    def store(offset):
        group = group_at(offset)
        copy = pltpu.make_async_copy(kv_all.at[group], kv_out.at[group], own_sem.at[3 + len(stores)])
        copy.start()
        stores.append(copy)

    for s in range(z):
        store(along(0, s))
        for piece in range(pieces):
            compute(along(0, s), piece)
            if s < z - 1:
                if s:
                    ring[(s + 1, piece)].wait_recv()
                elif piece == 0:
                    slot_arrived()
                send_on(s + 1, piece)
            for o in team.sides:
                side[(s, o, piece)].wait_recv()
                compute((s, o[1], 0, 0), piece)
        for o in team.sides:
            store((s, o[1], 0, 0))
    both(pending[0], None)
    total = accum[HD : HD + 1, :]
    out_t[...] = accum[:HD, :] / total
    lse[...] = top[...] + jnp.log(total) * LOG2E
    for n in range(team.size):
        o_mine[n] = pack_t(out_t[:, n * rows : (n + 1) * rows]).astype(low)
    o_copies = [to_team(o_mine, o_out.at[my_slot], o) for o in team.others]
    own_o = pltpu.make_async_copy(o_mine.at[my_slot], o_out.at[my_slot], own_sem.at[2])
    own_o.start()
    own_o.wait()
    for copy in o_copies:
        copy.wait_recv()
    for copy in stores:
        copy.wait()
    push.finish()


def attend(dims, lengths, q, kv, collective_id):
    team = Team(dims)
    z = dims[0]
    amount = team.size * kv.shape[1]
    pieces, query_step = 2, 256
    count = 4 * team.size + pieces * (z + z * len(team.sides))
    return pl.pallas_call(
        functools.partial(attend_kernel, team, query_step, 256, pieces),
        out_shape=(
            jax.ShapeDtypeStruct(q.shape, low),
            jax.ShapeDtypeStruct((1, amount), jnp.float32),
            jax.ShapeDtypeStruct((HD, amount), jnp.float32),
            jax.ShapeDtypeStruct(q.shape, low),
            jax.ShapeDtypeStruct((team.groups,) + kv.shape, low),
        ),
        in_specs=[SMEM_SPEC, VMEM_SPEC, VMEM_SPEC],
        out_specs=[VMEM_SPEC] * 4 + [ANY_SPEC],
        scratch_shapes=[
            pltpu.VMEM((team.groups,) + kv.shape, low),
            pltpu.VMEM((amount // pieces, LANES), low),
            pltpu.VMEM((HD + TILE, amount // pieces), low),
            pltpu.VMEM((amount // pieces, LANES), low),
            pltpu.VMEM((HD + TILE, amount // pieces), low),
            pltpu.VMEM((LANES, amount), low),
            pltpu.VMEM((1, amount), jnp.float32),
            pltpu.VMEM((HD + TILE, amount), jnp.float32),
            pltpu.VMEM((amount // pieces, query_step), jnp.float32),
            pltpu.VMEM((amount // pieces, query_step), jnp.float32),
            pltpu.VMEM((8, query_step), jnp.float32),
            pltpu.VMEM((8, query_step), jnp.float32),
            pltpu.VMEM(q.shape, low),
            pltpu.SemaphoreType.DMA((count,)),
            pltpu.SemaphoreType.DMA((count,)),
            pltpu.SemaphoreType.DMA((3 + team.groups,)),
        ],
        compiler_params=pltpu.CompilerParams(
            collective_id=collective_id, has_side_effects=True, vmem_limit_bytes=56 * MIB
        ),
        name="attend",
    )(lengths, q, kv)


def attend_back_kernel(
    team,
    key_step,
    query_step,
    pieces,
    lengths,
    q_all,
    kv_in,
    do_in,
    out_t,
    lse,
    d_q_out,
    d_kv_out,
    kv_all,
    do_all,
    even_keys_t,
    even_values_t,
    even_rows,
    odd_keys_t,
    odd_values_t,
    odd_rows,
    queries,
    douts,
    d_q_sum,
    q_rows,
    do_rows,
    even_probs,
    odd_probs,
    even_scores,
    odd_scores,
    side_out,
    side_in,
    ring_out,
    ring_in,
    mine,
    d_q_mine,
    d_kv_mine,
    send_sem,
    recv_sem,
    own_sem,
):
    dims = team.dims
    z = dims[0]
    me = my_place(dims)
    bounds = clip_bounds(lengths)
    rows = kv_all.shape[2]
    amount = team.size * rows
    loads = {}
    for s in range(1, z + 1):
        for o in team.sides + [(0, 0, 0, 0)]:
            offset = ((z - s) % z, o[1], 0, 0)
            group = team.group(shifted(dims, me, offset, 1))
            loads[offset] = pltpu.make_async_copy(
                kv_in.at[group], kv_all.at[group], own_sem.at[3 + len(loads)]
            )
            loads[offset].start()
    slots = team.size // pieces
    piece_rows = slots * rows
    my_group, my_slot = team.group(me), team.slot(me)
    ring_ends = sorted({along(0, 1 % z), along(0, (z - 1) % z)} - {(0, 0, 0, 0)})
    greet(dims, me, team.others + ring_ends + team.sides)
    push = Pushes(dims, me, send_sem, recv_sem)

    def to_team(src, dst, o):
        return push(src.at[team.slot(shifted(dims, me, o, 1))], dst, o)

    do_copies = [to_team(do_in, do_all.at[my_slot], o) for o in team.others]
    own_do = pltpu.make_async_copy(do_in.at[my_slot], do_all.at[my_slot], own_sem.at[0])
    own_do.start()
    place = lax.broadcasted_iota(jnp.int32, (HD, 1), 0)
    for n in range(team.size):
        at = slice(n * rows, (n + 1) * rows)
        q_t = unpack_t(q_all[n])
        extended = with_query_tail(bounds, my_group * amount + n * rows, q_t, lse[:, at])
        queries[at, :] = extended.astype(jnp.float32).T.astype(low)
        q_rows[:, at] = (q_t * SCORE_SCALE).astype(low)
    d_q_sum[...] = jnp.zeros(d_q_sum.shape, jnp.float32)
    own_do.wait()
    for copy in do_copies:
        copy.wait_recv()
    for n in range(team.size):
        at = slice(n * rows, (n + 1) * rows)
        do_t = unpack_t(do_all[n])
        delta = jnp.sum(do_t * out_t[:, at], 0, keepdims=True)
        extended = jnp.concatenate([in_three(place, -delta), do_t], 0).astype(low)
        douts[at, :] = extended.astype(jnp.float32).T.astype(low)
        do_rows[:, at] = do_t.astype(low)

    def both(now, later):
        if now is not None:
            n, (unused, unused, now_rows), now_probs, now_scores, target = now
            now_at = rows_of(n)
        if later is not None:
            n, (keys_t, values_t, unused), later_probs, later_scores, unused = later
            at = rows_of(n)
        for first in range(0, amount, query_step):
            part = slice(first, first + query_step)
            if later is not None:
                probs = jnp.exp2(product(queries[part, :], keys_t[:, at]).astype(low))
                d_probs = product(douts[part, :], values_t[:, at])
                later_probs[part, :] = probs
                later_scores[part, :] = (probs.astype(jnp.float32) * d_probs).astype(low)
            if now is not None:
                if first == 0:
                    d_value = product(do_rows[...], now_probs[...])
                if first == amount // 2:
                    d_key = product(q_rows[...], now_scores[...])
                d_q_sum[part, :] = d_q_sum[part, :] + product(now_scores[part, :], now_rows[now_at, :])
        if now is not None:
            target[now_at, :] = jnp.concatenate([d_key, d_value], 0).T.astype(target.dtype)

    def rows_of(k):
        return slice(k * key_step, (k + 1) * key_step)

    computed, pending = [], []

    def flush(later=None):
        if pending:
            now, after = pending.pop()
            both(now, later)
            after()
        elif later is not None:
            both(None, later)

    def compute(offset, piece, target, after):
        group = team.group(shifted(dims, me, offset, 1))
        keys = sides_of_keys[len(computed) % 2]
        computed.append(offset)
        if offset in loads:
            loads.pop(offset).wait()

        @pl.loop(0, slots)
        def build(n):
            at = pl.ds(pl.multiple_of(n * rows, rows), rows)
            slot = piece * slots + n
            block = kv_all[group, slot]
            extended = with_key_tail(bounds, group * amount + slot * rows, block)
            keys[0][:, at] = extended.astype(jnp.float32).T.astype(low)
            keys[1][:, at] = with_value_tail(block).astype(jnp.float32).T.astype(low)
            keys[2][at, :] = block

        steps = [
            (k, keys) + ((odd_probs, odd_scores) if k % 2 else (even_probs, even_scores)) + (target,)
            for k in range(piece_rows // key_step)
        ]
        flush(steps[0])
        for now, later in zip(steps[:-1], steps[1:]):
            both(now, later)
        pending.append((steps[-1], after))

    sides_of_keys = (
        (even_keys_t, even_values_t, even_rows),
        (odd_keys_t, odd_values_t, odd_rows),
    )
    side, ring = {}, {}

    def send_sides(s, piece):
        for o in team.sides:
            target = side_out.at[s - 1, o[1] - 1, piece]

            def send(o=o, target=target):
                side[(s, o, piece)] = push(target, side_in.at[s - 1, o[1] - 1, piece], o)

            compute(((z - s) % z, o[1], 0, 0), piece, target, send)

    def combine(s, piece):
        for o in team.sides:
            side[(s, o, piece)].wait_recv()
        if s > 1:
            ring[(s - 1, piece)].wait_recv()
        for n in range(slots):
            at = slice(n * rows, (n + 1) * rows)
            total = mine[piece, at, :]
            for o in team.sides:
                total = total + side_in[s - 1, o[1] - 1, piece, at, :].astype(jnp.float32)
            if s > 1:
                total = total + ring_in[s - 2, piece, at, :].astype(jnp.float32)
            if s < z:
                ring_out[s - 1, piece, at, :] = total.astype(low)
            else:
                d_kv_mine[piece * slots + n] = total.astype(low)
        if s == z:
            for copy, slot in d_kv_copies:
                pl.when((slot >= piece * slots) & (slot < (piece + 1) * slots))(copy.start)
        if s < z:
            ring[(s, piece)] = push(ring_out.at[s - 1, piece], ring_in.at[s - 1, piece], along(0, 1))

    d_kv_copies = []
    for o in team.others:
        slot = team.slot(shifted(dims, me, o, 1))
        d_kv_copies.append((push.later(d_kv_mine.at[slot], d_kv_out.at[my_slot], o), slot))
    for s in range(1, z + 1):
        for piece in range(pieces):
            send_sides(s, piece)
            after = functools.partial(combine, s, piece)
            compute((z - s if s < z else 0, 0, 0, 0), piece, mine.at[piece], after)
    flush()
    for n in range(team.size):
        at = slice(n * rows, (n + 1) * rows)
        d_q_mine[n] = pack(d_q_sum[at, :HD] * SCORE_SCALE).astype(low)
    copies = [to_team(d_q_mine, d_q_out.at[my_slot], o) for o in team.others]
    own_q = pltpu.make_async_copy(d_q_mine.at[my_slot], d_q_out.at[my_slot], own_sem.at[1])
    own_q.start()
    copies += [copy for copy, slot in d_kv_copies]
    own_kv = pltpu.make_async_copy(d_kv_mine.at[my_slot], d_kv_out.at[my_slot], own_sem.at[2])
    own_kv.start()
    own_q.wait()
    own_kv.wait()
    for copy in copies:
        copy.wait_recv()
    push.finish()


def attend_back(dims, lengths, q, kv, dout, out_t, lse, collective_id):
    team = Team(dims)
    z = dims[0]
    rows = kv.shape[2]
    amount = team.size * rows
    pieces, key_step = 2, 256
    piece = (pieces, amount // pieces, LANES)
    count = 3 * (team.size - 1) + pieces * (z + z * len(team.sides))
    others = max(len(team.sides), 1)
    ring_steps, side_steps = max(z - 1, 1), z if team.sides else 1
    return pl.pallas_call(
        functools.partial(attend_back_kernel, team, key_step, 256, pieces),
        out_shape=(
            jax.ShapeDtypeStruct(q.shape, low),
            jax.ShapeDtypeStruct(kv.shape[1:], low),
        ),
        in_specs=[SMEM_SPEC, VMEM_SPEC, ANY_SPEC] + [VMEM_SPEC] * 3,
        out_specs=[VMEM_SPEC] * 2,
        scratch_shapes=[
            pltpu.VMEM(kv.shape, low),
            pltpu.VMEM(q.shape, low),
            pltpu.VMEM((LANES, amount // pieces), low),
            pltpu.VMEM((LANES, amount // pieces), low),
            pltpu.VMEM((amount // pieces, LANES), low),
            pltpu.VMEM((LANES, amount // pieces), low),
            pltpu.VMEM((LANES, amount // pieces), low),
            pltpu.VMEM((amount // pieces, LANES), low),
            pltpu.VMEM((amount, LANES), low),
            pltpu.VMEM((amount, LANES), low),
            pltpu.VMEM((amount, LANES), jnp.float32),
            pltpu.VMEM((HD, amount), low),
            pltpu.VMEM((HD, amount), low),
            pltpu.VMEM((amount, key_step), low),
            pltpu.VMEM((amount, key_step), low),
            pltpu.VMEM((amount, key_step), low),
            pltpu.VMEM((amount, key_step), low),
            pltpu.VMEM((side_steps, others) + piece, low),
            pltpu.VMEM((side_steps, others) + piece, low),
            pltpu.VMEM((ring_steps,) + piece, low),
            pltpu.VMEM((ring_steps,) + piece, low),
            pltpu.VMEM(piece, jnp.float32),
            pltpu.VMEM(q.shape, low),
            pltpu.VMEM(kv.shape[1:], low),
            pltpu.SemaphoreType.DMA((count,)),
            pltpu.SemaphoreType.DMA((count,)),
            pltpu.SemaphoreType.DMA((3 + team.groups,)),
        ],
        compiler_params=pltpu.CompilerParams(
            collective_id=collective_id, has_side_effects=True, vmem_limit_bytes=60 * MIB
        ),
        name="attend_back",
    )(lengths, q, kv, dout, out_t, lse)


def part_shapes(n_head):
    width = HEADS // n_head * HD
    hidden = FF // n_head
    return (
        (D, width, True),
        (DI, 2 * width, True),
        (width, D, False),
        (D, 3 * width, True),
        (width, D, False),
        (D, hidden, True),
        (hidden, D, False),
        (D, C // n_head, True),
    )


def borders(n_head):
    result = [0]
    for rows, columns, joined in part_shapes(n_head):
        result.append(result[-1] + rows * columns // LANES)
    return result


def period(columns):
    amount = 1
    while amount * columns % LANES:
        amount *= 2
    return amount


def segments(start, amount, unit):
    result = []
    while amount > 0:
        which, at = divmod(start, unit)
        size = min(unit - at, amount)
        result.append((which, at, at + size))
        start, amount = start + size, amount - size
    return result


def joined_lanes(pieces):
    return pieces[0] if len(pieces) == 1 else jnp.concatenate(pieces, 1)


def lane_blocks(value):
    rows, columns = value.shape
    missing = -columns % LANES
    if missing:
        value = jnp.concatenate([value, jnp.zeros((rows, missing), value.dtype)], 1)
    return [value[:, i : i + LANES] for i in range(0, columns + missing, LANES)]


def every(first, amount, stride):
    return pl.ds(first, amount) if stride == 1 else pl.ds(first, amount, stride=stride)


def matrix_of(stage, first, rows, columns, line):
    if columns % LANES == 0:
        stride = columns // LANES
        for j in range(stride):
            yield j * LANES, stage[every(first + j, rows, stride), :]
        return
    height = period(columns)
    stride = height * columns // LANES
    for k in range(height):
        pieces = [
            stage[every(first + which, rows // height, stride), :][:, begin:end]
            for which, begin, end in segments(k * columns, columns, LANES)
        ]
        for i, piece in enumerate(lane_blocks(joined_lanes(pieces))):
            line[i, every(k, rows // height, height), :] = piece
    for i in range(-(-columns // LANES)):
        yield i * LANES, line[i, :rows, : min(columns - i * LANES, LANES)]


def matrix_into(stage, first, value, line):
    rows, columns = value.shape
    if columns % LANES == 0:
        stride = columns // LANES
        for j in range(stride):
            stage[every(first + j, rows, stride), :] = value[:, j * LANES : (j + 1) * LANES]
        return
    height = period(columns)
    stride = height * columns // LANES
    for i, piece in enumerate(lane_blocks(value)):
        line[i, :rows, :] = piece
    for i in range(stride):
        pieces = [
            line[which, every(k, rows // height, height), :][:, begin:end]
            for k, first_lane, last_lane in segments(i * LANES, LANES, columns)
            for which, begin, end in segments(first_lane, last_lane - first_lane, LANES)
        ]
        stage[every(first + i, rows // height, stride), :] = joined_lanes(pieces)


def load_stage(stage, held, first_shard, shard_rows, group):
    for b in range(held.shape[0]):
        stage[pl.ds(b * shard_rows, shard_rows), :] = held[b, group, :shard_rows, :].astype(jnp.float32)


def load_common(stage, held, valid):
    piece = held.shape[2]
    for b in range(held.shape[0]):
        for k in range(held.shape[1]):
            amount = min(piece, valid - k * piece)
            stage[b * valid + k * piece : b * valid + k * piece + amount, :] = held[b, k].astype(
                jnp.float32
            )[:amount]


def common_blocks(first_row, last_row, valid):
    return first_row // valid, -(-last_row // valid) - first_row // valid


def load_matrices(stage, first_row, n_head, group, which, targets, line):
    starts, shapes = borders(n_head), part_shapes(n_head)
    for m, target in zip(which, targets):
        rows, columns, joined = shapes[m]
        row = 0 if joined else group * rows
        column = group * columns if joined else 0
        for j, value in matrix_of(stage, starts[m] - first_row, rows, columns, line):
            size = value.shape[1]
            target[row : row + rows, column + j : column + j + size] = value.astype(target.dtype)


class Moves:
    def __init__(self, sems):
        self.sems, self.going = sems, []

    def __call__(self, src, dst):
        copy = pltpu.make_async_copy(src, dst, self.sems.at[len(self.going)])
        copy.start()
        self.going.append(copy)
        return copy


def normalized(x):
    centre = x - jnp.mean(x, -1, keepdims=True)
    rate = lax.rsqrt(jnp.mean(centre * centre, -1, keepdims=True) + norm_eps)
    return centre * rate, rate


def layer_norm(x, gain):
    return normalized(x)[0] * gain


def norm_pullback(x, gain, grad):
    unit, rate = normalized(x)
    inside = grad * gain
    both = jnp.mean(inside * unit, -1, keepdims=True)
    d_x = rate * (inside - jnp.mean(inside, -1, keepdims=True) - unit * both)
    return d_x, jnp.sum(grad * unit, 0, keepdims=True)


def turned(value):
    return value.astype(jnp.float32).T.astype(low)


def head_lanes(group, heads, value):
    width = heads * HD
    block = value[:, group * width : (group + 1) * width]
    lane = lax.broadcasted_iota(jnp.int32, (1, width), 1)
    result = []
    for a in range(heads):
        here = (lane >= a * HD) & (lane < (a + 1) * HD)
        result.append((here, jnp.where(here, block, jnp.zeros_like(block))))
    return result


def place_of(bounds, first, amount, axis):
    shape = (1, amount) if axis else (amount, 1)
    row = first + lax.broadcasted_iota(jnp.int32, shape, axis)
    opening = jnp.zeros(shape, jnp.int32)
    for begin, end in bounds:
        opening = jnp.where((row >= begin) & (row < end), begin, opening)
    offset = row - opening
    turns = jnp.floor((offset.astype(jnp.float32) + 0.5) * (1.0 / LAT)).astype(jnp.int32)
    return offset - turns * LAT


def picked_rows(bounds, rows, n_head, axis=0):
    first = lax.axis_index("blk") * (rows * n_head) + lax.axis_index("head") * rows
    shape = (LAT, rows) if axis else (rows, LAT)
    latent = lax.broadcasted_iota(jnp.int32, shape, 1 - axis)
    return jnp.where(latent == place_of(bounds, first, rows, axis), 1.0, 0.0).astype(low)


def enc_scores(q_head, keys):
    return against(q_head, keys) * (SCORE_SCALE * LOG2E)


def encode_kernel(
    n_head,
    shard_rows,
    valid,
    rows,
    lengths,
    weights,
    common,
    inputs_t,
    enc_query,
    enc_keyval,
    enc_output,
    self_project,
    gains,
    z_zero,
    h_zero,
    x_norm_t,
    q_enc,
    kv_enc,
    o_enc,
    z_one,
    h_one,
    q_self,
    kv_self,
    counts,
    label_counts,
    held,
    held_common,
    held_counts,
    stage,
    stage_common,
    line,
    latent_table,
    sems,
):
    heads = HEADS // n_head
    width = heads * HD
    shards = held.shape[0]
    bounds = clip_bounds(lengths)
    first = DQ * D // LANES
    block, blocks = common_blocks(first, first + (LAT + 4) * D // LANES, valid)
    tail = shard_rows // TILE * TILE
    copies = [
        pltpu.make_async_copy(common.at[pl.ds(block, blocks)], held_common, sems.at[0]),
        pltpu.make_async_copy(weights.at[pl.ds(0, shards)], held, sems.at[1]),
        pltpu.make_async_copy(weights.at[:, :, pl.ds(tail, TILE)], held_counts, sems.at[2]),
    ]
    for copy in copies:
        copy.start()
    centre = inputs_t[...].astype(jnp.float32)
    centre = centre - jnp.mean(centre, 0, keepdims=True)
    rate = lax.rsqrt(jnp.mean(centre * centre, 0, keepdims=True) + norm_eps)
    x_norm_t[...] = (centre * rate).astype(low)
    copies[0].wait()
    load_common(stage_common, held_common, valid)
    first = first - block * valid
    for j, value in matrix_of(stage_common, first, LAT, D, line):
        latent_table[:, j : j + LANES] = value.astype(low)
    for j, value in matrix_of(stage_common, first + LAT * D // LANES, 4, D, line):
        gains[:, j : j + LANES] = value
    picked = picked_rows(bounds, rows, n_head)
    z_zero[...] = product(picked, latent_table[...])
    h_zero[...] = layer_norm(z_zero[...], gains[0:1, :]).astype(low)
    copies[2].wait()
    counted = held_counts[...].astype(jnp.float32)[:, :, shard_rows - tail : shard_rows - tail + 1]
    counts[...] = jnp.broadcast_to(jnp.sum(counted, (0, 1)), counts.shape)
    label_counts[...] = counts[:1, :MODES]
    copies[1].wait()
    for g in range(n_head):
        load_stage(stage, held, 0, shard_rows, g)
        load_matrices(
            stage, 0, n_head, g, (0, 1, 2, 3), (enc_query, enc_keyval, enc_output, self_project), line
        )
    q_enc[...] = product(h_zero[...], enc_query[...]).astype(low)
    kv_enc[...] = contract_first(x_norm_t[...], enc_keyval[...]).astype(low)
    for g in range(n_head):
        keys = kv_enc[:, 2 * g * width : (2 * g + 1) * width]
        values = kv_enc[:, (2 * g + 1) * width : (2 * g + 2) * width]
        outcome = jnp.zeros((rows, width), jnp.float32)
        for here, q_head in head_lanes(g, heads, q_enc[...]):
            scores = enc_scores(q_head, keys)
            probs = jnp.exp2((scores - jnp.max(scores, 1, keepdims=True)).astype(low))
            total = jnp.sum(probs.astype(jnp.float32), 1, keepdims=True)
            outcome = jnp.where(here, product(probs, values) / total, outcome)
        o_enc[:, g * width : (g + 1) * width] = outcome.astype(low)
    z_one[...] = z_zero[...] + product(o_enc[...], enc_output[...])
    h_one[...] = layer_norm(z_one[...], gains[1:2, :]).astype(low)
    projected = product(h_one[...], self_project[...]).astype(low)
    for slot, (g, a) in enumerate(heads_of(n_head, q_self.shape[0])):
        query, key, value = (
            projected[:, (3 * g + i) * width + a * HD : (3 * g + i) * width + (a + 1) * HD]
            for i in range(3)
        )
        q_self[slot] = pack(query)
        kv_self[slot] = jnp.concatenate([key, value], 1)


LINE = pltpu.VMEM((4, round_up(max(D, DI), 8), LANES), jnp.float32)


def shards_of(n_head, shard_rows, first, last):
    starts = borders(n_head)
    begin = starts[first] // shard_rows
    return begin, -(-starts[last] // shard_rows) - begin


def encode(lengths, weights, common, inputs_t, valid, rows, slots, n_head, shard_rows):
    begin, shards = shards_of(n_head, shard_rows, 0, 4)
    query_rows = DQ * D // LANES
    block, blocks = common_blocks(query_rows, query_rows + (LAT + 4) * D // LANES, valid)
    keys = inputs_t.shape[1]
    return pl.pallas_call(
        functools.partial(encode_kernel, n_head, shard_rows, valid, rows),
        out_shape=[
            shape_of((D, D)),
            shape_of((DI, 2 * D)),
            shape_of((D, D)),
            shape_of((D, 3 * D)),
            shape_of((4, D), jnp.float32),
            shape_of((rows, D), jnp.float32),
            shape_of((rows, D)),
            shape_of(inputs_t.shape),
            shape_of((rows, D)),
            shape_of((keys, 2 * D)),
            shape_of((rows, D)),
            shape_of((rows, D), jnp.float32),
            shape_of((rows, D)),
            shape_of((slots, rows // 2, LANES)),
            shape_of((slots, rows, LANES)),
            shape_of((8, LANES), jnp.float32),
            shape_of((1, MODES), jnp.float32),
        ],
        in_specs=[SMEM_SPEC, ANY_SPEC, ANY_SPEC, VMEM_SPEC],
        out_specs=[VMEM_SPEC] * 17,
        scratch_shapes=[
            pltpu.VMEM((shards,) + weights.shape[1:], low),
            pltpu.VMEM((blocks,) + common.shape[1:], low),
            pltpu.VMEM(weights.shape[:2] + (TILE, LANES), low),
            pltpu.VMEM((shards * shard_rows, LANES), jnp.float32),
            pltpu.VMEM((blocks * valid, LANES), jnp.float32),
            LINE,
            pltpu.VMEM((LAT, D), low),
            pltpu.SemaphoreType.DMA((3,)),
        ],
        compiler_params=pltpu.CompilerParams(vmem_limit_bytes=56 * MIB),
        name="encode",
    )(lengths, weights, common, inputs_t)


def gelu_and_slope(x):
    rate = (2.0 / jnp.pi) ** 0.5
    cubic = 0.044715
    t = jnp.tanh(rate * (x + cubic * x * x * x))
    slope = 0.5 * (1.0 + t) + 0.5 * x * (1.0 - t * t) * rate * (1.0 + 3.0 * cubic * x * x)
    return 0.5 * x * (1.0 + t), slope


def my_column(marks, rows):
    turned = marks[...].astype(jnp.float32).T
    column = lax.broadcasted_iota(jnp.int32, turned.shape, 1)
    per_head = rows // LANES
    first = lax.axis_index("head") * per_head
    picked = [
        jnp.sum(jnp.where(column == first + k, turned, 0.0), 1, keepdims=True)
        for k in range(per_head)
    ]
    return jnp.concatenate(picked, 0) if per_head > 1 else picked[0]


def middle_kernel(
    n_head,
    shard_rows,
    valid,
    first_shard,
    rows,
    counts,
    weights,
    common,
    z_one,
    o_self,
    out_queries_t,
    labels,
    modality,
    labeled,
    gains,
    dout,
    d_two_out,
    tile,
    query_grad_out,
    gain_grads,
    grads,
    held,
    held_common,
    stage,
    stage_common,
    line,
    query_grad,
    self_output,
    hidden_in,
    hidden_out,
    class_table,
    query_table,
    slope,
    activ,
    sems,
):
    heads = HEADS // n_head
    width, hidden, classes = heads * HD, FF // n_head, C // n_head
    shards = held.shape[0]
    first_row = first_shard * shard_rows
    starts = borders(n_head)
    move = Moves(sems)
    shards_here = pl.ds(first_shard, shards)
    common_here = move(common.at[pl.ds(0, held_common.shape[0])], held_common)
    weights_here = [move(weights.at[shards_here, g], held.at[:, g]) for g in range(n_head)]
    common_here.wait()
    load_common(stage_common, held_common, valid)
    for j, value in matrix_of(stage_common, 0, DQ, D, line):
        query_table[:, j : j + LANES] = value.astype(low)
    for g in range(n_head):
        weights_here[g].wait()
        load_stage(stage, held, first_shard, shard_rows, g)
        load_matrices(
            stage, first_row, n_head, g, (4, 5, 6, 7), (self_output, hidden_in, hidden_out, class_table), line
        )
    gain_two, gain_three = gains[2:3, :], gains[3:4, :]
    o_heads = {head: unpack(o_self[s]) for s, head in enumerate(heads_of(n_head, o_self.shape[0]))}
    o_groups = [joined_lanes([o_heads[(g, a)] for a in range(heads)]) for g in range(n_head)]
    o_low = jnp.concatenate(o_groups, 1)
    z_two = z_one[...] + product(o_low, self_output[...])
    h_two = layer_norm(z_two, gain_two).astype(low)
    value, bend = gelu_and_slope(product(h_two, hidden_in[...]))
    activ[...] = value.astype(low)
    slope[...] = bend
    z_three = z_two + product(activ[...], hidden_out[...])
    queries_t = out_queries_t[...]
    decoded = layer_norm(z_three, gain_three) + contract_first(queries_t, query_table[...])
    decoded = decoded.astype(low)
    logits = product(decoded, class_table[...])
    label, kind, counted = (my_column(marks, rows) for marks in (labels, modality, labeled))
    lane = lax.broadcasted_iota(jnp.int32, (rows, C), 1).astype(jnp.float32)
    is_target = jnp.where(lane == label, 1.0, 0.0)
    row_top = jnp.max(logits, 1, keepdims=True)
    row_lse = row_top + jnp.log(jnp.sum(jnp.exp2((logits - row_top) * LOG2E), 1, keepdims=True))
    loss = row_lse - jnp.sum(is_target * logits, 1, keepdims=True)
    weight = jnp.zeros((rows, 1), jnp.float32)
    place = lax.broadcasted_iota(jnp.int32, (1, LANES), 1)
    losses = jnp.zeros((1, LANES), jnp.float32)
    for m in range(MODES):
        member = jnp.where((kind == m) & (counted == 1.0), 1.0, 0.0)
        weight = weight + member / jnp.maximum(counts[0:1, m : m + 1], 1.0)
        losses = losses + jnp.where(place == m, jnp.sum(loss * member, 0, keepdims=True), 0.0)
    tile[...] = jnp.broadcast_to(losses, tile.shape)
    dlogits = (weight * (jnp.exp2((logits - row_lse) * LOG2E) - is_target)).astype(low)
    d_decoded = against(dlogits, class_table[...])
    matrix_into(query_grad, 0, product(queries_t, d_decoded.astype(low)), line)
    stored = [move(query_grad, query_grad_out)]
    d_three, gain_three_grad = norm_pullback(z_three, gain_three, d_decoded)
    d_branch = d_three.astype(low)
    d_pre = (slope[...] * against(d_branch, hidden_out[...])).astype(low)
    d_middle, gain_two_grad = norm_pullback(z_two, gain_two, against(d_pre, hidden_in[...]))
    d_two = d_three + d_middle
    d_two_out[...] = d_two
    gain_grads[...] = jnp.concatenate([gain_two_grad, gain_three_grad], 0)
    d_two_low = d_two.astype(low)
    d_o = against(d_two_low, self_output[...]).astype(low)
    for slot, (g, a) in enumerate(heads_of(n_head, o_self.shape[0])):
        dout[slot] = pack(d_o[:, g * width + a * HD : g * width + (a + 1) * HD])
    h_two_t, decoded_t = turned(h_two), turned(decoded)
    for g in range(n_head):
        results = (
            contract_first(o_groups[g], d_two_low),
            product(h_two_t, d_pre[:, g * hidden : (g + 1) * hidden]),
            contract_first(activ[:, g * hidden : (g + 1) * hidden], d_branch),
            product(decoded_t, dlogits[:, g * classes : (g + 1) * classes]),
        )
        for m, result in zip((4, 5, 6, 7), results):
            matrix_into(stage, starts[m] - first_row, result, line)
        for b in range(shards):
            held[b, g, :shard_rows, :] = stage[pl.ds(b * shard_rows, shard_rows), :].astype(low)
        stored.append(move(held.at[:, g], grads.at[shards_here, g]))
    for copy in stored:
        copy.wait()


def middle(counts, weights, common, z_one, o_self, out_queries_t, marks, gains, valid, n_head, shard_rows):
    rows = z_one.shape[0]
    begin, shards = shards_of(n_head, shard_rows, 4, 8)
    query_rows = DQ * D // LANES
    block, blocks = common_blocks(0, query_rows, valid)
    return pl.pallas_call(
        functools.partial(middle_kernel, n_head, shard_rows, valid, begin, rows),
        grid=(1,),
        out_shape=[
            shape_of(o_self.shape),
            shape_of((rows, D), jnp.float32),
            shape_of((8, LANES), jnp.float32),
            shape_of((query_rows, LANES), jnp.float32),
            shape_of((2, D), jnp.float32),
            shape_of(weights.shape),
        ],
        in_specs=[
            VMEM_SPEC,
            ANY_SPEC,
            ANY_SPEC,
            VMEM_SPEC,
            VMEM_SPEC,
            pl.BlockSpec((DQ, rows), lambda i: (0, lax.axis_index("head"))),
            VMEM_SPEC,
            VMEM_SPEC,
            VMEM_SPEC,
            VMEM_SPEC,
        ],
        out_specs=[VMEM_SPEC] * 3 + [ANY_SPEC, VMEM_SPEC, ANY_SPEC],
        scratch_shapes=[
            pltpu.VMEM((shards,) + weights.shape[1:], low),
            pltpu.VMEM((blocks,) + common.shape[1:], low),
            pltpu.VMEM((shards * shard_rows, LANES), jnp.float32),
            pltpu.VMEM((blocks * valid, LANES), jnp.float32),
            LINE,
            pltpu.VMEM((query_rows, LANES), jnp.float32),
            pltpu.VMEM((D, D), low),
            pltpu.VMEM((D, FF), low),
            pltpu.VMEM((FF, D), low),
            pltpu.VMEM((D, C), low),
            pltpu.VMEM((DQ, D), low),
            pltpu.VMEM((rows, FF), jnp.float32),
            pltpu.VMEM((rows, FF), low),
            pltpu.SemaphoreType.DMA((2 + 2 * n_head,)),
        ],
        compiler_params=pltpu.CompilerParams(vmem_limit_bytes=56 * MIB),
        name="middle",
    )(counts, weights, common, z_one, o_self, out_queries_t, *marks, gains)


def ending_kernel(
    n_head,
    shard_rows,
    valid,
    rows,
    lengths,
    grads_in,
    d_q_self,
    d_kv_self,
    gains,
    gain_grads,
    *refs,
):
    kept_in, (grads, common_grad), kept = refs[:14], refs[14:16], refs[16:30]
    held, stage, stage_common, line, d_q, d_kv, sems = refs[30:]
    (
        d_two,
        query_grad,
        enc_query,
        enc_keyval,
        enc_output,
        self_project,
        z_zero,
        h_zero,
        x_norm_t,
        q_enc,
        kv_enc,
        o_enc,
        z_one,
        h_one,
    ) = kept
    move = Moves(sems)
    first_used = (12, 5, 0, 4, 10, 9, 2, 6, 1, 7, 8, 11, 3, 13)
    loads = {i: move(kept_in[i], kept[i]) for i in first_used}

    def need(*which):
        for i in which:
            loads[i].wait()

    heads = HEADS // n_head
    width = heads * HD
    shards = held.shape[0]
    starts = borders(n_head)
    shared = move(grads_in.at[pl.ds(shards - 1, 1)], held.at[pl.ds(shards - 1, 1)])
    d_heads = {}
    for slot, head in enumerate(heads_of(n_head, d_kv_self.shape[0])):
        d_kv_head = d_kv_self[slot]
        d_heads[head] = (unpack(d_q_self[slot]), d_kv_head[:, :HD], d_kv_head[:, HD:])
    d_projected = [
        jnp.concatenate([d_heads[(g, a)][i] for i in range(3) for a in range(heads)], 1)
        for g in range(n_head)
    ]
    whole = jnp.concatenate(d_projected, 1)
    need(12, 5, 0)
    d_middle, gain_one_grad = norm_pullback(
        z_one[...], gains[1:2, :], against(whole, self_project[...])
    )
    d_one = d_two[...] + d_middle
    d_one_low = d_one.astype(low)
    need(4, 10, 9)
    d_o = against(d_one_low, enc_output[...]).astype(low)
    for g in range(n_head):
        keys = kv_enc[:, 2 * g * width : (2 * g + 1) * width]
        values = kv_enc[:, (2 * g + 1) * width : (2 * g + 2) * width]
        d_key = jnp.zeros(keys.shape, jnp.float32)
        d_value = jnp.zeros(keys.shape, jnp.float32)
        d_query_t = []
        keys_t = turned(keys)
        for (here, q_head), (unused, do_head) in zip(
            head_lanes(g, heads, q_enc[...]), head_lanes(g, heads, d_o)
        ):
            scores = enc_scores(keys, q_head)
            probs = jnp.exp2((scores - jnp.max(scores, 0, keepdims=True)).astype(low))
            probs = probs.astype(jnp.float32)
            probs = probs / jnp.sum(probs, 0, keepdims=True)
            d_probs = against(values, do_head)
            delta = jnp.sum(probs * d_probs, 0, keepdims=True)
            d_scores = (probs * (d_probs - delta)).astype(low)
            d_value = d_value + product(probs.astype(low), do_head)
            d_key = d_key + product(d_scores, q_head)
            a = len(d_query_t)
            d_query_t.append(product(keys_t[a * HD : (a + 1) * HD], d_scores))
        d_query = jnp.concatenate(d_query_t, 0).T
        d_q[:, g * width : (g + 1) * width] = (d_query * SCORE_SCALE).astype(low)
        d_kv[:, 2 * g * width : (2 * g + 1) * width] = (d_key * SCORE_SCALE).astype(low)
        d_kv[:, (2 * g + 1) * width : (2 * g + 2) * width] = d_value.astype(low)
    need(2, 6)
    d_middle, gain_zero_grad = norm_pullback(
        z_zero[...], gains[0:1, :], against(d_q[...], enc_query[...])
    )
    d_zero = d_one + d_middle
    d_zero_top = d_zero.astype(low)
    d_zero_rest = (d_zero - d_zero_top.astype(jnp.float32)).astype(low)
    picked_t = picked_rows(clip_bounds(lengths), rows, n_head, 1)
    latent_grad = product(picked_t, d_zero_top) + product(picked_t, d_zero_rest)
    need(1, 7, 8, 11, 3, 13)
    query_rows = query_grad.shape[0]
    stage_common[:query_rows] = query_grad[...]
    matrix_into(stage_common, query_rows, latent_grad, line)
    all_gains = jnp.concatenate([gain_zero_grad, gain_one_grad, gain_grads[...]], 0)
    matrix_into(stage_common, query_rows + LAT * D // LANES, all_gains, line)
    piece = common_grad.shape[2]
    for b in range(common_grad.shape[0]):
        for k in range(common_grad.shape[1]):
            amount = min(piece, valid - k * piece)
            block = stage_common[b * valid + k * piece : b * valid + k * piece + amount, :]
            if amount < piece:
                block = jnp.concatenate([block, jnp.zeros((piece - amount, LANES), jnp.float32)], 0)
            common_grad[b, k] = block.astype(low)
    shared.wait()
    shared_rows = shards * shard_rows - starts[4]
    stored = []
    h_zero_t, h_one_t = turned(h_zero[...]), turned(h_one[...])
    for g in range(n_head):
        results = (
            product(h_zero_t, d_q[:, g * width : (g + 1) * width]),
            product(x_norm_t[...], d_kv[:, 2 * g * width : (2 * g + 2) * width]),
            contract_first(o_enc[:, g * width : (g + 1) * width], d_one_low),
            product(h_one_t, d_projected[g]),
        )
        if shared_rows:
            stage[pl.ds((shards - 1) * shard_rows, shard_rows), :] = held[
                shards - 1, g, :shard_rows, :
            ].astype(jnp.float32)
        for m, result in zip((0, 1, 2, 3), results):
            matrix_into(stage, starts[m], result, line)
        for b in range(shards):
            held[b, g, :shard_rows, :] = stage[pl.ds(b * shard_rows, shard_rows), :].astype(low)
        stored.append(move(held.at[:, g], grads.at[pl.ds(0, shards), g]))
    for copy in stored:
        copy.wait()


def ending(lengths, grads, d_self, d_two, gains, gain_grads, query_grad, kept, common_shape, valid, shard_rows):
    rows = d_two.shape[0]
    n_head = grads.shape[1]
    begin, shards = shards_of(n_head, shard_rows, 0, 4)
    kept = (d_two, query_grad) + tuple(kept)
    keys = kept[8].shape[1]
    common_rows = (DQ + LAT + 4) * D // LANES
    return pl.pallas_call(
        functools.partial(ending_kernel, n_head, shard_rows, valid, rows),
        out_shape=[shape_of(grads.shape), shape_of(common_shape)],
        in_specs=[SMEM_SPEC, ANY_SPEC] + [VMEM_SPEC] * 4 + [ANY_SPEC] * len(kept),
        out_specs=[ANY_SPEC, VMEM_SPEC],
        input_output_aliases={1: 0},
        scratch_shapes=[pltpu.VMEM(a.shape, a.dtype) for a in kept]
        + [
            pltpu.VMEM((shards,) + grads.shape[1:], low),
            pltpu.VMEM((shards * shard_rows, LANES), jnp.float32),
            pltpu.VMEM((common_rows, LANES), jnp.float32),
            LINE,
            pltpu.VMEM((rows, D), low),
            pltpu.VMEM((keys, 2 * D), low),
            pltpu.SemaphoreType.DMA((len(kept) + 1 + n_head,)),
        ],
        compiler_params=pltpu.CompilerParams(vmem_limit_bytes=56 * MIB),
        name="ending",
    )(lengths, grads, *d_self, gains, gain_grads, *kept)


def adam_step(weight, first, second, grad):
    first = beta_one * first + (1 - beta_one) * grad
    second = beta_two * second + (1 - beta_two) * grad * grad
    fixed_first = first / (1 - beta_one**STEP)
    fixed_second = second / (1 - beta_two**STEP)
    weight = weight - learn_rate * (
        fixed_first / (jnp.sqrt(fixed_second) + adam_eps) + weight_decay * weight
    )
    return (weight, first, second, weight.astype(low))


def per_device(
    inputs,
    out_queries,
    clip_lengths,
    labels,
    modality,
    labeled,
    head_params,
    head_first,
    head_second,
    common_params,
    common_first,
    common_second,
):
    n_head, n_blk = lax.axis_size("head"), lax.axis_size("blk")
    dims = grid_of(n_blk, n_head)
    rows = labels.shape[0] // n_head
    n_h, n_c = head_params.shape[0], common_params.shape[0]
    shard_rows, common_rows = n_h // LANES, -(-n_c // LANES)
    head_rows = round_up(shard_rows + 1, TILE)
    piece_rows = round_up(-(-common_rows // n_head), TILE)
    marks = [x.reshape(-1, LANES) for x in (labels, modality, labeled)]
    head_wide = head_params.reshape(shard_rows, LANES)
    common_wide = jnp.pad(common_params, (0, common_rows * LANES - n_c)).reshape(common_rows, LANES)
    weights, common = gather_all(dims, marks, (head_wide, common_wide), (head_rows, piece_rows), 0)
    valid = common_rows
    if n_c % LANES:
        common = common.reshape(n_blk, -1)[:, :n_c].reshape(-1, LANES)
        valid = common.shape[0]
        common = jnp.pad(common, ((0, -valid % TILE), (0, 0)))[None, None]

    encoded = encode(
        clip_lengths, weights, common, inputs.T, valid, rows, Team(dims).size, n_head, shard_rows
    )
    gains, z_one, counts = encoded[4], encoded[11], encoded[15]
    o_self, lse_self, out_self_t, q_all, kv_all = attend(
        dims, clip_lengths, encoded[13], encoded[14], 1
    )
    dout, d_two, tile, query_grad, gain_grads, grads = middle(
        counts, weights, common, z_one, o_self, out_queries.T, marks, gains, valid, n_head, shard_rows
    )
    d_self = attend_back(dims, clip_lengths, q_all, kv_all, dout, out_self_t, lse_self, 2)
    kept = encoded[:4] + encoded[5:13]
    grads, common_grad = ending(
        clip_lengths,
        grads,
        d_self,
        d_two,
        gains,
        gain_grads,
        query_grad,
        kept,
        common.shape,
        valid,
        shard_rows,
    )
    if n_c % LANES:
        common_grad = common_grad[0, 0, :valid].reshape(n_blk, n_c)
        common_grad = jnp.pad(common_grad, ((0, 0), (0, n_head * piece_rows * LANES - n_c)))
        common_grad = common_grad.reshape(n_blk, n_head, piece_rows, LANES)
    head_share, common_share, loss_sums, clip_norm, factor = reduce_all(
        dims, (grads, common_grad), (shard_rows, common_rows), tile, 3
    )
    label_counts, loss_sums = encoded[16].reshape(MODES), loss_sums.reshape(MODES)
    clip_norm, factor = clip_norm.reshape(()), factor.reshape(())
    head_share, common_share = head_share.reshape(-1), common_share.reshape(-1)[:n_c]
    head_out = adam_step(head_params, head_first, head_second, head_share * factor)
    common_out = adam_step(common_params, common_first, common_second, common_share * factor)
    return head_out + common_out + (loss_sums, label_counts, clip_norm)


def solution(mesh):
    placed = (
        P("blk", None),
        P("blk", None),
        P(),
        P("blk"),
        P("blk"),
        P("blk"),
        P(("head", "blk")),
        P(("head", "blk")),
        P(("head", "blk")),
        P("blk"),
        P("blk"),
        P("blk"),
    )
    return jax.shard_map(
        per_device,
        mesh=mesh,
        in_specs=placed,
        out_specs=(
            P(("head", "blk")),
            P(("head", "blk")),
            P(("head", "blk")),
            P(("head", "blk")),
            P("blk"),
            P("blk"),
            P("blk"),
            P("blk"),
            P(),
            P(),
            P(),
        ),
        check_vma=False,
    )
```

```python
import functools

import jax
import jax.numpy as jnp
from jax import lax
from jax.experimental import pallas as pl
from jax.experimental.pallas import tpu as pltpu
from jax.sharding import PartitionSpec as P

D = 512
HEADS = 8
HD = 64
FF = 2048
DI = 704
DQ = 1026
C = 704
LAT = 784
MODES = 3
STEP = 10
LANES = 128
TILE = 16

norm_eps = 1e-05
learn_rate = 0.1
beta_one = 0.9
beta_two = 0.999
adam_eps = 1e-08
weight_decay = 0.01
clip_limit = 0.05
big_negative = -1e30
low = jnp.bfloat16
LOG2E = 1.4426950408889634
SCORE_SCALE = HD ** (-0.5)
MESH = pl.DeviceIdType.MESH
MIB = 1 << 20
VMEM_SPEC = pl.BlockSpec(memory_space=pltpu.VMEM)
SMEM_SPEC = pl.BlockSpec(memory_space=pltpu.SMEM)
ANY_SPEC = pl.BlockSpec(memory_space=pl.ANY)


def shape_of(shape, dtype=low):
    return jax.ShapeDtypeStruct(shape, dtype)


def round_up(n, unit):
    return -(-n // unit) * unit


def grid_of(n_blk, n_head):
    cores = 2 if n_head % 2 == 0 else 1
    x = n_head // cores
    y = x if n_blk % x == 0 else 1
    return (n_blk // y, y, x, cores)


def my_place(dims):
    blk, head = lax.axis_index("blk"), lax.axis_index("head")
    return (blk // dims[1], lax.rem(blk, dims[1]), head // dims[3], lax.rem(head, dims[3]))


def shifted(dims, me, offset, sign):
    return tuple(
        m if o == 0 else lax.rem(m + (o if sign > 0 else n - o), n)
        for m, o, n in zip(me, offset, dims)
    )


def blk_of(dims, place):
    return place[0] * dims[1] + place[1]


def head_of(dims, place):
    return place[2] * dims[3] + place[3]


def device_of(dims, place):
    return {"blk": blk_of(dims, place), "head": head_of(dims, place)}


def along(axis, d):
    return tuple(d if a == axis else 0 for a in range(4))


def greet(dims, me, offsets):
    announce(dims, me, offsets)
    pl.semaphore_wait(pltpu.get_barrier_semaphore(), len(offsets))


def announce(dims, me, offsets):
    barrier = pltpu.get_barrier_semaphore()
    for offset in offsets:
        pl.semaphore_signal(
            barrier,
            inc=1,
            device_id=device_of(dims, shifted(dims, me, offset, 1)),
            device_id_type=MESH,
        )


def axis_peers(dims, axes):
    return [along(axis, d) for axis in axes for d in range(1, dims[axis])]


def remote(src, dst, send_sem, recv_sem, place, dims):
    return pltpu.make_async_remote_copy(
        src_ref=src,
        dst_ref=dst,
        send_sem=send_sem,
        recv_sem=recv_sem,
        device_id=device_of(dims, place),
        device_id_type=MESH,
    )


AHEAD = 6.0
RING = 0


def in_order(first, follow, size_of, ahead, result):
    queues, busy, flight = {}, {}, {}
    now = 0.0

    def ready(messages):
        for message in messages:
            queues.setdefault(message[1], []).append(message)

    ready(first)
    while True:
        for axis in sorted(queues):
            queue, going = queues[axis], flight.setdefault(axis, [])
            while queue and (not going or busy[axis] < now + ahead):
                message = min(queue)
                queue.remove(message)
                busy[axis] = max(now, busy.get(axis, 0.0)) + size_of(message)
                going.append((busy[axis] + 1.5, message))
                result.append((True, message))
        arrivals = [min(going) for going in flight.values() if going]
        if not arrivals:
            return now
        arrival = min(arrivals)
        flight[arrival[1][1]].remove(arrival)
        now = max(now, arrival[0])
        result.append((False, arrival[1]))
        ready(follow(arrival[1]))


def time_of(rows, axis):
    return rows * LANES * 2 / (300e3 if axis == 3 else 45e3)


def with_at(offset, axis, d):
    return offset[:axis] + (d,) + offset[axis + 1 :]


def gather_order(dims, parts):
    def onward(p, offset, position):
        order = parts[p][3]
        result = []
        for k in range(max(position, 0), 4):
            axis = order[k]
            n = dims[axis]
            if k > position:
                steps = [1] if axis == RING else range(1, n)
                steps = [d for d in steps if d < n]
            else:
                steps = [offset[axis] + 1] if axis == RING and offset[axis] + 1 < n else []
            for d in steps:
                result.append(((k, sum(offset), p), axis, p, with_at(offset, axis, d)))
        return result

    def follow(message):
        rank, axis, p, offset = message
        return onward(p, offset, rank[0])

    first = [m for p in range(len(parts)) for m in onward(p, (0, 0, 0, 0), -1)]
    result = []
    now = in_order(first, follow, lambda m: time_of(parts[m[2]][2], m[1]), AHEAD, result)
    return result, now


def gather_kernel(
    dims,
    parts,
    labels,
    modality,
    labeled,
    head_params,
    common_params,
    head_all,
    common_all,
    head_low,
    common_low,
    common_wide,
    send_sem,
    recv_sem,
    own_sem,
):
    me = my_place(dims)
    met = ring_and_others(dims)
    announce(dims, me, met)
    my_head = head_of(dims, me)
    n_head = dims[2] * dims[3]
    shard_rows, common_rows = head_params.shape[0], common_params.shape[0]
    per_head = labels.shape[0] // n_head
    row = lax.broadcasted_iota(jnp.int32, labels.shape, 0)
    mine = (row >= my_head * per_head) & (row < (my_head + 1) * per_head) & (labeled[...] == 1)
    lane = lax.broadcasted_iota(jnp.int32, (1, LANES), 1)
    counts = jnp.zeros((1, LANES), jnp.float32)
    for m in range(MODES):
        member = jnp.where(mine & (modality[...] == m), 1.0, 0.0)
        counts = counts + jnp.where(lane == m, jnp.sum(member, (0, 1), keepdims=True), 0.0)
    padding = head_low.shape[0] - shard_rows
    tail = shard_rows // TILE * TILE
    head_low[:tail] = head_params[:tail].astype(low)
    last = [jnp.broadcast_to(counts, (padding, LANES))]
    if shard_rows > tail:
        last = [head_params[tail:]] + last
    head_low[tail:] = jnp.concatenate(last, 0).astype(low)
    common_wide[...] = jnp.zeros(common_wide.shape, jnp.float32)
    common_wide[:common_rows] = common_params[...]
    piece = common_low.shape[0]
    common_low[...] = common_wide[pl.ds(pl.multiple_of(my_head * piece, TILE), piece)].astype(low)

    pl.semaphore_wait(pltpu.get_barrier_semaphore(), len(met))
    srcs, outs = (head_low, common_low), (head_all, common_all)
    copies = {}

    def block(p, offset):
        place = shifted(dims, me, offset, -1)
        array, first, rows, order = parts[p]
        return outs[array].at[blk_of(dims, place), head_of(dims, place), pl.ds(first, rows)]

    own = []
    for is_send, (rank, axis, p, offset) in gather_order(dims, parts)[0]:
        if is_send:
            step = 1 if axis == RING else offset[axis]
            before = with_at(offset, axis, offset[axis] - step)
            array, first, rows, order = parts[p]
            source = block(p, before) if any(before) else srcs[array].at[pl.ds(first, rows)]
            i = len(copies)
            copies[(p, offset)] = remote(
                source,
                block(p, before),
                send_sem.at[i],
                recv_sem.at[i],
                shifted(dims, me, along(axis, step), 1),
                dims,
            )
            copies[(p, offset)].start()
        else:
            if not own:
                for array in range(2):
                    copy = pltpu.make_async_copy(
                        srcs[array], outs[array].at[blk_of(dims, me), my_head], own_sem.at[array]
                    )
                    copy.start()
                    own.append(copy)
            copies[(p, offset)].wait_recv()
    for copy in copies.values():
        copy.wait_send()
    for copy in own:
        copy.wait()


def ring_and_others(dims):
    ring = {along(RING, 1 % dims[RING]), along(RING, (dims[RING] - 1) % dims[RING])}
    return sorted(ring - {(0, 0, 0, 0)}) + axis_peers(dims, (1, 2, 3))


def cut(array, rows, shares):
    result = []
    first, so_far = 0, 0
    whole = sum(share for share, order in shares)
    for share, order in shares:
        so_far += share
        end = rows * so_far // whole // TILE * TILE if so_far < whole else rows
        if end > first:
            result.append((array, first, end - first, order))
        first = end
    return tuple(result)


ZYXC, ZXYC, YXZC, XYZC = (0, 1, 2, 3), (0, 2, 1, 3), (1, 2, 0, 3), (2, 1, 0, 3)
HEAD_SHARES = ((15, ZYXC), (13, ZXYC), (4, YXZC), (5, XYZC))
COMMON_SHARES = ((1, ZYXC), (1, ZXYC))


def gather_all(dims, marks, params, rows, collective_id):
    z, y, x, cores = dims
    parts = cut(0, rows[0], HEAD_SHARES) + cut(1, rows[1], COMMON_SHARES)
    count = len(parts) * (z * y * x * cores - 1)
    return pl.pallas_call(
        functools.partial(gather_kernel, dims, parts),
        out_shape=[shape_of((z * y, x * cores, n, LANES)) for n in rows],
        in_specs=[VMEM_SPEC] * 5,
        out_specs=[ANY_SPEC] * 2,
        scratch_shapes=[pltpu.VMEM((n, LANES), low) for n in rows]
        + [
            pltpu.VMEM((x * cores * rows[1], LANES), jnp.float32),
            pltpu.SemaphoreType.DMA((count,)),
            pltpu.SemaphoreType.DMA((count,)),
            pltpu.SemaphoreType.DMA((2,)),
        ],
        compiler_params=pltpu.CompilerParams(collective_id=collective_id, has_side_effects=True),
        name="gather_weights",
    )(*marks, *params)


def reduce_order(dims, parts):
    ready, arrived, order = set(), set(), []

    def message(p, position, offset):
        z = offset[RING]
        rank = (dims[RING] - z if z else dims[RING], position, tuple(-o for o in offset), p)
        return (rank, parts[p][3][position], p, position, offset)

    def done(p, position, offset):
        ready.add((p, position, offset))
        if position == 4:
            return []
        axis = parts[p][3][position]
        d = offset[axis]
        first = d != 0 and (axis != RING or d == dims[axis] - 1)
        return ([message(p, position, offset)] if first else []) + advance(p, position, offset)

    def advance(p, position, offset):
        axis = parts[p][3][position]
        n = dims[axis]
        start = with_at(offset, axis, 0)
        if axis == RING:
            here = (p, position, offset)
            if here in ready and here in arrived:
                order.append((None, here))
                if offset[axis]:
                    return [message(p, position, offset)]
                return done(p, position + 1, offset)
        elif (p, position, start) in ready and (p, position + 1, start) not in ready:
            if all((p, position, with_at(start, axis, d)) in arrived for d in range(1, n)):
                order.append((None, (p, position, start)))
                return done(p, position + 1, start)
        return []

    def follow(sent):
        rank, axis, p, position, offset = sent
        here = with_at(offset, axis, offset[axis] - 1) if axis == RING else offset
        arrived.add((p, position, here))
        return advance(p, position, here)

    first = []
    for p in range(len(parts)):
        for offset in all_offsets(dims, range(4)):
            first += done(p, 0, offset)
    now = in_order(first, follow, lambda m: time_of(parts[m[2]][2], m[1]), AHEAD, order)
    return order, now


def all_offsets(dims, axes):
    offsets = [(0, 0, 0, 0)]
    for a in axes:
        offsets = [with_at(o, a, d) for o in offsets for d in range(dims[a])]
    return offsets


def reduce_kernel(dims, parts, *refs):
    srcs, tile = refs[:2], refs[2]
    head_out, common_out, losses, norm, factor = refs[3:8]
    places = len(parts) * 4
    buffers = refs[8 : 8 + places]
    head_sum, common_sum, shares, send_sem, recv_sem, near_tiles, far_tiles = refs[8 + places : 15 + places]
    held, held_sem = refs[15 + places : 17 + places], refs[17 + places]
    sums = (head_sum, common_sum)
    me = my_place(dims)
    z, y, x, cores = dims
    loads = [
        pltpu.make_async_copy(srcs[k].at[:, :, me[3]], held[k], held_sem.at[k]) for k in range(2)
    ]
    for load in loads:
        load.start()
    across = peers_across(dims)
    others = [o for o in all_offsets(dims, (0, 1)) if any(o)]
    met = ring_and_others(dims)
    greet(dims, me, met + [o for o in across + others if o not in met])
    push = Pushes(dims, me, send_sem, recv_sem)
    copies = {}

    def slot(p, position, offset):
        order = parts[p][3]
        axis = order[position]
        rest = [o for o in all_offsets(dims, order[position + 1 :])]
        k = rest.index(with_at(offset, axis, 0))
        return buffers[p * 4 + position].at[k, max(offset[axis] - 1, 0)]

    def summed(p, position, offset):
        array, first, rows, order = parts[p]
        if position == 0:
            place = shifted(dims, me, offset, 1)
            at = (blk_of(dims, place), place[2])
            if offset[3]:
                return srcs[array].at[(*at, place[3], pl.ds(first, rows))]
            if loads[array] is not None:
                loads[array].wait()
                loads[array] = None
            return held[array].at[(*at, pl.ds(first, rows))]
        return slot(p, position - 1, offset)

    def ring_slot(p, position, offset):
        axis = parts[p][3][position]
        return slot(p, position, with_at(offset, axis, offset[axis] + 1))

    def add(p, position, offset):
        array, first, rows, order = parts[p]
        axis = order[position]
        if axis == RING:
            arrivals = [ring_slot(p, position, offset)]
        else:
            arrivals = [slot(p, position, with_at(offset, axis, d)) for d in range(1, dims[axis])]
        mine = summed(p, position, offset)
        step = row_chunk(rows)

        @pl.loop(0, rows // step)
        def some_rows(n):
            at = pl.ds(pl.multiple_of(n * step, step), step)
            last = position == 3 and not any(offset)
            if len(arrivals) == 1 and not last:
                arrivals[0][at] = mine[at] + arrivals[0][at]
                return
            total = mine[at].astype(jnp.float32)
            for arrival in arrivals:
                total = total + arrival[at].astype(jnp.float32)
            if last:
                sums[array][pl.ds(pl.multiple_of(first + n * step, TILE), step)] = total
            else:
                arrivals[0][at] = total.astype(low)

    for is_send, what in reduce_order(dims, parts)[0]:
        if is_send is None:
            add(*what)
        elif is_send:
            rank, axis, p, position, offset = what
            d = offset[axis]
            started = axis != RING or d == dims[axis] - 1
            source = summed(p, position, offset) if started else ring_slot(p, position, offset)
            step = along(axis, 1 if axis == RING else d)
            copies[what] = push(source, slot(p, position, offset), step)
        else:
            copies[what].wait_recv()
    my_head, my_blk = head_of(dims, me), blk_of(dims, me)
    shares[my_head] = common_sum[...].astype(low)
    share_copies = [push(shares.at[my_head], shares.at[my_head], o) for o in across]
    amount = head_out.shape[0]
    head_out[...] = head_sum[:amount]
    squares = jnp.sum(head_sum[:amount] * head_sum[:amount], 0, keepdims=True)
    squares = squares + jnp.sum(common_sum[...] * common_sum[...], 0, keepdims=True)
    lane = lax.broadcasted_iota(jnp.int32, (1, LANES), 1)
    near_tiles[my_head] = tile[...] + jnp.where(
        lane == MODES, jnp.sum(squares, 1, keepdims=True), 0.0
    )
    near = [push(near_tiles.at[my_head], near_tiles.at[my_head], o) for o in across]
    for copy in near:
        copy.wait_recv()
    far_tiles[my_blk] = jnp.sum(near_tiles[...], 0)
    far = [push(far_tiles.at[my_blk], far_tiles.at[my_blk], o) for o in others]
    for copy in share_copies:
        copy.wait_recv()
    piece = shares.shape[1]
    for k in range(x * cores):
        amount = min(piece, common_out.shape[0] - k * piece)
        common_out[k * piece : k * piece + amount] = shares[k].astype(jnp.float32)[:amount]
    for copy in far:
        copy.wait_recv()
    totals = jnp.sum(far_tiles[...], 0)[:1]
    losses[...] = totals[:, :MODES]
    norm[...] = jnp.sqrt(totals[:, MODES : MODES + 1])
    factor[...] = jnp.minimum(1.0, clip_limit / norm[...])
    push.finish()


def row_chunk(rows):
    for count in (4, 3, 2):
        if rows % (count * TILE) == 0:
            return rows // count
    return rows


def reduce_all(dims, arrays, valid, tile, collective_id):
    z, y, x, cores = dims
    rows = [array.shape[2] for array in arrays]
    arrays = [array.reshape(z * y, x, cores, *array.shape[2:]) for array in arrays]
    parts = ()
    for array, shares in enumerate((HEAD_SHARES, COMMON_SHARES)):
        parts += cut(array, rows[array], [(share, order[::-1]) for share, order in shares])
    scratch = []
    for array, first, amount, order in parts:
        for position, axis in enumerate(order):
            rest = len(all_offsets(dims, order[position + 1 :]))
            scratch.append(pltpu.VMEM((rest, dims[axis] - 1, amount, LANES), low))
    count = len(parts) * (z * y * x * cores - 1) + 2 * (x * cores - 1) + z * y - 1
    return pl.pallas_call(
        functools.partial(reduce_kernel, dims, parts),
        out_shape=[
            shape_of((valid[0], LANES), jnp.float32),
            shape_of((valid[1], LANES), jnp.float32),
            shape_of((1, MODES), jnp.float32),
            shape_of((1, 1), jnp.float32),
            shape_of((1, 1), jnp.float32),
        ],
        in_specs=[ANY_SPEC] * 2 + [VMEM_SPEC],
        out_specs=[VMEM_SPEC] * 5,
        scratch_shapes=scratch
        + [pltpu.VMEM((n, LANES), jnp.float32) for n in rows]
        + [
            pltpu.VMEM((x * cores, rows[1], LANES), low),
            pltpu.SemaphoreType.DMA((count,)),
            pltpu.SemaphoreType.DMA((count,)),
            pltpu.VMEM((x * cores, 8, LANES), jnp.float32),
            pltpu.VMEM((z * y, 8, LANES), jnp.float32),
        ]
        + [pltpu.VMEM((z * y, x, n, LANES), low) for n in rows]
        + [pltpu.SemaphoreType.DMA((2,))],
        compiler_params=pltpu.CompilerParams(
            collective_id=collective_id, has_side_effects=True, vmem_limit_bytes=60 * MIB
        ),
        name="reduce_gradients",
    )(*arrays, tile)


def contract_first(a, b):
    return lax.dot_general(a, b, (((0,), (0,)), ((), ())), preferred_element_type=jnp.float32)


def product(a, b):
    return jnp.dot(a, b, preferred_element_type=jnp.float32)


def against(a, b):
    return lax.dot_general(a, b, (((1,), (1,)), ((), ())), preferred_element_type=jnp.float32)


def clip_bounds(lengths):
    result, first = [], 0
    for clip in range(lengths.shape[0]):
        end = first + lengths[clip]
        result.append((first, end))
        first = end
    return result


def clip_borders(bounds, place):
    opening = jnp.zeros(place.shape, jnp.int32)
    ending = jnp.full(place.shape, 1 << 30, jnp.int32)
    for clip, (begin, end) in enumerate(bounds):
        here = place == clip
        opening = jnp.where(here, begin, opening)
        ending = jnp.where(here, end, ending)
    return opening, ending


def low_half(axis):
    return lax.broadcasted_iota(jnp.int32, (1, LANES) if axis else (LANES, 1), axis) < HD


def with_key_tail(bounds, first_row, kv):
    clips = len(bounds)
    place = lax.broadcasted_iota(jnp.int32, (1, LANES), 1) - HD
    opening, ending = clip_borders(bounds, place)
    ones = jnp.where((place >= clips) & (place < clips + 3), 1.0, 0.0)
    row = first_row + lax.broadcasted_iota(jnp.int32, kv.shape, 0)
    tail = jnp.where((row >= opening) & (row < ending), ones, big_negative)
    return jnp.where(low_half(1), kv.astype(jnp.float32), tail).astype(low)


def with_value_tail(kv):
    place = lax.broadcasted_iota(jnp.int32, (1, LANES), 1)
    ones = jnp.where(place < 3, 1.0, 0.0)
    return jnp.where(low_half(1), ones, kv.astype(jnp.float32)).astype(low)


def in_three(place, value):
    top = value.astype(low).astype(jnp.float32)
    middle = (value - top).astype(low).astype(jnp.float32)
    bottom = value - top - middle
    return (
        jnp.where(place == 0, top, 0.0)
        + jnp.where(place == 1, middle, 0.0)
        + jnp.where(place == 2, bottom, 0.0)
    )


def with_query_tail(bounds, first_row, rows, extra):
    clips = len(bounds)
    place = lax.broadcasted_iota(jnp.int32, (HD, 1), 0)
    opening, ending = clip_borders(bounds, place)
    row = first_row + lax.broadcasted_iota(jnp.int32, (1, rows.shape[1]), 1)
    inside = (place < clips) & (row >= opening) & (row < ending)
    tail = jnp.where(inside, 1.0, 0.0)
    if extra is not None:
        tail = tail + in_three(place - clips, -extra)
    return jnp.concatenate([rows * (SCORE_SCALE * LOG2E), tail], 0).astype(low)


def pack(rows):
    half = rows.shape[0] // 2
    return jnp.concatenate([rows[:half], rows[half:]], 1)


def unpack(packed):
    return jnp.concatenate([packed[:, :HD], packed[:, HD:]], 0)


def unpack_t(packed):
    turned = packed.astype(jnp.float32).T
    return jnp.concatenate([turned[:HD], turned[HD:]], 1)


def pack_t(columns):
    half = columns.shape[1] // 2
    return jnp.concatenate([columns[:, :half], columns[:, half:]], 0).T


class Team:
    def __init__(self, dims):
        z, y, x, cores = dims
        self.dims = dims
        self.wide = HEADS // (x * cores) == y
        self.size = x * cores * (y if self.wide else 1)
        self.groups = z if self.wide else z * y
        axes = (1, 2, 3) if self.wide else (2, 3)
        offsets = [o for o in all_offsets(dims, axes) if any(o)]
        self.others = sorted(offsets, key=lambda o: (o[1] + o[2], o))
        self.sides = [] if self.wide else axis_peers(dims, (1,))

    def slot(self, place):
        head = head_of(self.dims, place)
        return place[1] * self.dims[2] * self.dims[3] + head if self.wide else head

    def group(self, place):
        return place[0] if self.wide else blk_of(self.dims, place)


def heads_of(n_head, slots):
    return [(s % n_head, s // n_head) for s in range(slots)]


class Pushes:
    def __init__(self, dims, me, send_sem, recv_sem):
        self.dims, self.me, self.send_sem, self.recv_sem = dims, me, send_sem, recv_sem
        self.started = []

    def later(self, src, dst, offset):
        i = len(self.started)
        place = shifted(self.dims, self.me, offset, 1)
        copy = remote(src, dst, self.send_sem.at[i], self.recv_sem.at[i], place, self.dims)
        self.started.append(copy)
        return copy

    def __call__(self, src, dst, offset):
        copy = self.later(src, dst, offset)
        copy.start()
        return copy

    def finish(self):
        for copy in self.started:
            copy.wait_send()


def peers_across(dims):
    z, y, x, cores = dims
    across = [(0, 0, a, c) for a in range(x) for c in range(cores) if (a, c) != (0, 0)]
    return sorted(across, key=lambda o: (o[2] == 0, o[3]))


def attend_kernel(
    team,
    query_step,
    key_step,
    pieces,
    lengths,
    q_in,
    kv_in,
    o_out,
    lse,
    out_t,
    q_all,
    kv_out,
    kv_all,
    even_keys,
    even_values_t,
    odd_keys,
    odd_values_t,
    queries,
    top,
    accum,
    even_scores,
    odd_scores,
    even_top,
    odd_top,
    o_mine,
    send_sem,
    recv_sem,
    own_sem,
):
    dims = team.dims
    z = dims[0]
    me = my_place(dims)
    bounds = clip_bounds(lengths)
    rows = kv_in.shape[1]
    amount = team.size * rows
    slots = team.size // pieces
    my_group, my_slot = team.group(me), team.slot(me)
    ring_ends = sorted({along(0, 1 % z), along(0, (z - 1) % z)} - {(0, 0, 0, 0)})
    greet(dims, me, team.others + ring_ends + team.sides)
    push = Pushes(dims, me, send_sem, recv_sem)
    own_kv = pltpu.make_async_copy(kv_in.at[my_slot], kv_all.at[my_group, my_slot], own_sem.at[0])
    own_q = pltpu.make_async_copy(q_in.at[my_slot], q_all.at[my_slot], own_sem.at[1])
    own_kv.start()
    own_q.start()

    def to_team(src, dst, o):
        return push(src.at[team.slot(shifted(dims, me, o, 1))], dst, o)

    kv_copies = {o: to_team(kv_in, kv_all.at[my_group, my_slot], o) for o in team.others}
    q_copies = [to_team(q_in, q_all.at[my_slot], o) for o in team.others]
    ring, side, slot_copies = {}, {}, []

    def group_at(offset):
        return team.group(shifted(dims, me, offset, -1))

    def send_slot(o):
        if z > 1:
            block = kv_all.at[my_group, team.slot(shifted(dims, me, o, -1))]
            slot_copies.append(push(block, block, along(0, 1)))

    def slot_arrived():
        for copy in slot_copies:
            copy.wait_recv()

    def send_on(s, piece):
        block = kv_all.at[group_at(along(0, s)), pl.ds(piece * slots, slots)]
        if 0 < s < z - 1:
            ring[(s + 1, piece)] = push(block, block, along(0, 1))
        for o in team.sides:
            side[(s, o, piece)] = push(block, block, o)

    def both(now, later):
        if now is not None:
            n, unused, now_values, now_scores, now_top = now
            at = tile(n)
            old = top[:, at]
            new = jnp.maximum(old, jnp.max(now_top[...], 0, keepdims=True))
            top[:, at] = new
            total = accum[:, at] * jnp.exp2(old - new)
        if later is not None:
            n, later_keys, unused, later_scores, later_top = later
            query = queries[:, tile(n)]
            highest = jnp.full(later_top.shape, -1e38, jnp.float32)
        for k in range(0, slots * rows, key_step):
            if later is not None:
                scores = product(later_keys[k : k + key_step, :], query)
                later_scores[k : k + key_step, :] = scores
                highest = jnp.maximum(
                    highest, jnp.max(scores.reshape(key_step // 8, 8, query_step), 0)
                )
            if now is not None:
                probs = jnp.exp2((now_scores[k : k + key_step, :] - new).astype(low))
                total = total + product(now_values[:, k : k + key_step], probs)
        if later is not None:
            later_top[...] = highest
        if now is not None:
            accum[:, at] = total

    def tile(n):
        return pl.ds(pl.multiple_of(n * query_step, query_step), query_step)

    computed, pending = [], [None]

    def compute(offset, piece):
        group = group_at(offset)
        keys, values_t = sides_of_keys[len(computed) % 2]
        computed.append(offset)

        @pl.loop(0, slots)
        def build(n):
            at = pl.ds(pl.multiple_of(n * rows, rows), rows)
            slot = piece * slots + n
            block = kv_all[group, slot]
            keys[at, :] = with_key_tail(bounds, group * amount + slot * rows, block)
            values_t[:HD, at] = block.astype(jnp.float32).T[HD:].astype(low)

        def even(n):
            return (n, keys, values_t, even_scores, even_top)

        def odd(n):
            return (n, keys, values_t, odd_scores, odd_top)

        tiles = amount // query_step
        both(pending[0], even(0))

        @pl.loop(0, tiles // 2 - 1)
        def query_blocks(n):
            both(even(2 * n), odd(2 * n + 1))
            both(odd(2 * n + 1), even(2 * n + 2))

        both(even(tiles - 2), odd(tiles - 1))
        pending[0] = odd(tiles - 1)

    sides_of_keys = ((even_keys, even_values_t), (odd_keys, odd_values_t))
    for unused, values_t in sides_of_keys:
        values_t[HD:, :] = jnp.ones((TILE, slots * rows), low)
    top[...] = jnp.full(top.shape, -1e38, jnp.float32)
    accum[...] = jnp.zeros(accum.shape, jnp.float32)
    own_kv.wait()
    send_slot((0, 0, 0, 0))
    for o in team.others:
        kv_copies[o].wait_recv()
        send_slot(o)
    for piece in range(pieces):
        send_on(0, piece)
    own_q.wait()
    for copy in q_copies:
        copy.wait_recv()
    for n in range(team.size):
        queries[:, n * rows : (n + 1) * rows] = with_query_tail(
            bounds, my_group * amount + n * rows, unpack_t(q_all[n]), None
        )
    stores = []

    def store(offset):
        group = group_at(offset)
        copy = pltpu.make_async_copy(kv_all.at[group], kv_out.at[group], own_sem.at[3 + len(stores)])
        copy.start()
        stores.append(copy)

    for s in range(z):
        store(along(0, s))
        for piece in range(pieces):
            compute(along(0, s), piece)
            if s < z - 1:
                if s:
                    ring[(s + 1, piece)].wait_recv()
                elif piece == 0:
                    slot_arrived()
                send_on(s + 1, piece)
            for o in team.sides:
                side[(s, o, piece)].wait_recv()
                compute((s, o[1], 0, 0), piece)
        for o in team.sides:
            store((s, o[1], 0, 0))
    both(pending[0], None)
    total = accum[HD : HD + 1, :]
    out_t[...] = accum[:HD, :] / total
    lse[...] = top[...] + jnp.log(total) * LOG2E
    for n in range(team.size):
        o_mine[n] = pack_t(out_t[:, n * rows : (n + 1) * rows]).astype(low)
    o_copies = [to_team(o_mine, o_out.at[my_slot], o) for o in team.others]
    own_o = pltpu.make_async_copy(o_mine.at[my_slot], o_out.at[my_slot], own_sem.at[2])
    own_o.start()
    own_o.wait()
    for copy in o_copies:
        copy.wait_recv()
    for copy in stores:
        copy.wait()
    push.finish()


def attend(dims, lengths, q, kv, collective_id):
    team = Team(dims)
    z = dims[0]
    amount = team.size * kv.shape[1]
    pieces, query_step = 2, 256
    count = 4 * team.size + pieces * (z + z * len(team.sides))
    return pl.pallas_call(
        functools.partial(attend_kernel, team, query_step, 256, pieces),
        out_shape=(
            jax.ShapeDtypeStruct(q.shape, low),
            jax.ShapeDtypeStruct((1, amount), jnp.float32),
            jax.ShapeDtypeStruct((HD, amount), jnp.float32),
            jax.ShapeDtypeStruct(q.shape, low),
            jax.ShapeDtypeStruct((team.groups,) + kv.shape, low),
        ),
        in_specs=[SMEM_SPEC, VMEM_SPEC, VMEM_SPEC],
        out_specs=[VMEM_SPEC] * 4 + [ANY_SPEC],
        scratch_shapes=[
            pltpu.VMEM((team.groups,) + kv.shape, low),
            pltpu.VMEM((amount // pieces, LANES), low),
            pltpu.VMEM((HD + TILE, amount // pieces), low),
            pltpu.VMEM((amount // pieces, LANES), low),
            pltpu.VMEM((HD + TILE, amount // pieces), low),
            pltpu.VMEM((LANES, amount), low),
            pltpu.VMEM((1, amount), jnp.float32),
            pltpu.VMEM((HD + TILE, amount), jnp.float32),
            pltpu.VMEM((amount // pieces, query_step), jnp.float32),
            pltpu.VMEM((amount // pieces, query_step), jnp.float32),
            pltpu.VMEM((8, query_step), jnp.float32),
            pltpu.VMEM((8, query_step), jnp.float32),
            pltpu.VMEM(q.shape, low),
            pltpu.SemaphoreType.DMA((count,)),
            pltpu.SemaphoreType.DMA((count,)),
            pltpu.SemaphoreType.DMA((3 + team.groups,)),
        ],
        compiler_params=pltpu.CompilerParams(
            collective_id=collective_id, has_side_effects=True, vmem_limit_bytes=56 * MIB
        ),
        name="attend",
    )(lengths, q, kv)


def attend_back_kernel(
    team,
    key_step,
    query_step,
    pieces,
    lengths,
    q_all,
    kv_in,
    do_in,
    out_t,
    lse,
    d_q_out,
    d_kv_out,
    kv_all,
    do_all,
    even_keys_t,
    even_values_t,
    even_rows,
    odd_keys_t,
    odd_values_t,
    odd_rows,
    queries,
    douts,
    d_q_sum,
    q_rows,
    do_rows,
    even_probs,
    odd_probs,
    even_scores,
    odd_scores,
    side_out,
    side_in,
    ring_out,
    ring_in,
    mine,
    d_q_mine,
    d_kv_mine,
    send_sem,
    recv_sem,
    own_sem,
):
    dims = team.dims
    z = dims[0]
    me = my_place(dims)
    bounds = clip_bounds(lengths)
    rows = kv_all.shape[2]
    amount = team.size * rows
    loads = {}
    for s in range(1, z + 1):
        for o in team.sides + [(0, 0, 0, 0)]:
            offset = ((z - s) % z, o[1], 0, 0)
            group = team.group(shifted(dims, me, offset, 1))
            loads[offset] = pltpu.make_async_copy(
                kv_in.at[group], kv_all.at[group], own_sem.at[3 + len(loads)]
            )
            loads[offset].start()
    slots = team.size // pieces
    piece_rows = slots * rows
    my_group, my_slot = team.group(me), team.slot(me)
    ring_ends = sorted({along(0, 1 % z), along(0, (z - 1) % z)} - {(0, 0, 0, 0)})
    greet(dims, me, team.others + ring_ends + team.sides)
    push = Pushes(dims, me, send_sem, recv_sem)

    def to_team(src, dst, o):
        return push(src.at[team.slot(shifted(dims, me, o, 1))], dst, o)

    do_copies = [to_team(do_in, do_all.at[my_slot], o) for o in team.others]
    own_do = pltpu.make_async_copy(do_in.at[my_slot], do_all.at[my_slot], own_sem.at[0])
    own_do.start()
    place = lax.broadcasted_iota(jnp.int32, (HD, 1), 0)
    for n in range(team.size):
        at = slice(n * rows, (n + 1) * rows)
        q_t = unpack_t(q_all[n])
        extended = with_query_tail(bounds, my_group * amount + n * rows, q_t, lse[:, at])
        queries[at, :] = extended.astype(jnp.float32).T.astype(low)
        q_rows[:, at] = (q_t * SCORE_SCALE).astype(low)
    d_q_sum[...] = jnp.zeros(d_q_sum.shape, jnp.float32)
    own_do.wait()
    for copy in do_copies:
        copy.wait_recv()
    for n in range(team.size):
        at = slice(n * rows, (n + 1) * rows)
        do_t = unpack_t(do_all[n])
        delta = jnp.sum(do_t * out_t[:, at], 0, keepdims=True)
        extended = jnp.concatenate([in_three(place, -delta), do_t], 0).astype(low)
        douts[at, :] = extended.astype(jnp.float32).T.astype(low)
        do_rows[:, at] = do_t.astype(low)

    def both(now, later):
        if now is not None:
            n, (unused, unused, now_rows), now_probs, now_scores, target = now
            now_at = rows_of(n)
        if later is not None:
            n, (keys_t, values_t, unused), later_probs, later_scores, unused = later
            at = rows_of(n)
        for first in range(0, amount, query_step):
            part = slice(first, first + query_step)
            if later is not None:
                probs = jnp.exp2(product(queries[part, :], keys_t[:, at]).astype(low))
                d_probs = product(douts[part, :], values_t[:, at])
                later_probs[part, :] = probs
                later_scores[part, :] = (probs.astype(jnp.float32) * d_probs).astype(low)
            if now is not None:
                if first == 0:
                    d_value = product(do_rows[...], now_probs[...])
                if first == amount // 2:
                    d_key = product(q_rows[...], now_scores[...])
                d_q_sum[part, :] = d_q_sum[part, :] + product(now_scores[part, :], now_rows[now_at, :])
        if now is not None:
            target[now_at, :] = jnp.concatenate([d_key, d_value], 0).T.astype(target.dtype)

    def rows_of(k):
        return slice(k * key_step, (k + 1) * key_step)

    computed, pending = [], []

    def flush(later=None):
        if pending:
            now, after = pending.pop()
            both(now, later)
            after()
        elif later is not None:
            both(None, later)

    def compute(offset, piece, target, after):
        group = team.group(shifted(dims, me, offset, 1))
        keys = sides_of_keys[len(computed) % 2]
        computed.append(offset)
        if offset in loads:
            loads.pop(offset).wait()

        @pl.loop(0, slots)
        def build(n):
            at = pl.ds(pl.multiple_of(n * rows, rows), rows)
            slot = piece * slots + n
            block = kv_all[group, slot]
            extended = with_key_tail(bounds, group * amount + slot * rows, block)
            keys[0][:, at] = extended.astype(jnp.float32).T.astype(low)
            keys[1][:, at] = with_value_tail(block).astype(jnp.float32).T.astype(low)
            keys[2][at, :] = block

        steps = [
            (k, keys) + ((odd_probs, odd_scores) if k % 2 else (even_probs, even_scores)) + (target,)
            for k in range(piece_rows // key_step)
        ]
        flush(steps[0])
        for now, later in zip(steps[:-1], steps[1:]):
            both(now, later)
        pending.append((steps[-1], after))

    sides_of_keys = (
        (even_keys_t, even_values_t, even_rows),
        (odd_keys_t, odd_values_t, odd_rows),
    )
    side, ring = {}, {}

    def send_sides(s, piece):
        for o in team.sides:
            target = side_out.at[s - 1, o[1] - 1, piece]

            def send(o=o, target=target):
                side[(s, o, piece)] = push(target, side_in.at[s - 1, o[1] - 1, piece], o)

            compute(((z - s) % z, o[1], 0, 0), piece, target, send)

    def combine(s, piece):
        for o in team.sides:
            side[(s, o, piece)].wait_recv()
        if s > 1:
            ring[(s - 1, piece)].wait_recv()
        for n in range(slots):
            at = slice(n * rows, (n + 1) * rows)
            total = mine[piece, at, :]
            for o in team.sides:
                total = total + side_in[s - 1, o[1] - 1, piece, at, :].astype(jnp.float32)
            if s > 1:
                total = total + ring_in[s - 2, piece, at, :].astype(jnp.float32)
            if s < z:
                ring_out[s - 1, piece, at, :] = total.astype(low)
            else:
                d_kv_mine[piece * slots + n] = total.astype(low)
        if s == z:
            for copy, slot in d_kv_copies:
                pl.when((slot >= piece * slots) & (slot < (piece + 1) * slots))(copy.start)
        if s < z:
            ring[(s, piece)] = push(ring_out.at[s - 1, piece], ring_in.at[s - 1, piece], along(0, 1))

    d_kv_copies = []
    for o in team.others:
        slot = team.slot(shifted(dims, me, o, 1))
        d_kv_copies.append((push.later(d_kv_mine.at[slot], d_kv_out.at[my_slot], o), slot))
    for s in range(1, z + 1):
        for piece in range(pieces):
            send_sides(s, piece)
            after = functools.partial(combine, s, piece)
            compute((z - s if s < z else 0, 0, 0, 0), piece, mine.at[piece], after)
    flush()
    for n in range(team.size):
        at = slice(n * rows, (n + 1) * rows)
        d_q_mine[n] = pack(d_q_sum[at, :HD] * SCORE_SCALE).astype(low)
    copies = [to_team(d_q_mine, d_q_out.at[my_slot], o) for o in team.others]
    own_q = pltpu.make_async_copy(d_q_mine.at[my_slot], d_q_out.at[my_slot], own_sem.at[1])
    own_q.start()
    copies += [copy for copy, slot in d_kv_copies]
    own_kv = pltpu.make_async_copy(d_kv_mine.at[my_slot], d_kv_out.at[my_slot], own_sem.at[2])
    own_kv.start()
    own_q.wait()
    own_kv.wait()
    for copy in copies:
        copy.wait_recv()
    push.finish()


def attend_back(dims, lengths, q, kv, dout, out_t, lse, collective_id):
    team = Team(dims)
    z = dims[0]
    rows = kv.shape[2]
    amount = team.size * rows
    pieces, key_step = 2, 256
    piece = (pieces, amount // pieces, LANES)
    count = 3 * (team.size - 1) + pieces * (z + z * len(team.sides))
    others = max(len(team.sides), 1)
    ring_steps, side_steps = max(z - 1, 1), z if team.sides else 1
    return pl.pallas_call(
        functools.partial(attend_back_kernel, team, key_step, 256, pieces),
        out_shape=(
            jax.ShapeDtypeStruct(q.shape, low),
            jax.ShapeDtypeStruct(kv.shape[1:], low),
        ),
        in_specs=[SMEM_SPEC, VMEM_SPEC, ANY_SPEC] + [VMEM_SPEC] * 3,
        out_specs=[VMEM_SPEC] * 2,
        scratch_shapes=[
            pltpu.VMEM(kv.shape, low),
            pltpu.VMEM(q.shape, low),
            pltpu.VMEM((LANES, amount // pieces), low),
            pltpu.VMEM((LANES, amount // pieces), low),
            pltpu.VMEM((amount // pieces, LANES), low),
            pltpu.VMEM((LANES, amount // pieces), low),
            pltpu.VMEM((LANES, amount // pieces), low),
            pltpu.VMEM((amount // pieces, LANES), low),
            pltpu.VMEM((amount, LANES), low),
            pltpu.VMEM((amount, LANES), low),
            pltpu.VMEM((amount, LANES), jnp.float32),
            pltpu.VMEM((HD, amount), low),
            pltpu.VMEM((HD, amount), low),
            pltpu.VMEM((amount, key_step), low),
            pltpu.VMEM((amount, key_step), low),
            pltpu.VMEM((amount, key_step), low),
            pltpu.VMEM((amount, key_step), low),
            pltpu.VMEM((side_steps, others) + piece, low),
            pltpu.VMEM((side_steps, others) + piece, low),
            pltpu.VMEM((ring_steps,) + piece, low),
            pltpu.VMEM((ring_steps,) + piece, low),
            pltpu.VMEM(piece, jnp.float32),
            pltpu.VMEM(q.shape, low),
            pltpu.VMEM(kv.shape[1:], low),
            pltpu.SemaphoreType.DMA((count,)),
            pltpu.SemaphoreType.DMA((count,)),
            pltpu.SemaphoreType.DMA((3 + team.groups,)),
        ],
        compiler_params=pltpu.CompilerParams(
            collective_id=collective_id, has_side_effects=True, vmem_limit_bytes=60 * MIB
        ),
        name="attend_back",
    )(lengths, q, kv, dout, out_t, lse)


def part_shapes(n_head):
    width = HEADS // n_head * HD
    hidden = FF // n_head
    return (
        (D, width, True),
        (DI, 2 * width, True),
        (width, D, False),
        (D, 3 * width, True),
        (width, D, False),
        (D, hidden, True),
        (hidden, D, False),
        (D, C // n_head, True),
    )


def borders(n_head):
    result = [0]
    for rows, columns, joined in part_shapes(n_head):
        result.append(result[-1] + rows * columns // LANES)
    return result


def period(columns):
    amount = 1
    while amount * columns % LANES:
        amount *= 2
    return amount


def segments(start, amount, unit):
    result = []
    while amount > 0:
        which, at = divmod(start, unit)
        size = min(unit - at, amount)
        result.append((which, at, at + size))
        start, amount = start + size, amount - size
    return result


def joined_lanes(pieces):
    return pieces[0] if len(pieces) == 1 else jnp.concatenate(pieces, 1)


def lane_blocks(value):
    rows, columns = value.shape
    missing = -columns % LANES
    if missing:
        value = jnp.concatenate([value, jnp.zeros((rows, missing), value.dtype)], 1)
    return [value[:, i : i + LANES] for i in range(0, columns + missing, LANES)]


def every(first, amount, stride):
    return pl.ds(first, amount) if stride == 1 else pl.ds(first, amount, stride=stride)


def matrix_of(stage, first, rows, columns, line):
    if columns % LANES == 0:
        stride = columns // LANES
        for j in range(stride):
            yield j * LANES, stage[every(first + j, rows, stride), :]
        return
    height = period(columns)
    stride = height * columns // LANES
    for k in range(height):
        pieces = [
            stage[every(first + which, rows // height, stride), :][:, begin:end]
            for which, begin, end in segments(k * columns, columns, LANES)
        ]
        for i, piece in enumerate(lane_blocks(joined_lanes(pieces))):
            line[i, every(k, rows // height, height), :] = piece
    for i in range(-(-columns // LANES)):
        yield i * LANES, line[i, :rows, : min(columns - i * LANES, LANES)]


def matrix_into(stage, first, value, line):
    rows, columns = value.shape
    if columns % LANES == 0:
        stride = columns // LANES
        for j in range(stride):
            stage[every(first + j, rows, stride), :] = value[:, j * LANES : (j + 1) * LANES]
        return
    height = period(columns)
    stride = height * columns // LANES
    for i, piece in enumerate(lane_blocks(value)):
        line[i, :rows, :] = piece
    for i in range(stride):
        pieces = [
            line[which, every(k, rows // height, height), :][:, begin:end]
            for k, first_lane, last_lane in segments(i * LANES, LANES, columns)
            for which, begin, end in segments(first_lane, last_lane - first_lane, LANES)
        ]
        stage[every(first + i, rows // height, stride), :] = joined_lanes(pieces)


def load_stage(stage, held, first_shard, shard_rows, group):
    for b in range(held.shape[0]):
        stage[pl.ds(b * shard_rows, shard_rows), :] = held[b, group, :shard_rows, :].astype(jnp.float32)


def load_common(stage, held, valid):
    piece = held.shape[2]
    for b in range(held.shape[0]):
        for k in range(held.shape[1]):
            amount = min(piece, valid - k * piece)
            stage[b * valid + k * piece : b * valid + k * piece + amount, :] = held[b, k].astype(
                jnp.float32
            )[:amount]


def common_blocks(first_row, last_row, valid):
    return first_row // valid, -(-last_row // valid) - first_row // valid


def load_matrices(stage, first_row, n_head, group, which, targets, line):
    starts, shapes = borders(n_head), part_shapes(n_head)
    for m, target in zip(which, targets):
        rows, columns, joined = shapes[m]
        row = 0 if joined else group * rows
        column = group * columns if joined else 0
        for j, value in matrix_of(stage, starts[m] - first_row, rows, columns, line):
            size = value.shape[1]
            target[row : row + rows, column + j : column + j + size] = value.astype(target.dtype)


class Moves:
    def __init__(self, sems):
        self.sems, self.going = sems, []

    def __call__(self, src, dst):
        copy = pltpu.make_async_copy(src, dst, self.sems.at[len(self.going)])
        copy.start()
        self.going.append(copy)
        return copy


def normalized(x):
    centre = x - jnp.mean(x, -1, keepdims=True)
    rate = lax.rsqrt(jnp.mean(centre * centre, -1, keepdims=True) + norm_eps)
    return centre * rate, rate


def layer_norm(x, gain):
    return normalized(x)[0] * gain


def norm_pullback(x, gain, grad):
    unit, rate = normalized(x)
    inside = grad * gain
    both = jnp.mean(inside * unit, -1, keepdims=True)
    d_x = rate * (inside - jnp.mean(inside, -1, keepdims=True) - unit * both)
    return d_x, jnp.sum(grad * unit, 0, keepdims=True)


def turned(value):
    return value.astype(jnp.float32).T.astype(low)


def head_lanes(group, heads, value):
    width = heads * HD
    block = value[:, group * width : (group + 1) * width]
    lane = lax.broadcasted_iota(jnp.int32, (1, width), 1)
    result = []
    for a in range(heads):
        here = (lane >= a * HD) & (lane < (a + 1) * HD)
        result.append((here, jnp.where(here, block, jnp.zeros_like(block))))
    return result


def place_of(bounds, first, amount, axis):
    shape = (1, amount) if axis else (amount, 1)
    row = first + lax.broadcasted_iota(jnp.int32, shape, axis)
    opening = jnp.zeros(shape, jnp.int32)
    for begin, end in bounds:
        opening = jnp.where((row >= begin) & (row < end), begin, opening)
    offset = row - opening
    turns = jnp.floor((offset.astype(jnp.float32) + 0.5) * (1.0 / LAT)).astype(jnp.int32)
    return offset - turns * LAT


def picked_rows(bounds, rows, n_head, axis=0):
    first = lax.axis_index("blk") * (rows * n_head) + lax.axis_index("head") * rows
    shape = (LAT, rows) if axis else (rows, LAT)
    latent = lax.broadcasted_iota(jnp.int32, shape, 1 - axis)
    return jnp.where(latent == place_of(bounds, first, rows, axis), 1.0, 0.0).astype(low)


def enc_scores(q_head, keys):
    return against(q_head, keys) * (SCORE_SCALE * LOG2E)


def encode_kernel(
    n_head,
    shard_rows,
    valid,
    rows,
    lengths,
    weights,
    common,
    inputs_t,
    enc_query,
    enc_keyval,
    enc_output,
    self_project,
    gains,
    z_zero,
    h_zero,
    x_norm_t,
    q_enc,
    kv_enc,
    o_enc,
    z_one,
    h_one,
    q_self,
    kv_self,
    counts,
    label_counts,
    held,
    held_common,
    held_counts,
    stage,
    stage_common,
    line,
    latent_table,
    sems,
):
    heads = HEADS // n_head
    width = heads * HD
    shards = held.shape[0]
    bounds = clip_bounds(lengths)
    first = DQ * D // LANES
    block, blocks = common_blocks(first, first + (LAT + 4) * D // LANES, valid)
    tail = shard_rows // TILE * TILE
    copies = [
        pltpu.make_async_copy(common.at[pl.ds(block, blocks)], held_common, sems.at[0]),
        pltpu.make_async_copy(weights.at[pl.ds(0, shards)], held, sems.at[1]),
        pltpu.make_async_copy(weights.at[:, :, pl.ds(tail, TILE)], held_counts, sems.at[2]),
    ]
    for copy in copies:
        copy.start()
    centre = inputs_t[...].astype(jnp.float32)
    centre = centre - jnp.mean(centre, 0, keepdims=True)
    rate = lax.rsqrt(jnp.mean(centre * centre, 0, keepdims=True) + norm_eps)
    x_norm_t[...] = (centre * rate).astype(low)
    copies[0].wait()
    load_common(stage_common, held_common, valid)
    first = first - block * valid
    for j, value in matrix_of(stage_common, first, LAT, D, line):
        latent_table[:, j : j + LANES] = value.astype(low)
    for j, value in matrix_of(stage_common, first + LAT * D // LANES, 4, D, line):
        gains[:, j : j + LANES] = value
    picked = picked_rows(bounds, rows, n_head)
    z_zero[...] = product(picked, latent_table[...])
    h_zero[...] = layer_norm(z_zero[...], gains[0:1, :]).astype(low)
    copies[2].wait()
    counted = held_counts[...].astype(jnp.float32)[:, :, shard_rows - tail : shard_rows - tail + 1]
    counts[...] = jnp.broadcast_to(jnp.sum(counted, (0, 1)), counts.shape)
    label_counts[...] = counts[:1, :MODES]
    copies[1].wait()
    for g in range(n_head):
        load_stage(stage, held, 0, shard_rows, g)
        load_matrices(
            stage, 0, n_head, g, (0, 1, 2, 3), (enc_query, enc_keyval, enc_output, self_project), line
        )
    q_enc[...] = product(h_zero[...], enc_query[...]).astype(low)
    kv_enc[...] = contract_first(x_norm_t[...], enc_keyval[...]).astype(low)
    for g in range(n_head):
        keys = kv_enc[:, 2 * g * width : (2 * g + 1) * width]
        values = kv_enc[:, (2 * g + 1) * width : (2 * g + 2) * width]
        outcome = jnp.zeros((rows, width), jnp.float32)
        for here, q_head in head_lanes(g, heads, q_enc[...]):
            scores = enc_scores(q_head, keys)
            probs = jnp.exp2((scores - jnp.max(scores, 1, keepdims=True)).astype(low))
            total = jnp.sum(probs.astype(jnp.float32), 1, keepdims=True)
            outcome = jnp.where(here, product(probs, values) / total, outcome)
        o_enc[:, g * width : (g + 1) * width] = outcome.astype(low)
    z_one[...] = z_zero[...] + product(o_enc[...], enc_output[...])
    h_one[...] = layer_norm(z_one[...], gains[1:2, :]).astype(low)
    projected = product(h_one[...], self_project[...]).astype(low)
    for slot, (g, a) in enumerate(heads_of(n_head, q_self.shape[0])):
        query, key, value = (
            projected[:, (3 * g + i) * width + a * HD : (3 * g + i) * width + (a + 1) * HD]
            for i in range(3)
        )
        q_self[slot] = pack(query)
        kv_self[slot] = jnp.concatenate([key, value], 1)


LINE = pltpu.VMEM((4, round_up(max(D, DI), 8), LANES), jnp.float32)


def shards_of(n_head, shard_rows, first, last):
    starts = borders(n_head)
    begin = starts[first] // shard_rows
    return begin, -(-starts[last] // shard_rows) - begin


def encode(lengths, weights, common, inputs_t, valid, rows, slots, n_head, shard_rows):
    begin, shards = shards_of(n_head, shard_rows, 0, 4)
    query_rows = DQ * D // LANES
    block, blocks = common_blocks(query_rows, query_rows + (LAT + 4) * D // LANES, valid)
    keys = inputs_t.shape[1]
    return pl.pallas_call(
        functools.partial(encode_kernel, n_head, shard_rows, valid, rows),
        out_shape=[
            shape_of((D, D)),
            shape_of((DI, 2 * D)),
            shape_of((D, D)),
            shape_of((D, 3 * D)),
            shape_of((4, D), jnp.float32),
            shape_of((rows, D), jnp.float32),
            shape_of((rows, D)),
            shape_of(inputs_t.shape),
            shape_of((rows, D)),
            shape_of((keys, 2 * D)),
            shape_of((rows, D)),
            shape_of((rows, D), jnp.float32),
            shape_of((rows, D)),
            shape_of((slots, rows // 2, LANES)),
            shape_of((slots, rows, LANES)),
            shape_of((8, LANES), jnp.float32),
            shape_of((1, MODES), jnp.float32),
        ],
        in_specs=[SMEM_SPEC, ANY_SPEC, ANY_SPEC, VMEM_SPEC],
        out_specs=[VMEM_SPEC] * 17,
        scratch_shapes=[
            pltpu.VMEM((shards,) + weights.shape[1:], low),
            pltpu.VMEM((blocks,) + common.shape[1:], low),
            pltpu.VMEM(weights.shape[:2] + (TILE, LANES), low),
            pltpu.VMEM((shards * shard_rows, LANES), jnp.float32),
            pltpu.VMEM((blocks * valid, LANES), jnp.float32),
            LINE,
            pltpu.VMEM((LAT, D), low),
            pltpu.SemaphoreType.DMA((3,)),
        ],
        compiler_params=pltpu.CompilerParams(vmem_limit_bytes=56 * MIB),
        name="encode",
    )(lengths, weights, common, inputs_t)


def gelu_and_slope(x):
    rate = (2.0 / jnp.pi) ** 0.5
    cubic = 0.044715
    t = jnp.tanh(rate * (x + cubic * x * x * x))
    slope = 0.5 * (1.0 + t) + 0.5 * x * (1.0 - t * t) * rate * (1.0 + 3.0 * cubic * x * x)
    return 0.5 * x * (1.0 + t), slope


def my_column(marks, rows):
    turned = marks[...].astype(jnp.float32).T
    column = lax.broadcasted_iota(jnp.int32, turned.shape, 1)
    per_head = rows // LANES
    first = lax.axis_index("head") * per_head
    picked = [
        jnp.sum(jnp.where(column == first + k, turned, 0.0), 1, keepdims=True)
        for k in range(per_head)
    ]
    return jnp.concatenate(picked, 0) if per_head > 1 else picked[0]


def middle_kernel(
    n_head,
    shard_rows,
    valid,
    first_shard,
    rows,
    counts,
    weights,
    common,
    z_one,
    o_self,
    out_queries_t,
    labels,
    modality,
    labeled,
    gains,
    dout,
    d_two_out,
    tile,
    query_grad_out,
    gain_grads,
    grads,
    held,
    held_common,
    stage,
    stage_common,
    line,
    query_grad,
    self_output,
    hidden_in,
    hidden_out,
    class_table,
    query_table,
    slope,
    activ,
    sems,
):
    heads = HEADS // n_head
    width, hidden, classes = heads * HD, FF // n_head, C // n_head
    shards = held.shape[0]
    first_row = first_shard * shard_rows
    starts = borders(n_head)
    move = Moves(sems)
    shards_here = pl.ds(first_shard, shards)
    common_here = move(common.at[pl.ds(0, held_common.shape[0])], held_common)
    weights_here = [move(weights.at[shards_here, g], held.at[:, g]) for g in range(n_head)]
    common_here.wait()
    load_common(stage_common, held_common, valid)
    for j, value in matrix_of(stage_common, 0, DQ, D, line):
        query_table[:, j : j + LANES] = value.astype(low)
    for g in range(n_head):
        weights_here[g].wait()
        load_stage(stage, held, first_shard, shard_rows, g)
        load_matrices(
            stage, first_row, n_head, g, (4, 5, 6, 7), (self_output, hidden_in, hidden_out, class_table), line
        )
    gain_two, gain_three = gains[2:3, :], gains[3:4, :]
    o_heads = {head: unpack(o_self[s]) for s, head in enumerate(heads_of(n_head, o_self.shape[0]))}
    o_groups = [joined_lanes([o_heads[(g, a)] for a in range(heads)]) for g in range(n_head)]
    o_low = jnp.concatenate(o_groups, 1)
    z_two = z_one[...] + product(o_low, self_output[...])
    h_two = layer_norm(z_two, gain_two).astype(low)
    value, bend = gelu_and_slope(product(h_two, hidden_in[...]))
    activ[...] = value.astype(low)
    slope[...] = bend
    z_three = z_two + product(activ[...], hidden_out[...])
    queries_t = out_queries_t[...]
    decoded = layer_norm(z_three, gain_three) + contract_first(queries_t, query_table[...])
    decoded = decoded.astype(low)
    logits = product(decoded, class_table[...])
    label, kind, counted = (my_column(marks, rows) for marks in (labels, modality, labeled))
    lane = lax.broadcasted_iota(jnp.int32, (rows, C), 1).astype(jnp.float32)
    is_target = jnp.where(lane == label, 1.0, 0.0)
    row_top = jnp.max(logits, 1, keepdims=True)
    row_lse = row_top + jnp.log(jnp.sum(jnp.exp2((logits - row_top) * LOG2E), 1, keepdims=True))
    loss = row_lse - jnp.sum(is_target * logits, 1, keepdims=True)
    weight = jnp.zeros((rows, 1), jnp.float32)
    place = lax.broadcasted_iota(jnp.int32, (1, LANES), 1)
    losses = jnp.zeros((1, LANES), jnp.float32)
    for m in range(MODES):
        member = jnp.where((kind == m) & (counted == 1.0), 1.0, 0.0)
        weight = weight + member / jnp.maximum(counts[0:1, m : m + 1], 1.0)
        losses = losses + jnp.where(place == m, jnp.sum(loss * member, 0, keepdims=True), 0.0)
    tile[...] = jnp.broadcast_to(losses, tile.shape)
    dlogits = (weight * (jnp.exp2((logits - row_lse) * LOG2E) - is_target)).astype(low)
    d_decoded = against(dlogits, class_table[...])
    matrix_into(query_grad, 0, product(queries_t, d_decoded.astype(low)), line)
    stored = [move(query_grad, query_grad_out)]
    d_three, gain_three_grad = norm_pullback(z_three, gain_three, d_decoded)
    d_branch = d_three.astype(low)
    d_pre = (slope[...] * against(d_branch, hidden_out[...])).astype(low)
    d_middle, gain_two_grad = norm_pullback(z_two, gain_two, against(d_pre, hidden_in[...]))
    d_two = d_three + d_middle
    d_two_out[...] = d_two
    gain_grads[...] = jnp.concatenate([gain_two_grad, gain_three_grad], 0)
    d_two_low = d_two.astype(low)
    d_o = against(d_two_low, self_output[...]).astype(low)
    for slot, (g, a) in enumerate(heads_of(n_head, o_self.shape[0])):
        dout[slot] = pack(d_o[:, g * width + a * HD : g * width + (a + 1) * HD])
    h_two_t, decoded_t = turned(h_two), turned(decoded)
    for g in range(n_head):
        results = (
            contract_first(o_groups[g], d_two_low),
            product(h_two_t, d_pre[:, g * hidden : (g + 1) * hidden]),
            contract_first(activ[:, g * hidden : (g + 1) * hidden], d_branch),
            product(decoded_t, dlogits[:, g * classes : (g + 1) * classes]),
        )
        for m, result in zip((4, 5, 6, 7), results):
            matrix_into(stage, starts[m] - first_row, result, line)
        for b in range(shards):
            held[b, g, :shard_rows, :] = stage[pl.ds(b * shard_rows, shard_rows), :].astype(low)
        stored.append(move(held.at[:, g], grads.at[shards_here, g]))
    for copy in stored:
        copy.wait()


def middle(counts, weights, common, z_one, o_self, out_queries_t, marks, gains, valid, n_head, shard_rows):
    rows = z_one.shape[0]
    begin, shards = shards_of(n_head, shard_rows, 4, 8)
    query_rows = DQ * D // LANES
    block, blocks = common_blocks(0, query_rows, valid)
    return pl.pallas_call(
        functools.partial(middle_kernel, n_head, shard_rows, valid, begin, rows),
        grid=(1,),
        out_shape=[
            shape_of(o_self.shape),
            shape_of((rows, D), jnp.float32),
            shape_of((8, LANES), jnp.float32),
            shape_of((query_rows, LANES), jnp.float32),
            shape_of((2, D), jnp.float32),
            shape_of(weights.shape),
        ],
        in_specs=[
            VMEM_SPEC,
            ANY_SPEC,
            ANY_SPEC,
            VMEM_SPEC,
            VMEM_SPEC,
            pl.BlockSpec((DQ, rows), lambda i: (0, lax.axis_index("head"))),
            VMEM_SPEC,
            VMEM_SPEC,
            VMEM_SPEC,
            VMEM_SPEC,
        ],
        out_specs=[VMEM_SPEC] * 3 + [ANY_SPEC, VMEM_SPEC, ANY_SPEC],
        scratch_shapes=[
            pltpu.VMEM((shards,) + weights.shape[1:], low),
            pltpu.VMEM((blocks,) + common.shape[1:], low),
            pltpu.VMEM((shards * shard_rows, LANES), jnp.float32),
            pltpu.VMEM((blocks * valid, LANES), jnp.float32),
            LINE,
            pltpu.VMEM((query_rows, LANES), jnp.float32),
            pltpu.VMEM((D, D), low),
            pltpu.VMEM((D, FF), low),
            pltpu.VMEM((FF, D), low),
            pltpu.VMEM((D, C), low),
            pltpu.VMEM((DQ, D), low),
            pltpu.VMEM((rows, FF), jnp.float32),
            pltpu.VMEM((rows, FF), low),
            pltpu.SemaphoreType.DMA((2 + 2 * n_head,)),
        ],
        compiler_params=pltpu.CompilerParams(vmem_limit_bytes=56 * MIB),
        name="middle",
    )(counts, weights, common, z_one, o_self, out_queries_t, *marks, gains)


def ending_kernel(
    n_head,
    shard_rows,
    valid,
    rows,
    lengths,
    grads_in,
    d_q_self,
    d_kv_self,
    gains,
    gain_grads,
    *refs,
):
    kept_in, (grads, common_grad), kept = refs[:14], refs[14:16], refs[16:30]
    held, stage, stage_common, line, d_q, d_kv, sems = refs[30:]
    (
        d_two,
        query_grad,
        enc_query,
        enc_keyval,
        enc_output,
        self_project,
        z_zero,
        h_zero,
        x_norm_t,
        q_enc,
        kv_enc,
        o_enc,
        z_one,
        h_one,
    ) = kept
    move = Moves(sems)
    first_used = (12, 5, 0, 4, 10, 9, 2, 6, 1, 7, 8, 11, 3, 13)
    loads = {i: move(kept_in[i], kept[i]) for i in first_used}

    def need(*which):
        for i in which:
            loads[i].wait()

    heads = HEADS // n_head
    width = heads * HD
    shards = held.shape[0]
    starts = borders(n_head)
    shared = move(grads_in.at[pl.ds(shards - 1, 1)], held.at[pl.ds(shards - 1, 1)])
    d_heads = {}
    for slot, head in enumerate(heads_of(n_head, d_kv_self.shape[0])):
        d_kv_head = d_kv_self[slot]
        d_heads[head] = (unpack(d_q_self[slot]), d_kv_head[:, :HD], d_kv_head[:, HD:])
    d_projected = [
        jnp.concatenate([d_heads[(g, a)][i] for i in range(3) for a in range(heads)], 1)
        for g in range(n_head)
    ]
    whole = jnp.concatenate(d_projected, 1)
    need(12, 5, 0)
    d_middle, gain_one_grad = norm_pullback(
        z_one[...], gains[1:2, :], against(whole, self_project[...])
    )
    d_one = d_two[...] + d_middle
    d_one_low = d_one.astype(low)
    need(4, 10, 9)
    d_o = against(d_one_low, enc_output[...]).astype(low)
    for g in range(n_head):
        keys = kv_enc[:, 2 * g * width : (2 * g + 1) * width]
        values = kv_enc[:, (2 * g + 1) * width : (2 * g + 2) * width]
        d_key = jnp.zeros(keys.shape, jnp.float32)
        d_value = jnp.zeros(keys.shape, jnp.float32)
        d_query_t = []
        keys_t = turned(keys)
        for (here, q_head), (unused, do_head) in zip(
            head_lanes(g, heads, q_enc[...]), head_lanes(g, heads, d_o)
        ):
            scores = enc_scores(keys, q_head)
            probs = jnp.exp2((scores - jnp.max(scores, 0, keepdims=True)).astype(low))
            probs = probs.astype(jnp.float32)
            probs = probs / jnp.sum(probs, 0, keepdims=True)
            d_probs = against(values, do_head)
            delta = jnp.sum(probs * d_probs, 0, keepdims=True)
            d_scores = (probs * (d_probs - delta)).astype(low)
            d_value = d_value + product(probs.astype(low), do_head)
            d_key = d_key + product(d_scores, q_head)
            a = len(d_query_t)
            d_query_t.append(product(keys_t[a * HD : (a + 1) * HD], d_scores))
        d_query = jnp.concatenate(d_query_t, 0).T
        d_q[:, g * width : (g + 1) * width] = (d_query * SCORE_SCALE).astype(low)
        d_kv[:, 2 * g * width : (2 * g + 1) * width] = (d_key * SCORE_SCALE).astype(low)
        d_kv[:, (2 * g + 1) * width : (2 * g + 2) * width] = d_value.astype(low)
    need(2, 6)
    d_middle, gain_zero_grad = norm_pullback(
        z_zero[...], gains[0:1, :], against(d_q[...], enc_query[...])
    )
    d_zero = d_one + d_middle
    d_zero_top = d_zero.astype(low)
    d_zero_rest = (d_zero - d_zero_top.astype(jnp.float32)).astype(low)
    picked_t = picked_rows(clip_bounds(lengths), rows, n_head, 1)
    latent_grad = product(picked_t, d_zero_top) + product(picked_t, d_zero_rest)
    need(1, 7, 8, 11, 3, 13)
    query_rows = query_grad.shape[0]
    stage_common[:query_rows] = query_grad[...]
    matrix_into(stage_common, query_rows, latent_grad, line)
    all_gains = jnp.concatenate([gain_zero_grad, gain_one_grad, gain_grads[...]], 0)
    matrix_into(stage_common, query_rows + LAT * D // LANES, all_gains, line)
    piece = common_grad.shape[2]
    for b in range(common_grad.shape[0]):
        for k in range(common_grad.shape[1]):
            amount = min(piece, valid - k * piece)
            block = stage_common[b * valid + k * piece : b * valid + k * piece + amount, :]
            if amount < piece:
                block = jnp.concatenate([block, jnp.zeros((piece - amount, LANES), jnp.float32)], 0)
            common_grad[b, k] = block.astype(low)
    shared.wait()
    shared_rows = shards * shard_rows - starts[4]
    stored = []
    h_zero_t, h_one_t = turned(h_zero[...]), turned(h_one[...])
    for g in range(n_head):
        results = (
            product(h_zero_t, d_q[:, g * width : (g + 1) * width]),
            product(x_norm_t[...], d_kv[:, 2 * g * width : (2 * g + 2) * width]),
            contract_first(o_enc[:, g * width : (g + 1) * width], d_one_low),
            product(h_one_t, d_projected[g]),
        )
        if shared_rows:
            stage[pl.ds((shards - 1) * shard_rows, shard_rows), :] = held[
                shards - 1, g, :shard_rows, :
            ].astype(jnp.float32)
        for m, result in zip((0, 1, 2, 3), results):
            matrix_into(stage, starts[m], result, line)
        for b in range(shards):
            held[b, g, :shard_rows, :] = stage[pl.ds(b * shard_rows, shard_rows), :].astype(low)
        stored.append(move(held.at[:, g], grads.at[pl.ds(0, shards), g]))
    for copy in stored:
        copy.wait()


def ending(lengths, grads, d_self, d_two, gains, gain_grads, query_grad, kept, common_shape, valid, shard_rows):
    rows = d_two.shape[0]
    n_head = grads.shape[1]
    begin, shards = shards_of(n_head, shard_rows, 0, 4)
    kept = (d_two, query_grad) + tuple(kept)
    keys = kept[8].shape[1]
    common_rows = (DQ + LAT + 4) * D // LANES
    return pl.pallas_call(
        functools.partial(ending_kernel, n_head, shard_rows, valid, rows),
        out_shape=[shape_of(grads.shape), shape_of(common_shape)],
        in_specs=[SMEM_SPEC, ANY_SPEC] + [VMEM_SPEC] * 4 + [ANY_SPEC] * len(kept),
        out_specs=[ANY_SPEC, VMEM_SPEC],
        input_output_aliases={1: 0},
        scratch_shapes=[pltpu.VMEM(a.shape, a.dtype) for a in kept]
        + [
            pltpu.VMEM((shards,) + grads.shape[1:], low),
            pltpu.VMEM((shards * shard_rows, LANES), jnp.float32),
            pltpu.VMEM((common_rows, LANES), jnp.float32),
            LINE,
            pltpu.VMEM((rows, D), low),
            pltpu.VMEM((keys, 2 * D), low),
            pltpu.SemaphoreType.DMA((len(kept) + 1 + n_head,)),
        ],
        compiler_params=pltpu.CompilerParams(vmem_limit_bytes=56 * MIB),
        name="ending",
    )(lengths, grads, *d_self, gains, gain_grads, *kept)


def adam_step(weight, first, second, grad):
    first = beta_one * first + (1 - beta_one) * grad
    second = beta_two * second + (1 - beta_two) * grad * grad
    fixed_first = first / (1 - beta_one**STEP)
    fixed_second = second / (1 - beta_two**STEP)
    weight = weight - learn_rate * (
        fixed_first / (jnp.sqrt(fixed_second) + adam_eps) + weight_decay * weight
    )
    return (weight, first, second, weight.astype(low))


def per_device(
    inputs,
    out_queries,
    clip_lengths,
    labels,
    modality,
    labeled,
    head_params,
    head_first,
    head_second,
    common_params,
    common_first,
    common_second,
):
    n_head, n_blk = lax.axis_size("head"), lax.axis_size("blk")
    dims = grid_of(n_blk, n_head)
    rows = labels.shape[0] // n_head
    n_h, n_c = head_params.shape[0], common_params.shape[0]
    shard_rows, common_rows = n_h // LANES, -(-n_c // LANES)
    head_rows = round_up(shard_rows + 1, TILE)
    piece_rows = round_up(-(-common_rows // n_head), TILE)
    marks = [x.reshape(-1, LANES) for x in (labels, modality, labeled)]
    head_wide = head_params.reshape(shard_rows, LANES)
    common_wide = jnp.pad(common_params, (0, common_rows * LANES - n_c)).reshape(common_rows, LANES)
    weights, common = gather_all(dims, marks, (head_wide, common_wide), (head_rows, piece_rows), 0)
    valid = common_rows
    if n_c % LANES:
        common = common.reshape(n_blk, -1)[:, :n_c].reshape(-1, LANES)
        valid = common.shape[0]
        common = jnp.pad(common, ((0, -valid % TILE), (0, 0)))[None, None]

    encoded = encode(
        clip_lengths, weights, common, inputs.T, valid, rows, Team(dims).size, n_head, shard_rows
    )
    gains, z_one, counts = encoded[4], encoded[11], encoded[15]
    o_self, lse_self, out_self_t, q_all, kv_all = attend(
        dims, clip_lengths, encoded[13], encoded[14], 1
    )
    dout, d_two, tile, query_grad, gain_grads, grads = middle(
        counts, weights, common, z_one, o_self, out_queries.T, marks, gains, valid, n_head, shard_rows
    )
    d_self = attend_back(dims, clip_lengths, q_all, kv_all, dout, out_self_t, lse_self, 2)
    kept = encoded[:4] + encoded[5:13]
    grads, common_grad = ending(
        clip_lengths,
        grads,
        d_self,
        d_two,
        gains,
        gain_grads,
        query_grad,
        kept,
        common.shape,
        valid,
        shard_rows,
    )
    if n_c % LANES:
        common_grad = common_grad[0, 0, :valid].reshape(n_blk, n_c)
        common_grad = jnp.pad(common_grad, ((0, 0), (0, n_head * piece_rows * LANES - n_c)))
        common_grad = common_grad.reshape(n_blk, n_head, piece_rows, LANES)
    head_share, common_share, loss_sums, clip_norm, factor = reduce_all(
        dims, (grads, common_grad), (shard_rows, common_rows), tile, 3
    )
    label_counts, loss_sums = encoded[16].reshape(MODES), loss_sums.reshape(MODES)
    clip_norm, factor = clip_norm.reshape(()), factor.reshape(())
    head_share, common_share = head_share.reshape(-1), common_share.reshape(-1)[:n_c]
    head_out = adam_step(head_params, head_first, head_second, head_share * factor)
    common_out = adam_step(common_params, common_first, common_second, common_share * factor)
    return head_out + common_out + (loss_sums, label_counts, clip_norm)


def solution(mesh):
    placed = (
        P("blk", None),
        P("blk", None),
        P(),
        P("blk"),
        P("blk"),
        P("blk"),
        P(("head", "blk")),
        P(("head", "blk")),
        P(("head", "blk")),
        P("blk"),
        P("blk"),
        P("blk"),
    )
    return jax.shard_map(
        per_device,
        mesh=mesh,
        in_specs=placed,
        out_specs=(
            P(("head", "blk")),
            P(("head", "blk")),
            P(("head", "blk")),
            P(("head", "blk")),
            P("blk"),
            P("blk"),
            P("blk"),
            P("blk"),
            P(),
            P(),
            P(),
        ),
        check_vma=False,
    )
```
